32 devices in a mesh: ep: 8 (over z, y), tp: 4 (over x, core).
Axes of the slice: x: 2, y: 2, z: 4, core: 2. Of those that a mesh axis runs over, the one named last changes fastest.
Arguments:
- tokens: bfloat16 [4096, 2048], P('ep'), may hold values from -6 to 6
- lengths: int32 [14], replicated, may hold values from 1 to 1024, as said below
- routes: int32 [4096, 4], P('ep'), may hold values from 0 to 11, all different within a row; in each aligned block of 512 rows (0 to 511, 512 to 1023, ...) at most 240 rows name the same one
- attn_gain: bfloat16 [2048], P('ep'), may hold values from 0.25 to 1.75
- w_query: bfloat16 [2048, 2048], P('ep', 'tp'), may hold values from -0.125 to 0.125
- w_key: bfloat16 [2048, 2048], P('ep', 'tp'), may hold values from -0.125 to 0.125
- w_value: bfloat16 [2048, 2048], P('ep', 'tp'), may hold values from -0.125 to 0.125
- w_out: bfloat16 [2048, 2048], P('ep', 'tp'), may hold values from -1 to 1
- ffn_gain: bfloat16 [2048], P('ep'), may hold values from 0.25 to 1.75
- w_router: bfloat16 [2048, 12], P('ep'), may hold values from -0.0625 to 0.0625
- shared_mix: bfloat16 [2048], P('ep'), may hold values from -0.125 to 0.125
- shared_gate: bfloat16 [2048, 5632], P('ep', 'tp'), may hold values from -0.125 to 0.125
- shared_up: bfloat16 [2048, 5632], P('ep', 'tp'), may hold values from -0.125 to 0.125
- shared_down: bfloat16 [2048, 5632], P('ep', 'tp'), may hold values from -0.078125 to 0.078125
- expert_gate: bfloat16 [16, 1408, 2048], P('ep', 'tp'), may hold values from -0.125 to 0.125
- expert_up: bfloat16 [16, 1408, 2048], P('ep', 'tp'), may hold values from -0.125 to 0.125
- expert_down: bfloat16 [16, 1408, 2048], P('ep', 'tp'), may hold values from -3.5 to 3.5
- cotangent: bfloat16 [4096, 2048], P('ep'), may hold values from -6 to 6
Outputs:
- block_out: bfloat16 [4096, 2048], P('ep')
- grad_tokens: float32 [4096, 2048], P('ep')
- grad_attn_gain: float32 [2048], P('ep')
- grad_query: float32 [2048, 2048], P('ep', 'tp')
- grad_key: float32 [2048, 2048], P('ep', 'tp')
- grad_value: float32 [2048, 2048], P('ep', 'tp')
- grad_out: float32 [2048, 2048], P('ep', 'tp')
- grad_ffn_gain: float32 [2048], P('ep')
- grad_router: float32 [2048, 12], P('ep')
- grad_shared_mix: float32 [2048], P('ep')
- grad_shared_gate: float32 [2048, 5632], P('ep', 'tp')
- grad_shared_up: float32 [2048, 5632], P('ep', 'tp')
- grad_shared_down: float32 [2048, 5632], P('ep', 'tp')
- grad_expert_gate: float32 [16, 1408, 2048], P('ep', 'tp')
- grad_expert_up: float32 [16, 1408, 2048], P('ep', 'tp')
- grad_expert_down: float32 [16, 1408, 2048], P('ep', 'tp')
The draws below stay inside these ranges and needn't reach their ends.
Inputs may be any that keep to these rules, and one draw needn't show every extreme that they name: `lengths`: the sequences lie end to end over all 4096 positions. One begins at position 0 and none at any other multiple of 512; every aligned block of 512 positions holds exactly two sequence starts except one block, neither the first nor the last, which holds none; exactly one sequence has 1024 tokens. `routes`: in each aligned block of 512 rows no expert is named by more than 240 rows, a bound that some block reaches.
All inputs are finite; a program needn't handle non-finite values.
Results may differ from the reference program's by a relative error of at most 0.018.
Values may be sent and summed in bfloat16 or wider, within the bound.
A program may use at most 384 MiB of HBM per device.

```python
import math
import jax
import jax.numpy as jnp
import numpy as np
from jax import lax

D = 2048
HEADS = 16
HD = 128
FF_E = 1408
SH = 5632
TOP = 4
TOK_DEV = 512
SLOTS = 16
ROUTED_EXPERTS = 12
TOKENS = 4096
SEQS = 14
CAP = 240
N_EP = 8


def draw_lengths(key, part):
    key = jax.random.fold_in(key, 7)
    pick, lower, upper, meet = jax.random.split(key, 4)
    device = jnp.arange(N_EP, dtype=jnp.int32)
    empty = jax.random.randint(pick, (), 1, N_EP - 1)
    joint = jax.random.randint(meet, (), 2, TOK_DEV - 1)
    base = jax.random.randint(lower, (N_EP,), 0, 1 << 20)
    spare = jax.random.randint(upper, (N_EP,), 0, 1 << 20)
    first = 1 + base % (TOK_DEV - 2)
    first = jnp.where(device == empty - 1, 1 + base % (joint - 1), first)
    first = jnp.where(device == empty + 1, joint, first)
    first = jnp.where(device == 0, 0, first)
    second = first + 1 + spare % (TOK_DEV - 1 - first)
    second = jnp.where(device == empty - 1, joint, second)
    starts = jnp.stack([first, second], axis=1) + device[:, None] * TOK_DEV
    keep = jnp.repeat(device != empty, 2)
    order = jnp.where(keep, starts.reshape(-1), TOKENS + starts.reshape(-1))
    kept = jnp.sort(order)[:SEQS]
    ends = jnp.concatenate([kept[1:], jnp.full((1,), TOKENS, jnp.int32)])
    return (ends - kept).astype(jnp.int32)


def raised(entries, key, source, target, blocks, factor):
    owner, partner = [(jnp.arange(entries.shape[position]) // (entries.shape[position] // blocks)).reshape([-1 if axis == position else 1 for axis in range(entries.ndim)]) for position in (source, target)]
    chosen = jax.random.permutation(key, blocks)[partner]
    strong = (owner == chosen) | (owner == (partner + blocks // 2) % blocks)
    return jnp.where(strong, factor * entries, entries)


def levels(own_key, shape, cuts, smallest, high):
    level, own = 1.0, jax.random.fold_in(own_key, 6)
    for position, blocks in cuts:
        heights = jnp.exp(jax.random.uniform(jax.random.fold_in(own, position), (blocks,), jnp.float32, smallest / len(cuts), high / len(cuts)))
        level = level * jnp.repeat(heights, shape[position] // blocks).reshape([-1 if axis == position else 1 for axis in range(len(shape))])
    return level


def deal_out(key, own, number, rows, amount, top, bound, slope):
    ranking = jax.random.permutation(key, amount)
    crowded, usual = shares(amount, rows * top, bound, slope, True), shares(amount, rows * top, bound, slope, False)
    places = jnp.arange(amount)

    def named(sizes, offset_by):
        used = int((sizes > 0).sum())
        fixed = max(1, used // 4)
        moved = fixed + (places - fixed + offset_by * (used - fixed)) % max(1, amount - fixed)
        return jnp.zeros((amount,), jnp.int32).at[ranking[jnp.where(places < fixed, places, moved)]].set(jnp.asarray(sizes, jnp.int32))

    sizes = jnp.where(number % 4 == 0, named(crowded, number // 4), named(usual, number - number // 4 - 1))
    mixed = jax.random.permutation(jax.random.fold_in(own, 3), amount)
    source_of, sink = mixed[0:amount // 2 * 2:2], mixed[1:amount // 2 * 2:2]
    margin = jnp.minimum(sizes[source_of] - 1, bound - sizes[sink]) // 2
    margin = jnp.where((source_of == ranking[0]) | (sink == ranking[0]) | (sizes[sink] == 0), 0, jnp.maximum(margin, 0))
    moved = jax.random.randint(jax.random.fold_in(own, 4), (amount // 2,), 0, 1 << 20) % (margin + 1)
    sizes = sizes.at[source_of].add(-moved).at[sink].add(moved)
    items = jnp.searchsorted(jnp.cumsum(sizes), jnp.arange(rows * top), side="right").astype(jnp.int32)
    grid = items.reshape(top, rows).T
    grid = grid[jax.random.permutation(jax.random.fold_in(own, 1), rows)]
    offset_by = jax.random.randint(jax.random.fold_in(own, 2), (rows, 1), 0, top)
    return jnp.take_along_axis(grid, (jnp.arange(top)[None, :] + offset_by) % top, axis=1)


def shares(count, total, bound, skew, full):
    portions = [(1 << 20) // math.isqrt(rank ** skew) + 1 for rank in range(1, count + 1)]
    largest = bound if full else min(bound, max(-(-total // count), total * portions[0] // sum(portions)))
    least = 1 if total - largest >= count - 1 else 0
    counts, rest = [largest] + [least] * (count - 1), total - largest - least * (count - 1)
    while rest > 0:
        candidates = [i for i in range(1, count) if counts[i] < largest] or [i for i in range(1, count) if counts[i] < bound]
        mass, remaining = sum([portions[i] for i in candidates]), rest
        for i in candidates:
            extra = min(bound - counts[i], max(1, remaining * portions[i] // mass), rest)
            counts[i] = counts[i] + extra
            rest = rest - extra
    return np.array(counts)


def bell_draw(stream_key, shape, scale, bound, shards=(), kind=jnp.bfloat16):
    level = levels(stream_key, shape, shards, -0.22, 0.18) if shards else 1.0
    values = jax.random.normal(stream_key, shape, jnp.float32) * scale * level
    return jnp.minimum(jnp.maximum(values, -bound), bound).astype(kind)


def bell_draw_with(own_key, dims, deviation, most, shards, heavy, kind=jnp.bfloat16):
    values = deviation * jax.random.normal(own_key, dims, jnp.float32)
    if shards:
        values = values * levels(own_key, dims, shards, -0.22, 0.18)
    return jnp.clip(raised(values, jax.random.fold_in(own_key, 3), *heavy), -most, most).astype(kind)


def setup_inputs(seed: int = 0) -> dict:
    key_of = jax.random.split(jax.random.key(seed), 19)
    tokens = bell_draw(key_of[0], (TOKENS, D), 1.0, 6.0, ((0, 8),))
    lengths = draw_lengths(jax.random.fold_in(key_of[18], 71), 0)
    routes_keys = jax.random.split(jax.random.fold_in(key_of[2], 1), TOKENS // TOK_DEV)
    routes_turns = jax.random.permutation(jax.random.fold_in(key_of[2], 3), TOKENS // TOK_DEV)
    routes = jax.vmap(lambda own, number: deal_out(jax.random.fold_in(key_of[2], 2), own, number, TOK_DEV, ROUTED_EXPERTS, TOP, CAP, 1))(routes_keys, routes_turns).reshape((TOKENS, TOP))
    attn_gain = jnp.clip(1.0 + 0.15 * jax.random.normal(key_of[3], (D,), jnp.float32), 0.25, 1.75).astype(jnp.bfloat16)
    w_query = bell_draw(key_of[4], (D, HEADS * HD), D ** -0.5, 0.125, ((0, 8), (1, 4)))
    w_key = bell_draw(key_of[5], (D, HEADS * HD), D ** -0.5, 0.125, ((0, 8), (1, 4)))
    w_value = bell_draw(key_of[6], (D, HEADS * HD), D ** -0.5, 0.125, ((0, 8), (1, 4)))
    w_out = bell_draw(key_of[7], (D, HEADS * HD), (max(D // 64, 1)) ** -0.5, 1.0, ((0, 8), (1, 4)))
    ffn_gain = jnp.clip(1.0 + 0.15 * jax.random.normal(key_of[8], (D,), jnp.float32), 0.25, 1.75).astype(jnp.bfloat16)
    w_router = bell_draw(key_of[9], (D, ROUTED_EXPERTS), (4 * D) ** -0.5, 0.0625, ((0, 8),))
    shared_mix = bell_draw(key_of[10], (D,), D ** -0.5, 0.125, ((0, 8),))
    shared_gate = bell_draw(key_of[11], (D, SH), D ** -0.5, 0.125, ((0, 8), (1, 4)))
    shared_up = bell_draw(key_of[12], (D, SH), D ** -0.5, 0.125, ((0, 8), (1, 4)))
    shared_down = bell_draw(key_of[13], (D, SH), SH ** -0.5, 0.078125, ((0, 8), (1, 4)))
    expert_gate = bell_draw(key_of[14], (SLOTS, FF_E, D), D ** -0.5, 0.125, ((0, 8), (1, 4)))
    expert_up = bell_draw(key_of[15], (SLOTS, FF_E, D), D ** -0.5, 0.125, ((0, 8), (1, 4)))
    expert_down = bell_draw(key_of[16], (SLOTS, FF_E, D), (max(FF_E // 400, 1)) ** -0.5, 3.5, ((0, 8), (1, 4)))
    cotangent = bell_draw_with(key_of[17], (TOKENS, D), 1.0, 6.0, ((0, 8),), (0, 1, 8, 2.0))
    return dict(tokens=tokens, lengths=lengths, routes=routes, attn_gain=attn_gain, w_query=w_query, w_key=w_key, w_value=w_value, w_out=w_out, ffn_gain=ffn_gain, w_router=w_router, shared_mix=shared_mix, shared_gate=shared_gate, shared_up=shared_up, shared_down=shared_down, expert_gate=expert_gate, expert_up=expert_up, expert_down=expert_down, cotangent=cotangent)


epsilon = 1e-06
rope_base = 1000000.0
highest = lax.Precision.HIGHEST

@jax.custom_vjp
def low(v):
    return lax.optimization_barrier(v.astype(jnp.bfloat16)).astype(jnp.float32)

@jax.custom_vjp
def low_back(v):
    return v

def low_keep(v):
    return (low(v), None)

def low_pass(kept, grad):
    return (grad,)

def back_keep(v):
    return (v, None)

def back_low(kept, grad):
    return (low(grad),)
low.defvjp(low_keep, low_pass)
low_back.defvjp(back_keep, back_low)

def matmul(left, right):
    return jnp.dot(left, right, precision=highest, preferred_element_type=jnp.float32)

def widen(array):
    return array.astype(jnp.float32)

def rms_norm(values, gain):
    scale = lax.rsqrt(lax.optimization_barrier(jnp.mean(values * values, axis=-1, keepdims=True)) + epsilon)
    return values * scale * gain

def rope_tables(positions, width):
    steps = jnp.arange(0, width, 2, dtype=jnp.float32) / width
    inverse = rope_base ** (-steps)
    angles = positions.astype(jnp.float32)[:, None] * inverse[None, :]
    angles = jnp.concatenate([angles, angles], axis=-1)
    return (jnp.cos(angles)[:, None, :], jnp.sin(angles)[:, None, :])

def turn_half(values):
    middle = values.shape[-1] // 2
    return jnp.concatenate([-values[..., middle:], values[..., :middle]], axis=-1)

def rotate(values, cosine, sine):
    return values * cosine + turn_half(values) * sine

def sequence_info(lengths, indices):
    starts = (jnp.cumsum(lengths) - lengths).astype(jnp.int32)
    inside = starts[None, :] <= indices[:, None]
    segment = (lax.optimization_barrier(jnp.sum(inside.astype(jnp.int32), axis=1)) - 1).astype(jnp.int32)
    first = lax.optimization_barrier(jnp.max(jnp.where(inside, starts[None, :], -1), axis=1)).astype(jnp.int32)
    return (segment, (indices - first).astype(jnp.int32))

def reference(tokens, lengths, routes, attn_gain, w_query, w_key, w_value, w_out, ffn_gain, w_router, shared_mix, shared_gate, shared_up, shared_down, expert_gate, expert_up, expert_down, cotangent):
    positions = jnp.arange(TOKENS, dtype=jnp.int32)
    segment, place = sequence_info(lengths, positions)
    cosine, sine = rope_tables(place, HD)
    score_scale = HD ** (-0.5)
    flat = routes.reshape(-1).astype(jnp.int32)
    owner = (jnp.arange(TOKENS * TOP, dtype=jnp.int32) // TOP).astype(jnp.int32)
    source = (owner // TOK_DEV).astype(jnp.int32)
    hot = (flat.reshape(N_EP, TOK_DEV * TOP)[:, :, None] == jnp.arange(ROUTED_EXPERTS, dtype=jnp.int32)[None, None, :]).astype(jnp.int32)
    rank = (lax.optimization_barrier(jnp.sum(jnp.cumsum(hot, axis=1) * hot, axis=2)) - 1).reshape(-1).astype(jnp.int32)
    row_index = (flat * (N_EP * CAP) + source * CAP + rank).astype(jnp.int32)
    token_for_row = jnp.zeros((ROUTED_EXPERTS * N_EP * CAP,), jnp.int32).at[row_index].set(owner).reshape(ROUTED_EXPERTS, N_EP * CAP)
    row_valid = jnp.zeros((ROUTED_EXPERTS * N_EP * CAP,), jnp.float32).at[row_index].set(1.0).reshape(ROUTED_EXPERTS, N_EP * CAP)
    expert_ids = jnp.arange(ROUTED_EXPERTS, dtype=jnp.int32)[:, None]
    blocks = jnp.arange(TOKENS // TOK_DEV, dtype=jnp.int32)

    def layer_forward(layer_input, first_norm_scale, query_weight_matrix, key_weight_matrix, value_weight_matrix, output_weight, second_norm_scale, router_weight, shared_mixer_weight, shared_gate_weight, shared_up_weight, shared_down_weight, expert_gate_weight, expert_up_weight, expert_down_weight):
        normed_one = low(rms_norm(layer_input, first_norm_scale))
        query_pre = low_back(matmul(normed_one, query_weight_matrix)).reshape(TOKENS, HEADS, HD)
        key_pre = low_back(matmul(normed_one, key_weight_matrix)).reshape(TOKENS, HEADS, HD)
        queries = low(rotate(query_pre, cosine, sine))
        keys = low(rotate(key_pre, cosine, sine))
        values = low(low_back(matmul(normed_one, value_weight_matrix))).reshape(TOKENS, HEADS, HD)
        front = jnp.zeros((2 * TOK_DEV, HEADS, HD), jnp.float32)
        keys_pad = jnp.concatenate([front, keys], axis=0)
        values_pad = jnp.concatenate([front, values], axis=0)

        def block_attention(block):
            start = (block * TOK_DEV).astype(jnp.int32)
            query_blk = lax.dynamic_slice_in_dim(queries, start, TOK_DEV, 0)
            key_blk = lax.dynamic_slice_in_dim(keys_pad, start, 3 * TOK_DEV, 0)
            value_blk = lax.dynamic_slice_in_dim(values_pad, start, 3 * TOK_DEV, 0)
            query_at = (start + jnp.arange(TOK_DEV, dtype=jnp.int32)).astype(jnp.int32)
            key_at = (start - 2 * TOK_DEV + jnp.arange(3 * TOK_DEV, dtype=jnp.int32)).astype(jnp.int32)
            query_seg, _ = sequence_info(lengths, query_at)
            key_seg, _ = sequence_info(lengths, key_at)
            allowed = (query_seg[:, None] == key_seg[None, :]) & (key_at[None, :] <= query_at[:, None]) & (key_at[None, :] >= 0)
            scores = low_back(jnp.einsum('qhd,khd->hqk', query_blk, key_blk, precision=highest) * score_scale)
            masked = jnp.where(allowed[None], scores, -jnp.inf)
            peak = lax.optimization_barrier(jnp.max(masked, axis=-1, keepdims=True))
            expo = jnp.exp(masked - peak)
            weights = expo / lax.optimization_barrier(jnp.sum(expo, axis=-1, keepdims=True))
            return jnp.einsum('hqk,khd->qhd', low(weights), value_blk, precision=highest)
        attended = lax.map(jax.checkpoint(block_attention), blocks)
        attended = low(low_back(attended.reshape(TOKENS, HEADS * HD)))
        resid = layer_input + low_back(matmul(attended, output_weight.T))
        normed_two = low(rms_norm(resid, second_norm_scale))
        router = jax.nn.softmax(matmul(normed_two, router_weight), axis=-1)
        mixer = jax.nn.sigmoid(matmul(normed_two, shared_mixer_weight))
        shared_g = low_back(matmul(normed_two, shared_gate_weight))
        shared_u = low_back(matmul(normed_two, shared_up_weight))
        shared_h = low(jax.nn.silu(shared_g) * shared_u)
        shared_o = low_back(matmul(shared_h, shared_down_weight.T))

        def expert_token_rows(item):
            gate_w, up_w, down_w, tokens_of = item
            rows = normed_two[tokens_of]
            route_g = low_back(matmul(rows, gate_w.T))
            route_u = low_back(matmul(rows, up_w.T))
            route_h = low(jax.nn.silu(route_g) * route_u)
            return low_back(matmul(route_h, down_w))
        routed_output = lax.map(jax.checkpoint(expert_token_rows), (expert_gate_weight[:ROUTED_EXPERTS], expert_up_weight[:ROUTED_EXPERTS], expert_down_weight[:ROUTED_EXPERTS], token_for_row))
        gate_rows = router[token_for_row, expert_ids] * row_valid
        routed = jnp.zeros((TOKENS, D), jnp.float32).at[token_for_row.reshape(-1)].add((routed_output * gate_rows[:, :, None]).reshape(-1, D))
        return resid + mixer[:, None] * shared_o + routed
    float_args = (widen(tokens), widen(attn_gain), widen(w_query), widen(w_key), widen(w_value), widen(w_out), widen(ffn_gain), widen(w_router), widen(shared_mix), widen(shared_gate), widen(shared_up), widen(shared_down), widen(expert_gate), widen(expert_up), widen(expert_down))
    result, pullback = jax.vjp(layer_forward, *float_args)
    grads = pullback(widen(cotangent))
    return (result.astype(jnp.bfloat16), grads[0], grads[1], grads[2], grads[3], grads[4], grads[5], grads[6], grads[7], grads[8], grads[9], grads[10], grads[11], grads[12], grads[13], grads[14])
```

```python
import jax
import jax.numpy as jnp
from jax import lax
from jax.sharding import PartitionSpec as P

HD = 128


epsilon = 1e-06
rope_base = 1000000.0
highest = lax.Precision.HIGHEST


def passed_along(block, axis, distance):
    devices = range(lax.axis_size(axis))
    route = [(i - distance, i) for i in devices if i - distance in devices]
    return lax.ppermute(block, axis, route)


def rope_tables(positions, width):
    steps = jnp.arange(0, width, 2, dtype=jnp.float32) / width
    inverse = rope_base ** (-steps)
    angles = positions.astype(jnp.float32)[:, None] * inverse[None, :]
    angles = jnp.concatenate([angles, angles], axis=-1)
    return (jnp.cos(angles)[:, None, :], jnp.sin(angles)[:, None, :])


def turn_half(values):
    middle = values.shape[-1] // 2
    return jnp.concatenate([-values[..., middle:], values[..., :middle]], axis=-1)


def rotate(values, cosine, sine):
    return values * cosine + turn_half(values) * sine


def unrotate(grads, cosine, sine):
    return grads * cosine - turn_half(grads * sine)


def sequence_info(lengths, indices):
    starts = jnp.cumsum(lengths) - lengths
    inside = starts[None, :] <= indices[:, None]
    segment = jnp.sum(inside.astype(jnp.int32), axis=1) - 1
    first = jnp.max(jnp.where(inside, starts[None, :], -1), axis=1)
    return (segment, indices - first)


def norm_forward(values, gain):
    scale = lax.rsqrt(jnp.mean(values * values, axis=-1, keepdims=True) + epsilon)
    return (values * scale * gain, scale)


def norm_backward(values, scale, gain, grads):
    unit = values * scale
    scaled = grads * gain
    inner = jnp.mean(scaled * unit, axis=-1, keepdims=True)
    return (scale * (scaled - unit * inner), jnp.sum(grads * unit, axis=0))


def deliver(rows):
    arrived_rows = lax.all_to_all(rows, "ep", split_axis=0, concat_axis=0, tiled=True)
    return arrived_rows


def bring_back(parts, target, rows_here, top_count):
    moved = lax.all_to_all(parts, "ep", split_axis=0, concat_axis=0, tiled=True)
    piece = moved.shape[3]
    return moved.reshape(-1, piece)[target].reshape(rows_here, top_count, piece)


def body(
    tokens,
    lengths,
    routes,
    attn_gain,
    w_query,
    w_key,
    w_value,
    w_out,
    ffn_gain,
    w_router,
    shared_mix,
    shared_gate,
    shared_up,
    shared_down,
    expert_gate,
    expert_up,
    expert_down,
    cotangent,
):
    rows_here = tokens.shape[0]
    width = tokens.shape[1]
    ep_count = lax.axis_size("ep")
    offset = lax.axis_index("ep") * rows_here
    slot_here = expert_gate.shape[0]
    top_count = routes.shape[1]
    gathered = (
        lax.all_gather(attn_gain, "ep", axis=0, tiled=True),
        lax.all_gather(w_query, "ep", axis=0, tiled=True),
        lax.all_gather(w_key, "ep", axis=0, tiled=True),
        lax.all_gather(w_value, "ep", axis=0, tiled=True),
        lax.all_gather(w_out, "ep", axis=0, tiled=True),
        lax.all_gather(ffn_gain, "ep", axis=0, tiled=True),
        lax.all_gather(w_router, "ep", axis=0, tiled=True),
        lax.all_gather(shared_mix, "ep", axis=0, tiled=True),
        lax.all_gather(shared_gate, "ep", axis=0, tiled=True),
        lax.all_gather(shared_up, "ep", axis=0, tiled=True),
        lax.all_gather(shared_down, "ep", axis=0, tiled=True),
    )
    (
        gain_first,
        query_weight_matrix,
        key_weight_matrix,
        value_weight_matrix,
        output_weight,
        gain_second,
        router_weight,
        shared_mixer_weight,
        shared_gate_weight,
        shared_up_weight,
        shared_down_weight,
    ) = gathered
    expert_count = router_weight.shape[1]
    capacity = (rows_here * top_count * 7 // (5 * expert_count) + 7) // 8 * 8
    heads_here = query_weight_matrix.shape[1] // HD
    score_scale = HD ** (-0.5)
    first_norm_scale = gain_first.astype(jnp.float32)
    second_norm_scale = gain_second.astype(jnp.float32)
    layer_input = tokens.astype(jnp.float32)
    normed_wide, norm_one = norm_forward(layer_input, first_norm_scale)
    normed_one = normed_wide.astype(jnp.bfloat16)
    query_at = offset + jnp.arange(rows_here, dtype=jnp.int32)
    key_at = offset - 2 * rows_here + jnp.arange(3 * rows_here, dtype=jnp.int32)
    query_seg, query_pos = sequence_info(lengths, query_at)
    key_seg, _ = sequence_info(lengths, key_at)
    cosine, sine = rope_tables(query_pos, HD)
    query_pre = jnp.dot(
        normed_one, query_weight_matrix, preferred_element_type=jnp.float32
    ).reshape(rows_here, heads_here, HD)
    key_pre = jnp.dot(normed_one, key_weight_matrix, preferred_element_type=jnp.float32).reshape(
        rows_here, heads_here, HD
    )
    queries = rotate(query_pre, cosine, sine).astype(jnp.bfloat16)
    keys = rotate(key_pre, cosine, sine).astype(jnp.bfloat16)
    values = (
        jnp.dot(normed_one, value_weight_matrix, preferred_element_type=jnp.float32)
        .astype(jnp.bfloat16)
        .reshape(rows_here, heads_here, HD)
    )
    carried = jnp.stack([keys, values], axis=0)
    window = [carried]
    for hop in range(2):
        carried = passed_along(carried, "ep", 1)
        window = [carried] + window
    joined = jnp.concatenate(window, axis=1)
    keys_win = joined[0]
    values_win = joined[1]
    allowed = (
        (query_seg[:, None] == key_seg[None, :])
        & (key_at[None, :] <= query_at[:, None])
        & (key_at[None, :] >= 0)
    )
    scores = (
        jnp.einsum("qhd,khd->hqk", queries, keys_win, preferred_element_type=jnp.float32)
        * score_scale
    )
    masked = jnp.where(allowed[None], scores, -1e30)
    peak = jnp.max(masked, axis=-1, keepdims=True)
    expo = jnp.exp(masked - peak)
    total = jnp.sum(expo, axis=-1, keepdims=True)
    log_total = peak + jnp.log(total)
    weights = expo / total
    attended = jnp.einsum(
        "hqk,khd->qhd", weights.astype(jnp.bfloat16), values_win, preferred_element_type=jnp.float32
    )
    attended = attended.reshape(rows_here, heads_here * HD).astype(jnp.bfloat16)
    attn_part = jnp.einsum("th,dh->td", attended, output_weight, preferred_element_type=jnp.float32)
    resid = layer_input + lax.psum(attn_part, "tp")
    normed_two_wide, norm_two = norm_forward(resid, second_norm_scale)
    normed_two = normed_two_wide.astype(jnp.bfloat16)
    normed_two_f = normed_two.astype(jnp.float32)
    router_f = router_weight.astype(jnp.float32)
    mix_f = shared_mixer_weight.astype(jnp.float32)
    router = jax.nn.softmax(jnp.dot(normed_two_f, router_f, precision=highest), axis=-1)
    picked = routes[:, :, None] == jnp.arange(expert_count, dtype=jnp.int32)[None, None, :]
    gates = jnp.sum(jnp.where(picked, router[:, None, :], 0.0), axis=-1)
    mixer = jax.nn.sigmoid(jnp.dot(normed_two_f, mix_f, precision=highest))
    shared_g = jnp.dot(normed_two, shared_gate_weight, preferred_element_type=jnp.float32)
    shared_u = jnp.dot(normed_two, shared_up_weight, preferred_element_type=jnp.float32)
    shared_h = (jax.nn.silu(shared_g) * shared_u).astype(jnp.bfloat16)
    shared_part = jnp.einsum(
        "tf,df->td", shared_h, shared_down_weight, preferred_element_type=jnp.float32
    )
    flat = routes.reshape(-1)
    hot = (flat[:, None] == jnp.arange(expert_count, dtype=jnp.int32)[None, :]).astype(jnp.int32)
    rank = jnp.sum(jnp.cumsum(hot, axis=0) * hot, axis=1) - 1
    target = flat * capacity + rank
    slot_total = ep_count * slot_here * capacity
    owner_route = (
        jnp.zeros((slot_total,), jnp.int32)
        .at[target]
        .set(jnp.arange(rows_here * top_count, dtype=jnp.int32))
    )
    filled = jnp.zeros((slot_total,), jnp.bool_).at[target].set(True)
    owner_token = owner_route // top_count
    send_rows = jnp.where(filled[:, None], normed_two[owner_token], jnp.zeros((), jnp.bfloat16))
    arrived_rows = deliver(send_rows.reshape(ep_count, slot_here, capacity, width))
    route_g = jnp.einsum(
        "nscd,sfd->nscf", arrived_rows, expert_gate, preferred_element_type=jnp.float32
    )
    route_u = jnp.einsum(
        "nscd,sfd->nscf", arrived_rows, expert_up, preferred_element_type=jnp.float32
    )
    route_h = (jax.nn.silu(route_g) * route_u).astype(jnp.bfloat16)
    route_part = jnp.einsum(
        "nscf,sfd->nscd", route_h, expert_down, preferred_element_type=jnp.float32
    )
    back_rows = bring_back(route_part, target, rows_here, top_count)
    upstream = cotangent.astype(jnp.float32)
    routed = jnp.sum(back_rows * gates[:, :, None], axis=1)
    ffn_part = mixer[:, None] * shared_part + routed
    route_dot = jnp.sum(back_rows * upstream[:, None, :], axis=-1)
    shared_dot = jnp.sum(shared_part * upstream, axis=-1)
    ffn_total, d_gate, d_mixer = lax.psum((ffn_part, route_dot, shared_dot), "tp")
    block_out = (resid + ffn_total).astype(jnp.bfloat16)
    d_router = jnp.sum(jnp.where(picked, d_gate[:, :, None], 0.0), axis=1)
    d_logits = router * (d_router - jnp.sum(router * d_router, axis=-1, keepdims=True))
    d_mixlogit = d_mixer * mixer * (1.0 - mixer)
    side = jnp.dot(d_logits, router_f.T, precision=highest) + d_mixlogit[:, None] * mix_f[None, :]
    grad_router = jnp.dot(normed_two_f.T, d_logits, precision=highest)
    grad_mix = jnp.dot(d_mixlogit, normed_two_f, precision=highest)
    d_shared = (mixer[:, None] * upstream).astype(jnp.bfloat16)
    d_sh = jnp.dot(d_shared, shared_down_weight, preferred_element_type=jnp.float32)
    sig_shared = jax.nn.sigmoid(shared_g)
    d_sg = (d_sh * shared_u * sig_shared * (1.0 + shared_g * (1.0 - sig_shared))).astype(
        jnp.bfloat16
    )
    d_su = (d_sh * shared_g * sig_shared).astype(jnp.bfloat16)
    d_normed_part = jnp.einsum(
        "tf,df->td", d_sg, shared_gate_weight, preferred_element_type=jnp.float32
    )
    d_normed_part = d_normed_part + jnp.einsum(
        "tf,df->td", d_su, shared_up_weight, preferred_element_type=jnp.float32
    )
    grad_sgate = jnp.einsum("td,tf->df", normed_two, d_sg, preferred_element_type=jnp.float32)
    grad_sup = jnp.einsum("td,tf->df", normed_two, d_su, preferred_element_type=jnp.float32)
    grad_sdown = jnp.einsum("td,tf->df", d_shared, shared_h, preferred_element_type=jnp.float32)
    d_route = (
        (gates[:, :, None] * upstream[:, None, :])
        .astype(jnp.bfloat16)
        .reshape(rows_here * top_count, width)
    )
    send_grads = jnp.where(filled[:, None], d_route[owner_route], jnp.zeros((), jnp.bfloat16))
    received_grads = deliver(send_grads.reshape(ep_count, slot_here, capacity, width))
    d_rh = jnp.einsum(
        "nscd,sfd->nscf", received_grads, expert_down, preferred_element_type=jnp.float32
    )
    sig_route = jax.nn.sigmoid(route_g)
    d_rg = (d_rh * route_u * sig_route * (1.0 + route_g * (1.0 - sig_route))).astype(jnp.bfloat16)
    routed_up_gradient = (d_rh * route_g * sig_route).astype(jnp.bfloat16)
    row_grads = jnp.einsum("nscf,sfd->nscd", d_rg, expert_gate, preferred_element_type=jnp.float32)
    row_grads = row_grads + jnp.einsum(
        "nscf,sfd->nscd", routed_up_gradient, expert_up, preferred_element_type=jnp.float32
    )
    grad_egate = jnp.einsum(
        "qxba,qxbr->xar", d_rg, arrived_rows, preferred_element_type=jnp.float32
    )
    expert_up_gradient = jnp.einsum(
        "qxba,qxbr->xar", routed_up_gradient, arrived_rows, preferred_element_type=jnp.float32
    )
    grad_edown = jnp.einsum(
        "qxba,qxbr->xar", route_h, received_grads, preferred_element_type=jnp.float32
    )
    grads_back = bring_back(row_grads, target, rows_here, top_count)
    d_routed = jnp.sum(grads_back, axis=1)
    d_normed_two = lax.psum(d_normed_part + d_routed, "tp") + side
    d_resid_norm, grad_gain_two = norm_backward(resid, norm_two, second_norm_scale, d_normed_two)
    d_resid = upstream + d_resid_norm
    d_resid_low = d_resid.astype(jnp.bfloat16)
    grad_outw = jnp.einsum("td,th->dh", d_resid_low, attended, preferred_element_type=jnp.float32)
    d_attended = jnp.einsum(
        "td,dh->th", d_resid_low, output_weight, preferred_element_type=jnp.float32
    )
    d_attended = d_attended.astype(jnp.bfloat16).reshape(rows_here, heads_here, HD)
    scores_again = (
        jnp.einsum("qhd,khd->hqk", queries, keys_win, preferred_element_type=jnp.float32)
        * score_scale
    )
    probs = jnp.where(allowed[None], jnp.exp(scores_again - log_total), 0.0)
    d_probs = jnp.einsum("qhd,khd->hqk", d_attended, values_win, preferred_element_type=jnp.float32)
    delta = jnp.sum(probs * d_probs, axis=-1, keepdims=True)
    d_scores = (probs * (d_probs - delta)).astype(jnp.bfloat16)
    d_queries = (
        jnp.einsum("hqk,khd->qhd", d_scores, keys_win, preferred_element_type=jnp.float32)
        * score_scale
    )
    d_keys_win = (
        jnp.einsum("hqk,qhd->khd", d_scores, queries, preferred_element_type=jnp.float32)
        * score_scale
    )
    d_values_win = jnp.einsum(
        "hqk,qhd->khd", probs.astype(jnp.bfloat16), d_attended, preferred_element_type=jnp.float32
    )
    pair_grads = jnp.stack([d_keys_win, d_values_win], axis=0)
    older = pair_grads[:, :rows_here]
    later = [pair_grads[:, rows_here : 2 * rows_here], pair_grads[:, 2 * rows_here :]]
    running = older
    for hop in range(2):
        running = passed_along(running, "ep", -1)
        running = running + later[hop]
    d_query_pre = (
        unrotate(d_queries, cosine, sine).astype(jnp.bfloat16).reshape(rows_here, heads_here * HD)
    )
    d_key_pre = (
        unrotate(running[0], cosine, sine).astype(jnp.bfloat16).reshape(rows_here, heads_here * HD)
    )
    d_values = running[1].astype(jnp.bfloat16).reshape(rows_here, heads_here * HD)
    grad_queryw = jnp.einsum(
        "td,th->dh", normed_one, d_query_pre, preferred_element_type=jnp.float32
    )
    grad_keyw = jnp.einsum("td,th->dh", normed_one, d_key_pre, preferred_element_type=jnp.float32)
    grad_valuew = jnp.einsum("td,th->dh", normed_one, d_values, preferred_element_type=jnp.float32)
    d_normed_one = jnp.einsum(
        "th,dh->td", d_query_pre, query_weight_matrix, preferred_element_type=jnp.float32
    )
    d_normed_one = d_normed_one + jnp.einsum(
        "th,dh->td", d_key_pre, key_weight_matrix, preferred_element_type=jnp.float32
    )
    d_normed_one = d_normed_one + jnp.einsum(
        "th,dh->td", d_values, value_weight_matrix, preferred_element_type=jnp.float32
    )
    d_normed_one = lax.psum(d_normed_one, "tp")
    d_input_norm, grad_gain_one = norm_backward(
        layer_input, norm_one, first_norm_scale, d_normed_one
    )
    grad_tokens = d_resid + d_input_norm
    summed = (
        lax.psum_scatter(grad_gain_one, "ep", scatter_dimension=0, tiled=True),
        lax.psum_scatter(grad_queryw, "ep", scatter_dimension=0, tiled=True),
        lax.psum_scatter(grad_keyw, "ep", scatter_dimension=0, tiled=True),
        lax.psum_scatter(grad_valuew, "ep", scatter_dimension=0, tiled=True),
        lax.psum_scatter(grad_outw, "ep", scatter_dimension=0, tiled=True),
        lax.psum_scatter(grad_gain_two, "ep", scatter_dimension=0, tiled=True),
        lax.psum_scatter(grad_router, "ep", scatter_dimension=0, tiled=True),
        lax.psum_scatter(grad_mix, "ep", scatter_dimension=0, tiled=True),
        lax.psum_scatter(grad_sgate, "ep", scatter_dimension=0, tiled=True),
        lax.psum_scatter(grad_sup, "ep", scatter_dimension=0, tiled=True),
        lax.psum_scatter(grad_sdown, "ep", scatter_dimension=0, tiled=True),
    )
    return (
        block_out,
        grad_tokens,
        summed[0],
        summed[1],
        summed[2],
        summed[3],
        summed[4],
        summed[5],
        summed[6],
        summed[7],
        summed[8],
        summed[9],
        summed[10],
        grad_egate,
        expert_up_gradient,
        grad_edown,
    )


def share_over_devices(weight, ep_count):
    rows, hidden = weight.shape
    pieces = weight.T.reshape(ep_count, hidden // ep_count, rows)
    moved = lax.all_to_all(pieces, "ep", split_axis=0, concat_axis=0, tiled=True)
    return moved.transpose(1, 0, 2).reshape(hidden // ep_count, ep_count * rows)


def share_back(grads, ep_count):
    units, width = grads.shape
    pieces = grads.reshape(units, ep_count, width // ep_count).transpose(1, 0, 2)
    moved = lax.all_to_all(pieces, "ep", split_axis=0, concat_axis=0, tiled=True)
    return moved.reshape(ep_count * units, width // ep_count).T


def dense_body(
    tokens,
    lengths,
    routes,
    attn_gain,
    w_query,
    w_key,
    w_value,
    w_out,
    ffn_gain,
    w_router,
    shared_mix,
    shared_gate,
    shared_up,
    shared_down,
    expert_gate,
    expert_up,
    expert_down,
    cotangent,
):
    everywhere = ("ep", "tp")
    rows_here, width = tokens.shape
    ep_count = lax.axis_size("ep")
    tp_count = lax.axis_size("tp")
    ep_index = lax.axis_index("ep")
    offset = ep_index * rows_here
    quarter = rows_here // tp_count
    first_row = lax.axis_index("tp") * quarter
    slot_here, slot_hidden = expert_gate.shape[0], expert_gate.shape[1]
    expert_count = w_router.shape[1]
    bf16, f32 = jnp.bfloat16, jnp.float32

    def my_rows(array):
        return lax.dynamic_slice_in_dim(array, first_row, quarter, 0)

    side_columns = jnp.concatenate(
        [attn_gain[:, None], ffn_gain[:, None], shared_mix[:, None], w_router], axis=1
    )
    side_columns = jnp.pad(side_columns, ((0, 0), (0, -side_columns.shape[1] % 128)))
    joined_weights = lax.all_gather(
        jnp.concatenate([w_query, w_key, w_value, side_columns], axis=1), "ep", axis=0, tiled=True
    )
    heads_width = w_query.shape[1]
    qkv_weight = joined_weights[:, : 3 * heads_width]
    side_weight = joined_weights[:, 3 * heads_width :]
    output_weight = lax.all_gather(w_out, "ep", axis=0, tiled=True)
    upstream_all = lax.all_gather(my_rows(cotangent), everywhere, axis=0, tiled=True)
    routes_all = lax.all_gather(my_rows(routes), everywhere, axis=0, tiled=True)
    gate_rows = share_over_devices(shared_gate, ep_count)
    up_rows = share_over_devices(shared_up, ep_count)
    down_rows = share_over_devices(shared_down, ep_count)
    gate_cat = jnp.concatenate([expert_gate.reshape(-1, width), gate_rows], axis=0)
    up_cat = jnp.concatenate([expert_up.reshape(-1, width), up_rows], axis=0)
    down_cat = jnp.concatenate([expert_down.reshape(-1, width), down_rows], axis=0)

    heads_here = heads_width // HD
    score_scale = HD ** (-0.5)
    first_norm_scale = side_weight[:, 0].astype(f32)
    second_norm_scale = side_weight[:, 1].astype(f32)
    mix_f = side_weight[:, 2].astype(f32)
    router_f = side_weight[:, 3 : 3 + expert_count].astype(f32)
    layer_input = tokens.astype(f32)
    normed_wide, norm_one = norm_forward(layer_input, first_norm_scale)
    normed_one = normed_wide.astype(bf16)
    query_at = offset + jnp.arange(rows_here, dtype=jnp.int32)
    key_at = offset - 2 * rows_here + jnp.arange(3 * rows_here, dtype=jnp.int32)
    query_seg, query_pos = sequence_info(lengths, query_at)
    key_seg, _ = sequence_info(lengths, key_at)
    cosine, sine = rope_tables(query_pos, HD)
    projected = jnp.dot(normed_one, qkv_weight, preferred_element_type=f32)
    projected = projected.reshape(rows_here, 3, heads_here, HD)
    queries = rotate(projected[:, 0], cosine, sine).astype(bf16)
    keys = rotate(projected[:, 1], cosine, sine).astype(bf16)
    values = projected[:, 2].astype(bf16)
    carried = jnp.stack([keys, values], axis=0)
    joined = jnp.concatenate(
        [passed_along(carried, "ep", 2), passed_along(carried, "ep", 1), carried], axis=1
    )
    keys_win = joined[0]
    values_win = joined[1]
    allowed = (
        (query_seg[:, None] == key_seg[None, :])
        & (key_at[None, :] <= query_at[:, None])
        & (key_at[None, :] >= 0)
    )
    scores = (
        jnp.einsum("qhd,khd->hqk", queries, keys_win, preferred_element_type=f32) * score_scale
    )
    masked = jnp.where(allowed[None], scores, -1e30)
    peak = jnp.max(masked, axis=-1, keepdims=True)
    expo = jnp.exp(masked - peak)
    total = jnp.sum(expo, axis=-1, keepdims=True)
    log_total = peak + jnp.log(total)
    weights = expo / total
    attended = jnp.einsum(
        "hqk,khd->qhd", weights.astype(bf16), values_win, preferred_element_type=f32
    )
    attended = attended.reshape(rows_here, heads_width).astype(bf16)
    attn_part = jnp.einsum("th,dh->td", attended, output_weight, preferred_element_type=f32)
    attn_sum = lax.psum_scatter(attn_part.astype(bf16), "tp", scatter_dimension=0, tiled=True)
    resid = my_rows(layer_input) + attn_sum.astype(f32)
    normed_two_wide, norm_two = norm_forward(resid, second_norm_scale)
    normed_two = normed_two_wide.astype(bf16)

    normed_all = lax.all_gather(normed_two, everywhere, axis=0, tiled=True)
    logits_all = jnp.dot(normed_all, side_weight, preferred_element_type=f32)
    router_all = jax.nn.softmax(logits_all[:, 3 : 3 + expert_count], axis=-1)
    mixer_all = jax.nn.sigmoid(logits_all[:, 2])
    slots = ep_index * slot_here + jnp.arange(slot_here, dtype=jnp.int32)
    own_slot = slots[:, None] == jnp.arange(expert_count, dtype=jnp.int32)[None, :]
    picked_all = jnp.any(
        routes_all[:, :, None] == jnp.arange(expert_count, dtype=jnp.int32), axis=1
    )
    routed_all = jnp.where(picked_all, router_all, 0.0)
    slot_gates = jnp.sum(jnp.where(own_slot[None], routed_all[:, None, :], 0.0), axis=-1)
    shared_units = gate_rows.shape[0]
    gates = jnp.concatenate(
        [
            jnp.repeat(slot_gates, slot_hidden, axis=1, total_repeat_length=slot_here * slot_hidden),
            jnp.broadcast_to(mixer_all[:, None], (mixer_all.shape[0], shared_units)),
        ],
        axis=1,
    )
    gate_pre = jnp.einsum("td,fd->tf", normed_all, gate_cat, preferred_element_type=f32)
    up_pre = jnp.einsum("td,fd->tf", normed_all, up_cat, preferred_element_type=f32)
    d_hidden = jnp.einsum("td,fd->tf", upstream_all, down_cat, preferred_element_type=f32)
    sig = jax.nn.sigmoid(gate_pre)
    hidden = gate_pre * sig * up_pre
    weighted_h = (gates * hidden).astype(bf16)
    gated = gates * d_hidden
    d_gate_pre = (gated * up_pre * sig * (1.0 + gate_pre * (1.0 - sig))).astype(bf16)
    d_up_pre = (gated * gate_pre * sig).astype(bf16)
    dots = hidden * d_hidden
    routed_units = slot_here * slot_hidden
    slot_dots = jnp.sum(dots[:, :routed_units].reshape(-1, slot_here, slot_hidden), axis=-1)
    mix_dots = jnp.sum(dots[:, routed_units:], axis=-1)
    gate_dots = jnp.sum(jnp.where(own_slot[None], slot_dots[:, :, None], 0.0), axis=1)
    dots_part = jnp.concatenate([gate_dots, mix_dots[:, None]], axis=1)
    ffn_part = jnp.dot(weighted_h, down_cat, preferred_element_type=f32).astype(bf16)
    d_normed_part = (
        jnp.dot(d_gate_pre, gate_cat, preferred_element_type=f32)
        + jnp.dot(d_up_pre, up_cat, preferred_element_type=f32)
    ).astype(bf16)
    ffn_sum = lax.psum_scatter(ffn_part, everywhere, scatter_dimension=0, tiled=True)
    d_normed_sum = lax.psum_scatter(d_normed_part, everywhere, scatter_dimension=0, tiled=True)
    dots_sum = lax.psum_scatter(dots_part, everywhere, scatter_dimension=0, tiled=True)
    grad_gate_cat = jnp.einsum("tf,td->fd", d_gate_pre, normed_all, preferred_element_type=f32)
    grad_up_cat = jnp.einsum("tf,td->fd", d_up_pre, normed_all, preferred_element_type=f32)
    grad_down_cat = jnp.einsum("tf,td->fd", weighted_h, upstream_all, preferred_element_type=f32)
    grad_shared = [
        share_back(grad[routed_units:].astype(bf16), ep_count).astype(f32)
        for grad in (grad_gate_cat, grad_up_cat, grad_down_cat)
    ]
    grad_experts = [
        grad[:routed_units].reshape(expert_gate.shape)
        for grad in (grad_gate_cat, grad_up_cat, grad_down_cat)
    ]

    block_out = lax.all_gather(
        (resid + ffn_sum.astype(f32)).astype(bf16), "tp", axis=0, tiled=True
    )
    here = offset + first_row
    router = lax.dynamic_slice_in_dim(router_all, here, quarter, 0)
    picked = lax.dynamic_slice_in_dim(picked_all, here, quarter, 0)
    mixer = lax.dynamic_slice_in_dim(mixer_all, here, quarter, 0)
    d_router = jnp.where(picked, dots_sum[:, :expert_count], 0.0)
    d_mixer = dots_sum[:, expert_count]
    d_logits = router * (d_router - jnp.sum(router * d_router, axis=-1, keepdims=True))
    d_mixlogit = d_mixer * mixer * (1.0 - mixer)
    side = jnp.dot(d_logits, router_f.T, precision=highest) + d_mixlogit[:, None] * mix_f[None, :]
    normed_two_f = normed_two.astype(f32)
    d_side = jnp.concatenate([d_mixlogit[:, None], d_logits], axis=1)
    grad_side = jnp.dot(normed_two_f.T, d_side, precision=highest)
    upstream = my_rows(cotangent).astype(f32)
    d_normed_two = d_normed_sum.astype(f32) + side
    d_resid_norm, grad_gain_two = norm_backward(resid, norm_two, second_norm_scale, d_normed_two)
    d_resid = upstream + d_resid_norm
    d_resid_low = lax.all_gather(d_resid.astype(bf16), "tp", axis=0, tiled=True)
    grad_outw = jnp.einsum("td,th->dh", d_resid_low, attended, preferred_element_type=f32)
    d_attended = jnp.einsum("td,dh->th", d_resid_low, output_weight, preferred_element_type=f32)
    d_attended = d_attended.astype(bf16).reshape(rows_here, heads_here, HD)
    scores_again = (
        jnp.einsum("qhd,khd->hqk", queries, keys_win, preferred_element_type=f32) * score_scale
    )
    probs = jnp.where(allowed[None], jnp.exp(scores_again - log_total), 0.0)
    d_probs = jnp.einsum("qhd,khd->hqk", d_attended, values_win, preferred_element_type=f32)
    delta = jnp.sum(probs * d_probs, axis=-1, keepdims=True)
    d_scores = (probs * (d_probs - delta)).astype(bf16)
    d_keys_win = (
        jnp.einsum("hqk,qhd->khd", d_scores, queries, preferred_element_type=f32) * score_scale
    )
    d_values_win = jnp.einsum(
        "hqk,qhd->khd", probs.astype(bf16), d_attended, preferred_element_type=f32
    )
    pair_grads = jnp.stack([d_keys_win, d_values_win], axis=0)
    passed = pair_grads[:, : 2 * rows_here].astype(bf16)
    from_two = passed_along(passed[:, :rows_here], "ep", -2)
    from_one = passed_along(passed[:, rows_here:], "ep", -1)
    d_queries = (
        jnp.einsum("hqk,khd->qhd", d_scores, keys_win, preferred_element_type=f32) * score_scale
    )
    running = pair_grads[:, 2 * rows_here :] + from_one.astype(f32) + from_two.astype(f32)
    d_projected = jnp.concatenate(
        [
            unrotate(d_queries, cosine, sine).astype(bf16).reshape(rows_here, heads_width),
            unrotate(running[0], cosine, sine).astype(bf16).reshape(rows_here, heads_width),
            running[1].astype(bf16).reshape(rows_here, heads_width),
        ],
        axis=1,
    )
    d_normed_one = jnp.einsum("th,dh->td", d_projected, qkv_weight, preferred_element_type=f32)
    d_normed_one = lax.psum_scatter(
        d_normed_one.astype(bf16), "tp", scatter_dimension=0, tiled=True
    ).astype(f32)
    grad_qkv = jnp.einsum("td,th->dh", normed_one, d_projected, preferred_element_type=f32)
    d_input_norm, grad_gain_one = norm_backward(
        my_rows(layer_input), my_rows(norm_one), first_norm_scale, d_normed_one
    )
    grad_tokens = lax.all_gather(
        (d_resid + d_input_norm).astype(bf16), "tp", axis=0, tiled=True
    ).astype(f32)
    grad_weights = lax.psum_scatter(
        jnp.concatenate([grad_qkv, grad_outw], axis=1).astype(bf16),
        "ep",
        scatter_dimension=0,
        tiled=True,
    ).astype(f32)
    small = jnp.concatenate([grad_gain_one[:, None], grad_gain_two[:, None], grad_side], axis=1)
    small = lax.psum(lax.psum_scatter(small, "ep", scatter_dimension=0, tiled=True), "tp")
    parts = [grad_weights[:, i * heads_width : (i + 1) * heads_width] for i in range(4)]
    return (
        block_out,
        grad_tokens,
        small[:, 0],
        parts[0],
        parts[1],
        parts[2],
        parts[3],
        small[:, 1],
        small[:, 3:],
        small[:, 2],
        grad_shared[0],
        grad_shared[1],
        grad_shared[2],
        grad_experts[0],
        grad_experts[1],
        grad_experts[2],
    )


def chosen_body(*arrays):
    rows_here, top_count = arrays[2].shape
    slot_here, expert_count = arrays[14].shape[0], arrays[9].shape[1]
    capacity = rows_here * top_count * 7 // (5 * expert_count)
    if rows_here < 2 * slot_here * capacity:
        return dense_body(*arrays)
    return body(*arrays)


def solution(mesh):
    placed = (
        P("ep", None),
        P(),
        P("ep", None),
        P("ep"),
        P("ep", "tp"),
        P("ep", "tp"),
        P("ep", "tp"),
        P("ep", "tp"),
        P("ep"),
        P("ep", None),
        P("ep"),
        P("ep", "tp"),
        P("ep", "tp"),
        P("ep", "tp"),
        P("ep", "tp", None),
        P("ep", "tp", None),
        P("ep", "tp", None),
        P("ep", None),
    )
    return jax.shard_map(
        chosen_body,
        mesh=mesh,
        in_specs=placed,
        out_specs=(
            P("ep", None),
            P("ep", None),
            P("ep"),
            P("ep", "tp"),
            P("ep", "tp"),
            P("ep", "tp"),
            P("ep", "tp"),
            P("ep"),
            P("ep", None),
            P("ep"),
            P("ep", "tp"),
            P("ep", "tp"),
            P("ep", "tp"),
            P("ep", "tp", None),
            P("ep", "tp", None),
            P("ep", "tp", None),
        ),
        check_vma=False,
    )
```

```python
import functools

import jax
import jax.numpy as jnp
from jax import lax
from jax.experimental import pallas as pl
from jax.experimental.pallas import tpu as pltpu
from jax.sharding import PartitionSpec as P

HD = 128


epsilon = 1e-06
rope_base = 1000000.0
highest = lax.Precision.HIGHEST
MESH = pl.DeviceIdType.MESH


def passed_along(block, axis, distance):
    devices = range(lax.axis_size(axis))
    route = [(i - distance, i) for i in devices if i - distance in devices]
    return lax.ppermute(block, axis, route)


def rope_tables(positions, width):
    steps = jnp.arange(0, width, 2, dtype=jnp.float32) / width
    inverse = rope_base ** (-steps)
    angles = positions.astype(jnp.float32)[:, None] * inverse[None, :]
    angles = jnp.concatenate([angles, angles], axis=-1)
    return (jnp.cos(angles)[:, None, :], jnp.sin(angles)[:, None, :])


def turn_half(values):
    middle = values.shape[-1] // 2
    return jnp.concatenate([-values[..., middle:], values[..., :middle]], axis=-1)


def rotate(values, cosine, sine):
    return values * cosine + turn_half(values) * sine


def unrotate(grads, cosine, sine):
    return grads * cosine - turn_half(grads * sine)


def sequence_info(lengths, indices):
    starts = jnp.cumsum(lengths) - lengths
    inside = starts[None, :] <= indices[:, None]
    segment = jnp.sum(inside.astype(jnp.int32), axis=1) - 1
    first = jnp.max(jnp.where(inside, starts[None, :], -1), axis=1)
    return (segment, indices - first)


def norm_forward(values, gain):
    scale = lax.rsqrt(jnp.mean(values * values, axis=-1, keepdims=True) + epsilon)
    return (values * scale * gain, scale)


def norm_backward(values, scale, gain, grads):
    unit = values * scale
    scaled = grads * gain
    inner = jnp.mean(scaled * unit, axis=-1, keepdims=True)
    return (scale * (scaled - unit * inner), jnp.sum(grads * unit, axis=0))


def deliver(rows):
    arrived_rows = lax.all_to_all(rows, "ep", split_axis=0, concat_axis=0, tiled=True)
    return arrived_rows


def bring_back(parts, target, rows_here, top_count):
    moved = lax.all_to_all(parts, "ep", split_axis=0, concat_axis=0, tiled=True)
    piece = moved.shape[3]
    return moved.reshape(-1, piece)[target].reshape(rows_here, top_count, piece)


def body(
    tokens,
    lengths,
    routes,
    attn_gain,
    w_query,
    w_key,
    w_value,
    w_out,
    ffn_gain,
    w_router,
    shared_mix,
    shared_gate,
    shared_up,
    shared_down,
    expert_gate,
    expert_up,
    expert_down,
    cotangent,
):
    rows_here = tokens.shape[0]
    width = tokens.shape[1]
    ep_count = lax.axis_size("ep")
    offset = lax.axis_index("ep") * rows_here
    slot_here = expert_gate.shape[0]
    top_count = routes.shape[1]
    gathered = (
        lax.all_gather(attn_gain, "ep", axis=0, tiled=True),
        lax.all_gather(w_query, "ep", axis=0, tiled=True),
        lax.all_gather(w_key, "ep", axis=0, tiled=True),
        lax.all_gather(w_value, "ep", axis=0, tiled=True),
        lax.all_gather(w_out, "ep", axis=0, tiled=True),
        lax.all_gather(ffn_gain, "ep", axis=0, tiled=True),
        lax.all_gather(w_router, "ep", axis=0, tiled=True),
        lax.all_gather(shared_mix, "ep", axis=0, tiled=True),
        lax.all_gather(shared_gate, "ep", axis=0, tiled=True),
        lax.all_gather(shared_up, "ep", axis=0, tiled=True),
        lax.all_gather(shared_down, "ep", axis=0, tiled=True),
    )
    (
        gain_first,
        query_weight_matrix,
        key_weight_matrix,
        value_weight_matrix,
        output_weight,
        gain_second,
        router_weight,
        shared_mixer_weight,
        shared_gate_weight,
        shared_up_weight,
        shared_down_weight,
    ) = gathered
    expert_count = router_weight.shape[1]
    capacity = (rows_here * top_count * 7 // (5 * expert_count) + 7) // 8 * 8
    heads_here = query_weight_matrix.shape[1] // HD
    score_scale = HD ** (-0.5)
    first_norm_scale = gain_first.astype(jnp.float32)
    second_norm_scale = gain_second.astype(jnp.float32)
    layer_input = tokens.astype(jnp.float32)
    normed_wide, norm_one = norm_forward(layer_input, first_norm_scale)
    normed_one = normed_wide.astype(jnp.bfloat16)
    query_at = offset + jnp.arange(rows_here, dtype=jnp.int32)
    key_at = offset - 2 * rows_here + jnp.arange(3 * rows_here, dtype=jnp.int32)
    query_seg, query_pos = sequence_info(lengths, query_at)
    key_seg, _ = sequence_info(lengths, key_at)
    cosine, sine = rope_tables(query_pos, HD)
    query_pre = jnp.dot(
        normed_one, query_weight_matrix, preferred_element_type=jnp.float32
    ).reshape(rows_here, heads_here, HD)
    key_pre = jnp.dot(normed_one, key_weight_matrix, preferred_element_type=jnp.float32).reshape(
        rows_here, heads_here, HD
    )
    queries = rotate(query_pre, cosine, sine).astype(jnp.bfloat16)
    keys = rotate(key_pre, cosine, sine).astype(jnp.bfloat16)
    values = (
        jnp.dot(normed_one, value_weight_matrix, preferred_element_type=jnp.float32)
        .astype(jnp.bfloat16)
        .reshape(rows_here, heads_here, HD)
    )
    carried = jnp.stack([keys, values], axis=0)
    window = [carried]
    for hop in range(2):
        carried = passed_along(carried, "ep", 1)
        window = [carried] + window
    joined = jnp.concatenate(window, axis=1)
    keys_win = joined[0]
    values_win = joined[1]
    allowed = (
        (query_seg[:, None] == key_seg[None, :])
        & (key_at[None, :] <= query_at[:, None])
        & (key_at[None, :] >= 0)
    )
    scores = (
        jnp.einsum("qhd,khd->hqk", queries, keys_win, preferred_element_type=jnp.float32)
        * score_scale
    )
    masked = jnp.where(allowed[None], scores, -1e30)
    peak = jnp.max(masked, axis=-1, keepdims=True)
    expo = jnp.exp(masked - peak)
    total = jnp.sum(expo, axis=-1, keepdims=True)
    log_total = peak + jnp.log(total)
    weights = expo / total
    attended = jnp.einsum(
        "hqk,khd->qhd", weights.astype(jnp.bfloat16), values_win, preferred_element_type=jnp.float32
    )
    attended = attended.reshape(rows_here, heads_here * HD).astype(jnp.bfloat16)
    attn_part = jnp.einsum("th,dh->td", attended, output_weight, preferred_element_type=jnp.float32)
    resid = layer_input + lax.psum(attn_part, "tp")
    normed_two_wide, norm_two = norm_forward(resid, second_norm_scale)
    normed_two = normed_two_wide.astype(jnp.bfloat16)
    normed_two_f = normed_two.astype(jnp.float32)
    router_f = router_weight.astype(jnp.float32)
    mix_f = shared_mixer_weight.astype(jnp.float32)
    router = jax.nn.softmax(jnp.dot(normed_two_f, router_f, precision=highest), axis=-1)
    picked = routes[:, :, None] == jnp.arange(expert_count, dtype=jnp.int32)[None, None, :]
    gates = jnp.sum(jnp.where(picked, router[:, None, :], 0.0), axis=-1)
    mixer = jax.nn.sigmoid(jnp.dot(normed_two_f, mix_f, precision=highest))
    shared_g = jnp.dot(normed_two, shared_gate_weight, preferred_element_type=jnp.float32)
    shared_u = jnp.dot(normed_two, shared_up_weight, preferred_element_type=jnp.float32)
    shared_h = (jax.nn.silu(shared_g) * shared_u).astype(jnp.bfloat16)
    shared_part = jnp.einsum(
        "tf,df->td", shared_h, shared_down_weight, preferred_element_type=jnp.float32
    )
    flat = routes.reshape(-1)
    hot = (flat[:, None] == jnp.arange(expert_count, dtype=jnp.int32)[None, :]).astype(jnp.int32)
    rank = jnp.sum(jnp.cumsum(hot, axis=0) * hot, axis=1) - 1
    target = flat * capacity + rank
    slot_total = ep_count * slot_here * capacity
    owner_route = (
        jnp.zeros((slot_total,), jnp.int32)
        .at[target]
        .set(jnp.arange(rows_here * top_count, dtype=jnp.int32))
    )
    filled = jnp.zeros((slot_total,), jnp.bool_).at[target].set(True)
    owner_token = owner_route // top_count
    send_rows = jnp.where(filled[:, None], normed_two[owner_token], jnp.zeros((), jnp.bfloat16))
    arrived_rows = deliver(send_rows.reshape(ep_count, slot_here, capacity, width))
    route_g = jnp.einsum(
        "nscd,sfd->nscf", arrived_rows, expert_gate, preferred_element_type=jnp.float32
    )
    route_u = jnp.einsum(
        "nscd,sfd->nscf", arrived_rows, expert_up, preferred_element_type=jnp.float32
    )
    route_h = (jax.nn.silu(route_g) * route_u).astype(jnp.bfloat16)
    route_part = jnp.einsum(
        "nscf,sfd->nscd", route_h, expert_down, preferred_element_type=jnp.float32
    )
    back_rows = bring_back(route_part, target, rows_here, top_count)
    upstream = cotangent.astype(jnp.float32)
    routed = jnp.sum(back_rows * gates[:, :, None], axis=1)
    ffn_part = mixer[:, None] * shared_part + routed
    route_dot = jnp.sum(back_rows * upstream[:, None, :], axis=-1)
    shared_dot = jnp.sum(shared_part * upstream, axis=-1)
    ffn_total, d_gate, d_mixer = lax.psum((ffn_part, route_dot, shared_dot), "tp")
    block_out = (resid + ffn_total).astype(jnp.bfloat16)
    d_router = jnp.sum(jnp.where(picked, d_gate[:, :, None], 0.0), axis=1)
    d_logits = router * (d_router - jnp.sum(router * d_router, axis=-1, keepdims=True))
    d_mixlogit = d_mixer * mixer * (1.0 - mixer)
    side = jnp.dot(d_logits, router_f.T, precision=highest) + d_mixlogit[:, None] * mix_f[None, :]
    grad_router = jnp.dot(normed_two_f.T, d_logits, precision=highest)
    grad_mix = jnp.dot(d_mixlogit, normed_two_f, precision=highest)
    d_shared = (mixer[:, None] * upstream).astype(jnp.bfloat16)
    d_sh = jnp.dot(d_shared, shared_down_weight, preferred_element_type=jnp.float32)
    sig_shared = jax.nn.sigmoid(shared_g)
    d_sg = (d_sh * shared_u * sig_shared * (1.0 + shared_g * (1.0 - sig_shared))).astype(
        jnp.bfloat16
    )
    d_su = (d_sh * shared_g * sig_shared).astype(jnp.bfloat16)
    d_normed_part = jnp.einsum(
        "tf,df->td", d_sg, shared_gate_weight, preferred_element_type=jnp.float32
    )
    d_normed_part = d_normed_part + jnp.einsum(
        "tf,df->td", d_su, shared_up_weight, preferred_element_type=jnp.float32
    )
    grad_sgate = jnp.einsum("td,tf->df", normed_two, d_sg, preferred_element_type=jnp.float32)
    grad_sup = jnp.einsum("td,tf->df", normed_two, d_su, preferred_element_type=jnp.float32)
    grad_sdown = jnp.einsum("td,tf->df", d_shared, shared_h, preferred_element_type=jnp.float32)
    d_route = (
        (gates[:, :, None] * upstream[:, None, :])
        .astype(jnp.bfloat16)
        .reshape(rows_here * top_count, width)
    )
    send_grads = jnp.where(filled[:, None], d_route[owner_route], jnp.zeros((), jnp.bfloat16))
    received_grads = deliver(send_grads.reshape(ep_count, slot_here, capacity, width))
    d_rh = jnp.einsum(
        "nscd,sfd->nscf", received_grads, expert_down, preferred_element_type=jnp.float32
    )
    sig_route = jax.nn.sigmoid(route_g)
    d_rg = (d_rh * route_u * sig_route * (1.0 + route_g * (1.0 - sig_route))).astype(jnp.bfloat16)
    routed_up_gradient = (d_rh * route_g * sig_route).astype(jnp.bfloat16)
    row_grads = jnp.einsum("nscf,sfd->nscd", d_rg, expert_gate, preferred_element_type=jnp.float32)
    row_grads = row_grads + jnp.einsum(
        "nscf,sfd->nscd", routed_up_gradient, expert_up, preferred_element_type=jnp.float32
    )
    grad_egate = jnp.einsum(
        "qxba,qxbr->xar", d_rg, arrived_rows, preferred_element_type=jnp.float32
    )
    expert_up_gradient = jnp.einsum(
        "qxba,qxbr->xar", routed_up_gradient, arrived_rows, preferred_element_type=jnp.float32
    )
    grad_edown = jnp.einsum(
        "qxba,qxbr->xar", route_h, received_grads, preferred_element_type=jnp.float32
    )
    grads_back = bring_back(row_grads, target, rows_here, top_count)
    d_routed = jnp.sum(grads_back, axis=1)
    d_normed_two = lax.psum(d_normed_part + d_routed, "tp") + side
    d_resid_norm, grad_gain_two = norm_backward(resid, norm_two, second_norm_scale, d_normed_two)
    d_resid = upstream + d_resid_norm
    d_resid_low = d_resid.astype(jnp.bfloat16)
    grad_outw = jnp.einsum("td,th->dh", d_resid_low, attended, preferred_element_type=jnp.float32)
    d_attended = jnp.einsum(
        "td,dh->th", d_resid_low, output_weight, preferred_element_type=jnp.float32
    )
    d_attended = d_attended.astype(jnp.bfloat16).reshape(rows_here, heads_here, HD)
    scores_again = (
        jnp.einsum("qhd,khd->hqk", queries, keys_win, preferred_element_type=jnp.float32)
        * score_scale
    )
    probs = jnp.where(allowed[None], jnp.exp(scores_again - log_total), 0.0)
    d_probs = jnp.einsum("qhd,khd->hqk", d_attended, values_win, preferred_element_type=jnp.float32)
    delta = jnp.sum(probs * d_probs, axis=-1, keepdims=True)
    d_scores = (probs * (d_probs - delta)).astype(jnp.bfloat16)
    d_queries = (
        jnp.einsum("hqk,khd->qhd", d_scores, keys_win, preferred_element_type=jnp.float32)
        * score_scale
    )
    d_keys_win = (
        jnp.einsum("hqk,qhd->khd", d_scores, queries, preferred_element_type=jnp.float32)
        * score_scale
    )
    d_values_win = jnp.einsum(
        "hqk,qhd->khd", probs.astype(jnp.bfloat16), d_attended, preferred_element_type=jnp.float32
    )
    pair_grads = jnp.stack([d_keys_win, d_values_win], axis=0)
    older = pair_grads[:, :rows_here]
    later = [pair_grads[:, rows_here : 2 * rows_here], pair_grads[:, 2 * rows_here :]]
    running = older
    for hop in range(2):
        running = passed_along(running, "ep", -1)
        running = running + later[hop]
    d_query_pre = (
        unrotate(d_queries, cosine, sine).astype(jnp.bfloat16).reshape(rows_here, heads_here * HD)
    )
    d_key_pre = (
        unrotate(running[0], cosine, sine).astype(jnp.bfloat16).reshape(rows_here, heads_here * HD)
    )
    d_values = running[1].astype(jnp.bfloat16).reshape(rows_here, heads_here * HD)
    grad_queryw = jnp.einsum(
        "td,th->dh", normed_one, d_query_pre, preferred_element_type=jnp.float32
    )
    grad_keyw = jnp.einsum("td,th->dh", normed_one, d_key_pre, preferred_element_type=jnp.float32)
    grad_valuew = jnp.einsum("td,th->dh", normed_one, d_values, preferred_element_type=jnp.float32)
    d_normed_one = jnp.einsum(
        "th,dh->td", d_query_pre, query_weight_matrix, preferred_element_type=jnp.float32
    )
    d_normed_one = d_normed_one + jnp.einsum(
        "th,dh->td", d_key_pre, key_weight_matrix, preferred_element_type=jnp.float32
    )
    d_normed_one = d_normed_one + jnp.einsum(
        "th,dh->td", d_values, value_weight_matrix, preferred_element_type=jnp.float32
    )
    d_normed_one = lax.psum(d_normed_one, "tp")
    d_input_norm, grad_gain_one = norm_backward(
        layer_input, norm_one, first_norm_scale, d_normed_one
    )
    grad_tokens = d_resid + d_input_norm
    summed = (
        lax.psum_scatter(grad_gain_one, "ep", scatter_dimension=0, tiled=True),
        lax.psum_scatter(grad_queryw, "ep", scatter_dimension=0, tiled=True),
        lax.psum_scatter(grad_keyw, "ep", scatter_dimension=0, tiled=True),
        lax.psum_scatter(grad_valuew, "ep", scatter_dimension=0, tiled=True),
        lax.psum_scatter(grad_outw, "ep", scatter_dimension=0, tiled=True),
        lax.psum_scatter(grad_gain_two, "ep", scatter_dimension=0, tiled=True),
        lax.psum_scatter(grad_router, "ep", scatter_dimension=0, tiled=True),
        lax.psum_scatter(grad_mix, "ep", scatter_dimension=0, tiled=True),
        lax.psum_scatter(grad_sgate, "ep", scatter_dimension=0, tiled=True),
        lax.psum_scatter(grad_sup, "ep", scatter_dimension=0, tiled=True),
        lax.psum_scatter(grad_sdown, "ep", scatter_dimension=0, tiled=True),
    )
    return (
        block_out,
        grad_tokens,
        summed[0],
        summed[1],
        summed[2],
        summed[3],
        summed[4],
        summed[5],
        summed[6],
        summed[7],
        summed[8],
        summed[9],
        summed[10],
        grad_egate,
        expert_up_gradient,
        grad_edown,
    )


class Place:
    def __init__(self):
        self.ep, self.tp = lax.axis_index("ep"), lax.axis_index("tp")
        self.z, self.y = self.ep // 2, self.ep % 2
        self.x, self.c = self.tp // 2, self.tp % 2
        self.depth = lax.axis_size("ep") // 2
        self.next_core = (self.ep, self.x * 2 + 1 - self.c)
        self.next_x = (self.ep, (1 - self.x) * 2 + self.c)
        self.next_y = (self.z * 2 + 1 - self.y, self.tp)

    def at_z(self, z):
        return (z * 2 + self.y, self.tp)

    def ahead(self, steps):
        return lax.rem(self.z + steps, self.depth)

    def behind(self, steps):
        return lax.rem(self.z + self.depth - steps, self.depth)

    def greet(self):
        barrier = pltpu.get_barrier_semaphore()
        peers = [self.next_core, self.next_x, self.next_y]
        peers += [self.at_z(self.ahead(k)) for k in range(1, self.depth)]
        for peer in peers:
            pl.semaphore_signal(barrier, inc=1, device_id=peer, device_id_type=MESH)
        pl.semaphore_wait(barrier, len(peers))


def remote(src, dst, send, recv, peer):
    return pltpu.make_async_remote_copy(
        src_ref=src, dst_ref=dst, send_sem=send, recv_sem=recv, device_id=peer, device_id_type=MESH
    )


def ffn_kernel(
    units,
    expert_count,
    rows_in,
    upstream_in,
    gate_in,
    up_in,
    down_in,
    side_in,
    rows_all,
    out_part,
    d_rows_part,
    weighted_out,
    d_gate_out,
    d_up_out,
    gate_w,
    up_w,
    down_w,
    side_w,
    rows_tile,
    upstream_tile,
    out_tile,
    d_rows_tile,
    weighted_tile,
    d_gate_tile,
    d_up_tile,
    weight_sem,
    own_sem,
    z_send,
    z_recv,
    plane_send,
    plane_recv,
    load_sem,
    store_sem,
):
    at = Place()
    depth = at.depth
    quarter = rows_in.shape[0]
    width = rows_in.shape[1]
    half = quarter // 2
    own, other_x = at.tp, (1 - at.x) * 2 + at.c

    def weight_copies():
        pairs = ((gate_in, gate_w), (up_in, up_w), (down_in, down_w), (side_in, side_w))
        return [
            pltpu.make_async_copy(src, dst, weight_sem.at[i]) for i, (src, dst) in enumerate(pairs)
        ]

    for copy in weight_copies():
        copy.start()

    def block(j, y, tp):
        return rows_all.at[at.behind(j), y, tp]

    def plane_copy(j, kind):
        y, other_y = at.y, 1 - at.y
        if kind == 0:
            src, peer = block(j, y, own), at.next_x
        elif kind == 1:
            src, peer = block(j, y, own), at.next_y
        elif kind == 2:
            src, peer = block(j, y, other_x).at[pl.ds(0, half)], at.next_y
        elif kind == 3:
            src, peer = block(j, other_y, own).at[pl.ds(half, half)], at.next_x
        else:
            src = block(j, other_y if kind >= 6 else y, other_x if kind % 2 else own)
            peer = at.next_core
        return remote(src, src, plane_send.at[j, kind], plane_recv.at[j, kind], peer)

    def z_copy(k):
        return remote(
            rows_in, block(0, at.y, own), z_send.at[k - 1], z_recv.at[k - 1], at.at_z(at.ahead(k))
        )

    def z_arrival(k):
        dst = block(k, at.y, own)
        return remote(dst, dst, z_send.at[k - 1], z_recv.at[k - 1], at.at_z(at.behind(k)))

    def begin(j):
        for kind in (0, 1, 4):
            plane_copy(j, kind).start()

    def spread(j):
        plane_copy(j, 0).wait_recv()
        plane_copy(j, 2).start()
        plane_copy(j, 5).start()
        plane_copy(j, 1).wait_recv()
        plane_copy(j, 3).start()
        plane_copy(j, 6).start()

    def begin_later(j):
        z_arrival(j).wait_recv()
        begin(j)

    def last_hop(j):
        plane_copy(j, 2).wait_recv()
        plane_copy(j, 3).wait_recv()
        plane_copy(j, 7).start()

    def near_ready(j):
        plane_copy(j, 4).wait_recv()
        plane_copy(j, 5).wait_recv()

    def far_ready(j):
        plane_copy(j, 6).wait_recv()
        plane_copy(j, 7).wait_recv()

    def tile_at(step):
        j = step // 2
        return at.behind(j), lax.rem(at.y + lax.rem(step, 2), 2)

    def load_rows(step):
        z, y = tile_at(step)
        slot = lax.rem(step, 2)
        return pltpu.make_async_copy(rows_all.at[z, y], rows_tile.at[slot], load_sem.at[0, slot])

    def load_upstream(step):
        z, y = tile_at(step)
        slot = lax.rem(step, 2)
        return pltpu.make_async_copy(
            upstream_in.at[z, y], upstream_tile.at[slot], load_sem.at[1, slot]
        )

    def stores(step):
        z, y = tile_at(step)
        slot = lax.rem(step, 2)
        pairs = (
            (out_tile, out_part),
            (d_rows_tile, d_rows_part),
            (weighted_tile, weighted_out),
            (d_gate_tile, d_gate_out),
            (d_up_tile, d_up_out),
        )
        return [
            pltpu.make_async_copy(src.at[slot], dst.at[z, y], store_sem.at[i, slot])
            for i, (src, dst) in enumerate(pairs)
        ]

    load_upstream(0).start()
    at.greet()
    for k in range(1, depth):
        z_copy(k).start()
    own_copy = pltpu.make_async_copy(rows_in, block(0, at.y, own), own_sem)
    own_copy.start()
    own_copy.wait()
    begin(0)
    spread(0)
    begin_later(1)
    near_ready(0)
    load_rows(0).start()
    for copy in weight_copies():
        copy.wait()

    tile = rows_tile.shape[1] * rows_tile.shape[2]
    hidden_total = gate_w.shape[0]
    lane = lax.broadcasted_iota(jnp.int32, (tile, 128), 1)
    unit = lax.broadcasted_iota(jnp.int32, (1, hidden_total), 1)
    slot_here, slot_hidden, shared_hidden = units
    routed = slot_here * slot_hidden
    across = (((1,), (1,)), ((), ()))
    f32, bf16 = jnp.float32, jnp.bfloat16

    def step_body(step, carry):
        slot = lax.rem(step, 2)
        load_upstream(step).wait()

        @pl.when(step + 1 < 2 * depth)
        def _():
            load_upstream(step + 1).start()

        upstream = upstream_tile[slot].reshape(tile, upstream_tile.shape[-1])
        d_hidden = lax.dot_general(
            upstream[:, :width], down_w[...], across, preferred_element_type=f32
        )
        load_rows(step).wait()
        rows = rows_tile[slot].reshape(tile, width)
        logits = jnp.dot(rows, side_w[...], preferred_element_type=f32)
        chooses = (lane >= 3) & (lane < 3 + expert_count)
        peak = jnp.max(jnp.where(chooses, logits, -1e30), axis=1, keepdims=True)
        expo = jnp.where(chooses, jnp.exp(jnp.where(chooses, logits, peak) - peak), 0.0)
        router = expo / jnp.sum(expo, axis=1, keepdims=True)
        routed_gate = router * upstream[:, width:].astype(f32)
        mix_pre = jnp.sum(jnp.where(lane == 2, logits, 0.0), axis=1, keepdims=True)
        mixer = 1.0 / (1.0 + jnp.exp(-mix_pre))
        factor = jnp.where(unit < routed + shared_hidden, mixer, 0.0)
        for s in range(slot_here):
            chosen = lane == 3 + at.ep * slot_here + s
            gate = jnp.sum(jnp.where(chosen, routed_gate, 0.0), axis=1, keepdims=True)
            inside = (unit >= s * slot_hidden) & (unit < (s + 1) * slot_hidden)
            factor = jnp.where(inside, gate, factor)
        gate_pre = lax.dot_general(rows, gate_w[...], across, preferred_element_type=f32)
        up_pre = lax.dot_general(rows, up_w[...], across, preferred_element_type=f32)

        @pl.when(step >= 2)
        def _():
            for copy in stores(step - 2):
                copy.wait()

        sig = 1.0 / (1.0 + jnp.exp(-gate_pre))
        silu = gate_pre * sig
        hidden = silu * up_pre
        product = hidden * d_hidden
        gated = factor * d_hidden
        weighted_tile[slot] = (factor * hidden).astype(bf16)
        d_gate_tile[slot] = (gated * up_pre * (sig + silu * (1.0 - sig))).astype(bf16)
        d_up_tile[slot] = (gated * silu).astype(bf16)
        dots = jnp.zeros((tile, 128), f32)
        for s in range(slot_here + 1):
            last = s == slot_here
            inside = unit >= s * slot_hidden
            if not last:
                inside = inside & (unit < (s + 1) * slot_hidden)
            dot = jnp.sum(jnp.where(inside, product, 0.0), axis=1, keepdims=True)
            where = lane == (2 if last else 3 + at.ep * slot_here + s)
            dots = jnp.where(where, dot, dots)
        out = jnp.dot(weighted_tile[slot], down_w[...], preferred_element_type=f32)
        out_tile[slot, :, :, :width] = out.astype(bf16).reshape(rows_tile.shape[1:])
        out_tile[slot, :, :, width:] = dots.astype(bf16).reshape(rows_tile.shape[1:3] + (128,))
        d_rows = jnp.dot(d_gate_tile[slot], gate_w[...], preferred_element_type=f32)
        d_rows = d_rows + jnp.dot(d_up_tile[slot], up_w[...], preferred_element_type=f32)
        d_rows_tile[slot] = d_rows.astype(bf16).reshape(rows_tile.shape[1:])
        for copy in stores(step):
            copy.start()
        j = step // 2
        even = lax.rem(step, 2) == 0

        @pl.when(even)
        def _():
            last_hop(j)

            @pl.when(j + 1 < depth)
            def _():
                spread(j + 1)

            @pl.when(j + 2 < depth)
            def _():
                begin_later(j + 2)

            far_ready(j)
            load_rows(step + 1).start()

        @pl.when(jnp.logical_not(even) & (j + 1 < depth))
        def _():
            near_ready(j + 1)
            load_rows(step + 1).start()

        return carry

    lax.fori_loop(0, 2 * depth, step_body, 0)
    for step in (2 * depth - 2, 2 * depth - 1):
        for copy in stores(step):
            copy.wait()
    for k in range(1, depth):
        z_copy(k).wait_send()

    def finish(j, carry):
        for kind in range(8):
            plane_copy(j, kind).wait_send()
        return carry

    lax.fori_loop(0, depth, finish, 0)


def ffn_over_all(rows, upstream_all, gate_w, up_w, down_w, side_w, units, expert_count):
    quarter, width = rows.shape
    ep_count, tp_count = lax.axis_size("ep"), lax.axis_size("tp")
    depth = ep_count // 2
    hidden = gate_w.shape[0]
    bf16 = jnp.bfloat16
    upstream_all = upstream_all.reshape(depth, 2, tp_count, quarter, upstream_all.shape[-1])
    block = (depth, 2, tp_count, quarter)
    tile_rows = tp_count * quarter
    hidden_shape = jax.ShapeDtypeStruct((depth, 2, tile_rows, hidden), bf16)
    anywhere = pl.BlockSpec(memory_space=pl.ANY)
    tokens = ep_count * tile_rows
    outs = pl.pallas_call(
        functools.partial(ffn_kernel, units, expert_count),
        out_shape=(
            jax.ShapeDtypeStruct(block + (width,), bf16),
            jax.ShapeDtypeStruct(block + (width + 128,), bf16),
            jax.ShapeDtypeStruct(block + (width,), bf16),
            hidden_shape,
            hidden_shape,
            hidden_shape,
        ),
        in_specs=[anywhere] * 6,
        out_specs=(anywhere,) * 6,
        scratch_shapes=[
            pltpu.VMEM((hidden, width), bf16),
            pltpu.VMEM((hidden, width), bf16),
            pltpu.VMEM((hidden, width), bf16),
            pltpu.VMEM((width, 128), bf16),
            pltpu.VMEM((2, tp_count, quarter, width), bf16),
            pltpu.VMEM((2, tp_count, quarter, width + 128), bf16),
            pltpu.VMEM((2, tp_count, quarter, width + 128), bf16),
            pltpu.VMEM((2, tp_count, quarter, width), bf16),
            pltpu.VMEM((2, tile_rows, hidden), bf16),
            pltpu.VMEM((2, tile_rows, hidden), bf16),
            pltpu.VMEM((2, tile_rows, hidden), bf16),
            pltpu.SemaphoreType.DMA((4,)),
            pltpu.SemaphoreType.DMA,
            pltpu.SemaphoreType.DMA((depth - 1,)),
            pltpu.SemaphoreType.DMA((depth - 1,)),
            pltpu.SemaphoreType.DMA((depth, 8)),
            pltpu.SemaphoreType.DMA((depth, 8)),
            pltpu.SemaphoreType.DMA((2, 2)),
            pltpu.SemaphoreType.DMA((5, 2)),
        ],
        compiler_params=pltpu.CompilerParams(
            collective_id=1, has_side_effects=True, vmem_limit_bytes=60 * 2**20
        ),
        cost_estimate=pl.CostEstimate(
            flops=12 * tokens * width * hidden,
            bytes_accessed=10 * tokens * width,
            transcendentals=tokens * hidden,
        ),
        name="ffn_all_tokens",
    )(rows, upstream_all, gate_w, up_w, down_w, side_w)
    rows_all, out_part, d_rows_part, weighted, d_gate, d_up = outs
    return (
        rows_all.reshape(tokens, width),
        out_part,
        d_rows_part,
        weighted.reshape(tokens, hidden),
        d_gate.reshape(tokens, hidden),
        d_up.reshape(tokens, hidden),
    )


def sum_kernel(
    first_in,
    second_in,
    first_out,
    second_out,
    first_own,
    second_own,
    first_core,
    second_core,
    first_hop,
    second_hop,
    first_hop2,
    second_hop2,
    first_z,
    second_z,
    load_sem,
    send_sem,
    recv_sem,
):
    at = Place()
    depth = at.depth
    f32 = jnp.float32

    def to(j):
        return at.ahead(j)

    ins, owns = (first_in, second_in), (first_own, second_own)
    cores, hops = (first_core, second_core), (first_hop, second_hop)
    hops2, zs = (first_hop2, second_hop2), (first_z, second_z)

    def load(a, j):
        return pltpu.make_async_copy(
            ins[a].at[to(j), :, :, at.c], owns[a].at[j], load_sem.at[a, j]
        )

    def core_copy(a, j):
        return remote(
            ins[a].at[to(j), :, :, 1 - at.c],
            cores[a].at[j],
            send_sem.at[a, 0, j],
            recv_sem.at[a, 0, j],
            at.next_core,
        )

    def hop_copy(a, j):
        src = owns[0].at[j, :, 1 - at.x] if a == 0 else owns[1].at[j, 1 - at.y]
        peer = at.next_x if a == 0 else at.next_y
        return remote(src, hops[a].at[j], send_sem.at[a, 1, j], recv_sem.at[a, 1, j], peer)

    def hop2_copy(a, j):
        src = owns[0].at[j, 1 - at.y, at.x] if a == 0 else owns[1].at[j, at.y, 1 - at.x]
        peer = at.next_y if a == 0 else at.next_x
        return remote(src, hops2[a].at[j], send_sem.at[a, 2, j], recv_sem.at[a, 2, j], peer)

    def z_copy(a, j):
        return remote(
            owns[a].at[j, at.y, at.x],
            zs[a].at[j - 1],
            send_sem.at[a, 3, j],
            recv_sem.at[a, 3, j],
            at.at_z(to(j)),
        )

    def add(into, other):
        rows = into.shape[0]
        step = 32

        def body(i, carry):
            part = pl.ds(pl.multiple_of(i * step, step), step)
            into[part] = (into[part].astype(f32) + other[part].astype(f32)).astype(into.dtype)
            return carry

        lax.fori_loop(0, rows // step, body, 0)

    def after_core(a, j):
        load(a, j).wait()
        core_copy(a, j).wait_recv()

        def body(i, carry):
            moved, other = 1 - i // 2, lax.rem(i, 2)
            if a == 0:
                y, x = other, lax.rem(at.x + moved, 2)
            else:
                y, x = lax.rem(at.y + moved, 2), other
            add(owns[a].at[j, y, x], cores[a].at[j, y, x])
            return carry

        lax.fori_loop(0, 2, body, 0)
        hop_copy(a, j).start()
        lax.fori_loop(2, 4, body, 0)

    def after_hop(a, j):
        hop_copy(a, j).wait_recv()
        for moved in (1, 0):
            if a == 0:
                y = lax.rem(at.y + moved, 2)
                add(owns[0].at[j, y, at.x], hops[0].at[j, y])
            else:
                x = lax.rem(at.x + moved, 2)
                add(owns[1].at[j, at.y, x], hops[1].at[j, x])
            if moved:
                hop2_copy(a, j).start()

    def after_hop2(a, j):
        hop2_copy(a, j).wait_recv()
        add(owns[a].at[j, at.y, at.x], hops2[a].at[j])
        if j > 0:
            z_copy(a, j).start()

    order = [j for j in range(1, depth)] + [0]
    for j in order:
        for a in (0, 1):
            load(a, j).start()
    at.greet()
    for j in order:
        for a in (0, 1):
            core_copy(a, j).start()
    for turn in range(depth + 2):
        for a in (0, 1):
            if turn < depth:
                after_core(a, order[turn])
        for a in (0, 1):
            if 0 <= turn - 1 < depth:
                after_hop(a, order[turn - 1])
        for a in (0, 1):
            if 0 <= turn - 2 < depth:
                after_hop2(a, order[turn - 2])
    for a, out in ((0, first_out), (1, second_out)):
        for k in range(1, depth):
            z_copy(a, k).wait_recv()
        rows = out.shape[0]
        step = 32

        def body(i, carry):
            part = pl.ds(pl.multiple_of(i * step, step), step)
            total = owns[a][0, at.y, at.x, part].astype(f32)
            for k in range(depth - 1):
                total = total + zs[a][k, part].astype(f32)
            out[part] = total
            return carry

        lax.fori_loop(0, rows // step, body, 0)
    for a in (0, 1):
        for j in range(depth):
            core_copy(a, j).wait_send()
            hop_copy(a, j).wait_send()
            hop2_copy(a, j).wait_send()
            if j > 0:
                z_copy(a, j).wait_send()


def sum_over_all(first, second):
    depth, _, _, rows, _ = first.shape
    widths = (first.shape[-1], second.shape[-1])
    dtype = first.dtype

    def both(*lead):
        return [pltpu.VMEM(lead + (rows, w), dtype) for w in widths]

    anywhere = pl.BlockSpec(memory_space=pl.ANY)
    moved = depth * 4 * rows * sum(widths)
    return pl.pallas_call(
        sum_kernel,
        out_shape=tuple(jax.ShapeDtypeStruct((rows, w), jnp.float32) for w in widths),
        in_specs=[anywhere] * 2,
        out_specs=(pl.BlockSpec(memory_space=pltpu.VMEM),) * 2,
        scratch_shapes=both(depth, 2, 2)
        + both(depth, 2, 2)
        + both(depth, 2)
        + both(depth)
        + both(depth - 1)
        + [
            pltpu.SemaphoreType.DMA((2, depth)),
            pltpu.SemaphoreType.DMA((2, 4, depth)),
            pltpu.SemaphoreType.DMA((2, 4, depth)),
        ],
        compiler_params=pltpu.CompilerParams(
            collective_id=2, has_side_effects=True, vmem_limit_bytes=60 * 2**20
        ),
        cost_estimate=pl.CostEstimate(
            flops=2 * moved, bytes_accessed=12 * moved, transcendentals=0
        ),
        name="sum_all_devices",
    )(first.reshape(depth, 2, 2, 2, rows, widths[0]), second.reshape(depth, 2, 2, 2, rows, widths[1]))


def over_tp(block, distance):
    devices = range(lax.axis_size("tp"))
    return lax.ppermute(block, "tp", [(i, i ^ distance) for i in devices])


def one_of(array, index, axis):
    return lax.dynamic_index_in_dim(array, index, axis, keepdims=False)


def sum_over_tp(part):
    rows, columns = part.shape
    tp = lax.axis_index("tp")
    x, c = tp // 2, tp % 2
    blocks = part.reshape(2, 2, rows // 4, columns)
    got = over_tp(one_of(blocks, 1 - c, 1).astype(jnp.bfloat16), 1)
    chip = one_of(blocks, c, 1).astype(jnp.float32) + got.astype(jnp.float32)
    got = over_tp(one_of(chip, 1 - x, 0).astype(jnp.bfloat16), 2)
    return one_of(chip, x, 0) + got.astype(jnp.float32)


def gather_over_tp(block):
    tp = lax.axis_index("tp")
    x, c = tp // 2, tp % 2
    got = over_tp(block, 2)
    pair = jnp.where(x == 0, jnp.stack([block, got]), jnp.stack([got, block]))
    got = over_tp(pair, 1)
    four = jnp.where(c == 0, jnp.stack([pair, got], axis=1), jnp.stack([got, pair], axis=1))
    return four.reshape(4 * block.shape[0], block.shape[1])


def share_over_devices(weights, ep_count):
    rows, hidden = weights[0].shape
    units = hidden // ep_count
    pieces = jnp.concatenate(
        [weight.T.reshape(ep_count, units, rows) for weight in weights], axis=1
    )
    moved = lax.all_to_all(pieces, "ep", split_axis=0, concat_axis=0, tiled=True)
    moved = moved.transpose(1, 0, 2).reshape(len(weights), units, ep_count * rows)
    return [moved[i] for i in range(len(weights))]


def share_back(grads, ep_count):
    units, width = grads[0].shape
    columns = width // ep_count
    pieces = jnp.concatenate(grads, axis=0).reshape(len(grads) * units, ep_count, columns)
    moved = lax.all_to_all(
        pieces.transpose(1, 0, 2), "ep", split_axis=0, concat_axis=0, tiled=True
    )
    moved = moved.reshape(ep_count, len(grads), units, columns)
    return [moved[:, i].reshape(ep_count * units, columns).T for i in range(len(grads))]


def dense_body(
    tokens,
    lengths,
    routes,
    attn_gain,
    w_query,
    w_key,
    w_value,
    w_out,
    ffn_gain,
    w_router,
    shared_mix,
    shared_gate,
    shared_up,
    shared_down,
    expert_gate,
    expert_up,
    expert_down,
    cotangent,
):
    everywhere = ("ep", "tp")
    rows_here, width = tokens.shape
    ep_count = lax.axis_size("ep")
    tp_count = lax.axis_size("tp")
    ep_index = lax.axis_index("ep")
    offset = ep_index * rows_here
    quarter = rows_here // tp_count
    first_row = lax.axis_index("tp") * quarter
    slot_here, slot_hidden = expert_gate.shape[0], expert_gate.shape[1]
    expert_count = w_router.shape[1]
    bf16, f32 = jnp.bfloat16, jnp.float32

    def my_rows(array):
        return lax.dynamic_slice_in_dim(array, first_row, quarter, 0)

    side_columns = jnp.concatenate(
        [attn_gain[:, None], ffn_gain[:, None], shared_mix[:, None], w_router], axis=1
    )
    side_columns = jnp.pad(side_columns, ((0, 0), (0, -side_columns.shape[1] % 128)))
    joined_weights = lax.all_gather(
        jnp.concatenate([w_query, w_key, w_value, w_out, side_columns], axis=1),
        "ep",
        axis=0,
        tiled=True,
    )
    heads_width = w_query.shape[1]
    qkv_weight = joined_weights[:, : 3 * heads_width]
    output_weight = joined_weights[:, 3 * heads_width : 4 * heads_width]
    side_weight = joined_weights[:, 4 * heads_width :]
    picked = jnp.any(
        my_rows(routes)[:, :, None] == jnp.arange(expert_count, dtype=jnp.int32), axis=1
    )
    picked_lanes = jnp.pad(picked.astype(bf16), ((0, 0), (3, 125 - expert_count)))
    upstream_all = lax.all_gather(
        jnp.concatenate([my_rows(cotangent), picked_lanes], axis=1), everywhere, axis=0, tiled=True
    )
    shared_rows = share_over_devices((shared_gate, shared_up, shared_down), ep_count)
    shared_units = shared_rows[0].shape[0]
    routed_units = slot_here * slot_hidden
    gate_cat, up_cat, down_cat = [
        jnp.pad(
            jnp.concatenate([expert.reshape(-1, width), shared], axis=0),
            ((0, -(routed_units + shared_units) % 128), (0, 0)),
        )
        for expert, shared in zip((expert_gate, expert_up, expert_down), shared_rows)
    ]

    heads_here = heads_width // HD
    score_scale = HD ** (-0.5)
    first_norm_scale = side_weight[:, 0].astype(f32)
    second_norm_scale = side_weight[:, 1].astype(f32)
    mix_f = side_weight[:, 2].astype(f32)
    router_f = side_weight[:, 3 : 3 + expert_count].astype(f32)
    layer_input = tokens.astype(f32)
    normed_wide, norm_one = norm_forward(layer_input, first_norm_scale)
    normed_one = normed_wide.astype(bf16)
    query_at = offset + jnp.arange(rows_here, dtype=jnp.int32)
    key_at = offset - 2 * rows_here + jnp.arange(3 * rows_here, dtype=jnp.int32)
    query_seg, query_pos = sequence_info(lengths, query_at)
    key_seg, _ = sequence_info(lengths, key_at)
    cosine, sine = rope_tables(query_pos, HD)
    projected = jnp.dot(normed_one, qkv_weight, preferred_element_type=f32)
    projected = projected.reshape(rows_here, 3, heads_here, HD)
    queries = rotate(projected[:, 0], cosine, sine).astype(bf16)
    keys = rotate(projected[:, 1], cosine, sine).astype(bf16)
    values = projected[:, 2].astype(bf16)
    carried = jnp.stack([keys, values], axis=0)
    joined = jnp.concatenate(
        [passed_along(carried, "ep", 2), passed_along(carried, "ep", 1), carried], axis=1
    )
    keys_win = joined[0]
    values_win = joined[1]
    allowed = (
        (query_seg[:, None] == key_seg[None, :])
        & (key_at[None, :] <= query_at[:, None])
        & (key_at[None, :] >= 0)
    )
    scores = (
        jnp.einsum("qhd,khd->hqk", queries, keys_win, preferred_element_type=f32) * score_scale
    )
    masked = jnp.where(allowed[None], scores, -1e30)
    peak = jnp.max(masked, axis=-1, keepdims=True)
    expo = jnp.exp(masked - peak)
    total = jnp.sum(expo, axis=-1, keepdims=True)
    log_total = peak + jnp.log(total)
    weights = expo / total
    attended = jnp.einsum(
        "hqk,khd->qhd", weights.astype(bf16), values_win, preferred_element_type=f32
    )
    attended = attended.reshape(rows_here, heads_width).astype(bf16)
    attn_part = jnp.einsum("th,dh->td", attended, output_weight, preferred_element_type=f32)
    resid = my_rows(layer_input) + sum_over_tp(attn_part)
    normed_two_wide, norm_two = norm_forward(resid, second_norm_scale)
    normed_two = normed_two_wide.astype(bf16)

    logits = jnp.dot(normed_two, side_weight, preferred_element_type=f32)
    router = jax.nn.softmax(logits[:, 3 : 3 + expert_count], axis=-1)
    mixer = jax.nn.sigmoid(logits[:, 2])
    normed_all, ffn_part, d_normed_part, weighted_h, d_gate_pre, d_up_pre = ffn_over_all(
        normed_two,
        upstream_all,
        gate_cat,
        up_cat,
        down_cat,
        side_weight,
        (slot_here, slot_hidden, shared_units),
        expert_count,
    )
    d_normed_sum, out_sum = sum_over_all(d_normed_part, ffn_part)
    ffn_sum = out_sum[:, :width]
    dots_sum = out_sum[:, width:]
    grad_gate_cat = jnp.einsum("tf,td->fd", d_gate_pre, normed_all, preferred_element_type=f32)
    grad_up_cat = jnp.einsum("tf,td->fd", d_up_pre, normed_all, preferred_element_type=f32)
    grad_down_cat = jnp.einsum(
        "tf,td->fd", weighted_h, upstream_all[:, :width], preferred_element_type=f32
    )
    grad_cats = (grad_gate_cat, grad_up_cat, grad_down_cat)
    grad_shared = share_back(
        [grad[routed_units : routed_units + shared_units].astype(bf16) for grad in grad_cats],
        ep_count,
    )
    grad_shared = [grad.astype(f32) for grad in grad_shared]
    grad_experts = [grad[:routed_units].reshape(expert_gate.shape) for grad in grad_cats]

    block_out = gather_over_tp((resid + ffn_sum).astype(bf16))
    d_router = jnp.where(picked, dots_sum[:, 3 : 3 + expert_count], 0.0)
    d_mixer = dots_sum[:, 2]
    d_logits = router * (d_router - jnp.sum(router * d_router, axis=-1, keepdims=True))
    d_mixlogit = d_mixer * mixer * (1.0 - mixer)
    side = jnp.dot(d_logits, router_f.T, precision=highest) + d_mixlogit[:, None] * mix_f[None, :]
    normed_two_f = normed_two.astype(f32)
    d_side = jnp.concatenate([d_mixlogit[:, None], d_logits], axis=1)
    grad_side = jnp.dot(normed_two_f.T, d_side, precision=highest)
    upstream = my_rows(cotangent).astype(f32)
    d_normed_two = d_normed_sum + side
    d_resid_norm, grad_gain_two = norm_backward(resid, norm_two, second_norm_scale, d_normed_two)
    d_resid = upstream + d_resid_norm
    d_resid_low = gather_over_tp(d_resid.astype(bf16))
    grad_outw = jnp.einsum("td,th->dh", d_resid_low, attended, preferred_element_type=f32)
    d_attended = jnp.einsum("td,dh->th", d_resid_low, output_weight, preferred_element_type=f32)
    d_attended = d_attended.astype(bf16).reshape(rows_here, heads_here, HD)
    scores_again = (
        jnp.einsum("qhd,khd->hqk", queries, keys_win, preferred_element_type=f32) * score_scale
    )
    probs = jnp.where(allowed[None], jnp.exp(scores_again - log_total), 0.0)
    d_probs = jnp.einsum("qhd,khd->hqk", d_attended, values_win, preferred_element_type=f32)
    delta = jnp.sum(probs * d_probs, axis=-1, keepdims=True)
    d_scores = (probs * (d_probs - delta)).astype(bf16)
    d_keys_win = (
        jnp.einsum("hqk,qhd->khd", d_scores, queries, preferred_element_type=f32) * score_scale
    )
    d_values_win = jnp.einsum(
        "hqk,qhd->khd", probs.astype(bf16), d_attended, preferred_element_type=f32
    )
    pair_grads = jnp.stack([d_keys_win, d_values_win], axis=0)
    passed = pair_grads[:, : 2 * rows_here].astype(bf16)
    from_two = passed_along(passed[:, :rows_here], "ep", -2)
    from_one = passed_along(passed[:, rows_here:], "ep", -1)
    d_queries = (
        jnp.einsum("hqk,khd->qhd", d_scores, keys_win, preferred_element_type=f32) * score_scale
    )
    running = pair_grads[:, 2 * rows_here :] + from_one.astype(f32) + from_two.astype(f32)
    d_projected = jnp.concatenate(
        [
            unrotate(d_queries, cosine, sine).astype(bf16).reshape(rows_here, heads_width),
            unrotate(running[0], cosine, sine).astype(bf16).reshape(rows_here, heads_width),
            running[1].astype(bf16).reshape(rows_here, heads_width),
        ],
        axis=1,
    )
    d_normed_one = jnp.einsum("th,dh->td", d_projected, qkv_weight, preferred_element_type=f32)
    d_normed_one = sum_over_tp(d_normed_one)
    grad_qkv = jnp.einsum("td,th->dh", normed_one, d_projected, preferred_element_type=f32)
    d_input_norm, grad_gain_one = norm_backward(
        my_rows(layer_input), my_rows(norm_one), first_norm_scale, d_normed_one
    )
    grad_tokens = gather_over_tp((d_resid + d_input_norm).astype(bf16)).astype(f32)
    grad_weights = lax.psum_scatter(
        jnp.concatenate([grad_qkv, grad_outw], axis=1).astype(bf16),
        "ep",
        scatter_dimension=0,
        tiled=True,
    ).astype(f32)
    small = jnp.concatenate([grad_gain_one[:, None], grad_gain_two[:, None], grad_side], axis=1)
    small = lax.psum(lax.psum_scatter(small, "ep", scatter_dimension=0, tiled=True), "tp")
    parts = [grad_weights[:, i * heads_width : (i + 1) * heads_width] for i in range(4)]
    return (
        block_out,
        grad_tokens,
        small[:, 0],
        parts[0],
        parts[1],
        parts[2],
        parts[3],
        small[:, 1],
        small[:, 3:],
        small[:, 2],
        grad_shared[0],
        grad_shared[1],
        grad_shared[2],
        grad_experts[0],
        grad_experts[1],
        grad_experts[2],
    )


def chosen_body(*arrays):
    rows_here, top_count = arrays[2].shape
    slot_here, expert_count = arrays[14].shape[0], arrays[9].shape[1]
    capacity = rows_here * top_count * 7 // (5 * expert_count)
    grid_of_two = lax.axis_size("ep") % 2 == 0 and lax.axis_size("tp") == 4
    if grid_of_two and rows_here < 2 * slot_here * capacity:
        return dense_body(*arrays)
    return body(*arrays)


def solution(mesh):
    placed = (
        P("ep", None),
        P(),
        P("ep", None),
        P("ep"),
        P("ep", "tp"),
        P("ep", "tp"),
        P("ep", "tp"),
        P("ep", "tp"),
        P("ep"),
        P("ep", None),
        P("ep"),
        P("ep", "tp"),
        P("ep", "tp"),
        P("ep", "tp"),
        P("ep", "tp", None),
        P("ep", "tp", None),
        P("ep", "tp", None),
        P("ep", None),
    )
    return jax.shard_map(
        chosen_body,
        mesh=mesh,
        in_specs=placed,
        out_specs=(
            P("ep", None),
            P("ep", None),
            P("ep"),
            P("ep", "tp"),
            P("ep", "tp"),
            P("ep", "tp"),
            P("ep", "tp"),
            P("ep"),
            P("ep", None),
            P("ep"),
            P("ep", "tp"),
            P("ep", "tp"),
            P("ep", "tp"),
            P("ep", "tp", None),
            P("ep", "tp", None),
            P("ep", "tp", None),
        ),
        check_vma=False,
    )
```

```python
import functools

import jax
import jax.numpy as jnp
from jax import lax
from jax.experimental import pallas as pl
from jax.experimental.pallas import tpu as pltpu
from jax.sharding import PartitionSpec as P

HD = 128


epsilon = 1e-06
rope_base = 1000000.0
highest = lax.Precision.HIGHEST
MESH = pl.DeviceIdType.MESH


def passed_along(block, axis, distance):
    devices = range(lax.axis_size(axis))
    route = [(i - distance, i) for i in devices if i - distance in devices]
    return lax.ppermute(block, axis, route)


def rope_tables(positions, width):
    steps = jnp.arange(0, width, 2, dtype=jnp.float32) / width
    inverse = rope_base ** (-steps)
    angles = positions.astype(jnp.float32)[:, None] * inverse[None, :]
    angles = jnp.concatenate([angles, angles], axis=-1)
    return (jnp.cos(angles)[:, None, :], jnp.sin(angles)[:, None, :])


def turn_half(values):
    middle = values.shape[-1] // 2
    return jnp.concatenate([-values[..., middle:], values[..., :middle]], axis=-1)


def rotate(values, cosine, sine):
    return values * cosine + turn_half(values) * sine


def unrotate(grads, cosine, sine):
    return grads * cosine - turn_half(grads * sine)


def sequence_info(lengths, indices):
    starts = jnp.cumsum(lengths) - lengths
    inside = starts[None, :] <= indices[:, None]
    segment = jnp.sum(inside.astype(jnp.int32), axis=1) - 1
    first = jnp.max(jnp.where(inside, starts[None, :], -1), axis=1)
    return (segment, indices - first)


def norm_forward(values, gain):
    scale = lax.rsqrt(jnp.mean(values * values, axis=-1, keepdims=True) + epsilon)
    return (values * scale * gain, scale)


def norm_backward(values, scale, gain, grads):
    unit = values * scale
    scaled = grads * gain
    inner = jnp.mean(scaled * unit, axis=-1, keepdims=True)
    return (scale * (scaled - unit * inner), jnp.sum(grads * unit, axis=0))


def deliver(rows):
    arrived_rows = lax.all_to_all(rows, "ep", split_axis=0, concat_axis=0, tiled=True)
    return arrived_rows


def bring_back(parts, target, rows_here, top_count):
    moved = lax.all_to_all(parts, "ep", split_axis=0, concat_axis=0, tiled=True)
    piece = moved.shape[3]
    return moved.reshape(-1, piece)[target].reshape(rows_here, top_count, piece)


def body(
    tokens,
    lengths,
    routes,
    attn_gain,
    w_query,
    w_key,
    w_value,
    w_out,
    ffn_gain,
    w_router,
    shared_mix,
    shared_gate,
    shared_up,
    shared_down,
    expert_gate,
    expert_up,
    expert_down,
    cotangent,
):
    rows_here = tokens.shape[0]
    width = tokens.shape[1]
    ep_count = lax.axis_size("ep")
    offset = lax.axis_index("ep") * rows_here
    slot_here = expert_gate.shape[0]
    top_count = routes.shape[1]
    gathered = (
        lax.all_gather(attn_gain, "ep", axis=0, tiled=True),
        lax.all_gather(w_query, "ep", axis=0, tiled=True),
        lax.all_gather(w_key, "ep", axis=0, tiled=True),
        lax.all_gather(w_value, "ep", axis=0, tiled=True),
        lax.all_gather(w_out, "ep", axis=0, tiled=True),
        lax.all_gather(ffn_gain, "ep", axis=0, tiled=True),
        lax.all_gather(w_router, "ep", axis=0, tiled=True),
        lax.all_gather(shared_mix, "ep", axis=0, tiled=True),
        lax.all_gather(shared_gate, "ep", axis=0, tiled=True),
        lax.all_gather(shared_up, "ep", axis=0, tiled=True),
        lax.all_gather(shared_down, "ep", axis=0, tiled=True),
    )
    (
        gain_first,
        query_weight_matrix,
        key_weight_matrix,
        value_weight_matrix,
        output_weight,
        gain_second,
        router_weight,
        shared_mixer_weight,
        shared_gate_weight,
        shared_up_weight,
        shared_down_weight,
    ) = gathered
    expert_count = router_weight.shape[1]
    capacity = (rows_here * top_count * 7 // (5 * expert_count) + 7) // 8 * 8
    heads_here = query_weight_matrix.shape[1] // HD
    score_scale = HD ** (-0.5)
    first_norm_scale = gain_first.astype(jnp.float32)
    second_norm_scale = gain_second.astype(jnp.float32)
    layer_input = tokens.astype(jnp.float32)
    normed_wide, norm_one = norm_forward(layer_input, first_norm_scale)
    normed_one = normed_wide.astype(jnp.bfloat16)
    query_at = offset + jnp.arange(rows_here, dtype=jnp.int32)
    key_at = offset - 2 * rows_here + jnp.arange(3 * rows_here, dtype=jnp.int32)
    query_seg, query_pos = sequence_info(lengths, query_at)
    key_seg, _ = sequence_info(lengths, key_at)
    cosine, sine = rope_tables(query_pos, HD)
    query_pre = jnp.dot(
        normed_one, query_weight_matrix, preferred_element_type=jnp.float32
    ).reshape(rows_here, heads_here, HD)
    key_pre = jnp.dot(normed_one, key_weight_matrix, preferred_element_type=jnp.float32).reshape(
        rows_here, heads_here, HD
    )
    queries = rotate(query_pre, cosine, sine).astype(jnp.bfloat16)
    keys = rotate(key_pre, cosine, sine).astype(jnp.bfloat16)
    values = (
        jnp.dot(normed_one, value_weight_matrix, preferred_element_type=jnp.float32)
        .astype(jnp.bfloat16)
        .reshape(rows_here, heads_here, HD)
    )
    carried = jnp.stack([keys, values], axis=0)
    window = [carried]
    for hop in range(2):
        carried = passed_along(carried, "ep", 1)
        window = [carried] + window
    joined = jnp.concatenate(window, axis=1)
    keys_win = joined[0]
    values_win = joined[1]
    allowed = (
        (query_seg[:, None] == key_seg[None, :])
        & (key_at[None, :] <= query_at[:, None])
        & (key_at[None, :] >= 0)
    )
    scores = (
        jnp.einsum("qhd,khd->hqk", queries, keys_win, preferred_element_type=jnp.float32)
        * score_scale
    )
    masked = jnp.where(allowed[None], scores, -1e30)
    peak = jnp.max(masked, axis=-1, keepdims=True)
    expo = jnp.exp(masked - peak)
    total = jnp.sum(expo, axis=-1, keepdims=True)
    log_total = peak + jnp.log(total)
    weights = expo / total
    attended = jnp.einsum(
        "hqk,khd->qhd", weights.astype(jnp.bfloat16), values_win, preferred_element_type=jnp.float32
    )
    attended = attended.reshape(rows_here, heads_here * HD).astype(jnp.bfloat16)
    attn_part = jnp.einsum("th,dh->td", attended, output_weight, preferred_element_type=jnp.float32)
    resid = layer_input + lax.psum(attn_part, "tp")
    normed_two_wide, norm_two = norm_forward(resid, second_norm_scale)
    normed_two = normed_two_wide.astype(jnp.bfloat16)
    normed_two_f = normed_two.astype(jnp.float32)
    router_f = router_weight.astype(jnp.float32)
    mix_f = shared_mixer_weight.astype(jnp.float32)
    router = jax.nn.softmax(jnp.dot(normed_two_f, router_f, precision=highest), axis=-1)
    picked = routes[:, :, None] == jnp.arange(expert_count, dtype=jnp.int32)[None, None, :]
    gates = jnp.sum(jnp.where(picked, router[:, None, :], 0.0), axis=-1)
    mixer = jax.nn.sigmoid(jnp.dot(normed_two_f, mix_f, precision=highest))
    shared_g = jnp.dot(normed_two, shared_gate_weight, preferred_element_type=jnp.float32)
    shared_u = jnp.dot(normed_two, shared_up_weight, preferred_element_type=jnp.float32)
    shared_h = (jax.nn.silu(shared_g) * shared_u).astype(jnp.bfloat16)
    shared_part = jnp.einsum(
        "tf,df->td", shared_h, shared_down_weight, preferred_element_type=jnp.float32
    )
    flat = routes.reshape(-1)
    hot = (flat[:, None] == jnp.arange(expert_count, dtype=jnp.int32)[None, :]).astype(jnp.int32)
    rank = jnp.sum(jnp.cumsum(hot, axis=0) * hot, axis=1) - 1
    target = flat * capacity + rank
    slot_total = ep_count * slot_here * capacity
    owner_route = (
        jnp.zeros((slot_total,), jnp.int32)
        .at[target]
        .set(jnp.arange(rows_here * top_count, dtype=jnp.int32))
    )
    filled = jnp.zeros((slot_total,), jnp.bool_).at[target].set(True)
    owner_token = owner_route // top_count
    send_rows = jnp.where(filled[:, None], normed_two[owner_token], jnp.zeros((), jnp.bfloat16))
    arrived_rows = deliver(send_rows.reshape(ep_count, slot_here, capacity, width))
    route_g = jnp.einsum(
        "nscd,sfd->nscf", arrived_rows, expert_gate, preferred_element_type=jnp.float32
    )
    route_u = jnp.einsum(
        "nscd,sfd->nscf", arrived_rows, expert_up, preferred_element_type=jnp.float32
    )
    route_h = (jax.nn.silu(route_g) * route_u).astype(jnp.bfloat16)
    route_part = jnp.einsum(
        "nscf,sfd->nscd", route_h, expert_down, preferred_element_type=jnp.float32
    )
    back_rows = bring_back(route_part, target, rows_here, top_count)
    upstream = cotangent.astype(jnp.float32)
    routed = jnp.sum(back_rows * gates[:, :, None], axis=1)
    ffn_part = mixer[:, None] * shared_part + routed
    route_dot = jnp.sum(back_rows * upstream[:, None, :], axis=-1)
    shared_dot = jnp.sum(shared_part * upstream, axis=-1)
    ffn_total, d_gate, d_mixer = lax.psum((ffn_part, route_dot, shared_dot), "tp")
    block_out = (resid + ffn_total).astype(jnp.bfloat16)
    d_router = jnp.sum(jnp.where(picked, d_gate[:, :, None], 0.0), axis=1)
    d_logits = router * (d_router - jnp.sum(router * d_router, axis=-1, keepdims=True))
    d_mixlogit = d_mixer * mixer * (1.0 - mixer)
    side = jnp.dot(d_logits, router_f.T, precision=highest) + d_mixlogit[:, None] * mix_f[None, :]
    grad_router = jnp.dot(normed_two_f.T, d_logits, precision=highest)
    grad_mix = jnp.dot(d_mixlogit, normed_two_f, precision=highest)
    d_shared = (mixer[:, None] * upstream).astype(jnp.bfloat16)
    d_sh = jnp.dot(d_shared, shared_down_weight, preferred_element_type=jnp.float32)
    sig_shared = jax.nn.sigmoid(shared_g)
    d_sg = (d_sh * shared_u * sig_shared * (1.0 + shared_g * (1.0 - sig_shared))).astype(
        jnp.bfloat16
    )
    d_su = (d_sh * shared_g * sig_shared).astype(jnp.bfloat16)
    d_normed_part = jnp.einsum(
        "tf,df->td", d_sg, shared_gate_weight, preferred_element_type=jnp.float32
    )
    d_normed_part = d_normed_part + jnp.einsum(
        "tf,df->td", d_su, shared_up_weight, preferred_element_type=jnp.float32
    )
    grad_sgate = jnp.einsum("td,tf->df", normed_two, d_sg, preferred_element_type=jnp.float32)
    grad_sup = jnp.einsum("td,tf->df", normed_two, d_su, preferred_element_type=jnp.float32)
    grad_sdown = jnp.einsum("td,tf->df", d_shared, shared_h, preferred_element_type=jnp.float32)
    d_route = (
        (gates[:, :, None] * upstream[:, None, :])
        .astype(jnp.bfloat16)
        .reshape(rows_here * top_count, width)
    )
    send_grads = jnp.where(filled[:, None], d_route[owner_route], jnp.zeros((), jnp.bfloat16))
    received_grads = deliver(send_grads.reshape(ep_count, slot_here, capacity, width))
    d_rh = jnp.einsum(
        "nscd,sfd->nscf", received_grads, expert_down, preferred_element_type=jnp.float32
    )
    sig_route = jax.nn.sigmoid(route_g)
    d_rg = (d_rh * route_u * sig_route * (1.0 + route_g * (1.0 - sig_route))).astype(jnp.bfloat16)
    routed_up_gradient = (d_rh * route_g * sig_route).astype(jnp.bfloat16)
    row_grads = jnp.einsum("nscf,sfd->nscd", d_rg, expert_gate, preferred_element_type=jnp.float32)
    row_grads = row_grads + jnp.einsum(
        "nscf,sfd->nscd", routed_up_gradient, expert_up, preferred_element_type=jnp.float32
    )
    grad_egate = jnp.einsum(
        "qxba,qxbr->xar", d_rg, arrived_rows, preferred_element_type=jnp.float32
    )
    expert_up_gradient = jnp.einsum(
        "qxba,qxbr->xar", routed_up_gradient, arrived_rows, preferred_element_type=jnp.float32
    )
    grad_edown = jnp.einsum(
        "qxba,qxbr->xar", route_h, received_grads, preferred_element_type=jnp.float32
    )
    grads_back = bring_back(row_grads, target, rows_here, top_count)
    d_routed = jnp.sum(grads_back, axis=1)
    d_normed_two = lax.psum(d_normed_part + d_routed, "tp") + side
    d_resid_norm, grad_gain_two = norm_backward(resid, norm_two, second_norm_scale, d_normed_two)
    d_resid = upstream + d_resid_norm
    d_resid_low = d_resid.astype(jnp.bfloat16)
    grad_outw = jnp.einsum("td,th->dh", d_resid_low, attended, preferred_element_type=jnp.float32)
    d_attended = jnp.einsum(
        "td,dh->th", d_resid_low, output_weight, preferred_element_type=jnp.float32
    )
    d_attended = d_attended.astype(jnp.bfloat16).reshape(rows_here, heads_here, HD)
    scores_again = (
        jnp.einsum("qhd,khd->hqk", queries, keys_win, preferred_element_type=jnp.float32)
        * score_scale
    )
    probs = jnp.where(allowed[None], jnp.exp(scores_again - log_total), 0.0)
    d_probs = jnp.einsum("qhd,khd->hqk", d_attended, values_win, preferred_element_type=jnp.float32)
    delta = jnp.sum(probs * d_probs, axis=-1, keepdims=True)
    d_scores = (probs * (d_probs - delta)).astype(jnp.bfloat16)
    d_queries = (
        jnp.einsum("hqk,khd->qhd", d_scores, keys_win, preferred_element_type=jnp.float32)
        * score_scale
    )
    d_keys_win = (
        jnp.einsum("hqk,qhd->khd", d_scores, queries, preferred_element_type=jnp.float32)
        * score_scale
    )
    d_values_win = jnp.einsum(
        "hqk,qhd->khd", probs.astype(jnp.bfloat16), d_attended, preferred_element_type=jnp.float32
    )
    pair_grads = jnp.stack([d_keys_win, d_values_win], axis=0)
    older = pair_grads[:, :rows_here]
    later = [pair_grads[:, rows_here : 2 * rows_here], pair_grads[:, 2 * rows_here :]]
    running = older
    for hop in range(2):
        running = passed_along(running, "ep", -1)
        running = running + later[hop]
    d_query_pre = (
        unrotate(d_queries, cosine, sine).astype(jnp.bfloat16).reshape(rows_here, heads_here * HD)
    )
    d_key_pre = (
        unrotate(running[0], cosine, sine).astype(jnp.bfloat16).reshape(rows_here, heads_here * HD)
    )
    d_values = running[1].astype(jnp.bfloat16).reshape(rows_here, heads_here * HD)
    grad_queryw = jnp.einsum(
        "td,th->dh", normed_one, d_query_pre, preferred_element_type=jnp.float32
    )
    grad_keyw = jnp.einsum("td,th->dh", normed_one, d_key_pre, preferred_element_type=jnp.float32)
    grad_valuew = jnp.einsum("td,th->dh", normed_one, d_values, preferred_element_type=jnp.float32)
    d_normed_one = jnp.einsum(
        "th,dh->td", d_query_pre, query_weight_matrix, preferred_element_type=jnp.float32
    )
    d_normed_one = d_normed_one + jnp.einsum(
        "th,dh->td", d_key_pre, key_weight_matrix, preferred_element_type=jnp.float32
    )
    d_normed_one = d_normed_one + jnp.einsum(
        "th,dh->td", d_values, value_weight_matrix, preferred_element_type=jnp.float32
    )
    d_normed_one = lax.psum(d_normed_one, "tp")
    d_input_norm, grad_gain_one = norm_backward(
        layer_input, norm_one, first_norm_scale, d_normed_one
    )
    grad_tokens = d_resid + d_input_norm
    summed = (
        lax.psum_scatter(grad_gain_one, "ep", scatter_dimension=0, tiled=True),
        lax.psum_scatter(grad_queryw, "ep", scatter_dimension=0, tiled=True),
        lax.psum_scatter(grad_keyw, "ep", scatter_dimension=0, tiled=True),
        lax.psum_scatter(grad_valuew, "ep", scatter_dimension=0, tiled=True),
        lax.psum_scatter(grad_outw, "ep", scatter_dimension=0, tiled=True),
        lax.psum_scatter(grad_gain_two, "ep", scatter_dimension=0, tiled=True),
        lax.psum_scatter(grad_router, "ep", scatter_dimension=0, tiled=True),
        lax.psum_scatter(grad_mix, "ep", scatter_dimension=0, tiled=True),
        lax.psum_scatter(grad_sgate, "ep", scatter_dimension=0, tiled=True),
        lax.psum_scatter(grad_sup, "ep", scatter_dimension=0, tiled=True),
        lax.psum_scatter(grad_sdown, "ep", scatter_dimension=0, tiled=True),
    )
    return (
        block_out,
        grad_tokens,
        summed[0],
        summed[1],
        summed[2],
        summed[3],
        summed[4],
        summed[5],
        summed[6],
        summed[7],
        summed[8],
        summed[9],
        summed[10],
        grad_egate,
        expert_up_gradient,
        grad_edown,
    )


class Place:
    def __init__(self):
        self.ep, self.tp = lax.axis_index("ep"), lax.axis_index("tp")
        self.z, self.y = self.ep // 2, self.ep % 2
        self.x, self.c = self.tp // 2, self.tp % 2
        self.depth = lax.axis_size("ep") // 2
        self.next_core = (self.ep, self.x * 2 + 1 - self.c)
        self.next_x = (self.ep, (1 - self.x) * 2 + self.c)
        self.next_y = (self.z * 2 + 1 - self.y, self.tp)

    def at_z(self, z):
        return (z * 2 + self.y, self.tp)

    def ahead(self, steps):
        return lax.rem(self.z + steps, self.depth)

    def behind(self, steps):
        return lax.rem(self.z + self.depth - steps, self.depth)

    def greet(self):
        barrier = pltpu.get_barrier_semaphore()
        peers = [self.next_core, self.next_x, self.next_y]
        peers += [self.at_z(self.ahead(k)) for k in range(1, self.depth)]
        for peer in peers:
            pl.semaphore_signal(barrier, inc=1, device_id=peer, device_id_type=MESH)
        pl.semaphore_wait(barrier, len(peers))


def remote(src, dst, send, recv, peer):
    return pltpu.make_async_remote_copy(
        src_ref=src, dst_ref=dst, send_sem=send, recv_sem=recv, device_id=peer, device_id_type=MESH
    )


def ffn_kernel(
    units,
    expert_count,
    rows_in,
    upstream_in,
    gate_in,
    up_in,
    down_in,
    side_in,
    rows_all,
    out_part,
    d_rows_part,
    weighted_out,
    d_gate_out,
    d_up_out,
    gate_w,
    up_w,
    down_w,
    side_w,
    rows_tile,
    upstream_tile,
    out_tile,
    d_rows_tile,
    weighted_tile,
    d_gate_tile,
    d_up_tile,
    weight_sem,
    own_sem,
    z_send,
    z_recv,
    plane_send,
    plane_recv,
    load_sem,
    store_sem,
):
    at = Place()
    depth = at.depth
    quarter = rows_in.shape[0]
    width = rows_in.shape[1]
    half = quarter // 2
    own, other_x = at.tp, (1 - at.x) * 2 + at.c

    def weight_copies():
        pairs = ((gate_in, gate_w), (up_in, up_w), (down_in, down_w), (side_in, side_w))
        return [
            pltpu.make_async_copy(src, dst, weight_sem.at[i]) for i, (src, dst) in enumerate(pairs)
        ]

    for copy in weight_copies():
        copy.start()

    def block(j, y, tp):
        return rows_all.at[at.behind(j), y, tp]

    def plane_copy(j, kind):
        y, other_y = at.y, 1 - at.y
        if kind == 0:
            src, peer = block(j, y, own), at.next_x
        elif kind == 1:
            src, peer = block(j, y, own), at.next_y
        elif kind == 2:
            src, peer = block(j, y, other_x).at[pl.ds(0, half)], at.next_y
        elif kind == 3:
            src, peer = block(j, other_y, own).at[pl.ds(half, half)], at.next_x
        else:
            src = block(j, other_y if kind >= 6 else y, other_x if kind % 2 else own)
            peer = at.next_core
        return remote(src, src, plane_send.at[j, kind], plane_recv.at[j, kind], peer)

    def z_copy(k):
        return remote(
            rows_in, block(0, at.y, own), z_send.at[k - 1], z_recv.at[k - 1], at.at_z(at.ahead(k))
        )

    def z_arrival(k):
        dst = block(k, at.y, own)
        return remote(dst, dst, z_send.at[k - 1], z_recv.at[k - 1], at.at_z(at.behind(k)))

    def begin(j):
        for kind in (0, 1, 4):
            plane_copy(j, kind).start()

    def spread(j):
        plane_copy(j, 0).wait_recv()
        plane_copy(j, 2).start()
        plane_copy(j, 5).start()
        plane_copy(j, 1).wait_recv()
        plane_copy(j, 3).start()
        plane_copy(j, 6).start()

    def begin_later(j):
        z_arrival(j).wait_recv()
        begin(j)

    def last_hop(j):
        plane_copy(j, 2).wait_recv()
        plane_copy(j, 3).wait_recv()
        plane_copy(j, 7).start()

    def near_ready(j):
        plane_copy(j, 4).wait_recv()
        plane_copy(j, 5).wait_recv()

    def far_ready(j):
        plane_copy(j, 6).wait_recv()
        plane_copy(j, 7).wait_recv()

    def tile_at(step):
        j = step // 2
        return at.behind(j), lax.rem(at.y + lax.rem(step, 2), 2)

    def load_rows(step):
        z, y = tile_at(step)
        slot = lax.rem(step, 2)
        return pltpu.make_async_copy(rows_all.at[z, y], rows_tile.at[slot], load_sem.at[0, slot])

    def load_upstream(step):
        z, y = tile_at(step)
        slot = lax.rem(step, 2)
        return pltpu.make_async_copy(
            upstream_in.at[z, y], upstream_tile.at[slot], load_sem.at[1, slot]
        )

    def stores(step):
        z, y = tile_at(step)
        slot = lax.rem(step, 2)
        pairs = (
            (out_tile, out_part),
            (d_rows_tile, d_rows_part),
            (weighted_tile, weighted_out),
            (d_gate_tile, d_gate_out),
            (d_up_tile, d_up_out),
        )
        return [
            pltpu.make_async_copy(src.at[slot], dst.at[z, y], store_sem.at[i, slot])
            for i, (src, dst) in enumerate(pairs)
        ]

    load_upstream(0).start()
    at.greet()
    for k in range(1, depth):
        z_copy(k).start()
    own_copy = pltpu.make_async_copy(rows_in, block(0, at.y, own), own_sem)
    own_copy.start()
    own_copy.wait()
    begin(0)
    spread(0)
    begin_later(1)
    near_ready(0)
    load_rows(0).start()
    for copy in weight_copies():
        copy.wait()

    tile = rows_tile.shape[1] * rows_tile.shape[2]
    hidden_total = gate_w.shape[0]
    lane = lax.broadcasted_iota(jnp.int32, (tile, 128), 1)
    unit = lax.broadcasted_iota(jnp.int32, (1, hidden_total), 1)
    slot_here, slot_hidden, shared_hidden = units
    routed = slot_here * slot_hidden
    across = (((1,), (1,)), ((), ()))
    f32, bf16 = jnp.float32, jnp.bfloat16

    def step_body(step, carry):
        slot = lax.rem(step, 2)
        load_upstream(step).wait()

        @pl.when(step + 1 < 2 * depth)
        def _():
            load_upstream(step + 1).start()

        upstream = upstream_tile[slot].reshape(tile, upstream_tile.shape[-1])
        d_hidden = lax.dot_general(
            upstream[:, :width], down_w[...], across, preferred_element_type=f32
        )
        load_rows(step).wait()
        rows = rows_tile[slot].reshape(tile, width)
        logits = jnp.dot(rows, side_w[...], preferred_element_type=f32)
        chooses = (lane >= 3) & (lane < 3 + expert_count)
        peak = jnp.max(jnp.where(chooses, logits, -1e30), axis=1, keepdims=True)
        expo = jnp.where(chooses, jnp.exp(jnp.where(chooses, logits, peak) - peak), 0.0)
        router = expo / jnp.sum(expo, axis=1, keepdims=True)
        routed_gate = router * upstream[:, width:].astype(f32)
        mix_pre = jnp.sum(jnp.where(lane == 2, logits, 0.0), axis=1, keepdims=True)
        mixer = 1.0 / (1.0 + jnp.exp(-mix_pre))
        factor = jnp.where(unit < routed + shared_hidden, mixer, 0.0)
        for s in range(slot_here):
            chosen = lane == 3 + at.ep * slot_here + s
            gate = jnp.sum(jnp.where(chosen, routed_gate, 0.0), axis=1, keepdims=True)
            inside = (unit >= s * slot_hidden) & (unit < (s + 1) * slot_hidden)
            factor = jnp.where(inside, gate, factor)
        gate_pre = lax.dot_general(rows, gate_w[...], across, preferred_element_type=f32)
        up_pre = lax.dot_general(rows, up_w[...], across, preferred_element_type=f32)

        @pl.when(step >= 2)
        def _():
            for copy in stores(step - 2):
                copy.wait()

        sig = 1.0 / (1.0 + jnp.exp(-gate_pre))
        silu = gate_pre * sig
        hidden = silu * up_pre
        product = hidden * d_hidden
        gated = factor * d_hidden
        weighted_tile[slot] = (factor * hidden).astype(bf16)
        d_gate_tile[slot] = (gated * up_pre * (sig + silu * (1.0 - sig))).astype(bf16)
        d_up_tile[slot] = (gated * silu).astype(bf16)
        dots = jnp.zeros((tile, 128), f32)
        for s in range(slot_here + 1):
            last = s == slot_here
            inside = unit >= s * slot_hidden
            if not last:
                inside = inside & (unit < (s + 1) * slot_hidden)
            dot = jnp.sum(jnp.where(inside, product, 0.0), axis=1, keepdims=True)
            where = lane == (2 if last else 3 + at.ep * slot_here + s)
            dots = jnp.where(where, dot, dots)
        out = jnp.dot(weighted_tile[slot], down_w[...], preferred_element_type=f32)
        out_tile[slot, :, :, :width] = out.astype(bf16).reshape(rows_tile.shape[1:])
        out_tile[slot, :, :, width:] = dots.astype(bf16).reshape(rows_tile.shape[1:3] + (128,))
        d_rows = jnp.dot(d_gate_tile[slot], gate_w[...], preferred_element_type=f32)
        d_rows = d_rows + jnp.dot(d_up_tile[slot], up_w[...], preferred_element_type=f32)
        d_rows_tile[slot] = d_rows.astype(bf16).reshape(rows_tile.shape[1:])
        for copy in stores(step):
            copy.start()
        j = step // 2
        even = lax.rem(step, 2) == 0

        @pl.when(even)
        def _():
            last_hop(j)

            @pl.when(j + 1 < depth)
            def _():
                spread(j + 1)

            @pl.when(j + 2 < depth)
            def _():
                begin_later(j + 2)

            far_ready(j)
            load_rows(step + 1).start()

        @pl.when(jnp.logical_not(even) & (j + 1 < depth))
        def _():
            near_ready(j + 1)
            load_rows(step + 1).start()

        return carry

    lax.fori_loop(0, 2 * depth, step_body, 0)
    for step in (2 * depth - 2, 2 * depth - 1):
        for copy in stores(step):
            copy.wait()
    for k in range(1, depth):
        z_copy(k).wait_send()

    def finish(j, carry):
        for kind in range(8):
            plane_copy(j, kind).wait_send()
        return carry

    lax.fori_loop(0, depth, finish, 0)


def ffn_over_all(rows, upstream_all, gate_w, up_w, down_w, side_w, units, expert_count):
    quarter, width = rows.shape
    ep_count, tp_count = lax.axis_size("ep"), lax.axis_size("tp")
    depth = ep_count // 2
    hidden = gate_w.shape[0]
    bf16 = jnp.bfloat16
    upstream_all = upstream_all.reshape(depth, 2, tp_count, quarter, upstream_all.shape[-1])
    block = (depth, 2, tp_count, quarter)
    tile_rows = tp_count * quarter
    hidden_shape = jax.ShapeDtypeStruct((depth, 2, tile_rows, hidden), bf16)
    anywhere = pl.BlockSpec(memory_space=pl.ANY)
    tokens = ep_count * tile_rows
    outs = pl.pallas_call(
        functools.partial(ffn_kernel, units, expert_count),
        out_shape=(
            jax.ShapeDtypeStruct(block + (width,), bf16),
            jax.ShapeDtypeStruct(block + (width + 128,), bf16),
            jax.ShapeDtypeStruct(block + (width,), bf16),
            hidden_shape,
            hidden_shape,
            hidden_shape,
        ),
        in_specs=[anywhere] * 6,
        out_specs=(anywhere,) * 6,
        scratch_shapes=[
            pltpu.VMEM((hidden, width), bf16),
            pltpu.VMEM((hidden, width), bf16),
            pltpu.VMEM((hidden, width), bf16),
            pltpu.VMEM((width, 128), bf16),
            pltpu.VMEM((2, tp_count, quarter, width), bf16),
            pltpu.VMEM((2, tp_count, quarter, width + 128), bf16),
            pltpu.VMEM((2, tp_count, quarter, width + 128), bf16),
            pltpu.VMEM((2, tp_count, quarter, width), bf16),
            pltpu.VMEM((2, tile_rows, hidden), bf16),
            pltpu.VMEM((2, tile_rows, hidden), bf16),
            pltpu.VMEM((2, tile_rows, hidden), bf16),
            pltpu.SemaphoreType.DMA((4,)),
            pltpu.SemaphoreType.DMA,
            pltpu.SemaphoreType.DMA((depth - 1,)),
            pltpu.SemaphoreType.DMA((depth - 1,)),
            pltpu.SemaphoreType.DMA((depth, 8)),
            pltpu.SemaphoreType.DMA((depth, 8)),
            pltpu.SemaphoreType.DMA((2, 2)),
            pltpu.SemaphoreType.DMA((5, 2)),
        ],
        compiler_params=pltpu.CompilerParams(
            collective_id=1, has_side_effects=True, vmem_limit_bytes=60 * 2**20
        ),
        cost_estimate=pl.CostEstimate(
            flops=12 * tokens * width * hidden,
            bytes_accessed=10 * tokens * width,
            transcendentals=tokens * hidden,
        ),
        name="ffn_all_tokens",
    )(rows, upstream_all, gate_w, up_w, down_w, side_w)
    rows_all, out_part, d_rows_part, weighted, d_gate, d_up = outs
    return (
        rows_all.reshape(tokens, width),
        out_part,
        d_rows_part,
        weighted.reshape(tokens, hidden),
        d_gate.reshape(tokens, hidden),
        d_up.reshape(tokens, hidden),
    )


def sum_kernel(
    first_in,
    second_in,
    first_out,
    second_out,
    first_own,
    second_own,
    first_core,
    second_core,
    first_hop,
    second_hop,
    first_hop2,
    second_hop2,
    first_z,
    second_z,
    load_sem,
    send_sem,
    recv_sem,
):
    at = Place()
    depth = at.depth
    f32 = jnp.float32

    def to(j):
        return at.ahead(j)

    ins, owns = (first_in, second_in), (first_own, second_own)
    cores, hops = (first_core, second_core), (first_hop, second_hop)
    hops2, zs = (first_hop2, second_hop2), (first_z, second_z)

    def load(a, j):
        return pltpu.make_async_copy(
            ins[a].at[to(j), :, :, at.c], owns[a].at[j], load_sem.at[a, j]
        )

    def core_copy(a, j):
        return remote(
            ins[a].at[to(j), :, :, 1 - at.c],
            cores[a].at[j],
            send_sem.at[a, 0, j],
            recv_sem.at[a, 0, j],
            at.next_core,
        )

    def hop_copy(a, j):
        src = owns[0].at[j, :, 1 - at.x] if a == 0 else owns[1].at[j, 1 - at.y]
        peer = at.next_x if a == 0 else at.next_y
        return remote(src, hops[a].at[j], send_sem.at[a, 1, j], recv_sem.at[a, 1, j], peer)

    def hop2_copy(a, j):
        src = owns[0].at[j, 1 - at.y, at.x] if a == 0 else owns[1].at[j, at.y, 1 - at.x]
        peer = at.next_y if a == 0 else at.next_x
        return remote(src, hops2[a].at[j], send_sem.at[a, 2, j], recv_sem.at[a, 2, j], peer)

    def z_copy(a, j):
        return remote(
            owns[a].at[j, at.y, at.x],
            zs[a].at[j - 1],
            send_sem.at[a, 3, j],
            recv_sem.at[a, 3, j],
            at.at_z(to(j)),
        )

    def add(into, other):
        rows = into.shape[0]
        step = 32

        def body(i, carry):
            part = pl.ds(pl.multiple_of(i * step, step), step)
            into[part] = (into[part].astype(f32) + other[part].astype(f32)).astype(into.dtype)
            return carry

        lax.fori_loop(0, rows // step, body, 0)

    def after_core(a, j):
        load(a, j).wait()
        core_copy(a, j).wait_recv()

        def body(i, carry):
            moved, other = 1 - i // 2, lax.rem(i, 2)
            if a == 0:
                y, x = other, lax.rem(at.x + moved, 2)
            else:
                y, x = lax.rem(at.y + moved, 2), other
            add(owns[a].at[j, y, x], cores[a].at[j, y, x])
            return carry

        lax.fori_loop(0, 2, body, 0)
        hop_copy(a, j).start()
        lax.fori_loop(2, 4, body, 0)

    def after_hop(a, j):
        hop_copy(a, j).wait_recv()
        for moved in (1, 0):
            if a == 0:
                y = lax.rem(at.y + moved, 2)
                add(owns[0].at[j, y, at.x], hops[0].at[j, y])
            else:
                x = lax.rem(at.x + moved, 2)
                add(owns[1].at[j, at.y, x], hops[1].at[j, x])
            if moved:
                hop2_copy(a, j).start()

    def after_hop2(a, j):
        hop2_copy(a, j).wait_recv()
        add(owns[a].at[j, at.y, at.x], hops2[a].at[j])
        if j > 0:
            z_copy(a, j).start()

    order = [j for j in range(1, depth)] + [0]
    for j in order:
        for a in (0, 1):
            load(a, j).start()
    at.greet()
    for j in order:
        for a in (0, 1):
            core_copy(a, j).start()
    for turn in range(depth + 2):
        for a in (0, 1):
            if turn < depth:
                after_core(a, order[turn])
        for a in (0, 1):
            if 0 <= turn - 1 < depth:
                after_hop(a, order[turn - 1])
        for a in (0, 1):
            if 0 <= turn - 2 < depth:
                after_hop2(a, order[turn - 2])
    for a, out in ((0, first_out), (1, second_out)):
        for k in range(1, depth):
            z_copy(a, k).wait_recv()
        rows = out.shape[0]
        step = 32

        def body(i, carry):
            part = pl.ds(pl.multiple_of(i * step, step), step)
            total = owns[a][0, at.y, at.x, part].astype(f32)
            for k in range(depth - 1):
                total = total + zs[a][k, part].astype(f32)
            out[part] = total
            return carry

        lax.fori_loop(0, rows // step, body, 0)
    for a in (0, 1):
        for j in range(depth):
            core_copy(a, j).wait_send()
            hop_copy(a, j).wait_send()
            hop2_copy(a, j).wait_send()
            if j > 0:
                z_copy(a, j).wait_send()


def sum_over_all(first, second):
    depth, _, _, rows, _ = first.shape
    widths = (first.shape[-1], second.shape[-1])
    dtype = first.dtype

    def both(*lead):
        return [pltpu.VMEM(lead + (rows, w), dtype) for w in widths]

    anywhere = pl.BlockSpec(memory_space=pl.ANY)
    moved = depth * 4 * rows * sum(widths)
    return pl.pallas_call(
        sum_kernel,
        out_shape=tuple(jax.ShapeDtypeStruct((rows, w), jnp.float32) for w in widths),
        in_specs=[anywhere] * 2,
        out_specs=(pl.BlockSpec(memory_space=pltpu.VMEM),) * 2,
        scratch_shapes=both(depth, 2, 2)
        + both(depth, 2, 2)
        + both(depth, 2)
        + both(depth)
        + both(depth - 1)
        + [
            pltpu.SemaphoreType.DMA((2, depth)),
            pltpu.SemaphoreType.DMA((2, 4, depth)),
            pltpu.SemaphoreType.DMA((2, 4, depth)),
        ],
        compiler_params=pltpu.CompilerParams(
            collective_id=2, has_side_effects=True, vmem_limit_bytes=60 * 2**20
        ),
        cost_estimate=pl.CostEstimate(
            flops=2 * moved, bytes_accessed=12 * moved, transcendentals=0
        ),
        name="sum_all_devices",
    )(first.reshape(depth, 2, 2, 2, rows, widths[0]), second.reshape(depth, 2, 2, 2, rows, widths[1]))


def over_tp(block, distance):
    devices = range(lax.axis_size("tp"))
    return lax.ppermute(block, "tp", [(i, i ^ distance) for i in devices])


def one_of(array, index, axis):
    return lax.dynamic_index_in_dim(array, index, axis, keepdims=False)


def sum_over_tp(part):
    rows, columns = part.shape
    tp = lax.axis_index("tp")
    x, c = tp // 2, tp % 2
    blocks = part.reshape(2, 2, rows // 4, columns)
    got = over_tp(one_of(blocks, 1 - c, 1).astype(jnp.bfloat16), 1)
    chip = one_of(blocks, c, 1).astype(jnp.float32) + got.astype(jnp.float32)
    got = over_tp(one_of(chip, 1 - x, 0).astype(jnp.bfloat16), 2)
    return one_of(chip, x, 0) + got.astype(jnp.float32)


def gather_over_tp(block):
    tp = lax.axis_index("tp")
    x, c = tp // 2, tp % 2
    got = over_tp(block, 2)
    pair = jnp.where(x == 0, jnp.stack([block, got]), jnp.stack([got, block]))
    got = over_tp(pair, 1)
    four = jnp.where(c == 0, jnp.stack([pair, got], axis=1), jnp.stack([got, pair], axis=1))
    return four.reshape(4 * block.shape[0], block.shape[1])


def weights_kernel(
    own_in, all_out, own_sem, z_send, z_recv, y_send, y_recv
):
    at = Place()
    depth = at.depth
    half = own_in.shape[0] // 2
    last = depth - 1

    def block(k, y, h):
        return all_out.at[at.z + k, y, pl.ds(h * half, half)]

    def z_copy(k, h, direction):
        if k == 0:
            src = own_in.at[pl.ds(h * half, half)]
        else:
            src = block(k, at.y, h)
        slot = last + k - direction
        return remote(
            src,
            block(k, at.y, h),
            z_send.at[last + k, h, (direction + 1) // 2],
            z_recv.at[slot, h],
            at.at_z(at.z + direction),
        )

    def z_arrival(k, h):
        direction = 1 if k > 0 else -1
        dst = block(k, at.y, h)
        return remote(
            dst, dst, z_send.at[last + k, h, 0], z_recv.at[last + k, h], at.at_z(at.z + direction)
        )

    def y_copy(k, h):
        src = own_in.at[pl.ds(h * half, half)] if k == 0 else block(k, at.y, h)
        return remote(
            src, block(k, at.y, h), y_send.at[last + k, h], y_recv.at[last + k, h], at.next_y
        )

    own_copy = pltpu.make_async_copy(own_in, all_out.at[at.z, at.y], own_sem)
    own_copy.start()
    has_up, has_down = at.z + 1 < depth, at.z > 0
    at.greet()

    for h in (0, 1):
        pl.when(has_up)(lambda: z_copy(0, h, 1).start())
        pl.when(has_down)(lambda: z_copy(0, h, -1).start())
        y_copy(0, h).start()
    for k in range(1, depth):
        for h in (0, 1):
            for sign in (-1, 1):
                there = at.z + sign * k
                exists = (there >= 0) & (there < depth)
                onward = at.z - sign
                goes_on = exists & (onward >= 0) & (onward < depth)

                @pl.when(exists)
                def _():
                    z_arrival(sign * k, h).wait_recv()

                @pl.when(goes_on)
                def _():
                    z_copy(sign * k, h, -sign).start()

                @pl.when(exists)
                def _():
                    y_copy(sign * k, h).start()

    own_copy.wait()
    for h in (0, 1):
        pl.when(has_up)(lambda: z_copy(0, h, 1).wait_send())
        pl.when(has_down)(lambda: z_copy(0, h, -1).wait_send())
    for k in range(-last, depth):
        there = at.z + k
        exists = (there >= 0) & (there < depth)
        sign = 1 if k > 0 else -1
        onward = at.z - sign
        goes_on = exists & (onward >= 0) & (onward < depth)
        for h in (0, 1):

            @pl.when(exists)
            def _():
                y_copy(k, h).wait()

            if k != 0:

                @pl.when(goes_on)
                def _():
                    z_copy(k, h, -sign).wait_send()


def gather_over_ep(block):
    rows, columns = block.shape
    depth = lax.axis_size("ep") // 2
    anywhere = pl.BlockSpec(memory_space=pl.ANY)
    slots = 2 * depth - 1
    out = pl.pallas_call(
        weights_kernel,
        out_shape=jax.ShapeDtypeStruct((depth, 2, rows, columns), block.dtype),
        in_specs=[anywhere],
        out_specs=anywhere,
        scratch_shapes=[
            pltpu.SemaphoreType.DMA,
            pltpu.SemaphoreType.DMA((slots, 2, 2)),
            pltpu.SemaphoreType.DMA((slots, 2)),
            pltpu.SemaphoreType.DMA((slots, 2)),
            pltpu.SemaphoreType.DMA((slots, 2)),
        ],
        compiler_params=pltpu.CompilerParams(collective_id=3, has_side_effects=True),
        cost_estimate=pl.CostEstimate(
            flops=0, bytes_accessed=8 * depth * rows * columns, transcendentals=0
        ),
        name="gather_weights",
    )(block)
    return out.reshape(2 * depth * rows, columns)


def grads_kernel(
    part_in, out, own, hop, from_z, load_sem, y_send, y_recv, z_send, z_recv
):
    at = Place()
    depth = at.depth
    rows = out.shape[0]
    half = rows // 2
    f32 = jnp.float32

    def part(h):
        return pl.ds(h * half, half)

    def load(j):
        return pltpu.make_async_copy(
            part_in.at[at.ahead(j), at.y], own.at[j], load_sem.at[j]
        )

    def y_copy(j, h):
        return remote(
            part_in.at[at.ahead(j), 1 - at.y, part(h)],
            hop.at[j, part(h)],
            y_send.at[j, h],
            y_recv.at[j, h],
            at.next_y,
        )

    def z_copy(j, h):
        return remote(
            own.at[j, part(h)],
            from_z.at[j - 1, part(h)],
            z_send.at[j, h],
            z_recv.at[j, h],
            at.at_z(at.ahead(j)),
        )

    order = [j for j in range(1, depth)] + [0]
    for j in order:
        load(j).start()
    at.greet()
    for j in order:
        for h in (0, 1):
            y_copy(j, h).start()
    step = 16
    for j in order:
        load(j).wait()
        for h in (0, 1):
            y_copy(j, h).wait_recv()

            def body(i, carry):
                some = pl.ds(pl.multiple_of(h * half + i * step, step), step)
                total = own[j, some].astype(f32) + hop[j, some].astype(f32)
                own[j, some] = total.astype(own.dtype)
                return carry

            lax.fori_loop(0, half // step, body, 0)
            if j > 0:
                z_copy(j, h).start()
    for h in (0, 1):
        for k in range(1, depth):
            z_copy(k, h).wait_recv()

        def body(i, carry):
            some = pl.ds(pl.multiple_of(h * half + i * step, step), step)
            total = own[0, some].astype(f32)
            for k in range(depth - 1):
                total = total + from_z[k, some].astype(f32)
            out[some] = total
            return carry

        lax.fori_loop(0, half // step, body, 0)
    for j in range(depth):
        for h in (0, 1):
            y_copy(j, h).wait_send()
            if j > 0:
                z_copy(j, h).wait_send()


def scatter_over_ep(parts):
    depth = lax.axis_size("ep") // 2
    rows, columns = parts.shape[0] // (2 * depth), parts.shape[1]
    dtype = parts.dtype
    return pl.pallas_call(
        grads_kernel,
        out_shape=jax.ShapeDtypeStruct((rows, columns), jnp.float32),
        in_specs=[pl.BlockSpec(memory_space=pl.ANY)],
        out_specs=pl.BlockSpec(memory_space=pltpu.VMEM),
        scratch_shapes=[
            pltpu.VMEM((depth, rows, columns), dtype),
            pltpu.VMEM((depth, rows, columns), dtype),
            pltpu.VMEM((depth - 1, rows, columns), dtype),
            pltpu.SemaphoreType.DMA((depth,)),
            pltpu.SemaphoreType.DMA((depth, 2)),
            pltpu.SemaphoreType.DMA((depth, 2)),
            pltpu.SemaphoreType.DMA((depth, 2)),
            pltpu.SemaphoreType.DMA((depth, 2)),
        ],
        compiler_params=pltpu.CompilerParams(
            collective_id=4, has_side_effects=True, vmem_limit_bytes=48 * 2**20
        ),
        cost_estimate=pl.CostEstimate(
            flops=2 * parts.size, bytes_accessed=6 * parts.size, transcendentals=0
        ),
        name="scatter_grads",
    )(parts.reshape(depth, 2, rows, columns))


def share_over_devices(weights, ep_count):
    rows, hidden = weights[0].shape
    units = hidden // ep_count
    pieces = jnp.concatenate(
        [weight.T.reshape(ep_count, units, rows) for weight in weights], axis=1
    )
    moved = lax.all_to_all(pieces, "ep", split_axis=0, concat_axis=0, tiled=True)
    moved = moved.transpose(1, 0, 2).reshape(len(weights), units, ep_count * rows)
    return [moved[i] for i in range(len(weights))]


def share_back(grads, ep_count):
    units, width = grads[0].shape
    columns = width // ep_count
    pieces = jnp.concatenate(grads, axis=0).reshape(len(grads) * units, ep_count, columns)
    moved = lax.all_to_all(
        pieces.transpose(1, 0, 2), "ep", split_axis=0, concat_axis=0, tiled=True
    )
    moved = moved.reshape(ep_count, len(grads), units, columns)
    return [moved[:, i].reshape(ep_count * units, columns).T for i in range(len(grads))]


def dense_body(
    tokens,
    lengths,
    routes,
    attn_gain,
    w_query,
    w_key,
    w_value,
    w_out,
    ffn_gain,
    w_router,
    shared_mix,
    shared_gate,
    shared_up,
    shared_down,
    expert_gate,
    expert_up,
    expert_down,
    cotangent,
):
    everywhere = ("ep", "tp")
    rows_here, width = tokens.shape
    ep_count = lax.axis_size("ep")
    tp_count = lax.axis_size("tp")
    ep_index = lax.axis_index("ep")
    offset = ep_index * rows_here
    quarter = rows_here // tp_count
    first_row = lax.axis_index("tp") * quarter
    slot_here, slot_hidden = expert_gate.shape[0], expert_gate.shape[1]
    expert_count = w_router.shape[1]
    bf16, f32 = jnp.bfloat16, jnp.float32

    def my_rows(array):
        return lax.dynamic_slice_in_dim(array, first_row, quarter, 0)

    side_columns = jnp.concatenate(
        [attn_gain[:, None], ffn_gain[:, None], shared_mix[:, None], w_router], axis=1
    )
    side_columns = jnp.pad(side_columns, ((0, 0), (0, -side_columns.shape[1] % 128)))
    joined_weights = gather_over_ep(
        jnp.concatenate([w_query, w_key, w_value, w_out, side_columns], axis=1)
    )
    heads_width = w_query.shape[1]
    qkv_weight = joined_weights[:, : 3 * heads_width]
    output_weight = joined_weights[:, 3 * heads_width : 4 * heads_width]
    side_weight = joined_weights[:, 4 * heads_width :]
    picked = jnp.any(
        my_rows(routes)[:, :, None] == jnp.arange(expert_count, dtype=jnp.int32), axis=1
    )
    picked_lanes = jnp.pad(picked.astype(bf16), ((0, 0), (3, 125 - expert_count)))
    upstream_all = lax.all_gather(
        jnp.concatenate([my_rows(cotangent), picked_lanes], axis=1), everywhere, axis=0, tiled=True
    )
    shared_rows = share_over_devices((shared_gate, shared_up, shared_down), ep_count)
    shared_units = shared_rows[0].shape[0]
    routed_units = slot_here * slot_hidden
    gate_cat, up_cat, down_cat = [
        jnp.pad(
            jnp.concatenate([expert.reshape(-1, width), shared], axis=0),
            ((0, -(routed_units + shared_units) % 128), (0, 0)),
        )
        for expert, shared in zip((expert_gate, expert_up, expert_down), shared_rows)
    ]

    heads_here = heads_width // HD
    score_scale = HD ** (-0.5)
    first_norm_scale = side_weight[:, 0].astype(f32)
    second_norm_scale = side_weight[:, 1].astype(f32)
    mix_f = side_weight[:, 2].astype(f32)
    router_f = side_weight[:, 3 : 3 + expert_count].astype(f32)
    layer_input = tokens.astype(f32)
    normed_wide, norm_one = norm_forward(layer_input, first_norm_scale)
    normed_one = normed_wide.astype(bf16)
    query_at = offset + jnp.arange(rows_here, dtype=jnp.int32)
    key_at = offset - 2 * rows_here + jnp.arange(3 * rows_here, dtype=jnp.int32)
    query_seg, query_pos = sequence_info(lengths, query_at)
    key_seg, _ = sequence_info(lengths, key_at)
    cosine, sine = rope_tables(query_pos, HD)
    projected = jnp.dot(normed_one, qkv_weight, preferred_element_type=f32)
    projected = projected.reshape(rows_here, 3, heads_here, HD)
    queries = rotate(projected[:, 0], cosine, sine).astype(bf16)
    keys = rotate(projected[:, 1], cosine, sine).astype(bf16)
    values = projected[:, 2].astype(bf16)
    carried = jnp.stack([keys, values], axis=0)
    joined = jnp.concatenate(
        [passed_along(carried, "ep", 2), passed_along(carried, "ep", 1), carried], axis=1
    )
    keys_win = joined[0]
    values_win = joined[1]
    allowed = (
        (query_seg[:, None] == key_seg[None, :])
        & (key_at[None, :] <= query_at[:, None])
        & (key_at[None, :] >= 0)
    )
    scores = (
        jnp.einsum("qhd,khd->hqk", queries, keys_win, preferred_element_type=f32) * score_scale
    )
    masked = jnp.where(allowed[None], scores, -1e30)
    peak = jnp.max(masked, axis=-1, keepdims=True)
    expo = jnp.exp(masked - peak)
    total = jnp.sum(expo, axis=-1, keepdims=True)
    log_total = peak + jnp.log(total)
    weights = expo / total
    attended = jnp.einsum(
        "hqk,khd->qhd", weights.astype(bf16), values_win, preferred_element_type=f32
    )
    attended = attended.reshape(rows_here, heads_width).astype(bf16)
    attn_part = jnp.einsum("th,dh->td", attended, output_weight, preferred_element_type=f32)
    resid = my_rows(layer_input) + sum_over_tp(attn_part)
    normed_two_wide, norm_two = norm_forward(resid, second_norm_scale)
    normed_two = normed_two_wide.astype(bf16)

    logits = jnp.dot(normed_two, side_weight, preferred_element_type=f32)
    router = jax.nn.softmax(logits[:, 3 : 3 + expert_count], axis=-1)
    mixer = jax.nn.sigmoid(logits[:, 2])
    normed_all, ffn_part, d_normed_part, weighted_h, d_gate_pre, d_up_pre = ffn_over_all(
        normed_two,
        upstream_all,
        gate_cat,
        up_cat,
        down_cat,
        side_weight,
        (slot_here, slot_hidden, shared_units),
        expert_count,
    )
    d_normed_sum, out_sum = sum_over_all(d_normed_part, ffn_part)
    ffn_sum = out_sum[:, :width]
    dots_sum = out_sum[:, width:]
    grad_gate_cat = jnp.einsum("tf,td->fd", d_gate_pre, normed_all, preferred_element_type=f32)
    grad_up_cat = jnp.einsum("tf,td->fd", d_up_pre, normed_all, preferred_element_type=f32)
    grad_down_cat = jnp.einsum(
        "tf,td->fd", weighted_h, upstream_all[:, :width], preferred_element_type=f32
    )
    grad_cats = (grad_gate_cat, grad_up_cat, grad_down_cat)
    grad_shared = share_back(
        [grad[routed_units : routed_units + shared_units].astype(bf16) for grad in grad_cats],
        ep_count,
    )
    grad_shared = [grad.astype(f32) for grad in grad_shared]
    grad_experts = [grad[:routed_units].reshape(expert_gate.shape) for grad in grad_cats]

    block_out = gather_over_tp((resid + ffn_sum).astype(bf16))
    d_router = jnp.where(picked, dots_sum[:, 3 : 3 + expert_count], 0.0)
    d_mixer = dots_sum[:, 2]
    d_logits = router * (d_router - jnp.sum(router * d_router, axis=-1, keepdims=True))
    d_mixlogit = d_mixer * mixer * (1.0 - mixer)
    side = jnp.dot(d_logits, router_f.T, precision=highest) + d_mixlogit[:, None] * mix_f[None, :]
    normed_two_f = normed_two.astype(f32)
    d_side = jnp.concatenate([d_mixlogit[:, None], d_logits], axis=1)
    grad_side = jnp.dot(normed_two_f.T, d_side, precision=highest)
    upstream = my_rows(cotangent).astype(f32)
    d_normed_two = d_normed_sum + side
    d_resid_norm, grad_gain_two = norm_backward(resid, norm_two, second_norm_scale, d_normed_two)
    d_resid = upstream + d_resid_norm
    d_resid_low = gather_over_tp(d_resid.astype(bf16))
    grad_out = jnp.einsum("td,th->dh", d_resid_low, attended, preferred_element_type=f32)
    grad_out = lax.psum_scatter(
        grad_out.astype(bf16), "ep", scatter_dimension=0, tiled=True
    ).astype(f32)
    d_attended = jnp.einsum("td,dh->th", d_resid_low, output_weight, preferred_element_type=f32)
    d_attended = d_attended.astype(bf16).reshape(rows_here, heads_here, HD)
    scores_again = (
        jnp.einsum("qhd,khd->hqk", queries, keys_win, preferred_element_type=f32) * score_scale
    )
    probs = jnp.where(allowed[None], jnp.exp(scores_again - log_total), 0.0)
    d_probs = jnp.einsum("qhd,khd->hqk", d_attended, values_win, preferred_element_type=f32)
    delta = jnp.sum(probs * d_probs, axis=-1, keepdims=True)
    d_scores = (probs * (d_probs - delta)).astype(bf16)
    d_keys_win = (
        jnp.einsum("hqk,qhd->khd", d_scores, queries, preferred_element_type=f32) * score_scale
    )
    d_values_win = jnp.einsum(
        "hqk,qhd->khd", probs.astype(bf16), d_attended, preferred_element_type=f32
    )
    pair_grads = jnp.stack([d_keys_win, d_values_win], axis=0)
    passed = pair_grads[:, : 2 * rows_here].astype(bf16)
    from_two = passed_along(passed[:, :rows_here], "ep", -2)
    from_one = passed_along(passed[:, rows_here:], "ep", -1)
    d_queries = (
        jnp.einsum("hqk,khd->qhd", d_scores, keys_win, preferred_element_type=f32) * score_scale
    )
    running = pair_grads[:, 2 * rows_here :] + from_one.astype(f32) + from_two.astype(f32)
    d_projected = jnp.concatenate(
        [
            unrotate(d_queries, cosine, sine).astype(bf16).reshape(rows_here, heads_width),
            unrotate(running[0], cosine, sine).astype(bf16).reshape(rows_here, heads_width),
            running[1].astype(bf16).reshape(rows_here, heads_width),
        ],
        axis=1,
    )
    d_normed_one = jnp.einsum("th,dh->td", d_projected, qkv_weight, preferred_element_type=f32)
    d_normed_one = sum_over_tp(d_normed_one)
    grad_qkv = jnp.einsum("td,th->dh", normed_one, d_projected, preferred_element_type=f32)
    d_input_norm, grad_gain_one = norm_backward(
        my_rows(layer_input), my_rows(norm_one), first_norm_scale, d_normed_one
    )
    grad_tokens = gather_over_tp((d_resid + d_input_norm).astype(bf16)).astype(f32)
    small = jnp.concatenate([grad_gain_one[:, None], grad_gain_two[:, None], grad_side], axis=1)
    small = jnp.pad(small, ((0, 0), (0, 128 - small.shape[1])))
    grad_weights = scatter_over_ep(jnp.concatenate([grad_qkv, small], axis=1).astype(bf16))
    small = grad_weights[:, 3 * heads_width :]
    small = small + over_tp(small, 1)
    small = small + over_tp(small, 2)
    parts = [grad_weights[:, i * heads_width : (i + 1) * heads_width] for i in range(3)]
    return (
        block_out,
        grad_tokens,
        small[:, 0],
        parts[0],
        parts[1],
        parts[2],
        grad_out,
        small[:, 1],
        small[:, 3 : 3 + expert_count],
        small[:, 2],
        grad_shared[0],
        grad_shared[1],
        grad_shared[2],
        grad_experts[0],
        grad_experts[1],
        grad_experts[2],
    )


def chosen_body(*arrays):
    rows_here, top_count = arrays[2].shape
    slot_here, expert_count = arrays[14].shape[0], arrays[9].shape[1]
    capacity = rows_here * top_count * 7 // (5 * expert_count)
    grid_of_two = lax.axis_size("ep") % 2 == 0 and lax.axis_size("tp") == 4
    if grid_of_two and rows_here < 2 * slot_here * capacity:
        return dense_body(*arrays)
    return body(*arrays)


def solution(mesh):
    placed = (
        P("ep", None),
        P(),
        P("ep", None),
        P("ep"),
        P("ep", "tp"),
        P("ep", "tp"),
        P("ep", "tp"),
        P("ep", "tp"),
        P("ep"),
        P("ep", None),
        P("ep"),
        P("ep", "tp"),
        P("ep", "tp"),
        P("ep", "tp"),
        P("ep", "tp", None),
        P("ep", "tp", None),
        P("ep", "tp", None),
        P("ep", None),
    )
    return jax.shard_map(
        chosen_body,
        mesh=mesh,
        in_specs=placed,
        out_specs=(
            P("ep", None),
            P("ep", None),
            P("ep"),
            P("ep", "tp"),
            P("ep", "tp"),
            P("ep", "tp"),
            P("ep", "tp"),
            P("ep"),
            P("ep", None),
            P("ep"),
            P("ep", "tp"),
            P("ep", "tp"),
            P("ep", "tp"),
            P("ep", "tp", None),
            P("ep", "tp", None),
            P("ep", "tp", None),
        ),
        check_vma=False,
    )
```

```python
import functools

import jax
import jax.numpy as jnp
from jax import lax
from jax.experimental import pallas as pl
from jax.experimental.pallas import tpu as pltpu
from jax.sharding import PartitionSpec as P

HD = 128


epsilon = 1e-06
rope_base = 1000000.0
highest = lax.Precision.HIGHEST
MESH = pl.DeviceIdType.MESH


def passed_along(block, axis, distance):
    devices = range(lax.axis_size(axis))
    route = [(i - distance, i) for i in devices if i - distance in devices]
    return lax.ppermute(block, axis, route)


def rope_tables(positions, width):
    steps = jnp.arange(0, width, 2, dtype=jnp.float32) / width
    inverse = rope_base ** (-steps)
    angles = positions.astype(jnp.float32)[:, None] * inverse[None, :]
    angles = jnp.concatenate([angles, angles], axis=-1)
    return (jnp.cos(angles)[:, None, :], jnp.sin(angles)[:, None, :])


def turn_half(values):
    middle = values.shape[-1] // 2
    return jnp.concatenate([-values[..., middle:], values[..., :middle]], axis=-1)


def rotate(values, cosine, sine):
    return values * cosine + turn_half(values) * sine


def unrotate(grads, cosine, sine):
    return grads * cosine - turn_half(grads * sine)


def sequence_info(lengths, indices):
    starts = jnp.cumsum(lengths) - lengths
    inside = starts[None, :] <= indices[:, None]
    segment = jnp.sum(inside.astype(jnp.int32), axis=1) - 1
    first = jnp.max(jnp.where(inside, starts[None, :], -1), axis=1)
    return (segment, indices - first)


def norm_forward(values, gain):
    scale = lax.rsqrt(jnp.mean(values * values, axis=-1, keepdims=True) + epsilon)
    return (values * scale * gain, scale)


def norm_backward(values, scale, gain, grads):
    unit = values * scale
    scaled = grads * gain
    inner = jnp.mean(scaled * unit, axis=-1, keepdims=True)
    return (scale * (scaled - unit * inner), jnp.sum(grads * unit, axis=0))


def deliver(rows):
    arrived_rows = lax.all_to_all(rows, "ep", split_axis=0, concat_axis=0, tiled=True)
    return arrived_rows


def bring_back(parts, target, rows_here, top_count):
    moved = lax.all_to_all(parts, "ep", split_axis=0, concat_axis=0, tiled=True)
    piece = moved.shape[3]
    return moved.reshape(-1, piece)[target].reshape(rows_here, top_count, piece)


def body(
    tokens,
    lengths,
    routes,
    attn_gain,
    w_query,
    w_key,
    w_value,
    w_out,
    ffn_gain,
    w_router,
    shared_mix,
    shared_gate,
    shared_up,
    shared_down,
    expert_gate,
    expert_up,
    expert_down,
    cotangent,
):
    rows_here = tokens.shape[0]
    width = tokens.shape[1]
    ep_count = lax.axis_size("ep")
    offset = lax.axis_index("ep") * rows_here
    slot_here = expert_gate.shape[0]
    top_count = routes.shape[1]
    gathered = (
        lax.all_gather(attn_gain, "ep", axis=0, tiled=True),
        lax.all_gather(w_query, "ep", axis=0, tiled=True),
        lax.all_gather(w_key, "ep", axis=0, tiled=True),
        lax.all_gather(w_value, "ep", axis=0, tiled=True),
        lax.all_gather(w_out, "ep", axis=0, tiled=True),
        lax.all_gather(ffn_gain, "ep", axis=0, tiled=True),
        lax.all_gather(w_router, "ep", axis=0, tiled=True),
        lax.all_gather(shared_mix, "ep", axis=0, tiled=True),
        lax.all_gather(shared_gate, "ep", axis=0, tiled=True),
        lax.all_gather(shared_up, "ep", axis=0, tiled=True),
        lax.all_gather(shared_down, "ep", axis=0, tiled=True),
    )
    (
        gain_first,
        query_weight_matrix,
        key_weight_matrix,
        value_weight_matrix,
        output_weight,
        gain_second,
        router_weight,
        shared_mixer_weight,
        shared_gate_weight,
        shared_up_weight,
        shared_down_weight,
    ) = gathered
    expert_count = router_weight.shape[1]
    capacity = (rows_here * top_count * 7 // (5 * expert_count) + 7) // 8 * 8
    heads_here = query_weight_matrix.shape[1] // HD
    score_scale = HD ** (-0.5)
    first_norm_scale = gain_first.astype(jnp.float32)
    second_norm_scale = gain_second.astype(jnp.float32)
    layer_input = tokens.astype(jnp.float32)
    normed_wide, norm_one = norm_forward(layer_input, first_norm_scale)
    normed_one = normed_wide.astype(jnp.bfloat16)
    query_at = offset + jnp.arange(rows_here, dtype=jnp.int32)
    key_at = offset - 2 * rows_here + jnp.arange(3 * rows_here, dtype=jnp.int32)
    query_seg, query_pos = sequence_info(lengths, query_at)
    key_seg, _ = sequence_info(lengths, key_at)
    cosine, sine = rope_tables(query_pos, HD)
    query_pre = jnp.dot(
        normed_one, query_weight_matrix, preferred_element_type=jnp.float32
    ).reshape(rows_here, heads_here, HD)
    key_pre = jnp.dot(normed_one, key_weight_matrix, preferred_element_type=jnp.float32).reshape(
        rows_here, heads_here, HD
    )
    queries = rotate(query_pre, cosine, sine).astype(jnp.bfloat16)
    keys = rotate(key_pre, cosine, sine).astype(jnp.bfloat16)
    values = (
        jnp.dot(normed_one, value_weight_matrix, preferred_element_type=jnp.float32)
        .astype(jnp.bfloat16)
        .reshape(rows_here, heads_here, HD)
    )
    carried = jnp.stack([keys, values], axis=0)
    window = [carried]
    for hop in range(2):
        carried = passed_along(carried, "ep", 1)
        window = [carried] + window
    joined = jnp.concatenate(window, axis=1)
    keys_win = joined[0]
    values_win = joined[1]
    allowed = (
        (query_seg[:, None] == key_seg[None, :])
        & (key_at[None, :] <= query_at[:, None])
        & (key_at[None, :] >= 0)
    )
    scores = (
        jnp.einsum("qhd,khd->hqk", queries, keys_win, preferred_element_type=jnp.float32)
        * score_scale
    )
    masked = jnp.where(allowed[None], scores, -1e30)
    peak = jnp.max(masked, axis=-1, keepdims=True)
    expo = jnp.exp(masked - peak)
    total = jnp.sum(expo, axis=-1, keepdims=True)
    log_total = peak + jnp.log(total)
    weights = expo / total
    attended = jnp.einsum(
        "hqk,khd->qhd", weights.astype(jnp.bfloat16), values_win, preferred_element_type=jnp.float32
    )
    attended = attended.reshape(rows_here, heads_here * HD).astype(jnp.bfloat16)
    attn_part = jnp.einsum("th,dh->td", attended, output_weight, preferred_element_type=jnp.float32)
    resid = layer_input + lax.psum(attn_part, "tp")
    normed_two_wide, norm_two = norm_forward(resid, second_norm_scale)
    normed_two = normed_two_wide.astype(jnp.bfloat16)
    normed_two_f = normed_two.astype(jnp.float32)
    router_f = router_weight.astype(jnp.float32)
    mix_f = shared_mixer_weight.astype(jnp.float32)
    router = jax.nn.softmax(jnp.dot(normed_two_f, router_f, precision=highest), axis=-1)
    picked = routes[:, :, None] == jnp.arange(expert_count, dtype=jnp.int32)[None, None, :]
    gates = jnp.sum(jnp.where(picked, router[:, None, :], 0.0), axis=-1)
    mixer = jax.nn.sigmoid(jnp.dot(normed_two_f, mix_f, precision=highest))
    shared_g = jnp.dot(normed_two, shared_gate_weight, preferred_element_type=jnp.float32)
    shared_u = jnp.dot(normed_two, shared_up_weight, preferred_element_type=jnp.float32)
    shared_h = (jax.nn.silu(shared_g) * shared_u).astype(jnp.bfloat16)
    shared_part = jnp.einsum(
        "tf,df->td", shared_h, shared_down_weight, preferred_element_type=jnp.float32
    )
    flat = routes.reshape(-1)
    hot = (flat[:, None] == jnp.arange(expert_count, dtype=jnp.int32)[None, :]).astype(jnp.int32)
    rank = jnp.sum(jnp.cumsum(hot, axis=0) * hot, axis=1) - 1
    target = flat * capacity + rank
    slot_total = ep_count * slot_here * capacity
    owner_route = (
        jnp.zeros((slot_total,), jnp.int32)
        .at[target]
        .set(jnp.arange(rows_here * top_count, dtype=jnp.int32))
    )
    filled = jnp.zeros((slot_total,), jnp.bool_).at[target].set(True)
    owner_token = owner_route // top_count
    send_rows = jnp.where(filled[:, None], normed_two[owner_token], jnp.zeros((), jnp.bfloat16))
    arrived_rows = deliver(send_rows.reshape(ep_count, slot_here, capacity, width))
    route_g = jnp.einsum(
        "nscd,sfd->nscf", arrived_rows, expert_gate, preferred_element_type=jnp.float32
    )
    route_u = jnp.einsum(
        "nscd,sfd->nscf", arrived_rows, expert_up, preferred_element_type=jnp.float32
    )
    route_h = (jax.nn.silu(route_g) * route_u).astype(jnp.bfloat16)
    route_part = jnp.einsum(
        "nscf,sfd->nscd", route_h, expert_down, preferred_element_type=jnp.float32
    )
    back_rows = bring_back(route_part, target, rows_here, top_count)
    upstream = cotangent.astype(jnp.float32)
    routed = jnp.sum(back_rows * gates[:, :, None], axis=1)
    ffn_part = mixer[:, None] * shared_part + routed
    route_dot = jnp.sum(back_rows * upstream[:, None, :], axis=-1)
    shared_dot = jnp.sum(shared_part * upstream, axis=-1)
    ffn_total, d_gate, d_mixer = lax.psum((ffn_part, route_dot, shared_dot), "tp")
    block_out = (resid + ffn_total).astype(jnp.bfloat16)
    d_router = jnp.sum(jnp.where(picked, d_gate[:, :, None], 0.0), axis=1)
    d_logits = router * (d_router - jnp.sum(router * d_router, axis=-1, keepdims=True))
    d_mixlogit = d_mixer * mixer * (1.0 - mixer)
    side = jnp.dot(d_logits, router_f.T, precision=highest) + d_mixlogit[:, None] * mix_f[None, :]
    grad_router = jnp.dot(normed_two_f.T, d_logits, precision=highest)
    grad_mix = jnp.dot(d_mixlogit, normed_two_f, precision=highest)
    d_shared = (mixer[:, None] * upstream).astype(jnp.bfloat16)
    d_sh = jnp.dot(d_shared, shared_down_weight, preferred_element_type=jnp.float32)
    sig_shared = jax.nn.sigmoid(shared_g)
    d_sg = (d_sh * shared_u * sig_shared * (1.0 + shared_g * (1.0 - sig_shared))).astype(
        jnp.bfloat16
    )
    d_su = (d_sh * shared_g * sig_shared).astype(jnp.bfloat16)
    d_normed_part = jnp.einsum(
        "tf,df->td", d_sg, shared_gate_weight, preferred_element_type=jnp.float32
    )
    d_normed_part = d_normed_part + jnp.einsum(
        "tf,df->td", d_su, shared_up_weight, preferred_element_type=jnp.float32
    )
    grad_sgate = jnp.einsum("td,tf->df", normed_two, d_sg, preferred_element_type=jnp.float32)
    grad_sup = jnp.einsum("td,tf->df", normed_two, d_su, preferred_element_type=jnp.float32)
    grad_sdown = jnp.einsum("td,tf->df", d_shared, shared_h, preferred_element_type=jnp.float32)
    d_route = (
        (gates[:, :, None] * upstream[:, None, :])
        .astype(jnp.bfloat16)
        .reshape(rows_here * top_count, width)
    )
    send_grads = jnp.where(filled[:, None], d_route[owner_route], jnp.zeros((), jnp.bfloat16))
    received_grads = deliver(send_grads.reshape(ep_count, slot_here, capacity, width))
    d_rh = jnp.einsum(
        "nscd,sfd->nscf", received_grads, expert_down, preferred_element_type=jnp.float32
    )
    sig_route = jax.nn.sigmoid(route_g)
    d_rg = (d_rh * route_u * sig_route * (1.0 + route_g * (1.0 - sig_route))).astype(jnp.bfloat16)
    routed_up_gradient = (d_rh * route_g * sig_route).astype(jnp.bfloat16)
    row_grads = jnp.einsum("nscf,sfd->nscd", d_rg, expert_gate, preferred_element_type=jnp.float32)
    row_grads = row_grads + jnp.einsum(
        "nscf,sfd->nscd", routed_up_gradient, expert_up, preferred_element_type=jnp.float32
    )
    grad_egate = jnp.einsum(
        "qxba,qxbr->xar", d_rg, arrived_rows, preferred_element_type=jnp.float32
    )
    expert_up_gradient = jnp.einsum(
        "qxba,qxbr->xar", routed_up_gradient, arrived_rows, preferred_element_type=jnp.float32
    )
    grad_edown = jnp.einsum(
        "qxba,qxbr->xar", route_h, received_grads, preferred_element_type=jnp.float32
    )
    grads_back = bring_back(row_grads, target, rows_here, top_count)
    d_routed = jnp.sum(grads_back, axis=1)
    d_normed_two = lax.psum(d_normed_part + d_routed, "tp") + side
    d_resid_norm, grad_gain_two = norm_backward(resid, norm_two, second_norm_scale, d_normed_two)
    d_resid = upstream + d_resid_norm
    d_resid_low = d_resid.astype(jnp.bfloat16)
    grad_outw = jnp.einsum("td,th->dh", d_resid_low, attended, preferred_element_type=jnp.float32)
    d_attended = jnp.einsum(
        "td,dh->th", d_resid_low, output_weight, preferred_element_type=jnp.float32
    )
    d_attended = d_attended.astype(jnp.bfloat16).reshape(rows_here, heads_here, HD)
    scores_again = (
        jnp.einsum("qhd,khd->hqk", queries, keys_win, preferred_element_type=jnp.float32)
        * score_scale
    )
    probs = jnp.where(allowed[None], jnp.exp(scores_again - log_total), 0.0)
    d_probs = jnp.einsum("qhd,khd->hqk", d_attended, values_win, preferred_element_type=jnp.float32)
    delta = jnp.sum(probs * d_probs, axis=-1, keepdims=True)
    d_scores = (probs * (d_probs - delta)).astype(jnp.bfloat16)
    d_queries = (
        jnp.einsum("hqk,khd->qhd", d_scores, keys_win, preferred_element_type=jnp.float32)
        * score_scale
    )
    d_keys_win = (
        jnp.einsum("hqk,qhd->khd", d_scores, queries, preferred_element_type=jnp.float32)
        * score_scale
    )
    d_values_win = jnp.einsum(
        "hqk,qhd->khd", probs.astype(jnp.bfloat16), d_attended, preferred_element_type=jnp.float32
    )
    pair_grads = jnp.stack([d_keys_win, d_values_win], axis=0)
    older = pair_grads[:, :rows_here]
    later = [pair_grads[:, rows_here : 2 * rows_here], pair_grads[:, 2 * rows_here :]]
    running = older
    for hop in range(2):
        running = passed_along(running, "ep", -1)
        running = running + later[hop]
    d_query_pre = (
        unrotate(d_queries, cosine, sine).astype(jnp.bfloat16).reshape(rows_here, heads_here * HD)
    )
    d_key_pre = (
        unrotate(running[0], cosine, sine).astype(jnp.bfloat16).reshape(rows_here, heads_here * HD)
    )
    d_values = running[1].astype(jnp.bfloat16).reshape(rows_here, heads_here * HD)
    grad_queryw = jnp.einsum(
        "td,th->dh", normed_one, d_query_pre, preferred_element_type=jnp.float32
    )
    grad_keyw = jnp.einsum("td,th->dh", normed_one, d_key_pre, preferred_element_type=jnp.float32)
    grad_valuew = jnp.einsum("td,th->dh", normed_one, d_values, preferred_element_type=jnp.float32)
    d_normed_one = jnp.einsum(
        "th,dh->td", d_query_pre, query_weight_matrix, preferred_element_type=jnp.float32
    )
    d_normed_one = d_normed_one + jnp.einsum(
        "th,dh->td", d_key_pre, key_weight_matrix, preferred_element_type=jnp.float32
    )
    d_normed_one = d_normed_one + jnp.einsum(
        "th,dh->td", d_values, value_weight_matrix, preferred_element_type=jnp.float32
    )
    d_normed_one = lax.psum(d_normed_one, "tp")
    d_input_norm, grad_gain_one = norm_backward(
        layer_input, norm_one, first_norm_scale, d_normed_one
    )
    grad_tokens = d_resid + d_input_norm
    summed = (
        lax.psum_scatter(grad_gain_one, "ep", scatter_dimension=0, tiled=True),
        lax.psum_scatter(grad_queryw, "ep", scatter_dimension=0, tiled=True),
        lax.psum_scatter(grad_keyw, "ep", scatter_dimension=0, tiled=True),
        lax.psum_scatter(grad_valuew, "ep", scatter_dimension=0, tiled=True),
        lax.psum_scatter(grad_outw, "ep", scatter_dimension=0, tiled=True),
        lax.psum_scatter(grad_gain_two, "ep", scatter_dimension=0, tiled=True),
        lax.psum_scatter(grad_router, "ep", scatter_dimension=0, tiled=True),
        lax.psum_scatter(grad_mix, "ep", scatter_dimension=0, tiled=True),
        lax.psum_scatter(grad_sgate, "ep", scatter_dimension=0, tiled=True),
        lax.psum_scatter(grad_sup, "ep", scatter_dimension=0, tiled=True),
        lax.psum_scatter(grad_sdown, "ep", scatter_dimension=0, tiled=True),
    )
    return (
        block_out,
        grad_tokens,
        summed[0],
        summed[1],
        summed[2],
        summed[3],
        summed[4],
        summed[5],
        summed[6],
        summed[7],
        summed[8],
        summed[9],
        summed[10],
        grad_egate,
        expert_up_gradient,
        grad_edown,
    )


class Place:
    def __init__(self):
        self.ep, self.tp = lax.axis_index("ep"), lax.axis_index("tp")
        self.z, self.y = self.ep // 2, self.ep % 2
        self.x, self.c = self.tp // 2, self.tp % 2
        self.depth = lax.axis_size("ep") // 2
        self.next_core = (self.ep, self.x * 2 + 1 - self.c)
        self.next_x = (self.ep, (1 - self.x) * 2 + self.c)
        self.next_y = (self.z * 2 + 1 - self.y, self.tp)

    def at_z(self, z):
        return (z * 2 + self.y, self.tp)

    def ahead(self, steps):
        return lax.rem(self.z + steps, self.depth)

    def behind(self, steps):
        return lax.rem(self.z + self.depth - steps, self.depth)

    def greet(self):
        barrier = pltpu.get_barrier_semaphore()
        peers = [self.next_core, self.next_x, self.next_y]
        peers += [self.at_z(self.ahead(k)) for k in range(1, self.depth)]
        for peer in peers:
            pl.semaphore_signal(barrier, inc=1, device_id=peer, device_id_type=MESH)
        pl.semaphore_wait(barrier, len(peers))


def remote(src, dst, send, recv, peer):
    return pltpu.make_async_remote_copy(
        src_ref=src, dst_ref=dst, send_sem=send, recv_sem=recv, device_id=peer, device_id_type=MESH
    )


def ffn_kernel(
    units,
    expert_count,
    rows_in,
    upstream_in,
    gate_in,
    up_in,
    down_in,
    side_in,
    rows_all,
    out_part,
    d_rows_part,
    weighted_out,
    d_gate_out,
    d_up_out,
    gate_w,
    up_w,
    down_w,
    side_w,
    rows_tile,
    upstream_tile,
    out_tile,
    d_rows_tile,
    weighted_tile,
    d_gate_tile,
    d_up_tile,
    weight_sem,
    own_sem,
    z_send,
    z_recv,
    plane_send,
    plane_recv,
    load_sem,
    store_sem,
):
    at = Place()
    depth = at.depth
    quarter = rows_in.shape[0]
    width = rows_in.shape[1]
    half = quarter // 2
    own, other_x = at.tp, (1 - at.x) * 2 + at.c

    def weight_copies():
        pairs = ((gate_in, gate_w), (up_in, up_w), (down_in, down_w), (side_in, side_w))
        return [
            pltpu.make_async_copy(src, dst, weight_sem.at[i]) for i, (src, dst) in enumerate(pairs)
        ]

    for copy in weight_copies():
        copy.start()

    def block(j, y, tp):
        return rows_all.at[at.behind(j), y, tp]

    def plane_copy(j, kind):
        y, other_y = at.y, 1 - at.y
        if kind == 0:
            src, peer = block(j, y, own), at.next_x
        elif kind == 1:
            src, peer = block(j, y, own), at.next_y
        elif kind == 2:
            src, peer = block(j, y, other_x).at[pl.ds(0, half)], at.next_y
        elif kind == 3:
            src, peer = block(j, other_y, own).at[pl.ds(half, half)], at.next_x
        else:
            src = block(j, other_y if kind >= 6 else y, other_x if kind % 2 else own)
            peer = at.next_core
        return remote(src, src, plane_send.at[j, kind], plane_recv.at[j, kind], peer)

    def z_copy(k):
        return remote(
            rows_in, block(0, at.y, own), z_send.at[k - 1], z_recv.at[k - 1], at.at_z(at.ahead(k))
        )

    def z_arrival(k):
        dst = block(k, at.y, own)
        return remote(dst, dst, z_send.at[k - 1], z_recv.at[k - 1], at.at_z(at.behind(k)))

    def begin(j):
        for kind in (0, 1, 4):
            plane_copy(j, kind).start()

    def spread(j):
        plane_copy(j, 0).wait_recv()
        plane_copy(j, 2).start()
        plane_copy(j, 5).start()
        plane_copy(j, 1).wait_recv()
        plane_copy(j, 3).start()
        plane_copy(j, 6).start()

    def begin_later(j):
        z_arrival(j).wait_recv()
        begin(j)

    def last_hop(j):
        plane_copy(j, 2).wait_recv()
        plane_copy(j, 3).wait_recv()
        plane_copy(j, 7).start()

    def near_ready(j):
        plane_copy(j, 4).wait_recv()
        plane_copy(j, 5).wait_recv()

    def far_ready(j):
        plane_copy(j, 6).wait_recv()
        plane_copy(j, 7).wait_recv()

    def tile_at(step):
        j = step // 2
        return at.behind(j), lax.rem(at.y + lax.rem(step, 2), 2)

    def load_rows(step):
        z, y = tile_at(step)
        slot = lax.rem(step, 2)
        return pltpu.make_async_copy(rows_all.at[z, y], rows_tile.at[slot], load_sem.at[0, slot])

    def load_upstream(step):
        z, y = tile_at(step)
        slot = lax.rem(step, 2)
        return pltpu.make_async_copy(
            upstream_in.at[z, y], upstream_tile.at[slot], load_sem.at[1, slot]
        )

    def stores(step):
        z, y = tile_at(step)
        slot = lax.rem(step, 2)
        pairs = (
            (out_tile, out_part),
            (d_rows_tile, d_rows_part),
            (weighted_tile, weighted_out),
            (d_gate_tile, d_gate_out),
            (d_up_tile, d_up_out),
        )
        return [
            pltpu.make_async_copy(src.at[slot], dst.at[z, y], store_sem.at[i, slot])
            for i, (src, dst) in enumerate(pairs)
        ]

    load_upstream(0).start()
    at.greet()
    for k in range(1, depth):
        z_copy(k).start()
    own_copy = pltpu.make_async_copy(rows_in, block(0, at.y, own), own_sem)
    own_copy.start()
    own_copy.wait()
    begin(0)
    spread(0)
    begin_later(1)
    near_ready(0)
    load_rows(0).start()
    for copy in weight_copies():
        copy.wait()

    tile = rows_tile.shape[1] * rows_tile.shape[2]
    hidden_total = gate_w.shape[0]
    lane = lax.broadcasted_iota(jnp.int32, (tile, 128), 1)
    unit = lax.broadcasted_iota(jnp.int32, (1, hidden_total), 1)
    slot_here, slot_hidden, shared_hidden = units
    routed = slot_here * slot_hidden
    across = (((1,), (1,)), ((), ()))
    f32, bf16 = jnp.float32, jnp.bfloat16

    def step_body(step, carry):
        slot = lax.rem(step, 2)
        load_upstream(step).wait()

        @pl.when(step + 1 < 2 * depth)
        def _():
            load_upstream(step + 1).start()

        upstream = upstream_tile[slot].reshape(tile, upstream_tile.shape[-1])
        d_hidden = lax.dot_general(
            upstream[:, :width], down_w[...], across, preferred_element_type=f32
        )
        load_rows(step).wait()
        rows = rows_tile[slot].reshape(tile, width)
        logits = jnp.dot(rows, side_w[...], preferred_element_type=f32)
        chooses = (lane >= 3) & (lane < 3 + expert_count)
        peak = jnp.max(jnp.where(chooses, logits, -1e30), axis=1, keepdims=True)
        expo = jnp.where(chooses, jnp.exp(jnp.where(chooses, logits, peak) - peak), 0.0)
        router = expo / jnp.sum(expo, axis=1, keepdims=True)
        routed_gate = router * upstream[:, width:].astype(f32)
        mix_pre = jnp.sum(jnp.where(lane == 2, logits, 0.0), axis=1, keepdims=True)
        mixer = 1.0 / (1.0 + jnp.exp(-mix_pre))
        factor = jnp.where(unit < routed + shared_hidden, mixer, 0.0)
        for s in range(slot_here):
            chosen = lane == 3 + at.ep * slot_here + s
            gate = jnp.sum(jnp.where(chosen, routed_gate, 0.0), axis=1, keepdims=True)
            inside = (unit >= s * slot_hidden) & (unit < (s + 1) * slot_hidden)
            factor = jnp.where(inside, gate, factor)
        gate_pre = lax.dot_general(rows, gate_w[...], across, preferred_element_type=f32)
        up_pre = lax.dot_general(rows, up_w[...], across, preferred_element_type=f32)

        @pl.when(step >= 2)
        def _():
            for copy in stores(step - 2):
                copy.wait()

        sig = 1.0 / (1.0 + jnp.exp(-gate_pre))
        silu = gate_pre * sig
        hidden = silu * up_pre
        product = hidden * d_hidden
        gated = factor * d_hidden
        weighted_tile[slot] = (factor * hidden).astype(bf16)
        d_gate_tile[slot] = (gated * up_pre * (sig + silu * (1.0 - sig))).astype(bf16)
        d_up_tile[slot] = (gated * silu).astype(bf16)
        dots = jnp.zeros((tile, 128), f32)
        for s in range(slot_here + 1):
            last = s == slot_here
            inside = unit >= s * slot_hidden
            if not last:
                inside = inside & (unit < (s + 1) * slot_hidden)
            dot = jnp.sum(jnp.where(inside, product, 0.0), axis=1, keepdims=True)
            where = lane == (2 if last else 3 + at.ep * slot_here + s)
            dots = jnp.where(where, dot, dots)
        out = jnp.dot(weighted_tile[slot], down_w[...], preferred_element_type=f32)
        out_tile[slot, :, :, :width] = out.astype(bf16).reshape(rows_tile.shape[1:])
        out_tile[slot, :, :, width:] = dots.astype(bf16).reshape(rows_tile.shape[1:3] + (128,))
        d_rows = jnp.dot(d_gate_tile[slot], gate_w[...], preferred_element_type=f32)
        d_rows = d_rows + jnp.dot(d_up_tile[slot], up_w[...], preferred_element_type=f32)
        d_rows_tile[slot] = d_rows.astype(bf16).reshape(rows_tile.shape[1:])
        for copy in stores(step):
            copy.start()
        j = step // 2
        even = lax.rem(step, 2) == 0

        @pl.when(even)
        def _():
            last_hop(j)

            @pl.when(j + 1 < depth)
            def _():
                spread(j + 1)

            @pl.when(j + 2 < depth)
            def _():
                begin_later(j + 2)

            far_ready(j)
            load_rows(step + 1).start()

        @pl.when(jnp.logical_not(even) & (j + 1 < depth))
        def _():
            near_ready(j + 1)
            load_rows(step + 1).start()

        return carry

    lax.fori_loop(0, 2 * depth, step_body, 0)
    for step in (2 * depth - 2, 2 * depth - 1):
        for copy in stores(step):
            copy.wait()
    for k in range(1, depth):
        z_copy(k).wait_send()

    def finish(j, carry):
        for kind in range(8):
            plane_copy(j, kind).wait_send()
        return carry

    lax.fori_loop(0, depth, finish, 0)


def ffn_over_all(rows, upstream_all, gate_w, up_w, down_w, side_w, units, expert_count):
    quarter, width = rows.shape
    ep_count, tp_count = lax.axis_size("ep"), lax.axis_size("tp")
    depth = ep_count // 2
    hidden = gate_w.shape[0]
    bf16 = jnp.bfloat16
    upstream_all = upstream_all.reshape(depth, 2, tp_count, quarter, upstream_all.shape[-1])
    block = (depth, 2, tp_count, quarter)
    tile_rows = tp_count * quarter
    hidden_shape = jax.ShapeDtypeStruct((depth, 2, tile_rows, hidden), bf16)
    anywhere = pl.BlockSpec(memory_space=pl.ANY)
    tokens = ep_count * tile_rows
    outs = pl.pallas_call(
        functools.partial(ffn_kernel, units, expert_count),
        out_shape=(
            jax.ShapeDtypeStruct(block + (width,), bf16),
            jax.ShapeDtypeStruct(block + (width + 128,), bf16),
            jax.ShapeDtypeStruct(block + (width,), bf16),
            hidden_shape,
            hidden_shape,
            hidden_shape,
        ),
        in_specs=[anywhere] * 6,
        out_specs=(anywhere,) * 6,
        scratch_shapes=[
            pltpu.VMEM((hidden, width), bf16),
            pltpu.VMEM((hidden, width), bf16),
            pltpu.VMEM((hidden, width), bf16),
            pltpu.VMEM((width, 128), bf16),
            pltpu.VMEM((2, tp_count, quarter, width), bf16),
            pltpu.VMEM((2, tp_count, quarter, width + 128), bf16),
            pltpu.VMEM((2, tp_count, quarter, width + 128), bf16),
            pltpu.VMEM((2, tp_count, quarter, width), bf16),
            pltpu.VMEM((2, tile_rows, hidden), bf16),
            pltpu.VMEM((2, tile_rows, hidden), bf16),
            pltpu.VMEM((2, tile_rows, hidden), bf16),
            pltpu.SemaphoreType.DMA((4,)),
            pltpu.SemaphoreType.DMA,
            pltpu.SemaphoreType.DMA((depth - 1,)),
            pltpu.SemaphoreType.DMA((depth - 1,)),
            pltpu.SemaphoreType.DMA((depth, 8)),
            pltpu.SemaphoreType.DMA((depth, 8)),
            pltpu.SemaphoreType.DMA((2, 2)),
            pltpu.SemaphoreType.DMA((5, 2)),
        ],
        compiler_params=pltpu.CompilerParams(
            collective_id=1, has_side_effects=True, vmem_limit_bytes=60 * 2**20
        ),
        cost_estimate=pl.CostEstimate(
            flops=12 * tokens * width * hidden,
            bytes_accessed=10 * tokens * width,
            transcendentals=tokens * hidden,
        ),
        name="ffn_all_tokens",
    )(rows, upstream_all, gate_w, up_w, down_w, side_w)
    rows_all, out_part, d_rows_part, weighted, d_gate, d_up = outs
    return (
        rows_all.reshape(tokens, width),
        out_part,
        d_rows_part,
        weighted.reshape(tokens, hidden),
        d_gate.reshape(tokens, hidden),
        d_up.reshape(tokens, hidden),
    )


def sum_kernel(
    first_in,
    second_in,
    first_out,
    second_out,
    first_own,
    second_own,
    first_core,
    second_core,
    first_hop,
    second_hop,
    first_hop2,
    second_hop2,
    first_z,
    second_z,
    load_sem,
    send_sem,
    recv_sem,
):
    at = Place()
    depth = at.depth
    f32 = jnp.float32

    def to(j):
        return at.ahead(j)

    ins, owns = (first_in, second_in), (first_own, second_own)
    cores, hops = (first_core, second_core), (first_hop, second_hop)
    hops2, zs = (first_hop2, second_hop2), (first_z, second_z)

    def load(a, j):
        return pltpu.make_async_copy(
            ins[a].at[to(j), :, :, at.c], owns[a].at[j], load_sem.at[a, j]
        )

    def core_copy(a, j):
        return remote(
            ins[a].at[to(j), :, :, 1 - at.c],
            cores[a].at[j],
            send_sem.at[a, 0, j],
            recv_sem.at[a, 0, j],
            at.next_core,
        )

    def hop_copy(a, j):
        src = owns[0].at[j, :, 1 - at.x] if a == 0 else owns[1].at[j, 1 - at.y]
        peer = at.next_x if a == 0 else at.next_y
        return remote(src, hops[a].at[j], send_sem.at[a, 1, j], recv_sem.at[a, 1, j], peer)

    def hop2_copy(a, j):
        src = owns[0].at[j, 1 - at.y, at.x] if a == 0 else owns[1].at[j, at.y, 1 - at.x]
        peer = at.next_y if a == 0 else at.next_x
        return remote(src, hops2[a].at[j], send_sem.at[a, 2, j], recv_sem.at[a, 2, j], peer)

    def z_copy(a, j):
        return remote(
            owns[a].at[j, at.y, at.x],
            zs[a].at[j - 1],
            send_sem.at[a, 3, j],
            recv_sem.at[a, 3, j],
            at.at_z(to(j)),
        )

    def add(into, other):
        rows = into.shape[0]
        step = 32

        def body(i, carry):
            part = pl.ds(pl.multiple_of(i * step, step), step)
            into[part] = (into[part].astype(f32) + other[part].astype(f32)).astype(into.dtype)
            return carry

        lax.fori_loop(0, rows // step, body, 0)

    def after_core(a, j):
        load(a, j).wait()
        core_copy(a, j).wait_recv()

        def body(i, carry):
            moved, other = 1 - i // 2, lax.rem(i, 2)
            if a == 0:
                y, x = other, lax.rem(at.x + moved, 2)
            else:
                y, x = lax.rem(at.y + moved, 2), other
            add(owns[a].at[j, y, x], cores[a].at[j, y, x])
            return carry

        lax.fori_loop(0, 2, body, 0)
        hop_copy(a, j).start()
        lax.fori_loop(2, 4, body, 0)

    def after_hop(a, j):
        hop_copy(a, j).wait_recv()
        for moved in (1, 0):
            if a == 0:
                y = lax.rem(at.y + moved, 2)
                add(owns[0].at[j, y, at.x], hops[0].at[j, y])
            else:
                x = lax.rem(at.x + moved, 2)
                add(owns[1].at[j, at.y, x], hops[1].at[j, x])
            if moved:
                hop2_copy(a, j).start()

    def after_hop2(a, j):
        hop2_copy(a, j).wait_recv()
        add(owns[a].at[j, at.y, at.x], hops2[a].at[j])
        if j > 0:
            z_copy(a, j).start()

    order = [j for j in range(1, depth)] + [0]
    for j in order:
        for a in (0, 1):
            load(a, j).start()
    at.greet()
    for j in order:
        for a in (0, 1):
            core_copy(a, j).start()
    for turn in range(depth + 2):
        for a in (0, 1):
            if turn < depth:
                after_core(a, order[turn])
        for a in (0, 1):
            if 0 <= turn - 1 < depth:
                after_hop(a, order[turn - 1])
        for a in (0, 1):
            if 0 <= turn - 2 < depth:
                after_hop2(a, order[turn - 2])
    for a, out in ((0, first_out), (1, second_out)):
        for k in range(1, depth):
            z_copy(a, k).wait_recv()
        rows = out.shape[0]
        step = 32

        def body(i, carry):
            part = pl.ds(pl.multiple_of(i * step, step), step)
            total = owns[a][0, at.y, at.x, part].astype(f32)
            for k in range(depth - 1):
                total = total + zs[a][k, part].astype(f32)
            out[part] = total
            return carry

        lax.fori_loop(0, rows // step, body, 0)
    for a in (0, 1):
        for j in range(depth):
            core_copy(a, j).wait_send()
            hop_copy(a, j).wait_send()
            hop2_copy(a, j).wait_send()
            if j > 0:
                z_copy(a, j).wait_send()


def sum_over_all(first, second):
    depth, _, _, rows, _ = first.shape
    widths = (first.shape[-1], second.shape[-1])
    dtype = first.dtype

    def both(*lead):
        return [pltpu.VMEM(lead + (rows, w), dtype) for w in widths]

    anywhere = pl.BlockSpec(memory_space=pl.ANY)
    moved = depth * 4 * rows * sum(widths)
    return pl.pallas_call(
        sum_kernel,
        out_shape=tuple(jax.ShapeDtypeStruct((rows, w), jnp.float32) for w in widths),
        in_specs=[anywhere] * 2,
        out_specs=(pl.BlockSpec(memory_space=pltpu.VMEM),) * 2,
        scratch_shapes=both(depth, 2, 2)
        + both(depth, 2, 2)
        + both(depth, 2)
        + both(depth)
        + both(depth - 1)
        + [
            pltpu.SemaphoreType.DMA((2, depth)),
            pltpu.SemaphoreType.DMA((2, 4, depth)),
            pltpu.SemaphoreType.DMA((2, 4, depth)),
        ],
        compiler_params=pltpu.CompilerParams(
            collective_id=2, has_side_effects=True, vmem_limit_bytes=60 * 2**20
        ),
        cost_estimate=pl.CostEstimate(
            flops=2 * moved, bytes_accessed=12 * moved, transcendentals=0
        ),
        name="sum_all_devices",
    )(first.reshape(depth, 2, 2, 2, rows, widths[0]), second.reshape(depth, 2, 2, 2, rows, widths[1]))


def over_tp(block, distance):
    devices = range(lax.axis_size("tp"))
    return lax.ppermute(block, "tp", [(i, i ^ distance) for i in devices])


def one_of(array, index, axis):
    return lax.dynamic_index_in_dim(array, index, axis, keepdims=False)


def sum_over_tp(part):
    rows, columns = part.shape
    tp = lax.axis_index("tp")
    x, c = tp // 2, tp % 2
    blocks = part.reshape(2, 2, rows // 4, columns)
    got = over_tp(one_of(blocks, 1 - c, 1).astype(jnp.bfloat16), 1)
    chip = one_of(blocks, c, 1).astype(jnp.float32) + got.astype(jnp.float32)
    got = over_tp(one_of(chip, 1 - x, 0).astype(jnp.bfloat16), 2)
    return one_of(chip, x, 0) + got.astype(jnp.float32)


def gather_over_tp(block):
    tp = lax.axis_index("tp")
    x, c = tp // 2, tp % 2
    got = over_tp(block, 2)
    pair = jnp.where(x == 0, jnp.stack([block, got]), jnp.stack([got, block]))
    got = over_tp(pair, 1)
    four = jnp.where(c == 0, jnp.stack([pair, got], axis=1), jnp.stack([got, pair], axis=1))
    return four.reshape(4 * block.shape[0], block.shape[1])


def weights_kernel(
    own_in, all_out, own_sem, z_send, z_recv, y_send, y_recv
):
    at = Place()
    depth = at.depth
    half = own_in.shape[0] // 2
    last = depth - 1

    def block(k, y, h):
        return all_out.at[at.z + k, y, pl.ds(h * half, half)]

    def z_copy(k, h, direction):
        if k == 0:
            src = own_in.at[pl.ds(h * half, half)]
        else:
            src = block(k, at.y, h)
        slot = last + k - direction
        return remote(
            src,
            block(k, at.y, h),
            z_send.at[last + k, h, (direction + 1) // 2],
            z_recv.at[slot, h],
            at.at_z(at.z + direction),
        )

    def z_arrival(k, h):
        direction = 1 if k > 0 else -1
        dst = block(k, at.y, h)
        return remote(
            dst, dst, z_send.at[last + k, h, 0], z_recv.at[last + k, h], at.at_z(at.z + direction)
        )

    def y_copy(k, h):
        src = own_in.at[pl.ds(h * half, half)] if k == 0 else block(k, at.y, h)
        return remote(
            src, block(k, at.y, h), y_send.at[last + k, h], y_recv.at[last + k, h], at.next_y
        )

    own_copy = pltpu.make_async_copy(own_in, all_out.at[at.z, at.y], own_sem)
    own_copy.start()
    has_up, has_down = at.z + 1 < depth, at.z > 0
    at.greet()

    for h in (0, 1):
        pl.when(has_up)(lambda: z_copy(0, h, 1).start())
        pl.when(has_down)(lambda: z_copy(0, h, -1).start())
        y_copy(0, h).start()
    for k in range(1, depth):
        for h in (0, 1):
            for sign in (-1, 1):
                there = at.z + sign * k
                exists = (there >= 0) & (there < depth)
                onward = at.z - sign
                goes_on = exists & (onward >= 0) & (onward < depth)

                @pl.when(exists)
                def _():
                    z_arrival(sign * k, h).wait_recv()

                @pl.when(goes_on)
                def _():
                    z_copy(sign * k, h, -sign).start()

                @pl.when(exists)
                def _():
                    y_copy(sign * k, h).start()

    own_copy.wait()
    for h in (0, 1):
        pl.when(has_up)(lambda: z_copy(0, h, 1).wait_send())
        pl.when(has_down)(lambda: z_copy(0, h, -1).wait_send())
    for k in range(-last, depth):
        there = at.z + k
        exists = (there >= 0) & (there < depth)
        sign = 1 if k > 0 else -1
        onward = at.z - sign
        goes_on = exists & (onward >= 0) & (onward < depth)
        for h in (0, 1):

            @pl.when(exists)
            def _():
                y_copy(k, h).wait()

            if k != 0:

                @pl.when(goes_on)
                def _():
                    z_copy(k, h, -sign).wait_send()


def gather_over_ep(block):
    rows, columns = block.shape
    depth = lax.axis_size("ep") // 2
    anywhere = pl.BlockSpec(memory_space=pl.ANY)
    slots = 2 * depth - 1
    out = pl.pallas_call(
        weights_kernel,
        out_shape=jax.ShapeDtypeStruct((depth, 2, rows, columns), block.dtype),
        in_specs=[anywhere],
        out_specs=anywhere,
        scratch_shapes=[
            pltpu.SemaphoreType.DMA,
            pltpu.SemaphoreType.DMA((slots, 2, 2)),
            pltpu.SemaphoreType.DMA((slots, 2)),
            pltpu.SemaphoreType.DMA((slots, 2)),
            pltpu.SemaphoreType.DMA((slots, 2)),
        ],
        compiler_params=pltpu.CompilerParams(collective_id=3, has_side_effects=True),
        cost_estimate=pl.CostEstimate(
            flops=0, bytes_accessed=8 * depth * rows * columns, transcendentals=0
        ),
        name="gather_weights",
    )(block)
    return out.reshape(2 * depth * rows, columns)


def grads_kernel(
    part_in, out, own, hop, from_z, load_sem, y_send, y_recv, z_send, z_recv
):
    at = Place()
    depth = at.depth
    rows = out.shape[0]
    half = rows // 2
    f32 = jnp.float32

    def part(h):
        return pl.ds(h * half, half)

    def load(j):
        return pltpu.make_async_copy(
            part_in.at[at.ahead(j), at.y], own.at[j], load_sem.at[j]
        )

    def y_copy(j, h):
        return remote(
            part_in.at[at.ahead(j), 1 - at.y, part(h)],
            hop.at[j, part(h)],
            y_send.at[j, h],
            y_recv.at[j, h],
            at.next_y,
        )

    def z_copy(j, h):
        return remote(
            own.at[j, part(h)],
            from_z.at[j - 1, part(h)],
            z_send.at[j, h],
            z_recv.at[j, h],
            at.at_z(at.ahead(j)),
        )

    order = [j for j in range(1, depth)] + [0]
    for j in order:
        load(j).start()
    at.greet()
    for j in order:
        for h in (0, 1):
            y_copy(j, h).start()
    step = 16
    for j in order:
        load(j).wait()
        for h in (0, 1):
            y_copy(j, h).wait_recv()

            def body(i, carry):
                some = pl.ds(pl.multiple_of(h * half + i * step, step), step)
                total = own[j, some].astype(f32) + hop[j, some].astype(f32)
                own[j, some] = total.astype(own.dtype)
                return carry

            lax.fori_loop(0, half // step, body, 0)
            if j > 0:
                z_copy(j, h).start()
    for h in (0, 1):
        for k in range(1, depth):
            z_copy(k, h).wait_recv()

        def body(i, carry):
            some = pl.ds(pl.multiple_of(h * half + i * step, step), step)
            total = own[0, some].astype(f32)
            for k in range(depth - 1):
                total = total + from_z[k, some].astype(f32)
            out[some] = total
            return carry

        lax.fori_loop(0, half // step, body, 0)
    for j in range(depth):
        for h in (0, 1):
            y_copy(j, h).wait_send()
            if j > 0:
                z_copy(j, h).wait_send()


def scatter_over_ep(parts):
    depth = lax.axis_size("ep") // 2
    rows, columns = parts.shape[0] // (2 * depth), parts.shape[1]
    dtype = parts.dtype
    return pl.pallas_call(
        grads_kernel,
        out_shape=jax.ShapeDtypeStruct((rows, columns), jnp.float32),
        in_specs=[pl.BlockSpec(memory_space=pl.ANY)],
        out_specs=pl.BlockSpec(memory_space=pltpu.VMEM),
        scratch_shapes=[
            pltpu.VMEM((depth, rows, columns), dtype),
            pltpu.VMEM((depth, rows, columns), dtype),
            pltpu.VMEM((depth - 1, rows, columns), dtype),
            pltpu.SemaphoreType.DMA((depth,)),
            pltpu.SemaphoreType.DMA((depth, 2)),
            pltpu.SemaphoreType.DMA((depth, 2)),
            pltpu.SemaphoreType.DMA((depth, 2)),
            pltpu.SemaphoreType.DMA((depth, 2)),
        ],
        compiler_params=pltpu.CompilerParams(
            collective_id=4, has_side_effects=True, vmem_limit_bytes=48 * 2**20
        ),
        cost_estimate=pl.CostEstimate(
            flops=2 * parts.size, bytes_accessed=6 * parts.size, transcendentals=0
        ),
        name="scatter_grads",
    )(parts.reshape(depth, 2, rows, columns))


def share_over_devices(weights, ep_count):
    rows, hidden = weights[0].shape
    units = hidden // ep_count
    pieces = jnp.concatenate(
        [weight.T.reshape(ep_count, units, rows) for weight in weights], axis=1
    )
    moved = lax.all_to_all(pieces, "ep", split_axis=0, concat_axis=0, tiled=True)
    moved = moved.transpose(1, 0, 2).reshape(len(weights), units, ep_count * rows)
    return [moved[i] for i in range(len(weights))]


def share_back(grads, ep_count):
    units, width = grads[0].shape
    columns = width // ep_count
    pieces = jnp.concatenate(grads, axis=0).reshape(len(grads) * units, ep_count, columns)
    moved = lax.all_to_all(
        pieces.transpose(1, 0, 2), "ep", split_axis=0, concat_axis=0, tiled=True
    )
    moved = moved.reshape(ep_count, len(grads), units, columns)
    return [moved[:, i].reshape(ep_count * units, columns).T for i in range(len(grads))]


def dense_body(
    tokens,
    lengths,
    routes,
    attn_gain,
    w_query,
    w_key,
    w_value,
    w_out,
    ffn_gain,
    w_router,
    shared_mix,
    shared_gate,
    shared_up,
    shared_down,
    expert_gate,
    expert_up,
    expert_down,
    cotangent,
):
    everywhere = ("ep", "tp")
    rows_here, width = tokens.shape
    ep_count = lax.axis_size("ep")
    tp_count = lax.axis_size("tp")
    ep_index = lax.axis_index("ep")
    offset = ep_index * rows_here
    quarter = rows_here // tp_count
    first_row = lax.axis_index("tp") * quarter
    slot_here, slot_hidden = expert_gate.shape[0], expert_gate.shape[1]
    expert_count = w_router.shape[1]
    bf16, f32 = jnp.bfloat16, jnp.float32

    def my_rows(array):
        return lax.dynamic_slice_in_dim(array, first_row, quarter, 0)

    side_columns = jnp.concatenate(
        [attn_gain[:, None], ffn_gain[:, None], shared_mix[:, None], w_router], axis=1
    )
    side_columns = jnp.pad(side_columns, ((0, 0), (0, -side_columns.shape[1] % 128)))
    joined_weights = gather_over_ep(
        jnp.concatenate([w_query, w_key, w_value, w_out, side_columns], axis=1)
    )
    cotangent_rows = my_rows(cotangent)
    joined_weights, cotangent_rows, shared_gate, shared_up, shared_down = lax.optimization_barrier(
        (joined_weights, cotangent_rows, shared_gate, shared_up, shared_down)
    )
    heads_width = w_query.shape[1]
    qkv_weight = joined_weights[:, : 3 * heads_width]
    output_weight = joined_weights[:, 3 * heads_width : 4 * heads_width]
    side_weight = joined_weights[:, 4 * heads_width :]
    picked = jnp.any(
        my_rows(routes)[:, :, None] == jnp.arange(expert_count, dtype=jnp.int32), axis=1
    )
    picked_lanes = jnp.pad(picked.astype(bf16), ((0, 0), (3, 125 - expert_count)))
    upstream_all = lax.all_gather(
        jnp.concatenate([cotangent_rows, picked_lanes], axis=1), everywhere, axis=0, tiled=True
    )
    shared_rows = share_over_devices((shared_gate, shared_up, shared_down), ep_count)
    shared_units = shared_rows[0].shape[0]
    routed_units = slot_here * slot_hidden
    gate_cat, up_cat, down_cat = [
        jnp.pad(
            jnp.concatenate([expert.reshape(-1, width), shared], axis=0),
            ((0, -(routed_units + shared_units) % 128), (0, 0)),
        )
        for expert, shared in zip((expert_gate, expert_up, expert_down), shared_rows)
    ]

    heads_here = heads_width // HD
    score_scale = HD ** (-0.5)
    first_norm_scale = side_weight[:, 0].astype(f32)
    second_norm_scale = side_weight[:, 1].astype(f32)
    mix_f = side_weight[:, 2].astype(f32)
    router_f = side_weight[:, 3 : 3 + expert_count].astype(f32)
    layer_input = tokens.astype(f32)
    normed_wide, norm_one = norm_forward(layer_input, first_norm_scale)
    normed_one = normed_wide.astype(bf16)
    query_at = offset + jnp.arange(rows_here, dtype=jnp.int32)
    key_at = offset - 2 * rows_here + jnp.arange(3 * rows_here, dtype=jnp.int32)
    query_seg, query_pos = sequence_info(lengths, query_at)
    key_seg, _ = sequence_info(lengths, key_at)
    cosine, sine = rope_tables(query_pos, HD)
    projected = jnp.dot(normed_one, qkv_weight, preferred_element_type=f32)
    projected = projected.reshape(rows_here, 3, heads_here, HD)
    queries = rotate(projected[:, 0], cosine, sine).astype(bf16)
    keys = rotate(projected[:, 1], cosine, sine).astype(bf16)
    values = projected[:, 2].astype(bf16)
    carried = jnp.stack([keys, values], axis=0)
    joined = jnp.concatenate(
        [passed_along(carried, "ep", 2), passed_along(carried, "ep", 1), carried], axis=1
    )
    joined, gate_cat, up_cat, down_cat = lax.optimization_barrier(
        (joined, gate_cat, up_cat, down_cat)
    )
    keys_win = joined[0]
    values_win = joined[1]
    allowed = (
        (query_seg[:, None] == key_seg[None, :])
        & (key_at[None, :] <= query_at[:, None])
        & (key_at[None, :] >= 0)
    )
    scores = (
        jnp.einsum("qhd,khd->hqk", queries, keys_win, preferred_element_type=f32) * score_scale
    )
    masked = jnp.where(allowed[None], scores, -1e30)
    peak = jnp.max(masked, axis=-1, keepdims=True)
    expo = jnp.exp(masked - peak)
    total = jnp.sum(expo, axis=-1, keepdims=True)
    log_total = peak + jnp.log(total)
    weights = expo / total
    attended = jnp.einsum(
        "hqk,khd->qhd", weights.astype(bf16), values_win, preferred_element_type=f32
    )
    attended = attended.reshape(rows_here, heads_width).astype(bf16)
    attn_part = jnp.einsum("th,dh->td", attended, output_weight, preferred_element_type=f32)
    resid = my_rows(layer_input) + sum_over_tp(attn_part)
    normed_two_wide, norm_two = norm_forward(resid, second_norm_scale)
    normed_two = normed_two_wide.astype(bf16)

    logits = jnp.dot(normed_two, side_weight, preferred_element_type=f32)
    router = jax.nn.softmax(logits[:, 3 : 3 + expert_count], axis=-1)
    mixer = jax.nn.sigmoid(logits[:, 2])
    normed_all, ffn_part, d_normed_part, weighted_h, d_gate_pre, d_up_pre = ffn_over_all(
        normed_two,
        upstream_all,
        gate_cat,
        up_cat,
        down_cat,
        side_weight,
        (slot_here, slot_hidden, shared_units),
        expert_count,
    )
    d_normed_sum, out_sum = sum_over_all(d_normed_part, ffn_part)
    ffn_sum = out_sum[:, :width]
    dots_sum = out_sum[:, width:]
    grad_down_cat = jnp.einsum(
        "tf,td->fd", weighted_h, upstream_all[:, :width], preferred_element_type=f32
    )
    block_out = gather_over_tp((resid + ffn_sum).astype(bf16))
    d_router = jnp.where(picked, dots_sum[:, 3 : 3 + expert_count], 0.0)
    d_mixer = dots_sum[:, 2]
    d_logits = router * (d_router - jnp.sum(router * d_router, axis=-1, keepdims=True))
    d_mixlogit = d_mixer * mixer * (1.0 - mixer)
    side = jnp.dot(d_logits, router_f.T, precision=highest) + d_mixlogit[:, None] * mix_f[None, :]
    normed_two_f = normed_two.astype(f32)
    d_side = jnp.concatenate([d_mixlogit[:, None], d_logits], axis=1)
    grad_side = jnp.dot(normed_two_f.T, d_side, precision=highest)
    upstream = my_rows(cotangent).astype(f32)
    d_normed_two = d_normed_sum + side
    d_resid_norm, grad_gain_two = norm_backward(resid, norm_two, second_norm_scale, d_normed_two)
    d_resid = upstream + d_resid_norm
    d_resid_low = gather_over_tp(d_resid.astype(bf16))
    grad_out = jnp.einsum("td,th->dh", d_resid_low, attended, preferred_element_type=f32)
    grad_out = lax.psum_scatter(
        grad_out.astype(bf16), "ep", scatter_dimension=0, tiled=True
    ).astype(f32)
    d_attended = jnp.einsum("td,dh->th", d_resid_low, output_weight, preferred_element_type=f32)
    d_attended = d_attended.astype(bf16).reshape(rows_here, heads_here, HD)
    scores_again = (
        jnp.einsum("qhd,khd->hqk", queries, keys_win, preferred_element_type=f32) * score_scale
    )
    probs = jnp.where(allowed[None], jnp.exp(scores_again - log_total), 0.0)
    d_probs = jnp.einsum("qhd,khd->hqk", d_attended, values_win, preferred_element_type=f32)
    delta = jnp.sum(probs * d_probs, axis=-1, keepdims=True)
    d_scores = (probs * (d_probs - delta)).astype(bf16)
    d_scores, d_gate_pre, d_up_pre = lax.optimization_barrier((d_scores, d_gate_pre, d_up_pre))
    grad_gate_cat = jnp.einsum("tf,td->fd", d_gate_pre, normed_all, preferred_element_type=f32)
    grad_up_cat = jnp.einsum("tf,td->fd", d_up_pre, normed_all, preferred_element_type=f32)
    grad_cats = (grad_gate_cat, grad_up_cat, grad_down_cat)
    grad_shared = share_back(
        [grad[routed_units : routed_units + shared_units].astype(bf16) for grad in grad_cats],
        ep_count,
    )
    grad_shared = [grad.astype(f32) for grad in grad_shared]
    grad_experts = [grad[:routed_units].reshape(expert_gate.shape) for grad in grad_cats]

    d_keys_win = (
        jnp.einsum("hqk,qhd->khd", d_scores, queries, preferred_element_type=f32) * score_scale
    )
    d_values_win = jnp.einsum(
        "hqk,qhd->khd", probs.astype(bf16), d_attended, preferred_element_type=f32
    )
    pair_grads = jnp.stack([d_keys_win, d_values_win], axis=0)
    passed = pair_grads[:, : 2 * rows_here].astype(bf16)
    from_two = passed_along(passed[:, :rows_here], "ep", -2)
    from_one = passed_along(passed[:, rows_here:], "ep", -1)
    d_queries = (
        jnp.einsum("hqk,khd->qhd", d_scores, keys_win, preferred_element_type=f32) * score_scale
    )
    running = pair_grads[:, 2 * rows_here :] + from_one.astype(f32) + from_two.astype(f32)
    d_projected = jnp.concatenate(
        [
            unrotate(d_queries, cosine, sine).astype(bf16).reshape(rows_here, heads_width),
            unrotate(running[0], cosine, sine).astype(bf16).reshape(rows_here, heads_width),
            running[1].astype(bf16).reshape(rows_here, heads_width),
        ],
        axis=1,
    )
    d_normed_one = jnp.einsum("th,dh->td", d_projected, qkv_weight, preferred_element_type=f32)
    d_normed_one = sum_over_tp(d_normed_one)
    grad_qkv = jnp.einsum("td,th->dh", normed_one, d_projected, preferred_element_type=f32)
    d_input_norm, grad_gain_one = norm_backward(
        my_rows(layer_input), my_rows(norm_one), first_norm_scale, d_normed_one
    )
    grad_tokens = gather_over_tp((d_resid + d_input_norm).astype(bf16)).astype(f32)
    small = jnp.concatenate([grad_gain_one[:, None], grad_gain_two[:, None], grad_side], axis=1)
    small = jnp.pad(small, ((0, 0), (0, 128 - small.shape[1])))
    grad_weights = scatter_over_ep(jnp.concatenate([grad_qkv, small], axis=1).astype(bf16))
    small = grad_weights[:, 3 * heads_width :]
    small = small + over_tp(small, 1)
    small = small + over_tp(small, 2)
    parts = [grad_weights[:, i * heads_width : (i + 1) * heads_width] for i in range(3)]
    return (
        block_out,
        grad_tokens,
        small[:, 0],
        parts[0],
        parts[1],
        parts[2],
        grad_out,
        small[:, 1],
        small[:, 3 : 3 + expert_count],
        small[:, 2],
        grad_shared[0],
        grad_shared[1],
        grad_shared[2],
        grad_experts[0],
        grad_experts[1],
        grad_experts[2],
    )


def chosen_body(*arrays):
    rows_here, top_count = arrays[2].shape
    slot_here, expert_count = arrays[14].shape[0], arrays[9].shape[1]
    capacity = rows_here * top_count * 7 // (5 * expert_count)
    grid_of_two = lax.axis_size("ep") % 2 == 0 and lax.axis_size("tp") == 4
    if grid_of_two and rows_here < 2 * slot_here * capacity:
        return dense_body(*arrays)
    return body(*arrays)


def solution(mesh):
    placed = (
        P("ep", None),
        P(),
        P("ep", None),
        P("ep"),
        P("ep", "tp"),
        P("ep", "tp"),
        P("ep", "tp"),
        P("ep", "tp"),
        P("ep"),
        P("ep", None),
        P("ep"),
        P("ep", "tp"),
        P("ep", "tp"),
        P("ep", "tp"),
        P("ep", "tp", None),
        P("ep", "tp", None),
        P("ep", "tp", None),
        P("ep", None),
    )
    return jax.shard_map(
        chosen_body,
        mesh=mesh,
        in_specs=placed,
        out_specs=(
            P("ep", None),
            P("ep", None),
            P("ep"),
            P("ep", "tp"),
            P("ep", "tp"),
            P("ep", "tp"),
            P("ep", "tp"),
            P("ep"),
            P("ep", None),
            P("ep"),
            P("ep", "tp"),
            P("ep", "tp"),
            P("ep", "tp"),
            P("ep", "tp", None),
            P("ep", "tp", None),
            P("ep", "tp", None),
        ),
        check_vma=False,
    )
```

```python
import functools

import jax
import jax.numpy as jnp
from jax import lax
from jax.experimental import pallas as pl
from jax.experimental.pallas import tpu as pltpu
from jax.sharding import PartitionSpec as P

HD = 128


epsilon = 1e-06
rope_base = 1000000.0
highest = lax.Precision.HIGHEST
MESH = pl.DeviceIdType.MESH


def passed_along(block, axis, distance):
    devices = range(lax.axis_size(axis))
    route = [(i - distance, i) for i in devices if i - distance in devices]
    return lax.ppermute(block, axis, route)


def rope_tables(positions, width):
    steps = jnp.arange(0, width, 2, dtype=jnp.float32) / width
    inverse = rope_base ** (-steps)
    angles = positions.astype(jnp.float32)[:, None] * inverse[None, :]
    angles = jnp.concatenate([angles, angles], axis=-1)
    return (jnp.cos(angles)[:, None, :], jnp.sin(angles)[:, None, :])


def turn_half(values):
    middle = values.shape[-1] // 2
    return jnp.concatenate([-values[..., middle:], values[..., :middle]], axis=-1)


def rotate(values, cosine, sine):
    return values * cosine + turn_half(values) * sine


def unrotate(grads, cosine, sine):
    return grads * cosine - turn_half(grads * sine)


def sequence_info(lengths, indices):
    starts = jnp.cumsum(lengths) - lengths
    inside = starts[None, :] <= indices[:, None]
    segment = jnp.sum(inside.astype(jnp.int32), axis=1) - 1
    first = jnp.max(jnp.where(inside, starts[None, :], -1), axis=1)
    return (segment, indices - first)


def norm_forward(values, gain):
    scale = lax.rsqrt(jnp.mean(values * values, axis=-1, keepdims=True) + epsilon)
    return (values * scale * gain, scale)


def norm_backward(values, scale, gain, grads):
    unit = values * scale
    scaled = grads * gain
    inner = jnp.mean(scaled * unit, axis=-1, keepdims=True)
    return (scale * (scaled - unit * inner), jnp.sum(grads * unit, axis=0))


def deliver(rows):
    arrived_rows = lax.all_to_all(rows, "ep", split_axis=0, concat_axis=0, tiled=True)
    return arrived_rows


def bring_back(parts, target, rows_here, top_count):
    moved = lax.all_to_all(parts, "ep", split_axis=0, concat_axis=0, tiled=True)
    piece = moved.shape[3]
    return moved.reshape(-1, piece)[target].reshape(rows_here, top_count, piece)


def body(
    tokens,
    lengths,
    routes,
    attn_gain,
    w_query,
    w_key,
    w_value,
    w_out,
    ffn_gain,
    w_router,
    shared_mix,
    shared_gate,
    shared_up,
    shared_down,
    expert_gate,
    expert_up,
    expert_down,
    cotangent,
):
    rows_here = tokens.shape[0]
    width = tokens.shape[1]
    ep_count = lax.axis_size("ep")
    offset = lax.axis_index("ep") * rows_here
    slot_here = expert_gate.shape[0]
    top_count = routes.shape[1]
    gathered = (
        lax.all_gather(attn_gain, "ep", axis=0, tiled=True),
        lax.all_gather(w_query, "ep", axis=0, tiled=True),
        lax.all_gather(w_key, "ep", axis=0, tiled=True),
        lax.all_gather(w_value, "ep", axis=0, tiled=True),
        lax.all_gather(w_out, "ep", axis=0, tiled=True),
        lax.all_gather(ffn_gain, "ep", axis=0, tiled=True),
        lax.all_gather(w_router, "ep", axis=0, tiled=True),
        lax.all_gather(shared_mix, "ep", axis=0, tiled=True),
        lax.all_gather(shared_gate, "ep", axis=0, tiled=True),
        lax.all_gather(shared_up, "ep", axis=0, tiled=True),
        lax.all_gather(shared_down, "ep", axis=0, tiled=True),
    )
    (
        gain_first,
        query_weight_matrix,
        key_weight_matrix,
        value_weight_matrix,
        output_weight,
        gain_second,
        router_weight,
        shared_mixer_weight,
        shared_gate_weight,
        shared_up_weight,
        shared_down_weight,
    ) = gathered
    expert_count = router_weight.shape[1]
    capacity = (rows_here * top_count * 7 // (5 * expert_count) + 7) // 8 * 8
    heads_here = query_weight_matrix.shape[1] // HD
    score_scale = HD ** (-0.5)
    first_norm_scale = gain_first.astype(jnp.float32)
    second_norm_scale = gain_second.astype(jnp.float32)
    layer_input = tokens.astype(jnp.float32)
    normed_wide, norm_one = norm_forward(layer_input, first_norm_scale)
    normed_one = normed_wide.astype(jnp.bfloat16)
    query_at = offset + jnp.arange(rows_here, dtype=jnp.int32)
    key_at = offset - 2 * rows_here + jnp.arange(3 * rows_here, dtype=jnp.int32)
    query_seg, query_pos = sequence_info(lengths, query_at)
    key_seg, _ = sequence_info(lengths, key_at)
    cosine, sine = rope_tables(query_pos, HD)
    query_pre = jnp.dot(
        normed_one, query_weight_matrix, preferred_element_type=jnp.float32
    ).reshape(rows_here, heads_here, HD)
    key_pre = jnp.dot(normed_one, key_weight_matrix, preferred_element_type=jnp.float32).reshape(
        rows_here, heads_here, HD
    )
    queries = rotate(query_pre, cosine, sine).astype(jnp.bfloat16)
    keys = rotate(key_pre, cosine, sine).astype(jnp.bfloat16)
    values = (
        jnp.dot(normed_one, value_weight_matrix, preferred_element_type=jnp.float32)
        .astype(jnp.bfloat16)
        .reshape(rows_here, heads_here, HD)
    )
    carried = jnp.stack([keys, values], axis=0)
    window = [carried]
    for hop in range(2):
        carried = passed_along(carried, "ep", 1)
        window = [carried] + window
    joined = jnp.concatenate(window, axis=1)
    keys_win = joined[0]
    values_win = joined[1]
    allowed = (
        (query_seg[:, None] == key_seg[None, :])
        & (key_at[None, :] <= query_at[:, None])
        & (key_at[None, :] >= 0)
    )
    scores = (
        jnp.einsum("qhd,khd->hqk", queries, keys_win, preferred_element_type=jnp.float32)
        * score_scale
    )
    masked = jnp.where(allowed[None], scores, -1e30)
    peak = jnp.max(masked, axis=-1, keepdims=True)
    expo = jnp.exp(masked - peak)
    total = jnp.sum(expo, axis=-1, keepdims=True)
    log_total = peak + jnp.log(total)
    weights = expo / total
    attended = jnp.einsum(
        "hqk,khd->qhd", weights.astype(jnp.bfloat16), values_win, preferred_element_type=jnp.float32
    )
    attended = attended.reshape(rows_here, heads_here * HD).astype(jnp.bfloat16)
    attn_part = jnp.einsum("th,dh->td", attended, output_weight, preferred_element_type=jnp.float32)
    resid = layer_input + lax.psum(attn_part, "tp")
    normed_two_wide, norm_two = norm_forward(resid, second_norm_scale)
    normed_two = normed_two_wide.astype(jnp.bfloat16)
    normed_two_f = normed_two.astype(jnp.float32)
    router_f = router_weight.astype(jnp.float32)
    mix_f = shared_mixer_weight.astype(jnp.float32)
    router = jax.nn.softmax(jnp.dot(normed_two_f, router_f, precision=highest), axis=-1)
    picked = routes[:, :, None] == jnp.arange(expert_count, dtype=jnp.int32)[None, None, :]
    gates = jnp.sum(jnp.where(picked, router[:, None, :], 0.0), axis=-1)
    mixer = jax.nn.sigmoid(jnp.dot(normed_two_f, mix_f, precision=highest))
    shared_g = jnp.dot(normed_two, shared_gate_weight, preferred_element_type=jnp.float32)
    shared_u = jnp.dot(normed_two, shared_up_weight, preferred_element_type=jnp.float32)
    shared_h = (jax.nn.silu(shared_g) * shared_u).astype(jnp.bfloat16)
    shared_part = jnp.einsum(
        "tf,df->td", shared_h, shared_down_weight, preferred_element_type=jnp.float32
    )
    flat = routes.reshape(-1)
    hot = (flat[:, None] == jnp.arange(expert_count, dtype=jnp.int32)[None, :]).astype(jnp.int32)
    rank = jnp.sum(jnp.cumsum(hot, axis=0) * hot, axis=1) - 1
    target = flat * capacity + rank
    slot_total = ep_count * slot_here * capacity
    owner_route = (
        jnp.zeros((slot_total,), jnp.int32)
        .at[target]
        .set(jnp.arange(rows_here * top_count, dtype=jnp.int32))
    )
    filled = jnp.zeros((slot_total,), jnp.bool_).at[target].set(True)
    owner_token = owner_route // top_count
    send_rows = jnp.where(filled[:, None], normed_two[owner_token], jnp.zeros((), jnp.bfloat16))
    arrived_rows = deliver(send_rows.reshape(ep_count, slot_here, capacity, width))
    route_g = jnp.einsum(
        "nscd,sfd->nscf", arrived_rows, expert_gate, preferred_element_type=jnp.float32
    )
    route_u = jnp.einsum(
        "nscd,sfd->nscf", arrived_rows, expert_up, preferred_element_type=jnp.float32
    )
    route_h = (jax.nn.silu(route_g) * route_u).astype(jnp.bfloat16)
    route_part = jnp.einsum(
        "nscf,sfd->nscd", route_h, expert_down, preferred_element_type=jnp.float32
    )
    back_rows = bring_back(route_part, target, rows_here, top_count)
    upstream = cotangent.astype(jnp.float32)
    routed = jnp.sum(back_rows * gates[:, :, None], axis=1)
    ffn_part = mixer[:, None] * shared_part + routed
    route_dot = jnp.sum(back_rows * upstream[:, None, :], axis=-1)
    shared_dot = jnp.sum(shared_part * upstream, axis=-1)
    ffn_total, d_gate, d_mixer = lax.psum((ffn_part, route_dot, shared_dot), "tp")
    block_out = (resid + ffn_total).astype(jnp.bfloat16)
    d_router = jnp.sum(jnp.where(picked, d_gate[:, :, None], 0.0), axis=1)
    d_logits = router * (d_router - jnp.sum(router * d_router, axis=-1, keepdims=True))
    d_mixlogit = d_mixer * mixer * (1.0 - mixer)
    side = jnp.dot(d_logits, router_f.T, precision=highest) + d_mixlogit[:, None] * mix_f[None, :]
    grad_router = jnp.dot(normed_two_f.T, d_logits, precision=highest)
    grad_mix = jnp.dot(d_mixlogit, normed_two_f, precision=highest)
    d_shared = (mixer[:, None] * upstream).astype(jnp.bfloat16)
    d_sh = jnp.dot(d_shared, shared_down_weight, preferred_element_type=jnp.float32)
    sig_shared = jax.nn.sigmoid(shared_g)
    d_sg = (d_sh * shared_u * sig_shared * (1.0 + shared_g * (1.0 - sig_shared))).astype(
        jnp.bfloat16
    )
    d_su = (d_sh * shared_g * sig_shared).astype(jnp.bfloat16)
    d_normed_part = jnp.einsum(
        "tf,df->td", d_sg, shared_gate_weight, preferred_element_type=jnp.float32
    )
    d_normed_part = d_normed_part + jnp.einsum(
        "tf,df->td", d_su, shared_up_weight, preferred_element_type=jnp.float32
    )
    grad_sgate = jnp.einsum("td,tf->df", normed_two, d_sg, preferred_element_type=jnp.float32)
    grad_sup = jnp.einsum("td,tf->df", normed_two, d_su, preferred_element_type=jnp.float32)
    grad_sdown = jnp.einsum("td,tf->df", d_shared, shared_h, preferred_element_type=jnp.float32)
    d_route = (
        (gates[:, :, None] * upstream[:, None, :])
        .astype(jnp.bfloat16)
        .reshape(rows_here * top_count, width)
    )
    send_grads = jnp.where(filled[:, None], d_route[owner_route], jnp.zeros((), jnp.bfloat16))
    received_grads = deliver(send_grads.reshape(ep_count, slot_here, capacity, width))
    d_rh = jnp.einsum(
        "nscd,sfd->nscf", received_grads, expert_down, preferred_element_type=jnp.float32
    )
    sig_route = jax.nn.sigmoid(route_g)
    d_rg = (d_rh * route_u * sig_route * (1.0 + route_g * (1.0 - sig_route))).astype(jnp.bfloat16)
    routed_up_gradient = (d_rh * route_g * sig_route).astype(jnp.bfloat16)
    row_grads = jnp.einsum("nscf,sfd->nscd", d_rg, expert_gate, preferred_element_type=jnp.float32)
    row_grads = row_grads + jnp.einsum(
        "nscf,sfd->nscd", routed_up_gradient, expert_up, preferred_element_type=jnp.float32
    )
    grad_egate = jnp.einsum(
        "qxba,qxbr->xar", d_rg, arrived_rows, preferred_element_type=jnp.float32
    )
    expert_up_gradient = jnp.einsum(
        "qxba,qxbr->xar", routed_up_gradient, arrived_rows, preferred_element_type=jnp.float32
    )
    grad_edown = jnp.einsum(
        "qxba,qxbr->xar", route_h, received_grads, preferred_element_type=jnp.float32
    )
    grads_back = bring_back(row_grads, target, rows_here, top_count)
    d_routed = jnp.sum(grads_back, axis=1)
    d_normed_two = lax.psum(d_normed_part + d_routed, "tp") + side
    d_resid_norm, grad_gain_two = norm_backward(resid, norm_two, second_norm_scale, d_normed_two)
    d_resid = upstream + d_resid_norm
    d_resid_low = d_resid.astype(jnp.bfloat16)
    grad_outw = jnp.einsum("td,th->dh", d_resid_low, attended, preferred_element_type=jnp.float32)
    d_attended = jnp.einsum(
        "td,dh->th", d_resid_low, output_weight, preferred_element_type=jnp.float32
    )
    d_attended = d_attended.astype(jnp.bfloat16).reshape(rows_here, heads_here, HD)
    scores_again = (
        jnp.einsum("qhd,khd->hqk", queries, keys_win, preferred_element_type=jnp.float32)
        * score_scale
    )
    probs = jnp.where(allowed[None], jnp.exp(scores_again - log_total), 0.0)
    d_probs = jnp.einsum("qhd,khd->hqk", d_attended, values_win, preferred_element_type=jnp.float32)
    delta = jnp.sum(probs * d_probs, axis=-1, keepdims=True)
    d_scores = (probs * (d_probs - delta)).astype(jnp.bfloat16)
    d_queries = (
        jnp.einsum("hqk,khd->qhd", d_scores, keys_win, preferred_element_type=jnp.float32)
        * score_scale
    )
    d_keys_win = (
        jnp.einsum("hqk,qhd->khd", d_scores, queries, preferred_element_type=jnp.float32)
        * score_scale
    )
    d_values_win = jnp.einsum(
        "hqk,qhd->khd", probs.astype(jnp.bfloat16), d_attended, preferred_element_type=jnp.float32
    )
    pair_grads = jnp.stack([d_keys_win, d_values_win], axis=0)
    older = pair_grads[:, :rows_here]
    later = [pair_grads[:, rows_here : 2 * rows_here], pair_grads[:, 2 * rows_here :]]
    running = older
    for hop in range(2):
        running = passed_along(running, "ep", -1)
        running = running + later[hop]
    d_query_pre = (
        unrotate(d_queries, cosine, sine).astype(jnp.bfloat16).reshape(rows_here, heads_here * HD)
    )
    d_key_pre = (
        unrotate(running[0], cosine, sine).astype(jnp.bfloat16).reshape(rows_here, heads_here * HD)
    )
    d_values = running[1].astype(jnp.bfloat16).reshape(rows_here, heads_here * HD)
    grad_queryw = jnp.einsum(
        "td,th->dh", normed_one, d_query_pre, preferred_element_type=jnp.float32
    )
    grad_keyw = jnp.einsum("td,th->dh", normed_one, d_key_pre, preferred_element_type=jnp.float32)
    grad_valuew = jnp.einsum("td,th->dh", normed_one, d_values, preferred_element_type=jnp.float32)
    d_normed_one = jnp.einsum(
        "th,dh->td", d_query_pre, query_weight_matrix, preferred_element_type=jnp.float32
    )
    d_normed_one = d_normed_one + jnp.einsum(
        "th,dh->td", d_key_pre, key_weight_matrix, preferred_element_type=jnp.float32
    )
    d_normed_one = d_normed_one + jnp.einsum(
        "th,dh->td", d_values, value_weight_matrix, preferred_element_type=jnp.float32
    )
    d_normed_one = lax.psum(d_normed_one, "tp")
    d_input_norm, grad_gain_one = norm_backward(
        layer_input, norm_one, first_norm_scale, d_normed_one
    )
    grad_tokens = d_resid + d_input_norm
    summed = (
        lax.psum_scatter(grad_gain_one, "ep", scatter_dimension=0, tiled=True),
        lax.psum_scatter(grad_queryw, "ep", scatter_dimension=0, tiled=True),
        lax.psum_scatter(grad_keyw, "ep", scatter_dimension=0, tiled=True),
        lax.psum_scatter(grad_valuew, "ep", scatter_dimension=0, tiled=True),
        lax.psum_scatter(grad_outw, "ep", scatter_dimension=0, tiled=True),
        lax.psum_scatter(grad_gain_two, "ep", scatter_dimension=0, tiled=True),
        lax.psum_scatter(grad_router, "ep", scatter_dimension=0, tiled=True),
        lax.psum_scatter(grad_mix, "ep", scatter_dimension=0, tiled=True),
        lax.psum_scatter(grad_sgate, "ep", scatter_dimension=0, tiled=True),
        lax.psum_scatter(grad_sup, "ep", scatter_dimension=0, tiled=True),
        lax.psum_scatter(grad_sdown, "ep", scatter_dimension=0, tiled=True),
    )
    return (
        block_out,
        grad_tokens,
        summed[0],
        summed[1],
        summed[2],
        summed[3],
        summed[4],
        summed[5],
        summed[6],
        summed[7],
        summed[8],
        summed[9],
        summed[10],
        grad_egate,
        expert_up_gradient,
        grad_edown,
    )


class Place:
    def __init__(self):
        self.ep, self.tp = lax.axis_index("ep"), lax.axis_index("tp")
        self.z, self.y = self.ep // 2, self.ep % 2
        self.x, self.c = self.tp // 2, self.tp % 2
        self.depth = lax.axis_size("ep") // 2
        self.next_core = (self.ep, self.x * 2 + 1 - self.c)
        self.next_x = (self.ep, (1 - self.x) * 2 + self.c)
        self.next_y = (self.z * 2 + 1 - self.y, self.tp)

    def at_z(self, z):
        return (z * 2 + self.y, self.tp)

    def ahead(self, steps):
        return lax.rem(self.z + steps, self.depth)

    def behind(self, steps):
        return lax.rem(self.z + self.depth - steps, self.depth)

    def greet(self):
        barrier = pltpu.get_barrier_semaphore()
        peers = [self.next_core, self.next_x, self.next_y]
        peers += [self.at_z(self.ahead(k)) for k in range(1, self.depth)]
        for peer in peers:
            pl.semaphore_signal(barrier, inc=1, device_id=peer, device_id_type=MESH)
        pl.semaphore_wait(barrier, len(peers))


def remote(src, dst, send, recv, peer):
    return pltpu.make_async_remote_copy(
        src_ref=src, dst_ref=dst, send_sem=send, recv_sem=recv, device_id=peer, device_id_type=MESH
    )


def ffn_kernel(
    units,
    expert_count,
    rows_in,
    upstream_in,
    gate_in,
    up_in,
    down_in,
    side_in,
    rows_all,
    weighted_out,
    d_gate_out,
    d_up_out,
    d_rows_sum,
    out_sum,
    gate_w,
    up_w,
    down_w,
    side_w,
    rows_tile,
    upstream_tile,
    weighted_tile,
    d_gate_tile,
    d_up_tile,
    d_rows_tile,
    out_tile,
    d_rows_core,
    out_core,
    d_rows_held,
    out_held,
    d_rows_hop,
    out_hop,
    d_rows_hop2,
    out_hop2,
    d_rows_z,
    out_z,
    weight_sem,
    own_sem,
    z_send,
    z_recv,
    plane_send,
    plane_recv,
    load_sem,
    store_sem,
    sum_send,
    sum_recv,
    end_send,
    end_recv,
    core_credit,
    hop_credit,
    hop2_credit,
):
    at = Place()
    depth = at.depth
    quarter, width = rows_in.shape
    half = quarter // 2
    f32, bf16 = jnp.float32, jnp.bfloat16

    def weight_copies():
        pairs = ((gate_in, gate_w), (up_in, up_w), (down_in, down_w), (side_in, side_w))
        return [
            pltpu.make_async_copy(src, dst, weight_sem.at[i]) for i, (src, dst) in enumerate(pairs)
        ]

    for copy in weight_copies():
        copy.start()

    def block(j, y, x):
        return rows_all.at[at.behind(j), y, x, at.c]

    def plane_copy(j, kind):
        y, other_y = at.y, 1 - at.y
        own, other_x = at.x, 1 - at.x
        if kind == 0:
            src, peer = block(j, y, own), at.next_x
        elif kind == 1:
            src, peer = block(j, y, own), at.next_y
        elif kind == 2:
            src, peer = block(j, y, other_x).at[pl.ds(0, half)], at.next_y
        elif kind == 3:
            src, peer = block(j, other_y, own).at[pl.ds(half, half)], at.next_x
        else:
            src = block(j, other_y if kind >= 6 else y, other_x if kind % 2 else own)
            peer = at.next_core
        return remote(src, src, plane_send.at[j, kind], plane_recv.at[j, kind], peer)

    def z_copy(k):
        return remote(
            rows_in, block(0, at.y, at.x), z_send.at[k - 1], z_recv.at[k - 1], at.at_z(at.ahead(k))
        )

    def z_arrival(k):
        dst = block(k, at.y, at.x)
        return remote(dst, dst, z_send.at[k - 1], z_recv.at[k - 1], at.at_z(at.behind(k)))

    def begin(j):
        for kind in (0, 1, 4):
            plane_copy(j, kind).start()

    def spread(j):
        plane_copy(j, 0).wait_recv()
        plane_copy(j, 2).start()
        plane_copy(j, 5).start()
        plane_copy(j, 1).wait_recv()
        plane_copy(j, 3).start()
        plane_copy(j, 6).start()

    def begin_later(j):
        z_arrival(j).wait_recv()
        begin(j)

    def last_hop(j):
        plane_copy(j, 2).wait_recv()
        plane_copy(j, 3).wait_recv()
        plane_copy(j, 7).start()

    def near_ready(j):
        plane_copy(j, 4).wait_recv()
        plane_copy(j, 5).wait_recv()

    def far_ready(j):
        plane_copy(j, 6).wait_recv()
        plane_copy(j, 7).wait_recv()

    def parity(step):
        return lax.rem(step, 2)

    def tile_at(step):
        return at.behind(step // 2), lax.rem(at.y + parity(step), 2)

    def load_rows(step):
        z, y = tile_at(step)
        return pltpu.make_async_copy(rows_all.at[z, y], rows_tile, load_sem.at[0])

    def load_upstream(step):
        z, y = tile_at(step)
        return pltpu.make_async_copy(upstream_in.at[z, y], upstream_tile, load_sem.at[1])

    def stores(step):
        z, y = tile_at(step)
        pairs = (
            (weighted_tile, weighted_out),
            (d_gate_tile, d_gate_out),
            (d_up_tile, d_up_out),
        )
        return [
            pltpu.make_async_copy(src, dst.at[z, y], store_sem.at[i])
            for i, (src, dst) in enumerate(pairs)
        ]

    tiles, cores = (d_rows_tile, out_tile), (d_rows_core, out_core)
    helds, sums = (d_rows_held, out_held), (d_rows_sum, out_sum)
    hops, hops2, zs = (d_rows_hop, out_hop), (d_rows_hop2, out_hop2), (d_rows_z, out_z)

    def core_sum(a, step):
        slot = parity(step)
        return remote(
            tiles[a].at[slot, :, 1 - at.c],
            cores[a].at[slot],
            sum_send.at[a, 0, slot],
            sum_recv.at[a, 0, slot],
            at.next_core,
        )

    def hop_sum(a, j):
        slot = parity(j)
        src = helds[0].at[slot, :, 1 - at.x] if a == 0 else helds[1].at[slot, 1 - at.y]
        peer = at.next_x if a == 0 else at.next_y
        return remote(src, hops[a].at[slot], sum_send.at[a, 1, slot], sum_recv.at[a, 1, slot], peer)

    def hop2_sum(a, j):
        slot = parity(j)
        if a == 0:
            src, peer = helds[0].at[slot, 1 - at.y, at.x], at.next_y
        else:
            src, peer = helds[1].at[slot, at.y, 1 - at.x], at.next_x
        return remote(
            src, hops2[a].at[slot], sum_send.at[a, 2, slot], sum_recv.at[a, 2, slot], peer
        )

    def z_sum(a, j):
        return remote(
            helds[a].at[parity(j), at.y, at.x],
            zs[a].at[j - 1],
            end_send.at[a, j - 1],
            end_recv.at[a, j - 1],
            at.at_z(at.behind(j)),
        )

    def allow(semaphore, peer):
        pl.semaphore_signal(semaphore, inc=1, device_id=peer, device_id_type=MESH)

    piece = 32

    def add(into, first, second):
        def body(i, carry):
            part = pl.ds(pl.multiple_of(i * piece, piece), piece)
            into[part] = first[part] + second[part]
            return carry

        lax.fori_loop(0, quarter // piece, body, 0)

    def after_core(step):
        slot, j = parity(step), step // 2
        held, y = parity(j), lax.rem(at.y + parity(step), 2)

        @pl.when((slot == 0) & (j >= 3))
        def _():
            for a in (0, 1):
                z_sum(a, j - 2).wait_send()

        for a in (0, 1):
            core_sum(a, step).wait_recv()
            for x in (0, 1):
                add(helds[a].at[held, y, x], tiles[a].at[slot, x, at.c], cores[a].at[slot, x])

        @pl.when(step + 2 < 2 * depth)
        def _():
            allow(core_credit, at.next_core)

        @pl.when(slot == 1)
        def _():
            @pl.when(j >= 2)
            def _():
                for a in (0, 1):
                    pl.semaphore_wait(hop_credit.at[a], 1)

            for a in (0, 1):
                hop_sum(a, j).start()

    def after_hop(j):
        slot = parity(j)

        @pl.when(j >= 2)
        def _():
            for a in (0, 1):
                pl.semaphore_wait(hop2_credit.at[a], 1)

        for a in (0, 1):
            hop_sum(a, j).wait()
            for moved in (1, 0):
                if a == 0:
                    y = lax.rem(at.y + moved, 2)
                    into, other = helds[0].at[slot, y, at.x], hops[0].at[slot, y]
                else:
                    x = lax.rem(at.x + moved, 2)
                    into, other = helds[1].at[slot, at.y, x], hops[1].at[slot, x]
                add(into, into, other)
                if moved:
                    hop2_sum(a, j).start()

        @pl.when(j + 2 < depth)
        def _():
            allow(hop_credit.at[0], at.next_x)
            allow(hop_credit.at[1], at.next_y)

    def after_hop2(j):
        slot = parity(j)
        for a in (0, 1):
            hop2_sum(a, j).wait()
            into = helds[a].at[slot, at.y, at.x]
            add(into, into, hops2[a].at[slot])

            @pl.when(j > 0)
            def _():
                z_sum(a, j).start()

            @pl.when(j == 0)
            def _():
                def body(i, carry):
                    part = pl.ds(pl.multiple_of(i * piece, piece), piece)
                    sums[a][part] = into[part].astype(f32)
                    return carry

                lax.fori_loop(0, quarter // piece, body, 0)

        @pl.when(j + 2 < depth)
        def _():
            allow(hop2_credit.at[0], at.next_y)
            allow(hop2_credit.at[1], at.next_x)

    load_upstream(0).start()
    at.greet()
    for k in range(1, depth):
        z_copy(k).start()
    own_copy = pltpu.make_async_copy(rows_in, block(0, at.y, at.x), own_sem)
    own_copy.start()
    own_copy.wait()
    begin(0)
    spread(0)
    begin_later(1)
    near_ready(0)
    load_rows(0).start()
    for copy in weight_copies():
        copy.wait()

    part_rows = 2 * quarter
    hidden_total = gate_w.shape[0]
    lane = lax.broadcasted_iota(jnp.int32, (part_rows, 128), 1)
    unit = lax.broadcasted_iota(jnp.int32, (1, hidden_total), 1)
    slot_here, slot_hidden, shared_hidden = units
    routed = slot_here * slot_hidden
    across = (((1,), (1,)), ((), ()))

    def tile_part(x, slot):
        here = pl.ds(pl.multiple_of(x * part_rows, part_rows), part_rows)
        upstream = upstream_tile[x].reshape(part_rows, upstream_tile.shape[-1])
        rows = rows_tile[x].reshape(part_rows, width)
        d_hidden = lax.dot_general(
            upstream[:, :width], down_w[...], across, preferred_element_type=f32
        )
        logits = jnp.dot(rows, side_w[...], preferred_element_type=f32)
        chooses = (lane >= 3) & (lane < 3 + expert_count)
        peak = jnp.max(jnp.where(chooses, logits, -1e30), axis=1, keepdims=True)
        expo = jnp.where(chooses, jnp.exp(jnp.where(chooses, logits, peak) - peak), 0.0)
        router = expo / jnp.sum(expo, axis=1, keepdims=True)
        routed_gate = router * upstream[:, width:].astype(f32)
        mix_pre = jnp.sum(jnp.where(lane == 2, logits, 0.0), axis=1, keepdims=True)
        mixer = 1.0 / (1.0 + jnp.exp(-mix_pre))
        factor = jnp.where(unit < routed + shared_hidden, mixer, 0.0)
        for s in range(slot_here):
            chosen = lane == 3 + at.ep * slot_here + s
            gate = jnp.sum(jnp.where(chosen, routed_gate, 0.0), axis=1, keepdims=True)
            inside = (unit >= s * slot_hidden) & (unit < (s + 1) * slot_hidden)
            factor = jnp.where(inside, gate, factor)
        gate_pre = lax.dot_general(rows, gate_w[...], across, preferred_element_type=f32)
        up_pre = lax.dot_general(rows, up_w[...], across, preferred_element_type=f32)
        sig = 1.0 / (1.0 + jnp.exp(-gate_pre))
        silu = gate_pre * sig
        hidden = silu * up_pre
        product = hidden * d_hidden
        gated = factor * d_hidden
        weighted_tile[here] = (factor * hidden).astype(bf16)
        d_gate_tile[here] = (gated * up_pre * (sig + silu * (1.0 - sig))).astype(bf16)
        d_up_tile[here] = (gated * silu).astype(bf16)
        dots = jnp.zeros((part_rows, 128), f32)
        for s in range(slot_here + 1):
            last = s == slot_here
            inside = unit >= s * slot_hidden
            if not last:
                inside = inside & (unit < (s + 1) * slot_hidden)
            dot = jnp.sum(jnp.where(inside, product, 0.0), axis=1, keepdims=True)
            where = lane == (2 if last else 3 + at.ep * slot_here + s)
            dots = jnp.where(where, dot, dots)
        blocks = (2, quarter)
        out = jnp.dot(weighted_tile[here], down_w[...], preferred_element_type=f32)
        out_tile[slot, x, :, :, :width] = out.astype(bf16).reshape(blocks + (width,))
        out_tile[slot, x, :, :, width:] = dots.astype(bf16).reshape(blocks + (128,))
        d_rows = jnp.dot(d_gate_tile[here], gate_w[...], preferred_element_type=f32)
        d_rows = d_rows + jnp.dot(d_up_tile[here], up_w[...], preferred_element_type=f32)
        d_rows_tile[slot, x] = d_rows.astype(bf16).reshape(blocks + (width,))

    def run_tile(step):
        slot, j = parity(step), step // 2
        load_upstream(step).wait()
        load_rows(step).wait()

        @pl.when(step >= 1)
        def _():
            for copy in stores(step - 1):
                copy.wait()

        @pl.when(step >= 2)
        def _():
            for a in (0, 1):
                core_sum(a, step - 2).wait_send()

        def part_body(x, carry):
            tile_part(x, slot)
            return carry

        lax.fori_loop(0, 2, part_body, 0)

        @pl.when(step >= 2)
        def _():
            pl.semaphore_wait(core_credit, 1)

        for a in (0, 1):
            core_sum(a, step).start()
        for copy in stores(step):
            copy.start()

        @pl.when(step + 1 < 2 * depth)
        def _():
            load_upstream(step + 1).start()

        @pl.when(slot == 0)
        def _():
            last_hop(j)

            @pl.when(j + 1 < depth)
            def _():
                spread(j + 1)

            @pl.when(j + 2 < depth)
            def _():
                begin_later(j + 2)

            far_ready(j)
            load_rows(step + 1).start()

        @pl.when((slot == 1) & (j + 1 < depth))
        def _():
            near_ready(j + 1)
            load_rows(step + 1).start()

    def step_body(step, carry):
        @pl.when(step < 2 * depth)
        def _():
            run_tile(step)

        @pl.when((step >= 1) & (step <= 2 * depth))
        def _():
            after_core(step - 1)

        odd = parity(step) == 1

        @pl.when(odd & (step >= 3) & (step < 2 * depth + 3))
        def _():
            after_hop((step - 3) // 2)

        @pl.when(jnp.logical_not(odd) & (step >= 4))
        def _():
            after_hop2((step - 4) // 2)

        return carry

    lax.fori_loop(0, 2 * depth + 3, step_body, 0)
    for a in (0, 1):
        for k in range(1, depth):
            z_sum(a, k).wait_recv()

        def total_body(i, carry):
            part = pl.ds(pl.multiple_of(i * piece, piece), piece)
            total = sums[a][part]
            for k in range(depth - 1):
                total = total + zs[a][k, part].astype(f32)
            sums[a][part] = total
            return carry

        lax.fori_loop(0, quarter // piece, total_body, 0)
    for copy in stores(2 * depth - 1):
        copy.wait()
    for a in (0, 1):
        for step in (2 * depth - 2, 2 * depth - 1):
            core_sum(a, step).wait_send()
        for j in range(max(1, depth - 2), depth):
            z_sum(a, j).wait_send()
    for k in range(1, depth):
        z_copy(k).wait_send()

    def finish(j, carry):
        for kind in range(8):
            plane_copy(j, kind).wait_send()
        return carry

    lax.fori_loop(0, depth, finish, 0)


def ffn_over_all(rows, upstream_all, gate_w, up_w, down_w, side_w, units, expert_count):
    quarter, width = rows.shape
    ep_count, tp_count = lax.axis_size("ep"), lax.axis_size("tp")
    depth = ep_count // 2
    hidden = gate_w.shape[0]
    bf16, f32 = jnp.bfloat16, jnp.float32
    wide = width + 128
    tile_rows = tp_count * quarter
    tokens = ep_count * tile_rows
    hidden_shape = jax.ShapeDtypeStruct((depth, 2, tile_rows, hidden), bf16)
    anywhere = pl.BlockSpec(memory_space=pl.ANY)
    in_vmem = pl.BlockSpec(memory_space=pltpu.VMEM)

    def both(*lead):
        return [pltpu.VMEM(lead + (quarter, columns), bf16) for columns in (width, wide)]

    dma = pltpu.SemaphoreType.DMA
    outs = pl.pallas_call(
        functools.partial(ffn_kernel, units, expert_count),
        out_shape=(
            jax.ShapeDtypeStruct((depth, 2, 2, 2, quarter, width), bf16),
            hidden_shape,
            hidden_shape,
            hidden_shape,
            jax.ShapeDtypeStruct((quarter, width), f32),
            jax.ShapeDtypeStruct((quarter, wide), f32),
        ),
        in_specs=[anywhere] * 6,
        out_specs=(anywhere,) * 4 + (in_vmem,) * 2,
        scratch_shapes=[
            pltpu.VMEM((hidden, width), bf16),
            pltpu.VMEM((hidden, width), bf16),
            pltpu.VMEM((hidden, width), bf16),
            pltpu.VMEM((width, 128), bf16),
            pltpu.VMEM((2, 2, quarter, width), bf16),
            pltpu.VMEM((2, 2, quarter, wide), bf16),
            pltpu.VMEM((tile_rows, hidden), bf16),
            pltpu.VMEM((tile_rows, hidden), bf16),
            pltpu.VMEM((tile_rows, hidden), bf16),
        ]
        + both(2, 2, 2)
        + both(2, 2)
        + both(2, 2, 2)
        + both(2, 2)
        + both(2)
        + both(depth - 1)
        + [
            dma((4,)),
            dma,
            dma((depth - 1,)),
            dma((depth - 1,)),
            dma((depth, 8)),
            dma((depth, 8)),
            dma((2,)),
            dma((3,)),
            dma((2, 3, 2)),
            dma((2, 3, 2)),
            dma((2, depth - 1)),
            dma((2, depth - 1)),
            pltpu.SemaphoreType.REGULAR,
            pltpu.SemaphoreType.REGULAR((2,)),
            pltpu.SemaphoreType.REGULAR((2,)),
        ],
        compiler_params=pltpu.CompilerParams(
            collective_id=1, has_side_effects=True, vmem_limit_bytes=62 * 2**20
        ),
        cost_estimate=pl.CostEstimate(
            flops=12 * tokens * width * hidden,
            bytes_accessed=10 * tokens * width,
            transcendentals=tokens * hidden,
        ),
        name="ffn_all_tokens",
    )(rows, upstream_all.reshape(depth, 2, 2, 2, quarter, wide), gate_w, up_w, down_w, side_w)
    rows_all, weighted, d_gate, d_up, d_rows_sum, out_sum = outs
    return (
        rows_all.reshape(tokens, width),
        weighted.reshape(tokens, hidden),
        d_gate.reshape(tokens, hidden),
        d_up.reshape(tokens, hidden),
        d_rows_sum,
        out_sum,
    )


def over_tp(block, distance):
    devices = range(lax.axis_size("tp"))
    return lax.ppermute(block, "tp", [(i, i ^ distance) for i in devices])


def one_of(array, index, axis):
    return lax.dynamic_index_in_dim(array, index, axis, keepdims=False)


def sum_over_tp(part):
    rows, columns = part.shape
    tp = lax.axis_index("tp")
    x, c = tp // 2, tp % 2
    blocks = part.reshape(2, 2, rows // 4, columns)
    got = over_tp(one_of(blocks, 1 - c, 1).astype(jnp.bfloat16), 1)
    chip = one_of(blocks, c, 1).astype(jnp.float32) + got.astype(jnp.float32)
    got = over_tp(one_of(chip, 1 - x, 0).astype(jnp.bfloat16), 2)
    return one_of(chip, x, 0) + got.astype(jnp.float32)


def gather_over_tp(block):
    tp = lax.axis_index("tp")
    x, c = tp // 2, tp % 2
    got = over_tp(block, 2)
    pair = jnp.where(x == 0, jnp.stack([block, got]), jnp.stack([got, block]))
    got = over_tp(pair, 1)
    four = jnp.where(c == 0, jnp.stack([pair, got], axis=1), jnp.stack([got, pair], axis=1))
    return four.reshape(4 * block.shape[0], block.shape[1])


def weights_kernel(
    own_in, all_out, own_sem, z_send, z_recv, y_send, y_recv
):
    at = Place()
    depth = at.depth
    half = own_in.shape[0] // 2
    last = depth - 1

    def block(k, y, h):
        return all_out.at[at.z + k, y, pl.ds(h * half, half)]

    def z_copy(k, h, direction):
        if k == 0:
            src = own_in.at[pl.ds(h * half, half)]
        else:
            src = block(k, at.y, h)
        slot = last + k - direction
        return remote(
            src,
            block(k, at.y, h),
            z_send.at[last + k, h, (direction + 1) // 2],
            z_recv.at[slot, h],
            at.at_z(at.z + direction),
        )

    def z_arrival(k, h):
        direction = 1 if k > 0 else -1
        dst = block(k, at.y, h)
        return remote(
            dst, dst, z_send.at[last + k, h, 0], z_recv.at[last + k, h], at.at_z(at.z + direction)
        )

    def y_copy(k, h):
        src = own_in.at[pl.ds(h * half, half)] if k == 0 else block(k, at.y, h)
        return remote(
            src, block(k, at.y, h), y_send.at[last + k, h], y_recv.at[last + k, h], at.next_y
        )

    own_copy = pltpu.make_async_copy(own_in, all_out.at[at.z, at.y], own_sem)
    own_copy.start()
    has_up, has_down = at.z + 1 < depth, at.z > 0
    at.greet()

    for h in (0, 1):
        pl.when(has_up)(lambda: z_copy(0, h, 1).start())
        pl.when(has_down)(lambda: z_copy(0, h, -1).start())
        y_copy(0, h).start()
    for k in range(1, depth):
        for h in (0, 1):
            for sign in (-1, 1):
                there = at.z + sign * k
                exists = (there >= 0) & (there < depth)
                onward = at.z - sign
                goes_on = exists & (onward >= 0) & (onward < depth)

                @pl.when(exists)
                def _():
                    z_arrival(sign * k, h).wait_recv()

                @pl.when(goes_on)
                def _():
                    z_copy(sign * k, h, -sign).start()

                @pl.when(exists)
                def _():
                    y_copy(sign * k, h).start()

    own_copy.wait()
    for h in (0, 1):
        pl.when(has_up)(lambda: z_copy(0, h, 1).wait_send())
        pl.when(has_down)(lambda: z_copy(0, h, -1).wait_send())
    for k in range(-last, depth):
        there = at.z + k
        exists = (there >= 0) & (there < depth)
        sign = 1 if k > 0 else -1
        onward = at.z - sign
        goes_on = exists & (onward >= 0) & (onward < depth)
        for h in (0, 1):

            @pl.when(exists)
            def _():
                y_copy(k, h).wait()

            if k != 0:

                @pl.when(goes_on)
                def _():
                    z_copy(k, h, -sign).wait_send()


def gather_over_ep(block):
    rows, columns = block.shape
    depth = lax.axis_size("ep") // 2
    anywhere = pl.BlockSpec(memory_space=pl.ANY)
    slots = 2 * depth - 1
    out = pl.pallas_call(
        weights_kernel,
        out_shape=jax.ShapeDtypeStruct((depth, 2, rows, columns), block.dtype),
        in_specs=[anywhere],
        out_specs=anywhere,
        scratch_shapes=[
            pltpu.SemaphoreType.DMA,
            pltpu.SemaphoreType.DMA((slots, 2, 2)),
            pltpu.SemaphoreType.DMA((slots, 2)),
            pltpu.SemaphoreType.DMA((slots, 2)),
            pltpu.SemaphoreType.DMA((slots, 2)),
        ],
        compiler_params=pltpu.CompilerParams(collective_id=3, has_side_effects=True),
        cost_estimate=pl.CostEstimate(
            flops=0, bytes_accessed=8 * depth * rows * columns, transcendentals=0
        ),
        name="gather_weights",
    )(block)
    return out.reshape(2 * depth * rows, columns)


def grads_kernel(
    part_in, out, own, hop, from_z, load_sem, y_send, y_recv, z_send, z_recv
):
    at = Place()
    depth = at.depth
    rows = out.shape[0]
    half = rows // 2
    f32 = jnp.float32

    def part(h):
        return pl.ds(h * half, half)

    def load(j):
        return pltpu.make_async_copy(
            part_in.at[at.ahead(j), at.y], own.at[j], load_sem.at[j]
        )

    def y_copy(j, h):
        return remote(
            part_in.at[at.ahead(j), 1 - at.y, part(h)],
            hop.at[j, part(h)],
            y_send.at[j, h],
            y_recv.at[j, h],
            at.next_y,
        )

    def z_copy(j, h):
        return remote(
            own.at[j, part(h)],
            from_z.at[j - 1, part(h)],
            z_send.at[j, h],
            z_recv.at[j, h],
            at.at_z(at.ahead(j)),
        )

    order = [j for j in range(1, depth)] + [0]
    for j in order:
        load(j).start()
    at.greet()
    for j in order:
        for h in (0, 1):
            y_copy(j, h).start()
    step = 16
    for j in order:
        load(j).wait()
        for h in (0, 1):
            y_copy(j, h).wait_recv()

            def body(i, carry):
                some = pl.ds(pl.multiple_of(h * half + i * step, step), step)
                total = own[j, some].astype(f32) + hop[j, some].astype(f32)
                own[j, some] = total.astype(own.dtype)
                return carry

            lax.fori_loop(0, half // step, body, 0)
            if j > 0:
                z_copy(j, h).start()
    for h in (0, 1):
        for k in range(1, depth):
            z_copy(k, h).wait_recv()

        def body(i, carry):
            some = pl.ds(pl.multiple_of(h * half + i * step, step), step)
            total = own[0, some].astype(f32)
            for k in range(depth - 1):
                total = total + from_z[k, some].astype(f32)
            out[some] = total
            return carry

        lax.fori_loop(0, half // step, body, 0)
    for j in range(depth):
        for h in (0, 1):
            y_copy(j, h).wait_send()
            if j > 0:
                z_copy(j, h).wait_send()


def scatter_over_ep(parts):
    depth = lax.axis_size("ep") // 2
    rows, columns = parts.shape[0] // (2 * depth), parts.shape[1]
    dtype = parts.dtype
    return pl.pallas_call(
        grads_kernel,
        out_shape=jax.ShapeDtypeStruct((rows, columns), jnp.float32),
        in_specs=[pl.BlockSpec(memory_space=pl.ANY)],
        out_specs=pl.BlockSpec(memory_space=pltpu.VMEM),
        scratch_shapes=[
            pltpu.VMEM((depth, rows, columns), dtype),
            pltpu.VMEM((depth, rows, columns), dtype),
            pltpu.VMEM((depth - 1, rows, columns), dtype),
            pltpu.SemaphoreType.DMA((depth,)),
            pltpu.SemaphoreType.DMA((depth, 2)),
            pltpu.SemaphoreType.DMA((depth, 2)),
            pltpu.SemaphoreType.DMA((depth, 2)),
            pltpu.SemaphoreType.DMA((depth, 2)),
        ],
        compiler_params=pltpu.CompilerParams(
            collective_id=4, has_side_effects=True, vmem_limit_bytes=48 * 2**20
        ),
        cost_estimate=pl.CostEstimate(
            flops=2 * parts.size, bytes_accessed=6 * parts.size, transcendentals=0
        ),
        name="scatter_grads",
    )(parts.reshape(depth, 2, rows, columns))


def share_over_devices(weights, ep_count):
    rows, hidden = weights[0].shape
    units = hidden // ep_count
    pieces = jnp.concatenate(
        [weight.T.reshape(ep_count, units, rows) for weight in weights], axis=1
    )
    moved = lax.all_to_all(pieces, "ep", split_axis=0, concat_axis=0, tiled=True)
    moved = moved.transpose(1, 0, 2).reshape(len(weights), units, ep_count * rows)
    return [moved[i] for i in range(len(weights))]


def share_back(grads, ep_count):
    units, width = grads[0].shape
    columns = width // ep_count
    pieces = jnp.concatenate(grads, axis=0).reshape(len(grads) * units, ep_count, columns)
    moved = lax.all_to_all(
        pieces.transpose(1, 0, 2), "ep", split_axis=0, concat_axis=0, tiled=True
    )
    moved = moved.reshape(ep_count, len(grads), units, columns)
    return [moved[:, i].reshape(ep_count * units, columns).T for i in range(len(grads))]


def dense_body(
    tokens,
    lengths,
    routes,
    attn_gain,
    w_query,
    w_key,
    w_value,
    w_out,
    ffn_gain,
    w_router,
    shared_mix,
    shared_gate,
    shared_up,
    shared_down,
    expert_gate,
    expert_up,
    expert_down,
    cotangent,
):
    everywhere = ("ep", "tp")
    rows_here, width = tokens.shape
    ep_count = lax.axis_size("ep")
    tp_count = lax.axis_size("tp")
    ep_index = lax.axis_index("ep")
    offset = ep_index * rows_here
    quarter = rows_here // tp_count
    first_row = lax.axis_index("tp") * quarter
    slot_here, slot_hidden = expert_gate.shape[0], expert_gate.shape[1]
    expert_count = w_router.shape[1]
    bf16, f32 = jnp.bfloat16, jnp.float32

    def my_rows(array):
        return lax.dynamic_slice_in_dim(array, first_row, quarter, 0)

    side_columns = jnp.concatenate(
        [attn_gain[:, None], ffn_gain[:, None], shared_mix[:, None], w_router], axis=1
    )
    side_columns = jnp.pad(side_columns, ((0, 0), (0, -side_columns.shape[1] % 128)))
    joined_weights = gather_over_ep(
        jnp.concatenate([w_query, w_key, w_value, w_out, side_columns], axis=1)
    )
    cotangent_rows = my_rows(cotangent)
    joined_weights, cotangent_rows = lax.optimization_barrier((joined_weights, cotangent_rows))
    heads_width = w_query.shape[1]
    qkv_weight = joined_weights[:, : 3 * heads_width]
    output_weight = joined_weights[:, 3 * heads_width : 4 * heads_width]
    side_weight = joined_weights[:, 4 * heads_width :]
    picked = jnp.any(
        my_rows(routes)[:, :, None] == jnp.arange(expert_count, dtype=jnp.int32), axis=1
    )
    picked_lanes = jnp.pad(picked.astype(bf16), ((0, 0), (3, 125 - expert_count)))
    upstream_all = lax.all_gather(
        jnp.concatenate([cotangent_rows, picked_lanes], axis=1), everywhere, axis=0, tiled=True
    )
    heads_here = heads_width // HD
    score_scale = HD ** (-0.5)
    first_norm_scale = side_weight[:, 0].astype(f32)
    second_norm_scale = side_weight[:, 1].astype(f32)
    mix_f = side_weight[:, 2].astype(f32)
    router_f = side_weight[:, 3 : 3 + expert_count].astype(f32)
    layer_input = tokens.astype(f32)
    normed_wide, norm_one = norm_forward(layer_input, first_norm_scale)
    normed_one = normed_wide.astype(bf16)
    query_at = offset + jnp.arange(rows_here, dtype=jnp.int32)
    key_at = offset - 2 * rows_here + jnp.arange(3 * rows_here, dtype=jnp.int32)
    query_seg, query_pos = sequence_info(lengths, query_at)
    key_seg, _ = sequence_info(lengths, key_at)
    cosine, sine = rope_tables(query_pos, HD)
    projected = jnp.dot(normed_one, qkv_weight, preferred_element_type=f32)
    projected = projected.reshape(rows_here, 3, heads_here, HD)
    queries = rotate(projected[:, 0], cosine, sine).astype(bf16)
    keys = rotate(projected[:, 1], cosine, sine).astype(bf16)
    values = projected[:, 2].astype(bf16)
    carried = jnp.stack([keys, values], axis=0)
    joined = jnp.concatenate(
        [passed_along(carried, "ep", 2), passed_along(carried, "ep", 1), carried], axis=1
    )
    joined, shared_gate, shared_up, shared_down = lax.optimization_barrier(
        (joined, shared_gate, shared_up, shared_down)
    )
    shared_rows = share_over_devices((shared_gate, shared_up, shared_down), ep_count)
    shared_units = shared_rows[0].shape[0]
    routed_units = slot_here * slot_hidden
    gate_cat, up_cat, down_cat = [
        jnp.pad(
            jnp.concatenate([expert.reshape(-1, width), shared], axis=0),
            ((0, -(routed_units + shared_units) % 128), (0, 0)),
        )
        for expert, shared in zip((expert_gate, expert_up, expert_down), shared_rows)
    ]
    keys_win = joined[0]
    values_win = joined[1]
    allowed = (
        (query_seg[:, None] == key_seg[None, :])
        & (key_at[None, :] <= query_at[:, None])
        & (key_at[None, :] >= 0)
    )
    scores = (
        jnp.einsum("qhd,khd->hqk", queries, keys_win, preferred_element_type=f32) * score_scale
    )
    masked = jnp.where(allowed[None], scores, -1e30)
    peak = jnp.max(masked, axis=-1, keepdims=True)
    expo = jnp.exp(masked - peak)
    total = jnp.sum(expo, axis=-1, keepdims=True)
    log_total = peak + jnp.log(total)
    weights = expo / total
    attended = jnp.einsum(
        "hqk,khd->qhd", weights.astype(bf16), values_win, preferred_element_type=f32
    )
    attended = attended.reshape(rows_here, heads_width).astype(bf16)
    attn_part = jnp.einsum("th,dh->td", attended, output_weight, preferred_element_type=f32)
    resid = my_rows(layer_input) + sum_over_tp(attn_part)
    normed_two_wide, norm_two = norm_forward(resid, second_norm_scale)
    normed_two = normed_two_wide.astype(bf16)

    logits = jnp.dot(normed_two, side_weight, preferred_element_type=f32)
    router = jax.nn.softmax(logits[:, 3 : 3 + expert_count], axis=-1)
    mixer = jax.nn.sigmoid(logits[:, 2])
    normed_all, weighted_h, d_gate_pre, d_up_pre, d_normed_sum, out_sum = ffn_over_all(
        normed_two,
        upstream_all,
        gate_cat,
        up_cat,
        down_cat,
        side_weight,
        (slot_here, slot_hidden, shared_units),
        expert_count,
    )
    ffn_sum = out_sum[:, :width]
    dots_sum = out_sum[:, width:]
    grad_down_cat = jnp.einsum(
        "tf,td->fd", weighted_h, upstream_all[:, :width], preferred_element_type=f32
    )
    block_out = gather_over_tp((resid + ffn_sum).astype(bf16))
    d_router = jnp.where(picked, dots_sum[:, 3 : 3 + expert_count], 0.0)
    d_mixer = dots_sum[:, 2]
    d_logits = router * (d_router - jnp.sum(router * d_router, axis=-1, keepdims=True))
    d_mixlogit = d_mixer * mixer * (1.0 - mixer)
    side = jnp.dot(d_logits, router_f.T, precision=highest) + d_mixlogit[:, None] * mix_f[None, :]
    normed_two_f = normed_two.astype(f32)
    d_side = jnp.concatenate([d_mixlogit[:, None], d_logits], axis=1)
    grad_side = jnp.dot(normed_two_f.T, d_side, precision=highest)
    upstream = my_rows(cotangent).astype(f32)
    d_normed_two = d_normed_sum + side
    d_resid_norm, grad_gain_two = norm_backward(resid, norm_two, second_norm_scale, d_normed_two)
    d_resid = upstream + d_resid_norm
    d_resid_low = gather_over_tp(d_resid.astype(bf16))
    grad_out = jnp.einsum("td,th->dh", d_resid_low, attended, preferred_element_type=f32)
    grad_out = lax.psum_scatter(
        grad_out.astype(bf16), "ep", scatter_dimension=0, tiled=True
    ).astype(f32)
    d_attended = jnp.einsum("td,dh->th", d_resid_low, output_weight, preferred_element_type=f32)
    d_attended = d_attended.astype(bf16).reshape(rows_here, heads_here, HD)
    scores_again = (
        jnp.einsum("qhd,khd->hqk", queries, keys_win, preferred_element_type=f32) * score_scale
    )
    probs = jnp.where(allowed[None], jnp.exp(scores_again - log_total), 0.0)
    d_probs = jnp.einsum("qhd,khd->hqk", d_attended, values_win, preferred_element_type=f32)
    delta = jnp.sum(probs * d_probs, axis=-1, keepdims=True)
    delta, d_gate_pre, d_up_pre = lax.optimization_barrier((delta, d_gate_pre, d_up_pre))
    d_scores = (probs * (d_probs - delta)).astype(bf16)
    grad_gate_cat = jnp.einsum("tf,td->fd", d_gate_pre, normed_all, preferred_element_type=f32)
    grad_up_cat = jnp.einsum("tf,td->fd", d_up_pre, normed_all, preferred_element_type=f32)
    grad_cats = (grad_gate_cat, grad_up_cat, grad_down_cat)
    grad_shared = share_back(
        [grad[routed_units : routed_units + shared_units].astype(bf16) for grad in grad_cats],
        ep_count,
    )
    grad_shared = [grad.astype(f32) for grad in grad_shared]
    grad_experts = [grad[:routed_units].reshape(expert_gate.shape) for grad in grad_cats]

    d_keys_win = (
        jnp.einsum("hqk,qhd->khd", d_scores, queries, preferred_element_type=f32) * score_scale
    )
    d_values_win = jnp.einsum(
        "hqk,qhd->khd", probs.astype(bf16), d_attended, preferred_element_type=f32
    )
    pair_grads = jnp.stack([d_keys_win, d_values_win], axis=0)
    passed = pair_grads[:, : 2 * rows_here].astype(bf16)
    from_two = passed_along(passed[:, :rows_here], "ep", -2)
    from_one = passed_along(passed[:, rows_here:], "ep", -1)
    d_queries = (
        jnp.einsum("hqk,khd->qhd", d_scores, keys_win, preferred_element_type=f32) * score_scale
    )
    running = pair_grads[:, 2 * rows_here :] + from_one.astype(f32) + from_two.astype(f32)
    d_projected = jnp.concatenate(
        [
            unrotate(d_queries, cosine, sine).astype(bf16).reshape(rows_here, heads_width),
            unrotate(running[0], cosine, sine).astype(bf16).reshape(rows_here, heads_width),
            running[1].astype(bf16).reshape(rows_here, heads_width),
        ],
        axis=1,
    )
    d_normed_one = jnp.einsum("th,dh->td", d_projected, qkv_weight, preferred_element_type=f32)
    d_normed_one = sum_over_tp(d_normed_one)
    grad_qkv = jnp.einsum("td,th->dh", normed_one, d_projected, preferred_element_type=f32)
    d_input_norm, grad_gain_one = norm_backward(
        my_rows(layer_input), my_rows(norm_one), first_norm_scale, d_normed_one
    )
    grad_tokens = gather_over_tp((d_resid + d_input_norm).astype(bf16)).astype(f32)
    small = jnp.concatenate([grad_gain_one[:, None], grad_gain_two[:, None], grad_side], axis=1)
    small = jnp.pad(small, ((0, 0), (0, 128 - small.shape[1])))
    grad_weights = scatter_over_ep(jnp.concatenate([grad_qkv, small], axis=1).astype(bf16))
    small = grad_weights[:, 3 * heads_width :]
    small = small + over_tp(small, 1)
    small = small + over_tp(small, 2)
    parts = [grad_weights[:, i * heads_width : (i + 1) * heads_width] for i in range(3)]
    return (
        block_out,
        grad_tokens,
        small[:, 0],
        parts[0],
        parts[1],
        parts[2],
        grad_out,
        small[:, 1],
        small[:, 3 : 3 + expert_count],
        small[:, 2],
        grad_shared[0],
        grad_shared[1],
        grad_shared[2],
        grad_experts[0],
        grad_experts[1],
        grad_experts[2],
    )


def chosen_body(*arrays):
    rows_here, top_count = arrays[2].shape
    slot_here, expert_count = arrays[14].shape[0], arrays[9].shape[1]
    capacity = rows_here * top_count * 7 // (5 * expert_count)
    grid_of_two = lax.axis_size("ep") % 2 == 0 and lax.axis_size("tp") == 4
    if grid_of_two and rows_here < 2 * slot_here * capacity:
        return dense_body(*arrays)
    return body(*arrays)


def solution(mesh):
    placed = (
        P("ep", None),
        P(),
        P("ep", None),
        P("ep"),
        P("ep", "tp"),
        P("ep", "tp"),
        P("ep", "tp"),
        P("ep", "tp"),
        P("ep"),
        P("ep", None),
        P("ep"),
        P("ep", "tp"),
        P("ep", "tp"),
        P("ep", "tp"),
        P("ep", "tp", None),
        P("ep", "tp", None),
        P("ep", "tp", None),
        P("ep", None),
    )
    return jax.shard_map(
        chosen_body,
        mesh=mesh,
        in_specs=placed,
        out_specs=(
            P("ep", None),
            P("ep", None),
            P("ep"),
            P("ep", "tp"),
            P("ep", "tp"),
            P("ep", "tp"),
            P("ep", "tp"),
            P("ep"),
            P("ep", None),
            P("ep"),
            P("ep", "tp"),
            P("ep", "tp"),
            P("ep", "tp"),
            P("ep", "tp", None),
            P("ep", "tp", None),
            P("ep", "tp", None),
        ),
        check_vma=False,
    )
```

```python
import functools

import jax
import jax.numpy as jnp
from jax import lax
from jax.experimental import pallas as pl
from jax.experimental.pallas import tpu as pltpu
from jax.sharding import PartitionSpec as P

HD = 128


epsilon = 1e-06
rope_base = 1000000.0
highest = lax.Precision.HIGHEST
MESH = pl.DeviceIdType.MESH


def passed_along(block, axis, distance):
    devices = range(lax.axis_size(axis))
    route = [(i - distance, i) for i in devices if i - distance in devices]
    return lax.ppermute(block, axis, route)


def rope_tables(positions, width):
    steps = jnp.arange(0, width, 2, dtype=jnp.float32) / width
    inverse = rope_base ** (-steps)
    angles = positions.astype(jnp.float32)[:, None] * inverse[None, :]
    angles = jnp.concatenate([angles, angles], axis=-1)
    return (jnp.cos(angles)[:, None, :], jnp.sin(angles)[:, None, :])


def turn_half(values):
    middle = values.shape[-1] // 2
    return jnp.concatenate([-values[..., middle:], values[..., :middle]], axis=-1)


def rotate(values, cosine, sine):
    return values * cosine + turn_half(values) * sine


def unrotate(grads, cosine, sine):
    return grads * cosine - turn_half(grads * sine)


def sequence_info(lengths, indices):
    starts = jnp.cumsum(lengths) - lengths
    inside = starts[None, :] <= indices[:, None]
    segment = jnp.sum(inside.astype(jnp.int32), axis=1) - 1
    first = jnp.max(jnp.where(inside, starts[None, :], -1), axis=1)
    return (segment, indices - first)


def norm_forward(values, gain):
    scale = lax.rsqrt(jnp.mean(values * values, axis=-1, keepdims=True) + epsilon)
    return (values * scale * gain, scale)


def norm_backward(values, scale, gain, grads):
    unit = values * scale
    scaled = grads * gain
    inner = jnp.mean(scaled * unit, axis=-1, keepdims=True)
    return (scale * (scaled - unit * inner), jnp.sum(grads * unit, axis=0))


def deliver(rows):
    arrived_rows = lax.all_to_all(rows, "ep", split_axis=0, concat_axis=0, tiled=True)
    return arrived_rows


def bring_back(parts, target, rows_here, top_count):
    moved = lax.all_to_all(parts, "ep", split_axis=0, concat_axis=0, tiled=True)
    piece = moved.shape[3]
    return moved.reshape(-1, piece)[target].reshape(rows_here, top_count, piece)


def body(
    tokens,
    lengths,
    routes,
    attn_gain,
    w_query,
    w_key,
    w_value,
    w_out,
    ffn_gain,
    w_router,
    shared_mix,
    shared_gate,
    shared_up,
    shared_down,
    expert_gate,
    expert_up,
    expert_down,
    cotangent,
):
    rows_here = tokens.shape[0]
    width = tokens.shape[1]
    ep_count = lax.axis_size("ep")
    offset = lax.axis_index("ep") * rows_here
    slot_here = expert_gate.shape[0]
    top_count = routes.shape[1]
    gathered = (
        lax.all_gather(attn_gain, "ep", axis=0, tiled=True),
        lax.all_gather(w_query, "ep", axis=0, tiled=True),
        lax.all_gather(w_key, "ep", axis=0, tiled=True),
        lax.all_gather(w_value, "ep", axis=0, tiled=True),
        lax.all_gather(w_out, "ep", axis=0, tiled=True),
        lax.all_gather(ffn_gain, "ep", axis=0, tiled=True),
        lax.all_gather(w_router, "ep", axis=0, tiled=True),
        lax.all_gather(shared_mix, "ep", axis=0, tiled=True),
        lax.all_gather(shared_gate, "ep", axis=0, tiled=True),
        lax.all_gather(shared_up, "ep", axis=0, tiled=True),
        lax.all_gather(shared_down, "ep", axis=0, tiled=True),
    )
    (
        gain_first,
        query_weight_matrix,
        key_weight_matrix,
        value_weight_matrix,
        output_weight,
        gain_second,
        router_weight,
        shared_mixer_weight,
        shared_gate_weight,
        shared_up_weight,
        shared_down_weight,
    ) = gathered
    expert_count = router_weight.shape[1]
    capacity = (rows_here * top_count * 7 // (5 * expert_count) + 7) // 8 * 8
    heads_here = query_weight_matrix.shape[1] // HD
    score_scale = HD ** (-0.5)
    first_norm_scale = gain_first.astype(jnp.float32)
    second_norm_scale = gain_second.astype(jnp.float32)
    layer_input = tokens.astype(jnp.float32)
    normed_wide, norm_one = norm_forward(layer_input, first_norm_scale)
    normed_one = normed_wide.astype(jnp.bfloat16)
    query_at = offset + jnp.arange(rows_here, dtype=jnp.int32)
    key_at = offset - 2 * rows_here + jnp.arange(3 * rows_here, dtype=jnp.int32)
    query_seg, query_pos = sequence_info(lengths, query_at)
    key_seg, _ = sequence_info(lengths, key_at)
    cosine, sine = rope_tables(query_pos, HD)
    query_pre = jnp.dot(
        normed_one, query_weight_matrix, preferred_element_type=jnp.float32
    ).reshape(rows_here, heads_here, HD)
    key_pre = jnp.dot(normed_one, key_weight_matrix, preferred_element_type=jnp.float32).reshape(
        rows_here, heads_here, HD
    )
    queries = rotate(query_pre, cosine, sine).astype(jnp.bfloat16)
    keys = rotate(key_pre, cosine, sine).astype(jnp.bfloat16)
    values = (
        jnp.dot(normed_one, value_weight_matrix, preferred_element_type=jnp.float32)
        .astype(jnp.bfloat16)
        .reshape(rows_here, heads_here, HD)
    )
    carried = jnp.stack([keys, values], axis=0)
    window = [carried]
    for hop in range(2):
        carried = passed_along(carried, "ep", 1)
        window = [carried] + window
    joined = jnp.concatenate(window, axis=1)
    keys_win = joined[0]
    values_win = joined[1]
    allowed = (
        (query_seg[:, None] == key_seg[None, :])
        & (key_at[None, :] <= query_at[:, None])
        & (key_at[None, :] >= 0)
    )
    scores = (
        jnp.einsum("qhd,khd->hqk", queries, keys_win, preferred_element_type=jnp.float32)
        * score_scale
    )
    masked = jnp.where(allowed[None], scores, -1e30)
    peak = jnp.max(masked, axis=-1, keepdims=True)
    expo = jnp.exp(masked - peak)
    total = jnp.sum(expo, axis=-1, keepdims=True)
    log_total = peak + jnp.log(total)
    weights = expo / total
    attended = jnp.einsum(
        "hqk,khd->qhd", weights.astype(jnp.bfloat16), values_win, preferred_element_type=jnp.float32
    )
    attended = attended.reshape(rows_here, heads_here * HD).astype(jnp.bfloat16)
    attn_part = jnp.einsum("th,dh->td", attended, output_weight, preferred_element_type=jnp.float32)
    resid = layer_input + lax.psum(attn_part, "tp")
    normed_two_wide, norm_two = norm_forward(resid, second_norm_scale)
    normed_two = normed_two_wide.astype(jnp.bfloat16)
    normed_two_f = normed_two.astype(jnp.float32)
    router_f = router_weight.astype(jnp.float32)
    mix_f = shared_mixer_weight.astype(jnp.float32)
    router = jax.nn.softmax(jnp.dot(normed_two_f, router_f, precision=highest), axis=-1)
    picked = routes[:, :, None] == jnp.arange(expert_count, dtype=jnp.int32)[None, None, :]
    gates = jnp.sum(jnp.where(picked, router[:, None, :], 0.0), axis=-1)
    mixer = jax.nn.sigmoid(jnp.dot(normed_two_f, mix_f, precision=highest))
    shared_g = jnp.dot(normed_two, shared_gate_weight, preferred_element_type=jnp.float32)
    shared_u = jnp.dot(normed_two, shared_up_weight, preferred_element_type=jnp.float32)
    shared_h = (jax.nn.silu(shared_g) * shared_u).astype(jnp.bfloat16)
    shared_part = jnp.einsum(
        "tf,df->td", shared_h, shared_down_weight, preferred_element_type=jnp.float32
    )
    flat = routes.reshape(-1)
    hot = (flat[:, None] == jnp.arange(expert_count, dtype=jnp.int32)[None, :]).astype(jnp.int32)
    rank = jnp.sum(jnp.cumsum(hot, axis=0) * hot, axis=1) - 1
    target = flat * capacity + rank
    slot_total = ep_count * slot_here * capacity
    owner_route = (
        jnp.zeros((slot_total,), jnp.int32)
        .at[target]
        .set(jnp.arange(rows_here * top_count, dtype=jnp.int32))
    )
    filled = jnp.zeros((slot_total,), jnp.bool_).at[target].set(True)
    owner_token = owner_route // top_count
    send_rows = jnp.where(filled[:, None], normed_two[owner_token], jnp.zeros((), jnp.bfloat16))
    arrived_rows = deliver(send_rows.reshape(ep_count, slot_here, capacity, width))
    route_g = jnp.einsum(
        "nscd,sfd->nscf", arrived_rows, expert_gate, preferred_element_type=jnp.float32
    )
    route_u = jnp.einsum(
        "nscd,sfd->nscf", arrived_rows, expert_up, preferred_element_type=jnp.float32
    )
    route_h = (jax.nn.silu(route_g) * route_u).astype(jnp.bfloat16)
    route_part = jnp.einsum(
        "nscf,sfd->nscd", route_h, expert_down, preferred_element_type=jnp.float32
    )
    back_rows = bring_back(route_part, target, rows_here, top_count)
    upstream = cotangent.astype(jnp.float32)
    routed = jnp.sum(back_rows * gates[:, :, None], axis=1)
    ffn_part = mixer[:, None] * shared_part + routed
    route_dot = jnp.sum(back_rows * upstream[:, None, :], axis=-1)
    shared_dot = jnp.sum(shared_part * upstream, axis=-1)
    ffn_total, d_gate, d_mixer = lax.psum((ffn_part, route_dot, shared_dot), "tp")
    block_out = (resid + ffn_total).astype(jnp.bfloat16)
    d_router = jnp.sum(jnp.where(picked, d_gate[:, :, None], 0.0), axis=1)
    d_logits = router * (d_router - jnp.sum(router * d_router, axis=-1, keepdims=True))
    d_mixlogit = d_mixer * mixer * (1.0 - mixer)
    side = jnp.dot(d_logits, router_f.T, precision=highest) + d_mixlogit[:, None] * mix_f[None, :]
    grad_router = jnp.dot(normed_two_f.T, d_logits, precision=highest)
    grad_mix = jnp.dot(d_mixlogit, normed_two_f, precision=highest)
    d_shared = (mixer[:, None] * upstream).astype(jnp.bfloat16)
    d_sh = jnp.dot(d_shared, shared_down_weight, preferred_element_type=jnp.float32)
    sig_shared = jax.nn.sigmoid(shared_g)
    d_sg = (d_sh * shared_u * sig_shared * (1.0 + shared_g * (1.0 - sig_shared))).astype(
        jnp.bfloat16
    )
    d_su = (d_sh * shared_g * sig_shared).astype(jnp.bfloat16)
    d_normed_part = jnp.einsum(
        "tf,df->td", d_sg, shared_gate_weight, preferred_element_type=jnp.float32
    )
    d_normed_part = d_normed_part + jnp.einsum(
        "tf,df->td", d_su, shared_up_weight, preferred_element_type=jnp.float32
    )
    grad_sgate = jnp.einsum("td,tf->df", normed_two, d_sg, preferred_element_type=jnp.float32)
    grad_sup = jnp.einsum("td,tf->df", normed_two, d_su, preferred_element_type=jnp.float32)
    grad_sdown = jnp.einsum("td,tf->df", d_shared, shared_h, preferred_element_type=jnp.float32)
    d_route = (
        (gates[:, :, None] * upstream[:, None, :])
        .astype(jnp.bfloat16)
        .reshape(rows_here * top_count, width)
    )
    send_grads = jnp.where(filled[:, None], d_route[owner_route], jnp.zeros((), jnp.bfloat16))
    received_grads = deliver(send_grads.reshape(ep_count, slot_here, capacity, width))
    d_rh = jnp.einsum(
        "nscd,sfd->nscf", received_grads, expert_down, preferred_element_type=jnp.float32
    )
    sig_route = jax.nn.sigmoid(route_g)
    d_rg = (d_rh * route_u * sig_route * (1.0 + route_g * (1.0 - sig_route))).astype(jnp.bfloat16)
    routed_up_gradient = (d_rh * route_g * sig_route).astype(jnp.bfloat16)
    row_grads = jnp.einsum("nscf,sfd->nscd", d_rg, expert_gate, preferred_element_type=jnp.float32)
    row_grads = row_grads + jnp.einsum(
        "nscf,sfd->nscd", routed_up_gradient, expert_up, preferred_element_type=jnp.float32
    )
    grad_egate = jnp.einsum(
        "qxba,qxbr->xar", d_rg, arrived_rows, preferred_element_type=jnp.float32
    )
    expert_up_gradient = jnp.einsum(
        "qxba,qxbr->xar", routed_up_gradient, arrived_rows, preferred_element_type=jnp.float32
    )
    grad_edown = jnp.einsum(
        "qxba,qxbr->xar", route_h, received_grads, preferred_element_type=jnp.float32
    )
    grads_back = bring_back(row_grads, target, rows_here, top_count)
    d_routed = jnp.sum(grads_back, axis=1)
    d_normed_two = lax.psum(d_normed_part + d_routed, "tp") + side
    d_resid_norm, grad_gain_two = norm_backward(resid, norm_two, second_norm_scale, d_normed_two)
    d_resid = upstream + d_resid_norm
    d_resid_low = d_resid.astype(jnp.bfloat16)
    grad_outw = jnp.einsum("td,th->dh", d_resid_low, attended, preferred_element_type=jnp.float32)
    d_attended = jnp.einsum(
        "td,dh->th", d_resid_low, output_weight, preferred_element_type=jnp.float32
    )
    d_attended = d_attended.astype(jnp.bfloat16).reshape(rows_here, heads_here, HD)
    scores_again = (
        jnp.einsum("qhd,khd->hqk", queries, keys_win, preferred_element_type=jnp.float32)
        * score_scale
    )
    probs = jnp.where(allowed[None], jnp.exp(scores_again - log_total), 0.0)
    d_probs = jnp.einsum("qhd,khd->hqk", d_attended, values_win, preferred_element_type=jnp.float32)
    delta = jnp.sum(probs * d_probs, axis=-1, keepdims=True)
    d_scores = (probs * (d_probs - delta)).astype(jnp.bfloat16)
    d_queries = (
        jnp.einsum("hqk,khd->qhd", d_scores, keys_win, preferred_element_type=jnp.float32)
        * score_scale
    )
    d_keys_win = (
        jnp.einsum("hqk,qhd->khd", d_scores, queries, preferred_element_type=jnp.float32)
        * score_scale
    )
    d_values_win = jnp.einsum(
        "hqk,qhd->khd", probs.astype(jnp.bfloat16), d_attended, preferred_element_type=jnp.float32
    )
    pair_grads = jnp.stack([d_keys_win, d_values_win], axis=0)
    older = pair_grads[:, :rows_here]
    later = [pair_grads[:, rows_here : 2 * rows_here], pair_grads[:, 2 * rows_here :]]
    running = older
    for hop in range(2):
        running = passed_along(running, "ep", -1)
        running = running + later[hop]
    d_query_pre = (
        unrotate(d_queries, cosine, sine).astype(jnp.bfloat16).reshape(rows_here, heads_here * HD)
    )
    d_key_pre = (
        unrotate(running[0], cosine, sine).astype(jnp.bfloat16).reshape(rows_here, heads_here * HD)
    )
    d_values = running[1].astype(jnp.bfloat16).reshape(rows_here, heads_here * HD)
    grad_queryw = jnp.einsum(
        "td,th->dh", normed_one, d_query_pre, preferred_element_type=jnp.float32
    )
    grad_keyw = jnp.einsum("td,th->dh", normed_one, d_key_pre, preferred_element_type=jnp.float32)
    grad_valuew = jnp.einsum("td,th->dh", normed_one, d_values, preferred_element_type=jnp.float32)
    d_normed_one = jnp.einsum(
        "th,dh->td", d_query_pre, query_weight_matrix, preferred_element_type=jnp.float32
    )
    d_normed_one = d_normed_one + jnp.einsum(
        "th,dh->td", d_key_pre, key_weight_matrix, preferred_element_type=jnp.float32
    )
    d_normed_one = d_normed_one + jnp.einsum(
        "th,dh->td", d_values, value_weight_matrix, preferred_element_type=jnp.float32
    )
    d_normed_one = lax.psum(d_normed_one, "tp")
    d_input_norm, grad_gain_one = norm_backward(
        layer_input, norm_one, first_norm_scale, d_normed_one
    )
    grad_tokens = d_resid + d_input_norm
    summed = (
        lax.psum_scatter(grad_gain_one, "ep", scatter_dimension=0, tiled=True),
        lax.psum_scatter(grad_queryw, "ep", scatter_dimension=0, tiled=True),
        lax.psum_scatter(grad_keyw, "ep", scatter_dimension=0, tiled=True),
        lax.psum_scatter(grad_valuew, "ep", scatter_dimension=0, tiled=True),
        lax.psum_scatter(grad_outw, "ep", scatter_dimension=0, tiled=True),
        lax.psum_scatter(grad_gain_two, "ep", scatter_dimension=0, tiled=True),
        lax.psum_scatter(grad_router, "ep", scatter_dimension=0, tiled=True),
        lax.psum_scatter(grad_mix, "ep", scatter_dimension=0, tiled=True),
        lax.psum_scatter(grad_sgate, "ep", scatter_dimension=0, tiled=True),
        lax.psum_scatter(grad_sup, "ep", scatter_dimension=0, tiled=True),
        lax.psum_scatter(grad_sdown, "ep", scatter_dimension=0, tiled=True),
    )
    return (
        block_out,
        grad_tokens,
        summed[0],
        summed[1],
        summed[2],
        summed[3],
        summed[4],
        summed[5],
        summed[6],
        summed[7],
        summed[8],
        summed[9],
        summed[10],
        grad_egate,
        expert_up_gradient,
        grad_edown,
    )


class Place:
    def __init__(self):
        self.ep, self.tp = lax.axis_index("ep"), lax.axis_index("tp")
        self.z, self.y = self.ep // 2, self.ep % 2
        self.x, self.c = self.tp // 2, self.tp % 2
        self.depth = lax.axis_size("ep") // 2
        self.next_core = (self.ep, self.x * 2 + 1 - self.c)
        self.next_x = (self.ep, (1 - self.x) * 2 + self.c)
        self.next_y = (self.z * 2 + 1 - self.y, self.tp)

    def at_z(self, z):
        return (z * 2 + self.y, self.tp)

    def ahead(self, steps):
        return lax.rem(self.z + steps, self.depth)

    def behind(self, steps):
        return lax.rem(self.z + self.depth - steps, self.depth)

    def greet(self):
        barrier = pltpu.get_barrier_semaphore()
        peers = [self.next_core, self.next_x, self.next_y]
        peers += [self.at_z(self.ahead(k)) for k in range(1, self.depth)]
        for peer in peers:
            pl.semaphore_signal(barrier, inc=1, device_id=peer, device_id_type=MESH)
        pl.semaphore_wait(barrier, len(peers))

    def greet_ep(self):
        barrier = pltpu.get_barrier_semaphore()
        count = 2 * self.depth
        for k in range(1, count):
            peer = (lax.rem(self.ep + k, count), self.tp)
            pl.semaphore_signal(barrier, inc=1, device_id=peer, device_id_type=MESH)
        pl.semaphore_wait(barrier, count - 1)


def remote(src, dst, send, recv, peer):
    return pltpu.make_async_remote_copy(
        src_ref=src, dst_ref=dst, send_sem=send, recv_sem=recv, device_id=peer, device_id_type=MESH
    )


def ffn_kernel(
    units,
    expert_count,
    rows_in,
    upstream_in,
    pair_in,
    down_in,
    side_in,
    rows_all,
    weighted_out,
    d_pair_out,
    d_rows_sum,
    out_sum,
    pair_w,
    down_w,
    side_w,
    rows_tile,
    upstream_tile,
    pair_pre,
    d_hidden,
    factors,
    dots,
    weighted_tile,
    d_pair_tile,
    d_rows_tile,
    out_tile,
    d_rows_core,
    out_core,
    d_rows_held,
    out_held,
    d_rows_hop,
    out_hop,
    d_rows_hop2,
    out_hop2,
    d_rows_z,
    out_z,
    weight_sem,
    own_sem,
    z_send,
    z_recv,
    plane_send,
    plane_recv,
    load_sem,
    store_sem,
    sum_send,
    sum_recv,
    end_send,
    end_recv,
    core_credit,
    hop_credit,
    hop2_credit,
):
    at = Place()
    depth = at.depth
    quarter, width = rows_in.shape
    half = quarter // 2
    f32, bf16 = jnp.float32, jnp.bfloat16

    def weight_copies():
        pairs = ((pair_in, pair_w), (down_in, down_w), (side_in, side_w))
        return [
            pltpu.make_async_copy(src, dst, weight_sem.at[i]) for i, (src, dst) in enumerate(pairs)
        ]

    for copy in weight_copies():
        copy.start()

    def block(j, y, x):
        return rows_all.at[at.behind(j), y, x, at.c]

    def plane_copy(j, kind):
        y, other_y = at.y, 1 - at.y
        own, other_x = at.x, 1 - at.x
        if kind == 0:
            src, peer = block(j, y, own), at.next_x
        elif kind == 1:
            src, peer = block(j, y, own), at.next_y
        elif kind == 2:
            src, peer = block(j, y, other_x).at[pl.ds(0, half)], at.next_y
        elif kind == 3:
            src, peer = block(j, other_y, own).at[pl.ds(half, half)], at.next_x
        else:
            src = block(j, other_y if kind >= 6 else y, other_x if kind % 2 else own)
            peer = at.next_core
        return remote(src, src, plane_send.at[j, kind], plane_recv.at[j, kind], peer)

    def z_copy(k):
        return remote(
            rows_in, block(0, at.y, at.x), z_send.at[k - 1], z_recv.at[k - 1], at.at_z(at.ahead(k))
        )

    def z_arrival(k):
        dst = block(k, at.y, at.x)
        return remote(dst, dst, z_send.at[k - 1], z_recv.at[k - 1], at.at_z(at.behind(k)))

    def begin(j):
        for kind in (0, 1, 4):
            plane_copy(j, kind).start()

    def spread(j):
        plane_copy(j, 0).wait_recv()
        plane_copy(j, 2).start()
        plane_copy(j, 5).start()
        plane_copy(j, 1).wait_recv()
        plane_copy(j, 3).start()
        plane_copy(j, 6).start()

    def begin_later(j):
        z_arrival(j).wait_recv()
        begin(j)

    def last_hop(j):
        plane_copy(j, 2).wait_recv()
        plane_copy(j, 3).wait_recv()
        plane_copy(j, 7).start()

    def near_ready(j):
        plane_copy(j, 4).wait_recv()
        plane_copy(j, 5).wait_recv()

    def far_ready(j):
        plane_copy(j, 6).wait_recv()
        plane_copy(j, 7).wait_recv()

    def parity(step):
        return lax.rem(step, 2)

    def slot_of(turn):
        return lax.rem(turn + 1, depth)

    def tile_at(step):
        return at.behind(slot_of(step // 2)), lax.rem(at.y + parity(step), 2)

    def load_rows(step):
        z, y = tile_at(step)
        return pltpu.make_async_copy(rows_all.at[z, y], rows_tile, load_sem.at[0])

    def load_upstream(step):
        z, y = tile_at(step)
        return pltpu.make_async_copy(upstream_in.at[z, y], upstream_tile, load_sem.at[1])

    def stores(step):
        z, y = tile_at(step)
        pairs = ((weighted_tile, weighted_out), (d_pair_tile, d_pair_out))
        return [
            pltpu.make_async_copy(src, dst.at[z, y], store_sem.at[i])
            for i, (src, dst) in enumerate(pairs)
        ]

    tiles, cores = (d_rows_tile, out_tile), (d_rows_core, out_core)
    helds, sums = (d_rows_held, out_held), (d_rows_sum, out_sum)
    hops, hops2, zs = (d_rows_hop, out_hop), (d_rows_hop2, out_hop2), (d_rows_z, out_z)

    def sum_copy(a, kind, src, dst, peer):
        return remote(src, dst, sum_send.at[a, kind], sum_recv.at[a, kind], peer)

    def core_sum(a):
        return sum_copy(a, 0, tiles[a].at[:, 1 - at.c], cores[a], at.next_core)

    def hop_sum(a, turn):
        slot = parity(turn)
        src = helds[0].at[slot, :, 1 - at.x] if a == 0 else helds[1].at[slot, 1 - at.y]
        return sum_copy(a, 1, src, hops[a], at.next_x if a == 0 else at.next_y)

    def hop2_sum(a, turn):
        slot = parity(turn)
        if a == 0:
            src, peer = helds[0].at[slot, 1 - at.y, at.x], at.next_y
        else:
            src, peer = helds[1].at[slot, at.y, 1 - at.x], at.next_x
        return sum_copy(a, 2, src, hops2[a], peer)

    def z_sum(a, turn):
        return remote(
            helds[a].at[parity(turn), at.y, at.x],
            zs[a].at[turn],
            end_send.at[a, turn],
            end_recv.at[a, turn],
            at.at_z(at.behind(turn + 1)),
        )

    def allow(semaphore, peer):
        pl.semaphore_signal(semaphore, inc=1, device_id=peer, device_id_type=MESH)

    piece = 32

    def add(into, first, second):
        def body(i, carry):
            part = pl.ds(pl.multiple_of(i * piece, piece), piece)
            into[part] = first[part] + second[part]
            return carry

        lax.fori_loop(0, quarter // piece, body, 0)

    def after_core(step):
        turn = step // 2
        held, y = parity(turn), lax.rem(at.y + parity(step), 2)

        @pl.when((parity(step) == 0) & (turn >= 2))
        def _():
            for a in (0, 1):
                z_sum(a, turn - 2).wait_send()

        for a in (0, 1):
            core_sum(a).wait()
            for x in (0, 1):
                add(helds[a].at[held, y, x], tiles[a].at[x, at.c], cores[a].at[x])

        @pl.when(step + 1 < 2 * depth)
        def _():
            allow(core_credit, at.next_core)

        @pl.when(parity(step) == 1)
        def _():
            @pl.when(turn >= 1)
            def _():
                for a in (0, 1):
                    pl.semaphore_wait(hop_credit.at[a], 1)

            for a in (0, 1):
                hop_sum(a, turn).start()

    def after_hop(turn):
        slot = parity(turn)

        @pl.when(turn >= 1)
        def _():
            for a in (0, 1):
                pl.semaphore_wait(hop2_credit.at[a], 1)

        for a in (0, 1):
            hop_sum(a, turn).wait()
            for moved in (1, 0):
                if a == 0:
                    y = lax.rem(at.y + moved, 2)
                    into, other = helds[0].at[slot, y, at.x], hops[0].at[y]
                else:
                    x = lax.rem(at.x + moved, 2)
                    into, other = helds[1].at[slot, at.y, x], hops[1].at[x]
                add(into, into, other)
                if moved:
                    hop2_sum(a, turn).start()

        @pl.when(turn + 1 < depth)
        def _():
            allow(hop_credit.at[0], at.next_x)
            allow(hop_credit.at[1], at.next_y)

    def after_hop2(turn):
        slot = parity(turn)
        for a in (0, 1):
            hop2_sum(a, turn).wait()
            into = helds[a].at[slot, at.y, at.x]
            add(into, into, hops2[a])

            @pl.when(turn + 1 < depth)
            def _():
                z_sum(a, turn).start()

        @pl.when(turn + 1 < depth)
        def _():
            allow(hop2_credit.at[0], at.next_y)
            allow(hop2_credit.at[1], at.next_x)

    load_upstream(0).start()
    at.greet()
    z_copy(1).start()
    own_copy = pltpu.make_async_copy(rows_in, block(0, at.y, at.x), own_sem)
    own_copy.start()
    own_copy.wait()
    begin(0)
    begin_later(1)
    for k in range(2, depth):
        z_copy(k).start()
    spread(1)
    near_ready(1)
    load_rows(0).start()
    for copy in weight_copies():
        copy.wait()

    tile_rows = 4 * quarter
    hidden_total = down_w.shape[0]
    lane = lax.broadcasted_iota(jnp.int32, (tile_rows, 128), 1)
    slot_here, slot_hidden, shared_hidden = units
    routed = slot_here * slot_hidden
    across = (((1,), (1,)), ((), ()))
    few = 16

    def gate_factors(rows, picked):
        logits = jnp.dot(rows, side_w[...], preferred_element_type=f32)
        chooses = (lane >= 3) & (lane < 3 + expert_count)
        peak = jnp.max(jnp.where(chooses, logits, -1e30), axis=1, keepdims=True)
        expo = jnp.where(chooses, jnp.exp(jnp.where(chooses, logits, peak) - peak), 0.0)
        routed_gate = expo / jnp.sum(expo, axis=1, keepdims=True) * picked.astype(f32)
        mix_pre = jnp.sum(jnp.where(lane == 2, logits, 0.0), axis=1, keepdims=True)
        result = jnp.where(lane == slot_here, 1.0 / (1.0 + jnp.exp(-mix_pre)), 0.0)
        for s in range(slot_here):
            chosen = lane == 3 + at.ep * slot_here + s
            gate = jnp.sum(jnp.where(chosen, routed_gate, 0.0), axis=1, keepdims=True)
            result = jnp.where(lane == s, gate, result)
        return result

    unit = lax.broadcasted_iota(jnp.int32, (few, hidden_total), 1)
    few_lane = lax.broadcasted_iota(jnp.int32, (few, 128), 1)
    slot_bounds = [s * slot_hidden for s in range(slot_here)] + [routed, hidden_total]

    def hidden_rows(i, carry):
        here = pl.ds(pl.multiple_of(i * few, few), few)
        gate_pre = pair_pre[here, :hidden_total]
        up_pre = pair_pre[here, hidden_total:]
        d_h = d_hidden[here]
        factor = jnp.broadcast_to(factors[here, slot_here : slot_here + 1], unit.shape)
        for s in reversed(range(slot_here)):
            gate = factors[here, s : s + 1]
            factor = jnp.where(unit < slot_bounds[s + 1], gate, factor)
        sig = 1.0 / (1.0 + jnp.exp(-gate_pre))
        silu = gate_pre * sig
        hidden = silu * up_pre
        product = hidden * d_h
        gated = factor * d_h
        weighted_tile[here] = (factor * hidden).astype(bf16)
        d_pair_tile[here, :hidden_total] = (gated * up_pre * (sig + silu * (1.0 - sig))).astype(bf16)
        d_pair_tile[here, hidden_total:] = (gated * silu).astype(bf16)
        result = jnp.zeros((few, 128), f32)
        for s in range(slot_here + 1):
            inside = (unit >= slot_bounds[s]) & (unit < slot_bounds[s + 1])
            dot = jnp.sum(jnp.where(inside, product, 0.0), axis=1, keepdims=True)
            where = few_lane == (2 if s == slot_here else 3 + at.ep * slot_here + s)
            result = jnp.where(where, dot, result)
        dots[here] = result.astype(bf16)
        return carry

    def first_half(step):
        load_upstream(step).wait()
        upstream = upstream_tile[...].reshape(tile_rows, upstream_tile.shape[-1])
        d_hidden[...] = lax.dot_general(
            upstream[:, :width], down_w[...], across, preferred_element_type=f32
        )
        load_rows(step).wait()
        rows = rows_tile[...].reshape(tile_rows, width)
        factors[...] = gate_factors(rows, upstream[:, width:])
        pair_pre[...] = lax.dot_general(rows, pair_w[...], across, preferred_element_type=f32)

        @pl.when(step + 1 < 2 * depth)
        def _():
            load_upstream(step + 1).start()

        @pl.when(step >= 1)
        def _():
            for copy in stores(step - 1):
                copy.wait()

        lax.fori_loop(0, tile_rows // few, hidden_rows, 0, unroll=2)
        for copy in stores(step):
            copy.start()
        turn = step // 2

        @pl.when(parity(step) == 0)
        def _():
            last_hop(slot_of(turn))

            @pl.when(turn + 2 < depth)
            def _():
                begin_later(slot_of(turn + 1))

        @pl.when((parity(step) == 1) & (turn + 1 < depth))
        def _():
            spread(slot_of(turn + 1))

    def second_half(step):
        blocks = (2, 2, quarter)
        some = width // 2
        for n in range(2):
            columns = slice(n * some, (n + 1) * some)
            part = jnp.dot(weighted_tile[...], down_w[:, columns], preferred_element_type=f32)
            out_tile[:, :, :, columns] = part.astype(bf16).reshape(blocks + (some,))
            part = jnp.dot(d_pair_tile[...], pair_w[:, columns], preferred_element_type=f32)
            d_rows_tile[:, :, :, columns] = part.astype(bf16).reshape(blocks + (some,))
        out_tile[:, :, :, width:] = dots[...].reshape(blocks + (128,))

        @pl.when(step >= 1)
        def _():
            pl.semaphore_wait(core_credit, 1)

        for a in (0, 1):
            core_sum(a).start()
        turn = step // 2

        @pl.when(parity(step) == 0)
        def _():
            far_ready(slot_of(turn))
            load_rows(step + 1).start()

        @pl.when((parity(step) == 1) & (turn + 1 < depth))
        def _():
            near_ready(slot_of(turn + 1))
            load_rows(step + 1).start()

    def step_body(step, carry):
        @pl.when(step < 2 * depth)
        def _():
            first_half(step)

        @pl.when((step >= 1) & (step <= 2 * depth))
        def _():
            after_core(step - 1)

        odd = parity(step) == 1

        @pl.when(odd & (step >= 3))
        def _():
            after_hop((step - 3) // 2)

        @pl.when(jnp.logical_not(odd) & (step >= 4))
        def _():
            after_hop2((step - 4) // 2)

        @pl.when(step < 2 * depth)
        def _():
            second_half(step)

        return carry

    lax.fori_loop(0, 2 * depth + 3, step_body, 0)
    last = parity(depth - 1)
    for a in (0, 1):
        for turn in range(depth - 1):
            z_sum(a, turn).wait_recv()

        def total_body(i, carry):
            part = pl.ds(pl.multiple_of(i * piece, piece), piece)
            total = helds[a][last, at.y, at.x, part].astype(f32)
            for k in range(depth - 1):
                total = total + zs[a][k, part].astype(f32)
            sums[a][part] = total
            return carry

        lax.fori_loop(0, quarter // piece, total_body, 0)
    for copy in stores(2 * depth - 1):
        copy.wait()
    for a in (0, 1):
        z_sum(a, depth - 2).wait_send()
    for k in range(1, depth):
        z_copy(k).wait_send()

    def finish(j, carry):
        for kind in range(8):
            plane_copy(j, kind).wait_send()
        return carry

    lax.fori_loop(0, depth, finish, 0)


def ffn_over_all(rows, upstream_all, pair_w, down_w, side_w, units, expert_count):
    quarter, width = rows.shape
    ep_count, tp_count = lax.axis_size("ep"), lax.axis_size("tp")
    depth = ep_count // 2
    hidden = down_w.shape[0]
    bf16, f32 = jnp.bfloat16, jnp.float32
    wide = width + 128
    tile_rows = tp_count * quarter
    tokens = ep_count * tile_rows
    anywhere = pl.BlockSpec(memory_space=pl.ANY)
    in_vmem = pl.BlockSpec(memory_space=pltpu.VMEM)

    def both(*lead):
        return [pltpu.VMEM(lead + (quarter, columns), bf16) for columns in (width, wide)]

    dma = pltpu.SemaphoreType.DMA
    outs = pl.pallas_call(
        functools.partial(ffn_kernel, units, expert_count),
        out_shape=(
            jax.ShapeDtypeStruct((depth, 2, 2, 2, quarter, width), bf16),
            jax.ShapeDtypeStruct((depth, 2, tile_rows, hidden), bf16),
            jax.ShapeDtypeStruct((depth, 2, tile_rows, 2 * hidden), bf16),
            jax.ShapeDtypeStruct((quarter, width), f32),
            jax.ShapeDtypeStruct((quarter, wide), f32),
        ),
        in_specs=[anywhere] * 5,
        out_specs=(anywhere,) * 3 + (in_vmem,) * 2,
        scratch_shapes=[
            pltpu.VMEM((2 * hidden, width), bf16),
            pltpu.VMEM((hidden, width), bf16),
            pltpu.VMEM((width, 128), bf16),
            pltpu.VMEM((2, 2, quarter, width), bf16),
            pltpu.VMEM((2, 2, quarter, wide), bf16),
            pltpu.VMEM((tile_rows, 2 * hidden), f32),
            pltpu.VMEM((tile_rows, hidden), f32),
            pltpu.VMEM((tile_rows, 128), f32),
            pltpu.VMEM((tile_rows, 128), bf16),
            pltpu.VMEM((tile_rows, hidden), bf16),
            pltpu.VMEM((tile_rows, 2 * hidden), bf16),
        ]
        + both(2, 2)
        + both(2)
        + both(2, 2, 2)
        + both(2)
        + both()
        + both(depth - 1)
        + [
            dma((3,)),
            dma,
            dma((depth - 1,)),
            dma((depth - 1,)),
            dma((depth, 8)),
            dma((depth, 8)),
            dma((2,)),
            dma((2,)),
            dma((2, 3)),
            dma((2, 3)),
            dma((2, depth - 1)),
            dma((2, depth - 1)),
            pltpu.SemaphoreType.REGULAR,
            pltpu.SemaphoreType.REGULAR((2,)),
            pltpu.SemaphoreType.REGULAR((2,)),
        ],
        compiler_params=pltpu.CompilerParams(
            collective_id=1, has_side_effects=True, vmem_limit_bytes=62 * 2**20
        ),
        cost_estimate=pl.CostEstimate(
            flops=12 * tokens * width * hidden,
            bytes_accessed=10 * tokens * width,
            transcendentals=tokens * hidden,
        ),
        name="ffn_all_tokens",
    )(rows, upstream_all.reshape(depth, 2, 2, 2, quarter, wide), pair_w, down_w, side_w)
    rows_all, weighted, d_pair, d_rows_sum, out_sum = outs
    return (
        rows_all.reshape(tokens, width),
        weighted.reshape(tokens, hidden),
        d_pair.reshape(tokens, 2 * hidden),
        d_rows_sum,
        out_sum,
    )


def over_tp(block, distance):
    devices = range(lax.axis_size("tp"))
    return lax.ppermute(block, "tp", [(i, i ^ distance) for i in devices])


def one_of(array, index, axis):
    return lax.dynamic_index_in_dim(array, index, axis, keepdims=False)


def sum_over_tp(part):
    rows, columns = part.shape
    tp = lax.axis_index("tp")
    x, c = tp // 2, tp % 2
    blocks = part.reshape(2, 2, rows // 4, columns)
    got = over_tp(one_of(blocks, 1 - c, 1).astype(jnp.bfloat16), 1)
    chip = one_of(blocks, c, 1).astype(jnp.float32) + got.astype(jnp.float32)
    got = over_tp(one_of(chip, 1 - x, 0).astype(jnp.bfloat16), 2)
    return one_of(chip, x, 0) + got.astype(jnp.float32)


def gather_over_tp(block):
    tp = lax.axis_index("tp")
    x, c = tp // 2, tp % 2
    got = over_tp(block, 2)
    pair = jnp.where(x == 0, jnp.stack([block, got]), jnp.stack([got, block]))
    got = over_tp(pair, 1)
    four = jnp.where(c == 0, jnp.stack([pair, got], axis=1), jnp.stack([got, pair], axis=1))
    return four.reshape(4 * block.shape[0], block.shape[1])


def swap_copies(at, pieces_in, pieces_out, send_sem, recv_sem, leave):
    count = 2 * at.depth
    copies = []
    for k in range(1, count):
        to, back = lax.rem(at.ep + k, count), lax.rem(at.ep + count - k, count)
        if leave:
            src, dst, peer = pieces_in.at[to], pieces_out.at[at.ep], to
        else:
            src, dst, peer = pieces_in.at[back], pieces_out.at[back], back
        copies.append(remote(src, dst, send_sem.at[k], recv_sem.at[k], (peer, at.tp)))
    return copies


def weights_kernel(
    own_in,
    pieces_in,
    all_out,
    pieces_out,
    own_sem,
    z_send,
    z_recv,
    y_send,
    y_recv,
    swap_send,
    swap_recv,
):
    at = Place()
    depth = at.depth
    half = own_in.shape[0] // 2
    last = depth - 1

    def block(k, y, h):
        return all_out.at[at.z + k, y, pl.ds(h * half, half)]

    def z_copy(k, h, direction):
        if k == 0:
            src = own_in.at[pl.ds(h * half, half)]
        else:
            src = block(k, at.y, h)
        slot = last + k - direction
        return remote(
            src,
            block(k, at.y, h),
            z_send.at[last + k, h, (direction + 1) // 2],
            z_recv.at[slot, h],
            at.at_z(at.z + direction),
        )

    def z_arrival(k, h):
        direction = 1 if k > 0 else -1
        dst = block(k, at.y, h)
        return remote(
            dst, dst, z_send.at[last + k, h, 0], z_recv.at[last + k, h], at.at_z(at.z + direction)
        )

    def y_copy(k, h):
        src = own_in.at[pl.ds(h * half, half)] if k == 0 else block(k, at.y, h)
        return remote(
            src, block(k, at.y, h), y_send.at[last + k, h], y_recv.at[last + k, h], at.next_y
        )

    own_copies = [
        pltpu.make_async_copy(own_in, all_out.at[at.z, at.y], own_sem.at[0]),
        pltpu.make_async_copy(pieces_in.at[at.ep], pieces_out.at[at.ep], own_sem.at[1]),
    ]
    for copy in own_copies:
        copy.start()
    has_up, has_down = at.z + 1 < depth, at.z > 0
    at.greet_ep()

    for h in (0, 1):
        pl.when(has_up)(lambda: z_copy(0, h, 1).start())
        pl.when(has_down)(lambda: z_copy(0, h, -1).start())
        y_copy(0, h).start()
    swap = (at, pieces_in, pieces_out, swap_send, swap_recv)
    for copy in swap_copies(*swap, True):
        copy.start()
    for k in range(1, depth):
        for h in (0, 1):
            for sign in (-1, 1):
                there = at.z + sign * k
                exists = (there >= 0) & (there < depth)
                onward = at.z - sign
                goes_on = exists & (onward >= 0) & (onward < depth)

                @pl.when(exists)
                def _():
                    z_arrival(sign * k, h).wait_recv()

                @pl.when(goes_on)
                def _():
                    z_copy(sign * k, h, -sign).start()

                @pl.when(exists)
                def _():
                    y_copy(sign * k, h).start()

    for copy in own_copies:
        copy.wait()
    for copy in swap_copies(*swap, False):
        copy.wait_recv()
    for copy in swap_copies(*swap, True):
        copy.wait_send()
    for h in (0, 1):
        pl.when(has_up)(lambda: z_copy(0, h, 1).wait_send())
        pl.when(has_down)(lambda: z_copy(0, h, -1).wait_send())
    for k in range(-last, depth):
        there = at.z + k
        exists = (there >= 0) & (there < depth)
        sign = 1 if k > 0 else -1
        onward = at.z - sign
        goes_on = exists & (onward >= 0) & (onward < depth)
        for h in (0, 1):

            @pl.when(exists)
            def _():
                y_copy(k, h).wait()

            if k != 0:

                @pl.when(goes_on)
                def _():
                    z_copy(k, h, -sign).wait_send()


def gather_over_ep(block, pieces):
    rows, columns = block.shape
    depth = lax.axis_size("ep") // 2
    anywhere = pl.BlockSpec(memory_space=pl.ANY)
    slots = 2 * depth - 1
    out, pieces = pl.pallas_call(
        weights_kernel,
        out_shape=(
            jax.ShapeDtypeStruct((depth, 2, rows, columns), block.dtype),
            jax.ShapeDtypeStruct(pieces.shape, pieces.dtype),
        ),
        in_specs=[anywhere] * 2,
        out_specs=(anywhere,) * 2,
        scratch_shapes=[
            pltpu.SemaphoreType.DMA((2,)),
            pltpu.SemaphoreType.DMA((slots, 2, 2)),
            pltpu.SemaphoreType.DMA((slots, 2)),
            pltpu.SemaphoreType.DMA((slots, 2)),
            pltpu.SemaphoreType.DMA((slots, 2)),
            pltpu.SemaphoreType.DMA((2 * depth,)),
            pltpu.SemaphoreType.DMA((2 * depth,)),
        ],
        compiler_params=pltpu.CompilerParams(collective_id=3, has_side_effects=True),
        cost_estimate=pl.CostEstimate(
            flops=0, bytes_accessed=8 * depth * rows * columns, transcendentals=0
        ),
        name="gather_weights",
    )(block, pieces)
    return out.reshape(2 * depth * rows, columns), pieces


def grads_kernel(
    part_in, out, own, hop, from_z, load_sem, y_send, y_recv, z_send, z_recv
):
    at = Place()
    depth = at.depth
    rows = out.shape[0]
    half = rows // 2
    f32 = jnp.float32

    def part(h):
        return pl.ds(h * half, half)

    def load(j):
        return pltpu.make_async_copy(
            part_in.at[at.ahead(j), at.y], own.at[j], load_sem.at[j]
        )

    def y_copy(j, h):
        return remote(
            part_in.at[at.ahead(j), 1 - at.y, part(h)],
            hop.at[j, part(h)],
            y_send.at[j, h],
            y_recv.at[j, h],
            at.next_y,
        )

    def z_copy(j, h):
        return remote(
            own.at[j, part(h)],
            from_z.at[j - 1, part(h)],
            z_send.at[j, h],
            z_recv.at[j, h],
            at.at_z(at.ahead(j)),
        )

    order = [j for j in range(1, depth)] + [0]
    for j in order:
        load(j).start()
    at.greet()
    for j in order:
        for h in (0, 1):
            y_copy(j, h).start()
    step = 16
    for j in order:
        load(j).wait()
        for h in (0, 1):
            y_copy(j, h).wait_recv()

            def body(i, carry):
                some = pl.ds(pl.multiple_of(h * half + i * step, step), step)
                total = own[j, some].astype(f32) + hop[j, some].astype(f32)
                own[j, some] = total.astype(own.dtype)
                return carry

            lax.fori_loop(0, half // step, body, 0)
            if j > 0:
                z_copy(j, h).start()
    for h in (0, 1):
        for k in range(1, depth):
            z_copy(k, h).wait_recv()

        def body(i, carry):
            some = pl.ds(pl.multiple_of(h * half + i * step, step), step)
            total = own[0, some].astype(f32)
            for k in range(depth - 1):
                total = total + from_z[k, some].astype(f32)
            out[some] = total
            return carry

        lax.fori_loop(0, half // step, body, 0)
    for j in range(depth):
        for h in (0, 1):
            y_copy(j, h).wait_send()
            if j > 0:
                z_copy(j, h).wait_send()


def scatter_over_ep(parts):
    depth = lax.axis_size("ep") // 2
    rows, columns = parts.shape[0] // (2 * depth), parts.shape[1]
    dtype = parts.dtype
    return pl.pallas_call(
        grads_kernel,
        out_shape=jax.ShapeDtypeStruct((rows, columns), jnp.float32),
        in_specs=[pl.BlockSpec(memory_space=pl.ANY)],
        out_specs=pl.BlockSpec(memory_space=pltpu.VMEM),
        scratch_shapes=[
            pltpu.VMEM((depth, rows, columns), dtype),
            pltpu.VMEM((depth, rows, columns), dtype),
            pltpu.VMEM((depth - 1, rows, columns), dtype),
            pltpu.SemaphoreType.DMA((depth,)),
            pltpu.SemaphoreType.DMA((depth, 2)),
            pltpu.SemaphoreType.DMA((depth, 2)),
            pltpu.SemaphoreType.DMA((depth, 2)),
            pltpu.SemaphoreType.DMA((depth, 2)),
        ],
        compiler_params=pltpu.CompilerParams(
            collective_id=4, has_side_effects=True, vmem_limit_bytes=48 * 2**20
        ),
        cost_estimate=pl.CostEstimate(
            flops=2 * parts.size, bytes_accessed=6 * parts.size, transcendentals=0
        ),
        name="scatter_grads",
    )(parts.reshape(depth, 2, rows, columns))


def shared_pieces(weights, ep_count):
    rows, hidden = weights[0].shape
    units = hidden // ep_count
    return jnp.concatenate([weight.T.reshape(ep_count, units, rows) for weight in weights], axis=1)


def shared_units_of(pieces, count):
    ep_count, units, rows = pieces.shape
    return pieces.transpose(1, 0, 2).reshape(count, units // count, ep_count * rows)


def share_back(grads, ep_count):
    units, width = grads[0].shape
    columns = width // ep_count
    pieces = jnp.concatenate(grads, axis=0).reshape(len(grads) * units, ep_count, columns)
    moved = lax.all_to_all(
        pieces.transpose(1, 0, 2), "ep", split_axis=0, concat_axis=0, tiled=True
    )
    moved = moved.reshape(ep_count, len(grads), units, columns)
    return [moved[:, i].reshape(ep_count * units, columns).T for i in range(len(grads))]


def dense_body(
    tokens,
    lengths,
    routes,
    attn_gain,
    w_query,
    w_key,
    w_value,
    w_out,
    ffn_gain,
    w_router,
    shared_mix,
    shared_gate,
    shared_up,
    shared_down,
    expert_gate,
    expert_up,
    expert_down,
    cotangent,
):
    everywhere = ("ep", "tp")
    rows_here, width = tokens.shape
    ep_count = lax.axis_size("ep")
    tp_count = lax.axis_size("tp")
    ep_index = lax.axis_index("ep")
    offset = ep_index * rows_here
    quarter = rows_here // tp_count
    first_row = lax.axis_index("tp") * quarter
    slot_here, slot_hidden = expert_gate.shape[0], expert_gate.shape[1]
    expert_count = w_router.shape[1]
    bf16, f32 = jnp.bfloat16, jnp.float32

    def my_rows(array):
        return lax.dynamic_slice_in_dim(array, first_row, quarter, 0)

    side_columns = jnp.concatenate(
        [attn_gain[:, None], ffn_gain[:, None], shared_mix[:, None], w_router], axis=1
    )
    side_columns = jnp.pad(side_columns, ((0, 0), (0, -side_columns.shape[1] % 128)))
    joined_weights, pieces = gather_over_ep(
        jnp.concatenate([w_query, w_key, w_value, w_out, side_columns], axis=1),
        shared_pieces((shared_gate, shared_up, shared_down), ep_count),
    )
    cotangent_rows = my_rows(cotangent)
    joined_weights, cotangent_rows = lax.optimization_barrier((joined_weights, cotangent_rows))
    heads_width = w_query.shape[1]
    qkv_weight = joined_weights[:, : 3 * heads_width]
    output_weight = joined_weights[:, 3 * heads_width : 4 * heads_width]
    side_weight = joined_weights[:, 4 * heads_width :]
    picked = jnp.any(
        my_rows(routes)[:, :, None] == jnp.arange(expert_count, dtype=jnp.int32), axis=1
    )
    picked_lanes = jnp.pad(picked.astype(bf16), ((0, 0), (3, 125 - expert_count)))
    upstream_all = lax.all_gather(
        jnp.concatenate([cotangent_rows, picked_lanes], axis=1), everywhere, axis=0, tiled=True
    )
    shared_rows = shared_units_of(pieces, 3)
    shared_units = shared_rows.shape[1]
    routed_units = slot_here * slot_hidden
    gate_cat, up_cat, down_cat = [
        jnp.pad(
            jnp.concatenate([expert.reshape(-1, width), shared], axis=0),
            ((0, -(routed_units + shared_units) % 128), (0, 0)),
        )
        for expert, shared in zip((expert_gate, expert_up, expert_down), shared_rows)
    ]
    pair_cat = jnp.concatenate([gate_cat, up_cat], axis=0)
    hidden_total = gate_cat.shape[0]

    heads_here = heads_width // HD
    score_scale = HD ** (-0.5)
    first_norm_scale = side_weight[:, 0].astype(f32)
    second_norm_scale = side_weight[:, 1].astype(f32)
    mix_f = side_weight[:, 2].astype(f32)
    router_f = side_weight[:, 3 : 3 + expert_count].astype(f32)
    layer_input = tokens.astype(f32)
    normed_wide, norm_one = norm_forward(layer_input, first_norm_scale)
    normed_one = normed_wide.astype(bf16)
    query_at = offset + jnp.arange(rows_here, dtype=jnp.int32)
    key_at = offset - 2 * rows_here + jnp.arange(3 * rows_here, dtype=jnp.int32)
    query_seg, query_pos = sequence_info(lengths, query_at)
    key_seg, _ = sequence_info(lengths, key_at)
    cosine, sine = rope_tables(query_pos, HD)
    projected = jnp.dot(normed_one, qkv_weight, preferred_element_type=f32)
    projected = projected.reshape(rows_here, 3, heads_here, HD)
    queries = rotate(projected[:, 0], cosine, sine).astype(bf16)
    keys = rotate(projected[:, 1], cosine, sine).astype(bf16)
    values = projected[:, 2].astype(bf16)
    carried = jnp.stack([keys, values], axis=0)
    joined = jnp.concatenate(
        [passed_along(carried, "ep", 2), passed_along(carried, "ep", 1), carried], axis=1
    )
    keys_win = joined[0]
    values_win = joined[1]
    allowed = (
        (query_seg[:, None] == key_seg[None, :])
        & (key_at[None, :] <= query_at[:, None])
        & (key_at[None, :] >= 0)
    )
    scores = (
        jnp.einsum("qhd,khd->hqk", queries, keys_win, preferred_element_type=f32) * score_scale
    )
    masked = jnp.where(allowed[None], scores, -1e30)
    peak = jnp.max(masked, axis=-1, keepdims=True)
    expo = jnp.exp(masked - peak)
    total = jnp.sum(expo, axis=-1, keepdims=True)
    log_total = peak + jnp.log(total)
    weights = expo / total
    attended = jnp.einsum(
        "hqk,khd->qhd", weights.astype(bf16), values_win, preferred_element_type=f32
    )
    attended = attended.reshape(rows_here, heads_width).astype(bf16)
    attn_part = jnp.einsum("th,dh->td", attended, output_weight, preferred_element_type=f32)
    resid = my_rows(layer_input) + sum_over_tp(attn_part)
    normed_two_wide, norm_two = norm_forward(resid, second_norm_scale)
    normed_two = normed_two_wide.astype(bf16)

    logits = jnp.dot(normed_two, side_weight, preferred_element_type=f32)
    router = jax.nn.softmax(logits[:, 3 : 3 + expert_count], axis=-1)
    mixer = jax.nn.sigmoid(logits[:, 2])
    normed_all, weighted_h, d_pair_pre, d_normed_sum, out_sum = ffn_over_all(
        normed_two,
        upstream_all,
        pair_cat,
        down_cat,
        side_weight,
        (slot_here, slot_hidden, shared_units),
        expert_count,
    )
    ffn_sum = out_sum[:, :width]
    dots_sum = out_sum[:, width:]
    grad_down_cat = jnp.einsum(
        "tf,td->fd", weighted_h, upstream_all[:, :width], preferred_element_type=f32
    )
    block_out = gather_over_tp((resid + ffn_sum).astype(bf16))
    d_router = jnp.where(picked, dots_sum[:, 3 : 3 + expert_count], 0.0)
    d_mixer = dots_sum[:, 2]
    d_logits = router * (d_router - jnp.sum(router * d_router, axis=-1, keepdims=True))
    d_mixlogit = d_mixer * mixer * (1.0 - mixer)
    side = jnp.dot(d_logits, router_f.T, precision=highest) + d_mixlogit[:, None] * mix_f[None, :]
    normed_two_f = normed_two.astype(f32)
    d_side = jnp.concatenate([d_mixlogit[:, None], d_logits], axis=1)
    grad_side = jnp.dot(normed_two_f.T, d_side, precision=highest)
    upstream = my_rows(cotangent).astype(f32)
    d_normed_two = d_normed_sum + side
    d_resid_norm, grad_gain_two = norm_backward(resid, norm_two, second_norm_scale, d_normed_two)
    d_resid = upstream + d_resid_norm
    d_resid_low = gather_over_tp(d_resid.astype(bf16))
    grad_out = jnp.einsum("td,th->dh", d_resid_low, attended, preferred_element_type=f32)
    grad_out = lax.psum_scatter(
        grad_out.astype(bf16), "ep", scatter_dimension=0, tiled=True
    ).astype(f32)
    d_attended = jnp.einsum("td,dh->th", d_resid_low, output_weight, preferred_element_type=f32)
    d_attended = d_attended.astype(bf16).reshape(rows_here, heads_here, HD)
    scores_again = (
        jnp.einsum("qhd,khd->hqk", queries, keys_win, preferred_element_type=f32) * score_scale
    )
    probs = jnp.where(allowed[None], jnp.exp(scores_again - log_total), 0.0)
    d_probs = jnp.einsum("qhd,khd->hqk", d_attended, values_win, preferred_element_type=f32)
    delta = jnp.sum(probs * d_probs, axis=-1, keepdims=True)
    delta, d_pair_pre = lax.optimization_barrier((delta, d_pair_pre))
    d_scores = (probs * (d_probs - delta)).astype(bf16)
    grad_pair = jnp.einsum("tf,td->fd", d_pair_pre, normed_all, preferred_element_type=f32)
    grad_cats = (grad_pair[:hidden_total], grad_pair[hidden_total:], grad_down_cat)
    grad_shared = share_back(
        [grad[routed_units : routed_units + shared_units].astype(bf16) for grad in grad_cats],
        ep_count,
    )
    grad_shared = [grad.astype(f32) for grad in grad_shared]
    grad_experts = [grad[:routed_units].reshape(expert_gate.shape) for grad in grad_cats]

    d_keys_win = (
        jnp.einsum("hqk,qhd->khd", d_scores, queries, preferred_element_type=f32) * score_scale
    )
    d_values_win = jnp.einsum(
        "hqk,qhd->khd", probs.astype(bf16), d_attended, preferred_element_type=f32
    )
    pair_grads = jnp.stack([d_keys_win, d_values_win], axis=0)
    passed = pair_grads[:, : 2 * rows_here].astype(bf16)
    from_two = passed_along(passed[:, :rows_here], "ep", -2)
    from_one = passed_along(passed[:, rows_here:], "ep", -1)
    d_queries = (
        jnp.einsum("hqk,khd->qhd", d_scores, keys_win, preferred_element_type=f32) * score_scale
    )
    running = pair_grads[:, 2 * rows_here :] + from_one.astype(f32) + from_two.astype(f32)
    d_projected = jnp.concatenate(
        [
            unrotate(d_queries, cosine, sine).astype(bf16).reshape(rows_here, heads_width),
            unrotate(running[0], cosine, sine).astype(bf16).reshape(rows_here, heads_width),
            running[1].astype(bf16).reshape(rows_here, heads_width),
        ],
        axis=1,
    )
    d_normed_one = jnp.einsum("th,dh->td", d_projected, qkv_weight, preferred_element_type=f32)
    d_normed_one = sum_over_tp(d_normed_one)
    grad_qkv = jnp.einsum("td,th->dh", normed_one, d_projected, preferred_element_type=f32)
    d_input_norm, grad_gain_one = norm_backward(
        my_rows(layer_input), my_rows(norm_one), first_norm_scale, d_normed_one
    )
    grad_tokens = gather_over_tp((d_resid + d_input_norm).astype(bf16)).astype(f32)
    small = jnp.concatenate([grad_gain_one[:, None], grad_gain_two[:, None], grad_side], axis=1)
    small = jnp.pad(small, ((0, 0), (0, 128 - small.shape[1])))
    grad_weights = scatter_over_ep(jnp.concatenate([grad_qkv, small], axis=1).astype(bf16))
    small = grad_weights[:, 3 * heads_width :]
    small = small + over_tp(small, 1)
    small = small + over_tp(small, 2)
    parts = [grad_weights[:, i * heads_width : (i + 1) * heads_width] for i in range(3)]
    return (
        block_out,
        grad_tokens,
        small[:, 0],
        parts[0],
        parts[1],
        parts[2],
        grad_out,
        small[:, 1],
        small[:, 3 : 3 + expert_count],
        small[:, 2],
        grad_shared[0],
        grad_shared[1],
        grad_shared[2],
        grad_experts[0],
        grad_experts[1],
        grad_experts[2],
    )


def chosen_body(*arrays):
    rows_here, top_count = arrays[2].shape
    slot_here, expert_count = arrays[14].shape[0], arrays[9].shape[1]
    capacity = rows_here * top_count * 7 // (5 * expert_count)
    grid_of_two = lax.axis_size("ep") % 2 == 0 and lax.axis_size("tp") == 4
    if grid_of_two and rows_here < 2 * slot_here * capacity:
        return dense_body(*arrays)
    return body(*arrays)


def solution(mesh):
    placed = (
        P("ep", None),
        P(),
        P("ep", None),
        P("ep"),
        P("ep", "tp"),
        P("ep", "tp"),
        P("ep", "tp"),
        P("ep", "tp"),
        P("ep"),
        P("ep", None),
        P("ep"),
        P("ep", "tp"),
        P("ep", "tp"),
        P("ep", "tp"),
        P("ep", "tp", None),
        P("ep", "tp", None),
        P("ep", "tp", None),
        P("ep", None),
    )
    return jax.shard_map(
        chosen_body,
        mesh=mesh,
        in_specs=placed,
        out_specs=(
            P("ep", None),
            P("ep", None),
            P("ep"),
            P("ep", "tp"),
            P("ep", "tp"),
            P("ep", "tp"),
            P("ep", "tp"),
            P("ep"),
            P("ep", None),
            P("ep"),
            P("ep", "tp"),
            P("ep", "tp"),
            P("ep", "tp"),
            P("ep", "tp", None),
            P("ep", "tp", None),
            P("ep", "tp", None),
        ),
        check_vma=False,
    )
```

```python
import functools

import jax
import jax.numpy as jnp
from jax import lax
from jax.experimental import pallas as pl
from jax.experimental.pallas import tpu as pltpu
from jax.sharding import PartitionSpec as P

HD = 128


epsilon = 1e-06
rope_base = 1000000.0
highest = lax.Precision.HIGHEST
MESH = pl.DeviceIdType.MESH


def passed_along(block, axis, distance):
    devices = range(lax.axis_size(axis))
    route = [(i - distance, i) for i in devices if i - distance in devices]
    return lax.ppermute(block, axis, route)


def rope_tables(positions, width):
    steps = jnp.arange(0, width, 2, dtype=jnp.float32) / width
    inverse = rope_base ** (-steps)
    angles = positions.astype(jnp.float32)[:, None] * inverse[None, :]
    angles = jnp.concatenate([angles, angles], axis=-1)
    return (jnp.cos(angles)[:, None, :], jnp.sin(angles)[:, None, :])


def turn_half(values):
    middle = values.shape[-1] // 2
    return jnp.concatenate([-values[..., middle:], values[..., :middle]], axis=-1)


def rotate(values, cosine, sine):
    return values * cosine + turn_half(values) * sine


def unrotate(grads, cosine, sine):
    return grads * cosine - turn_half(grads * sine)


def sequence_info(lengths, indices):
    starts = jnp.cumsum(lengths) - lengths
    inside = starts[None, :] <= indices[:, None]
    segment = jnp.sum(inside.astype(jnp.int32), axis=1) - 1
    first = jnp.max(jnp.where(inside, starts[None, :], -1), axis=1)
    return (segment, indices - first)


def norm_forward(values, gain):
    scale = lax.rsqrt(jnp.mean(values * values, axis=-1, keepdims=True) + epsilon)
    return (values * scale * gain, scale)


def norm_backward(values, scale, gain, grads):
    unit = values * scale
    scaled = grads * gain
    inner = jnp.mean(scaled * unit, axis=-1, keepdims=True)
    return (scale * (scaled - unit * inner), jnp.sum(grads * unit, axis=0))


def deliver(rows):
    arrived_rows = lax.all_to_all(rows, "ep", split_axis=0, concat_axis=0, tiled=True)
    return arrived_rows


def bring_back(parts, target, rows_here, top_count):
    moved = lax.all_to_all(parts, "ep", split_axis=0, concat_axis=0, tiled=True)
    piece = moved.shape[3]
    return moved.reshape(-1, piece)[target].reshape(rows_here, top_count, piece)


def body(
    tokens,
    lengths,
    routes,
    attn_gain,
    w_query,
    w_key,
    w_value,
    w_out,
    ffn_gain,
    w_router,
    shared_mix,
    shared_gate,
    shared_up,
    shared_down,
    expert_gate,
    expert_up,
    expert_down,
    cotangent,
):
    rows_here = tokens.shape[0]
    width = tokens.shape[1]
    ep_count = lax.axis_size("ep")
    offset = lax.axis_index("ep") * rows_here
    slot_here = expert_gate.shape[0]
    top_count = routes.shape[1]
    gathered = (
        lax.all_gather(attn_gain, "ep", axis=0, tiled=True),
        lax.all_gather(w_query, "ep", axis=0, tiled=True),
        lax.all_gather(w_key, "ep", axis=0, tiled=True),
        lax.all_gather(w_value, "ep", axis=0, tiled=True),
        lax.all_gather(w_out, "ep", axis=0, tiled=True),
        lax.all_gather(ffn_gain, "ep", axis=0, tiled=True),
        lax.all_gather(w_router, "ep", axis=0, tiled=True),
        lax.all_gather(shared_mix, "ep", axis=0, tiled=True),
        lax.all_gather(shared_gate, "ep", axis=0, tiled=True),
        lax.all_gather(shared_up, "ep", axis=0, tiled=True),
        lax.all_gather(shared_down, "ep", axis=0, tiled=True),
    )
    (
        gain_first,
        query_weight_matrix,
        key_weight_matrix,
        value_weight_matrix,
        output_weight,
        gain_second,
        router_weight,
        shared_mixer_weight,
        shared_gate_weight,
        shared_up_weight,
        shared_down_weight,
    ) = gathered
    expert_count = router_weight.shape[1]
    capacity = (rows_here * top_count * 7 // (5 * expert_count) + 7) // 8 * 8
    heads_here = query_weight_matrix.shape[1] // HD
    score_scale = HD ** (-0.5)
    first_norm_scale = gain_first.astype(jnp.float32)
    second_norm_scale = gain_second.astype(jnp.float32)
    layer_input = tokens.astype(jnp.float32)
    normed_wide, norm_one = norm_forward(layer_input, first_norm_scale)
    normed_one = normed_wide.astype(jnp.bfloat16)
    query_at = offset + jnp.arange(rows_here, dtype=jnp.int32)
    key_at = offset - 2 * rows_here + jnp.arange(3 * rows_here, dtype=jnp.int32)
    query_seg, query_pos = sequence_info(lengths, query_at)
    key_seg, _ = sequence_info(lengths, key_at)
    cosine, sine = rope_tables(query_pos, HD)
    query_pre = jnp.dot(
        normed_one, query_weight_matrix, preferred_element_type=jnp.float32
    ).reshape(rows_here, heads_here, HD)
    key_pre = jnp.dot(normed_one, key_weight_matrix, preferred_element_type=jnp.float32).reshape(
        rows_here, heads_here, HD
    )
    queries = rotate(query_pre, cosine, sine).astype(jnp.bfloat16)
    keys = rotate(key_pre, cosine, sine).astype(jnp.bfloat16)
    values = (
        jnp.dot(normed_one, value_weight_matrix, preferred_element_type=jnp.float32)
        .astype(jnp.bfloat16)
        .reshape(rows_here, heads_here, HD)
    )
    carried = jnp.stack([keys, values], axis=0)
    window = [carried]
    for hop in range(2):
        carried = passed_along(carried, "ep", 1)
        window = [carried] + window
    joined = jnp.concatenate(window, axis=1)
    keys_win = joined[0]
    values_win = joined[1]
    allowed = (
        (query_seg[:, None] == key_seg[None, :])
        & (key_at[None, :] <= query_at[:, None])
        & (key_at[None, :] >= 0)
    )
    scores = (
        jnp.einsum("qhd,khd->hqk", queries, keys_win, preferred_element_type=jnp.float32)
        * score_scale
    )
    masked = jnp.where(allowed[None], scores, -1e30)
    peak = jnp.max(masked, axis=-1, keepdims=True)
    expo = jnp.exp(masked - peak)
    total = jnp.sum(expo, axis=-1, keepdims=True)
    log_total = peak + jnp.log(total)
    weights = expo / total
    attended = jnp.einsum(
        "hqk,khd->qhd", weights.astype(jnp.bfloat16), values_win, preferred_element_type=jnp.float32
    )
    attended = attended.reshape(rows_here, heads_here * HD).astype(jnp.bfloat16)
    attn_part = jnp.einsum("th,dh->td", attended, output_weight, preferred_element_type=jnp.float32)
    resid = layer_input + lax.psum(attn_part, "tp")
    normed_two_wide, norm_two = norm_forward(resid, second_norm_scale)
    normed_two = normed_two_wide.astype(jnp.bfloat16)
    normed_two_f = normed_two.astype(jnp.float32)
    router_f = router_weight.astype(jnp.float32)
    mix_f = shared_mixer_weight.astype(jnp.float32)
    router = jax.nn.softmax(jnp.dot(normed_two_f, router_f, precision=highest), axis=-1)
    picked = routes[:, :, None] == jnp.arange(expert_count, dtype=jnp.int32)[None, None, :]
    gates = jnp.sum(jnp.where(picked, router[:, None, :], 0.0), axis=-1)
    mixer = jax.nn.sigmoid(jnp.dot(normed_two_f, mix_f, precision=highest))
    shared_g = jnp.dot(normed_two, shared_gate_weight, preferred_element_type=jnp.float32)
    shared_u = jnp.dot(normed_two, shared_up_weight, preferred_element_type=jnp.float32)
    shared_h = (jax.nn.silu(shared_g) * shared_u).astype(jnp.bfloat16)
    shared_part = jnp.einsum(
        "tf,df->td", shared_h, shared_down_weight, preferred_element_type=jnp.float32
    )
    flat = routes.reshape(-1)
    hot = (flat[:, None] == jnp.arange(expert_count, dtype=jnp.int32)[None, :]).astype(jnp.int32)
    rank = jnp.sum(jnp.cumsum(hot, axis=0) * hot, axis=1) - 1
    target = flat * capacity + rank
    slot_total = ep_count * slot_here * capacity
    owner_route = (
        jnp.zeros((slot_total,), jnp.int32)
        .at[target]
        .set(jnp.arange(rows_here * top_count, dtype=jnp.int32))
    )
    filled = jnp.zeros((slot_total,), jnp.bool_).at[target].set(True)
    owner_token = owner_route // top_count
    send_rows = jnp.where(filled[:, None], normed_two[owner_token], jnp.zeros((), jnp.bfloat16))
    arrived_rows = deliver(send_rows.reshape(ep_count, slot_here, capacity, width))
    route_g = jnp.einsum(
        "nscd,sfd->nscf", arrived_rows, expert_gate, preferred_element_type=jnp.float32
    )
    route_u = jnp.einsum(
        "nscd,sfd->nscf", arrived_rows, expert_up, preferred_element_type=jnp.float32
    )
    route_h = (jax.nn.silu(route_g) * route_u).astype(jnp.bfloat16)
    route_part = jnp.einsum(
        "nscf,sfd->nscd", route_h, expert_down, preferred_element_type=jnp.float32
    )
    back_rows = bring_back(route_part, target, rows_here, top_count)
    upstream = cotangent.astype(jnp.float32)
    routed = jnp.sum(back_rows * gates[:, :, None], axis=1)
    ffn_part = mixer[:, None] * shared_part + routed
    route_dot = jnp.sum(back_rows * upstream[:, None, :], axis=-1)
    shared_dot = jnp.sum(shared_part * upstream, axis=-1)
    ffn_total, d_gate, d_mixer = lax.psum((ffn_part, route_dot, shared_dot), "tp")
    block_out = (resid + ffn_total).astype(jnp.bfloat16)
    d_router = jnp.sum(jnp.where(picked, d_gate[:, :, None], 0.0), axis=1)
    d_logits = router * (d_router - jnp.sum(router * d_router, axis=-1, keepdims=True))
    d_mixlogit = d_mixer * mixer * (1.0 - mixer)
    side = jnp.dot(d_logits, router_f.T, precision=highest) + d_mixlogit[:, None] * mix_f[None, :]
    grad_router = jnp.dot(normed_two_f.T, d_logits, precision=highest)
    grad_mix = jnp.dot(d_mixlogit, normed_two_f, precision=highest)
    d_shared = (mixer[:, None] * upstream).astype(jnp.bfloat16)
    d_sh = jnp.dot(d_shared, shared_down_weight, preferred_element_type=jnp.float32)
    sig_shared = jax.nn.sigmoid(shared_g)
    d_sg = (d_sh * shared_u * sig_shared * (1.0 + shared_g * (1.0 - sig_shared))).astype(
        jnp.bfloat16
    )
    d_su = (d_sh * shared_g * sig_shared).astype(jnp.bfloat16)
    d_normed_part = jnp.einsum(
        "tf,df->td", d_sg, shared_gate_weight, preferred_element_type=jnp.float32
    )
    d_normed_part = d_normed_part + jnp.einsum(
        "tf,df->td", d_su, shared_up_weight, preferred_element_type=jnp.float32
    )
    grad_sgate = jnp.einsum("td,tf->df", normed_two, d_sg, preferred_element_type=jnp.float32)
    grad_sup = jnp.einsum("td,tf->df", normed_two, d_su, preferred_element_type=jnp.float32)
    grad_sdown = jnp.einsum("td,tf->df", d_shared, shared_h, preferred_element_type=jnp.float32)
    d_route = (
        (gates[:, :, None] * upstream[:, None, :])
        .astype(jnp.bfloat16)
        .reshape(rows_here * top_count, width)
    )
    send_grads = jnp.where(filled[:, None], d_route[owner_route], jnp.zeros((), jnp.bfloat16))
    received_grads = deliver(send_grads.reshape(ep_count, slot_here, capacity, width))
    d_rh = jnp.einsum(
        "nscd,sfd->nscf", received_grads, expert_down, preferred_element_type=jnp.float32
    )
    sig_route = jax.nn.sigmoid(route_g)
    d_rg = (d_rh * route_u * sig_route * (1.0 + route_g * (1.0 - sig_route))).astype(jnp.bfloat16)
    routed_up_gradient = (d_rh * route_g * sig_route).astype(jnp.bfloat16)
    row_grads = jnp.einsum("nscf,sfd->nscd", d_rg, expert_gate, preferred_element_type=jnp.float32)
    row_grads = row_grads + jnp.einsum(
        "nscf,sfd->nscd", routed_up_gradient, expert_up, preferred_element_type=jnp.float32
    )
    grad_egate = jnp.einsum(
        "qxba,qxbr->xar", d_rg, arrived_rows, preferred_element_type=jnp.float32
    )
    expert_up_gradient = jnp.einsum(
        "qxba,qxbr->xar", routed_up_gradient, arrived_rows, preferred_element_type=jnp.float32
    )
    grad_edown = jnp.einsum(
        "qxba,qxbr->xar", route_h, received_grads, preferred_element_type=jnp.float32
    )
    grads_back = bring_back(row_grads, target, rows_here, top_count)
    d_routed = jnp.sum(grads_back, axis=1)
    d_normed_two = lax.psum(d_normed_part + d_routed, "tp") + side
    d_resid_norm, grad_gain_two = norm_backward(resid, norm_two, second_norm_scale, d_normed_two)
    d_resid = upstream + d_resid_norm
    d_resid_low = d_resid.astype(jnp.bfloat16)
    grad_outw = jnp.einsum("td,th->dh", d_resid_low, attended, preferred_element_type=jnp.float32)
    d_attended = jnp.einsum(
        "td,dh->th", d_resid_low, output_weight, preferred_element_type=jnp.float32
    )
    d_attended = d_attended.astype(jnp.bfloat16).reshape(rows_here, heads_here, HD)
    scores_again = (
        jnp.einsum("qhd,khd->hqk", queries, keys_win, preferred_element_type=jnp.float32)
        * score_scale
    )
    probs = jnp.where(allowed[None], jnp.exp(scores_again - log_total), 0.0)
    d_probs = jnp.einsum("qhd,khd->hqk", d_attended, values_win, preferred_element_type=jnp.float32)
    delta = jnp.sum(probs * d_probs, axis=-1, keepdims=True)
    d_scores = (probs * (d_probs - delta)).astype(jnp.bfloat16)
    d_queries = (
        jnp.einsum("hqk,khd->qhd", d_scores, keys_win, preferred_element_type=jnp.float32)
        * score_scale
    )
    d_keys_win = (
        jnp.einsum("hqk,qhd->khd", d_scores, queries, preferred_element_type=jnp.float32)
        * score_scale
    )
    d_values_win = jnp.einsum(
        "hqk,qhd->khd", probs.astype(jnp.bfloat16), d_attended, preferred_element_type=jnp.float32
    )
    pair_grads = jnp.stack([d_keys_win, d_values_win], axis=0)
    older = pair_grads[:, :rows_here]
    later = [pair_grads[:, rows_here : 2 * rows_here], pair_grads[:, 2 * rows_here :]]
    running = older
    for hop in range(2):
        running = passed_along(running, "ep", -1)
        running = running + later[hop]
    d_query_pre = (
        unrotate(d_queries, cosine, sine).astype(jnp.bfloat16).reshape(rows_here, heads_here * HD)
    )
    d_key_pre = (
        unrotate(running[0], cosine, sine).astype(jnp.bfloat16).reshape(rows_here, heads_here * HD)
    )
    d_values = running[1].astype(jnp.bfloat16).reshape(rows_here, heads_here * HD)
    grad_queryw = jnp.einsum(
        "td,th->dh", normed_one, d_query_pre, preferred_element_type=jnp.float32
    )
    grad_keyw = jnp.einsum("td,th->dh", normed_one, d_key_pre, preferred_element_type=jnp.float32)
    grad_valuew = jnp.einsum("td,th->dh", normed_one, d_values, preferred_element_type=jnp.float32)
    d_normed_one = jnp.einsum(
        "th,dh->td", d_query_pre, query_weight_matrix, preferred_element_type=jnp.float32
    )
    d_normed_one = d_normed_one + jnp.einsum(
        "th,dh->td", d_key_pre, key_weight_matrix, preferred_element_type=jnp.float32
    )
    d_normed_one = d_normed_one + jnp.einsum(
        "th,dh->td", d_values, value_weight_matrix, preferred_element_type=jnp.float32
    )
    d_normed_one = lax.psum(d_normed_one, "tp")
    d_input_norm, grad_gain_one = norm_backward(
        layer_input, norm_one, first_norm_scale, d_normed_one
    )
    grad_tokens = d_resid + d_input_norm
    summed = (
        lax.psum_scatter(grad_gain_one, "ep", scatter_dimension=0, tiled=True),
        lax.psum_scatter(grad_queryw, "ep", scatter_dimension=0, tiled=True),
        lax.psum_scatter(grad_keyw, "ep", scatter_dimension=0, tiled=True),
        lax.psum_scatter(grad_valuew, "ep", scatter_dimension=0, tiled=True),
        lax.psum_scatter(grad_outw, "ep", scatter_dimension=0, tiled=True),
        lax.psum_scatter(grad_gain_two, "ep", scatter_dimension=0, tiled=True),
        lax.psum_scatter(grad_router, "ep", scatter_dimension=0, tiled=True),
        lax.psum_scatter(grad_mix, "ep", scatter_dimension=0, tiled=True),
        lax.psum_scatter(grad_sgate, "ep", scatter_dimension=0, tiled=True),
        lax.psum_scatter(grad_sup, "ep", scatter_dimension=0, tiled=True),
        lax.psum_scatter(grad_sdown, "ep", scatter_dimension=0, tiled=True),
    )
    return (
        block_out,
        grad_tokens,
        summed[0],
        summed[1],
        summed[2],
        summed[3],
        summed[4],
        summed[5],
        summed[6],
        summed[7],
        summed[8],
        summed[9],
        summed[10],
        grad_egate,
        expert_up_gradient,
        grad_edown,
    )


class Place:
    def __init__(self):
        self.ep, self.tp = lax.axis_index("ep"), lax.axis_index("tp")
        self.z, self.y = self.ep // 2, self.ep % 2
        self.x, self.c = self.tp // 2, self.tp % 2
        self.depth = lax.axis_size("ep") // 2
        self.next_core = (self.ep, self.x * 2 + 1 - self.c)
        self.next_x = (self.ep, (1 - self.x) * 2 + self.c)
        self.next_y = (self.z * 2 + 1 - self.y, self.tp)

    def at_z(self, z):
        return (z * 2 + self.y, self.tp)

    def ahead(self, steps):
        return lax.rem(self.z + steps, self.depth)

    def behind(self, steps):
        return lax.rem(self.z + self.depth - steps, self.depth)

    def greet(self):
        barrier = pltpu.get_barrier_semaphore()
        peers = [self.next_core, self.next_x, self.next_y]
        peers += [self.at_z(self.ahead(k)) for k in range(1, self.depth)]
        for peer in peers:
            pl.semaphore_signal(barrier, inc=1, device_id=peer, device_id_type=MESH)
        pl.semaphore_wait(barrier, len(peers))

    def greet_row(self):
        barrier = pltpu.get_barrier_semaphore()
        count = 2 * self.depth
        peers = [(lax.rem(self.ep + k, count), self.tp) for k in range(1, count)]
        peers += [self.next_core, self.next_x]
        for peer in peers:
            pl.semaphore_signal(barrier, inc=1, device_id=peer, device_id_type=MESH)
        pl.semaphore_wait(barrier, len(peers))

    def greet_ep(self):
        barrier = pltpu.get_barrier_semaphore()
        count = 2 * self.depth
        for k in range(1, count):
            peer = (lax.rem(self.ep + k, count), self.tp)
            pl.semaphore_signal(barrier, inc=1, device_id=peer, device_id_type=MESH)
        pl.semaphore_wait(barrier, count - 1)


def remote(src, dst, send, recv, peer):
    return pltpu.make_async_remote_copy(
        src_ref=src, dst_ref=dst, send_sem=send, recv_sem=recv, device_id=peer, device_id_type=MESH
    )


def ffn_kernel(
    units,
    expert_count,
    rows_in,
    upstream_in,
    pair_in,
    down_in,
    side_in,
    rows_all,
    weighted_out,
    d_pair_out,
    d_rows_sum,
    out_sum,
    pair_w,
    down_w,
    side_w,
    rows_tile,
    upstream_tile,
    pair_pre,
    d_hidden,
    factors,
    dots,
    weighted_tile,
    d_pair_tile,
    d_rows_tile,
    out_tile,
    d_rows_core,
    out_core,
    d_rows_held,
    out_held,
    d_rows_hop,
    out_hop,
    d_rows_hop2,
    out_hop2,
    d_rows_z,
    out_z,
    weight_sem,
    own_sem,
    z_send,
    z_recv,
    plane_send,
    plane_recv,
    load_sem,
    store_sem,
    sum_send,
    sum_recv,
    end_send,
    end_recv,
    core_credit,
    hop_credit,
    hop2_credit,
):
    at = Place()
    depth = at.depth
    quarter, width = rows_in.shape
    half = quarter // 2
    f32, bf16 = jnp.float32, jnp.bfloat16

    def weight_copies():
        pairs = ((pair_in, pair_w), (down_in, down_w), (side_in, side_w))
        return [
            pltpu.make_async_copy(src, dst, weight_sem.at[i]) for i, (src, dst) in enumerate(pairs)
        ]

    for copy in weight_copies():
        copy.start()

    def block(j, y, x):
        return rows_all.at[at.behind(j), y, x, at.c]

    def plane_copy(j, kind):
        y, other_y = at.y, 1 - at.y
        own, other_x = at.x, 1 - at.x
        if kind == 0:
            src, peer = block(j, y, own), at.next_x
        elif kind == 1:
            src, peer = block(j, y, own), at.next_y
        elif kind == 2:
            src, peer = block(j, y, other_x).at[pl.ds(0, half)], at.next_y
        elif kind == 3:
            src, peer = block(j, other_y, own).at[pl.ds(half, half)], at.next_x
        else:
            src = block(j, other_y if kind >= 6 else y, other_x if kind % 2 else own)
            peer = at.next_core
        return remote(src, src, plane_send.at[j, kind], plane_recv.at[j, kind], peer)

    def z_copy(k):
        return remote(
            rows_in, block(0, at.y, at.x), z_send.at[k - 1], z_recv.at[k - 1], at.at_z(at.ahead(k))
        )

    def z_arrival(k):
        dst = block(k, at.y, at.x)
        return remote(dst, dst, z_send.at[k - 1], z_recv.at[k - 1], at.at_z(at.behind(k)))

    def begin(j):
        for kind in (0, 1, 4):
            plane_copy(j, kind).start()

    def spread(j):
        plane_copy(j, 0).wait_recv()
        plane_copy(j, 2).start()
        plane_copy(j, 5).start()
        plane_copy(j, 1).wait_recv()
        plane_copy(j, 3).start()
        plane_copy(j, 6).start()

    def begin_later(j):
        z_arrival(j).wait_recv()
        begin(j)

    def last_hop(j):
        plane_copy(j, 2).wait_recv()
        plane_copy(j, 3).wait_recv()
        plane_copy(j, 7).start()

    def near_ready(j):
        plane_copy(j, 4).wait_recv()
        plane_copy(j, 5).wait_recv()

    def far_ready(j):
        plane_copy(j, 6).wait_recv()
        plane_copy(j, 7).wait_recv()

    def parity(step):
        return lax.rem(step, 2)

    def slot_of(turn):
        return lax.rem(turn + 1, depth)

    def tile_at(step):
        return at.behind(slot_of(step // 2)), lax.rem(at.y + parity(step), 2)

    def load_rows(step):
        z, y = tile_at(step)
        return pltpu.make_async_copy(rows_all.at[z, y], rows_tile, load_sem.at[0])

    def load_upstream(step):
        z, y = tile_at(step)
        return pltpu.make_async_copy(upstream_in.at[z, y], upstream_tile, load_sem.at[1])

    def stores(step):
        z, y = tile_at(step)
        pairs = ((weighted_tile, weighted_out), (d_pair_tile, d_pair_out))
        return [
            pltpu.make_async_copy(src, dst.at[z, y], store_sem.at[i])
            for i, (src, dst) in enumerate(pairs)
        ]

    tiles, cores = (d_rows_tile, out_tile), (d_rows_core, out_core)
    helds, sums = (d_rows_held, out_held), (d_rows_sum, out_sum)
    hops, hops2, zs = (d_rows_hop, out_hop), (d_rows_hop2, out_hop2), (d_rows_z, out_z)

    def sum_copy(a, kind, src, dst, peer):
        return remote(src, dst, sum_send.at[a, kind], sum_recv.at[a, kind], peer)

    def core_sum(a):
        return sum_copy(a, 0, tiles[a].at[:, 1 - at.c], cores[a], at.next_core)

    def hop_sum(a, turn):
        slot = parity(turn)
        src = helds[0].at[slot, :, 1 - at.x] if a == 0 else helds[1].at[slot, 1 - at.y]
        return sum_copy(a, 1, src, hops[a], at.next_x if a == 0 else at.next_y)

    def hop2_sum(a, turn):
        slot = parity(turn)
        if a == 0:
            src, peer = helds[0].at[slot, 1 - at.y, at.x], at.next_y
        else:
            src, peer = helds[1].at[slot, at.y, 1 - at.x], at.next_x
        return sum_copy(a, 2, src, hops2[a], peer)

    def z_sum(a, turn):
        return remote(
            helds[a].at[parity(turn), at.y, at.x],
            zs[a].at[turn],
            end_send.at[a, turn],
            end_recv.at[a, turn],
            at.at_z(at.behind(turn + 1)),
        )

    def allow(semaphore, peer):
        pl.semaphore_signal(semaphore, inc=1, device_id=peer, device_id_type=MESH)

    piece = 32

    def add(into, first, second):
        def body(i, carry):
            part = pl.ds(pl.multiple_of(i * piece, piece), piece)
            into[part] = first[part] + second[part]
            return carry

        lax.fori_loop(0, quarter // piece, body, 0)

    def after_core(step):
        turn = step // 2
        held, y = parity(turn), lax.rem(at.y + parity(step), 2)

        @pl.when((parity(step) == 0) & (turn >= 2))
        def _():
            for a in (0, 1):
                z_sum(a, turn - 2).wait_send()

        for a in (0, 1):
            core_sum(a).wait()
            for x in (0, 1):
                add(helds[a].at[held, y, x], tiles[a].at[x, at.c], cores[a].at[x])

        @pl.when(step + 1 < 2 * depth)
        def _():
            allow(core_credit, at.next_core)

        @pl.when(parity(step) == 1)
        def _():
            @pl.when(turn >= 1)
            def _():
                for a in (0, 1):
                    pl.semaphore_wait(hop_credit.at[a], 1)

            for a in (0, 1):
                hop_sum(a, turn).start()

    def after_hop(turn):
        slot = parity(turn)

        @pl.when(turn >= 1)
        def _():
            for a in (0, 1):
                pl.semaphore_wait(hop2_credit.at[a], 1)

        for a in (0, 1):
            hop_sum(a, turn).wait()
            for moved in (1, 0):
                if a == 0:
                    y = lax.rem(at.y + moved, 2)
                    into, other = helds[0].at[slot, y, at.x], hops[0].at[y]
                else:
                    x = lax.rem(at.x + moved, 2)
                    into, other = helds[1].at[slot, at.y, x], hops[1].at[x]
                add(into, into, other)
                if moved:
                    hop2_sum(a, turn).start()

        @pl.when(turn + 1 < depth)
        def _():
            allow(hop_credit.at[0], at.next_x)
            allow(hop_credit.at[1], at.next_y)

    def after_hop2(turn):
        slot = parity(turn)
        for a in (0, 1):
            hop2_sum(a, turn).wait()
            into = helds[a].at[slot, at.y, at.x]
            add(into, into, hops2[a])

            @pl.when(turn + 1 < depth)
            def _():
                z_sum(a, turn).start()

        @pl.when(turn + 1 < depth)
        def _():
            allow(hop2_credit.at[0], at.next_y)
            allow(hop2_credit.at[1], at.next_x)

    load_upstream(0).start()
    at.greet()
    z_copy(1).start()
    own_copy = pltpu.make_async_copy(rows_in, block(0, at.y, at.x), own_sem)
    own_copy.start()
    own_copy.wait()
    begin(0)
    begin_later(1)
    for k in range(2, depth):
        z_copy(k).start()
    spread(1)
    near_ready(1)
    load_rows(0).start()
    for copy in weight_copies():
        copy.wait()

    tile_rows = 4 * quarter
    hidden_total = down_w.shape[0]
    lane = lax.broadcasted_iota(jnp.int32, (tile_rows, 128), 1)
    slot_here, slot_hidden, shared_hidden = units
    routed = slot_here * slot_hidden
    across = (((1,), (1,)), ((), ()))
    few = 16

    def gate_factors(rows, picked):
        logits = jnp.dot(rows, side_w[...], preferred_element_type=f32)
        chooses = (lane >= 3) & (lane < 3 + expert_count)
        peak = jnp.max(jnp.where(chooses, logits, -1e30), axis=1, keepdims=True)
        expo = jnp.where(chooses, jnp.exp(jnp.where(chooses, logits, peak) - peak), 0.0)
        routed_gate = expo / jnp.sum(expo, axis=1, keepdims=True) * picked.astype(f32)
        mix_pre = jnp.sum(jnp.where(lane == 2, logits, 0.0), axis=1, keepdims=True)
        result = jnp.where(lane == slot_here, 1.0 / (1.0 + jnp.exp(-mix_pre)), 0.0)
        for s in range(slot_here):
            chosen = lane == 3 + at.ep * slot_here + s
            gate = jnp.sum(jnp.where(chosen, routed_gate, 0.0), axis=1, keepdims=True)
            result = jnp.where(lane == s, gate, result)
        return result

    unit = lax.broadcasted_iota(jnp.int32, (few, hidden_total), 1)
    few_lane = lax.broadcasted_iota(jnp.int32, (few, 128), 1)
    slot_bounds = [s * slot_hidden for s in range(slot_here)] + [routed, hidden_total]

    def hidden_rows(i, carry):
        here = pl.ds(pl.multiple_of(i * few, few), few)
        gate_pre = pair_pre[here, :hidden_total]
        up_pre = pair_pre[here, hidden_total:]
        d_h = d_hidden[here]
        factor = jnp.broadcast_to(factors[here, slot_here : slot_here + 1], unit.shape)
        for s in reversed(range(slot_here)):
            gate = factors[here, s : s + 1]
            factor = jnp.where(unit < slot_bounds[s + 1], gate, factor)
        sig = 1.0 / (1.0 + jnp.exp(-gate_pre))
        silu = gate_pre * sig
        hidden = silu * up_pre
        product = hidden * d_h
        gated = factor * d_h
        weighted_tile[here] = (factor * hidden).astype(bf16)
        d_pair_tile[here, :hidden_total] = (gated * up_pre * (sig + silu * (1.0 - sig))).astype(bf16)
        d_pair_tile[here, hidden_total:] = (gated * silu).astype(bf16)
        result = jnp.zeros((few, 128), f32)
        for s in range(slot_here + 1):
            inside = (unit >= slot_bounds[s]) & (unit < slot_bounds[s + 1])
            dot = jnp.sum(jnp.where(inside, product, 0.0), axis=1, keepdims=True)
            where = few_lane == (2 if s == slot_here else 3 + at.ep * slot_here + s)
            result = jnp.where(where, dot, result)
        dots[here] = result.astype(bf16)
        return carry

    def first_half(step):
        load_upstream(step).wait()
        upstream = upstream_tile[...].reshape(tile_rows, upstream_tile.shape[-1])
        d_hidden[...] = lax.dot_general(
            upstream[:, :width], down_w[...], across, preferred_element_type=f32
        )
        load_rows(step).wait()
        rows = rows_tile[...].reshape(tile_rows, width)
        factors[...] = gate_factors(rows, upstream[:, width:])
        pair_pre[...] = lax.dot_general(rows, pair_w[...], across, preferred_element_type=f32)

        @pl.when(step + 1 < 2 * depth)
        def _():
            load_upstream(step + 1).start()

        @pl.when(step >= 1)
        def _():
            for copy in stores(step - 1):
                copy.wait()

        lax.fori_loop(0, tile_rows // few, hidden_rows, 0, unroll=2)
        for copy in stores(step):
            copy.start()
        turn = step // 2

        @pl.when(parity(step) == 0)
        def _():
            last_hop(slot_of(turn))

            @pl.when(turn + 2 < depth)
            def _():
                begin_later(slot_of(turn + 1))

        @pl.when((parity(step) == 1) & (turn + 1 < depth))
        def _():
            spread(slot_of(turn + 1))

    def second_half(step):
        blocks = (2, 2, quarter)
        some = width // 2
        for n in range(2):
            columns = slice(n * some, (n + 1) * some)
            part = jnp.dot(weighted_tile[...], down_w[:, columns], preferred_element_type=f32)
            out_tile[:, :, :, columns] = part.astype(bf16).reshape(blocks + (some,))
            part = jnp.dot(d_pair_tile[...], pair_w[:, columns], preferred_element_type=f32)
            d_rows_tile[:, :, :, columns] = part.astype(bf16).reshape(blocks + (some,))
        out_tile[:, :, :, width:] = dots[...].reshape(blocks + (128,))

        @pl.when(step >= 1)
        def _():
            pl.semaphore_wait(core_credit, 1)

        for a in (0, 1):
            core_sum(a).start()
        turn = step // 2

        @pl.when(parity(step) == 0)
        def _():
            far_ready(slot_of(turn))
            load_rows(step + 1).start()

        @pl.when((parity(step) == 1) & (turn + 1 < depth))
        def _():
            near_ready(slot_of(turn + 1))
            load_rows(step + 1).start()

    def step_body(step, carry):
        @pl.when(step < 2 * depth)
        def _():
            first_half(step)

        @pl.when((step >= 1) & (step <= 2 * depth))
        def _():
            after_core(step - 1)

        odd = parity(step) == 1

        @pl.when(odd & (step >= 3))
        def _():
            after_hop((step - 3) // 2)

        @pl.when(jnp.logical_not(odd) & (step >= 4))
        def _():
            after_hop2((step - 4) // 2)

        @pl.when(step < 2 * depth)
        def _():
            second_half(step)

        return carry

    lax.fori_loop(0, 2 * depth + 3, step_body, 0)
    last = parity(depth - 1)
    for a in (0, 1):
        for turn in range(depth - 1):
            z_sum(a, turn).wait_recv()

        def total_body(i, carry):
            part = pl.ds(pl.multiple_of(i * piece, piece), piece)
            total = helds[a][last, at.y, at.x, part].astype(f32)
            for k in range(depth - 1):
                total = total + zs[a][k, part].astype(f32)
            sums[a][part] = total
            return carry

        lax.fori_loop(0, quarter // piece, total_body, 0)
    for copy in stores(2 * depth - 1):
        copy.wait()
    for a in (0, 1):
        z_sum(a, depth - 2).wait_send()
    for k in range(1, depth):
        z_copy(k).wait_send()

    def finish(j, carry):
        for kind in range(8):
            plane_copy(j, kind).wait_send()
        return carry

    lax.fori_loop(0, depth, finish, 0)


def ffn_over_all(rows, upstream_all, pair_w, down_w, side_w, units, expert_count):
    quarter, width = rows.shape
    ep_count, tp_count = lax.axis_size("ep"), lax.axis_size("tp")
    depth = ep_count // 2
    hidden = down_w.shape[0]
    bf16, f32 = jnp.bfloat16, jnp.float32
    wide = width + 128
    tile_rows = tp_count * quarter
    tokens = ep_count * tile_rows
    anywhere = pl.BlockSpec(memory_space=pl.ANY)
    in_vmem = pl.BlockSpec(memory_space=pltpu.VMEM)

    def both(*lead):
        return [pltpu.VMEM(lead + (quarter, columns), bf16) for columns in (width, wide)]

    dma = pltpu.SemaphoreType.DMA
    outs = pl.pallas_call(
        functools.partial(ffn_kernel, units, expert_count),
        out_shape=(
            jax.ShapeDtypeStruct((depth, 2, 2, 2, quarter, width), bf16),
            jax.ShapeDtypeStruct((depth, 2, tile_rows, hidden), bf16),
            jax.ShapeDtypeStruct((depth, 2, tile_rows, 2 * hidden), bf16),
            jax.ShapeDtypeStruct((quarter, width), f32),
            jax.ShapeDtypeStruct((quarter, wide), f32),
        ),
        in_specs=[anywhere] * 5,
        out_specs=(anywhere,) * 3 + (in_vmem,) * 2,
        scratch_shapes=[
            pltpu.VMEM((2 * hidden, width), bf16),
            pltpu.VMEM((hidden, width), bf16),
            pltpu.VMEM((width, 128), bf16),
            pltpu.VMEM((2, 2, quarter, width), bf16),
            pltpu.VMEM((2, 2, quarter, wide), bf16),
            pltpu.VMEM((tile_rows, 2 * hidden), f32),
            pltpu.VMEM((tile_rows, hidden), f32),
            pltpu.VMEM((tile_rows, 128), f32),
            pltpu.VMEM((tile_rows, 128), bf16),
            pltpu.VMEM((tile_rows, hidden), bf16),
            pltpu.VMEM((tile_rows, 2 * hidden), bf16),
        ]
        + both(2, 2)
        + both(2)
        + both(2, 2, 2)
        + both(2)
        + both()
        + both(depth - 1)
        + [
            dma((3,)),
            dma,
            dma((depth - 1,)),
            dma((depth - 1,)),
            dma((depth, 8)),
            dma((depth, 8)),
            dma((2,)),
            dma((2,)),
            dma((2, 3)),
            dma((2, 3)),
            dma((2, depth - 1)),
            dma((2, depth - 1)),
            pltpu.SemaphoreType.REGULAR,
            pltpu.SemaphoreType.REGULAR((2,)),
            pltpu.SemaphoreType.REGULAR((2,)),
        ],
        compiler_params=pltpu.CompilerParams(
            collective_id=1, has_side_effects=True, vmem_limit_bytes=62 * 2**20
        ),
        cost_estimate=pl.CostEstimate(
            flops=12 * tokens * width * hidden,
            bytes_accessed=10 * tokens * width,
            transcendentals=tokens * hidden,
        ),
        name="ffn_all_tokens",
    )(rows, upstream_all.reshape(depth, 2, 2, 2, quarter, wide), pair_w, down_w, side_w)
    rows_all, weighted, d_pair, d_rows_sum, out_sum = outs
    return (
        rows_all.reshape(tokens, width),
        weighted.reshape(tokens, hidden),
        d_pair.reshape(tokens, 2 * hidden),
        d_rows_sum,
        out_sum,
    )


def over_tp(block, distance):
    devices = range(lax.axis_size("tp"))
    return lax.ppermute(block, "tp", [(i, i ^ distance) for i in devices])


def one_of(array, index, axis):
    return lax.dynamic_index_in_dim(array, index, axis, keepdims=False)


def sum_over_tp(part):
    rows, columns = part.shape
    tp = lax.axis_index("tp")
    x, c = tp // 2, tp % 2
    blocks = part.reshape(2, 2, rows // 4, columns)
    got = over_tp(one_of(blocks, 1 - c, 1).astype(jnp.bfloat16), 1)
    chip = one_of(blocks, c, 1).astype(jnp.float32) + got.astype(jnp.float32)
    got = over_tp(one_of(chip, 1 - x, 0).astype(jnp.bfloat16), 2)
    return one_of(chip, x, 0) + got.astype(jnp.float32)


def gather_over_tp(block):
    tp = lax.axis_index("tp")
    x, c = tp // 2, tp % 2
    got = over_tp(block, 2)
    pair = jnp.where(x == 0, jnp.stack([block, got]), jnp.stack([got, block]))
    got = over_tp(pair, 1)
    four = jnp.where(c == 0, jnp.stack([pair, got], axis=1), jnp.stack([got, pair], axis=1))
    return four.reshape(4 * block.shape[0], block.shape[1])


def swap_copies(at, pieces_in, pieces_out, send_sem, recv_sem, leave):
    count = 2 * at.depth
    copies = []
    for k in range(1, count):
        to, back = lax.rem(at.ep + k, count), lax.rem(at.ep + count - k, count)
        if leave:
            src, dst, peer = pieces_in.at[to], pieces_out.at[at.ep], to
        else:
            src, dst, peer = pieces_in.at[back], pieces_out.at[back], back
        copies.append(remote(src, dst, send_sem.at[k], recv_sem.at[k], (peer, at.tp)))
    return copies


def weights_kernel(
    own_in,
    pieces_in,
    all_out,
    pieces_out,
    own_sem,
    z_send,
    z_recv,
    y_send,
    y_recv,
    swap_send,
    swap_recv,
):
    at = Place()
    depth = at.depth
    half = own_in.shape[0] // 2
    last = depth - 1

    def block(k, y, h):
        return all_out.at[at.z + k, y, pl.ds(h * half, half)]

    def z_copy(k, h, direction):
        if k == 0:
            src = own_in.at[pl.ds(h * half, half)]
        else:
            src = block(k, at.y, h)
        slot = last + k - direction
        return remote(
            src,
            block(k, at.y, h),
            z_send.at[last + k, h, (direction + 1) // 2],
            z_recv.at[slot, h],
            at.at_z(at.z + direction),
        )

    def z_arrival(k, h):
        direction = 1 if k > 0 else -1
        dst = block(k, at.y, h)
        return remote(
            dst, dst, z_send.at[last + k, h, 0], z_recv.at[last + k, h], at.at_z(at.z + direction)
        )

    def y_copy(k, h):
        src = own_in.at[pl.ds(h * half, half)] if k == 0 else block(k, at.y, h)
        return remote(
            src, block(k, at.y, h), y_send.at[last + k, h], y_recv.at[last + k, h], at.next_y
        )

    own_copies = [
        pltpu.make_async_copy(own_in, all_out.at[at.z, at.y], own_sem.at[0]),
        pltpu.make_async_copy(pieces_in.at[at.ep], pieces_out.at[at.ep], own_sem.at[1]),
    ]
    for copy in own_copies:
        copy.start()
    has_up, has_down = at.z + 1 < depth, at.z > 0
    at.greet_ep()

    for h in (0, 1):
        pl.when(has_up)(lambda: z_copy(0, h, 1).start())
        pl.when(has_down)(lambda: z_copy(0, h, -1).start())
        y_copy(0, h).start()
    swap = (at, pieces_in, pieces_out, swap_send, swap_recv)
    for copy in swap_copies(*swap, True):
        copy.start()
    for k in range(1, depth):
        for h in (0, 1):
            for sign in (-1, 1):
                there = at.z + sign * k
                exists = (there >= 0) & (there < depth)
                onward = at.z - sign
                goes_on = exists & (onward >= 0) & (onward < depth)

                @pl.when(exists)
                def _():
                    z_arrival(sign * k, h).wait_recv()

                @pl.when(goes_on)
                def _():
                    z_copy(sign * k, h, -sign).start()

                @pl.when(exists)
                def _():
                    y_copy(sign * k, h).start()

    for copy in own_copies:
        copy.wait()
    for copy in swap_copies(*swap, False):
        copy.wait_recv()
    for copy in swap_copies(*swap, True):
        copy.wait_send()
    for h in (0, 1):
        pl.when(has_up)(lambda: z_copy(0, h, 1).wait_send())
        pl.when(has_down)(lambda: z_copy(0, h, -1).wait_send())
    for k in range(-last, depth):
        there = at.z + k
        exists = (there >= 0) & (there < depth)
        sign = 1 if k > 0 else -1
        onward = at.z - sign
        goes_on = exists & (onward >= 0) & (onward < depth)
        for h in (0, 1):

            @pl.when(exists)
            def _():
                y_copy(k, h).wait()

            if k != 0:

                @pl.when(goes_on)
                def _():
                    z_copy(k, h, -sign).wait_send()


def gather_over_ep(block, pieces):
    rows, columns = block.shape
    depth = lax.axis_size("ep") // 2
    anywhere = pl.BlockSpec(memory_space=pl.ANY)
    slots = 2 * depth - 1
    out, pieces = pl.pallas_call(
        weights_kernel,
        out_shape=(
            jax.ShapeDtypeStruct((depth, 2, rows, columns), block.dtype),
            jax.ShapeDtypeStruct(pieces.shape, pieces.dtype),
        ),
        in_specs=[anywhere] * 2,
        out_specs=(anywhere,) * 2,
        scratch_shapes=[
            pltpu.SemaphoreType.DMA((2,)),
            pltpu.SemaphoreType.DMA((slots, 2, 2)),
            pltpu.SemaphoreType.DMA((slots, 2)),
            pltpu.SemaphoreType.DMA((slots, 2)),
            pltpu.SemaphoreType.DMA((slots, 2)),
            pltpu.SemaphoreType.DMA((2 * depth,)),
            pltpu.SemaphoreType.DMA((2 * depth,)),
        ],
        compiler_params=pltpu.CompilerParams(collective_id=3, has_side_effects=True),
        cost_estimate=pl.CostEstimate(
            flops=0, bytes_accessed=8 * depth * rows * columns, transcendentals=0
        ),
        name="gather_weights",
    )(block, pieces)
    return out.reshape(2 * depth * rows, columns), pieces


def grads_kernel(
    routed,
    part_in,
    own_rows_in,
    rows_in,
    d_pair_in,
    upstream_in,
    weighted_in,
    out,
    rows_out,
    gate_out,
    up_out,
    down_out,
    own,
    hop,
    from_z,
    small,
    small_got,
    rows_tile,
    d_pair_tile,
    upstream_tile,
    weighted_tile,
    turned,
    gate_total,
    up_total,
    down_total,
    load_sem,
    y_send,
    y_recv,
    z_send,
    z_recv,
    rows_send,
    rows_recv,
    small_send,
    small_recv,
    own_sem,
    tile_sem,
    store_sem,
):
    at = Place()
    depth = at.depth
    rows, columns = out.shape
    half = rows // 2
    f32 = jnp.float32
    tiles = 2 * depth
    step = 16

    def part(h):
        return pl.ds(h * half, half)

    def load(j):
        return pltpu.make_async_copy(part_in.at[at.ahead(j), at.y], own.at[j], load_sem.at[j])

    def y_copy(j, h):
        return remote(
            part_in.at[at.ahead(j), 1 - at.y, part(h)],
            hop.at[j, part(h)],
            y_send.at[j, h],
            y_recv.at[j, h],
            at.next_y,
        )

    def z_copy(j, h):
        return remote(
            own.at[j, part(h)],
            from_z.at[j - 1, part(h)],
            z_send.at[j, h],
            z_recv.at[j, h],
            at.at_z(at.ahead(j)),
        )

    def rows_copy(kind):
        if kind == 0:
            src, dst, peer = own_rows_in, rows_out.at[at.x, at.c], at.next_x
        elif kind == 1:
            src, dst, peer = own_rows_in, rows_out.at[at.x, at.c], at.next_core
        else:
            src = dst = rows_out.at[1 - at.x, at.c]
            peer = at.next_core
        return remote(src, dst, rows_send.at[kind], rows_recv.at[kind], peer)

    def small_copy(kind):
        peer = at.next_core if kind == 0 else at.next_x
        return remote(
            small.at[kind], small_got.at[kind], small_send.at[kind], small_recv.at[kind], peer
        )

    def tile_loads(tile):
        slot = lax.rem(tile, 2)
        pairs = (
            (rows_in, rows_tile),
            (d_pair_in, d_pair_tile),
            (upstream_in, upstream_tile),
            (weighted_in, weighted_tile),
        )
        return [
            pltpu.make_async_copy(src.at[tile], dst.at[slot], tile_sem.at[i, slot])
            for i, (src, dst) in enumerate(pairs)
        ]

    order = [j for j in range(1, depth)] + [0]
    for copy in tile_loads(0):
        copy.start()
    for j in order:
        load(j).start()
    at.greet_row()
    for j in order:
        for h in (0, 1):
            y_copy(j, h).start()
    for kind in (0, 1):
        rows_copy(kind).start()
    own_copy = pltpu.make_async_copy(own_rows_in, rows_out.at[at.x, at.c], own_sem)
    own_copy.start()

    def after_y(j, moves_on):
        load(j).wait()
        for h in (0, 1):
            y_copy(j, h).wait_recv()

            def body(i, carry):
                some = pl.ds(pl.multiple_of(h * half + i * step, step), step)
                own[j, some] = own[j, some] + hop[j, some]
                return carry

            lax.fori_loop(0, half // step, body, 0)

            @pl.when(moves_on)
            def _():
                z_copy(j, h).start()

    width = gate_total.shape[1]
    hidden = weighted_tile.shape[2]
    some_columns = width // 4

    def tile_body(tile, carry):
        slot = lax.rem(tile, 2)
        for copy in tile_loads(tile):
            copy.wait()

        @pl.when(tile + 1 < tiles)
        def _():
            for copy in tile_loads(tile + 1):
                copy.start()

        for total, left, first, right in (
            (gate_total, d_pair_tile, 0, rows_tile),
            (up_total, d_pair_tile, hidden, rows_tile),
            (down_total, weighted_tile, 0, upstream_tile),
        ):
            turned[...] = left[slot, :, first : first + turned.shape[0]].T
            for n in range(4):
                these = slice(n * some_columns, (n + 1) * some_columns)
                product = jnp.dot(
                    turned[...], right[slot, :, these], preferred_element_type=f32
                )
                product = product[:routed]

                @pl.when(tile == 0)
                def _():
                    total[:, these] = product

                @pl.when(tile > 0)
                def _():
                    total[:, these] += product

        @pl.when(lax.rem(tile, 2) == 1)
        def _():
            after_y(lax.rem(tile // 2 + 1, depth), tile + 1 < tiles)

        @pl.when(tile == 1)
        def _():
            rows_copy(0).wait_recv()
            rows_copy(2).start()

        return carry

    lax.fori_loop(0, tiles, tile_body, 0)
    stores = [
        pltpu.make_async_copy(total, dst, store_sem.at[i])
        for i, (total, dst) in enumerate(
            ((gate_total, gate_out), (up_total, up_out), (down_total, down_out))
        )
    ]
    for copy in stores:
        copy.start()
    for h in (0, 1):
        for k in range(1, depth):
            z_copy(k, h).wait_recv()

        def body(i, carry):
            some = pl.ds(pl.multiple_of(h * half + i * step, step), step)
            total = own[0, some].astype(f32)
            for k in range(depth - 1):
                total = total + from_z[k, some].astype(f32)
            out[some] = total
            return carry

        lax.fori_loop(0, half // step, body, 0)
    small_columns = small.shape[2]
    for kind in (0, 1):
        small[kind] = out[:, columns - small_columns :]
        small_copy(kind).start()
        small_copy(kind).wait()
        out[:, columns - small_columns :] = small[kind] + small_got[kind]
    for j in range(depth):
        for h in (0, 1):
            y_copy(j, h).wait_send()
            if j > 0:
                z_copy(j, h).wait_send()
    own_copy.wait()
    rows_copy(0).wait_send()
    for kind in (1, 2):
        rows_copy(kind).wait()
    for copy in stores:
        copy.wait()


def scatter_over_ep(parts, own_rows, rows_all, d_pair, upstream_all, weighted, routed):
    depth = lax.axis_size("ep") // 2
    rows, columns = parts.shape[0] // (2 * depth), parts.shape[1]
    dtype = parts.dtype
    quarter, width = own_rows.shape
    tokens, hidden = weighted.shape
    tiles = 2 * depth
    tile = tokens // tiles
    f32 = jnp.float32
    anywhere = pl.BlockSpec(memory_space=pl.ANY)
    in_vmem = pl.BlockSpec(memory_space=pltpu.VMEM)
    dma = pltpu.SemaphoreType.DMA
    total = jax.ShapeDtypeStruct((routed, width), f32)
    left = -(-routed // 128) * 128
    wide = upstream_all.shape[1]
    out, gathered, gate, up, down = pl.pallas_call(
        functools.partial(grads_kernel, routed),
        out_shape=(
            jax.ShapeDtypeStruct((rows, columns), f32),
            jax.ShapeDtypeStruct((2, 2, quarter, width), dtype),
            total,
            total,
            total,
        ),
        in_specs=[anywhere] * 6,
        out_specs=(in_vmem, anywhere, anywhere, anywhere, anywhere),
        scratch_shapes=[
            pltpu.VMEM((depth, rows, columns), dtype),
            pltpu.VMEM((depth, rows, columns), dtype),
            pltpu.VMEM((depth - 1, rows, columns), dtype),
            pltpu.VMEM((2, rows, 128), f32),
            pltpu.VMEM((2, rows, 128), f32),
            pltpu.VMEM((2, tile, width), dtype),
            pltpu.VMEM((2, tile, 2 * hidden), dtype),
            pltpu.VMEM((2, tile, wide), dtype),
            pltpu.VMEM((2, tile, hidden), dtype),
            pltpu.VMEM((left, tile), dtype),
            pltpu.VMEM((routed, width), f32),
            pltpu.VMEM((routed, width), f32),
            pltpu.VMEM((routed, width), f32),
            dma((depth,)),
            dma((depth, 2)),
            dma((depth, 2)),
            dma((depth, 2)),
            dma((depth, 2)),
            dma((3,)),
            dma((3,)),
            dma((2,)),
            dma((2,)),
            dma,
            dma((4, 2)),
            dma((3,)),
        ],
        compiler_params=pltpu.CompilerParams(
            collective_id=4, has_side_effects=True, vmem_limit_bytes=62 * 2**20
        ),
        cost_estimate=pl.CostEstimate(
            flops=6 * tokens * width * left, bytes_accessed=10 * tokens * width, transcendentals=0
        ),
        name="scatter_grads",
    )(
        parts.reshape(depth, 2, rows, columns),
        own_rows,
        rows_all.reshape(tiles, tile, width),
        d_pair.reshape(tiles, tile, 2 * hidden),
        upstream_all.reshape(tiles, tile, wide),
        weighted.reshape(tiles, tile, hidden),
    )
    return out, gathered.reshape(4 * quarter, width), (gate, up, down)


def shared_pieces(weights, ep_count):
    rows, hidden = weights[0].shape
    units = hidden // ep_count
    return jnp.concatenate([weight.T.reshape(ep_count, units, rows) for weight in weights], axis=1)


def shared_units_of(pieces, count):
    ep_count, units, rows = pieces.shape
    return pieces.transpose(1, 0, 2).reshape(count, units // count, ep_count * rows)


def share_back(grads, ep_count):
    units, width = grads[0].shape
    columns = width // ep_count
    pieces = jnp.concatenate(grads, axis=0).reshape(len(grads) * units, ep_count, columns)
    moved = lax.all_to_all(
        pieces.transpose(1, 0, 2), "ep", split_axis=0, concat_axis=0, tiled=True
    )
    moved = moved.reshape(ep_count, len(grads), units, columns)
    return [moved[:, i].reshape(ep_count * units, columns).T for i in range(len(grads))]


def dense_body(
    tokens,
    lengths,
    routes,
    attn_gain,
    w_query,
    w_key,
    w_value,
    w_out,
    ffn_gain,
    w_router,
    shared_mix,
    shared_gate,
    shared_up,
    shared_down,
    expert_gate,
    expert_up,
    expert_down,
    cotangent,
):
    everywhere = ("ep", "tp")
    rows_here, width = tokens.shape
    ep_count = lax.axis_size("ep")
    tp_count = lax.axis_size("tp")
    ep_index = lax.axis_index("ep")
    offset = ep_index * rows_here
    quarter = rows_here // tp_count
    first_row = lax.axis_index("tp") * quarter
    slot_here, slot_hidden = expert_gate.shape[0], expert_gate.shape[1]
    expert_count = w_router.shape[1]
    bf16, f32 = jnp.bfloat16, jnp.float32

    def my_rows(array):
        return lax.dynamic_slice_in_dim(array, first_row, quarter, 0)

    side_columns = jnp.concatenate(
        [attn_gain[:, None], ffn_gain[:, None], shared_mix[:, None], w_router], axis=1
    )
    side_columns = jnp.pad(side_columns, ((0, 0), (0, -side_columns.shape[1] % 128)))
    joined_weights, pieces = gather_over_ep(
        jnp.concatenate([w_query, w_key, w_value, w_out, side_columns], axis=1),
        shared_pieces((shared_gate, shared_up, shared_down), ep_count),
    )
    cotangent_rows = my_rows(cotangent)
    joined_weights, cotangent_rows = lax.optimization_barrier((joined_weights, cotangent_rows))
    heads_width = w_query.shape[1]
    qkv_weight = joined_weights[:, : 3 * heads_width]
    output_weight = joined_weights[:, 3 * heads_width : 4 * heads_width]
    side_weight = joined_weights[:, 4 * heads_width :]
    picked = jnp.any(
        my_rows(routes)[:, :, None] == jnp.arange(expert_count, dtype=jnp.int32), axis=1
    )
    picked_lanes = jnp.pad(picked.astype(bf16), ((0, 0), (3, 125 - expert_count)))
    upstream_all = lax.all_gather(
        jnp.concatenate([cotangent_rows, picked_lanes], axis=1), everywhere, axis=0, tiled=True
    )
    shared_rows = shared_units_of(pieces, 3)
    shared_units = shared_rows.shape[1]
    routed_units = slot_here * slot_hidden
    gate_cat, up_cat, down_cat = [
        jnp.pad(
            jnp.concatenate([expert.reshape(-1, width), shared], axis=0),
            ((0, -(routed_units + shared_units) % 128), (0, 0)),
        )
        for expert, shared in zip((expert_gate, expert_up, expert_down), shared_rows)
    ]
    pair_cat = jnp.concatenate([gate_cat, up_cat], axis=0)
    hidden_total = gate_cat.shape[0]

    heads_here = heads_width // HD
    score_scale = HD ** (-0.5)
    first_norm_scale = side_weight[:, 0].astype(f32)
    second_norm_scale = side_weight[:, 1].astype(f32)
    mix_f = side_weight[:, 2].astype(f32)
    router_f = side_weight[:, 3 : 3 + expert_count].astype(f32)
    layer_input = tokens.astype(f32)
    normed_wide, norm_one = norm_forward(layer_input, first_norm_scale)
    normed_one = normed_wide.astype(bf16)
    query_at = offset + jnp.arange(rows_here, dtype=jnp.int32)
    key_at = offset - 2 * rows_here + jnp.arange(3 * rows_here, dtype=jnp.int32)
    query_seg, query_pos = sequence_info(lengths, query_at)
    key_seg, _ = sequence_info(lengths, key_at)
    cosine, sine = rope_tables(query_pos, HD)
    projected = jnp.dot(normed_one, qkv_weight, preferred_element_type=f32)
    projected = projected.reshape(rows_here, 3, heads_here, HD)
    queries = rotate(projected[:, 0], cosine, sine).astype(bf16)
    keys = rotate(projected[:, 1], cosine, sine).astype(bf16)
    values = projected[:, 2].astype(bf16)
    carried = jnp.stack([keys, values], axis=0)
    joined = jnp.concatenate(
        [passed_along(carried, "ep", 2), passed_along(carried, "ep", 1), carried], axis=1
    )
    keys_win = joined[0]
    values_win = joined[1]
    allowed = (
        (query_seg[:, None] == key_seg[None, :])
        & (key_at[None, :] <= query_at[:, None])
        & (key_at[None, :] >= 0)
    )
    scores = (
        jnp.einsum("qhd,khd->hqk", queries, keys_win, preferred_element_type=f32) * score_scale
    )
    masked = jnp.where(allowed[None], scores, -1e30)
    peak = jnp.max(masked, axis=-1, keepdims=True)
    expo = jnp.exp(masked - peak)
    total = jnp.sum(expo, axis=-1, keepdims=True)
    log_total = peak + jnp.log(total)
    weights = expo / total
    attended = jnp.einsum(
        "hqk,khd->qhd", weights.astype(bf16), values_win, preferred_element_type=f32
    )
    attended = attended.reshape(rows_here, heads_width).astype(bf16)
    attn_part = jnp.einsum("th,dh->td", attended, output_weight, preferred_element_type=f32)
    resid = my_rows(layer_input) + sum_over_tp(attn_part)
    normed_two_wide, norm_two = norm_forward(resid, second_norm_scale)
    normed_two = normed_two_wide.astype(bf16)

    logits = jnp.dot(normed_two, side_weight, preferred_element_type=f32)
    router = jax.nn.softmax(logits[:, 3 : 3 + expert_count], axis=-1)
    mixer = jax.nn.sigmoid(logits[:, 2])
    normed_all, weighted_h, d_pair_pre, d_normed_sum, out_sum = ffn_over_all(
        normed_two,
        upstream_all,
        pair_cat,
        down_cat,
        side_weight,
        (slot_here, slot_hidden, shared_units),
        expert_count,
    )
    ffn_sum = out_sum[:, :width]
    dots_sum = out_sum[:, width:]
    block_out = gather_over_tp((resid + ffn_sum).astype(bf16))
    d_router = jnp.where(picked, dots_sum[:, 3 : 3 + expert_count], 0.0)
    d_mixer = dots_sum[:, 2]
    d_logits = router * (d_router - jnp.sum(router * d_router, axis=-1, keepdims=True))
    d_mixlogit = d_mixer * mixer * (1.0 - mixer)
    side = jnp.dot(d_logits, router_f.T, precision=highest) + d_mixlogit[:, None] * mix_f[None, :]
    normed_two_f = normed_two.astype(f32)
    d_side = jnp.concatenate([d_mixlogit[:, None], d_logits], axis=1)
    grad_side = jnp.dot(normed_two_f.T, d_side, precision=highest)
    upstream = my_rows(cotangent).astype(f32)
    d_normed_two = d_normed_sum + side
    d_resid_norm, grad_gain_two = norm_backward(resid, norm_two, second_norm_scale, d_normed_two)
    d_resid = upstream + d_resid_norm
    d_resid_low = gather_over_tp(d_resid.astype(bf16))
    grad_out = jnp.einsum("td,th->dh", d_resid_low, attended, preferred_element_type=f32)
    grad_out = lax.psum_scatter(
        grad_out.astype(bf16), "ep", scatter_dimension=0, tiled=True
    ).astype(f32)
    d_attended = jnp.einsum("td,dh->th", d_resid_low, output_weight, preferred_element_type=f32)
    d_attended = d_attended.astype(bf16).reshape(rows_here, heads_here, HD)
    scores_again = (
        jnp.einsum("qhd,khd->hqk", queries, keys_win, preferred_element_type=f32) * score_scale
    )
    probs = jnp.where(allowed[None], jnp.exp(scores_again - log_total), 0.0)
    d_probs = jnp.einsum("qhd,khd->hqk", d_attended, values_win, preferred_element_type=f32)
    delta = jnp.sum(probs * d_probs, axis=-1, keepdims=True)
    delta, d_pair_late, weighted_late = lax.optimization_barrier((delta, d_pair_pre, weighted_h))
    d_scores = (probs * (d_probs - delta)).astype(bf16)
    shared_at = slice(routed_units, routed_units + shared_units)
    shared_up_at = slice(hidden_total + routed_units, hidden_total + routed_units + shared_units)
    shared_pair = jnp.concatenate([d_pair_late[:, shared_at], d_pair_late[:, shared_up_at]], axis=1)
    grad_shared_pair = jnp.einsum(
        "tf,td->fd", shared_pair, normed_all, preferred_element_type=f32
    ).astype(bf16)
    grad_shared_down = jnp.einsum(
        "tf,td->fd", weighted_late[:, shared_at], upstream_all[:, :width], preferred_element_type=f32
    ).astype(bf16)
    grad_shared = share_back(
        [grad_shared_pair[:shared_units], grad_shared_pair[shared_units:], grad_shared_down],
        ep_count,
    )
    grad_shared = [grad.astype(f32) for grad in grad_shared]

    d_keys_win = (
        jnp.einsum("hqk,qhd->khd", d_scores, queries, preferred_element_type=f32) * score_scale
    )
    d_values_win = jnp.einsum(
        "hqk,qhd->khd", probs.astype(bf16), d_attended, preferred_element_type=f32
    )
    pair_grads = jnp.stack([d_keys_win, d_values_win], axis=0)
    passed = pair_grads[:, : 2 * rows_here].astype(bf16)
    from_two = passed_along(passed[:, :rows_here], "ep", -2)
    from_one = passed_along(passed[:, rows_here:], "ep", -1)
    d_queries = (
        jnp.einsum("hqk,khd->qhd", d_scores, keys_win, preferred_element_type=f32) * score_scale
    )
    running = pair_grads[:, 2 * rows_here :] + from_one.astype(f32) + from_two.astype(f32)
    d_projected = jnp.concatenate(
        [
            unrotate(d_queries, cosine, sine).astype(bf16).reshape(rows_here, heads_width),
            unrotate(running[0], cosine, sine).astype(bf16).reshape(rows_here, heads_width),
            running[1].astype(bf16).reshape(rows_here, heads_width),
        ],
        axis=1,
    )
    d_normed_one = jnp.einsum("th,dh->td", d_projected, qkv_weight, preferred_element_type=f32)
    d_normed_one = sum_over_tp(d_normed_one)
    grad_qkv = jnp.einsum("td,th->dh", normed_one, d_projected, preferred_element_type=f32)
    d_input_norm, grad_gain_one = norm_backward(
        my_rows(layer_input), my_rows(norm_one), first_norm_scale, d_normed_one
    )
    small = jnp.concatenate([grad_gain_one[:, None], grad_gain_two[:, None], grad_side], axis=1)
    small = jnp.pad(small, ((0, 0), (0, 128 - small.shape[1])))
    grad_weights, grad_tokens, grad_experts = scatter_over_ep(
        jnp.concatenate([grad_qkv, small], axis=1).astype(bf16),
        (d_resid + d_input_norm).astype(bf16),
        normed_all,
        d_pair_pre,
        upstream_all,
        weighted_h,
        routed_units,
    )
    grad_tokens = grad_tokens.astype(f32)
    grad_experts = [grad.reshape(expert_gate.shape) for grad in grad_experts]
    small = grad_weights[:, 3 * heads_width :]
    parts = [grad_weights[:, i * heads_width : (i + 1) * heads_width] for i in range(3)]
    return (
        block_out,
        grad_tokens,
        small[:, 0],
        parts[0],
        parts[1],
        parts[2],
        grad_out,
        small[:, 1],
        small[:, 3 : 3 + expert_count],
        small[:, 2],
        grad_shared[0],
        grad_shared[1],
        grad_shared[2],
        grad_experts[0],
        grad_experts[1],
        grad_experts[2],
    )


def chosen_body(*arrays):
    rows_here, top_count = arrays[2].shape
    slot_here, expert_count = arrays[14].shape[0], arrays[9].shape[1]
    capacity = rows_here * top_count * 7 // (5 * expert_count)
    grid_of_two = lax.axis_size("ep") % 2 == 0 and lax.axis_size("tp") == 4
    if grid_of_two and rows_here < 2 * slot_here * capacity:
        return dense_body(*arrays)
    return body(*arrays)


def solution(mesh):
    placed = (
        P("ep", None),
        P(),
        P("ep", None),
        P("ep"),
        P("ep", "tp"),
        P("ep", "tp"),
        P("ep", "tp"),
        P("ep", "tp"),
        P("ep"),
        P("ep", None),
        P("ep"),
        P("ep", "tp"),
        P("ep", "tp"),
        P("ep", "tp"),
        P("ep", "tp", None),
        P("ep", "tp", None),
        P("ep", "tp", None),
        P("ep", None),
    )
    return jax.shard_map(
        chosen_body,
        mesh=mesh,
        in_specs=placed,
        out_specs=(
            P("ep", None),
            P("ep", None),
            P("ep"),
            P("ep", "tp"),
            P("ep", "tp"),
            P("ep", "tp"),
            P("ep", "tp"),
            P("ep"),
            P("ep", None),
            P("ep"),
            P("ep", "tp"),
            P("ep", "tp"),
            P("ep", "tp"),
            P("ep", "tp", None),
            P("ep", "tp", None),
            P("ep", "tp", None),
        ),
        check_vma=False,
    )
```

```python
import functools

import jax
import jax.numpy as jnp
from jax import lax
from jax.experimental import pallas as pl
from jax.experimental.pallas import tpu as pltpu
from jax.sharding import PartitionSpec as P

HD = 128


epsilon = 1e-06
rope_base = 1000000.0
highest = lax.Precision.HIGHEST
MESH = pl.DeviceIdType.MESH


def passed_along(block, axis, distance):
    devices = range(lax.axis_size(axis))
    route = [(i - distance, i) for i in devices if i - distance in devices]
    return lax.ppermute(block, axis, route)


def rope_tables(positions, width):
    steps = jnp.arange(0, width, 2, dtype=jnp.float32) / width
    inverse = rope_base ** (-steps)
    angles = positions.astype(jnp.float32)[:, None] * inverse[None, :]
    angles = jnp.concatenate([angles, angles], axis=-1)
    return (jnp.cos(angles)[:, None, :], jnp.sin(angles)[:, None, :])


def turn_half(values):
    middle = values.shape[-1] // 2
    return jnp.concatenate([-values[..., middle:], values[..., :middle]], axis=-1)


def rotate(values, cosine, sine):
    return values * cosine + turn_half(values) * sine


def unrotate(grads, cosine, sine):
    return grads * cosine - turn_half(grads * sine)


def sequence_info(lengths, indices):
    starts = jnp.cumsum(lengths) - lengths
    inside = starts[None, :] <= indices[:, None]
    segment = jnp.sum(inside.astype(jnp.int32), axis=1) - 1
    first = jnp.max(jnp.where(inside, starts[None, :], -1), axis=1)
    return (segment, indices - first)


def norm_forward(values, gain):
    scale = lax.rsqrt(jnp.mean(values * values, axis=-1, keepdims=True) + epsilon)
    return (values * scale * gain, scale)


def norm_backward(values, scale, gain, grads):
    unit = values * scale
    scaled = grads * gain
    inner = jnp.mean(scaled * unit, axis=-1, keepdims=True)
    return (scale * (scaled - unit * inner), jnp.sum(grads * unit, axis=0))


def deliver(rows):
    arrived_rows = lax.all_to_all(rows, "ep", split_axis=0, concat_axis=0, tiled=True)
    return arrived_rows


def bring_back(parts, target, rows_here, top_count):
    moved = lax.all_to_all(parts, "ep", split_axis=0, concat_axis=0, tiled=True)
    piece = moved.shape[3]
    return moved.reshape(-1, piece)[target].reshape(rows_here, top_count, piece)


def body(
    tokens,
    lengths,
    routes,
    attn_gain,
    w_query,
    w_key,
    w_value,
    w_out,
    ffn_gain,
    w_router,
    shared_mix,
    shared_gate,
    shared_up,
    shared_down,
    expert_gate,
    expert_up,
    expert_down,
    cotangent,
):
    rows_here = tokens.shape[0]
    width = tokens.shape[1]
    ep_count = lax.axis_size("ep")
    offset = lax.axis_index("ep") * rows_here
    slot_here = expert_gate.shape[0]
    top_count = routes.shape[1]
    gathered = (
        lax.all_gather(attn_gain, "ep", axis=0, tiled=True),
        lax.all_gather(w_query, "ep", axis=0, tiled=True),
        lax.all_gather(w_key, "ep", axis=0, tiled=True),
        lax.all_gather(w_value, "ep", axis=0, tiled=True),
        lax.all_gather(w_out, "ep", axis=0, tiled=True),
        lax.all_gather(ffn_gain, "ep", axis=0, tiled=True),
        lax.all_gather(w_router, "ep", axis=0, tiled=True),
        lax.all_gather(shared_mix, "ep", axis=0, tiled=True),
        lax.all_gather(shared_gate, "ep", axis=0, tiled=True),
        lax.all_gather(shared_up, "ep", axis=0, tiled=True),
        lax.all_gather(shared_down, "ep", axis=0, tiled=True),
    )
    (
        gain_first,
        query_weight_matrix,
        key_weight_matrix,
        value_weight_matrix,
        output_weight,
        gain_second,
        router_weight,
        shared_mixer_weight,
        shared_gate_weight,
        shared_up_weight,
        shared_down_weight,
    ) = gathered
    expert_count = router_weight.shape[1]
    capacity = (rows_here * top_count * 7 // (5 * expert_count) + 7) // 8 * 8
    heads_here = query_weight_matrix.shape[1] // HD
    score_scale = HD ** (-0.5)
    first_norm_scale = gain_first.astype(jnp.float32)
    second_norm_scale = gain_second.astype(jnp.float32)
    layer_input = tokens.astype(jnp.float32)
    normed_wide, norm_one = norm_forward(layer_input, first_norm_scale)
    normed_one = normed_wide.astype(jnp.bfloat16)
    query_at = offset + jnp.arange(rows_here, dtype=jnp.int32)
    key_at = offset - 2 * rows_here + jnp.arange(3 * rows_here, dtype=jnp.int32)
    query_seg, query_pos = sequence_info(lengths, query_at)
    key_seg, _ = sequence_info(lengths, key_at)
    cosine, sine = rope_tables(query_pos, HD)
    query_pre = jnp.dot(
        normed_one, query_weight_matrix, preferred_element_type=jnp.float32
    ).reshape(rows_here, heads_here, HD)
    key_pre = jnp.dot(normed_one, key_weight_matrix, preferred_element_type=jnp.float32).reshape(
        rows_here, heads_here, HD
    )
    queries = rotate(query_pre, cosine, sine).astype(jnp.bfloat16)
    keys = rotate(key_pre, cosine, sine).astype(jnp.bfloat16)
    values = (
        jnp.dot(normed_one, value_weight_matrix, preferred_element_type=jnp.float32)
        .astype(jnp.bfloat16)
        .reshape(rows_here, heads_here, HD)
    )
    carried = jnp.stack([keys, values], axis=0)
    window = [carried]
    for hop in range(2):
        carried = passed_along(carried, "ep", 1)
        window = [carried] + window
    joined = jnp.concatenate(window, axis=1)
    keys_win = joined[0]
    values_win = joined[1]
    allowed = (
        (query_seg[:, None] == key_seg[None, :])
        & (key_at[None, :] <= query_at[:, None])
        & (key_at[None, :] >= 0)
    )
    scores = (
        jnp.einsum("qhd,khd->hqk", queries, keys_win, preferred_element_type=jnp.float32)
        * score_scale
    )
    masked = jnp.where(allowed[None], scores, -1e30)
    peak = jnp.max(masked, axis=-1, keepdims=True)
    expo = jnp.exp(masked - peak)
    total = jnp.sum(expo, axis=-1, keepdims=True)
    log_total = peak + jnp.log(total)
    weights = expo / total
    attended = jnp.einsum(
        "hqk,khd->qhd", weights.astype(jnp.bfloat16), values_win, preferred_element_type=jnp.float32
    )
    attended = attended.reshape(rows_here, heads_here * HD).astype(jnp.bfloat16)
    attn_part = jnp.einsum("th,dh->td", attended, output_weight, preferred_element_type=jnp.float32)
    resid = layer_input + lax.psum(attn_part, "tp")
    normed_two_wide, norm_two = norm_forward(resid, second_norm_scale)
    normed_two = normed_two_wide.astype(jnp.bfloat16)
    normed_two_f = normed_two.astype(jnp.float32)
    router_f = router_weight.astype(jnp.float32)
    mix_f = shared_mixer_weight.astype(jnp.float32)
    router = jax.nn.softmax(jnp.dot(normed_two_f, router_f, precision=highest), axis=-1)
    picked = routes[:, :, None] == jnp.arange(expert_count, dtype=jnp.int32)[None, None, :]
    gates = jnp.sum(jnp.where(picked, router[:, None, :], 0.0), axis=-1)
    mixer = jax.nn.sigmoid(jnp.dot(normed_two_f, mix_f, precision=highest))
    shared_g = jnp.dot(normed_two, shared_gate_weight, preferred_element_type=jnp.float32)
    shared_u = jnp.dot(normed_two, shared_up_weight, preferred_element_type=jnp.float32)
    shared_h = (jax.nn.silu(shared_g) * shared_u).astype(jnp.bfloat16)
    shared_part = jnp.einsum(
        "tf,df->td", shared_h, shared_down_weight, preferred_element_type=jnp.float32
    )
    flat = routes.reshape(-1)
    hot = (flat[:, None] == jnp.arange(expert_count, dtype=jnp.int32)[None, :]).astype(jnp.int32)
    rank = jnp.sum(jnp.cumsum(hot, axis=0) * hot, axis=1) - 1
    target = flat * capacity + rank
    slot_total = ep_count * slot_here * capacity
    owner_route = (
        jnp.zeros((slot_total,), jnp.int32)
        .at[target]
        .set(jnp.arange(rows_here * top_count, dtype=jnp.int32))
    )
    filled = jnp.zeros((slot_total,), jnp.bool_).at[target].set(True)
    owner_token = owner_route // top_count
    send_rows = jnp.where(filled[:, None], normed_two[owner_token], jnp.zeros((), jnp.bfloat16))
    arrived_rows = deliver(send_rows.reshape(ep_count, slot_here, capacity, width))
    route_g = jnp.einsum(
        "nscd,sfd->nscf", arrived_rows, expert_gate, preferred_element_type=jnp.float32
    )
    route_u = jnp.einsum(
        "nscd,sfd->nscf", arrived_rows, expert_up, preferred_element_type=jnp.float32
    )
    route_h = (jax.nn.silu(route_g) * route_u).astype(jnp.bfloat16)
    route_part = jnp.einsum(
        "nscf,sfd->nscd", route_h, expert_down, preferred_element_type=jnp.float32
    )
    back_rows = bring_back(route_part, target, rows_here, top_count)
    upstream = cotangent.astype(jnp.float32)
    routed = jnp.sum(back_rows * gates[:, :, None], axis=1)
    ffn_part = mixer[:, None] * shared_part + routed
    route_dot = jnp.sum(back_rows * upstream[:, None, :], axis=-1)
    shared_dot = jnp.sum(shared_part * upstream, axis=-1)
    ffn_total, d_gate, d_mixer = lax.psum((ffn_part, route_dot, shared_dot), "tp")
    block_out = (resid + ffn_total).astype(jnp.bfloat16)
    d_router = jnp.sum(jnp.where(picked, d_gate[:, :, None], 0.0), axis=1)
    d_logits = router * (d_router - jnp.sum(router * d_router, axis=-1, keepdims=True))
    d_mixlogit = d_mixer * mixer * (1.0 - mixer)
    side = jnp.dot(d_logits, router_f.T, precision=highest) + d_mixlogit[:, None] * mix_f[None, :]
    grad_router = jnp.dot(normed_two_f.T, d_logits, precision=highest)
    grad_mix = jnp.dot(d_mixlogit, normed_two_f, precision=highest)
    d_shared = (mixer[:, None] * upstream).astype(jnp.bfloat16)
    d_sh = jnp.dot(d_shared, shared_down_weight, preferred_element_type=jnp.float32)
    sig_shared = jax.nn.sigmoid(shared_g)
    d_sg = (d_sh * shared_u * sig_shared * (1.0 + shared_g * (1.0 - sig_shared))).astype(
        jnp.bfloat16
    )
    d_su = (d_sh * shared_g * sig_shared).astype(jnp.bfloat16)
    d_normed_part = jnp.einsum(
        "tf,df->td", d_sg, shared_gate_weight, preferred_element_type=jnp.float32
    )
    d_normed_part = d_normed_part + jnp.einsum(
        "tf,df->td", d_su, shared_up_weight, preferred_element_type=jnp.float32
    )
    grad_sgate = jnp.einsum("td,tf->df", normed_two, d_sg, preferred_element_type=jnp.float32)
    grad_sup = jnp.einsum("td,tf->df", normed_two, d_su, preferred_element_type=jnp.float32)
    grad_sdown = jnp.einsum("td,tf->df", d_shared, shared_h, preferred_element_type=jnp.float32)
    d_route = (
        (gates[:, :, None] * upstream[:, None, :])
        .astype(jnp.bfloat16)
        .reshape(rows_here * top_count, width)
    )
    send_grads = jnp.where(filled[:, None], d_route[owner_route], jnp.zeros((), jnp.bfloat16))
    received_grads = deliver(send_grads.reshape(ep_count, slot_here, capacity, width))
    d_rh = jnp.einsum(
        "nscd,sfd->nscf", received_grads, expert_down, preferred_element_type=jnp.float32
    )
    sig_route = jax.nn.sigmoid(route_g)
    d_rg = (d_rh * route_u * sig_route * (1.0 + route_g * (1.0 - sig_route))).astype(jnp.bfloat16)
    routed_up_gradient = (d_rh * route_g * sig_route).astype(jnp.bfloat16)
    row_grads = jnp.einsum("nscf,sfd->nscd", d_rg, expert_gate, preferred_element_type=jnp.float32)
    row_grads = row_grads + jnp.einsum(
        "nscf,sfd->nscd", routed_up_gradient, expert_up, preferred_element_type=jnp.float32
    )
    grad_egate = jnp.einsum(
        "qxba,qxbr->xar", d_rg, arrived_rows, preferred_element_type=jnp.float32
    )
    expert_up_gradient = jnp.einsum(
        "qxba,qxbr->xar", routed_up_gradient, arrived_rows, preferred_element_type=jnp.float32
    )
    grad_edown = jnp.einsum(
        "qxba,qxbr->xar", route_h, received_grads, preferred_element_type=jnp.float32
    )
    grads_back = bring_back(row_grads, target, rows_here, top_count)
    d_routed = jnp.sum(grads_back, axis=1)
    d_normed_two = lax.psum(d_normed_part + d_routed, "tp") + side
    d_resid_norm, grad_gain_two = norm_backward(resid, norm_two, second_norm_scale, d_normed_two)
    d_resid = upstream + d_resid_norm
    d_resid_low = d_resid.astype(jnp.bfloat16)
    grad_outw = jnp.einsum("td,th->dh", d_resid_low, attended, preferred_element_type=jnp.float32)
    d_attended = jnp.einsum(
        "td,dh->th", d_resid_low, output_weight, preferred_element_type=jnp.float32
    )
    d_attended = d_attended.astype(jnp.bfloat16).reshape(rows_here, heads_here, HD)
    scores_again = (
        jnp.einsum("qhd,khd->hqk", queries, keys_win, preferred_element_type=jnp.float32)
        * score_scale
    )
    probs = jnp.where(allowed[None], jnp.exp(scores_again - log_total), 0.0)
    d_probs = jnp.einsum("qhd,khd->hqk", d_attended, values_win, preferred_element_type=jnp.float32)
    delta = jnp.sum(probs * d_probs, axis=-1, keepdims=True)
    d_scores = (probs * (d_probs - delta)).astype(jnp.bfloat16)
    d_queries = (
        jnp.einsum("hqk,khd->qhd", d_scores, keys_win, preferred_element_type=jnp.float32)
        * score_scale
    )
    d_keys_win = (
        jnp.einsum("hqk,qhd->khd", d_scores, queries, preferred_element_type=jnp.float32)
        * score_scale
    )
    d_values_win = jnp.einsum(
        "hqk,qhd->khd", probs.astype(jnp.bfloat16), d_attended, preferred_element_type=jnp.float32
    )
    pair_grads = jnp.stack([d_keys_win, d_values_win], axis=0)
    older = pair_grads[:, :rows_here]
    later = [pair_grads[:, rows_here : 2 * rows_here], pair_grads[:, 2 * rows_here :]]
    running = older
    for hop in range(2):
        running = passed_along(running, "ep", -1)
        running = running + later[hop]
    d_query_pre = (
        unrotate(d_queries, cosine, sine).astype(jnp.bfloat16).reshape(rows_here, heads_here * HD)
    )
    d_key_pre = (
        unrotate(running[0], cosine, sine).astype(jnp.bfloat16).reshape(rows_here, heads_here * HD)
    )
    d_values = running[1].astype(jnp.bfloat16).reshape(rows_here, heads_here * HD)
    grad_queryw = jnp.einsum(
        "td,th->dh", normed_one, d_query_pre, preferred_element_type=jnp.float32
    )
    grad_keyw = jnp.einsum("td,th->dh", normed_one, d_key_pre, preferred_element_type=jnp.float32)
    grad_valuew = jnp.einsum("td,th->dh", normed_one, d_values, preferred_element_type=jnp.float32)
    d_normed_one = jnp.einsum(
        "th,dh->td", d_query_pre, query_weight_matrix, preferred_element_type=jnp.float32
    )
    d_normed_one = d_normed_one + jnp.einsum(
        "th,dh->td", d_key_pre, key_weight_matrix, preferred_element_type=jnp.float32
    )
    d_normed_one = d_normed_one + jnp.einsum(
        "th,dh->td", d_values, value_weight_matrix, preferred_element_type=jnp.float32
    )
    d_normed_one = lax.psum(d_normed_one, "tp")
    d_input_norm, grad_gain_one = norm_backward(
        layer_input, norm_one, first_norm_scale, d_normed_one
    )
    grad_tokens = d_resid + d_input_norm
    summed = (
        lax.psum_scatter(grad_gain_one, "ep", scatter_dimension=0, tiled=True),
        lax.psum_scatter(grad_queryw, "ep", scatter_dimension=0, tiled=True),
        lax.psum_scatter(grad_keyw, "ep", scatter_dimension=0, tiled=True),
        lax.psum_scatter(grad_valuew, "ep", scatter_dimension=0, tiled=True),
        lax.psum_scatter(grad_outw, "ep", scatter_dimension=0, tiled=True),
        lax.psum_scatter(grad_gain_two, "ep", scatter_dimension=0, tiled=True),
        lax.psum_scatter(grad_router, "ep", scatter_dimension=0, tiled=True),
        lax.psum_scatter(grad_mix, "ep", scatter_dimension=0, tiled=True),
        lax.psum_scatter(grad_sgate, "ep", scatter_dimension=0, tiled=True),
        lax.psum_scatter(grad_sup, "ep", scatter_dimension=0, tiled=True),
        lax.psum_scatter(grad_sdown, "ep", scatter_dimension=0, tiled=True),
    )
    return (
        block_out,
        grad_tokens,
        summed[0],
        summed[1],
        summed[2],
        summed[3],
        summed[4],
        summed[5],
        summed[6],
        summed[7],
        summed[8],
        summed[9],
        summed[10],
        grad_egate,
        expert_up_gradient,
        grad_edown,
    )


class Place:
    def __init__(self):
        self.ep, self.tp = lax.axis_index("ep"), lax.axis_index("tp")
        self.z, self.y = self.ep // 2, self.ep % 2
        self.x, self.c = self.tp // 2, self.tp % 2
        self.depth = lax.axis_size("ep") // 2
        self.next_core = (self.ep, self.x * 2 + 1 - self.c)
        self.next_x = (self.ep, (1 - self.x) * 2 + self.c)
        self.next_y = (self.z * 2 + 1 - self.y, self.tp)

    def at_z(self, z):
        return (z * 2 + self.y, self.tp)

    def ahead(self, steps):
        return lax.rem(self.z + steps, self.depth)

    def behind(self, steps):
        return lax.rem(self.z + self.depth - steps, self.depth)

    def greet(self):
        barrier = pltpu.get_barrier_semaphore()
        peers = [self.next_core, self.next_x, self.next_y]
        peers += [self.at_z(self.ahead(k)) for k in range(1, self.depth)]
        for peer in peers:
            pl.semaphore_signal(barrier, inc=1, device_id=peer, device_id_type=MESH)
        pl.semaphore_wait(barrier, len(peers))

    def greet_row(self):
        barrier = pltpu.get_barrier_semaphore()
        count = 2 * self.depth
        peers = [(lax.rem(self.ep + k, count), self.tp) for k in range(1, count)]
        peers += [self.next_core, self.next_x]
        for peer in peers:
            pl.semaphore_signal(barrier, inc=1, device_id=peer, device_id_type=MESH)
        pl.semaphore_wait(barrier, len(peers))

    def greet_ep(self):
        barrier = pltpu.get_barrier_semaphore()
        count = 2 * self.depth
        for k in range(1, count):
            peer = (lax.rem(self.ep + k, count), self.tp)
            pl.semaphore_signal(barrier, inc=1, device_id=peer, device_id_type=MESH)
        pl.semaphore_wait(barrier, count - 1)


def remote(src, dst, send, recv, peer):
    return pltpu.make_async_remote_copy(
        src_ref=src, dst_ref=dst, send_sem=send, recv_sem=recv, device_id=peer, device_id_type=MESH
    )


def ffn_kernel(
    units,
    expert_count,
    rows_in,
    upstream_in,
    pair_in,
    down_in,
    side_in,
    resid_in,
    gain_in,
    rows_all,
    weighted_out,
    d_pair_out,
    block_out,
    d_resid_low_out,
    d_resid_out,
    d_gain_out,
    d_side_out,
    d_rows_sum,
    out_sum,
    pair_w,
    down_w,
    side_w,
    rows_tile,
    upstream_tile,
    pair_pre,
    d_hidden,
    factors,
    dots,
    weighted_tile,
    d_pair_tile,
    own_rows,
    own_upstream,
    block_low,
    d_resid_low,
    d_rows_tile,
    out_tile,
    d_rows_core,
    out_core,
    d_rows_held,
    out_held,
    d_rows_hop,
    out_hop,
    d_rows_hop2,
    out_hop2,
    d_rows_z,
    out_z,
    d_rows_to_z,
    out_to_z,
    gathered_send,
    gathered_recv,
    weight_sem,
    own_sem,
    z_send,
    z_recv,
    plane_send,
    plane_recv,
    load_sem,
    store_sem,
    sum_send,
    sum_recv,
    end_send,
    end_recv,
    core_credit,
    hop_credit,
    hop2_credit,
):
    at = Place()
    depth = at.depth
    quarter, width = rows_in.shape
    half = quarter // 2
    f32, bf16 = jnp.float32, jnp.bfloat16

    def weight_copies():
        pairs = (
            (pair_in, pair_w),
            (down_in, down_w),
            (side_in, side_w),
            (rows_in, own_rows),
            (upstream_in.at[at.z, at.y, at.x, at.c], own_upstream),
        )
        return [
            pltpu.make_async_copy(src, dst, weight_sem.at[i]) for i, (src, dst) in enumerate(pairs)
        ]

    for copy in weight_copies():
        copy.start()

    def block(j, y, x):
        return rows_all.at[at.behind(j), y, x, at.c]

    def plane_copy(j, kind):
        y, other_y = at.y, 1 - at.y
        own, other_x = at.x, 1 - at.x
        if kind == 0:
            src, peer = block(j, y, own), at.next_x
        elif kind == 1:
            src, peer = block(j, y, own), at.next_y
        elif kind == 2:
            src, peer = block(j, y, other_x).at[pl.ds(0, half)], at.next_y
        elif kind == 3:
            src, peer = block(j, other_y, own).at[pl.ds(half, half)], at.next_x
        else:
            src = block(j, other_y if kind >= 6 else y, other_x if kind % 2 else own)
            peer = at.next_core
        return remote(src, src, plane_send.at[j, kind], plane_recv.at[j, kind], peer)

    def z_copy(k):
        return remote(
            rows_in, block(0, at.y, at.x), z_send.at[k - 1], z_recv.at[k - 1], at.at_z(at.ahead(k))
        )

    def z_arrival(k):
        dst = block(k, at.y, at.x)
        return remote(dst, dst, z_send.at[k - 1], z_recv.at[k - 1], at.at_z(at.behind(k)))

    def begin(j):
        for kind in (0, 1, 4):
            plane_copy(j, kind).start()

    def spread(j):
        plane_copy(j, 0).wait_recv()
        plane_copy(j, 2).start()
        plane_copy(j, 5).start()
        plane_copy(j, 1).wait_recv()
        plane_copy(j, 3).start()
        plane_copy(j, 6).start()

    def begin_later(j):
        z_arrival(j).wait_recv()
        begin(j)

    def last_hop(j):
        plane_copy(j, 2).wait_recv()
        plane_copy(j, 3).wait_recv()
        plane_copy(j, 7).start()

    def near_ready(j):
        plane_copy(j, 4).wait_recv()
        plane_copy(j, 5).wait_recv()

    def far_ready(j):
        plane_copy(j, 6).wait_recv()
        plane_copy(j, 7).wait_recv()

    def parity(step):
        return lax.rem(step, 2)

    def slot_of(turn):
        return lax.rem(turn + 1, depth)

    def tile_at(step):
        return at.behind(slot_of(step // 2)), lax.rem(at.y + parity(step), 2)

    def load_rows(step):
        z, y = tile_at(step)
        return pltpu.make_async_copy(rows_all.at[z, y], rows_tile, load_sem.at[0])

    def load_upstream(step):
        z, y = tile_at(step)
        return pltpu.make_async_copy(upstream_in.at[z, y], upstream_tile, load_sem.at[1])

    def stores(step):
        z, y = tile_at(step)
        pairs = ((weighted_tile, weighted_out), (d_pair_tile, d_pair_out))
        return [
            pltpu.make_async_copy(src, dst.at[z, y], store_sem.at[i])
            for i, (src, dst) in enumerate(pairs)
        ]

    tiles, cores = (d_rows_tile, out_tile), (d_rows_core, out_core)
    helds, sums = (d_rows_held, out_held), (d_rows_sum, out_sum)
    hops, hops2, zs = (d_rows_hop, out_hop), (d_rows_hop2, out_hop2), (d_rows_z, out_z)
    to_zs = (d_rows_to_z, out_to_z)

    def sum_copy(a, kind, src, dst, peer):
        return remote(src, dst, sum_send.at[a, kind], sum_recv.at[a, kind], peer)

    def core_sum(a):
        return sum_copy(a, 0, tiles[a].at[:, 1 - at.c], cores[a], at.next_core)

    def hop_sum(a, turn):
        slot = parity(turn)
        src = helds[0].at[slot, :, 1 - at.x] if a == 0 else helds[1].at[slot, 1 - at.y]
        return sum_copy(a, 1, src, hops[a], at.next_x if a == 0 else at.next_y)

    def hop2_sum(a, turn):
        slot = parity(turn)
        if a == 0:
            src, peer = helds[0].at[slot, 1 - at.y, at.x], at.next_y
        else:
            src, peer = helds[1].at[slot, at.y, 1 - at.x], at.next_x
        return sum_copy(a, 2, src, hops2[a], peer)

    def z_sum(a, turn):
        return remote(
            to_zs[a].at[turn],
            zs[a].at[turn],
            end_send.at[a, turn],
            end_recv.at[a, turn],
            at.at_z(at.behind(turn + 1)),
        )

    def allow(semaphore, peer):
        pl.semaphore_signal(semaphore, inc=1, device_id=peer, device_id_type=MESH)

    piece = 32

    def add(into, first, second):
        def body(i, carry):
            part = pl.ds(pl.multiple_of(i * piece, piece), piece)
            into[part] = first[part] + second[part]
            return carry

        lax.fori_loop(0, quarter // piece, body, 0)

    def after_core(step):
        turn = step // 2
        held, y = parity(turn), lax.rem(at.y + parity(step), 2)

        for a in (0, 1):
            core_sum(a).wait()
            for x in (0, 1):
                add(helds[a].at[held, y, x], tiles[a].at[x, at.c], cores[a].at[x])

        @pl.when(step + 1 < 2 * depth)
        def _():
            allow(core_credit, at.next_core)

        @pl.when(parity(step) == 1)
        def _():
            @pl.when(turn >= 1)
            def _():
                for a in (0, 1):
                    pl.semaphore_wait(hop_credit.at[a], 1)

            for a in (0, 1):
                hop_sum(a, turn).start()

    def after_hop(turn):
        slot = parity(turn)

        @pl.when(turn >= 1)
        def _():
            for a in (0, 1):
                pl.semaphore_wait(hop2_credit.at[a], 1)

        for a in (0, 1):
            hop_sum(a, turn).wait()
            for moved in (1, 0):
                if a == 0:
                    y = lax.rem(at.y + moved, 2)
                    into, other = helds[0].at[slot, y, at.x], hops[0].at[y]
                else:
                    x = lax.rem(at.x + moved, 2)
                    into, other = helds[1].at[slot, at.y, x], hops[1].at[x]
                add(into, into, other)
                if moved:
                    hop2_sum(a, turn).start()

        @pl.when(turn + 1 < depth)
        def _():
            allow(hop_credit.at[0], at.next_x)
            allow(hop_credit.at[1], at.next_y)

    def after_hop2(turn):
        slot = parity(turn)
        for a in (0, 1):
            hop2_sum(a, turn).wait()
            held = helds[a].at[slot, at.y, at.x]

            @pl.when(turn + 1 < depth)
            def _():
                add(to_zs[a].at[turn], held, hops2[a])
                z_sum(a, turn).start()

            @pl.when(turn + 1 == depth)
            def _():
                add(held, held, hops2[a])

        @pl.when(turn + 1 < depth)
        def _():
            allow(hop2_credit.at[0], at.next_y)
            allow(hop2_credit.at[1], at.next_x)

    load_upstream(0).start()
    at.greet()
    z_copy(1).start()
    own_copy = pltpu.make_async_copy(rows_in, block(0, at.y, at.x), own_sem)
    own_copy.start()
    own_copy.wait()
    begin(0)
    begin_later(1)
    for k in range(2, depth):
        z_copy(k).start()
    spread(0)
    spread(1)
    near_ready(1)
    load_rows(0).start()
    for copy in weight_copies():
        copy.wait()

    tile_rows = 4 * quarter
    hidden_total = down_w.shape[0]
    lane = lax.broadcasted_iota(jnp.int32, (tile_rows, 128), 1)
    slot_here, slot_hidden, shared_hidden = units
    routed = slot_here * slot_hidden
    across = (((1,), (1,)), ((), ()))
    few = 16

    def gate_factors(rows, picked):
        logits = jnp.dot(rows, side_w[...], preferred_element_type=f32)
        chooses = (lane >= 3) & (lane < 3 + expert_count)
        peak = jnp.max(jnp.where(chooses, logits, -1e30), axis=1, keepdims=True)
        expo = jnp.where(chooses, jnp.exp(jnp.where(chooses, logits, peak) - peak), 0.0)
        routed_gate = expo / jnp.sum(expo, axis=1, keepdims=True) * picked.astype(f32)
        mix_pre = jnp.sum(jnp.where(lane == 2, logits, 0.0), axis=1, keepdims=True)
        result = jnp.where(lane == slot_here, 1.0 / (1.0 + jnp.exp(-mix_pre)), 0.0)
        for s in range(slot_here):
            chosen = lane == 3 + at.ep * slot_here + s
            gate = jnp.sum(jnp.where(chosen, routed_gate, 0.0), axis=1, keepdims=True)
            result = jnp.where(lane == s, gate, result)
        return result

    unit = lax.broadcasted_iota(jnp.int32, (few, hidden_total), 1)
    few_lane = lax.broadcasted_iota(jnp.int32, (few, 128), 1)
    slot_bounds = [s * slot_hidden for s in range(slot_here)] + [routed, hidden_total]

    def hidden_rows(i, carry):
        here = pl.ds(pl.multiple_of(i * few, few), few)
        gate_pre = pair_pre[here, :hidden_total]
        up_pre = pair_pre[here, hidden_total:]
        d_h = d_hidden[here]
        factor = jnp.broadcast_to(factors[here, slot_here : slot_here + 1], unit.shape)
        for s in reversed(range(slot_here)):
            gate = factors[here, s : s + 1]
            factor = jnp.where(unit < slot_bounds[s + 1], gate, factor)
        sig = 1.0 / (1.0 + jnp.exp(-gate_pre))
        silu = gate_pre * sig
        hidden = silu * up_pre
        product = hidden * d_h
        gated = factor * d_h
        weighted_tile[here] = (factor * hidden).astype(bf16)
        d_pair_tile[here, :hidden_total] = (gated * up_pre * (sig + silu * (1.0 - sig))).astype(bf16)
        d_pair_tile[here, hidden_total:] = (gated * silu).astype(bf16)
        result = jnp.zeros((few, 128), f32)
        for s in range(slot_here + 1):
            inside = (unit >= slot_bounds[s]) & (unit < slot_bounds[s + 1])
            dot = jnp.sum(jnp.where(inside, product, 0.0), axis=1, keepdims=True)
            where = few_lane == (2 if s == slot_here else 3 + at.ep * slot_here + s)
            result = jnp.where(where, dot, result)
        dots[here] = result.astype(bf16)
        return carry

    def first_half(step):
        load_upstream(step).wait()
        upstream = upstream_tile[...].reshape(tile_rows, upstream_tile.shape[-1])
        d_hidden[...] = lax.dot_general(
            upstream[:, :width], down_w[...], across, preferred_element_type=f32
        )
        load_rows(step).wait()
        rows = rows_tile[...].reshape(tile_rows, width)
        factors[...] = gate_factors(rows, upstream[:, width:])
        pair_pre[...] = lax.dot_general(rows, pair_w[...], across, preferred_element_type=f32)

        @pl.when(step + 1 < 2 * depth)
        def _():
            load_upstream(step + 1).start()

        @pl.when(step >= 1)
        def _():
            for copy in stores(step - 1):
                copy.wait()

        lax.fori_loop(0, tile_rows // few, hidden_rows, 0, unroll=2)
        for copy in stores(step):
            copy.start()
        turn = step // 2

        @pl.when(step == 0)
        def _():
            last_hop(0)

        @pl.when((parity(step) == 0) & (turn + 1 < depth))
        def _():
            last_hop(turn + 1)

        @pl.when((step >= 1) & (step + 1 < depth))
        def _():
            spread(step + 1)

        @pl.when(step + 2 < depth)
        def _():
            begin_later(step + 2)

    def second_half(step):
        blocks = (2, 2, quarter)
        some = width // 2
        for n in range(2):
            columns = slice(n * some, (n + 1) * some)
            part = jnp.dot(weighted_tile[...], down_w[:, columns], preferred_element_type=f32)
            out_tile[:, :, :, columns] = part.astype(bf16).reshape(blocks + (some,))
            part = jnp.dot(d_pair_tile[...], pair_w[:, columns], preferred_element_type=f32)
            d_rows_tile[:, :, :, columns] = part.astype(bf16).reshape(blocks + (some,))
        out_tile[:, :, :, width:] = dots[...].reshape(blocks + (128,))

        @pl.when(step >= 1)
        def _():
            pl.semaphore_wait(core_credit, 1)

        for a in (0, 1):
            core_sum(a).start()
        turn = step // 2

        @pl.when(parity(step) == 0)
        def _():
            far_ready(slot_of(turn))
            load_rows(step + 1).start()

        @pl.when((parity(step) == 1) & (turn + 1 < depth))
        def _():
            near_ready(slot_of(turn + 1))
            load_rows(step + 1).start()

    def step_body(step, carry):
        @pl.when(step < 2 * depth)
        def _():
            first_half(step)

        @pl.when((step >= 1) & (step <= 2 * depth))
        def _():
            after_core(step - 1)

        odd = parity(step) == 1

        @pl.when(odd & (step >= 3))
        def _():
            after_hop((step - 3) // 2)

        @pl.when(jnp.logical_not(odd) & (step >= 4))
        def _():
            after_hop2((step - 4) // 2)

        @pl.when(step < 2 * depth)
        def _():
            second_half(step)

        return carry

    lax.fori_loop(0, 2 * depth + 3, step_body, 0)
    last = parity(depth - 1)
    for a in (0, 1):
        for turn in range(depth - 1):
            z_sum(a, turn).wait_recv()

        def total_body(i, carry):
            part = pl.ds(pl.multiple_of(i * piece, piece), piece)
            total = helds[a][last, at.y, at.x, part].astype(f32)
            for k in range(depth - 1):
                total = total + zs[a][k, part].astype(f32)
            sums[a][part] = total
            return carry

        lax.fori_loop(0, quarter // piece, total_body, 0)
    own_lane = lax.broadcasted_iota(jnp.int32, (quarter, 128), 1)
    chooses = (own_lane >= 3) & (own_lane < 3 + expert_count)
    rows = own_rows[...]
    logits = jnp.dot(rows, side_w[...], preferred_element_type=f32)
    peak = jnp.max(jnp.where(chooses, logits, -1e30), axis=1, keepdims=True)
    expo = jnp.where(chooses, jnp.exp(jnp.where(chooses, logits, peak) - peak), 0.0)
    router = expo / jnp.sum(expo, axis=1, keepdims=True)
    mixer = 1.0 / (1.0 + jnp.exp(-jnp.where(own_lane == 2, logits, 0.0)))
    gate_dots = out_sum[:, width:]
    d_router = jnp.where(chooses, gate_dots * own_upstream[:, width:].astype(f32), 0.0)
    d_logits = router * (d_router - jnp.sum(router * d_router, axis=1, keepdims=True))
    d_mix = gate_dots * mixer * (1.0 - mixer)
    d_side = jnp.where(own_lane == 2, d_mix, jnp.where(chooses, d_logits, 0.0))
    d_side_out[...] = d_side
    high = d_side.astype(bf16)
    lower = (d_side - high.astype(f32)).astype(bf16)
    d_rows_sum[...] += lax.dot_general(high, side_w[...], across, preferred_element_type=f32)
    d_rows_sum[...] += lax.dot_general(lower, side_w[...], across, preferred_element_type=f32)

    def end_body(i, carry):
        part = pl.ds(pl.multiple_of(i * few, few), few)
        resid = resid_in[part]
        block_low[part] = (resid + out_sum[part, :width]).astype(bf16)
        scale = lax.rsqrt(jnp.mean(resid * resid, axis=1, keepdims=True) + epsilon)
        unit_rows = resid * scale
        grads = d_rows_sum[part]
        scaled = grads * gain_in[...]
        inner = jnp.mean(scaled * unit_rows, axis=1, keepdims=True)
        d_resid = own_upstream[part, :width].astype(f32) + scale * (scaled - unit_rows * inner)
        d_resid_out[part] = d_resid
        d_resid_low[part] = d_resid.astype(bf16)
        return carry + jnp.sum(grads * unit_rows, axis=0, keepdims=True)

    d_gain_out[...] = lax.fori_loop(0, quarter // few, end_body, jnp.zeros((1, width), f32))
    ends = ((d_resid_low, d_resid_low_out), (block_low, block_out))

    def gather_copy(a, kind):
        low, gathered = ends[a]
        if kind == 2:
            src = dst = gathered.at[1 - at.x, at.c]
        else:
            src, dst = low, gathered.at[at.x, at.c]
        peer = at.next_x if kind == 0 else at.next_core
        return remote(src, dst, gathered_send.at[a, kind], gathered_recv.at[a, kind], peer)

    own_ends = [
        pltpu.make_async_copy(ends[a][0], ends[a][1].at[at.x, at.c], load_sem.at[a])
        for a in (0, 1)
    ]
    for a in (0, 1):
        for kind in (0, 1):
            gather_copy(a, kind).start()
        own_ends[a].start()
    for a in (0, 1):
        gather_copy(a, 0).wait_recv()
        gather_copy(a, 2).start()
    for a in (0, 1):
        own_ends[a].wait()
        gather_copy(a, 0).wait_send()
        gather_copy(a, 1).wait()
        gather_copy(a, 2).wait()
    for copy in stores(2 * depth - 1):
        copy.wait()
    for a in (0, 1):
        for turn in range(depth - 1):
            z_sum(a, turn).wait_send()
    for k in range(1, depth):
        z_copy(k).wait_send()

    def finish(j, carry):
        for kind in range(8):
            plane_copy(j, kind).wait_send()
        return carry

    lax.fori_loop(0, depth, finish, 0)


def ffn_over_all(rows, upstream_all, pair_w, down_w, side_w, resid, gain, units, expert_count):
    quarter, width = rows.shape
    ep_count, tp_count = lax.axis_size("ep"), lax.axis_size("tp")
    depth = ep_count // 2
    hidden = down_w.shape[0]
    bf16, f32 = jnp.bfloat16, jnp.float32
    wide = width + 128
    tile_rows = tp_count * quarter
    tokens = ep_count * tile_rows
    anywhere = pl.BlockSpec(memory_space=pl.ANY)
    in_vmem = pl.BlockSpec(memory_space=pltpu.VMEM)

    def both(*lead):
        return [pltpu.VMEM(lead + (quarter, columns), bf16) for columns in (width, wide)]

    dma = pltpu.SemaphoreType.DMA
    outs = pl.pallas_call(
        functools.partial(ffn_kernel, units, expert_count),
        out_shape=(
            jax.ShapeDtypeStruct((depth, 2, 2, 2, quarter, width), bf16),
            jax.ShapeDtypeStruct((depth, 2, tile_rows, hidden), bf16),
            jax.ShapeDtypeStruct((depth, 2, tile_rows, 2 * hidden), bf16),
            jax.ShapeDtypeStruct((2, 2, quarter, width), bf16),
            jax.ShapeDtypeStruct((2, 2, quarter, width), bf16),
            jax.ShapeDtypeStruct((quarter, width), f32),
            jax.ShapeDtypeStruct((1, width), f32),
            jax.ShapeDtypeStruct((quarter, 128), f32),
        ),
        in_specs=[anywhere] * 5 + [in_vmem] * 2,
        out_specs=(anywhere,) * 5 + (in_vmem,) * 3,
        scratch_shapes=[
            pltpu.VMEM((quarter, width), f32),
            pltpu.VMEM((quarter, wide), f32),
            pltpu.VMEM((2 * hidden, width), bf16),
            pltpu.VMEM((hidden, width), bf16),
            pltpu.VMEM((width, 128), bf16),
            pltpu.VMEM((2, 2, quarter, width), bf16),
            pltpu.VMEM((2, 2, quarter, wide), bf16),
            pltpu.VMEM((tile_rows, 2 * hidden), f32),
            pltpu.VMEM((tile_rows, hidden), f32),
            pltpu.VMEM((tile_rows, 128), f32),
            pltpu.VMEM((tile_rows, 128), bf16),
            pltpu.VMEM((tile_rows, hidden), bf16),
            pltpu.VMEM((tile_rows, 2 * hidden), bf16),
            pltpu.VMEM((quarter, width), bf16),
            pltpu.VMEM((quarter, wide), bf16),
            pltpu.VMEM((quarter, width), bf16),
            pltpu.VMEM((quarter, width), bf16),
        ]
        + both(2, 2)
        + both(2)
        + both(2, 2, 2)
        + both(2)
        + both()
        + both(depth - 1)
        + both(depth - 1)
        + [
            dma((2, 3)),
            dma((2, 3)),
            dma((5,)),
            dma,
            dma((depth - 1,)),
            dma((depth - 1,)),
            dma((depth, 8)),
            dma((depth, 8)),
            dma((2,)),
            dma((2,)),
            dma((2, 3)),
            dma((2, 3)),
            dma((2, depth - 1)),
            dma((2, depth - 1)),
            pltpu.SemaphoreType.REGULAR,
            pltpu.SemaphoreType.REGULAR((2,)),
            pltpu.SemaphoreType.REGULAR((2,)),
        ],
        compiler_params=pltpu.CompilerParams(
            collective_id=1, has_side_effects=True, vmem_limit_bytes=62 * 2**20
        ),
        cost_estimate=pl.CostEstimate(
            flops=12 * tokens * width * hidden,
            bytes_accessed=10 * tokens * width,
            transcendentals=tokens * hidden,
        ),
        name="ffn_all_tokens",
    )(
        rows,
        upstream_all.reshape(depth, 2, 2, 2, quarter, wide),
        pair_w,
        down_w,
        side_w,
        resid,
        gain,
    )
    rows_all, weighted, d_pair, block_out, d_resid_low, d_resid, d_gain, d_side = outs
    return (
        rows_all.reshape(tokens, width),
        weighted.reshape(tokens, hidden),
        d_pair.reshape(tokens, 2 * hidden),
        block_out.reshape(tile_rows, width),
        d_resid_low.reshape(tile_rows, width),
        d_resid,
        d_gain[0],
        d_side,
    )


def over_tp(block, distance):
    devices = range(lax.axis_size("tp"))
    return lax.ppermute(block, "tp", [(i, i ^ distance) for i in devices])


def one_of(array, index, axis):
    return lax.dynamic_index_in_dim(array, index, axis, keepdims=False)


def sum_over_tp(part):
    rows, columns = part.shape
    tp = lax.axis_index("tp")
    x, c = tp // 2, tp % 2
    blocks = part.reshape(2, 2, rows // 4, columns)
    got = over_tp(one_of(blocks, 1 - c, 1).astype(jnp.bfloat16), 1)
    chip = one_of(blocks, c, 1).astype(jnp.float32) + got.astype(jnp.float32)
    got = over_tp(one_of(chip, 1 - x, 0).astype(jnp.bfloat16), 2)
    return one_of(chip, x, 0) + got.astype(jnp.float32)


def gather_over_tp(block):
    tp = lax.axis_index("tp")
    x, c = tp // 2, tp % 2
    got = over_tp(block, 2)
    pair = jnp.where(x == 0, jnp.stack([block, got]), jnp.stack([got, block]))
    got = over_tp(pair, 1)
    four = jnp.where(c == 0, jnp.stack([pair, got], axis=1), jnp.stack([got, pair], axis=1))
    return four.reshape(4 * block.shape[0], block.shape[1])


def swap_copies(at, pieces_in, pieces_out, send_sem, recv_sem, leave):
    count = 2 * at.depth
    copies = []
    for k in range(1, count):
        to, back = lax.rem(at.ep + k, count), lax.rem(at.ep + count - k, count)
        if leave:
            src, dst, peer = pieces_in.at[to], pieces_out.at[at.ep], to
        else:
            src, dst, peer = pieces_in.at[back], pieces_out.at[back], back
        copies.append(remote(src, dst, send_sem.at[k], recv_sem.at[k], (peer, at.tp)))
    return copies


def weights_kernel(
    own_in,
    pieces_in,
    all_out,
    pieces_out,
    own_sem,
    z_send,
    z_recv,
    y_send,
    y_recv,
    swap_send,
    swap_recv,
):
    at = Place()
    depth = at.depth
    half = own_in.shape[0] // 2
    last = depth - 1

    def block(k, y, h):
        return all_out.at[at.z + k, y, pl.ds(h * half, half)]

    def z_copy(k, h, direction):
        if k == 0:
            src = own_in.at[pl.ds(h * half, half)]
        else:
            src = block(k, at.y, h)
        slot = last + k - direction
        return remote(
            src,
            block(k, at.y, h),
            z_send.at[last + k, h, (direction + 1) // 2],
            z_recv.at[slot, h],
            at.at_z(at.z + direction),
        )

    def z_arrival(k, h):
        direction = 1 if k > 0 else -1
        dst = block(k, at.y, h)
        return remote(
            dst, dst, z_send.at[last + k, h, 0], z_recv.at[last + k, h], at.at_z(at.z + direction)
        )

    def y_copy(k, h):
        src = own_in.at[pl.ds(h * half, half)] if k == 0 else block(k, at.y, h)
        return remote(
            src, block(k, at.y, h), y_send.at[last + k, h], y_recv.at[last + k, h], at.next_y
        )

    own_copies = [
        pltpu.make_async_copy(own_in, all_out.at[at.z, at.y], own_sem.at[0]),
        pltpu.make_async_copy(pieces_in.at[at.ep], pieces_out.at[at.ep], own_sem.at[1]),
    ]
    for copy in own_copies:
        copy.start()
    has_up, has_down = at.z + 1 < depth, at.z > 0
    at.greet_ep()

    for h in (0, 1):
        pl.when(has_up)(lambda: z_copy(0, h, 1).start())
        pl.when(has_down)(lambda: z_copy(0, h, -1).start())
        y_copy(0, h).start()
    swap = (at, pieces_in, pieces_out, swap_send, swap_recv)
    for copy in swap_copies(*swap, True):
        copy.start()
    for k in range(1, depth):
        for h in (0, 1):
            for sign in (-1, 1):
                there = at.z + sign * k
                exists = (there >= 0) & (there < depth)
                onward = at.z - sign
                goes_on = exists & (onward >= 0) & (onward < depth)

                @pl.when(exists)
                def _():
                    z_arrival(sign * k, h).wait_recv()

                @pl.when(goes_on)
                def _():
                    z_copy(sign * k, h, -sign).start()

                @pl.when(exists)
                def _():
                    y_copy(sign * k, h).start()

    for copy in own_copies:
        copy.wait()
    for copy in swap_copies(*swap, False):
        copy.wait_recv()
    for copy in swap_copies(*swap, True):
        copy.wait_send()
    for h in (0, 1):
        pl.when(has_up)(lambda: z_copy(0, h, 1).wait_send())
        pl.when(has_down)(lambda: z_copy(0, h, -1).wait_send())
    for k in range(-last, depth):
        there = at.z + k
        exists = (there >= 0) & (there < depth)
        sign = 1 if k > 0 else -1
        onward = at.z - sign
        goes_on = exists & (onward >= 0) & (onward < depth)
        for h in (0, 1):

            @pl.when(exists)
            def _():
                y_copy(k, h).wait()

            if k != 0:

                @pl.when(goes_on)
                def _():
                    z_copy(k, h, -sign).wait_send()


def gather_over_ep(block, pieces):
    rows, columns = block.shape
    depth = lax.axis_size("ep") // 2
    anywhere = pl.BlockSpec(memory_space=pl.ANY)
    slots = 2 * depth - 1
    out, pieces = pl.pallas_call(
        weights_kernel,
        out_shape=(
            jax.ShapeDtypeStruct((depth, 2, rows, columns), block.dtype),
            jax.ShapeDtypeStruct(pieces.shape, pieces.dtype),
        ),
        in_specs=[anywhere] * 2,
        out_specs=(anywhere,) * 2,
        scratch_shapes=[
            pltpu.SemaphoreType.DMA((2,)),
            pltpu.SemaphoreType.DMA((slots, 2, 2)),
            pltpu.SemaphoreType.DMA((slots, 2)),
            pltpu.SemaphoreType.DMA((slots, 2)),
            pltpu.SemaphoreType.DMA((slots, 2)),
            pltpu.SemaphoreType.DMA((2 * depth,)),
            pltpu.SemaphoreType.DMA((2 * depth,)),
        ],
        compiler_params=pltpu.CompilerParams(collective_id=3, has_side_effects=True),
        cost_estimate=pl.CostEstimate(
            flops=0, bytes_accessed=8 * depth * rows * columns, transcendentals=0
        ),
        name="gather_weights",
    )(block, pieces)
    return out.reshape(2 * depth * rows, columns), pieces


def grads_kernel(
    routed,
    part_in,
    own_rows_in,
    rows_in,
    d_pair_in,
    upstream_in,
    weighted_in,
    out,
    rows_out,
    gate_out,
    up_out,
    down_out,
    own,
    hop,
    from_z,
    small,
    small_got,
    rows_tile,
    d_pair_tile,
    upstream_tile,
    weighted_tile,
    turned,
    gate_total,
    up_total,
    down_total,
    load_sem,
    y_send,
    y_recv,
    z_send,
    z_recv,
    rows_send,
    rows_recv,
    small_send,
    small_recv,
    own_sem,
    tile_sem,
    store_sem,
):
    at = Place()
    depth = at.depth
    rows, columns = out.shape
    half = rows // 2
    f32 = jnp.float32
    tiles = 2 * depth
    step = 16

    def part(h):
        return pl.ds(h * half, half)

    def load(j):
        return pltpu.make_async_copy(part_in.at[at.ahead(j), at.y], own.at[j], load_sem.at[j])

    def y_copy(j, h):
        return remote(
            part_in.at[at.ahead(j), 1 - at.y, part(h)],
            hop.at[j, part(h)],
            y_send.at[j, h],
            y_recv.at[j, h],
            at.next_y,
        )

    def z_copy(j, h):
        return remote(
            own.at[j, part(h)],
            from_z.at[j - 1, part(h)],
            z_send.at[j, h],
            z_recv.at[j, h],
            at.at_z(at.ahead(j)),
        )

    def rows_copy(kind):
        if kind == 0:
            src, dst, peer = own_rows_in, rows_out.at[at.x, at.c], at.next_x
        elif kind == 1:
            src, dst, peer = own_rows_in, rows_out.at[at.x, at.c], at.next_core
        else:
            src = dst = rows_out.at[1 - at.x, at.c]
            peer = at.next_core
        return remote(src, dst, rows_send.at[kind], rows_recv.at[kind], peer)

    def small_copy(kind):
        peer = at.next_core if kind == 0 else at.next_x
        return remote(
            small.at[kind], small_got.at[kind], small_send.at[kind], small_recv.at[kind], peer
        )

    def tile_loads(tile):
        slot = lax.rem(tile, 2)
        pairs = (
            (rows_in, rows_tile),
            (d_pair_in, d_pair_tile),
            (upstream_in, upstream_tile),
            (weighted_in, weighted_tile),
        )
        return [
            pltpu.make_async_copy(src.at[tile], dst.at[slot], tile_sem.at[i, slot])
            for i, (src, dst) in enumerate(pairs)
        ]

    order = [j for j in range(1, depth)] + [0]
    for copy in tile_loads(0):
        copy.start()
    for j in order:
        load(j).start()
    at.greet_row()
    for j in order:
        for h in (0, 1):
            y_copy(j, h).start()
    for kind in (0, 1):
        rows_copy(kind).start()
    own_copy = pltpu.make_async_copy(own_rows_in, rows_out.at[at.x, at.c], own_sem)
    own_copy.start()

    def after_y(j, moves_on):
        load(j).wait()
        for h in (0, 1):
            y_copy(j, h).wait_recv()

            def body(i, carry):
                some = pl.ds(pl.multiple_of(h * half + i * step, step), step)
                own[j, some] = own[j, some] + hop[j, some]
                return carry

            lax.fori_loop(0, half // step, body, 0)

            @pl.when(moves_on)
            def _():
                z_copy(j, h).start()

    width = gate_total.shape[1]
    hidden = weighted_tile.shape[2]
    some_columns = width // 4

    def tile_body(tile, carry):
        slot = lax.rem(tile, 2)
        for copy in tile_loads(tile):
            copy.wait()

        @pl.when(tile + 1 < tiles)
        def _():
            for copy in tile_loads(tile + 1):
                copy.start()

        for total, left, first, right in (
            (gate_total, d_pair_tile, 0, rows_tile),
            (up_total, d_pair_tile, hidden, rows_tile),
            (down_total, weighted_tile, 0, upstream_tile),
        ):
            turned[...] = left[slot, :, first : first + turned.shape[0]].T
            for n in range(4):
                these = slice(n * some_columns, (n + 1) * some_columns)
                product = jnp.dot(
                    turned[...], right[slot, :, these], preferred_element_type=f32
                )
                product = product[:routed]

                @pl.when(tile == 0)
                def _():
                    total[:, these] = product

                @pl.when(tile > 0)
                def _():
                    total[:, these] += product

        @pl.when(lax.rem(tile, 2) == 1)
        def _():
            after_y(lax.rem(tile // 2 + 1, depth), tile + 1 < tiles)

        @pl.when(tile == 1)
        def _():
            rows_copy(0).wait_recv()
            rows_copy(2).start()

        return carry

    lax.fori_loop(0, tiles, tile_body, 0)
    stores = [
        pltpu.make_async_copy(total, dst, store_sem.at[i])
        for i, (total, dst) in enumerate(
            ((gate_total, gate_out), (up_total, up_out), (down_total, down_out))
        )
    ]
    for copy in stores:
        copy.start()
    for h in (0, 1):
        for k in range(1, depth):
            z_copy(k, h).wait_recv()

        def body(i, carry):
            some = pl.ds(pl.multiple_of(h * half + i * step, step), step)
            total = own[0, some].astype(f32)
            for k in range(depth - 1):
                total = total + from_z[k, some].astype(f32)
            out[some] = total
            return carry

        lax.fori_loop(0, half // step, body, 0)
    small_columns = small.shape[2]
    for kind in (0, 1):
        small[kind] = out[:, columns - small_columns :]
        small_copy(kind).start()
        small_copy(kind).wait()
        out[:, columns - small_columns :] = small[kind] + small_got[kind]
    for j in range(depth):
        for h in (0, 1):
            y_copy(j, h).wait_send()
            if j > 0:
                z_copy(j, h).wait_send()
    own_copy.wait()
    rows_copy(0).wait_send()
    for kind in (1, 2):
        rows_copy(kind).wait()
    for copy in stores:
        copy.wait()


def scatter_over_ep(parts, own_rows, rows_all, d_pair, upstream_all, weighted, routed):
    depth = lax.axis_size("ep") // 2
    rows, columns = parts.shape[0] // (2 * depth), parts.shape[1]
    dtype = parts.dtype
    quarter, width = own_rows.shape
    tokens, hidden = weighted.shape
    tiles = 2 * depth
    tile = tokens // tiles
    f32 = jnp.float32
    anywhere = pl.BlockSpec(memory_space=pl.ANY)
    in_vmem = pl.BlockSpec(memory_space=pltpu.VMEM)
    dma = pltpu.SemaphoreType.DMA
    total = jax.ShapeDtypeStruct((routed, width), f32)
    left = -(-routed // 128) * 128
    wide = upstream_all.shape[1]
    out, gathered, gate, up, down = pl.pallas_call(
        functools.partial(grads_kernel, routed),
        out_shape=(
            jax.ShapeDtypeStruct((rows, columns), f32),
            jax.ShapeDtypeStruct((2, 2, quarter, width), dtype),
            total,
            total,
            total,
        ),
        in_specs=[anywhere] * 6,
        out_specs=(in_vmem, anywhere, anywhere, anywhere, anywhere),
        scratch_shapes=[
            pltpu.VMEM((depth, rows, columns), dtype),
            pltpu.VMEM((depth, rows, columns), dtype),
            pltpu.VMEM((depth - 1, rows, columns), dtype),
            pltpu.VMEM((2, rows, 128), f32),
            pltpu.VMEM((2, rows, 128), f32),
            pltpu.VMEM((2, tile, width), dtype),
            pltpu.VMEM((2, tile, 2 * hidden), dtype),
            pltpu.VMEM((2, tile, wide), dtype),
            pltpu.VMEM((2, tile, hidden), dtype),
            pltpu.VMEM((left, tile), dtype),
            pltpu.VMEM((routed, width), f32),
            pltpu.VMEM((routed, width), f32),
            pltpu.VMEM((routed, width), f32),
            dma((depth,)),
            dma((depth, 2)),
            dma((depth, 2)),
            dma((depth, 2)),
            dma((depth, 2)),
            dma((3,)),
            dma((3,)),
            dma((2,)),
            dma((2,)),
            dma,
            dma((4, 2)),
            dma((3,)),
        ],
        compiler_params=pltpu.CompilerParams(
            collective_id=4, has_side_effects=True, vmem_limit_bytes=62 * 2**20
        ),
        cost_estimate=pl.CostEstimate(
            flops=6 * tokens * width * left, bytes_accessed=10 * tokens * width, transcendentals=0
        ),
        name="scatter_grads",
    )(
        parts.reshape(depth, 2, rows, columns),
        own_rows,
        rows_all.reshape(tiles, tile, width),
        d_pair.reshape(tiles, tile, 2 * hidden),
        upstream_all.reshape(tiles, tile, wide),
        weighted.reshape(tiles, tile, hidden),
    )
    return out, gathered.reshape(4 * quarter, width), (gate, up, down)


def shared_pieces(weights, ep_count):
    rows, hidden = weights[0].shape
    units = hidden // ep_count
    return jnp.concatenate([weight.T.reshape(ep_count, units, rows) for weight in weights], axis=1)


def shared_units_of(pieces, count):
    ep_count, units, rows = pieces.shape
    return pieces.transpose(1, 0, 2).reshape(count, units // count, ep_count * rows)


def share_back(grads, ep_count):
    units, width = grads[0].shape
    columns = width // ep_count
    pieces = jnp.concatenate(grads, axis=0).reshape(len(grads) * units, ep_count, columns)
    moved = lax.all_to_all(
        pieces.transpose(1, 0, 2), "ep", split_axis=0, concat_axis=0, tiled=True
    )
    moved = moved.reshape(ep_count, len(grads), units, columns)
    return [moved[:, i].reshape(ep_count * units, columns).T for i in range(len(grads))]


def dense_body(
    tokens,
    lengths,
    routes,
    attn_gain,
    w_query,
    w_key,
    w_value,
    w_out,
    ffn_gain,
    w_router,
    shared_mix,
    shared_gate,
    shared_up,
    shared_down,
    expert_gate,
    expert_up,
    expert_down,
    cotangent,
):
    everywhere = ("ep", "tp")
    rows_here, width = tokens.shape
    ep_count = lax.axis_size("ep")
    tp_count = lax.axis_size("tp")
    ep_index = lax.axis_index("ep")
    offset = ep_index * rows_here
    quarter = rows_here // tp_count
    first_row = lax.axis_index("tp") * quarter
    slot_here, slot_hidden = expert_gate.shape[0], expert_gate.shape[1]
    expert_count = w_router.shape[1]
    bf16, f32 = jnp.bfloat16, jnp.float32

    def my_rows(array):
        return lax.dynamic_slice_in_dim(array, first_row, quarter, 0)

    side_columns = jnp.concatenate(
        [attn_gain[:, None], ffn_gain[:, None], shared_mix[:, None], w_router], axis=1
    )
    side_columns = jnp.pad(side_columns, ((0, 0), (0, -side_columns.shape[1] % 128)))
    joined_weights, pieces = gather_over_ep(
        jnp.concatenate([w_query, w_key, w_value, w_out, side_columns], axis=1),
        shared_pieces((shared_gate, shared_up, shared_down), ep_count),
    )
    cotangent_rows = my_rows(cotangent)
    joined_weights, cotangent_rows = lax.optimization_barrier((joined_weights, cotangent_rows))
    heads_width = w_query.shape[1]
    qkv_weight = joined_weights[:, : 3 * heads_width]
    output_weight = joined_weights[:, 3 * heads_width : 4 * heads_width]
    side_weight = joined_weights[:, 4 * heads_width :]
    picked = jnp.any(
        my_rows(routes)[:, :, None] == jnp.arange(expert_count, dtype=jnp.int32), axis=1
    )
    picked_lanes = jnp.pad(picked.astype(bf16), ((0, 0), (3, 125 - expert_count)))
    upstream_all = lax.all_gather(
        jnp.concatenate([cotangent_rows, picked_lanes], axis=1), everywhere, axis=0, tiled=True
    )
    shared_rows = shared_units_of(pieces, 3)
    shared_units = shared_rows.shape[1]
    routed_units = slot_here * slot_hidden
    gate_cat, up_cat, down_cat = [
        jnp.pad(
            jnp.concatenate([expert.reshape(-1, width), shared], axis=0),
            ((0, -(routed_units + shared_units) % 128), (0, 0)),
        )
        for expert, shared in zip((expert_gate, expert_up, expert_down), shared_rows)
    ]
    pair_cat = jnp.concatenate([gate_cat, up_cat], axis=0)
    hidden_total = gate_cat.shape[0]

    heads_here = heads_width // HD
    score_scale = HD ** (-0.5)
    first_norm_scale = side_weight[:, 0].astype(f32)
    second_norm_scale = side_weight[:, 1].astype(f32)
    mix_f = side_weight[:, 2].astype(f32)
    router_f = side_weight[:, 3 : 3 + expert_count].astype(f32)
    layer_input = tokens.astype(f32)
    normed_wide, norm_one = norm_forward(layer_input, first_norm_scale)
    normed_one = normed_wide.astype(bf16)
    query_at = offset + jnp.arange(rows_here, dtype=jnp.int32)
    key_at = offset - 2 * rows_here + jnp.arange(3 * rows_here, dtype=jnp.int32)
    query_seg, query_pos = sequence_info(lengths, query_at)
    key_seg, _ = sequence_info(lengths, key_at)
    cosine, sine = rope_tables(query_pos, HD)
    projected = jnp.dot(normed_one, qkv_weight, preferred_element_type=f32)
    projected = projected.reshape(rows_here, 3, heads_here, HD)
    queries = rotate(projected[:, 0], cosine, sine).astype(bf16)
    keys = rotate(projected[:, 1], cosine, sine).astype(bf16)
    values = projected[:, 2].astype(bf16)
    carried = jnp.stack([keys, values], axis=0)
    joined = jnp.concatenate(
        [passed_along(carried, "ep", 2), passed_along(carried, "ep", 1), carried], axis=1
    )
    keys_win = joined[0]
    values_win = joined[1]
    allowed = (
        (query_seg[:, None] == key_seg[None, :])
        & (key_at[None, :] <= query_at[:, None])
        & (key_at[None, :] >= 0)
    )
    scores = (
        jnp.einsum("qhd,khd->hqk", queries, keys_win, preferred_element_type=f32) * score_scale
    )
    masked = jnp.where(allowed[None], scores, -1e30)
    peak = jnp.max(masked, axis=-1, keepdims=True)
    expo = jnp.exp(masked - peak)
    total = jnp.sum(expo, axis=-1, keepdims=True)
    log_total = peak + jnp.log(total)
    weights = expo / total
    attended = jnp.einsum(
        "hqk,khd->qhd", weights.astype(bf16), values_win, preferred_element_type=f32
    )
    attended = attended.reshape(rows_here, heads_width).astype(bf16)
    attn_part = jnp.einsum("th,dh->td", attended, output_weight, preferred_element_type=f32)
    resid = my_rows(layer_input) + sum_over_tp(attn_part)
    normed_two_wide, norm_two = norm_forward(resid, second_norm_scale)
    normed_two = normed_two_wide.astype(bf16)

    (
        normed_all,
        weighted_h,
        d_pair_pre,
        block_out,
        d_resid_low,
        d_resid,
        grad_gain_two,
        d_side,
    ) = ffn_over_all(
        normed_two,
        upstream_all,
        pair_cat,
        down_cat,
        side_weight,
        resid,
        second_norm_scale[None, :],
        (slot_here, slot_hidden, shared_units),
        expert_count,
    )
    grad_side = jnp.dot(normed_two.astype(f32).T, d_side, precision=highest)
    grad_out = jnp.einsum("td,th->dh", d_resid_low, attended, preferred_element_type=f32)
    grad_out = lax.psum_scatter(
        grad_out.astype(bf16), "ep", scatter_dimension=0, tiled=True
    ).astype(f32)
    d_attended = jnp.einsum("td,dh->th", d_resid_low, output_weight, preferred_element_type=f32)
    d_attended = d_attended.astype(bf16).reshape(rows_here, heads_here, HD)
    scores_again = (
        jnp.einsum("qhd,khd->hqk", queries, keys_win, preferred_element_type=f32) * score_scale
    )
    probs = jnp.where(allowed[None], jnp.exp(scores_again - log_total), 0.0)
    d_probs = jnp.einsum("qhd,khd->hqk", d_attended, values_win, preferred_element_type=f32)
    delta = jnp.sum(probs * d_probs, axis=-1, keepdims=True)
    delta, d_pair_late, weighted_late = lax.optimization_barrier((delta, d_pair_pre, weighted_h))
    d_scores = (probs * (d_probs - delta)).astype(bf16)
    shared_at = slice(routed_units, routed_units + shared_units)
    shared_up_at = slice(hidden_total + routed_units, hidden_total + routed_units + shared_units)
    shared_pair = jnp.concatenate([d_pair_late[:, shared_at], d_pair_late[:, shared_up_at]], axis=1)
    grad_shared_pair = jnp.einsum(
        "tf,td->fd", shared_pair, normed_all, preferred_element_type=f32
    ).astype(bf16)
    grad_shared_down = jnp.einsum(
        "tf,td->fd", weighted_late[:, shared_at], upstream_all[:, :width], preferred_element_type=f32
    ).astype(bf16)
    grad_shared = share_back(
        [grad_shared_pair[:shared_units], grad_shared_pair[shared_units:], grad_shared_down],
        ep_count,
    )
    grad_shared = [grad.astype(f32) for grad in grad_shared]

    d_keys_win = (
        jnp.einsum("hqk,qhd->khd", d_scores, queries, preferred_element_type=f32) * score_scale
    )
    d_values_win = jnp.einsum(
        "hqk,qhd->khd", probs.astype(bf16), d_attended, preferred_element_type=f32
    )
    pair_grads = jnp.stack([d_keys_win, d_values_win], axis=0)
    passed = pair_grads[:, : 2 * rows_here].astype(bf16)
    from_two = passed_along(passed[:, :rows_here], "ep", -2)
    from_one = passed_along(passed[:, rows_here:], "ep", -1)
    d_queries = (
        jnp.einsum("hqk,khd->qhd", d_scores, keys_win, preferred_element_type=f32) * score_scale
    )
    running = pair_grads[:, 2 * rows_here :] + from_one.astype(f32) + from_two.astype(f32)
    d_projected = jnp.concatenate(
        [
            unrotate(d_queries, cosine, sine).astype(bf16).reshape(rows_here, heads_width),
            unrotate(running[0], cosine, sine).astype(bf16).reshape(rows_here, heads_width),
            running[1].astype(bf16).reshape(rows_here, heads_width),
        ],
        axis=1,
    )
    d_normed_one = jnp.einsum("th,dh->td", d_projected, qkv_weight, preferred_element_type=f32)
    d_normed_one = sum_over_tp(d_normed_one)
    grad_qkv = jnp.einsum("td,th->dh", normed_one, d_projected, preferred_element_type=f32)
    d_input_norm, grad_gain_one = norm_backward(
        my_rows(layer_input), my_rows(norm_one), first_norm_scale, d_normed_one
    )
    gains = jnp.stack([grad_gain_one, grad_gain_two], axis=1)
    small = jnp.concatenate([gains, grad_side[:, 2:]], axis=1)
    grad_weights, grad_tokens, grad_experts = scatter_over_ep(
        jnp.concatenate([grad_qkv, small], axis=1).astype(bf16),
        (d_resid + d_input_norm).astype(bf16),
        normed_all,
        d_pair_pre,
        upstream_all,
        weighted_h,
        routed_units,
    )
    grad_tokens = grad_tokens.astype(f32)
    grad_experts = [grad.reshape(expert_gate.shape) for grad in grad_experts]
    small = grad_weights[:, 3 * heads_width :]
    parts = [grad_weights[:, i * heads_width : (i + 1) * heads_width] for i in range(3)]
    return (
        block_out,
        grad_tokens,
        small[:, 0],
        parts[0],
        parts[1],
        parts[2],
        grad_out,
        small[:, 1],
        small[:, 3 : 3 + expert_count],
        small[:, 2],
        grad_shared[0],
        grad_shared[1],
        grad_shared[2],
        grad_experts[0],
        grad_experts[1],
        grad_experts[2],
    )


def chosen_body(*arrays):
    rows_here, top_count = arrays[2].shape
    slot_here, expert_count = arrays[14].shape[0], arrays[9].shape[1]
    capacity = rows_here * top_count * 7 // (5 * expert_count)
    grid_of_two = lax.axis_size("ep") % 2 == 0 and lax.axis_size("tp") == 4
    if grid_of_two and rows_here < 2 * slot_here * capacity:
        return dense_body(*arrays)
    return body(*arrays)


def solution(mesh):
    placed = (
        P("ep", None),
        P(),
        P("ep", None),
        P("ep"),
        P("ep", "tp"),
        P("ep", "tp"),
        P("ep", "tp"),
        P("ep", "tp"),
        P("ep"),
        P("ep", None),
        P("ep"),
        P("ep", "tp"),
        P("ep", "tp"),
        P("ep", "tp"),
        P("ep", "tp", None),
        P("ep", "tp", None),
        P("ep", "tp", None),
        P("ep", None),
    )
    return jax.shard_map(
        chosen_body,
        mesh=mesh,
        in_specs=placed,
        out_specs=(
            P("ep", None),
            P("ep", None),
            P("ep"),
            P("ep", "tp"),
            P("ep", "tp"),
            P("ep", "tp"),
            P("ep", "tp"),
            P("ep"),
            P("ep", None),
            P("ep"),
            P("ep", "tp"),
            P("ep", "tp"),
            P("ep", "tp"),
            P("ep", "tp", None),
            P("ep", "tp", None),
            P("ep", "tp", None),
        ),
        check_vma=False,
    )
```

```python
import functools

import jax
import jax.numpy as jnp
from jax import lax
from jax.experimental import pallas as pl
from jax.experimental.pallas import tpu as pltpu
from jax.sharding import PartitionSpec as P

HD = 128


epsilon = 1e-06
rope_base = 1000000.0
highest = lax.Precision.HIGHEST
MESH = pl.DeviceIdType.MESH


def passed_along(block, axis, distance):
    devices = range(lax.axis_size(axis))
    route = [(i - distance, i) for i in devices if i - distance in devices]
    return lax.ppermute(block, axis, route)


def rope_tables(positions, width):
    steps = jnp.arange(0, width, 2, dtype=jnp.float32) / width
    inverse = rope_base ** (-steps)
    angles = positions.astype(jnp.float32)[:, None] * inverse[None, :]
    angles = jnp.concatenate([angles, angles], axis=-1)
    return (jnp.cos(angles)[:, None, :], jnp.sin(angles)[:, None, :])


def turn_half(values):
    middle = values.shape[-1] // 2
    return jnp.concatenate([-values[..., middle:], values[..., :middle]], axis=-1)


def rotate(values, cosine, sine):
    return values * cosine + turn_half(values) * sine


def unrotate(grads, cosine, sine):
    return grads * cosine - turn_half(grads * sine)


def sequence_info(lengths, indices):
    starts = jnp.cumsum(lengths) - lengths
    inside = starts[None, :] <= indices[:, None]
    segment = jnp.sum(inside.astype(jnp.int32), axis=1) - 1
    first = jnp.max(jnp.where(inside, starts[None, :], -1), axis=1)
    return (segment, indices - first)


def norm_forward(values, gain):
    scale = lax.rsqrt(jnp.mean(values * values, axis=-1, keepdims=True) + epsilon)
    return (values * scale * gain, scale)


def norm_backward(values, scale, gain, grads):
    unit = values * scale
    scaled = grads * gain
    inner = jnp.mean(scaled * unit, axis=-1, keepdims=True)
    return (scale * (scaled - unit * inner), jnp.sum(grads * unit, axis=0))


def deliver(rows):
    arrived_rows = lax.all_to_all(rows, "ep", split_axis=0, concat_axis=0, tiled=True)
    return arrived_rows


def bring_back(parts, target, rows_here, top_count):
    moved = lax.all_to_all(parts, "ep", split_axis=0, concat_axis=0, tiled=True)
    piece = moved.shape[3]
    return moved.reshape(-1, piece)[target].reshape(rows_here, top_count, piece)


def body(
    tokens,
    lengths,
    routes,
    attn_gain,
    w_query,
    w_key,
    w_value,
    w_out,
    ffn_gain,
    w_router,
    shared_mix,
    shared_gate,
    shared_up,
    shared_down,
    expert_gate,
    expert_up,
    expert_down,
    cotangent,
):
    rows_here = tokens.shape[0]
    width = tokens.shape[1]
    ep_count = lax.axis_size("ep")
    offset = lax.axis_index("ep") * rows_here
    slot_here = expert_gate.shape[0]
    top_count = routes.shape[1]
    gathered = (
        lax.all_gather(attn_gain, "ep", axis=0, tiled=True),
        lax.all_gather(w_query, "ep", axis=0, tiled=True),
        lax.all_gather(w_key, "ep", axis=0, tiled=True),
        lax.all_gather(w_value, "ep", axis=0, tiled=True),
        lax.all_gather(w_out, "ep", axis=0, tiled=True),
        lax.all_gather(ffn_gain, "ep", axis=0, tiled=True),
        lax.all_gather(w_router, "ep", axis=0, tiled=True),
        lax.all_gather(shared_mix, "ep", axis=0, tiled=True),
        lax.all_gather(shared_gate, "ep", axis=0, tiled=True),
        lax.all_gather(shared_up, "ep", axis=0, tiled=True),
        lax.all_gather(shared_down, "ep", axis=0, tiled=True),
    )
    (
        gain_first,
        query_weight_matrix,
        key_weight_matrix,
        value_weight_matrix,
        output_weight,
        gain_second,
        router_weight,
        shared_mixer_weight,
        shared_gate_weight,
        shared_up_weight,
        shared_down_weight,
    ) = gathered
    expert_count = router_weight.shape[1]
    capacity = (rows_here * top_count * 7 // (5 * expert_count) + 7) // 8 * 8
    heads_here = query_weight_matrix.shape[1] // HD
    score_scale = HD ** (-0.5)
    first_norm_scale = gain_first.astype(jnp.float32)
    second_norm_scale = gain_second.astype(jnp.float32)
    layer_input = tokens.astype(jnp.float32)
    normed_wide, norm_one = norm_forward(layer_input, first_norm_scale)
    normed_one = normed_wide.astype(jnp.bfloat16)
    query_at = offset + jnp.arange(rows_here, dtype=jnp.int32)
    key_at = offset - 2 * rows_here + jnp.arange(3 * rows_here, dtype=jnp.int32)
    query_seg, query_pos = sequence_info(lengths, query_at)
    key_seg, _ = sequence_info(lengths, key_at)
    cosine, sine = rope_tables(query_pos, HD)
    query_pre = jnp.dot(
        normed_one, query_weight_matrix, preferred_element_type=jnp.float32
    ).reshape(rows_here, heads_here, HD)
    key_pre = jnp.dot(normed_one, key_weight_matrix, preferred_element_type=jnp.float32).reshape(
        rows_here, heads_here, HD
    )
    queries = rotate(query_pre, cosine, sine).astype(jnp.bfloat16)
    keys = rotate(key_pre, cosine, sine).astype(jnp.bfloat16)
    values = (
        jnp.dot(normed_one, value_weight_matrix, preferred_element_type=jnp.float32)
        .astype(jnp.bfloat16)
        .reshape(rows_here, heads_here, HD)
    )
    carried = jnp.stack([keys, values], axis=0)
    window = [carried]
    for hop in range(2):
        carried = passed_along(carried, "ep", 1)
        window = [carried] + window
    joined = jnp.concatenate(window, axis=1)
    keys_win = joined[0]
    values_win = joined[1]
    allowed = (
        (query_seg[:, None] == key_seg[None, :])
        & (key_at[None, :] <= query_at[:, None])
        & (key_at[None, :] >= 0)
    )
    scores = (
        jnp.einsum("qhd,khd->hqk", queries, keys_win, preferred_element_type=jnp.float32)
        * score_scale
    )
    masked = jnp.where(allowed[None], scores, -1e30)
    peak = jnp.max(masked, axis=-1, keepdims=True)
    expo = jnp.exp(masked - peak)
    total = jnp.sum(expo, axis=-1, keepdims=True)
    log_total = peak + jnp.log(total)
    weights = expo / total
    attended = jnp.einsum(
        "hqk,khd->qhd", weights.astype(jnp.bfloat16), values_win, preferred_element_type=jnp.float32
    )
    attended = attended.reshape(rows_here, heads_here * HD).astype(jnp.bfloat16)
    attn_part = jnp.einsum("th,dh->td", attended, output_weight, preferred_element_type=jnp.float32)
    resid = layer_input + lax.psum(attn_part, "tp")
    normed_two_wide, norm_two = norm_forward(resid, second_norm_scale)
    normed_two = normed_two_wide.astype(jnp.bfloat16)
    normed_two_f = normed_two.astype(jnp.float32)
    router_f = router_weight.astype(jnp.float32)
    mix_f = shared_mixer_weight.astype(jnp.float32)
    router = jax.nn.softmax(jnp.dot(normed_two_f, router_f, precision=highest), axis=-1)
    picked = routes[:, :, None] == jnp.arange(expert_count, dtype=jnp.int32)[None, None, :]
    gates = jnp.sum(jnp.where(picked, router[:, None, :], 0.0), axis=-1)
    mixer = jax.nn.sigmoid(jnp.dot(normed_two_f, mix_f, precision=highest))
    shared_g = jnp.dot(normed_two, shared_gate_weight, preferred_element_type=jnp.float32)
    shared_u = jnp.dot(normed_two, shared_up_weight, preferred_element_type=jnp.float32)
    shared_h = (jax.nn.silu(shared_g) * shared_u).astype(jnp.bfloat16)
    shared_part = jnp.einsum(
        "tf,df->td", shared_h, shared_down_weight, preferred_element_type=jnp.float32
    )
    flat = routes.reshape(-1)
    hot = (flat[:, None] == jnp.arange(expert_count, dtype=jnp.int32)[None, :]).astype(jnp.int32)
    rank = jnp.sum(jnp.cumsum(hot, axis=0) * hot, axis=1) - 1
    target = flat * capacity + rank
    slot_total = ep_count * slot_here * capacity
    owner_route = (
        jnp.zeros((slot_total,), jnp.int32)
        .at[target]
        .set(jnp.arange(rows_here * top_count, dtype=jnp.int32))
    )
    filled = jnp.zeros((slot_total,), jnp.bool_).at[target].set(True)
    owner_token = owner_route // top_count
    send_rows = jnp.where(filled[:, None], normed_two[owner_token], jnp.zeros((), jnp.bfloat16))
    arrived_rows = deliver(send_rows.reshape(ep_count, slot_here, capacity, width))
    route_g = jnp.einsum(
        "nscd,sfd->nscf", arrived_rows, expert_gate, preferred_element_type=jnp.float32
    )
    route_u = jnp.einsum(
        "nscd,sfd->nscf", arrived_rows, expert_up, preferred_element_type=jnp.float32
    )
    route_h = (jax.nn.silu(route_g) * route_u).astype(jnp.bfloat16)
    route_part = jnp.einsum(
        "nscf,sfd->nscd", route_h, expert_down, preferred_element_type=jnp.float32
    )
    back_rows = bring_back(route_part, target, rows_here, top_count)
    upstream = cotangent.astype(jnp.float32)
    routed = jnp.sum(back_rows * gates[:, :, None], axis=1)
    ffn_part = mixer[:, None] * shared_part + routed
    route_dot = jnp.sum(back_rows * upstream[:, None, :], axis=-1)
    shared_dot = jnp.sum(shared_part * upstream, axis=-1)
    ffn_total, d_gate, d_mixer = lax.psum((ffn_part, route_dot, shared_dot), "tp")
    block_out = (resid + ffn_total).astype(jnp.bfloat16)
    d_router = jnp.sum(jnp.where(picked, d_gate[:, :, None], 0.0), axis=1)
    d_logits = router * (d_router - jnp.sum(router * d_router, axis=-1, keepdims=True))
    d_mixlogit = d_mixer * mixer * (1.0 - mixer)
    side = jnp.dot(d_logits, router_f.T, precision=highest) + d_mixlogit[:, None] * mix_f[None, :]
    grad_router = jnp.dot(normed_two_f.T, d_logits, precision=highest)
    grad_mix = jnp.dot(d_mixlogit, normed_two_f, precision=highest)
    d_shared = (mixer[:, None] * upstream).astype(jnp.bfloat16)
    d_sh = jnp.dot(d_shared, shared_down_weight, preferred_element_type=jnp.float32)
    sig_shared = jax.nn.sigmoid(shared_g)
    d_sg = (d_sh * shared_u * sig_shared * (1.0 + shared_g * (1.0 - sig_shared))).astype(
        jnp.bfloat16
    )
    d_su = (d_sh * shared_g * sig_shared).astype(jnp.bfloat16)
    d_normed_part = jnp.einsum(
        "tf,df->td", d_sg, shared_gate_weight, preferred_element_type=jnp.float32
    )
    d_normed_part = d_normed_part + jnp.einsum(
        "tf,df->td", d_su, shared_up_weight, preferred_element_type=jnp.float32
    )
    grad_sgate = jnp.einsum("td,tf->df", normed_two, d_sg, preferred_element_type=jnp.float32)
    grad_sup = jnp.einsum("td,tf->df", normed_two, d_su, preferred_element_type=jnp.float32)
    grad_sdown = jnp.einsum("td,tf->df", d_shared, shared_h, preferred_element_type=jnp.float32)
    d_route = (
        (gates[:, :, None] * upstream[:, None, :])
        .astype(jnp.bfloat16)
        .reshape(rows_here * top_count, width)
    )
    send_grads = jnp.where(filled[:, None], d_route[owner_route], jnp.zeros((), jnp.bfloat16))
    received_grads = deliver(send_grads.reshape(ep_count, slot_here, capacity, width))
    d_rh = jnp.einsum(
        "nscd,sfd->nscf", received_grads, expert_down, preferred_element_type=jnp.float32
    )
    sig_route = jax.nn.sigmoid(route_g)
    d_rg = (d_rh * route_u * sig_route * (1.0 + route_g * (1.0 - sig_route))).astype(jnp.bfloat16)
    routed_up_gradient = (d_rh * route_g * sig_route).astype(jnp.bfloat16)
    row_grads = jnp.einsum("nscf,sfd->nscd", d_rg, expert_gate, preferred_element_type=jnp.float32)
    row_grads = row_grads + jnp.einsum(
        "nscf,sfd->nscd", routed_up_gradient, expert_up, preferred_element_type=jnp.float32
    )
    grad_egate = jnp.einsum(
        "qxba,qxbr->xar", d_rg, arrived_rows, preferred_element_type=jnp.float32
    )
    expert_up_gradient = jnp.einsum(
        "qxba,qxbr->xar", routed_up_gradient, arrived_rows, preferred_element_type=jnp.float32
    )
    grad_edown = jnp.einsum(
        "qxba,qxbr->xar", route_h, received_grads, preferred_element_type=jnp.float32
    )
    grads_back = bring_back(row_grads, target, rows_here, top_count)
    d_routed = jnp.sum(grads_back, axis=1)
    d_normed_two = lax.psum(d_normed_part + d_routed, "tp") + side
    d_resid_norm, grad_gain_two = norm_backward(resid, norm_two, second_norm_scale, d_normed_two)
    d_resid = upstream + d_resid_norm
    d_resid_low = d_resid.astype(jnp.bfloat16)
    grad_outw = jnp.einsum("td,th->dh", d_resid_low, attended, preferred_element_type=jnp.float32)
    d_attended = jnp.einsum(
        "td,dh->th", d_resid_low, output_weight, preferred_element_type=jnp.float32
    )
    d_attended = d_attended.astype(jnp.bfloat16).reshape(rows_here, heads_here, HD)
    scores_again = (
        jnp.einsum("qhd,khd->hqk", queries, keys_win, preferred_element_type=jnp.float32)
        * score_scale
    )
    probs = jnp.where(allowed[None], jnp.exp(scores_again - log_total), 0.0)
    d_probs = jnp.einsum("qhd,khd->hqk", d_attended, values_win, preferred_element_type=jnp.float32)
    delta = jnp.sum(probs * d_probs, axis=-1, keepdims=True)
    d_scores = (probs * (d_probs - delta)).astype(jnp.bfloat16)
    d_queries = (
        jnp.einsum("hqk,khd->qhd", d_scores, keys_win, preferred_element_type=jnp.float32)
        * score_scale
    )
    d_keys_win = (
        jnp.einsum("hqk,qhd->khd", d_scores, queries, preferred_element_type=jnp.float32)
        * score_scale
    )
    d_values_win = jnp.einsum(
        "hqk,qhd->khd", probs.astype(jnp.bfloat16), d_attended, preferred_element_type=jnp.float32
    )
    pair_grads = jnp.stack([d_keys_win, d_values_win], axis=0)
    older = pair_grads[:, :rows_here]
    later = [pair_grads[:, rows_here : 2 * rows_here], pair_grads[:, 2 * rows_here :]]
    running = older
    for hop in range(2):
        running = passed_along(running, "ep", -1)
        running = running + later[hop]
    d_query_pre = (
        unrotate(d_queries, cosine, sine).astype(jnp.bfloat16).reshape(rows_here, heads_here * HD)
    )
    d_key_pre = (
        unrotate(running[0], cosine, sine).astype(jnp.bfloat16).reshape(rows_here, heads_here * HD)
    )
    d_values = running[1].astype(jnp.bfloat16).reshape(rows_here, heads_here * HD)
    grad_queryw = jnp.einsum(
        "td,th->dh", normed_one, d_query_pre, preferred_element_type=jnp.float32
    )
    grad_keyw = jnp.einsum("td,th->dh", normed_one, d_key_pre, preferred_element_type=jnp.float32)
    grad_valuew = jnp.einsum("td,th->dh", normed_one, d_values, preferred_element_type=jnp.float32)
    d_normed_one = jnp.einsum(
        "th,dh->td", d_query_pre, query_weight_matrix, preferred_element_type=jnp.float32
    )
    d_normed_one = d_normed_one + jnp.einsum(
        "th,dh->td", d_key_pre, key_weight_matrix, preferred_element_type=jnp.float32
    )
    d_normed_one = d_normed_one + jnp.einsum(
        "th,dh->td", d_values, value_weight_matrix, preferred_element_type=jnp.float32
    )
    d_normed_one = lax.psum(d_normed_one, "tp")
    d_input_norm, grad_gain_one = norm_backward(
        layer_input, norm_one, first_norm_scale, d_normed_one
    )
    grad_tokens = d_resid + d_input_norm
    summed = (
        lax.psum_scatter(grad_gain_one, "ep", scatter_dimension=0, tiled=True),
        lax.psum_scatter(grad_queryw, "ep", scatter_dimension=0, tiled=True),
        lax.psum_scatter(grad_keyw, "ep", scatter_dimension=0, tiled=True),
        lax.psum_scatter(grad_valuew, "ep", scatter_dimension=0, tiled=True),
        lax.psum_scatter(grad_outw, "ep", scatter_dimension=0, tiled=True),
        lax.psum_scatter(grad_gain_two, "ep", scatter_dimension=0, tiled=True),
        lax.psum_scatter(grad_router, "ep", scatter_dimension=0, tiled=True),
        lax.psum_scatter(grad_mix, "ep", scatter_dimension=0, tiled=True),
        lax.psum_scatter(grad_sgate, "ep", scatter_dimension=0, tiled=True),
        lax.psum_scatter(grad_sup, "ep", scatter_dimension=0, tiled=True),
        lax.psum_scatter(grad_sdown, "ep", scatter_dimension=0, tiled=True),
    )
    return (
        block_out,
        grad_tokens,
        summed[0],
        summed[1],
        summed[2],
        summed[3],
        summed[4],
        summed[5],
        summed[6],
        summed[7],
        summed[8],
        summed[9],
        summed[10],
        grad_egate,
        expert_up_gradient,
        grad_edown,
    )


class Place:
    def __init__(self):
        self.ep, self.tp = lax.axis_index("ep"), lax.axis_index("tp")
        self.z, self.y = self.ep // 2, self.ep % 2
        self.x, self.c = self.tp // 2, self.tp % 2
        self.depth = lax.axis_size("ep") // 2
        self.next_core = (self.ep, self.x * 2 + 1 - self.c)
        self.next_x = (self.ep, (1 - self.x) * 2 + self.c)
        self.next_y = (self.z * 2 + 1 - self.y, self.tp)

    def at_z(self, z):
        return (z * 2 + self.y, self.tp)

    def ahead(self, steps):
        return lax.rem(self.z + steps, self.depth)

    def behind(self, steps):
        return lax.rem(self.z + self.depth - steps, self.depth)

    def greet(self):
        barrier = pltpu.get_barrier_semaphore()
        peers = [self.next_core, self.next_x, self.next_y]
        peers += [self.at_z(self.ahead(k)) for k in range(1, self.depth)]
        for peer in peers:
            pl.semaphore_signal(barrier, inc=1, device_id=peer, device_id_type=MESH)
        pl.semaphore_wait(barrier, len(peers))

    def greet_row(self):
        barrier = pltpu.get_barrier_semaphore()
        count = 2 * self.depth
        peers = [(lax.rem(self.ep + k, count), self.tp) for k in range(1, count)]
        peers += [self.next_core, self.next_x]
        for peer in peers:
            pl.semaphore_signal(barrier, inc=1, device_id=peer, device_id_type=MESH)
        pl.semaphore_wait(barrier, len(peers))

    def greet_ep(self):
        barrier = pltpu.get_barrier_semaphore()
        count = 2 * self.depth
        for k in range(1, count):
            peer = (lax.rem(self.ep + k, count), self.tp)
            pl.semaphore_signal(barrier, inc=1, device_id=peer, device_id_type=MESH)
        pl.semaphore_wait(barrier, count - 1)


def remote(src, dst, send, recv, peer):
    return pltpu.make_async_remote_copy(
        src_ref=src, dst_ref=dst, send_sem=send, recv_sem=recv, device_id=peer, device_id_type=MESH
    )


def ffn_kernel(
    units,
    expert_count,
    rows_in,
    upstream_in,
    pair_in,
    down_in,
    side_in,
    resid_in,
    gain_in,
    rows_all,
    weighted_out,
    d_pair_out,
    block_out,
    d_resid_low_out,
    d_resid_out,
    d_gain_out,
    d_side_out,
    d_rows_sum,
    out_sum,
    pair_w,
    down_w,
    side_w,
    rows_tile,
    upstream_tile,
    pair_pre,
    d_hidden,
    factors,
    dots,
    weighted_tile,
    d_pair_tile,
    own_rows,
    own_upstream,
    block_low,
    d_resid_low,
    d_rows_tile,
    out_tile,
    d_rows_core,
    out_core,
    d_rows_held,
    out_held,
    d_rows_hop,
    out_hop,
    d_rows_hop2,
    out_hop2,
    d_rows_z,
    out_z,
    d_rows_to_z,
    out_to_z,
    gathered_send,
    gathered_recv,
    weight_sem,
    own_sem,
    z_send,
    z_recv,
    plane_send,
    plane_recv,
    load_sem,
    store_sem,
    sum_send,
    sum_recv,
    end_send,
    end_recv,
    core_credit,
    hop_credit,
    hop2_credit,
):
    at = Place()
    depth = at.depth
    quarter, width = rows_in.shape
    half = quarter // 2
    f32, bf16 = jnp.float32, jnp.bfloat16

    def weight_copies():
        pairs = (
            (pair_in, pair_w),
            (down_in, down_w),
            (side_in, side_w),
            (rows_in, own_rows),
            (upstream_in.at[at.z, at.y, at.x, at.c], own_upstream),
        )
        return [
            pltpu.make_async_copy(src, dst, weight_sem.at[i]) for i, (src, dst) in enumerate(pairs)
        ]

    for copy in weight_copies():
        copy.start()

    def block(j, y, x):
        return rows_all.at[at.behind(j), y, x, at.c]

    def plane_copy(j, kind):
        y, other_y = at.y, 1 - at.y
        own, other_x = at.x, 1 - at.x
        if kind == 0:
            src, peer = block(j, y, own), at.next_x
        elif kind == 1:
            src, peer = block(j, y, own), at.next_y
        elif kind == 2:
            src, peer = block(j, y, other_x).at[pl.ds(0, half)], at.next_y
        elif kind == 3:
            src, peer = block(j, other_y, own).at[pl.ds(half, half)], at.next_x
        else:
            src = block(j, other_y if kind >= 6 else y, other_x if kind % 2 else own)
            peer = at.next_core
        return remote(src, src, plane_send.at[j, kind], plane_recv.at[j, kind], peer)

    def z_copy(k):
        return remote(
            rows_in, block(0, at.y, at.x), z_send.at[k - 1], z_recv.at[k - 1], at.at_z(at.ahead(k))
        )

    def z_arrival(k):
        dst = block(k, at.y, at.x)
        return remote(dst, dst, z_send.at[k - 1], z_recv.at[k - 1], at.at_z(at.behind(k)))

    def begin(j):
        for kind in (0, 1, 4):
            plane_copy(j, kind).start()

    def spread(j):
        plane_copy(j, 0).wait_recv()
        plane_copy(j, 2).start()
        plane_copy(j, 5).start()
        plane_copy(j, 1).wait_recv()
        plane_copy(j, 3).start()
        plane_copy(j, 6).start()

    def begin_later(j):
        z_arrival(j).wait_recv()
        begin(j)

    def last_hop(j):
        plane_copy(j, 2).wait_recv()
        plane_copy(j, 3).wait_recv()
        plane_copy(j, 7).start()

    def near_ready(j):
        plane_copy(j, 4).wait_recv()
        plane_copy(j, 5).wait_recv()

    def far_ready(j):
        plane_copy(j, 6).wait_recv()
        plane_copy(j, 7).wait_recv()

    def parity(step):
        return lax.rem(step, 2)

    def slot_of(turn):
        return lax.rem(turn + 1, depth)

    def tile_at(step):
        return at.behind(slot_of(step // 2)), lax.rem(at.y + parity(step), 2)

    def load_rows(step):
        z, y = tile_at(step)
        return pltpu.make_async_copy(rows_all.at[z, y], rows_tile, load_sem.at[0])

    def load_upstream(step):
        z, y = tile_at(step)
        return pltpu.make_async_copy(upstream_in.at[z, y], upstream_tile, load_sem.at[1])

    def stores(step):
        z, y = tile_at(step)
        pairs = ((weighted_tile, weighted_out), (d_pair_tile, d_pair_out))
        return [
            pltpu.make_async_copy(src, dst.at[z, y], store_sem.at[i])
            for i, (src, dst) in enumerate(pairs)
        ]

    tiles, cores = (d_rows_tile, out_tile), (d_rows_core, out_core)
    helds, sums = (d_rows_held, out_held), (d_rows_sum, out_sum)
    hops, hops2, zs = (d_rows_hop, out_hop), (d_rows_hop2, out_hop2), (d_rows_z, out_z)
    to_zs = (d_rows_to_z, out_to_z)

    def sum_copy(a, kind, src, dst, peer):
        return remote(src, dst, sum_send.at[a, kind], sum_recv.at[a, kind], peer)

    def core_sum(a):
        return sum_copy(a, 0, tiles[a].at[:, 1 - at.c], cores[a], at.next_core)

    def hop_sum(a, turn):
        slot = parity(turn)
        src = helds[0].at[slot, :, 1 - at.x] if a == 0 else helds[1].at[slot, 1 - at.y]
        return sum_copy(a, 1, src, hops[a], at.next_x if a == 0 else at.next_y)

    def hop2_sum(a, turn):
        slot = parity(turn)
        if a == 0:
            src, peer = helds[0].at[slot, 1 - at.y, at.x], at.next_y
        else:
            src, peer = helds[1].at[slot, at.y, 1 - at.x], at.next_x
        return sum_copy(a, 2, src, hops2[a], peer)

    def z_sum(a, turn):
        return remote(
            to_zs[a].at[turn],
            zs[a].at[turn],
            end_send.at[a, turn],
            end_recv.at[a, turn],
            at.at_z(at.behind(turn + 1)),
        )

    def allow(semaphore, peer):
        pl.semaphore_signal(semaphore, inc=1, device_id=peer, device_id_type=MESH)

    piece = 32

    def add(into, first, second):
        def body(i, carry):
            part = pl.ds(pl.multiple_of(i * piece, piece), piece)
            into[part] = first[part] + second[part]
            return carry

        lax.fori_loop(0, quarter // piece, body, 0)

    def after_core(step):
        turn = step // 2
        held, y = parity(turn), lax.rem(at.y + parity(step), 2)

        for a in (0, 1):
            core_sum(a).wait()
            for x in (0, 1):
                add(helds[a].at[held, y, x], tiles[a].at[x, at.c], cores[a].at[x])

        @pl.when(step + 1 < 2 * depth)
        def _():
            allow(core_credit, at.next_core)

        @pl.when(parity(step) == 1)
        def _():
            @pl.when(turn >= 1)
            def _():
                for a in (0, 1):
                    pl.semaphore_wait(hop_credit.at[a], 1)

            for a in (0, 1):
                hop_sum(a, turn).start()

    def after_hop(turn):
        slot = parity(turn)

        @pl.when(turn >= 1)
        def _():
            for a in (0, 1):
                pl.semaphore_wait(hop2_credit.at[a], 1)

        for a in (0, 1):
            hop_sum(a, turn).wait()
            for moved in (1, 0):
                if a == 0:
                    y = lax.rem(at.y + moved, 2)
                    into, other = helds[0].at[slot, y, at.x], hops[0].at[y]
                else:
                    x = lax.rem(at.x + moved, 2)
                    into, other = helds[1].at[slot, at.y, x], hops[1].at[x]
                add(into, into, other)
                if moved:
                    hop2_sum(a, turn).start()

        @pl.when(turn + 1 < depth)
        def _():
            allow(hop_credit.at[0], at.next_x)
            allow(hop_credit.at[1], at.next_y)

    def after_hop2(turn):
        slot = parity(turn)
        for a in (0, 1):
            hop2_sum(a, turn).wait()
            held = helds[a].at[slot, at.y, at.x]

            @pl.when(turn + 1 < depth)
            def _():
                add(to_zs[a].at[turn], held, hops2[a])
                z_sum(a, turn).start()

            @pl.when(turn + 1 == depth)
            def _():
                add(held, held, hops2[a])

        @pl.when(turn + 1 < depth)
        def _():
            allow(hop2_credit.at[0], at.next_y)
            allow(hop2_credit.at[1], at.next_x)

    load_upstream(0).start()
    at.greet()
    z_copy(1).start()
    own_copy = pltpu.make_async_copy(rows_in, block(0, at.y, at.x), own_sem)
    own_copy.start()
    own_copy.wait()
    begin(0)
    begin_later(1)
    for k in range(2, depth):
        z_copy(k).start()
    spread(0)
    spread(1)
    near_ready(1)
    load_rows(0).start()
    for copy in weight_copies():
        copy.wait()

    tile_rows = 4 * quarter
    hidden_total = down_w.shape[0]
    lane = lax.broadcasted_iota(jnp.int32, (tile_rows, 128), 1)
    slot_here, slot_hidden, shared_hidden = units
    routed = slot_here * slot_hidden
    across = (((1,), (1,)), ((), ()))
    few = 16

    def gate_factors(rows, picked):
        logits = jnp.dot(rows, side_w[...], preferred_element_type=f32)
        chooses = (lane >= 3) & (lane < 3 + expert_count)
        peak = jnp.max(jnp.where(chooses, logits, -1e30), axis=1, keepdims=True)
        expo = jnp.where(chooses, jnp.exp(jnp.where(chooses, logits, peak) - peak), 0.0)
        routed_gate = expo / jnp.sum(expo, axis=1, keepdims=True) * picked.astype(f32)
        mix_pre = jnp.sum(jnp.where(lane == 2, logits, 0.0), axis=1, keepdims=True)
        result = jnp.where(lane == slot_here, 1.0 / (1.0 + jnp.exp(-mix_pre)), 0.0)
        for s in range(slot_here):
            chosen = lane == 3 + at.ep * slot_here + s
            gate = jnp.sum(jnp.where(chosen, routed_gate, 0.0), axis=1, keepdims=True)
            result = jnp.where(lane == s, gate, result)
        return result

    unit = lax.broadcasted_iota(jnp.int32, (few, hidden_total), 1)
    few_lane = lax.broadcasted_iota(jnp.int32, (few, 128), 1)
    slot_bounds = [s * slot_hidden for s in range(slot_here)] + [routed, hidden_total]

    def hidden_rows(i, carry):
        here = pl.ds(pl.multiple_of(i * few, few), few)
        gate_pre = pair_pre[here, :hidden_total]
        up_pre = pair_pre[here, hidden_total:]
        d_h = d_hidden[here]
        factor = jnp.broadcast_to(factors[here, slot_here : slot_here + 1], unit.shape)
        for s in reversed(range(slot_here)):
            gate = factors[here, s : s + 1]
            factor = jnp.where(unit < slot_bounds[s + 1], gate, factor)
        sig = 1.0 / (1.0 + jnp.exp(-gate_pre))
        silu = gate_pre * sig
        hidden = silu * up_pre
        product = hidden * d_h
        gated = factor * d_h
        weighted_tile[here] = (factor * hidden).astype(bf16)
        d_pair_tile[here, :hidden_total] = (gated * up_pre * (sig + silu * (1.0 - sig))).astype(bf16)
        d_pair_tile[here, hidden_total:] = (gated * silu).astype(bf16)
        result = jnp.zeros((few, 128), f32)
        for s in range(slot_here + 1):
            inside = (unit >= slot_bounds[s]) & (unit < slot_bounds[s + 1])
            dot = jnp.sum(jnp.where(inside, product, 0.0), axis=1, keepdims=True)
            where = few_lane == (2 if s == slot_here else 3 + at.ep * slot_here + s)
            result = jnp.where(where, dot, result)
        dots[here] = result.astype(bf16)
        return carry

    def first_half(step):
        load_upstream(step).wait()
        upstream = upstream_tile[...].reshape(tile_rows, upstream_tile.shape[-1])
        d_hidden[...] = lax.dot_general(
            upstream[:, :width], down_w[...], across, preferred_element_type=f32
        )
        load_rows(step).wait()
        rows = rows_tile[...].reshape(tile_rows, width)
        factors[...] = gate_factors(rows, upstream[:, width:])
        pair_pre[...] = lax.dot_general(rows, pair_w[...], across, preferred_element_type=f32)

        @pl.when(step + 1 < 2 * depth)
        def _():
            load_upstream(step + 1).start()

        @pl.when(step >= 1)
        def _():
            for copy in stores(step - 1):
                copy.wait()

        lax.fori_loop(0, tile_rows // few, hidden_rows, 0, unroll=2)
        for copy in stores(step):
            copy.start()
        turn = step // 2

        @pl.when(step == 0)
        def _():
            last_hop(0)

        @pl.when((parity(step) == 0) & (turn + 1 < depth))
        def _():
            last_hop(turn + 1)

        @pl.when((step >= 1) & (step + 1 < depth))
        def _():
            spread(step + 1)

        @pl.when(step + 2 < depth)
        def _():
            begin_later(step + 2)

    def second_half(step):
        blocks = (2, 2, quarter)
        some = width // 2
        for n in range(2):
            columns = slice(n * some, (n + 1) * some)
            part = jnp.dot(weighted_tile[...], down_w[:, columns], preferred_element_type=f32)
            out_tile[:, :, :, columns] = part.astype(bf16).reshape(blocks + (some,))
            part = jnp.dot(d_pair_tile[...], pair_w[:, columns], preferred_element_type=f32)
            d_rows_tile[:, :, :, columns] = part.astype(bf16).reshape(blocks + (some,))
        out_tile[:, :, :, width:] = dots[...].reshape(blocks + (128,))

        @pl.when(step >= 1)
        def _():
            pl.semaphore_wait(core_credit, 1)

        for a in (0, 1):
            core_sum(a).start()
        turn = step // 2

        @pl.when(parity(step) == 0)
        def _():
            far_ready(slot_of(turn))
            load_rows(step + 1).start()

        @pl.when((parity(step) == 1) & (turn + 1 < depth))
        def _():
            near_ready(slot_of(turn + 1))
            load_rows(step + 1).start()

    def step_body(step, carry):
        @pl.when(step < 2 * depth)
        def _():
            first_half(step)

        @pl.when((step >= 1) & (step <= 2 * depth))
        def _():
            after_core(step - 1)

        odd = parity(step) == 1

        @pl.when(odd & (step >= 3))
        def _():
            after_hop((step - 3) // 2)

        @pl.when(jnp.logical_not(odd) & (step >= 4))
        def _():
            after_hop2((step - 4) // 2)

        @pl.when(step < 2 * depth)
        def _():
            second_half(step)

        return carry

    lax.fori_loop(0, 2 * depth + 3, step_body, 0)
    last = parity(depth - 1)
    for a in (0, 1):
        for turn in range(depth - 1):
            z_sum(a, turn).wait_recv()

        def total_body(i, carry):
            part = pl.ds(pl.multiple_of(i * piece, piece), piece)
            total = helds[a][last, at.y, at.x, part].astype(f32)
            for k in range(depth - 1):
                total = total + zs[a][k, part].astype(f32)
            sums[a][part] = total
            return carry

        lax.fori_loop(0, quarter // piece, total_body, 0)
    own_lane = lax.broadcasted_iota(jnp.int32, (quarter, 128), 1)
    chooses = (own_lane >= 3) & (own_lane < 3 + expert_count)
    rows = own_rows[...]
    logits = jnp.dot(rows, side_w[...], preferred_element_type=f32)
    peak = jnp.max(jnp.where(chooses, logits, -1e30), axis=1, keepdims=True)
    expo = jnp.where(chooses, jnp.exp(jnp.where(chooses, logits, peak) - peak), 0.0)
    router = expo / jnp.sum(expo, axis=1, keepdims=True)
    mixer = 1.0 / (1.0 + jnp.exp(-jnp.where(own_lane == 2, logits, 0.0)))
    gate_dots = out_sum[:, width:]
    d_router = jnp.where(chooses, gate_dots * own_upstream[:, width:].astype(f32), 0.0)
    d_logits = router * (d_router - jnp.sum(router * d_router, axis=1, keepdims=True))
    d_mix = gate_dots * mixer * (1.0 - mixer)
    d_side = jnp.where(own_lane == 2, d_mix, jnp.where(chooses, d_logits, 0.0))
    d_side_out[...] = d_side
    high = d_side.astype(bf16)
    lower = (d_side - high.astype(f32)).astype(bf16)
    d_rows_sum[...] += lax.dot_general(high, side_w[...], across, preferred_element_type=f32)
    d_rows_sum[...] += lax.dot_general(lower, side_w[...], across, preferred_element_type=f32)

    def end_body(i, carry):
        part = pl.ds(pl.multiple_of(i * few, few), few)
        resid = resid_in[part]
        block_low[part] = (resid + out_sum[part, :width]).astype(bf16)
        scale = lax.rsqrt(jnp.mean(resid * resid, axis=1, keepdims=True) + epsilon)
        unit_rows = resid * scale
        grads = d_rows_sum[part]
        scaled = grads * gain_in[...]
        inner = jnp.mean(scaled * unit_rows, axis=1, keepdims=True)
        d_resid = own_upstream[part, :width].astype(f32) + scale * (scaled - unit_rows * inner)
        d_resid_out[part] = d_resid
        d_resid_low[part] = d_resid.astype(bf16)
        return carry + jnp.sum(grads * unit_rows, axis=0, keepdims=True)

    d_gain_out[...] = lax.fori_loop(0, quarter // few, end_body, jnp.zeros((1, width), f32))
    ends = ((d_resid_low, d_resid_low_out), (block_low, block_out))

    def gather_copy(a, kind):
        low, gathered = ends[a]
        if kind == 2:
            src = dst = gathered.at[1 - at.x, at.c]
        else:
            src, dst = low, gathered.at[at.x, at.c]
        peer = at.next_x if kind == 0 else at.next_core
        return remote(src, dst, gathered_send.at[a, kind], gathered_recv.at[a, kind], peer)

    own_ends = [
        pltpu.make_async_copy(ends[a][0], ends[a][1].at[at.x, at.c], load_sem.at[a])
        for a in (0, 1)
    ]
    for a in (0, 1):
        for kind in (0, 1):
            gather_copy(a, kind).start()
        own_ends[a].start()
    for a in (0, 1):
        gather_copy(a, 0).wait_recv()
        gather_copy(a, 2).start()
    for a in (0, 1):
        own_ends[a].wait()
        gather_copy(a, 0).wait_send()
        gather_copy(a, 1).wait()
        gather_copy(a, 2).wait()
    for copy in stores(2 * depth - 1):
        copy.wait()
    for a in (0, 1):
        for turn in range(depth - 1):
            z_sum(a, turn).wait_send()
    for k in range(1, depth):
        z_copy(k).wait_send()

    def finish(j, carry):
        for kind in range(8):
            plane_copy(j, kind).wait_send()
        return carry

    lax.fori_loop(0, depth, finish, 0)


def ffn_over_all(rows, upstream_all, pair_w, down_w, side_w, resid, gain, units, expert_count):
    quarter, width = rows.shape
    ep_count, tp_count = lax.axis_size("ep"), lax.axis_size("tp")
    depth = ep_count // 2
    hidden = down_w.shape[0]
    bf16, f32 = jnp.bfloat16, jnp.float32
    wide = width + 128
    tile_rows = tp_count * quarter
    tokens = ep_count * tile_rows
    anywhere = pl.BlockSpec(memory_space=pl.ANY)
    in_vmem = pl.BlockSpec(memory_space=pltpu.VMEM)

    def both(*lead):
        return [pltpu.VMEM(lead + (quarter, columns), bf16) for columns in (width, wide)]

    dma = pltpu.SemaphoreType.DMA
    outs = pl.pallas_call(
        functools.partial(ffn_kernel, units, expert_count),
        out_shape=(
            jax.ShapeDtypeStruct((depth, 2, 2, 2, quarter, width), bf16),
            jax.ShapeDtypeStruct((depth, 2, tile_rows, hidden), bf16),
            jax.ShapeDtypeStruct((depth, 2, tile_rows, 2 * hidden), bf16),
            jax.ShapeDtypeStruct((2, 2, quarter, width), bf16),
            jax.ShapeDtypeStruct((2, 2, quarter, width), bf16),
            jax.ShapeDtypeStruct((quarter, width), f32),
            jax.ShapeDtypeStruct((1, width), f32),
            jax.ShapeDtypeStruct((quarter, 128), f32),
        ),
        in_specs=[anywhere] * 5 + [in_vmem] * 2,
        out_specs=(anywhere,) * 5 + (in_vmem,) * 3,
        scratch_shapes=[
            pltpu.VMEM((quarter, width), f32),
            pltpu.VMEM((quarter, wide), f32),
            pltpu.VMEM((2 * hidden, width), bf16),
            pltpu.VMEM((hidden, width), bf16),
            pltpu.VMEM((width, 128), bf16),
            pltpu.VMEM((2, 2, quarter, width), bf16),
            pltpu.VMEM((2, 2, quarter, wide), bf16),
            pltpu.VMEM((tile_rows, 2 * hidden), f32),
            pltpu.VMEM((tile_rows, hidden), f32),
            pltpu.VMEM((tile_rows, 128), f32),
            pltpu.VMEM((tile_rows, 128), bf16),
            pltpu.VMEM((tile_rows, hidden), bf16),
            pltpu.VMEM((tile_rows, 2 * hidden), bf16),
            pltpu.VMEM((quarter, width), bf16),
            pltpu.VMEM((quarter, wide), bf16),
            pltpu.VMEM((quarter, width), bf16),
            pltpu.VMEM((quarter, width), bf16),
        ]
        + both(2, 2)
        + both(2)
        + both(2, 2, 2)
        + both(2)
        + both()
        + both(depth - 1)
        + both(depth - 1)
        + [
            dma((2, 3)),
            dma((2, 3)),
            dma((5,)),
            dma,
            dma((depth - 1,)),
            dma((depth - 1,)),
            dma((depth, 8)),
            dma((depth, 8)),
            dma((2,)),
            dma((2,)),
            dma((2, 3)),
            dma((2, 3)),
            dma((2, depth - 1)),
            dma((2, depth - 1)),
            pltpu.SemaphoreType.REGULAR,
            pltpu.SemaphoreType.REGULAR((2,)),
            pltpu.SemaphoreType.REGULAR((2,)),
        ],
        compiler_params=pltpu.CompilerParams(
            collective_id=1, has_side_effects=True, vmem_limit_bytes=62 * 2**20
        ),
        cost_estimate=pl.CostEstimate(
            flops=12 * tokens * width * hidden,
            bytes_accessed=10 * tokens * width,
            transcendentals=tokens * hidden,
        ),
        name="ffn_all_tokens",
    )(
        rows,
        upstream_all.reshape(depth, 2, 2, 2, quarter, wide),
        pair_w,
        down_w,
        side_w,
        resid,
        gain,
    )
    rows_all, weighted, d_pair, block_out, d_resid_low, d_resid, d_gain, d_side = outs
    return (
        rows_all.reshape(tokens, width),
        weighted.reshape(tokens, hidden),
        d_pair.reshape(tokens, 2 * hidden),
        block_out.reshape(tile_rows, width),
        d_resid_low.reshape(tile_rows, width),
        d_resid,
        d_gain[0],
        d_side,
    )


def over_tp(block, distance):
    devices = range(lax.axis_size("tp"))
    return lax.ppermute(block, "tp", [(i, i ^ distance) for i in devices])


def one_of(array, index, axis):
    return lax.dynamic_index_in_dim(array, index, axis, keepdims=False)


def sum_over_tp(part):
    rows, columns = part.shape
    tp = lax.axis_index("tp")
    x, c = tp // 2, tp % 2
    blocks = part.reshape(2, 2, rows // 4, columns)
    got = over_tp(one_of(blocks, 1 - c, 1).astype(jnp.bfloat16), 1)
    chip = one_of(blocks, c, 1).astype(jnp.float32) + got.astype(jnp.float32)
    got = over_tp(one_of(chip, 1 - x, 0).astype(jnp.bfloat16), 2)
    return one_of(chip, x, 0) + got.astype(jnp.float32)


def gather_over_tp(block):
    tp = lax.axis_index("tp")
    x, c = tp // 2, tp % 2
    got = over_tp(block, 2)
    pair = jnp.where(x == 0, jnp.stack([block, got]), jnp.stack([got, block]))
    got = over_tp(pair, 1)
    four = jnp.where(c == 0, jnp.stack([pair, got], axis=1), jnp.stack([got, pair], axis=1))
    return four.reshape(4 * block.shape[0], block.shape[1])


def swap_copies(at, pieces_in, pieces_out, send_sem, recv_sem, leave):
    count = 2 * at.depth
    copies = []
    for k in range(1, count):
        to, back = lax.rem(at.ep + k, count), lax.rem(at.ep + count - k, count)
        if leave:
            src, dst, peer = pieces_in.at[to], pieces_out.at[at.ep], to
        else:
            src, dst, peer = pieces_in.at[back], pieces_out.at[back], back
        copies.append(remote(src, dst, send_sem.at[k], recv_sem.at[k], (peer, at.tp)))
    return copies


def weights_kernel(
    own_in,
    pieces_in,
    all_out,
    pieces_out,
    own_sem,
    z_send,
    z_recv,
    y_send,
    y_recv,
    swap_send,
    swap_recv,
):
    at = Place()
    depth = at.depth
    half = own_in.shape[0] // 2
    last = depth - 1

    def block(k, y, h):
        return all_out.at[at.z + k, y, pl.ds(h * half, half)]

    def z_copy(k, h, direction):
        if k == 0:
            src = own_in.at[pl.ds(h * half, half)]
        else:
            src = block(k, at.y, h)
        slot = last + k - direction
        return remote(
            src,
            block(k, at.y, h),
            z_send.at[last + k, h, (direction + 1) // 2],
            z_recv.at[slot, h],
            at.at_z(at.z + direction),
        )

    def z_arrival(k, h):
        direction = 1 if k > 0 else -1
        dst = block(k, at.y, h)
        return remote(
            dst, dst, z_send.at[last + k, h, 0], z_recv.at[last + k, h], at.at_z(at.z + direction)
        )

    def y_copy(k, h):
        src = own_in.at[pl.ds(h * half, half)] if k == 0 else block(k, at.y, h)
        return remote(
            src, block(k, at.y, h), y_send.at[last + k, h], y_recv.at[last + k, h], at.next_y
        )

    own_copies = [
        pltpu.make_async_copy(own_in, all_out.at[at.z, at.y], own_sem.at[0]),
        pltpu.make_async_copy(pieces_in.at[at.ep], pieces_out.at[at.ep], own_sem.at[1]),
    ]
    for copy in own_copies:
        copy.start()
    has_up, has_down = at.z + 1 < depth, at.z > 0
    at.greet_ep()

    for h in (0, 1):
        pl.when(has_up)(lambda: z_copy(0, h, 1).start())
        pl.when(has_down)(lambda: z_copy(0, h, -1).start())
        y_copy(0, h).start()
    swap = (at, pieces_in, pieces_out, swap_send, swap_recv)
    for copy in swap_copies(*swap, True):
        copy.start()
    for k in range(1, depth):
        for h in (0, 1):
            for sign in (-1, 1):
                there = at.z + sign * k
                exists = (there >= 0) & (there < depth)
                onward = at.z - sign
                goes_on = exists & (onward >= 0) & (onward < depth)

                @pl.when(exists)
                def _():
                    z_arrival(sign * k, h).wait_recv()

                @pl.when(goes_on)
                def _():
                    z_copy(sign * k, h, -sign).start()

                @pl.when(exists)
                def _():
                    y_copy(sign * k, h).start()

    for copy in own_copies:
        copy.wait()
    for copy in swap_copies(*swap, False):
        copy.wait_recv()
    for copy in swap_copies(*swap, True):
        copy.wait_send()
    for h in (0, 1):
        pl.when(has_up)(lambda: z_copy(0, h, 1).wait_send())
        pl.when(has_down)(lambda: z_copy(0, h, -1).wait_send())
    for k in range(-last, depth):
        there = at.z + k
        exists = (there >= 0) & (there < depth)
        sign = 1 if k > 0 else -1
        onward = at.z - sign
        goes_on = exists & (onward >= 0) & (onward < depth)
        for h in (0, 1):

            @pl.when(exists)
            def _():
                y_copy(k, h).wait()

            if k != 0:

                @pl.when(goes_on)
                def _():
                    z_copy(k, h, -sign).wait_send()


def gather_over_ep(block, pieces):
    rows, columns = block.shape
    depth = lax.axis_size("ep") // 2
    anywhere = pl.BlockSpec(memory_space=pl.ANY)
    slots = 2 * depth - 1
    out, pieces = pl.pallas_call(
        weights_kernel,
        out_shape=(
            jax.ShapeDtypeStruct((depth, 2, rows, columns), block.dtype),
            jax.ShapeDtypeStruct(pieces.shape, pieces.dtype),
        ),
        in_specs=[anywhere] * 2,
        out_specs=(anywhere,) * 2,
        scratch_shapes=[
            pltpu.SemaphoreType.DMA((2,)),
            pltpu.SemaphoreType.DMA((slots, 2, 2)),
            pltpu.SemaphoreType.DMA((slots, 2)),
            pltpu.SemaphoreType.DMA((slots, 2)),
            pltpu.SemaphoreType.DMA((slots, 2)),
            pltpu.SemaphoreType.DMA((2 * depth,)),
            pltpu.SemaphoreType.DMA((2 * depth,)),
        ],
        compiler_params=pltpu.CompilerParams(collective_id=3, has_side_effects=True),
        cost_estimate=pl.CostEstimate(
            flops=0, bytes_accessed=8 * depth * rows * columns, transcendentals=0
        ),
        name="gather_weights",
    )(block, pieces)
    return out.reshape(2 * depth * rows, columns), pieces


def grads_kernel(
    routed,
    part_in,
    small_in,
    pieces_in,
    own_rows_in,
    rows_in,
    d_pair_in,
    upstream_in,
    weighted_in,
    out,
    small_out,
    pieces_out,
    rows_out,
    gate_out,
    up_out,
    down_out,
    own,
    hop,
    from_z,
    small_own,
    small_hop,
    small_z,
    small,
    small_got,
    rows_tile,
    d_pair_tile,
    upstream_tile,
    weighted_tile,
    turned,
    gate_total,
    up_total,
    down_total,
    load_sem,
    y_send,
    y_recv,
    z_send,
    z_recv,
    rows_send,
    rows_recv,
    small_send,
    small_recv,
    own_sem,
    tile_sem,
    store_sem,
    little_load,
    little_send,
    little_recv,
    swap_send,
    swap_recv,
):
    at = Place()
    depth = at.depth
    rows, columns = out.shape
    half = rows // 2
    f32 = jnp.float32
    tiles = 2 * depth
    step = 16

    def part(h):
        return pl.ds(h * half, half)

    def load(j):
        return pltpu.make_async_copy(part_in.at[at.ahead(j), at.y], own.at[j], load_sem.at[j])

    def y_copy(j, h):
        return remote(
            part_in.at[at.ahead(j), 1 - at.y, part(h)],
            hop.at[j, part(h)],
            y_send.at[j, h],
            y_recv.at[j, h],
            at.next_y,
        )

    def z_copy(j, h):
        return remote(
            own.at[j, part(h)],
            from_z.at[j - 1, part(h)],
            z_send.at[j, h],
            z_recv.at[j, h],
            at.at_z(at.ahead(j)),
        )

    def little(j):
        return pltpu.make_async_copy(
            small_in.at[at.ahead(j), at.y], small_own.at[j], little_load.at[j]
        )

    def little_y(j):
        return remote(
            small_in.at[at.ahead(j), 1 - at.y],
            small_hop.at[j],
            little_send.at[0, j],
            little_recv.at[0, j],
            at.next_y,
        )

    def little_z(j):
        return remote(
            small_own.at[j],
            small_z.at[j - 1],
            little_send.at[1, j],
            little_recv.at[1, j],
            at.at_z(at.ahead(j)),
        )

    def rows_copy(kind):
        if kind == 0:
            src, dst, peer = own_rows_in, rows_out.at[at.x, at.c], at.next_x
        elif kind == 1:
            src, dst, peer = own_rows_in, rows_out.at[at.x, at.c], at.next_core
        else:
            src = dst = rows_out.at[1 - at.x, at.c]
            peer = at.next_core
        return remote(src, dst, rows_send.at[kind], rows_recv.at[kind], peer)

    def small_copy(kind):
        peer = at.next_core if kind == 0 else at.next_x
        return remote(
            small.at[kind], small_got.at[kind], small_send.at[kind], small_recv.at[kind], peer
        )

    def tile_loads(tile):
        slot = lax.rem(tile, 2)
        pairs = (
            (rows_in, rows_tile),
            (d_pair_in, d_pair_tile),
            (upstream_in, upstream_tile),
            (weighted_in, weighted_tile),
        )
        return [
            pltpu.make_async_copy(src.at[tile], dst.at[slot], tile_sem.at[i, slot])
            for i, (src, dst) in enumerate(pairs)
        ]

    order = [j for j in range(1, depth)] + [0]
    for copy in tile_loads(0):
        copy.start()
    for j in order:
        load(j).start()
        little(j).start()
    at.greet_row()
    for j in order:
        for h in (0, 1):
            y_copy(j, h).start()
        little_y(j).start()
    for kind in (0, 1):
        rows_copy(kind).start()
    own_copies = [
        pltpu.make_async_copy(own_rows_in, rows_out.at[at.x, at.c], own_sem.at[0]),
        pltpu.make_async_copy(pieces_in.at[at.ep], pieces_out.at[at.ep], own_sem.at[1]),
    ]
    for copy in own_copies:
        copy.start()
    swap = (at, pieces_in, pieces_out, swap_send, swap_recv)
    for copy in swap_copies(*swap, True):
        copy.start()

    def after_y(j, moves_on):
        load(j).wait()
        for h in (0, 1):
            y_copy(j, h).wait_recv()

            def body(i, carry):
                some = pl.ds(pl.multiple_of(h * half + i * step, step), step)
                own[j, some] = own[j, some] + hop[j, some]
                return carry

            lax.fori_loop(0, half // step, body, 0)

            @pl.when(moves_on)
            def _():
                z_copy(j, h).start()

        little(j).wait()
        little_y(j).wait_recv()
        small_own[j] = small_own[j] + small_hop[j]

        @pl.when(moves_on)
        def _():
            little_z(j).start()

    width = gate_total.shape[1]
    hidden = weighted_tile.shape[2]
    some_columns = width // 4

    def tile_body(tile, carry):
        slot = lax.rem(tile, 2)
        for copy in tile_loads(tile):
            copy.wait()

        @pl.when(tile + 1 < tiles)
        def _():
            for copy in tile_loads(tile + 1):
                copy.start()

        for total, left, first, right in (
            (gate_total, d_pair_tile, 0, rows_tile),
            (up_total, d_pair_tile, hidden, rows_tile),
            (down_total, weighted_tile, 0, upstream_tile),
        ):
            turned[...] = left[slot, :, first : first + turned.shape[0]].T
            for n in range(4):
                these = slice(n * some_columns, (n + 1) * some_columns)
                product = jnp.dot(
                    turned[...], right[slot, :, these], preferred_element_type=f32
                )
                product = product[:routed]

                @pl.when(tile == 0)
                def _():
                    total[:, these] = product

                @pl.when(tile > 0)
                def _():
                    total[:, these] += product

        @pl.when(lax.rem(tile, 2) == 1)
        def _():
            after_y(lax.rem(tile // 2 + 1, depth), tile + 1 < tiles)

        @pl.when(tile == 1)
        def _():
            rows_copy(0).wait_recv()
            rows_copy(2).start()

        return carry

    lax.fori_loop(0, tiles, tile_body, 0)
    stores = [
        pltpu.make_async_copy(total, dst, store_sem.at[i])
        for i, (total, dst) in enumerate(
            ((gate_total, gate_out), (up_total, up_out), (down_total, down_out))
        )
    ]
    for copy in stores:
        copy.start()
    for h in (0, 1):
        for k in range(1, depth):
            z_copy(k, h).wait_recv()

        def body(i, carry):
            some = pl.ds(pl.multiple_of(h * half + i * step, step), step)
            total = own[0, some].astype(f32)
            for k in range(depth - 1):
                total = total + from_z[k, some].astype(f32)
            out[some] = total
            return carry

        lax.fori_loop(0, half // step, body, 0)
    total = small_own[0].astype(f32)
    for j in range(1, depth):
        little_z(j).wait_recv()
        total = total + small_z[j - 1].astype(f32)
    for kind in (0, 1):
        small[kind] = total
        small_copy(kind).start()
        small_copy(kind).wait()
        total = small[kind] + small_got[kind]
    small_out[...] = total
    for j in range(depth):
        for h in (0, 1):
            y_copy(j, h).wait_send()
            if j > 0:
                z_copy(j, h).wait_send()
        little_y(j).wait_send()
        if j > 0:
            little_z(j).wait_send()
    for copy in own_copies:
        copy.wait()
    for copy in swap_copies(*swap, False):
        copy.wait_recv()
    for copy in swap_copies(*swap, True):
        copy.wait_send()
    rows_copy(0).wait_send()
    for kind in (1, 2):
        rows_copy(kind).wait()
    for copy in stores:
        copy.wait()


def scatter_over_ep(parts, smalls, pieces, own_rows, tiles_of, routed):
    rows_all, d_pair, upstream_all, weighted = tiles_of
    depth = lax.axis_size("ep") // 2
    rows, columns = parts.shape[0] // (2 * depth), parts.shape[1]
    dtype = parts.dtype
    quarter, width = own_rows.shape
    tiles, tile, hidden = weighted.shape
    tokens = tiles * tile
    f32 = jnp.float32
    anywhere = pl.BlockSpec(memory_space=pl.ANY)
    in_vmem = pl.BlockSpec(memory_space=pltpu.VMEM)
    dma = pltpu.SemaphoreType.DMA
    total = jax.ShapeDtypeStruct((routed, width), f32)
    left = -(-routed // 128) * 128
    wide = upstream_all.shape[2]
    out, small, pieces, gathered, gate, up, down = pl.pallas_call(
        functools.partial(grads_kernel, routed),
        out_shape=(
            jax.ShapeDtypeStruct((rows, columns), f32),
            jax.ShapeDtypeStruct((rows, 128), f32),
            jax.ShapeDtypeStruct(pieces.shape, dtype),
            jax.ShapeDtypeStruct((2, 2, quarter, width), dtype),
            total,
            total,
            total,
        ),
        in_specs=[anywhere] * 8,
        out_specs=(in_vmem, in_vmem) + (anywhere,) * 5,
        scratch_shapes=[
            pltpu.VMEM((depth, rows, columns), dtype),
            pltpu.VMEM((depth, rows, columns), dtype),
            pltpu.VMEM((depth - 1, rows, columns), dtype),
            pltpu.VMEM((depth, rows, 128), dtype),
            pltpu.VMEM((depth, rows, 128), dtype),
            pltpu.VMEM((depth - 1, rows, 128), dtype),
            pltpu.VMEM((2, rows, 128), f32),
            pltpu.VMEM((2, rows, 128), f32),
            pltpu.VMEM((2, tile, width), dtype),
            pltpu.VMEM((2, tile, 2 * hidden), dtype),
            pltpu.VMEM((2, tile, wide), dtype),
            pltpu.VMEM((2, tile, hidden), dtype),
            pltpu.VMEM((left, tile), dtype),
            pltpu.VMEM((routed, width), f32),
            pltpu.VMEM((routed, width), f32),
            pltpu.VMEM((routed, width), f32),
            dma((depth,)),
            dma((depth, 2)),
            dma((depth, 2)),
            dma((depth, 2)),
            dma((depth, 2)),
            dma((3,)),
            dma((3,)),
            dma((2,)),
            dma((2,)),
            dma((2,)),
            dma((4, 2)),
            dma((3,)),
            dma((depth,)),
            dma((2, depth)),
            dma((2, depth)),
            dma((2 * depth,)),
            dma((2 * depth,)),
        ],
        compiler_params=pltpu.CompilerParams(
            collective_id=4, has_side_effects=True, vmem_limit_bytes=62 * 2**20
        ),
        cost_estimate=pl.CostEstimate(
            flops=6 * tokens * width * left, bytes_accessed=10 * tokens * width, transcendentals=0
        ),
        name="scatter_grads",
    )(
        parts.reshape(depth, 2, rows, columns),
        smalls.reshape(depth, 2, rows, 128),
        pieces,
        own_rows,
        rows_all,
        d_pair,
        upstream_all,
        weighted,
    )
    return out, small, pieces, gathered.reshape(4 * quarter, width), (gate, up, down)


def attention_back_kernel(
    units,
    score_scale,
    d_low_in,
    weights_in,
    q_in,
    k_in,
    v_in,
    lse_in,
    query_seg,
    key_seg,
    query_at,
    key_at,
    cos_in,
    sin_in,
    turned_in,
    own_rows_in,
    gain_in,
    d_resid_in,
    rows_in,
    d_pair_in,
    upstream_in,
    weighted_in,
    part_out,
    pieces_out,
    d_rows_out,
    d_gain_out,
    d_low,
    out_w,
    qkv_w,
    q_all,
    k_all,
    v_all,
    d_att,
    probs,
    d_probs,
    d_out,
    d_got,
    d_own,
    d_proj,
    turned,
    part,
    core_got,
    x_got,
    rows_tile,
    gate_tile,
    up_tile,
    upstream_tile,
    weighted_tile,
    gate_total,
    up_total,
    down_total,
    block_tile,
    load_sem,
    d_send,
    d_recv,
    tp_send,
    tp_recv,
    tile_sem,
    store_sem,
):
    at = Place()
    count = 2 * at.depth
    heads, tokens, head = q_all.shape
    heads_width = heads * head
    windows = k_all.shape[1] // tokens
    quarter, width = d_rows_out.shape
    f32, bf16 = jnp.float32, jnp.bfloat16
    across = (((1,), (1,)), ((), ()))
    slot_here, slot_hidden, shared_hidden = units
    routed = slot_here * slot_hidden
    hidden = weighted_in.shape[2]
    lanes = gate_tile.shape[2]
    skipped = routed - (hidden - lanes)

    def loads():
        pairs = (
            (d_low_in, d_low),
            (weights_in.at[:, pl.ds(3 * heads_width, heads_width)], out_w),
            (q_in, q_all),
            (k_in, k_all),
            (v_in, v_all),
            (weights_in.at[:, pl.ds(0, 3 * heads_width)], qkv_w),
            (turned_in, turned),
        )
        return [pltpu.make_async_copy(src, dst, load_sem.at[i]) for i, (src, dst) in enumerate(pairs)]

    def tile_loads(tile):
        slot = lax.rem(tile, 2)
        pairs = (
            (rows_in.at[tile], rows_tile),
            (d_pair_in.at[tile, :, pl.ds(hidden - lanes, lanes)], gate_tile),
            (d_pair_in.at[tile, :, pl.ds(2 * hidden - lanes, lanes)], up_tile),
            (upstream_in.at[tile, :, pl.ds(0, width)], upstream_tile),
            (weighted_in.at[tile, :, pl.ds(hidden - lanes, lanes)], weighted_tile),
        )
        return [
            pltpu.make_async_copy(src, dst.at[slot], tile_sem.at[i, slot])
            for i, (src, dst) in enumerate(pairs)
        ]

    def d_copy(w, h):
        peer = (at.ep - (2 - w), at.tp)
        return remote(d_out.at[w, h], d_got.at[w, h], d_send.at[w, h], d_recv.at[w, h], peer)

    def d_arrival(w, h):
        peer = (at.ep + (2 - w), at.tp)
        dst = d_got.at[w, h]
        return remote(dst, dst, d_send.at[w, h], d_recv.at[w, h], peer)

    def core_copy():
        return remote(part.at[:, 1 - at.c], core_got, tp_send.at[0], tp_recv.at[0], at.next_core)

    def x_copy():
        return remote(
            part.at[1 - at.x, at.c], x_got, tp_send.at[1], tp_recv.at[1], at.next_x
        )

    copies = loads()
    for copy in copies:
        copy.start()
    for copy in tile_loads(0):
        copy.start()
    at.greet_row()
    copies[0].wait()
    copies[1].wait()
    d_attended = jnp.dot(d_low[...], out_w[...], preferred_element_type=f32).astype(bf16)
    for h in range(heads):
        d_att[h] = d_attended[:, h * head : (h + 1) * head]
    for copy in copies[2:5]:
        copy.wait()
    lane = lax.broadcasted_iota(jnp.int32, (tokens, head), 1)
    sign = jnp.where(lane < head // 2, -1.0, 1.0)

    def unrotated(grads):
        turned_part = pltpu.roll(grads * sin_in[...], head // 2, 1) * sign
        return grads * cos_in[...] - turned_part

    def head_body(h, carry):
        queries, d_a = q_all[h], d_att[h]
        delta = jnp.zeros((1, tokens), f32)
        for w in range(windows):
            some = slice(w * tokens, (w + 1) * tokens)
            scores = lax.dot_general(k_all[h, some], queries, across, preferred_element_type=f32)
            allowed = (key_seg[some] == query_seg[...]) & (key_at[some] <= query_at[...])
            p = jnp.where(allowed, jnp.exp(scores * score_scale - lse_in[h]), 0.0)
            d_p = lax.dot_general(v_all[h, some], d_a, across, preferred_element_type=f32)
            probs[w] = p
            d_probs[w] = d_p
            delta = delta + jnp.sum(p * d_p, axis=0, keepdims=True)
        d_queries = jnp.zeros((head, tokens), f32)
        for w in range(windows):
            some = slice(w * tokens, (w + 1) * tokens)
            p = probs[w]
            d_scores = (p * (d_probs[w] - delta)).astype(bf16)
            d_keys = jnp.dot(d_scores, queries, preferred_element_type=f32) * score_scale
            d_values = jnp.dot(p.astype(bf16), d_a, preferred_element_type=f32)
            if w < windows - 1:
                d_out[w, h, :, :head] = d_keys.astype(bf16)
                d_out[w, h, :, head:] = d_values.astype(bf16)

                @pl.when(at.ep >= 2 - w)
                def _():
                    d_copy(w, h).start()

            else:
                d_own[h, :, :head] = d_keys
                d_own[h, :, head:] = d_values
            d_queries = d_queries + jnp.dot(
                k_all[h, some].T, d_scores, preferred_element_type=f32
            )
        here = pl.ds(pl.multiple_of(h * head, head), head)
        d_proj[:, here] = unrotated((d_queries * score_scale).T).astype(bf16)
        return carry

    lax.fori_loop(0, heads, head_body, 0)

    def tile_body(tile, carry):
        slot = lax.rem(tile, 2)
        for copy in tile_loads(tile):
            copy.wait()

        @pl.when(tile + 1 < count)
        def _():
            for copy in tile_loads(tile + 1):
                copy.start()

        for total, left, right in (
            (gate_total, gate_tile, rows_tile),
            (up_total, up_tile, rows_tile),
            (down_total, weighted_tile, upstream_tile),
        ):
            product = jnp.dot(left[slot].T, right[slot], preferred_element_type=f32)

            @pl.when(tile == 0)
            def _():
                total[...] = product

            @pl.when(tile > 0)
            def _():
                total[...] += product

        return carry

    lax.fori_loop(0, count, tile_body, 0)
    columns = width // count
    for i, total in enumerate((gate_total, up_total, down_total)):
        for e in range(count):
            pieces_out[e, i * shared_hidden : (i + 1) * shared_hidden] = total[
                skipped : skipped + shared_hidden, e * columns : (e + 1) * columns
            ].astype(bf16)

    def own_body(h, carry):
        for w in range(windows - 1):

            @pl.when(at.ep + (2 - w) < count)
            def _():
                d_arrival(w, h).wait_recv()
                d_own[h] += d_got[w, h].astype(f32)

        k_here = pl.ds(pl.multiple_of(heads_width + h * head, head), head)
        v_here = pl.ds(pl.multiple_of(2 * heads_width + h * head, head), head)
        d_proj[:, k_here] = unrotated(d_own[h, :, :head]).astype(bf16)
        d_proj[:, v_here] = d_own[h, :, head:].astype(bf16)
        return carry

    lax.fori_loop(0, heads, own_body, 0)
    copies[5].wait()
    copies[6].wait()
    for n in range(2):
        some = slice(n * (width // 2), (n + 1) * (width // 2))
        product = lax.dot_general(d_proj[...], qkv_w[some], across, preferred_element_type=f32)
        part[:, :, :, some] = product.astype(bf16).reshape(2, 2, quarter, width // 2)
    core_copy().start()
    rows = part_out.shape[0] // count

    def store(e):
        slot = lax.rem(e, 2)
        here = pl.ds(pl.multiple_of(e * rows, rows), rows)
        return pltpu.make_async_copy(block_tile.at[slot], part_out.at[here], store_sem.at[slot])

    def part_body(e, carry):
        @pl.when(e >= 2)
        def _():
            store(e - 2).wait()

        here = pl.ds(pl.multiple_of(e * rows, rows), rows)
        product = jnp.dot(turned[here], d_proj[...], preferred_element_type=f32)
        block_tile[lax.rem(e, 2)] = product.astype(bf16)
        store(e).start()
        return carry

    lax.fori_loop(0, count // 2, part_body, 0)
    core_copy().wait()
    for x in (0, 1):
        part[x, at.c] = part[x, at.c] + core_got[x]
    x_copy().start()
    lax.fori_loop(count // 2, count, part_body, 0)
    x_copy().wait()
    few = 16

    def end_body(i, carry):
        here = pl.ds(pl.multiple_of(i * few, few), few)
        grads = part[at.x, at.c, here].astype(f32) + x_got[here].astype(f32)
        inputs = own_rows_in[here].astype(f32)
        scale = lax.rsqrt(jnp.mean(inputs * inputs, axis=1, keepdims=True) + epsilon)
        unit_rows = inputs * scale
        scaled = grads * gain_in[...]
        inner = jnp.mean(scaled * unit_rows, axis=1, keepdims=True)
        d_rows = d_resid_in[here] + scale * (scaled - unit_rows * inner)
        d_rows_out[here] = d_rows.astype(bf16)
        return carry + jnp.sum(grads * unit_rows, axis=0, keepdims=True)

    d_gain_out[...] = lax.fori_loop(0, quarter // few, end_body, jnp.zeros((1, width), f32))
    for e in (count - 2, count - 1):
        store(e).wait()

    def finish(h, carry):
        for w in range(windows - 1):

            @pl.when(at.ep >= 2 - w)
            def _():
                d_copy(w, h).wait_send()

        return carry

    lax.fori_loop(0, heads, finish, 0)


def attention_back(
    d_low, weights, queries, keys, values, lse, places, tables, turned, own, tiles_of, units, scale
):
    heads, tokens, head = queries.shape
    width = d_low.shape[1]
    ep_count = lax.axis_size("ep")
    quarter = own[0].shape[0]
    window = keys.shape[1]
    windows = window // tokens
    heads_width = heads * head
    hidden = tiles_of[3].shape[2]
    shared_hidden = units[2]
    lanes = -(-shared_hidden // 128) * 128
    f32, bf16 = jnp.float32, jnp.bfloat16
    anywhere = pl.BlockSpec(memory_space=pl.ANY)
    in_vmem = pl.BlockSpec(memory_space=pltpu.VMEM)
    dma = pltpu.SemaphoreType.DMA

    def vmem(*shape, dtype=bf16):
        return pltpu.VMEM(shape, dtype)

    return pl.pallas_call(
        functools.partial(attention_back_kernel, units, scale),
        out_shape=(
            jax.ShapeDtypeStruct((width, 3 * heads_width), bf16),
            jax.ShapeDtypeStruct((ep_count, 3 * shared_hidden, width // ep_count), bf16),
            jax.ShapeDtypeStruct((quarter, width), bf16),
            jax.ShapeDtypeStruct((1, width), f32),
        ),
        in_specs=[anywhere] * 5 + [in_vmem] * 7 + [anywhere] + [in_vmem] * 3 + [anywhere] * 4,
        out_specs=(anywhere, in_vmem, in_vmem, in_vmem),
        scratch_shapes=[
            vmem(tokens, width),
            vmem(width, heads_width),
            vmem(width, 3 * heads_width),
            vmem(heads, tokens, head),
            vmem(heads, window, head),
            vmem(heads, window, head),
            vmem(heads, tokens, head),
            vmem(windows, tokens, tokens, dtype=f32),
            vmem(windows, tokens, tokens, dtype=f32),
            vmem(windows - 1, heads, tokens, 2 * head),
            vmem(windows - 1, heads, tokens, 2 * head),
            vmem(heads, tokens, 2 * head, dtype=f32),
            vmem(tokens, 3 * heads_width),
            vmem(width, tokens),
            vmem(2, 2, quarter, width),
            vmem(2, quarter, width),
            vmem(quarter, width),
            vmem(2, tokens, width),
            vmem(2, tokens, lanes),
            vmem(2, tokens, lanes),
            vmem(2, tokens, width),
            vmem(2, tokens, lanes),
            vmem(lanes, width, dtype=f32),
            vmem(lanes, width, dtype=f32),
            vmem(lanes, width, dtype=f32),
            vmem(2, width // ep_count, 3 * heads_width),
            dma((7,)),
            dma((windows - 1, heads)),
            dma((windows - 1, heads)),
            dma((2,)),
            dma((2,)),
            dma((5, 2)),
            dma((2,)),
        ],
        compiler_params=pltpu.CompilerParams(
            collective_id=5, has_side_effects=True, vmem_limit_bytes=62 * 2**20
        ),
        cost_estimate=pl.CostEstimate(
            flops=10 * heads * tokens * window * head + 20 * tokens * width * heads_width,
            bytes_accessed=2 * ep_count * tokens * width * 2,
            transcendentals=heads * tokens * window,
        ),
        name="attention_back",
    )(d_low, weights, queries, keys, values, lse, *places, *tables, turned, *own, *tiles_of)


def shared_pieces(weights, ep_count):
    rows, hidden = weights[0].shape
    units = hidden // ep_count
    return jnp.concatenate([weight.T.reshape(ep_count, units, rows) for weight in weights], axis=1)


def shared_units_of(pieces, count):
    ep_count, units, rows = pieces.shape
    return pieces.transpose(1, 0, 2).reshape(count, units // count, ep_count * rows)


def shared_whole(pieces, count):
    ep_count, units, columns = pieces.shape
    units = units // count
    pieces = pieces.reshape(ep_count, count, units, columns).astype(jnp.float32)
    return [pieces[:, i].reshape(ep_count * units, columns).T for i in range(count)]


def dense_body(
    tokens,
    lengths,
    routes,
    attn_gain,
    w_query,
    w_key,
    w_value,
    w_out,
    ffn_gain,
    w_router,
    shared_mix,
    shared_gate,
    shared_up,
    shared_down,
    expert_gate,
    expert_up,
    expert_down,
    cotangent,
):
    everywhere = ("ep", "tp")
    rows_here, width = tokens.shape
    ep_count = lax.axis_size("ep")
    tp_count = lax.axis_size("tp")
    ep_index = lax.axis_index("ep")
    offset = ep_index * rows_here
    quarter = rows_here // tp_count
    first_row = lax.axis_index("tp") * quarter
    slot_here, slot_hidden = expert_gate.shape[0], expert_gate.shape[1]
    expert_count = w_router.shape[1]
    bf16, f32 = jnp.bfloat16, jnp.float32

    def my_rows(array):
        return lax.dynamic_slice_in_dim(array, first_row, quarter, 0)

    side_columns = jnp.concatenate(
        [attn_gain[:, None], ffn_gain[:, None], shared_mix[:, None], w_router], axis=1
    )
    side_columns = jnp.pad(side_columns, ((0, 0), (0, -side_columns.shape[1] % 128)))
    joined_weights, pieces = gather_over_ep(
        jnp.concatenate([w_query, w_key, w_value, w_out, side_columns], axis=1),
        shared_pieces((shared_gate, shared_up, shared_down), ep_count),
    )
    cotangent_rows = my_rows(cotangent)
    joined_weights, cotangent_rows = lax.optimization_barrier((joined_weights, cotangent_rows))
    heads_width = w_query.shape[1]
    qkv_weight = joined_weights[:, : 3 * heads_width]
    output_weight = joined_weights[:, 3 * heads_width : 4 * heads_width]
    side_weight = joined_weights[:, 4 * heads_width :]
    picked = jnp.any(
        my_rows(routes)[:, :, None] == jnp.arange(expert_count, dtype=jnp.int32), axis=1
    )
    picked_lanes = jnp.pad(picked.astype(bf16), ((0, 0), (3, 125 - expert_count)))
    upstream_all = lax.all_gather(
        jnp.concatenate([cotangent_rows, picked_lanes], axis=1), everywhere, axis=0, tiled=True
    )
    shared_rows = shared_units_of(pieces, 3)
    shared_units = shared_rows.shape[1]
    routed_units = slot_here * slot_hidden
    gate_cat, up_cat, down_cat = [
        jnp.pad(
            jnp.concatenate([expert.reshape(-1, width), shared], axis=0),
            ((0, -(routed_units + shared_units) % 128), (0, 0)),
        )
        for expert, shared in zip((expert_gate, expert_up, expert_down), shared_rows)
    ]
    pair_cat = jnp.concatenate([gate_cat, up_cat], axis=0)
    hidden_total = gate_cat.shape[0]

    heads_here = heads_width // HD
    score_scale = HD ** (-0.5)
    first_norm_scale = side_weight[:, 0].astype(f32)
    second_norm_scale = side_weight[:, 1].astype(f32)
    mix_f = side_weight[:, 2].astype(f32)
    router_f = side_weight[:, 3 : 3 + expert_count].astype(f32)
    layer_input = tokens.astype(f32)
    normed_wide, norm_one = norm_forward(layer_input, first_norm_scale)
    normed_one = normed_wide.astype(bf16)
    query_at = offset + jnp.arange(rows_here, dtype=jnp.int32)
    key_at = offset - 2 * rows_here + jnp.arange(3 * rows_here, dtype=jnp.int32)
    query_seg, query_pos = sequence_info(lengths, query_at)
    key_seg, _ = sequence_info(lengths, key_at)
    cosine, sine = rope_tables(query_pos, HD)
    projected = jnp.dot(normed_one, qkv_weight, preferred_element_type=f32)
    projected = projected.reshape(rows_here, 3, heads_here, HD)
    queries = rotate(projected[:, 0], cosine, sine).astype(bf16)
    keys = rotate(projected[:, 1], cosine, sine).astype(bf16)
    values = projected[:, 2].astype(bf16)
    carried = jnp.stack([keys, values], axis=0)
    joined = jnp.concatenate(
        [passed_along(carried, "ep", 2), passed_along(carried, "ep", 1), carried], axis=1
    )
    keys_win = joined[0]
    values_win = joined[1]
    allowed = (
        (query_seg[:, None] == key_seg[None, :])
        & (key_at[None, :] <= query_at[:, None])
        & (key_at[None, :] >= 0)
    )
    scores = (
        jnp.einsum("qhd,khd->hqk", queries, keys_win, preferred_element_type=f32) * score_scale
    )
    masked = jnp.where(allowed[None], scores, -1e30)
    peak = jnp.max(masked, axis=-1, keepdims=True)
    expo = jnp.exp(masked - peak)
    total = jnp.sum(expo, axis=-1, keepdims=True)
    log_total = peak + jnp.log(total)
    weights = expo / total
    attended = jnp.einsum(
        "hqk,khd->qhd", weights.astype(bf16), values_win, preferred_element_type=f32
    )
    attended = attended.reshape(rows_here, heads_width).astype(bf16)
    attn_part = jnp.einsum("th,dh->td", attended, output_weight, preferred_element_type=f32)
    resid = my_rows(layer_input) + sum_over_tp(attn_part)
    normed_two_wide, norm_two = norm_forward(resid, second_norm_scale)
    normed_two = normed_two_wide.astype(bf16)

    (
        normed_all,
        weighted_h,
        d_pair_pre,
        block_out,
        d_resid_low,
        d_resid,
        grad_gain_two,
        d_side,
    ) = ffn_over_all(
        normed_two,
        upstream_all,
        pair_cat,
        down_cat,
        side_weight,
        resid,
        second_norm_scale[None, :],
        (slot_here, slot_hidden, shared_units),
        expert_count,
    )
    grad_side = jnp.dot(normed_two.astype(f32).T, d_side, precision=highest)
    grad_out = jnp.einsum("td,th->dh", d_resid_low, attended, preferred_element_type=f32)
    grad_out = lax.psum_scatter(
        grad_out.astype(bf16), "ep", scatter_dimension=0, tiled=True
    ).astype(f32)
    def by_head(array):
        return array.transpose(1, 0, 2)

    place_in_row = (query_seg[None, :], jnp.where(key_at >= 0, key_seg, -1)[:, None])
    places = place_in_row + (query_at[None, :], key_at[:, None])
    tile_shape = (ep_count, rows_here, -1)
    tiles_of = tuple(
        array.reshape(tile_shape) for array in (normed_all, d_pair_pre, upstream_all, weighted_h)
    )
    units = (slot_here, slot_hidden, shared_units)
    grad_qkv, grad_pieces, d_rows, grad_gain_one = attention_back(
        d_resid_low,
        joined_weights,
        by_head(queries),
        by_head(keys_win),
        by_head(values_win),
        log_total.reshape(heads_here, 1, rows_here),
        places,
        (cosine[:, 0], sine[:, 0]),
        normed_one.T,
        (my_rows(tokens), first_norm_scale[None, :], d_resid),
        tiles_of,
        units,
        score_scale,
    )
    gains = jnp.stack([grad_gain_one[0], grad_gain_two], axis=1)
    small = jnp.concatenate([gains, grad_side[:, 2:]], axis=1).astype(bf16)
    grad_weights, small, grad_pieces, grad_tokens, grad_experts = scatter_over_ep(
        grad_qkv, small, grad_pieces, d_rows, tiles_of, routed_units
    )
    grad_shared = shared_whole(grad_pieces, 3)
    grad_tokens = grad_tokens.astype(f32)
    grad_experts = [grad.reshape(expert_gate.shape) for grad in grad_experts]
    parts = [grad_weights[:, i * heads_width : (i + 1) * heads_width] for i in range(3)]
    return (
        block_out,
        grad_tokens,
        small[:, 0],
        parts[0],
        parts[1],
        parts[2],
        grad_out,
        small[:, 1],
        small[:, 3 : 3 + expert_count],
        small[:, 2],
        grad_shared[0],
        grad_shared[1],
        grad_shared[2],
        grad_experts[0],
        grad_experts[1],
        grad_experts[2],
    )


def chosen_body(*arrays):
    rows_here, top_count = arrays[2].shape
    slot_here, expert_count = arrays[14].shape[0], arrays[9].shape[1]
    capacity = rows_here * top_count * 7 // (5 * expert_count)
    grid_of_two = lax.axis_size("ep") % 2 == 0 and lax.axis_size("tp") == 4
    if grid_of_two and rows_here < 2 * slot_here * capacity:
        return dense_body(*arrays)
    return body(*arrays)


def solution(mesh):
    placed = (
        P("ep", None),
        P(),
        P("ep", None),
        P("ep"),
        P("ep", "tp"),
        P("ep", "tp"),
        P("ep", "tp"),
        P("ep", "tp"),
        P("ep"),
        P("ep", None),
        P("ep"),
        P("ep", "tp"),
        P("ep", "tp"),
        P("ep", "tp"),
        P("ep", "tp", None),
        P("ep", "tp", None),
        P("ep", "tp", None),
        P("ep", None),
    )
    return jax.shard_map(
        chosen_body,
        mesh=mesh,
        in_specs=placed,
        out_specs=(
            P("ep", None),
            P("ep", None),
            P("ep"),
            P("ep", "tp"),
            P("ep", "tp"),
            P("ep", "tp"),
            P("ep", "tp"),
            P("ep"),
            P("ep", None),
            P("ep"),
            P("ep", "tp"),
            P("ep", "tp"),
            P("ep", "tp"),
            P("ep", "tp", None),
            P("ep", "tp", None),
            P("ep", "tp", None),
        ),
        check_vma=False,
    )
```

```python
import functools

import jax
import jax.numpy as jnp
from jax import lax
from jax.experimental import pallas as pl
from jax.experimental.pallas import tpu as pltpu
from jax.sharding import PartitionSpec as P

HD = 128


epsilon = 1e-06
rope_base = 1000000.0
highest = lax.Precision.HIGHEST
MESH = pl.DeviceIdType.MESH


def passed_along(block, axis, distance):
    devices = range(lax.axis_size(axis))
    route = [(i - distance, i) for i in devices if i - distance in devices]
    return lax.ppermute(block, axis, route)


def rope_tables(positions, width):
    steps = jnp.arange(0, width, 2, dtype=jnp.float32) / width
    inverse = rope_base ** (-steps)
    angles = positions.astype(jnp.float32)[:, None] * inverse[None, :]
    angles = jnp.concatenate([angles, angles], axis=-1)
    return (jnp.cos(angles)[:, None, :], jnp.sin(angles)[:, None, :])


def turn_half(values):
    middle = values.shape[-1] // 2
    return jnp.concatenate([-values[..., middle:], values[..., :middle]], axis=-1)


def rotate(values, cosine, sine):
    return values * cosine + turn_half(values) * sine


def unrotate(grads, cosine, sine):
    return grads * cosine - turn_half(grads * sine)


def sequence_info(lengths, indices):
    starts = jnp.cumsum(lengths) - lengths
    inside = starts[None, :] <= indices[:, None]
    segment = jnp.sum(inside.astype(jnp.int32), axis=1) - 1
    first = jnp.max(jnp.where(inside, starts[None, :], -1), axis=1)
    return (segment, indices - first)


def norm_forward(values, gain):
    scale = lax.rsqrt(jnp.mean(values * values, axis=-1, keepdims=True) + epsilon)
    return (values * scale * gain, scale)


def norm_backward(values, scale, gain, grads):
    unit = values * scale
    scaled = grads * gain
    inner = jnp.mean(scaled * unit, axis=-1, keepdims=True)
    return (scale * (scaled - unit * inner), jnp.sum(grads * unit, axis=0))


def deliver(rows):
    arrived_rows = lax.all_to_all(rows, "ep", split_axis=0, concat_axis=0, tiled=True)
    return arrived_rows


def bring_back(parts, target, rows_here, top_count):
    moved = lax.all_to_all(parts, "ep", split_axis=0, concat_axis=0, tiled=True)
    piece = moved.shape[3]
    return moved.reshape(-1, piece)[target].reshape(rows_here, top_count, piece)


def body(
    tokens,
    lengths,
    routes,
    attn_gain,
    w_query,
    w_key,
    w_value,
    w_out,
    ffn_gain,
    w_router,
    shared_mix,
    shared_gate,
    shared_up,
    shared_down,
    expert_gate,
    expert_up,
    expert_down,
    cotangent,
):
    rows_here = tokens.shape[0]
    width = tokens.shape[1]
    ep_count = lax.axis_size("ep")
    offset = lax.axis_index("ep") * rows_here
    slot_here = expert_gate.shape[0]
    top_count = routes.shape[1]
    gathered = (
        lax.all_gather(attn_gain, "ep", axis=0, tiled=True),
        lax.all_gather(w_query, "ep", axis=0, tiled=True),
        lax.all_gather(w_key, "ep", axis=0, tiled=True),
        lax.all_gather(w_value, "ep", axis=0, tiled=True),
        lax.all_gather(w_out, "ep", axis=0, tiled=True),
        lax.all_gather(ffn_gain, "ep", axis=0, tiled=True),
        lax.all_gather(w_router, "ep", axis=0, tiled=True),
        lax.all_gather(shared_mix, "ep", axis=0, tiled=True),
        lax.all_gather(shared_gate, "ep", axis=0, tiled=True),
        lax.all_gather(shared_up, "ep", axis=0, tiled=True),
        lax.all_gather(shared_down, "ep", axis=0, tiled=True),
    )
    (
        gain_first,
        query_weight_matrix,
        key_weight_matrix,
        value_weight_matrix,
        output_weight,
        gain_second,
        router_weight,
        shared_mixer_weight,
        shared_gate_weight,
        shared_up_weight,
        shared_down_weight,
    ) = gathered
    expert_count = router_weight.shape[1]
    capacity = (rows_here * top_count * 7 // (5 * expert_count) + 7) // 8 * 8
    heads_here = query_weight_matrix.shape[1] // HD
    score_scale = HD ** (-0.5)
    first_norm_scale = gain_first.astype(jnp.float32)
    second_norm_scale = gain_second.astype(jnp.float32)
    layer_input = tokens.astype(jnp.float32)
    normed_wide, norm_one = norm_forward(layer_input, first_norm_scale)
    normed_one = normed_wide.astype(jnp.bfloat16)
    query_at = offset + jnp.arange(rows_here, dtype=jnp.int32)
    key_at = offset - 2 * rows_here + jnp.arange(3 * rows_here, dtype=jnp.int32)
    query_seg, query_pos = sequence_info(lengths, query_at)
    key_seg, _ = sequence_info(lengths, key_at)
    cosine, sine = rope_tables(query_pos, HD)
    query_pre = jnp.dot(
        normed_one, query_weight_matrix, preferred_element_type=jnp.float32
    ).reshape(rows_here, heads_here, HD)
    key_pre = jnp.dot(normed_one, key_weight_matrix, preferred_element_type=jnp.float32).reshape(
        rows_here, heads_here, HD
    )
    queries = rotate(query_pre, cosine, sine).astype(jnp.bfloat16)
    keys = rotate(key_pre, cosine, sine).astype(jnp.bfloat16)
    values = (
        jnp.dot(normed_one, value_weight_matrix, preferred_element_type=jnp.float32)
        .astype(jnp.bfloat16)
        .reshape(rows_here, heads_here, HD)
    )
    carried = jnp.stack([keys, values], axis=0)
    window = [carried]
    for hop in range(2):
        carried = passed_along(carried, "ep", 1)
        window = [carried] + window
    joined = jnp.concatenate(window, axis=1)
    keys_win = joined[0]
    values_win = joined[1]
    allowed = (
        (query_seg[:, None] == key_seg[None, :])
        & (key_at[None, :] <= query_at[:, None])
        & (key_at[None, :] >= 0)
    )
    scores = (
        jnp.einsum("qhd,khd->hqk", queries, keys_win, preferred_element_type=jnp.float32)
        * score_scale
    )
    masked = jnp.where(allowed[None], scores, -1e30)
    peak = jnp.max(masked, axis=-1, keepdims=True)
    expo = jnp.exp(masked - peak)
    total = jnp.sum(expo, axis=-1, keepdims=True)
    log_total = peak + jnp.log(total)
    weights = expo / total
    attended = jnp.einsum(
        "hqk,khd->qhd", weights.astype(jnp.bfloat16), values_win, preferred_element_type=jnp.float32
    )
    attended = attended.reshape(rows_here, heads_here * HD).astype(jnp.bfloat16)
    attn_part = jnp.einsum("th,dh->td", attended, output_weight, preferred_element_type=jnp.float32)
    resid = layer_input + lax.psum(attn_part, "tp")
    normed_two_wide, norm_two = norm_forward(resid, second_norm_scale)
    normed_two = normed_two_wide.astype(jnp.bfloat16)
    normed_two_f = normed_two.astype(jnp.float32)
    router_f = router_weight.astype(jnp.float32)
    mix_f = shared_mixer_weight.astype(jnp.float32)
    router = jax.nn.softmax(jnp.dot(normed_two_f, router_f, precision=highest), axis=-1)
    picked = routes[:, :, None] == jnp.arange(expert_count, dtype=jnp.int32)[None, None, :]
    gates = jnp.sum(jnp.where(picked, router[:, None, :], 0.0), axis=-1)
    mixer = jax.nn.sigmoid(jnp.dot(normed_two_f, mix_f, precision=highest))
    shared_g = jnp.dot(normed_two, shared_gate_weight, preferred_element_type=jnp.float32)
    shared_u = jnp.dot(normed_two, shared_up_weight, preferred_element_type=jnp.float32)
    shared_h = (jax.nn.silu(shared_g) * shared_u).astype(jnp.bfloat16)
    shared_part = jnp.einsum(
        "tf,df->td", shared_h, shared_down_weight, preferred_element_type=jnp.float32
    )
    flat = routes.reshape(-1)
    hot = (flat[:, None] == jnp.arange(expert_count, dtype=jnp.int32)[None, :]).astype(jnp.int32)
    rank = jnp.sum(jnp.cumsum(hot, axis=0) * hot, axis=1) - 1
    target = flat * capacity + rank
    slot_total = ep_count * slot_here * capacity
    owner_route = (
        jnp.zeros((slot_total,), jnp.int32)
        .at[target]
        .set(jnp.arange(rows_here * top_count, dtype=jnp.int32))
    )
    filled = jnp.zeros((slot_total,), jnp.bool_).at[target].set(True)
    owner_token = owner_route // top_count
    send_rows = jnp.where(filled[:, None], normed_two[owner_token], jnp.zeros((), jnp.bfloat16))
    arrived_rows = deliver(send_rows.reshape(ep_count, slot_here, capacity, width))
    route_g = jnp.einsum(
        "nscd,sfd->nscf", arrived_rows, expert_gate, preferred_element_type=jnp.float32
    )
    route_u = jnp.einsum(
        "nscd,sfd->nscf", arrived_rows, expert_up, preferred_element_type=jnp.float32
    )
    route_h = (jax.nn.silu(route_g) * route_u).astype(jnp.bfloat16)
    route_part = jnp.einsum(
        "nscf,sfd->nscd", route_h, expert_down, preferred_element_type=jnp.float32
    )
    back_rows = bring_back(route_part, target, rows_here, top_count)
    upstream = cotangent.astype(jnp.float32)
    routed = jnp.sum(back_rows * gates[:, :, None], axis=1)
    ffn_part = mixer[:, None] * shared_part + routed
    route_dot = jnp.sum(back_rows * upstream[:, None, :], axis=-1)
    shared_dot = jnp.sum(shared_part * upstream, axis=-1)
    ffn_total, d_gate, d_mixer = lax.psum((ffn_part, route_dot, shared_dot), "tp")
    block_out = (resid + ffn_total).astype(jnp.bfloat16)
    d_router = jnp.sum(jnp.where(picked, d_gate[:, :, None], 0.0), axis=1)
    d_logits = router * (d_router - jnp.sum(router * d_router, axis=-1, keepdims=True))
    d_mixlogit = d_mixer * mixer * (1.0 - mixer)
    side = jnp.dot(d_logits, router_f.T, precision=highest) + d_mixlogit[:, None] * mix_f[None, :]
    grad_router = jnp.dot(normed_two_f.T, d_logits, precision=highest)
    grad_mix = jnp.dot(d_mixlogit, normed_two_f, precision=highest)
    d_shared = (mixer[:, None] * upstream).astype(jnp.bfloat16)
    d_sh = jnp.dot(d_shared, shared_down_weight, preferred_element_type=jnp.float32)
    sig_shared = jax.nn.sigmoid(shared_g)
    d_sg = (d_sh * shared_u * sig_shared * (1.0 + shared_g * (1.0 - sig_shared))).astype(
        jnp.bfloat16
    )
    d_su = (d_sh * shared_g * sig_shared).astype(jnp.bfloat16)
    d_normed_part = jnp.einsum(
        "tf,df->td", d_sg, shared_gate_weight, preferred_element_type=jnp.float32
    )
    d_normed_part = d_normed_part + jnp.einsum(
        "tf,df->td", d_su, shared_up_weight, preferred_element_type=jnp.float32
    )
    grad_sgate = jnp.einsum("td,tf->df", normed_two, d_sg, preferred_element_type=jnp.float32)
    grad_sup = jnp.einsum("td,tf->df", normed_two, d_su, preferred_element_type=jnp.float32)
    grad_sdown = jnp.einsum("td,tf->df", d_shared, shared_h, preferred_element_type=jnp.float32)
    d_route = (
        (gates[:, :, None] * upstream[:, None, :])
        .astype(jnp.bfloat16)
        .reshape(rows_here * top_count, width)
    )
    send_grads = jnp.where(filled[:, None], d_route[owner_route], jnp.zeros((), jnp.bfloat16))
    received_grads = deliver(send_grads.reshape(ep_count, slot_here, capacity, width))
    d_rh = jnp.einsum(
        "nscd,sfd->nscf", received_grads, expert_down, preferred_element_type=jnp.float32
    )
    sig_route = jax.nn.sigmoid(route_g)
    d_rg = (d_rh * route_u * sig_route * (1.0 + route_g * (1.0 - sig_route))).astype(jnp.bfloat16)
    routed_up_gradient = (d_rh * route_g * sig_route).astype(jnp.bfloat16)
    row_grads = jnp.einsum("nscf,sfd->nscd", d_rg, expert_gate, preferred_element_type=jnp.float32)
    row_grads = row_grads + jnp.einsum(
        "nscf,sfd->nscd", routed_up_gradient, expert_up, preferred_element_type=jnp.float32
    )
    grad_egate = jnp.einsum(
        "qxba,qxbr->xar", d_rg, arrived_rows, preferred_element_type=jnp.float32
    )
    expert_up_gradient = jnp.einsum(
        "qxba,qxbr->xar", routed_up_gradient, arrived_rows, preferred_element_type=jnp.float32
    )
    grad_edown = jnp.einsum(
        "qxba,qxbr->xar", route_h, received_grads, preferred_element_type=jnp.float32
    )
    grads_back = bring_back(row_grads, target, rows_here, top_count)
    d_routed = jnp.sum(grads_back, axis=1)
    d_normed_two = lax.psum(d_normed_part + d_routed, "tp") + side
    d_resid_norm, grad_gain_two = norm_backward(resid, norm_two, second_norm_scale, d_normed_two)
    d_resid = upstream + d_resid_norm
    d_resid_low = d_resid.astype(jnp.bfloat16)
    grad_outw = jnp.einsum("td,th->dh", d_resid_low, attended, preferred_element_type=jnp.float32)
    d_attended = jnp.einsum(
        "td,dh->th", d_resid_low, output_weight, preferred_element_type=jnp.float32
    )
    d_attended = d_attended.astype(jnp.bfloat16).reshape(rows_here, heads_here, HD)
    scores_again = (
        jnp.einsum("qhd,khd->hqk", queries, keys_win, preferred_element_type=jnp.float32)
        * score_scale
    )
    probs = jnp.where(allowed[None], jnp.exp(scores_again - log_total), 0.0)
    d_probs = jnp.einsum("qhd,khd->hqk", d_attended, values_win, preferred_element_type=jnp.float32)
    delta = jnp.sum(probs * d_probs, axis=-1, keepdims=True)
    d_scores = (probs * (d_probs - delta)).astype(jnp.bfloat16)
    d_queries = (
        jnp.einsum("hqk,khd->qhd", d_scores, keys_win, preferred_element_type=jnp.float32)
        * score_scale
    )
    d_keys_win = (
        jnp.einsum("hqk,qhd->khd", d_scores, queries, preferred_element_type=jnp.float32)
        * score_scale
    )
    d_values_win = jnp.einsum(
        "hqk,qhd->khd", probs.astype(jnp.bfloat16), d_attended, preferred_element_type=jnp.float32
    )
    pair_grads = jnp.stack([d_keys_win, d_values_win], axis=0)
    older = pair_grads[:, :rows_here]
    later = [pair_grads[:, rows_here : 2 * rows_here], pair_grads[:, 2 * rows_here :]]
    running = older
    for hop in range(2):
        running = passed_along(running, "ep", -1)
        running = running + later[hop]
    d_query_pre = (
        unrotate(d_queries, cosine, sine).astype(jnp.bfloat16).reshape(rows_here, heads_here * HD)
    )
    d_key_pre = (
        unrotate(running[0], cosine, sine).astype(jnp.bfloat16).reshape(rows_here, heads_here * HD)
    )
    d_values = running[1].astype(jnp.bfloat16).reshape(rows_here, heads_here * HD)
    grad_queryw = jnp.einsum(
        "td,th->dh", normed_one, d_query_pre, preferred_element_type=jnp.float32
    )
    grad_keyw = jnp.einsum("td,th->dh", normed_one, d_key_pre, preferred_element_type=jnp.float32)
    grad_valuew = jnp.einsum("td,th->dh", normed_one, d_values, preferred_element_type=jnp.float32)
    d_normed_one = jnp.einsum(
        "th,dh->td", d_query_pre, query_weight_matrix, preferred_element_type=jnp.float32
    )
    d_normed_one = d_normed_one + jnp.einsum(
        "th,dh->td", d_key_pre, key_weight_matrix, preferred_element_type=jnp.float32
    )
    d_normed_one = d_normed_one + jnp.einsum(
        "th,dh->td", d_values, value_weight_matrix, preferred_element_type=jnp.float32
    )
    d_normed_one = lax.psum(d_normed_one, "tp")
    d_input_norm, grad_gain_one = norm_backward(
        layer_input, norm_one, first_norm_scale, d_normed_one
    )
    grad_tokens = d_resid + d_input_norm
    summed = (
        lax.psum_scatter(grad_gain_one, "ep", scatter_dimension=0, tiled=True),
        lax.psum_scatter(grad_queryw, "ep", scatter_dimension=0, tiled=True),
        lax.psum_scatter(grad_keyw, "ep", scatter_dimension=0, tiled=True),
        lax.psum_scatter(grad_valuew, "ep", scatter_dimension=0, tiled=True),
        lax.psum_scatter(grad_outw, "ep", scatter_dimension=0, tiled=True),
        lax.psum_scatter(grad_gain_two, "ep", scatter_dimension=0, tiled=True),
        lax.psum_scatter(grad_router, "ep", scatter_dimension=0, tiled=True),
        lax.psum_scatter(grad_mix, "ep", scatter_dimension=0, tiled=True),
        lax.psum_scatter(grad_sgate, "ep", scatter_dimension=0, tiled=True),
        lax.psum_scatter(grad_sup, "ep", scatter_dimension=0, tiled=True),
        lax.psum_scatter(grad_sdown, "ep", scatter_dimension=0, tiled=True),
    )
    return (
        block_out,
        grad_tokens,
        summed[0],
        summed[1],
        summed[2],
        summed[3],
        summed[4],
        summed[5],
        summed[6],
        summed[7],
        summed[8],
        summed[9],
        summed[10],
        grad_egate,
        expert_up_gradient,
        grad_edown,
    )


class Place:
    def __init__(self):
        self.ep, self.tp = lax.axis_index("ep"), lax.axis_index("tp")
        self.z, self.y = self.ep // 2, self.ep % 2
        self.x, self.c = self.tp // 2, self.tp % 2
        self.depth = lax.axis_size("ep") // 2
        self.next_core = (self.ep, self.x * 2 + 1 - self.c)
        self.next_x = (self.ep, (1 - self.x) * 2 + self.c)
        self.next_y = (self.z * 2 + 1 - self.y, self.tp)

    def at_z(self, z):
        return (z * 2 + self.y, self.tp)

    def ahead(self, steps):
        return lax.rem(self.z + steps, self.depth)

    def behind(self, steps):
        return lax.rem(self.z + self.depth - steps, self.depth)

    def greet(self):
        barrier = pltpu.get_barrier_semaphore()
        peers = [self.next_core, self.next_x, self.next_y]
        peers += [self.at_z(self.ahead(k)) for k in range(1, self.depth)]
        for peer in peers:
            pl.semaphore_signal(barrier, inc=1, device_id=peer, device_id_type=MESH)
        pl.semaphore_wait(barrier, len(peers))

    def greet_row(self):
        barrier = pltpu.get_barrier_semaphore()
        count = 2 * self.depth
        peers = [(lax.rem(self.ep + k, count), self.tp) for k in range(1, count)]
        peers += [self.next_core, self.next_x]
        for peer in peers:
            pl.semaphore_signal(barrier, inc=1, device_id=peer, device_id_type=MESH)
        pl.semaphore_wait(barrier, len(peers))

    def greet_ep(self):
        barrier = pltpu.get_barrier_semaphore()
        count = 2 * self.depth
        for k in range(1, count):
            peer = (lax.rem(self.ep + k, count), self.tp)
            pl.semaphore_signal(barrier, inc=1, device_id=peer, device_id_type=MESH)
        pl.semaphore_wait(barrier, count - 1)


def remote(src, dst, send, recv, peer):
    return pltpu.make_async_remote_copy(
        src_ref=src, dst_ref=dst, send_sem=send, recv_sem=recv, device_id=peer, device_id_type=MESH
    )


def ffn_kernel(
    units,
    expert_count,
    rows_in,
    upstream_in,
    pair_in,
    down_in,
    side_in,
    resid_in,
    gain_in,
    rows_all,
    weighted_out,
    d_pair_out,
    block_out,
    d_resid_low_out,
    d_resid_out,
    d_gain_out,
    d_side_out,
    d_rows_sum,
    out_sum,
    pair_w,
    down_w,
    side_w,
    rows_tile,
    upstream_tile,
    pair_pre,
    d_hidden,
    factors,
    dots,
    weighted_tile,
    d_pair_tile,
    own_rows,
    own_upstream,
    d_resid_low,
    d_rows_tile,
    out_tile,
    d_rows_core,
    out_core,
    d_rows_held,
    out_held,
    d_rows_hop,
    out_hop,
    d_rows_hop2,
    out_hop2,
    d_rows_z,
    out_z,
    d_rows_to_z,
    out_to_z,
    gathered_send,
    gathered_recv,
    hop_send,
    hop_recv,
    weight_sem,
    own_sem,
    z_send,
    z_recv,
    plane_send,
    plane_recv,
    load_sem,
    store_sem,
    sum_send,
    sum_recv,
    end_send,
    end_recv,
    core_credit,
    hop_credit,
    hop2_credit,
):
    at = Place()
    depth = at.depth
    quarter, width = rows_in.shape
    half = quarter // 2
    f32, bf16 = jnp.float32, jnp.bfloat16

    def weight_copies():
        pairs = (
            (pair_in, pair_w),
            (down_in, down_w),
            (side_in, side_w),
            (rows_in, own_rows),
            (upstream_in.at[at.z, at.y, at.x, at.c], own_upstream),
        )
        return [
            pltpu.make_async_copy(src, dst, weight_sem.at[i]) for i, (src, dst) in enumerate(pairs)
        ]

    for copy in weight_copies():
        copy.start()

    def block(j, y, x):
        return rows_all.at[at.behind(j), y, x, at.c]

    def plane_copy(j, kind):
        y, other_y = at.y, 1 - at.y
        own, other_x = at.x, 1 - at.x
        if kind == 0:
            src, peer = block(j, y, own), at.next_x
        elif kind == 1:
            src, peer = block(j, y, own), at.next_y
        elif kind == 2:
            src, peer = block(j, y, other_x).at[pl.ds(0, half)], at.next_y
        elif kind == 3:
            src, peer = block(j, other_y, own).at[pl.ds(half, half)], at.next_x
        else:
            src = block(j, other_y if kind >= 6 else y, other_x if kind % 2 else own)
            peer = at.next_core
        return remote(src, src, plane_send.at[j, kind], plane_recv.at[j, kind], peer)

    def z_copy(k):
        return remote(
            rows_in, block(0, at.y, at.x), z_send.at[k - 1], z_recv.at[k - 1], at.at_z(at.ahead(k))
        )

    def z_arrival(k):
        dst = block(k, at.y, at.x)
        return remote(dst, dst, z_send.at[k - 1], z_recv.at[k - 1], at.at_z(at.behind(k)))

    def begin(j):
        for kind in (0, 1, 4):
            plane_copy(j, kind).start()

    def spread(j):
        plane_copy(j, 0).wait_recv()
        plane_copy(j, 2).start()
        plane_copy(j, 5).start()
        plane_copy(j, 1).wait_recv()
        plane_copy(j, 3).start()
        plane_copy(j, 6).start()

    def begin_later(j):
        z_arrival(j).wait_recv()
        begin(j)

    def last_hop(j):
        plane_copy(j, 2).wait_recv()
        plane_copy(j, 3).wait_recv()
        plane_copy(j, 7).start()

    def near_ready(j):
        plane_copy(j, 4).wait_recv()
        plane_copy(j, 5).wait_recv()

    def far_ready(j):
        plane_copy(j, 6).wait_recv()
        plane_copy(j, 7).wait_recv()

    def parity(step):
        return lax.rem(step, 2)

    def slot_of(turn):
        return lax.rem(turn + 1, depth)

    def other_y(step):
        return lax.rem(parity(step) + (step // 2 + 1) // depth, 2)

    def tile_at(step):
        return at.behind(slot_of(step // 2)), lax.rem(at.y + other_y(step), 2)

    def load_rows(step):
        z, y = tile_at(step)
        return pltpu.make_async_copy(rows_all.at[z, y], rows_tile, load_sem.at[0])

    def load_upstream(step):
        z, y = tile_at(step)
        return pltpu.make_async_copy(upstream_in.at[z, y], upstream_tile, load_sem.at[1])

    def stores(step):
        z, y = tile_at(step)
        pairs = ((weighted_tile, weighted_out), (d_pair_tile, d_pair_out))
        return [
            pltpu.make_async_copy(src, dst.at[z, y], store_sem.at[i])
            for i, (src, dst) in enumerate(pairs)
        ]

    tiles, cores = (d_rows_tile, out_tile), (d_rows_core, out_core)
    helds, sums = (d_rows_held, out_held), (d_rows_sum, out_sum)
    hops, hops2, zs = (d_rows_hop, out_hop), (d_rows_hop2, out_hop2), (d_rows_z, out_z)
    to_zs = (d_rows_to_z, out_to_z)

    def sum_copy(a, kind, src, dst, peer):
        return remote(src, dst, sum_send.at[a, kind], sum_recv.at[a, kind], peer)

    def core_sum(a):
        return sum_copy(a, 0, tiles[a].at[:, 1 - at.c], cores[a], at.next_core)

    def row_hop(turn, other):
        y = lax.rem(at.y + other, 2)
        src = d_rows_held.at[parity(turn), y, 1 - at.x]
        return remote(src, d_rows_hop.at[y], hop_send.at[other], hop_recv.at[other], at.next_x)

    def out_hop_sum(turn):
        return sum_copy(1, 1, out_held.at[parity(turn), 1 - at.y], out_hop, at.next_y)

    def hop2_sum(a, turn):
        slot = parity(turn)
        if a == 0:
            src, peer = helds[0].at[slot, 1 - at.y, at.x], at.next_y
        else:
            src, peer = helds[1].at[slot, at.y, 1 - at.x], at.next_x
        return sum_copy(a, 2, src, hops2[a], peer)

    def z_sum(a, turn):
        return remote(
            to_zs[a].at[turn],
            zs[a].at[turn],
            end_send.at[a, turn],
            end_recv.at[a, turn],
            at.at_z(at.behind(turn + 1)),
        )

    def allow(semaphore, peer):
        pl.semaphore_signal(semaphore, inc=1, device_id=peer, device_id_type=MESH)

    piece = 32

    def add(into, first, second):
        def body(i, carry):
            part = pl.ds(pl.multiple_of(i * piece, piece), piece)
            into[part] = first[part] + second[part]
            return carry

        lax.fori_loop(0, quarter // piece, body, 0)

    def after_core(step):
        turn = step // 2
        other = other_y(step)
        held, y = parity(turn), lax.rem(at.y + other, 2)

        @pl.when((parity(step) == 0) & (turn >= 1))
        def _():
            for a in (0, 1):
                pl.semaphore_wait(hop_credit.at[a], 1)

        for a in (0, 1):
            core_sum(a).wait()
            for x in (1 - at.x, at.x):
                add(helds[a].at[held, y, x], tiles[a].at[x, at.c], cores[a].at[x])
            if a == 0:
                row_hop(turn, other).start()
            else:

                @pl.when(other == 1)
                def _():
                    out_hop_sum(turn).start()

        @pl.when(step + 1 < 2 * depth)
        def _():
            allow(core_credit, at.next_core)

    def after_row_hop(turn, other):
        slot, y = parity(turn), lax.rem(at.y + other, 2)
        row_hop(turn, other).wait()
        into = d_rows_held.at[slot, y, at.x]
        add(into, into, d_rows_hop.at[y])

    def after_out_hop(turn):
        slot = parity(turn)
        out_hop_sum(turn).wait()
        for x in (1 - at.x, at.x):
            into = out_held.at[slot, at.y, x]
            add(into, into, out_hop.at[x])

    def may_hop2(turn, a):
        @pl.when(turn >= 1)
        def _():
            pl.semaphore_wait(hop2_credit.at[a], 1)

    def after_hop(turn):
        after_row_hop(turn, 1)
        may_hop2(turn, 0)
        hop2_sum(0, turn).start()
        after_row_hop(turn, 0)
        after_out_hop(turn)
        may_hop2(turn, 1)
        hop2_sum(1, turn).start()
        allow(hop_credit.at[0], at.next_x)
        allow(hop_credit.at[1], at.next_y)

    def after_hop2(turn):
        slot = parity(turn)
        for a in (0, 1):
            hop2_sum(a, turn).wait()
            add(to_zs[a].at[turn], helds[a].at[slot, at.y, at.x], hops2[a])
            z_sum(a, turn).start()
        allow(hop2_credit.at[0], at.next_y)
        allow(hop2_credit.at[1], at.next_x)

    load_upstream(0).start()
    at.greet()
    z_copy(1).start()
    own_copy = pltpu.make_async_copy(rows_in, block(0, at.y, at.x), own_sem)
    own_copy.start()
    own_copy.wait()
    begin(0)
    begin_later(1)
    for k in range(2, depth):
        z_copy(k).start()
    spread(0)
    spread(1)
    near_ready(1)
    load_rows(0).start()
    for copy in weight_copies():
        copy.wait()

    tile_rows = 4 * quarter
    hidden_total = down_w.shape[0]
    lane = lax.broadcasted_iota(jnp.int32, (tile_rows, 128), 1)
    slot_here, slot_hidden, shared_hidden = units
    routed = slot_here * slot_hidden
    across = (((1,), (1,)), ((), ()))
    few = 16

    def gate_factors(rows, picked):
        logits = jnp.dot(rows, side_w[...], preferred_element_type=f32)
        chooses = (lane >= 3) & (lane < 3 + expert_count)
        peak = jnp.max(jnp.where(chooses, logits, -1e30), axis=1, keepdims=True)
        expo = jnp.where(chooses, jnp.exp(jnp.where(chooses, logits, peak) - peak), 0.0)
        routed_gate = expo / jnp.sum(expo, axis=1, keepdims=True) * picked.astype(f32)
        mix_pre = jnp.sum(jnp.where(lane == 2, logits, 0.0), axis=1, keepdims=True)
        result = jnp.where(lane == slot_here, 1.0 / (1.0 + jnp.exp(-mix_pre)), 0.0)
        for s in range(slot_here):
            chosen = lane == 3 + at.ep * slot_here + s
            gate = jnp.sum(jnp.where(chosen, routed_gate, 0.0), axis=1, keepdims=True)
            result = jnp.where(lane == s, gate, result)
        return result

    few_lane = lax.broadcasted_iota(jnp.int32, (few, 128), 1)
    bounds = [s * slot_hidden for s in range(slot_here)] + [routed, hidden_total]

    def owners(group):
        found = []
        for s in range(slot_here + 1):
            low, high = max(bounds[s] - group * 128, 0), min(bounds[s + 1] - group * 128, 128)
            if low < high:
                found.append((s, low, high))
        return found

    def hidden_rows(i, carry):
        here = pl.ds(pl.multiple_of(i * few, few), few)
        gates = [
            jnp.broadcast_to(factors[here, s : s + 1], (few, 128)) for s in range(slot_here + 1)
        ]
        parts = [None] * (slot_here + 1)
        for group in range(hidden_total // 128):
            units_here = slice(group * 128, (group + 1) * 128)
            units_up = slice(hidden_total + group * 128, hidden_total + (group + 1) * 128)
            gate_pre, up_pre = pair_pre[here, units_here], pair_pre[here, units_up]
            d_h = d_hidden[here, units_here]
            found = owners(group)
            factor = gates[found[0][0]]
            for s, low, _ in found[1:]:
                factor = jnp.where(few_lane >= low, gates[s], factor)
            sig = 0.5 + 0.5 * jnp.tanh(0.5 * gate_pre)
            silu = gate_pre * sig
            hidden = silu * up_pre
            product = hidden * d_h
            gated = factor * d_h
            weighted_tile[here, units_here] = (factor * hidden).astype(bf16)
            slope = sig + silu * (1.0 - sig)
            d_pair_tile[here, units_here] = (gated * up_pre * slope).astype(bf16)
            d_pair_tile[here, units_up] = (gated * silu).astype(bf16)
            for s, low, high in found:
                mine = product
                if high < 128:
                    mine = jnp.where(few_lane < high, mine, 0.0)
                if low > 0:
                    mine = jnp.where(few_lane >= low, mine, 0.0)
                parts[s] = mine if parts[s] is None else parts[s] + mine
        result = jnp.zeros((few, 128), f32)
        for s in range(slot_here + 1):
            dot = jnp.sum(parts[s], axis=1, keepdims=True)
            where = few_lane == (2 if s == slot_here else 3 + at.ep * slot_here + s)
            result = jnp.where(where, dot, result)
        dots[here] = result.astype(bf16)
        return carry

    def first_half(step):
        load_upstream(step).wait()
        upstream = upstream_tile[...].reshape(tile_rows, upstream_tile.shape[-1])
        d_hidden[...] = lax.dot_general(
            upstream[:, :width], down_w[...], across, preferred_element_type=f32
        )
        load_rows(step).wait()
        rows = rows_tile[...].reshape(tile_rows, width)
        factors[...] = gate_factors(rows, upstream[:, width:])
        pair_pre[...] = lax.dot_general(rows, pair_w[...], across, preferred_element_type=f32)

        @pl.when(step + 1 < 2 * depth)
        def _():
            load_upstream(step + 1).start()

        @pl.when(step >= 1)
        def _():
            for copy in stores(step - 1):
                copy.wait()

        lax.fori_loop(0, tile_rows // few, hidden_rows, 0, unroll=2)
        for copy in stores(step):
            copy.start()
        turn = step // 2

        @pl.when(step == 0)
        def _():
            last_hop(0)

        @pl.when((parity(step) == 0) & (turn + 1 < depth))
        def _():
            last_hop(turn + 1)

        @pl.when((step >= 1) & (step + 1 < depth))
        def _():
            spread(step + 1)

        @pl.when(step + 2 < depth)
        def _():
            begin_later(step + 2)

    def second_half(step):
        blocks = (2, 2, quarter)
        some = width // 2
        for n in range(2):
            columns = slice(n * some, (n + 1) * some)
            part = jnp.dot(weighted_tile[...], down_w[:, columns], preferred_element_type=f32)
            out_tile[:, :, :, columns] = part.astype(bf16).reshape(blocks + (some,))
            part = jnp.dot(d_pair_tile[...], pair_w[:, columns], preferred_element_type=f32)
            d_rows_tile[:, :, :, columns] = part.astype(bf16).reshape(blocks + (some,))
        d_rows_tile[:, :, :, width:] = dots[...].reshape(blocks + (128,))

        @pl.when(step >= 1)
        def _():
            pl.semaphore_wait(core_credit, 1)

        for a in (0, 1):
            core_sum(a).start()
        turn = step // 2

        @pl.when((parity(step) == 0) & (turn + 1 < depth))
        def _():
            far_ready(slot_of(turn))

        @pl.when((parity(step) == 1) & (turn + 1 < depth))
        def _():
            near_ready(slot_of(turn + 1))

        @pl.when(step == 2 * depth - 3)
        def _():
            far_ready(slot_of(turn + 1))

        @pl.when(step + 1 < 2 * depth)
        def _():
            load_rows(step + 1).start()

    def step_body(step, carry):
        first_half(step)

        odd = parity(step) == 1

        @pl.when(odd & (step >= 3))
        def _():
            after_hop((step - 3) // 2)

        @pl.when(jnp.logical_not(odd) & (step >= 4))
        def _():
            after_hop2((step - 4) // 2)

        @pl.when(step >= 1)
        def _():
            after_core(step - 1)

        second_half(step)
        return carry

    lax.fori_loop(0, 2 * depth, step_body, 0)
    last = depth - 1
    after_hop2(last - 1)
    after_row_hop(last, 1)
    may_hop2(last, 0)
    hop2_sum(0, last).start()
    after_core(2 * depth - 1)
    after_out_hop(last)
    may_hop2(last, 1)
    hop2_sum(1, last).start()
    after_row_hop(last, 0)

    def total_of(a):
        hop2_sum(a, last).wait()
        held = helds[a].at[last % 2, at.y, at.x]
        for turn in range(last):
            z_sum(a, turn).wait_recv()

        def total_body(i, carry):
            part = pl.ds(pl.multiple_of(i * piece, piece), piece)
            total = held[part].astype(f32) + hops2[a][part].astype(f32)
            for k in range(last):
                total = total + zs[a][k, part].astype(f32)
            sums[a][part] = total
            return carry

        lax.fori_loop(0, quarter // piece, total_body, 0)

    total_of(0)
    own_lane = lax.broadcasted_iota(jnp.int32, (quarter, 128), 1)
    chooses = (own_lane >= 3) & (own_lane < 3 + expert_count)
    rows = own_rows[...]
    logits = jnp.dot(rows, side_w[...], preferred_element_type=f32)
    peak = jnp.max(jnp.where(chooses, logits, -1e30), axis=1, keepdims=True)
    expo = jnp.where(chooses, jnp.exp(jnp.where(chooses, logits, peak) - peak), 0.0)
    router = expo / jnp.sum(expo, axis=1, keepdims=True)
    mixer = 1.0 / (1.0 + jnp.exp(-jnp.where(own_lane == 2, logits, 0.0)))
    gate_dots = d_rows_sum[:, width:]
    d_router = jnp.where(chooses, gate_dots * own_upstream[:, width:].astype(f32), 0.0)
    d_logits = router * (d_router - jnp.sum(router * d_router, axis=1, keepdims=True))
    d_mix = gate_dots * mixer * (1.0 - mixer)
    d_side = jnp.where(own_lane == 2, d_mix, jnp.where(chooses, d_logits, 0.0))
    d_side_out[...] = d_side
    high = d_side.astype(bf16)
    lower = (d_side - high.astype(f32)).astype(bf16)
    for split in (high, lower):
        d_rows_sum[:, :width] += lax.dot_general(
            split, side_w[...], across, preferred_element_type=f32
        )

    def end_body(i, carry):
        part = pl.ds(pl.multiple_of(i * few, few), few)
        resid = resid_in[part]
        scale = lax.rsqrt(jnp.mean(resid * resid, axis=1, keepdims=True) + epsilon)
        unit_rows = resid * scale
        grads = d_rows_sum[part, :width]
        scaled = grads * gain_in[...]
        inner = jnp.mean(scaled * unit_rows, axis=1, keepdims=True)
        d_resid = own_upstream[part, :width].astype(f32) + scale * (scaled - unit_rows * inner)
        d_resid_out[part] = d_resid
        d_resid_low[part] = d_resid.astype(bf16)
        return carry + jnp.sum(grads * unit_rows, axis=0, keepdims=True)

    d_gain_out[...] = lax.fori_loop(0, quarter // few, end_body, jnp.zeros((1, width), f32))

    def gather_copy(kind):
        if kind == 2:
            src = dst = d_resid_low_out.at[1 - at.x, at.c]
        else:
            src, dst = d_resid_low, d_resid_low_out.at[at.x, at.c]
        peer = at.next_x if kind == 0 else at.next_core
        return remote(src, dst, gathered_send.at[kind], gathered_recv.at[kind], peer)

    own_end = pltpu.make_async_copy(d_resid_low, d_resid_low_out.at[at.x, at.c], own_sem)
    own_end.start()
    for kind in (0, 1):
        gather_copy(kind).start()
    total_of(1)
    block_out[...] = (resid_in[...] + out_sum[...]).astype(bf16)
    gather_copy(0).wait_recv()
    gather_copy(2).start()
    own_end.wait()
    gather_copy(0).wait_send()
    gather_copy(1).wait()
    gather_copy(2).wait()
    for copy in stores(2 * depth - 1):
        copy.wait()
    for a in (0, 1):
        for turn in range(depth - 1):
            z_sum(a, turn).wait_send()
    for k in range(1, depth):
        z_copy(k).wait_send()

    def finish(j, carry):
        for kind in range(8):
            plane_copy(j, kind).wait_send()
        return carry

    lax.fori_loop(0, depth, finish, 0)


def ffn_over_all(rows, upstream_all, pair_w, down_w, side_w, resid, gain, units, expert_count):
    quarter, width = rows.shape
    ep_count, tp_count = lax.axis_size("ep"), lax.axis_size("tp")
    depth = ep_count // 2
    hidden = down_w.shape[0]
    bf16, f32 = jnp.bfloat16, jnp.float32
    wide = width + 128
    tile_rows = tp_count * quarter
    tokens = ep_count * tile_rows
    anywhere = pl.BlockSpec(memory_space=pl.ANY)
    in_vmem = pl.BlockSpec(memory_space=pltpu.VMEM)

    def both(*lead):
        return [pltpu.VMEM(lead + (quarter, columns), bf16) for columns in (wide, width)]

    dma = pltpu.SemaphoreType.DMA
    outs = pl.pallas_call(
        functools.partial(ffn_kernel, units, expert_count),
        out_shape=(
            jax.ShapeDtypeStruct((depth, 2, 2, 2, quarter, width), bf16),
            jax.ShapeDtypeStruct((depth, 2, tile_rows, hidden), bf16),
            jax.ShapeDtypeStruct((depth, 2, tile_rows, 2 * hidden), bf16),
            jax.ShapeDtypeStruct((quarter, width), bf16),
            jax.ShapeDtypeStruct((2, 2, quarter, width), bf16),
            jax.ShapeDtypeStruct((quarter, width), f32),
            jax.ShapeDtypeStruct((1, width), f32),
            jax.ShapeDtypeStruct((quarter, 128), f32),
        ),
        in_specs=[anywhere] * 5 + [in_vmem] * 2,
        out_specs=(anywhere,) * 3 + (in_vmem, anywhere) + (in_vmem,) * 3,
        scratch_shapes=[
            pltpu.VMEM((quarter, wide), f32),
            pltpu.VMEM((quarter, width), f32),
            pltpu.VMEM((2 * hidden, width), bf16),
            pltpu.VMEM((hidden, width), bf16),
            pltpu.VMEM((width, 128), bf16),
            pltpu.VMEM((2, 2, quarter, width), bf16),
            pltpu.VMEM((2, 2, quarter, wide), bf16),
            pltpu.VMEM((tile_rows, 2 * hidden), f32),
            pltpu.VMEM((tile_rows, hidden), f32),
            pltpu.VMEM((tile_rows, 128), f32),
            pltpu.VMEM((tile_rows, 128), bf16),
            pltpu.VMEM((tile_rows, hidden), bf16),
            pltpu.VMEM((tile_rows, 2 * hidden), bf16),
            pltpu.VMEM((quarter, width), bf16),
            pltpu.VMEM((quarter, wide), bf16),
            pltpu.VMEM((quarter, width), bf16),
        ]
        + both(2, 2)
        + both(2)
        + both(2, 2, 2)
        + both(2)
        + both()
        + both(depth - 1)
        + both(depth - 1)
        + [
            dma((3,)),
            dma((3,)),
            dma((2,)),
            dma((2,)),
            dma((5,)),
            dma,
            dma((depth - 1,)),
            dma((depth - 1,)),
            dma((depth, 8)),
            dma((depth, 8)),
            dma((2,)),
            dma((2,)),
            dma((2, 3)),
            dma((2, 3)),
            dma((2, depth - 1)),
            dma((2, depth - 1)),
            pltpu.SemaphoreType.REGULAR,
            pltpu.SemaphoreType.REGULAR((2,)),
            pltpu.SemaphoreType.REGULAR((2,)),
        ],
        compiler_params=pltpu.CompilerParams(
            collective_id=1, has_side_effects=True, vmem_limit_bytes=62 * 2**20
        ),
        cost_estimate=pl.CostEstimate(
            flops=12 * tokens * width * hidden,
            bytes_accessed=10 * tokens * width,
            transcendentals=tokens * hidden,
        ),
        name="ffn_all_tokens",
    )(
        rows,
        upstream_all.reshape(depth, 2, 2, 2, quarter, wide),
        pair_w,
        down_w,
        side_w,
        resid,
        gain,
    )
    rows_all, weighted, d_pair, block_out, d_resid_low, d_resid, d_gain, d_side = outs
    return (
        rows_all.reshape(tokens, width),
        weighted.reshape(tokens, hidden),
        d_pair.reshape(tokens, 2 * hidden),
        block_out,
        d_resid_low.reshape(tile_rows, width),
        d_resid,
        d_gain[0],
        d_side,
    )


def over_tp(block, distance):
    devices = range(lax.axis_size("tp"))
    return lax.ppermute(block, "tp", [(i, i ^ distance) for i in devices])


def one_of(array, index, axis):
    return lax.dynamic_index_in_dim(array, index, axis, keepdims=False)


def sum_over_tp(part):
    rows, columns = part.shape
    tp = lax.axis_index("tp")
    x, c = tp // 2, tp % 2
    blocks = part.reshape(2, 2, rows // 4, columns)
    got = over_tp(one_of(blocks, 1 - c, 1).astype(jnp.bfloat16), 1)
    chip = one_of(blocks, c, 1).astype(jnp.float32) + got.astype(jnp.float32)
    got = over_tp(one_of(chip, 1 - x, 0).astype(jnp.bfloat16), 2)
    return one_of(chip, x, 0) + got.astype(jnp.float32)


def gather_over_tp(block):
    tp = lax.axis_index("tp")
    x, c = tp // 2, tp % 2
    got = over_tp(block, 2)
    pair = jnp.where(x == 0, jnp.stack([block, got]), jnp.stack([got, block]))
    got = over_tp(pair, 1)
    four = jnp.where(c == 0, jnp.stack([pair, got], axis=1), jnp.stack([got, pair], axis=1))
    return four.reshape(4 * block.shape[0], block.shape[1])


def swap_copies(at, pieces_in, pieces_out, send_sem, recv_sem, leave):
    count = 2 * at.depth
    copies = []
    for k in range(1, count):
        to, back = lax.rem(at.ep + k, count), lax.rem(at.ep + count - k, count)
        if leave:
            src, dst, peer = pieces_in.at[to], pieces_out.at[at.ep], to
        else:
            src, dst, peer = pieces_in.at[back], pieces_out.at[back], back
        copies.append(remote(src, dst, send_sem.at[k], recv_sem.at[k], (peer, at.tp)))
    return copies


def weights_kernel(
    own_in,
    pieces_in,
    all_out,
    pieces_out,
    own_sem,
    z_send,
    z_recv,
    y_send,
    y_recv,
    swap_send,
    swap_recv,
):
    at = Place()
    depth = at.depth
    half = own_in.shape[0] // 2
    last = depth - 1

    def block(k, y, h):
        return all_out.at[at.z + k, y, pl.ds(h * half, half)]

    def z_copy(k, h, direction):
        if k == 0:
            src = own_in.at[pl.ds(h * half, half)]
        else:
            src = block(k, at.y, h)
        slot = last + k - direction
        return remote(
            src,
            block(k, at.y, h),
            z_send.at[last + k, h, (direction + 1) // 2],
            z_recv.at[slot, h],
            at.at_z(at.z + direction),
        )

    def z_arrival(k, h):
        direction = 1 if k > 0 else -1
        dst = block(k, at.y, h)
        return remote(
            dst, dst, z_send.at[last + k, h, 0], z_recv.at[last + k, h], at.at_z(at.z + direction)
        )

    def y_copy(k, h):
        src = own_in.at[pl.ds(h * half, half)] if k == 0 else block(k, at.y, h)
        return remote(
            src, block(k, at.y, h), y_send.at[last + k, h], y_recv.at[last + k, h], at.next_y
        )

    own_copies = [
        pltpu.make_async_copy(own_in, all_out.at[at.z, at.y], own_sem.at[0]),
        pltpu.make_async_copy(pieces_in.at[at.ep], pieces_out.at[at.ep], own_sem.at[1]),
    ]
    for copy in own_copies:
        copy.start()
    has_up, has_down = at.z + 1 < depth, at.z > 0
    at.greet_ep()

    for h in (0, 1):
        pl.when(has_up)(lambda: z_copy(0, h, 1).start())
        pl.when(has_down)(lambda: z_copy(0, h, -1).start())
        y_copy(0, h).start()
    swap = (at, pieces_in, pieces_out, swap_send, swap_recv)
    for copy in swap_copies(*swap, True):
        copy.start()
    for k in range(1, depth):
        for h in (0, 1):
            for sign in (-1, 1):
                there = at.z + sign * k
                exists = (there >= 0) & (there < depth)
                onward = at.z - sign
                goes_on = exists & (onward >= 0) & (onward < depth)

                @pl.when(exists)
                def _():
                    z_arrival(sign * k, h).wait_recv()

                @pl.when(goes_on)
                def _():
                    z_copy(sign * k, h, -sign).start()

                @pl.when(exists)
                def _():
                    y_copy(sign * k, h).start()

    for copy in own_copies:
        copy.wait()
    for copy in swap_copies(*swap, False):
        copy.wait_recv()
    for copy in swap_copies(*swap, True):
        copy.wait_send()
    for h in (0, 1):
        pl.when(has_up)(lambda: z_copy(0, h, 1).wait_send())
        pl.when(has_down)(lambda: z_copy(0, h, -1).wait_send())
    for k in range(-last, depth):
        there = at.z + k
        exists = (there >= 0) & (there < depth)
        sign = 1 if k > 0 else -1
        onward = at.z - sign
        goes_on = exists & (onward >= 0) & (onward < depth)
        for h in (0, 1):

            @pl.when(exists)
            def _():
                y_copy(k, h).wait()

            if k != 0:

                @pl.when(goes_on)
                def _():
                    z_copy(k, h, -sign).wait_send()


def gather_over_ep(block, pieces):
    rows, columns = block.shape
    depth = lax.axis_size("ep") // 2
    anywhere = pl.BlockSpec(memory_space=pl.ANY)
    slots = 2 * depth - 1
    out, pieces = pl.pallas_call(
        weights_kernel,
        out_shape=(
            jax.ShapeDtypeStruct((depth, 2, rows, columns), block.dtype),
            jax.ShapeDtypeStruct(pieces.shape, pieces.dtype),
        ),
        in_specs=[anywhere] * 2,
        out_specs=(anywhere,) * 2,
        scratch_shapes=[
            pltpu.SemaphoreType.DMA((2,)),
            pltpu.SemaphoreType.DMA((slots, 2, 2)),
            pltpu.SemaphoreType.DMA((slots, 2)),
            pltpu.SemaphoreType.DMA((slots, 2)),
            pltpu.SemaphoreType.DMA((slots, 2)),
            pltpu.SemaphoreType.DMA((2 * depth,)),
            pltpu.SemaphoreType.DMA((2 * depth,)),
        ],
        compiler_params=pltpu.CompilerParams(collective_id=3, has_side_effects=True),
        cost_estimate=pl.CostEstimate(
            flops=0, bytes_accessed=8 * depth * rows * columns, transcendentals=0
        ),
        name="gather_weights",
    )(block, pieces)
    return out.reshape(2 * depth * rows, columns), pieces


def grads_kernel(
    routed,
    part_in,
    small_in,
    own_rows_in,
    rows_in,
    d_pair_in,
    upstream_in,
    weighted_in,
    out,
    small_out,
    rows_out,
    gate_out,
    up_out,
    down_out,
    own,
    hop,
    from_z,
    small_own,
    small_hop,
    small_z,
    small,
    small_got,
    rows_tile,
    d_pair_tile,
    upstream_tile,
    weighted_tile,
    turned,
    gate_total,
    up_total,
    down_total,
    load_sem,
    y_send,
    y_recv,
    z_send,
    z_recv,
    rows_send,
    rows_recv,
    small_send,
    small_recv,
    own_sem,
    tile_sem,
    store_sem,
    little_load,
    little_send,
    little_recv,
):
    at = Place()
    depth = at.depth
    rows, columns = out.shape
    half = rows // 2
    f32 = jnp.float32
    tiles = 2 * depth
    step = 16

    def part(h):
        return pl.ds(h * half, half)

    def load(j):
        return pltpu.make_async_copy(part_in.at[at.ahead(j), at.y], own.at[j], load_sem.at[j])

    def y_copy(j, h):
        return remote(
            part_in.at[at.ahead(j), 1 - at.y, part(h)],
            hop.at[j, part(h)],
            y_send.at[j, h],
            y_recv.at[j, h],
            at.next_y,
        )

    def z_copy(j, h):
        return remote(
            own.at[j, part(h)],
            from_z.at[j - 1, part(h)],
            z_send.at[j, h],
            z_recv.at[j, h],
            at.at_z(at.ahead(j)),
        )

    def little(j):
        return pltpu.make_async_copy(
            small_in.at[at.ahead(j), at.y], small_own.at[j], little_load.at[j]
        )

    def little_y(j):
        return remote(
            small_in.at[at.ahead(j), 1 - at.y],
            small_hop.at[j],
            little_send.at[0, j],
            little_recv.at[0, j],
            at.next_y,
        )

    def little_z(j):
        return remote(
            small_own.at[j],
            small_z.at[j - 1],
            little_send.at[1, j],
            little_recv.at[1, j],
            at.at_z(at.ahead(j)),
        )

    def rows_copy(kind):
        if kind == 0:
            src, dst, peer = own_rows_in, rows_out.at[at.x, at.c], at.next_x
        elif kind == 1:
            src, dst, peer = own_rows_in, rows_out.at[at.x, at.c], at.next_core
        else:
            src = dst = rows_out.at[1 - at.x, at.c]
            peer = at.next_core
        return remote(src, dst, rows_send.at[kind], rows_recv.at[kind], peer)

    def small_copy(kind):
        peer = at.next_core if kind == 0 else at.next_x
        return remote(
            small.at[kind], small_got.at[kind], small_send.at[kind], small_recv.at[kind], peer
        )

    def tile_loads(tile):
        slot = lax.rem(tile, 2)
        pairs = (
            (rows_in, rows_tile),
            (d_pair_in, d_pair_tile),
            (upstream_in, upstream_tile),
            (weighted_in, weighted_tile),
        )
        return [
            pltpu.make_async_copy(src.at[tile], dst.at[slot], tile_sem.at[i, slot])
            for i, (src, dst) in enumerate(pairs)
        ]

    order = [j for j in range(1, depth)] + [0]
    for copy in tile_loads(0):
        copy.start()
    for j in order:
        load(j).start()
        little(j).start()
    at.greet_row()
    for j in order:
        for h in (0, 1):
            y_copy(j, h).start()
        little_y(j).start()
    for kind in (0, 1):
        rows_copy(kind).start()
    own_copy = pltpu.make_async_copy(own_rows_in, rows_out.at[at.x, at.c], own_sem)
    own_copy.start()

    def after_y(j, moves_on):
        load(j).wait()
        for h in (0, 1):
            y_copy(j, h).wait_recv()

            def body(i, carry):
                some = pl.ds(pl.multiple_of(h * half + i * step, step), step)
                own[j, some] = own[j, some] + hop[j, some]
                return carry

            lax.fori_loop(0, half // step, body, 0)

            @pl.when(moves_on)
            def _():
                z_copy(j, h).start()

        little(j).wait()
        little_y(j).wait_recv()
        small_own[j] = small_own[j] + small_hop[j]

        @pl.when(moves_on)
        def _():
            little_z(j).start()

    width = gate_total.shape[1]
    hidden = weighted_tile.shape[2]
    some_columns = width // 4

    def tile_body(tile, carry):
        slot = lax.rem(tile, 2)
        for copy in tile_loads(tile):
            copy.wait()

        @pl.when(tile + 1 < tiles)
        def _():
            for copy in tile_loads(tile + 1):
                copy.start()

        for total, left, first, right in (
            (gate_total, d_pair_tile, 0, rows_tile),
            (up_total, d_pair_tile, hidden, rows_tile),
            (down_total, weighted_tile, 0, upstream_tile),
        ):
            turned[...] = left[slot, :, first : first + turned.shape[0]].T
            for n in range(4):
                these = slice(n * some_columns, (n + 1) * some_columns)
                product = jnp.dot(
                    turned[...], right[slot, :, these], preferred_element_type=f32
                )
                product = product[:routed]

                @pl.when(tile == 0)
                def _():
                    total[:, these] = product

                @pl.when(tile > 0)
                def _():
                    total[:, these] += product

        @pl.when(lax.rem(tile, 2) == 1)
        def _():
            after_y(lax.rem(tile // 2 + 1, depth), tile + 1 < tiles)

        @pl.when(tile == 1)
        def _():
            rows_copy(0).wait_recv()
            rows_copy(2).start()

        return carry

    lax.fori_loop(0, tiles, tile_body, 0)
    stores = [
        pltpu.make_async_copy(total, dst, store_sem.at[i])
        for i, (total, dst) in enumerate(
            ((gate_total, gate_out), (up_total, up_out), (down_total, down_out))
        )
    ]
    for copy in stores:
        copy.start()
    for h in (0, 1):
        for k in range(1, depth):
            z_copy(k, h).wait_recv()

        def body(i, carry):
            some = pl.ds(pl.multiple_of(h * half + i * step, step), step)
            total = own[0, some].astype(f32)
            for k in range(depth - 1):
                total = total + from_z[k, some].astype(f32)
            out[some] = total
            return carry

        lax.fori_loop(0, half // step, body, 0)
    total = small_own[0].astype(f32)
    for j in range(1, depth):
        little_z(j).wait_recv()
        total = total + small_z[j - 1].astype(f32)
    for kind in (0, 1):
        small[kind] = total
        small_copy(kind).start()
        small_copy(kind).wait()
        total = small[kind] + small_got[kind]
    small_out[...] = total
    for j in range(depth):
        for h in (0, 1):
            y_copy(j, h).wait_send()
            if j > 0:
                z_copy(j, h).wait_send()
        little_y(j).wait_send()
        if j > 0:
            little_z(j).wait_send()
    own_copy.wait()
    rows_copy(0).wait_send()
    for kind in (1, 2):
        rows_copy(kind).wait()
    for copy in stores:
        copy.wait()


def scatter_over_ep(parts, smalls, own_rows, tiles_of, routed):
    rows_all, d_pair, upstream_all, weighted = tiles_of
    depth = lax.axis_size("ep") // 2
    rows, columns = parts.shape[0] // (2 * depth), parts.shape[1]
    dtype = parts.dtype
    kinds, quarter, width = own_rows.shape
    tiles, tile, hidden = weighted.shape
    tokens = tiles * tile
    f32 = jnp.float32
    anywhere = pl.BlockSpec(memory_space=pl.ANY)
    in_vmem = pl.BlockSpec(memory_space=pltpu.VMEM)
    dma = pltpu.SemaphoreType.DMA
    total = jax.ShapeDtypeStruct((routed, width), f32)
    left = -(-routed // 128) * 128
    wide = upstream_all.shape[2]
    out, small, gathered, gate, up, down = pl.pallas_call(
        functools.partial(grads_kernel, routed),
        out_shape=(
            jax.ShapeDtypeStruct((rows, columns), f32),
            jax.ShapeDtypeStruct((rows, 128), f32),
            jax.ShapeDtypeStruct((2, 2, kinds, quarter, width), dtype),
            total,
            total,
            total,
        ),
        in_specs=[anywhere] * 7,
        out_specs=(in_vmem, in_vmem) + (anywhere,) * 4,
        scratch_shapes=[
            pltpu.VMEM((depth, rows, columns), dtype),
            pltpu.VMEM((depth, rows, columns), dtype),
            pltpu.VMEM((depth - 1, rows, columns), dtype),
            pltpu.VMEM((depth, rows, 128), dtype),
            pltpu.VMEM((depth, rows, 128), dtype),
            pltpu.VMEM((depth - 1, rows, 128), dtype),
            pltpu.VMEM((2, rows, 128), f32),
            pltpu.VMEM((2, rows, 128), f32),
            pltpu.VMEM((2, tile, width), dtype),
            pltpu.VMEM((2, tile, 2 * hidden), dtype),
            pltpu.VMEM((2, tile, wide), dtype),
            pltpu.VMEM((2, tile, hidden), dtype),
            pltpu.VMEM((left, tile), dtype),
            pltpu.VMEM((routed, width), f32),
            pltpu.VMEM((routed, width), f32),
            pltpu.VMEM((routed, width), f32),
            dma((depth,)),
            dma((depth, 2)),
            dma((depth, 2)),
            dma((depth, 2)),
            dma((depth, 2)),
            dma((3,)),
            dma((3,)),
            dma((2,)),
            dma((2,)),
            dma,
            dma((4, 2)),
            dma((3,)),
            dma((depth,)),
            dma((2, depth)),
            dma((2, depth)),
        ],
        compiler_params=pltpu.CompilerParams(
            collective_id=4, has_side_effects=True, vmem_limit_bytes=62 * 2**20
        ),
        cost_estimate=pl.CostEstimate(
            flops=6 * tokens * width * left, bytes_accessed=10 * tokens * width, transcendentals=0
        ),
        name="scatter_grads",
    )(
        parts.reshape(depth, 2, rows, columns),
        smalls.reshape(depth, 2, rows, 128),
        own_rows,
        rows_all,
        d_pair,
        upstream_all,
        weighted,
    )
    gathered = [gathered[:, :, i].reshape(4 * quarter, width) for i in range(kinds)]
    return out, small, gathered, (gate, up, down)


def attention_back_kernel(
    units,
    score_scale,
    d_low_in,
    weights_in,
    q_in,
    k_in,
    v_in,
    lse_in,
    query_seg,
    key_seg,
    query_at,
    key_at,
    cos_in,
    sin_in,
    turned_in,
    own_rows_in,
    gain_in,
    d_resid_in,
    rows_in,
    d_pair_in,
    upstream_in,
    weighted_in,
    part_out,
    pieces_got,
    d_rows_out,
    d_gain_out,
    pieces_out,
    d_low,
    out_w,
    qkv_w,
    q_all,
    k_all,
    v_all,
    d_att,
    probs,
    d_probs,
    d_out,
    d_got,
    d_own,
    d_proj,
    turned,
    part,
    core_got,
    x_got,
    rows_tile,
    gate_tile,
    up_tile,
    upstream_tile,
    weighted_tile,
    gate_total,
    up_total,
    down_total,
    block_tile,
    load_sem,
    d_send,
    d_recv,
    tp_send,
    tp_recv,
    tile_sem,
    store_sem,
    swap_send,
    swap_recv,
    own_sem,
):
    at = Place()
    count = 2 * at.depth
    heads, tokens, head = q_all.shape
    heads_width = heads * head
    windows = k_all.shape[1] // tokens
    quarter, width = d_rows_out.shape
    f32, bf16 = jnp.float32, jnp.bfloat16
    across = (((1,), (1,)), ((), ()))
    slot_here, slot_hidden, shared_hidden = units
    routed = slot_here * slot_hidden
    hidden = weighted_in.shape[2]
    lanes = gate_tile.shape[2]
    skipped = routed - (hidden - lanes)

    def loads():
        pairs = (
            (d_low_in, d_low),
            (weights_in.at[:, pl.ds(3 * heads_width, heads_width)], out_w),
            (q_in, q_all),
            (k_in, k_all),
            (v_in, v_all),
            (weights_in.at[:, pl.ds(0, 3 * heads_width)], qkv_w),
            (turned_in, turned),
        )
        return [pltpu.make_async_copy(src, dst, load_sem.at[i]) for i, (src, dst) in enumerate(pairs)]

    def tile_loads(tile):
        slot = lax.rem(tile, 2)
        pairs = (
            (rows_in.at[tile], rows_tile),
            (d_pair_in.at[tile, :, pl.ds(hidden - lanes, lanes)], gate_tile),
            (d_pair_in.at[tile, :, pl.ds(2 * hidden - lanes, lanes)], up_tile),
            (upstream_in.at[tile, :, pl.ds(0, width)], upstream_tile),
            (weighted_in.at[tile, :, pl.ds(hidden - lanes, lanes)], weighted_tile),
        )
        return [
            pltpu.make_async_copy(src, dst.at[slot], tile_sem.at[i, slot])
            for i, (src, dst) in enumerate(pairs)
        ]

    def d_copy(w, h):
        peer = (at.ep - (2 - w), at.tp)
        return remote(d_out.at[w, h], d_got.at[w, h], d_send.at[w, h], d_recv.at[w, h], peer)

    def d_arrival(w, h):
        peer = (at.ep + (2 - w), at.tp)
        dst = d_got.at[w, h]
        return remote(dst, dst, d_send.at[w, h], d_recv.at[w, h], peer)

    def core_copy():
        return remote(part.at[:, 1 - at.c], core_got, tp_send.at[0], tp_recv.at[0], at.next_core)

    def x_copy():
        return remote(
            part.at[1 - at.x, at.c], x_got, tp_send.at[1], tp_recv.at[1], at.next_x
        )

    copies = loads()
    for copy in copies:
        copy.start()
    for copy in tile_loads(0):
        copy.start()
    at.greet_row()
    copies[0].wait()
    copies[1].wait()
    d_attended = jnp.dot(d_low[...], out_w[...], preferred_element_type=f32).astype(bf16)
    for h in range(heads):
        d_att[h] = d_attended[:, h * head : (h + 1) * head]
    for copy in copies[2:5]:
        copy.wait()
    lane = lax.broadcasted_iota(jnp.int32, (tokens, head), 1)
    sign = jnp.where(lane < head // 2, -1.0, 1.0)

    def unrotated(grads):
        turned_part = pltpu.roll(grads * sin_in[...], head // 2, 1) * sign
        return grads * cos_in[...] - turned_part

    def head_body(h, carry):
        queries, d_a = q_all[h], d_att[h]
        delta = jnp.zeros((1, tokens), f32)
        for w in range(windows):
            some = slice(w * tokens, (w + 1) * tokens)
            scores = lax.dot_general(k_all[h, some], queries, across, preferred_element_type=f32)
            allowed = (key_seg[some] == query_seg[...]) & (key_at[some] <= query_at[...])
            p = jnp.where(allowed, jnp.exp(scores * score_scale - lse_in[h]), 0.0)
            d_p = lax.dot_general(v_all[h, some], d_a, across, preferred_element_type=f32)
            probs[w] = p
            d_probs[w] = d_p
            delta = delta + jnp.sum(p * d_p, axis=0, keepdims=True)
        d_queries = jnp.zeros((head, tokens), f32)
        for w in range(windows):
            some = slice(w * tokens, (w + 1) * tokens)
            p = probs[w]
            d_scores = (p * (d_probs[w] - delta)).astype(bf16)
            d_keys = jnp.dot(d_scores, queries, preferred_element_type=f32) * score_scale
            d_values = jnp.dot(p.astype(bf16), d_a, preferred_element_type=f32)
            if w < windows - 1:
                d_out[w, h, :, :head] = d_keys.astype(bf16)
                d_out[w, h, :, head:] = d_values.astype(bf16)

                @pl.when(at.ep >= 2 - w)
                def _():
                    d_copy(w, h).start()

            else:
                d_own[h, :, :head] = d_keys
                d_own[h, :, head:] = d_values
            d_queries = d_queries + jnp.dot(
                k_all[h, some].T, d_scores, preferred_element_type=f32
            )
        here = pl.ds(pl.multiple_of(h * head, head), head)
        d_proj[:, here] = unrotated((d_queries * score_scale).T).astype(bf16)
        return carry

    lax.fori_loop(0, heads, head_body, 0)

    def tile_body(tile, carry):
        slot = lax.rem(tile, 2)
        for copy in tile_loads(tile):
            copy.wait()

        @pl.when(tile + 1 < count)
        def _():
            for copy in tile_loads(tile + 1):
                copy.start()

        for total, left, right in (
            (gate_total, gate_tile, rows_tile),
            (up_total, up_tile, rows_tile),
            (down_total, weighted_tile, upstream_tile),
        ):
            product = jnp.dot(left[slot].T, right[slot], preferred_element_type=f32)

            @pl.when(tile == 0)
            def _():
                total[...] = product

            @pl.when(tile > 0)
            def _():
                total[...] += product

        return carry

    lax.fori_loop(0, count, tile_body, 0)
    columns = width // count
    for i, total in enumerate((gate_total, up_total, down_total)):
        for e in range(count):
            pieces_out[e, i * shared_hidden : (i + 1) * shared_hidden] = total[
                skipped : skipped + shared_hidden, e * columns : (e + 1) * columns
            ].astype(bf16)
    own_piece = pltpu.make_async_copy(pieces_out.at[at.ep], pieces_got.at[at.ep], own_sem)
    own_piece.start()
    swap = (at, pieces_out, pieces_got, swap_send, swap_recv)
    for copy in swap_copies(*swap, True):
        copy.start()

    def own_body(h, carry):
        for w in range(windows - 1):

            @pl.when(at.ep + (2 - w) < count)
            def _():
                d_arrival(w, h).wait_recv()
                d_own[h] += d_got[w, h].astype(f32)

        k_here = pl.ds(pl.multiple_of(heads_width + h * head, head), head)
        v_here = pl.ds(pl.multiple_of(2 * heads_width + h * head, head), head)
        d_proj[:, k_here] = unrotated(d_own[h, :, :head]).astype(bf16)
        d_proj[:, v_here] = d_own[h, :, head:].astype(bf16)
        return carry

    lax.fori_loop(0, heads, own_body, 0)
    copies[5].wait()
    copies[6].wait()
    for n in range(2):
        some = slice(n * (width // 2), (n + 1) * (width // 2))
        product = lax.dot_general(d_proj[...], qkv_w[some], across, preferred_element_type=f32)
        part[:, :, :, some] = product.astype(bf16).reshape(2, 2, quarter, width // 2)
    core_copy().start()
    rows = part_out.shape[0] // count

    def store(e):
        slot = lax.rem(e, 2)
        here = pl.ds(pl.multiple_of(e * rows, rows), rows)
        return pltpu.make_async_copy(block_tile.at[slot], part_out.at[here], store_sem.at[slot])

    def part_body(e, carry):
        @pl.when(e >= 2)
        def _():
            store(e - 2).wait()

        here = pl.ds(pl.multiple_of(e * rows, rows), rows)
        product = jnp.dot(turned[here], d_proj[...], preferred_element_type=f32)
        block_tile[lax.rem(e, 2)] = product.astype(bf16)
        store(e).start()
        return carry

    lax.fori_loop(0, count // 2, part_body, 0)
    core_copy().wait()
    for x in (0, 1):
        part[x, at.c] = part[x, at.c] + core_got[x]
    x_copy().start()
    lax.fori_loop(count // 2, count, part_body, 0)
    x_copy().wait()
    few = 16

    def end_body(i, carry):
        here = pl.ds(pl.multiple_of(i * few, few), few)
        grads = part[at.x, at.c, here].astype(f32) + x_got[here].astype(f32)
        inputs = own_rows_in[here].astype(f32)
        scale = lax.rsqrt(jnp.mean(inputs * inputs, axis=1, keepdims=True) + epsilon)
        unit_rows = inputs * scale
        scaled = grads * gain_in[...]
        inner = jnp.mean(scaled * unit_rows, axis=1, keepdims=True)
        d_rows = d_resid_in[here] + scale * (scaled - unit_rows * inner)
        d_rows_out[here] = d_rows.astype(bf16)
        return carry + jnp.sum(grads * unit_rows, axis=0, keepdims=True)

    d_gain_out[...] = lax.fori_loop(0, quarter // few, end_body, jnp.zeros((1, width), f32))
    for e in (count - 2, count - 1):
        store(e).wait()

    def finish(h, carry):
        for w in range(windows - 1):

            @pl.when(at.ep >= 2 - w)
            def _():
                d_copy(w, h).wait_send()

        return carry

    lax.fori_loop(0, heads, finish, 0)
    own_piece.wait()
    for copy in swap_copies(*swap, False):
        copy.wait_recv()
    for copy in swap_copies(*swap, True):
        copy.wait_send()


def attention_back(
    d_low, weights, queries, keys, values, lse, places, tables, turned, own, tiles_of, units, scale
):
    heads, tokens, head = queries.shape
    width = d_low.shape[1]
    ep_count = lax.axis_size("ep")
    quarter = own[0].shape[0]
    window = keys.shape[1]
    windows = window // tokens
    heads_width = heads * head
    hidden = tiles_of[3].shape[2]
    shared_hidden = units[2]
    lanes = -(-shared_hidden // 128) * 128
    f32, bf16 = jnp.float32, jnp.bfloat16
    anywhere = pl.BlockSpec(memory_space=pl.ANY)
    in_vmem = pl.BlockSpec(memory_space=pltpu.VMEM)
    dma = pltpu.SemaphoreType.DMA

    def vmem(*shape, dtype=bf16):
        return pltpu.VMEM(shape, dtype)

    return pl.pallas_call(
        functools.partial(attention_back_kernel, units, scale),
        out_shape=(
            jax.ShapeDtypeStruct((width, 3 * heads_width), bf16),
            jax.ShapeDtypeStruct((ep_count, 3 * shared_hidden, width // ep_count), bf16),
            jax.ShapeDtypeStruct((quarter, width), bf16),
            jax.ShapeDtypeStruct((1, width), f32),
        ),
        in_specs=[anywhere] * 5 + [in_vmem] * 7 + [anywhere] + [in_vmem] * 3 + [anywhere] * 4,
        out_specs=(anywhere, anywhere, in_vmem, in_vmem),
        scratch_shapes=[
            vmem(ep_count, 3 * shared_hidden, width // ep_count),
            vmem(tokens, width),
            vmem(width, heads_width),
            vmem(width, 3 * heads_width),
            vmem(heads, tokens, head),
            vmem(heads, window, head),
            vmem(heads, window, head),
            vmem(heads, tokens, head),
            vmem(windows, tokens, tokens, dtype=f32),
            vmem(windows, tokens, tokens, dtype=f32),
            vmem(windows - 1, heads, tokens, 2 * head),
            vmem(windows - 1, heads, tokens, 2 * head),
            vmem(heads, tokens, 2 * head, dtype=f32),
            vmem(tokens, 3 * heads_width),
            vmem(width, tokens),
            vmem(2, 2, quarter, width),
            vmem(2, quarter, width),
            vmem(quarter, width),
            vmem(2, tokens, width),
            vmem(2, tokens, lanes),
            vmem(2, tokens, lanes),
            vmem(2, tokens, width),
            vmem(2, tokens, lanes),
            vmem(lanes, width, dtype=f32),
            vmem(lanes, width, dtype=f32),
            vmem(lanes, width, dtype=f32),
            vmem(2, width // ep_count, 3 * heads_width),
            dma((7,)),
            dma((windows - 1, heads)),
            dma((windows - 1, heads)),
            dma((2,)),
            dma((2,)),
            dma((5, 2)),
            dma((2,)),
            dma((ep_count,)),
            dma((ep_count,)),
            dma,
        ],
        compiler_params=pltpu.CompilerParams(
            collective_id=5, has_side_effects=True, vmem_limit_bytes=62 * 2**20
        ),
        cost_estimate=pl.CostEstimate(
            flops=10 * heads * tokens * window * head + 20 * tokens * width * heads_width,
            bytes_accessed=2 * ep_count * tokens * width * 2,
            transcendentals=heads * tokens * window,
        ),
        name="attention_back",
    )(d_low, weights, queries, keys, values, lse, *places, *tables, turned, *own, *tiles_of)


def shared_pieces(weights, ep_count):
    rows, hidden = weights[0].shape
    units = hidden // ep_count
    return jnp.concatenate([weight.T.reshape(ep_count, units, rows) for weight in weights], axis=1)


def shared_units_of(pieces, count):
    ep_count, units, rows = pieces.shape
    return pieces.transpose(1, 0, 2).reshape(count, units // count, ep_count * rows)


def shared_whole(pieces, count):
    ep_count, units, columns = pieces.shape
    units = units // count
    pieces = pieces.reshape(ep_count, count, units, columns).astype(jnp.float32)
    return [pieces[:, i].reshape(ep_count * units, columns).T for i in range(count)]


def dense_body(
    tokens,
    lengths,
    routes,
    attn_gain,
    w_query,
    w_key,
    w_value,
    w_out,
    ffn_gain,
    w_router,
    shared_mix,
    shared_gate,
    shared_up,
    shared_down,
    expert_gate,
    expert_up,
    expert_down,
    cotangent,
):
    everywhere = ("ep", "tp")
    rows_here, width = tokens.shape
    ep_count = lax.axis_size("ep")
    tp_count = lax.axis_size("tp")
    ep_index = lax.axis_index("ep")
    offset = ep_index * rows_here
    quarter = rows_here // tp_count
    first_row = lax.axis_index("tp") * quarter
    slot_here, slot_hidden = expert_gate.shape[0], expert_gate.shape[1]
    expert_count = w_router.shape[1]
    bf16, f32 = jnp.bfloat16, jnp.float32

    def my_rows(array):
        return lax.dynamic_slice_in_dim(array, first_row, quarter, 0)

    side_columns = jnp.concatenate(
        [attn_gain[:, None], ffn_gain[:, None], shared_mix[:, None], w_router], axis=1
    )
    side_columns = jnp.pad(side_columns, ((0, 0), (0, -side_columns.shape[1] % 128)))
    joined_weights, pieces = gather_over_ep(
        jnp.concatenate([w_query, w_key, w_value, w_out, side_columns], axis=1),
        shared_pieces((shared_gate, shared_up, shared_down), ep_count),
    )
    cotangent_rows = my_rows(cotangent)
    joined_weights, cotangent_rows = lax.optimization_barrier((joined_weights, cotangent_rows))
    heads_width = w_query.shape[1]
    qkv_weight = joined_weights[:, : 3 * heads_width]
    output_weight = joined_weights[:, 3 * heads_width : 4 * heads_width]
    side_weight = joined_weights[:, 4 * heads_width :]
    picked = jnp.any(
        my_rows(routes)[:, :, None] == jnp.arange(expert_count, dtype=jnp.int32), axis=1
    )
    picked_lanes = jnp.pad(picked.astype(bf16), ((0, 0), (3, 125 - expert_count)))
    upstream_all = lax.all_gather(
        jnp.concatenate([cotangent_rows, picked_lanes], axis=1), everywhere, axis=0, tiled=True
    )
    shared_rows = shared_units_of(pieces, 3)
    shared_units = shared_rows.shape[1]
    routed_units = slot_here * slot_hidden
    gate_cat, up_cat, down_cat = [
        jnp.pad(
            jnp.concatenate([expert.reshape(-1, width), shared], axis=0),
            ((0, -(routed_units + shared_units) % 128), (0, 0)),
        )
        for expert, shared in zip((expert_gate, expert_up, expert_down), shared_rows)
    ]
    pair_cat = jnp.concatenate([gate_cat, up_cat], axis=0)
    hidden_total = gate_cat.shape[0]

    heads_here = heads_width // HD
    score_scale = HD ** (-0.5)
    first_norm_scale = side_weight[:, 0].astype(f32)
    second_norm_scale = side_weight[:, 1].astype(f32)
    mix_f = side_weight[:, 2].astype(f32)
    router_f = side_weight[:, 3 : 3 + expert_count].astype(f32)
    layer_input = tokens.astype(f32)
    normed_wide, norm_one = norm_forward(layer_input, first_norm_scale)
    normed_one = normed_wide.astype(bf16)
    query_at = offset + jnp.arange(rows_here, dtype=jnp.int32)
    key_at = offset - 2 * rows_here + jnp.arange(3 * rows_here, dtype=jnp.int32)
    query_seg, query_pos = sequence_info(lengths, query_at)
    key_seg, _ = sequence_info(lengths, key_at)
    cosine, sine = rope_tables(query_pos, HD)
    projected = jnp.dot(normed_one, qkv_weight, preferred_element_type=f32)
    projected = projected.reshape(rows_here, 3, heads_here, HD)
    queries = rotate(projected[:, 0], cosine, sine).astype(bf16)
    keys = rotate(projected[:, 1], cosine, sine).astype(bf16)
    values = projected[:, 2].astype(bf16)
    carried = jnp.stack([keys, values], axis=0)
    joined = jnp.concatenate(
        [passed_along(carried, "ep", 2), passed_along(carried, "ep", 1), carried], axis=1
    )
    keys_win = joined[0]
    values_win = joined[1]
    allowed = (
        (query_seg[:, None] == key_seg[None, :])
        & (key_at[None, :] <= query_at[:, None])
        & (key_at[None, :] >= 0)
    )
    scores = (
        jnp.einsum("qhd,khd->hqk", queries, keys_win, preferred_element_type=f32) * score_scale
    )
    masked = jnp.where(allowed[None], scores, -1e30)
    peak = jnp.max(masked, axis=-1, keepdims=True)
    expo = jnp.exp(masked - peak)
    total = jnp.sum(expo, axis=-1, keepdims=True)
    log_total = peak + jnp.log(total)
    weights = expo / total
    attended = jnp.einsum(
        "hqk,khd->qhd", weights.astype(bf16), values_win, preferred_element_type=f32
    )
    attended = attended.reshape(rows_here, heads_width).astype(bf16)
    attn_part = jnp.einsum("th,dh->td", attended, output_weight, preferred_element_type=f32)
    resid = my_rows(layer_input) + sum_over_tp(attn_part)
    normed_two_wide, norm_two = norm_forward(resid, second_norm_scale)
    normed_two = normed_two_wide.astype(bf16)

    (
        normed_all,
        weighted_h,
        d_pair_pre,
        block_rows,
        d_resid_low,
        d_resid,
        grad_gain_two,
        d_side,
    ) = ffn_over_all(
        normed_two,
        upstream_all,
        pair_cat,
        down_cat,
        side_weight,
        resid,
        second_norm_scale[None, :],
        (slot_here, slot_hidden, shared_units),
        expert_count,
    )
    grad_side = jnp.dot(normed_two.astype(f32).T, d_side, precision=highest)
    grad_out = jnp.einsum("td,th->dh", d_resid_low, attended, preferred_element_type=f32)
    grad_out = lax.psum_scatter(
        grad_out.astype(bf16), "ep", scatter_dimension=0, tiled=True
    ).astype(f32)
    def by_head(array):
        return array.transpose(1, 0, 2)

    place_in_row = (query_seg[None, :], jnp.where(key_at >= 0, key_seg, -1)[:, None])
    places = place_in_row + (query_at[None, :], key_at[:, None])
    tile_shape = (ep_count, rows_here, -1)
    tiles_of = tuple(
        array.reshape(tile_shape) for array in (normed_all, d_pair_pre, upstream_all, weighted_h)
    )
    units = (slot_here, slot_hidden, shared_units)
    grad_qkv, grad_pieces, d_rows, grad_gain_one = attention_back(
        d_resid_low,
        joined_weights,
        by_head(queries),
        by_head(keys_win),
        by_head(values_win),
        log_total.reshape(heads_here, 1, rows_here),
        places,
        (cosine[:, 0], sine[:, 0]),
        normed_one.T,
        (my_rows(tokens), first_norm_scale[None, :], d_resid),
        tiles_of,
        units,
        score_scale,
    )
    gains = jnp.stack([grad_gain_one[0], grad_gain_two], axis=1)
    small = jnp.concatenate([gains, grad_side[:, 2:]], axis=1).astype(bf16)
    grad_shared = shared_whole(grad_pieces, 3)
    grad_weights, small, gathered_rows, grad_experts = scatter_over_ep(
        grad_qkv, small, jnp.stack([d_rows, block_rows]), tiles_of, routed_units
    )
    grad_tokens, block_out = gathered_rows
    grad_tokens = grad_tokens.astype(f32)
    grad_experts = [grad.reshape(expert_gate.shape) for grad in grad_experts]
    parts = [grad_weights[:, i * heads_width : (i + 1) * heads_width] for i in range(3)]
    return (
        block_out,
        grad_tokens,
        small[:, 0],
        parts[0],
        parts[1],
        parts[2],
        grad_out,
        small[:, 1],
        small[:, 3 : 3 + expert_count],
        small[:, 2],
        grad_shared[0],
        grad_shared[1],
        grad_shared[2],
        grad_experts[0],
        grad_experts[1],
        grad_experts[2],
    )


def chosen_body(*arrays):
    rows_here, top_count = arrays[2].shape
    slot_here, expert_count = arrays[14].shape[0], arrays[9].shape[1]
    capacity = rows_here * top_count * 7 // (5 * expert_count)
    grid_of_two = lax.axis_size("ep") % 2 == 0 and lax.axis_size("tp") == 4
    if grid_of_two and rows_here < 2 * slot_here * capacity:
        return dense_body(*arrays)
    return body(*arrays)


def solution(mesh):
    placed = (
        P("ep", None),
        P(),
        P("ep", None),
        P("ep"),
        P("ep", "tp"),
        P("ep", "tp"),
        P("ep", "tp"),
        P("ep", "tp"),
        P("ep"),
        P("ep", None),
        P("ep"),
        P("ep", "tp"),
        P("ep", "tp"),
        P("ep", "tp"),
        P("ep", "tp", None),
        P("ep", "tp", None),
        P("ep", "tp", None),
        P("ep", None),
    )
    return jax.shard_map(
        chosen_body,
        mesh=mesh,
        in_specs=placed,
        out_specs=(
            P("ep", None),
            P("ep", None),
            P("ep"),
            P("ep", "tp"),
            P("ep", "tp"),
            P("ep", "tp"),
            P("ep", "tp"),
            P("ep"),
            P("ep", None),
            P("ep"),
            P("ep", "tp"),
            P("ep", "tp"),
            P("ep", "tp"),
            P("ep", "tp", None),
            P("ep", "tp", None),
            P("ep", "tp", None),
        ),
        check_vma=False,
    )
```

```python
import functools

import jax
import jax.numpy as jnp
from jax import lax
from jax.experimental import pallas as pl
from jax.experimental.pallas import tpu as pltpu
from jax.sharding import PartitionSpec as P

HD = 128


epsilon = 1e-06
rope_base = 1000000.0
highest = lax.Precision.HIGHEST
MESH = pl.DeviceIdType.MESH


def passed_along(block, axis, distance):
    devices = range(lax.axis_size(axis))
    route = [(i - distance, i) for i in devices if i - distance in devices]
    return lax.ppermute(block, axis, route)


def rope_tables(positions, width):
    steps = jnp.arange(0, width, 2, dtype=jnp.float32) / width
    inverse = rope_base ** (-steps)
    angles = positions.astype(jnp.float32)[:, None] * inverse[None, :]
    angles = jnp.concatenate([angles, angles], axis=-1)
    return (jnp.cos(angles)[:, None, :], jnp.sin(angles)[:, None, :])


def turn_half(values):
    middle = values.shape[-1] // 2
    return jnp.concatenate([-values[..., middle:], values[..., :middle]], axis=-1)


def rotate(values, cosine, sine):
    return values * cosine + turn_half(values) * sine


def unrotate(grads, cosine, sine):
    return grads * cosine - turn_half(grads * sine)


def sequence_info(lengths, indices):
    starts = jnp.cumsum(lengths) - lengths
    inside = starts[None, :] <= indices[:, None]
    segment = jnp.sum(inside.astype(jnp.int32), axis=1) - 1
    first = jnp.max(jnp.where(inside, starts[None, :], -1), axis=1)
    return (segment, indices - first)


def norm_forward(values, gain):
    scale = lax.rsqrt(jnp.mean(values * values, axis=-1, keepdims=True) + epsilon)
    return (values * scale * gain, scale)


def norm_backward(values, scale, gain, grads):
    unit = values * scale
    scaled = grads * gain
    inner = jnp.mean(scaled * unit, axis=-1, keepdims=True)
    return (scale * (scaled - unit * inner), jnp.sum(grads * unit, axis=0))


def deliver(rows):
    arrived_rows = lax.all_to_all(rows, "ep", split_axis=0, concat_axis=0, tiled=True)
    return arrived_rows


def bring_back(parts, target, rows_here, top_count):
    moved = lax.all_to_all(parts, "ep", split_axis=0, concat_axis=0, tiled=True)
    piece = moved.shape[3]
    return moved.reshape(-1, piece)[target].reshape(rows_here, top_count, piece)


def body(
    tokens,
    lengths,
    routes,
    attn_gain,
    w_query,
    w_key,
    w_value,
    w_out,
    ffn_gain,
    w_router,
    shared_mix,
    shared_gate,
    shared_up,
    shared_down,
    expert_gate,
    expert_up,
    expert_down,
    cotangent,
):
    rows_here = tokens.shape[0]
    width = tokens.shape[1]
    ep_count = lax.axis_size("ep")
    offset = lax.axis_index("ep") * rows_here
    slot_here = expert_gate.shape[0]
    top_count = routes.shape[1]
    gathered = (
        lax.all_gather(attn_gain, "ep", axis=0, tiled=True),
        lax.all_gather(w_query, "ep", axis=0, tiled=True),
        lax.all_gather(w_key, "ep", axis=0, tiled=True),
        lax.all_gather(w_value, "ep", axis=0, tiled=True),
        lax.all_gather(w_out, "ep", axis=0, tiled=True),
        lax.all_gather(ffn_gain, "ep", axis=0, tiled=True),
        lax.all_gather(w_router, "ep", axis=0, tiled=True),
        lax.all_gather(shared_mix, "ep", axis=0, tiled=True),
        lax.all_gather(shared_gate, "ep", axis=0, tiled=True),
        lax.all_gather(shared_up, "ep", axis=0, tiled=True),
        lax.all_gather(shared_down, "ep", axis=0, tiled=True),
    )
    (
        gain_first,
        query_weight_matrix,
        key_weight_matrix,
        value_weight_matrix,
        output_weight,
        gain_second,
        router_weight,
        shared_mixer_weight,
        shared_gate_weight,
        shared_up_weight,
        shared_down_weight,
    ) = gathered
    expert_count = router_weight.shape[1]
    capacity = (rows_here * top_count * 7 // (5 * expert_count) + 7) // 8 * 8
    heads_here = query_weight_matrix.shape[1] // HD
    score_scale = HD ** (-0.5)
    first_norm_scale = gain_first.astype(jnp.float32)
    second_norm_scale = gain_second.astype(jnp.float32)
    layer_input = tokens.astype(jnp.float32)
    normed_wide, norm_one = norm_forward(layer_input, first_norm_scale)
    normed_one = normed_wide.astype(jnp.bfloat16)
    query_at = offset + jnp.arange(rows_here, dtype=jnp.int32)
    key_at = offset - 2 * rows_here + jnp.arange(3 * rows_here, dtype=jnp.int32)
    query_seg, query_pos = sequence_info(lengths, query_at)
    key_seg, _ = sequence_info(lengths, key_at)
    cosine, sine = rope_tables(query_pos, HD)
    query_pre = jnp.dot(
        normed_one, query_weight_matrix, preferred_element_type=jnp.float32
    ).reshape(rows_here, heads_here, HD)
    key_pre = jnp.dot(normed_one, key_weight_matrix, preferred_element_type=jnp.float32).reshape(
        rows_here, heads_here, HD
    )
    queries = rotate(query_pre, cosine, sine).astype(jnp.bfloat16)
    keys = rotate(key_pre, cosine, sine).astype(jnp.bfloat16)
    values = (
        jnp.dot(normed_one, value_weight_matrix, preferred_element_type=jnp.float32)
        .astype(jnp.bfloat16)
        .reshape(rows_here, heads_here, HD)
    )
    carried = jnp.stack([keys, values], axis=0)
    window = [carried]
    for hop in range(2):
        carried = passed_along(carried, "ep", 1)
        window = [carried] + window
    joined = jnp.concatenate(window, axis=1)
    keys_win = joined[0]
    values_win = joined[1]
    allowed = (
        (query_seg[:, None] == key_seg[None, :])
        & (key_at[None, :] <= query_at[:, None])
        & (key_at[None, :] >= 0)
    )
    scores = (
        jnp.einsum("qhd,khd->hqk", queries, keys_win, preferred_element_type=jnp.float32)
        * score_scale
    )
    masked = jnp.where(allowed[None], scores, -1e30)
    peak = jnp.max(masked, axis=-1, keepdims=True)
    expo = jnp.exp(masked - peak)
    total = jnp.sum(expo, axis=-1, keepdims=True)
    log_total = peak + jnp.log(total)
    weights = expo / total
    attended = jnp.einsum(
        "hqk,khd->qhd", weights.astype(jnp.bfloat16), values_win, preferred_element_type=jnp.float32
    )
    attended = attended.reshape(rows_here, heads_here * HD).astype(jnp.bfloat16)
    attn_part = jnp.einsum("th,dh->td", attended, output_weight, preferred_element_type=jnp.float32)
    resid = layer_input + lax.psum(attn_part, "tp")
    normed_two_wide, norm_two = norm_forward(resid, second_norm_scale)
    normed_two = normed_two_wide.astype(jnp.bfloat16)
    normed_two_f = normed_two.astype(jnp.float32)
    router_f = router_weight.astype(jnp.float32)
    mix_f = shared_mixer_weight.astype(jnp.float32)
    router = jax.nn.softmax(jnp.dot(normed_two_f, router_f, precision=highest), axis=-1)
    picked = routes[:, :, None] == jnp.arange(expert_count, dtype=jnp.int32)[None, None, :]
    gates = jnp.sum(jnp.where(picked, router[:, None, :], 0.0), axis=-1)
    mixer = jax.nn.sigmoid(jnp.dot(normed_two_f, mix_f, precision=highest))
    shared_g = jnp.dot(normed_two, shared_gate_weight, preferred_element_type=jnp.float32)
    shared_u = jnp.dot(normed_two, shared_up_weight, preferred_element_type=jnp.float32)
    shared_h = (jax.nn.silu(shared_g) * shared_u).astype(jnp.bfloat16)
    shared_part = jnp.einsum(
        "tf,df->td", shared_h, shared_down_weight, preferred_element_type=jnp.float32
    )
    flat = routes.reshape(-1)
    hot = (flat[:, None] == jnp.arange(expert_count, dtype=jnp.int32)[None, :]).astype(jnp.int32)
    rank = jnp.sum(jnp.cumsum(hot, axis=0) * hot, axis=1) - 1
    target = flat * capacity + rank
    slot_total = ep_count * slot_here * capacity
    owner_route = (
        jnp.zeros((slot_total,), jnp.int32)
        .at[target]
        .set(jnp.arange(rows_here * top_count, dtype=jnp.int32))
    )
    filled = jnp.zeros((slot_total,), jnp.bool_).at[target].set(True)
    owner_token = owner_route // top_count
    send_rows = jnp.where(filled[:, None], normed_two[owner_token], jnp.zeros((), jnp.bfloat16))
    arrived_rows = deliver(send_rows.reshape(ep_count, slot_here, capacity, width))
    route_g = jnp.einsum(
        "nscd,sfd->nscf", arrived_rows, expert_gate, preferred_element_type=jnp.float32
    )
    route_u = jnp.einsum(
        "nscd,sfd->nscf", arrived_rows, expert_up, preferred_element_type=jnp.float32
    )
    route_h = (jax.nn.silu(route_g) * route_u).astype(jnp.bfloat16)
    route_part = jnp.einsum(
        "nscf,sfd->nscd", route_h, expert_down, preferred_element_type=jnp.float32
    )
    back_rows = bring_back(route_part, target, rows_here, top_count)
    upstream = cotangent.astype(jnp.float32)
    routed = jnp.sum(back_rows * gates[:, :, None], axis=1)
    ffn_part = mixer[:, None] * shared_part + routed
    route_dot = jnp.sum(back_rows * upstream[:, None, :], axis=-1)
    shared_dot = jnp.sum(shared_part * upstream, axis=-1)
    ffn_total, d_gate, d_mixer = lax.psum((ffn_part, route_dot, shared_dot), "tp")
    block_out = (resid + ffn_total).astype(jnp.bfloat16)
    d_router = jnp.sum(jnp.where(picked, d_gate[:, :, None], 0.0), axis=1)
    d_logits = router * (d_router - jnp.sum(router * d_router, axis=-1, keepdims=True))
    d_mixlogit = d_mixer * mixer * (1.0 - mixer)
    side = jnp.dot(d_logits, router_f.T, precision=highest) + d_mixlogit[:, None] * mix_f[None, :]
    grad_router = jnp.dot(normed_two_f.T, d_logits, precision=highest)
    grad_mix = jnp.dot(d_mixlogit, normed_two_f, precision=highest)
    d_shared = (mixer[:, None] * upstream).astype(jnp.bfloat16)
    d_sh = jnp.dot(d_shared, shared_down_weight, preferred_element_type=jnp.float32)
    sig_shared = jax.nn.sigmoid(shared_g)
    d_sg = (d_sh * shared_u * sig_shared * (1.0 + shared_g * (1.0 - sig_shared))).astype(
        jnp.bfloat16
    )
    d_su = (d_sh * shared_g * sig_shared).astype(jnp.bfloat16)
    d_normed_part = jnp.einsum(
        "tf,df->td", d_sg, shared_gate_weight, preferred_element_type=jnp.float32
    )
    d_normed_part = d_normed_part + jnp.einsum(
        "tf,df->td", d_su, shared_up_weight, preferred_element_type=jnp.float32
    )
    grad_sgate = jnp.einsum("td,tf->df", normed_two, d_sg, preferred_element_type=jnp.float32)
    grad_sup = jnp.einsum("td,tf->df", normed_two, d_su, preferred_element_type=jnp.float32)
    grad_sdown = jnp.einsum("td,tf->df", d_shared, shared_h, preferred_element_type=jnp.float32)
    d_route = (
        (gates[:, :, None] * upstream[:, None, :])
        .astype(jnp.bfloat16)
        .reshape(rows_here * top_count, width)
    )
    send_grads = jnp.where(filled[:, None], d_route[owner_route], jnp.zeros((), jnp.bfloat16))
    received_grads = deliver(send_grads.reshape(ep_count, slot_here, capacity, width))
    d_rh = jnp.einsum(
        "nscd,sfd->nscf", received_grads, expert_down, preferred_element_type=jnp.float32
    )
    sig_route = jax.nn.sigmoid(route_g)
    d_rg = (d_rh * route_u * sig_route * (1.0 + route_g * (1.0 - sig_route))).astype(jnp.bfloat16)
    routed_up_gradient = (d_rh * route_g * sig_route).astype(jnp.bfloat16)
    row_grads = jnp.einsum("nscf,sfd->nscd", d_rg, expert_gate, preferred_element_type=jnp.float32)
    row_grads = row_grads + jnp.einsum(
        "nscf,sfd->nscd", routed_up_gradient, expert_up, preferred_element_type=jnp.float32
    )
    grad_egate = jnp.einsum(
        "qxba,qxbr->xar", d_rg, arrived_rows, preferred_element_type=jnp.float32
    )
    expert_up_gradient = jnp.einsum(
        "qxba,qxbr->xar", routed_up_gradient, arrived_rows, preferred_element_type=jnp.float32
    )
    grad_edown = jnp.einsum(
        "qxba,qxbr->xar", route_h, received_grads, preferred_element_type=jnp.float32
    )
    grads_back = bring_back(row_grads, target, rows_here, top_count)
    d_routed = jnp.sum(grads_back, axis=1)
    d_normed_two = lax.psum(d_normed_part + d_routed, "tp") + side
    d_resid_norm, grad_gain_two = norm_backward(resid, norm_two, second_norm_scale, d_normed_two)
    d_resid = upstream + d_resid_norm
    d_resid_low = d_resid.astype(jnp.bfloat16)
    grad_outw = jnp.einsum("td,th->dh", d_resid_low, attended, preferred_element_type=jnp.float32)
    d_attended = jnp.einsum(
        "td,dh->th", d_resid_low, output_weight, preferred_element_type=jnp.float32
    )
    d_attended = d_attended.astype(jnp.bfloat16).reshape(rows_here, heads_here, HD)
    scores_again = (
        jnp.einsum("qhd,khd->hqk", queries, keys_win, preferred_element_type=jnp.float32)
        * score_scale
    )
    probs = jnp.where(allowed[None], jnp.exp(scores_again - log_total), 0.0)
    d_probs = jnp.einsum("qhd,khd->hqk", d_attended, values_win, preferred_element_type=jnp.float32)
    delta = jnp.sum(probs * d_probs, axis=-1, keepdims=True)
    d_scores = (probs * (d_probs - delta)).astype(jnp.bfloat16)
    d_queries = (
        jnp.einsum("hqk,khd->qhd", d_scores, keys_win, preferred_element_type=jnp.float32)
        * score_scale
    )
    d_keys_win = (
        jnp.einsum("hqk,qhd->khd", d_scores, queries, preferred_element_type=jnp.float32)
        * score_scale
    )
    d_values_win = jnp.einsum(
        "hqk,qhd->khd", probs.astype(jnp.bfloat16), d_attended, preferred_element_type=jnp.float32
    )
    pair_grads = jnp.stack([d_keys_win, d_values_win], axis=0)
    older = pair_grads[:, :rows_here]
    later = [pair_grads[:, rows_here : 2 * rows_here], pair_grads[:, 2 * rows_here :]]
    running = older
    for hop in range(2):
        running = passed_along(running, "ep", -1)
        running = running + later[hop]
    d_query_pre = (
        unrotate(d_queries, cosine, sine).astype(jnp.bfloat16).reshape(rows_here, heads_here * HD)
    )
    d_key_pre = (
        unrotate(running[0], cosine, sine).astype(jnp.bfloat16).reshape(rows_here, heads_here * HD)
    )
    d_values = running[1].astype(jnp.bfloat16).reshape(rows_here, heads_here * HD)
    grad_queryw = jnp.einsum(
        "td,th->dh", normed_one, d_query_pre, preferred_element_type=jnp.float32
    )
    grad_keyw = jnp.einsum("td,th->dh", normed_one, d_key_pre, preferred_element_type=jnp.float32)
    grad_valuew = jnp.einsum("td,th->dh", normed_one, d_values, preferred_element_type=jnp.float32)
    d_normed_one = jnp.einsum(
        "th,dh->td", d_query_pre, query_weight_matrix, preferred_element_type=jnp.float32
    )
    d_normed_one = d_normed_one + jnp.einsum(
        "th,dh->td", d_key_pre, key_weight_matrix, preferred_element_type=jnp.float32
    )
    d_normed_one = d_normed_one + jnp.einsum(
        "th,dh->td", d_values, value_weight_matrix, preferred_element_type=jnp.float32
    )
    d_normed_one = lax.psum(d_normed_one, "tp")
    d_input_norm, grad_gain_one = norm_backward(
        layer_input, norm_one, first_norm_scale, d_normed_one
    )
    grad_tokens = d_resid + d_input_norm
    summed = (
        lax.psum_scatter(grad_gain_one, "ep", scatter_dimension=0, tiled=True),
        lax.psum_scatter(grad_queryw, "ep", scatter_dimension=0, tiled=True),
        lax.psum_scatter(grad_keyw, "ep", scatter_dimension=0, tiled=True),
        lax.psum_scatter(grad_valuew, "ep", scatter_dimension=0, tiled=True),
        lax.psum_scatter(grad_outw, "ep", scatter_dimension=0, tiled=True),
        lax.psum_scatter(grad_gain_two, "ep", scatter_dimension=0, tiled=True),
        lax.psum_scatter(grad_router, "ep", scatter_dimension=0, tiled=True),
        lax.psum_scatter(grad_mix, "ep", scatter_dimension=0, tiled=True),
        lax.psum_scatter(grad_sgate, "ep", scatter_dimension=0, tiled=True),
        lax.psum_scatter(grad_sup, "ep", scatter_dimension=0, tiled=True),
        lax.psum_scatter(grad_sdown, "ep", scatter_dimension=0, tiled=True),
    )
    return (
        block_out,
        grad_tokens,
        summed[0],
        summed[1],
        summed[2],
        summed[3],
        summed[4],
        summed[5],
        summed[6],
        summed[7],
        summed[8],
        summed[9],
        summed[10],
        grad_egate,
        expert_up_gradient,
        grad_edown,
    )


class Place:
    def __init__(self):
        self.ep, self.tp = lax.axis_index("ep"), lax.axis_index("tp")
        self.z, self.y = self.ep // 2, self.ep % 2
        self.x, self.c = self.tp // 2, self.tp % 2
        self.depth = lax.axis_size("ep") // 2
        self.next_core = (self.ep, self.x * 2 + 1 - self.c)
        self.next_x = (self.ep, (1 - self.x) * 2 + self.c)
        self.next_y = (self.z * 2 + 1 - self.y, self.tp)

    def at_z(self, z):
        return (z * 2 + self.y, self.tp)

    def ahead(self, steps):
        return lax.rem(self.z + steps, self.depth)

    def behind(self, steps):
        return lax.rem(self.z + self.depth - steps, self.depth)

    def greet(self):
        barrier = pltpu.get_barrier_semaphore()
        peers = [self.next_core, self.next_x, self.next_y]
        peers += [self.at_z(self.ahead(k)) for k in range(1, self.depth)]
        for peer in peers:
            pl.semaphore_signal(barrier, inc=1, device_id=peer, device_id_type=MESH)
        pl.semaphore_wait(barrier, len(peers))

    def greet_row(self):
        barrier = pltpu.get_barrier_semaphore()
        count = 2 * self.depth
        peers = [(lax.rem(self.ep + k, count), self.tp) for k in range(1, count)]
        peers += [self.next_core, self.next_x]
        for peer in peers:
            pl.semaphore_signal(barrier, inc=1, device_id=peer, device_id_type=MESH)
        pl.semaphore_wait(barrier, len(peers))

    def greet_ep(self):
        barrier = pltpu.get_barrier_semaphore()
        count = 2 * self.depth
        for k in range(1, count):
            peer = (lax.rem(self.ep + k, count), self.tp)
            pl.semaphore_signal(barrier, inc=1, device_id=peer, device_id_type=MESH)
        pl.semaphore_wait(barrier, count - 1)


def remote(src, dst, send, recv, peer):
    return pltpu.make_async_remote_copy(
        src_ref=src, dst_ref=dst, send_sem=send, recv_sem=recv, device_id=peer, device_id_type=MESH
    )


def ffn_kernel(
    units,
    expert_count,
    rows_in,
    upstream_in,
    pair_in,
    down_in,
    side_in,
    resid_in,
    gain_in,
    rows_all,
    weighted_out,
    d_pair_out,
    block_out,
    d_resid_low_out,
    d_resid_out,
    d_gain_out,
    d_side_out,
    d_rows_sum,
    out_sum,
    pair_w,
    down_w,
    side_w,
    rows_tile,
    upstream_tile,
    pair_pre,
    d_hidden,
    factors,
    dots,
    weighted_tile,
    d_pair_tile,
    own_rows,
    own_upstream,
    d_resid_low,
    d_rows_tile,
    out_tile,
    d_rows_core,
    out_core,
    d_rows_held,
    out_held,
    d_rows_hop,
    out_hop,
    d_rows_hop2,
    out_hop2,
    d_rows_z,
    out_z,
    d_rows_to_z,
    out_to_z,
    gathered_send,
    gathered_recv,
    hop_send,
    hop_recv,
    weight_sem,
    own_sem,
    z_send,
    z_recv,
    plane_send,
    plane_recv,
    load_sem,
    store_sem,
    sum_send,
    sum_recv,
    end_send,
    end_recv,
    core_credit,
    hop_credit,
    hop2_credit,
):
    at = Place()
    depth = at.depth
    quarter, width = rows_in.shape
    half = quarter // 2
    f32, bf16 = jnp.float32, jnp.bfloat16

    def weight_copies():
        pairs = (
            (pair_in, pair_w),
            (down_in, down_w),
            (side_in, side_w),
            (rows_in, own_rows),
            (upstream_in.at[at.z, at.y, at.x, at.c], own_upstream),
        )
        return [
            pltpu.make_async_copy(src, dst, weight_sem.at[i]) for i, (src, dst) in enumerate(pairs)
        ]

    for copy in weight_copies():
        copy.start()

    def block(j, y, x):
        return rows_all.at[at.behind(j), y, x, at.c]

    def plane_copy(j, kind):
        y, other_y = at.y, 1 - at.y
        own, other_x = at.x, 1 - at.x
        if kind == 0:
            src, peer = block(j, y, own), at.next_x
        elif kind == 1:
            src, peer = block(j, y, own), at.next_y
        elif kind == 2:
            src, peer = block(j, y, other_x).at[pl.ds(0, half)], at.next_y
        elif kind == 3:
            src, peer = block(j, other_y, own).at[pl.ds(half, half)], at.next_x
        else:
            src = block(j, other_y if kind >= 6 else y, other_x if kind % 2 else own)
            peer = at.next_core
        return remote(src, src, plane_send.at[j, kind], plane_recv.at[j, kind], peer)

    def z_copy(k):
        return remote(
            rows_in, block(0, at.y, at.x), z_send.at[k - 1], z_recv.at[k - 1], at.at_z(at.ahead(k))
        )

    def z_arrival(k):
        dst = block(k, at.y, at.x)
        return remote(dst, dst, z_send.at[k - 1], z_recv.at[k - 1], at.at_z(at.behind(k)))

    def begin(j):
        for kind in (0, 1, 4):
            plane_copy(j, kind).start()

    def spread(j):
        plane_copy(j, 0).wait_recv()
        plane_copy(j, 2).start()
        plane_copy(j, 5).start()
        plane_copy(j, 1).wait_recv()
        plane_copy(j, 3).start()
        plane_copy(j, 6).start()

    def begin_later(j):
        z_arrival(j).wait_recv()
        begin(j)

    def last_hop(j):
        plane_copy(j, 2).wait_recv()
        plane_copy(j, 3).wait_recv()
        plane_copy(j, 7).start()

    def near_ready(j):
        plane_copy(j, 4).wait_recv()
        plane_copy(j, 5).wait_recv()

    def far_ready(j):
        plane_copy(j, 6).wait_recv()
        plane_copy(j, 7).wait_recv()

    def parity(step):
        return lax.rem(step, 2)

    def slot_of(turn):
        return lax.rem(turn + 1, depth)

    def other_y(step):
        return lax.rem(parity(step) + (step // 2 + 1) // depth, 2)

    def tile_at(step):
        return at.behind(slot_of(step // 2)), lax.rem(at.y + other_y(step), 2)

    def load_rows(step):
        z, y = tile_at(step)
        return pltpu.make_async_copy(rows_all.at[z, y], rows_tile, load_sem.at[0])

    def load_upstream(step):
        z, y = tile_at(step)
        return pltpu.make_async_copy(upstream_in.at[z, y], upstream_tile, load_sem.at[1])

    def stores(step):
        z, y = tile_at(step)
        pairs = ((weighted_tile, weighted_out), (d_pair_tile, d_pair_out))
        return [
            pltpu.make_async_copy(src, dst.at[z, y], store_sem.at[i])
            for i, (src, dst) in enumerate(pairs)
        ]

    tiles, cores = (d_rows_tile, out_tile), (d_rows_core, out_core)
    helds, sums = (d_rows_held, out_held), (d_rows_sum, out_sum)
    hops, hops2, zs = (d_rows_hop, out_hop), (d_rows_hop2, out_hop2), (d_rows_z, out_z)
    to_zs = (d_rows_to_z, out_to_z)

    def sum_copy(a, kind, src, dst, peer):
        return remote(src, dst, sum_send.at[a, kind], sum_recv.at[a, kind], peer)

    def core_sum(a):
        return sum_copy(a, 0, tiles[a].at[:, 1 - at.c], cores[a], at.next_core)

    def row_hop(turn, other):
        y = lax.rem(at.y + other, 2)
        src = d_rows_held.at[parity(turn), y, 1 - at.x]
        return remote(src, d_rows_hop.at[y], hop_send.at[other], hop_recv.at[other], at.next_x)

    def out_hop_sum(turn):
        return sum_copy(1, 1, out_held.at[parity(turn), 1 - at.y], out_hop, at.next_y)

    def hop2_sum(a, turn):
        slot = parity(turn)
        if a == 0:
            src, peer = helds[0].at[slot, 1 - at.y, at.x], at.next_y
        else:
            src, peer = helds[1].at[slot, at.y, 1 - at.x], at.next_x
        return sum_copy(a, 2, src, hops2[a], peer)

    def z_sum(a, turn):
        return remote(
            to_zs[a].at[turn],
            zs[a].at[turn],
            end_send.at[a, turn],
            end_recv.at[a, turn],
            at.at_z(at.behind(turn + 1)),
        )

    def allow(semaphore, peer):
        pl.semaphore_signal(semaphore, inc=1, device_id=peer, device_id_type=MESH)

    piece = 32

    def add(into, first, second):
        def body(i, carry):
            part = pl.ds(pl.multiple_of(i * piece, piece), piece)
            into[part] = first[part] + second[part]
            return carry

        lax.fori_loop(0, quarter // piece, body, 0)

    def after_core(step):
        turn = step // 2
        other = other_y(step)
        held, y = parity(turn), lax.rem(at.y + other, 2)

        @pl.when((parity(step) == 0) & (turn >= 1))
        def _():
            for a in (0, 1):
                pl.semaphore_wait(hop_credit.at[a], 1)

        for a in (0, 1):
            core_sum(a).wait()
            for x in (1 - at.x, at.x):
                add(helds[a].at[held, y, x], tiles[a].at[x, at.c], cores[a].at[x])
            if a == 0:
                row_hop(turn, other).start()
            else:

                @pl.when(other == 1)
                def _():
                    out_hop_sum(turn).start()

        @pl.when(step + 1 < 2 * depth)
        def _():
            allow(core_credit, at.next_core)

    def after_row_hop(turn, other):
        slot, y = parity(turn), lax.rem(at.y + other, 2)
        row_hop(turn, other).wait()
        into = d_rows_held.at[slot, y, at.x]
        add(into, into, d_rows_hop.at[y])

    def after_out_hop(turn):
        slot = parity(turn)
        out_hop_sum(turn).wait()
        for x in (1 - at.x, at.x):
            into = out_held.at[slot, at.y, x]
            add(into, into, out_hop.at[x])

    def may_hop2(turn, a):
        @pl.when(turn >= 1)
        def _():
            pl.semaphore_wait(hop2_credit.at[a], 1)

    def after_hop(turn):
        after_row_hop(turn, 1)
        may_hop2(turn, 0)
        hop2_sum(0, turn).start()
        after_row_hop(turn, 0)
        after_out_hop(turn)
        may_hop2(turn, 1)
        hop2_sum(1, turn).start()
        allow(hop_credit.at[0], at.next_x)
        allow(hop_credit.at[1], at.next_y)

    def after_hop2(turn):
        slot = parity(turn)
        for a in (0, 1):
            hop2_sum(a, turn).wait()
            add(to_zs[a].at[turn], helds[a].at[slot, at.y, at.x], hops2[a])
            z_sum(a, turn).start()
        allow(hop2_credit.at[0], at.next_y)
        allow(hop2_credit.at[1], at.next_x)

    load_upstream(0).start()
    at.greet()
    z_copy(1).start()
    own_copy = pltpu.make_async_copy(rows_in, block(0, at.y, at.x), own_sem)
    own_copy.start()
    own_copy.wait()
    begin(0)
    begin_later(1)
    for k in range(2, depth):
        z_copy(k).start()
    spread(0)
    spread(1)
    near_ready(1)
    load_rows(0).start()
    for copy in weight_copies():
        copy.wait()

    tile_rows = 4 * quarter
    hidden_total = down_w.shape[0]
    lane = lax.broadcasted_iota(jnp.int32, (tile_rows, 128), 1)
    slot_here, slot_hidden, shared_hidden = units
    routed = slot_here * slot_hidden
    across = (((1,), (1,)), ((), ()))
    few = 16

    def gate_factors(rows, picked):
        logits = jnp.dot(rows, side_w[...], preferred_element_type=f32)
        chooses = (lane >= 3) & (lane < 3 + expert_count)
        peak = jnp.max(jnp.where(chooses, logits, -1e30), axis=1, keepdims=True)
        expo = jnp.where(chooses, jnp.exp(jnp.where(chooses, logits, peak) - peak), 0.0)
        routed_gate = expo / jnp.sum(expo, axis=1, keepdims=True) * picked.astype(f32)
        mix_pre = jnp.sum(jnp.where(lane == 2, logits, 0.0), axis=1, keepdims=True)
        result = jnp.where(lane == slot_here, 1.0 / (1.0 + jnp.exp(-mix_pre)), 0.0)
        for s in range(slot_here):
            chosen = lane == 3 + at.ep * slot_here + s
            gate = jnp.sum(jnp.where(chosen, routed_gate, 0.0), axis=1, keepdims=True)
            result = jnp.where(lane == s, gate, result)
        return result

    few_lane = lax.broadcasted_iota(jnp.int32, (few, 128), 1)
    bounds = [s * slot_hidden for s in range(slot_here)] + [routed, hidden_total]

    def owners(group):
        found = []
        for s in range(slot_here + 1):
            low, high = max(bounds[s] - group * 128, 0), min(bounds[s + 1] - group * 128, 128)
            if low < high:
                found.append((s, low, high))
        return found

    def hidden_rows(i, carry):
        here = pl.ds(pl.multiple_of(i * few, few), few)
        gates = [
            jnp.broadcast_to(factors[here, s : s + 1], (few, 128)) for s in range(slot_here + 1)
        ]
        parts = [None] * (slot_here + 1)
        for group in range(hidden_total // 128):
            units_here = slice(group * 128, (group + 1) * 128)
            units_up = slice(hidden_total + group * 128, hidden_total + (group + 1) * 128)
            gate_pre, up_pre = pair_pre[here, units_here], pair_pre[here, units_up]
            d_h = d_hidden[here, units_here]
            found = owners(group)
            factor = gates[found[0][0]]
            for s, low, _ in found[1:]:
                factor = jnp.where(few_lane >= low, gates[s], factor)
            sig = 0.5 + 0.5 * jnp.tanh(0.5 * gate_pre)
            silu = gate_pre * sig
            hidden = silu * up_pre
            product = hidden * d_h
            gated = factor * d_h
            weighted_tile[here, units_here] = (factor * hidden).astype(bf16)
            slope = sig + silu * (1.0 - sig)
            d_pair_tile[here, units_here] = (gated * up_pre * slope).astype(bf16)
            d_pair_tile[here, units_up] = (gated * silu).astype(bf16)
            for s, low, high in found:
                mine = product
                if high < 128:
                    mine = jnp.where(few_lane < high, mine, 0.0)
                if low > 0:
                    mine = jnp.where(few_lane >= low, mine, 0.0)
                parts[s] = mine if parts[s] is None else parts[s] + mine
        result = jnp.zeros((few, 128), f32)
        for s in range(slot_here + 1):
            dot = jnp.sum(parts[s], axis=1, keepdims=True)
            where = few_lane == (2 if s == slot_here else 3 + at.ep * slot_here + s)
            result = jnp.where(where, dot, result)
        dots[here] = result.astype(bf16)
        return carry

    def first_half(step):
        load_upstream(step).wait()
        upstream = upstream_tile[...].reshape(tile_rows, upstream_tile.shape[-1])
        d_hidden[...] = lax.dot_general(
            upstream[:, :width], down_w[...], across, preferred_element_type=f32
        )
        load_rows(step).wait()
        rows = rows_tile[...].reshape(tile_rows, width)
        factors[...] = gate_factors(rows, upstream[:, width:])
        pair_pre[...] = lax.dot_general(rows, pair_w[...], across, preferred_element_type=f32)

        @pl.when(step + 1 < 2 * depth)
        def _():
            load_upstream(step + 1).start()

        @pl.when(step >= 1)
        def _():
            for copy in stores(step - 1):
                copy.wait()

        lax.fori_loop(0, tile_rows // few, hidden_rows, 0, unroll=2)
        for copy in stores(step):
            copy.start()
        turn = step // 2

        @pl.when(step == 0)
        def _():
            last_hop(0)

        @pl.when((parity(step) == 0) & (turn + 1 < depth))
        def _():
            last_hop(turn + 1)

        @pl.when((step >= 1) & (step + 1 < depth))
        def _():
            spread(step + 1)

        @pl.when(step + 2 < depth)
        def _():
            begin_later(step + 2)

    def second_half(step):
        blocks = (2, 2, quarter)
        some = width // 2
        for n in range(2):
            columns = slice(n * some, (n + 1) * some)
            part = jnp.dot(weighted_tile[...], down_w[:, columns], preferred_element_type=f32)
            out_tile[:, :, :, columns] = part.astype(bf16).reshape(blocks + (some,))
            part = jnp.dot(d_pair_tile[...], pair_w[:, columns], preferred_element_type=f32)
            d_rows_tile[:, :, :, columns] = part.astype(bf16).reshape(blocks + (some,))
        d_rows_tile[:, :, :, width:] = dots[...].reshape(blocks + (128,))

        @pl.when(step >= 1)
        def _():
            pl.semaphore_wait(core_credit, 1)

        for a in (0, 1):
            core_sum(a).start()
        turn = step // 2

        @pl.when((parity(step) == 0) & (turn + 1 < depth))
        def _():
            far_ready(slot_of(turn))

        @pl.when((parity(step) == 1) & (turn + 1 < depth))
        def _():
            near_ready(slot_of(turn + 1))

        @pl.when(step == 2 * depth - 3)
        def _():
            far_ready(slot_of(turn + 1))

        @pl.when(step + 1 < 2 * depth)
        def _():
            load_rows(step + 1).start()

    def step_body(step, carry):
        first_half(step)

        odd = parity(step) == 1

        @pl.when(odd & (step >= 3))
        def _():
            after_hop((step - 3) // 2)

        @pl.when(jnp.logical_not(odd) & (step >= 4))
        def _():
            after_hop2((step - 4) // 2)

        @pl.when(step >= 1)
        def _():
            after_core(step - 1)

        second_half(step)
        return carry

    lax.fori_loop(0, 2 * depth, step_body, 0)
    last = depth - 1
    after_hop2(last - 1)
    after_row_hop(last, 1)
    may_hop2(last, 0)
    hop2_sum(0, last).start()
    after_core(2 * depth - 1)
    after_out_hop(last)
    may_hop2(last, 1)
    hop2_sum(1, last).start()
    after_row_hop(last, 0)

    def total_of(a):
        hop2_sum(a, last).wait()
        held = helds[a].at[last % 2, at.y, at.x]
        for turn in range(last):
            z_sum(a, turn).wait_recv()

        def total_body(i, carry):
            part = pl.ds(pl.multiple_of(i * piece, piece), piece)
            total = held[part].astype(f32) + hops2[a][part].astype(f32)
            for k in range(last):
                total = total + zs[a][k, part].astype(f32)
            sums[a][part] = total
            return carry

        lax.fori_loop(0, quarter // piece, total_body, 0)

    total_of(0)
    own_lane = lax.broadcasted_iota(jnp.int32, (quarter, 128), 1)
    chooses = (own_lane >= 3) & (own_lane < 3 + expert_count)
    rows = own_rows[...]
    logits = jnp.dot(rows, side_w[...], preferred_element_type=f32)
    peak = jnp.max(jnp.where(chooses, logits, -1e30), axis=1, keepdims=True)
    expo = jnp.where(chooses, jnp.exp(jnp.where(chooses, logits, peak) - peak), 0.0)
    router = expo / jnp.sum(expo, axis=1, keepdims=True)
    mixer = 1.0 / (1.0 + jnp.exp(-jnp.where(own_lane == 2, logits, 0.0)))
    gate_dots = d_rows_sum[:, width:]
    d_router = jnp.where(chooses, gate_dots * own_upstream[:, width:].astype(f32), 0.0)
    d_logits = router * (d_router - jnp.sum(router * d_router, axis=1, keepdims=True))
    d_mix = gate_dots * mixer * (1.0 - mixer)
    d_side = jnp.where(own_lane == 2, d_mix, jnp.where(chooses, d_logits, 0.0))
    d_side_out[...] = d_side
    high = d_side.astype(bf16)
    lower = (d_side - high.astype(f32)).astype(bf16)
    for split in (high, lower):
        d_rows_sum[:, :width] += lax.dot_general(
            split, side_w[...], across, preferred_element_type=f32
        )

    def end_body(i, carry):
        part = pl.ds(pl.multiple_of(i * few, few), few)
        resid = resid_in[part]
        scale = lax.rsqrt(jnp.mean(resid * resid, axis=1, keepdims=True) + epsilon)
        unit_rows = resid * scale
        grads = d_rows_sum[part, :width]
        scaled = grads * gain_in[...]
        inner = jnp.mean(scaled * unit_rows, axis=1, keepdims=True)
        d_resid = own_upstream[part, :width].astype(f32) + scale * (scaled - unit_rows * inner)
        d_resid_out[part] = d_resid
        d_resid_low[part] = d_resid.astype(bf16)
        return carry + jnp.sum(grads * unit_rows, axis=0, keepdims=True)

    d_gain_out[...] = lax.fori_loop(0, quarter // few, end_body, jnp.zeros((1, width), f32))

    def gather_copy(kind):
        if kind == 2:
            src = dst = d_resid_low_out.at[1 - at.x, at.c]
        else:
            src, dst = d_resid_low, d_resid_low_out.at[at.x, at.c]
        peer = at.next_x if kind == 0 else at.next_core
        return remote(src, dst, gathered_send.at[kind], gathered_recv.at[kind], peer)

    own_end = pltpu.make_async_copy(d_resid_low, d_resid_low_out.at[at.x, at.c], own_sem)
    own_end.start()
    for kind in (0, 1):
        gather_copy(kind).start()
    total_of(1)
    block_out[...] = (resid_in[...] + out_sum[...]).astype(bf16)
    gather_copy(0).wait_recv()
    gather_copy(2).start()
    own_end.wait()
    gather_copy(0).wait_send()
    gather_copy(1).wait()
    gather_copy(2).wait()
    for copy in stores(2 * depth - 1):
        copy.wait()
    for a in (0, 1):
        for turn in range(depth - 1):
            z_sum(a, turn).wait_send()
    for k in range(1, depth):
        z_copy(k).wait_send()

    def finish(j, carry):
        for kind in range(8):
            plane_copy(j, kind).wait_send()
        return carry

    lax.fori_loop(0, depth, finish, 0)


def ffn_over_all(rows, upstream_all, pair_w, down_w, side_w, resid, gain, units, expert_count):
    quarter, width = rows.shape
    ep_count, tp_count = lax.axis_size("ep"), lax.axis_size("tp")
    depth = ep_count // 2
    hidden = down_w.shape[0]
    bf16, f32 = jnp.bfloat16, jnp.float32
    wide = width + 128
    tile_rows = tp_count * quarter
    tokens = ep_count * tile_rows
    anywhere = pl.BlockSpec(memory_space=pl.ANY)
    in_vmem = pl.BlockSpec(memory_space=pltpu.VMEM)

    def both(*lead):
        return [pltpu.VMEM(lead + (quarter, columns), bf16) for columns in (wide, width)]

    dma = pltpu.SemaphoreType.DMA
    outs = pl.pallas_call(
        functools.partial(ffn_kernel, units, expert_count),
        out_shape=(
            jax.ShapeDtypeStruct((depth, 2, 2, 2, quarter, width), bf16),
            jax.ShapeDtypeStruct((depth, 2, tile_rows, hidden), bf16),
            jax.ShapeDtypeStruct((depth, 2, tile_rows, 2 * hidden), bf16),
            jax.ShapeDtypeStruct((quarter, width), bf16),
            jax.ShapeDtypeStruct((2, 2, quarter, width), bf16),
            jax.ShapeDtypeStruct((quarter, width), f32),
            jax.ShapeDtypeStruct((1, width), f32),
            jax.ShapeDtypeStruct((quarter, 128), f32),
        ),
        in_specs=[anywhere] * 5 + [in_vmem] * 2,
        out_specs=(anywhere,) * 3 + (in_vmem, anywhere) + (in_vmem,) * 3,
        scratch_shapes=[
            pltpu.VMEM((quarter, wide), f32),
            pltpu.VMEM((quarter, width), f32),
            pltpu.VMEM((2 * hidden, width), bf16),
            pltpu.VMEM((hidden, width), bf16),
            pltpu.VMEM((width, 128), bf16),
            pltpu.VMEM((2, 2, quarter, width), bf16),
            pltpu.VMEM((2, 2, quarter, wide), bf16),
            pltpu.VMEM((tile_rows, 2 * hidden), f32),
            pltpu.VMEM((tile_rows, hidden), f32),
            pltpu.VMEM((tile_rows, 128), f32),
            pltpu.VMEM((tile_rows, 128), bf16),
            pltpu.VMEM((tile_rows, hidden), bf16),
            pltpu.VMEM((tile_rows, 2 * hidden), bf16),
            pltpu.VMEM((quarter, width), bf16),
            pltpu.VMEM((quarter, wide), bf16),
            pltpu.VMEM((quarter, width), bf16),
        ]
        + both(2, 2)
        + both(2)
        + both(2, 2, 2)
        + both(2)
        + both()
        + both(depth - 1)
        + both(depth - 1)
        + [
            dma((3,)),
            dma((3,)),
            dma((2,)),
            dma((2,)),
            dma((5,)),
            dma,
            dma((depth - 1,)),
            dma((depth - 1,)),
            dma((depth, 8)),
            dma((depth, 8)),
            dma((2,)),
            dma((2,)),
            dma((2, 3)),
            dma((2, 3)),
            dma((2, depth - 1)),
            dma((2, depth - 1)),
            pltpu.SemaphoreType.REGULAR,
            pltpu.SemaphoreType.REGULAR((2,)),
            pltpu.SemaphoreType.REGULAR((2,)),
        ],
        compiler_params=pltpu.CompilerParams(
            collective_id=1, has_side_effects=True, vmem_limit_bytes=62 * 2**20
        ),
        cost_estimate=pl.CostEstimate(
            flops=12 * tokens * width * hidden,
            bytes_accessed=10 * tokens * width,
            transcendentals=tokens * hidden,
        ),
        name="ffn_all_tokens",
    )(
        rows,
        upstream_all.reshape(depth, 2, 2, 2, quarter, wide),
        pair_w,
        down_w,
        side_w,
        resid,
        gain,
    )
    rows_all, weighted, d_pair, block_out, d_resid_low, d_resid, d_gain, d_side = outs
    return (
        rows_all.reshape(tokens, width),
        weighted.reshape(tokens, hidden),
        d_pair.reshape(tokens, 2 * hidden),
        block_out,
        d_resid_low.reshape(tile_rows, width),
        d_resid,
        d_gain[0],
        d_side,
    )


def over_tp(block, distance):
    devices = range(lax.axis_size("tp"))
    return lax.ppermute(block, "tp", [(i, i ^ distance) for i in devices])


def one_of(array, index, axis):
    return lax.dynamic_index_in_dim(array, index, axis, keepdims=False)


def sum_over_tp(part):
    rows, columns = part.shape
    tp = lax.axis_index("tp")
    x, c = tp // 2, tp % 2
    blocks = part.reshape(2, 2, rows // 4, columns)
    got = over_tp(one_of(blocks, 1 - c, 1).astype(jnp.bfloat16), 1)
    chip = one_of(blocks, c, 1).astype(jnp.float32) + got.astype(jnp.float32)
    got = over_tp(one_of(chip, 1 - x, 0).astype(jnp.bfloat16), 2)
    return one_of(chip, x, 0) + got.astype(jnp.float32)


def gather_over_tp(block):
    tp = lax.axis_index("tp")
    x, c = tp // 2, tp % 2
    got = over_tp(block, 2)
    pair = jnp.where(x == 0, jnp.stack([block, got]), jnp.stack([got, block]))
    got = over_tp(pair, 1)
    four = jnp.where(c == 0, jnp.stack([pair, got], axis=1), jnp.stack([got, pair], axis=1))
    return four.reshape(4 * block.shape[0], block.shape[1])


def swap_copies(at, pieces_in, pieces_out, send_sem, recv_sem, leave):
    count = 2 * at.depth
    copies = []
    for k in range(1, count):
        to, back = lax.rem(at.ep + k, count), lax.rem(at.ep + count - k, count)
        if leave:
            src, dst, peer = pieces_in.at[to], pieces_out.at[at.ep], to
        else:
            src, dst, peer = pieces_in.at[back], pieces_out.at[back], back
        copies.append(remote(src, dst, send_sem.at[k], recv_sem.at[k], (peer, at.tp)))
    return copies


def weights_kernel(
    own_in,
    pieces_in,
    all_out,
    pieces_out,
    own_sem,
    z_send,
    z_recv,
    y_send,
    y_recv,
    swap_send,
    swap_recv,
):
    at = Place()
    depth = at.depth
    half = own_in.shape[0] // 2
    last = depth - 1

    def block(k, y, h):
        return all_out.at[at.z + k, y, pl.ds(h * half, half)]

    def z_copy(k, h, direction):
        if k == 0:
            src = own_in.at[pl.ds(h * half, half)]
        else:
            src = block(k, at.y, h)
        slot = last + k - direction
        return remote(
            src,
            block(k, at.y, h),
            z_send.at[last + k, h, (direction + 1) // 2],
            z_recv.at[slot, h],
            at.at_z(at.z + direction),
        )

    def z_arrival(k, h):
        direction = 1 if k > 0 else -1
        dst = block(k, at.y, h)
        return remote(
            dst, dst, z_send.at[last + k, h, 0], z_recv.at[last + k, h], at.at_z(at.z + direction)
        )

    def y_copy(k, h):
        src = own_in.at[pl.ds(h * half, half)] if k == 0 else block(k, at.y, h)
        return remote(
            src, block(k, at.y, h), y_send.at[last + k, h], y_recv.at[last + k, h], at.next_y
        )

    own_copies = [
        pltpu.make_async_copy(own_in, all_out.at[at.z, at.y], own_sem.at[0]),
        pltpu.make_async_copy(pieces_in.at[at.ep], pieces_out.at[at.ep], own_sem.at[1]),
    ]
    for copy in own_copies:
        copy.start()
    has_up, has_down = at.z + 1 < depth, at.z > 0
    at.greet_ep()

    for h in (0, 1):
        pl.when(has_up)(lambda: z_copy(0, h, 1).start())
        pl.when(has_down)(lambda: z_copy(0, h, -1).start())
        y_copy(0, h).start()
    swap = (at, pieces_in, pieces_out, swap_send, swap_recv)
    for copy in swap_copies(*swap, True):
        copy.start()
    for k in range(1, depth):
        for h in (0, 1):
            for sign in (-1, 1):
                there = at.z + sign * k
                exists = (there >= 0) & (there < depth)
                onward = at.z - sign
                goes_on = exists & (onward >= 0) & (onward < depth)

                @pl.when(exists)
                def _():
                    z_arrival(sign * k, h).wait_recv()

                @pl.when(goes_on)
                def _():
                    z_copy(sign * k, h, -sign).start()

                @pl.when(exists)
                def _():
                    y_copy(sign * k, h).start()

    for copy in own_copies:
        copy.wait()
    for copy in swap_copies(*swap, False):
        copy.wait_recv()
    for copy in swap_copies(*swap, True):
        copy.wait_send()
    for h in (0, 1):
        pl.when(has_up)(lambda: z_copy(0, h, 1).wait_send())
        pl.when(has_down)(lambda: z_copy(0, h, -1).wait_send())
    for k in range(-last, depth):
        there = at.z + k
        exists = (there >= 0) & (there < depth)
        sign = 1 if k > 0 else -1
        onward = at.z - sign
        goes_on = exists & (onward >= 0) & (onward < depth)
        for h in (0, 1):

            @pl.when(exists)
            def _():
                y_copy(k, h).wait()

            if k != 0:

                @pl.when(goes_on)
                def _():
                    z_copy(k, h, -sign).wait_send()


def gather_over_ep(block, pieces):
    rows, columns = block.shape
    depth = lax.axis_size("ep") // 2
    anywhere = pl.BlockSpec(memory_space=pl.ANY)
    slots = 2 * depth - 1
    out, pieces = pl.pallas_call(
        weights_kernel,
        out_shape=(
            jax.ShapeDtypeStruct((depth, 2, rows, columns), block.dtype),
            jax.ShapeDtypeStruct(pieces.shape, pieces.dtype),
        ),
        in_specs=[anywhere] * 2,
        out_specs=(anywhere,) * 2,
        scratch_shapes=[
            pltpu.SemaphoreType.DMA((2,)),
            pltpu.SemaphoreType.DMA((slots, 2, 2)),
            pltpu.SemaphoreType.DMA((slots, 2)),
            pltpu.SemaphoreType.DMA((slots, 2)),
            pltpu.SemaphoreType.DMA((slots, 2)),
            pltpu.SemaphoreType.DMA((2 * depth,)),
            pltpu.SemaphoreType.DMA((2 * depth,)),
        ],
        compiler_params=pltpu.CompilerParams(collective_id=3, has_side_effects=True),
        cost_estimate=pl.CostEstimate(
            flops=0, bytes_accessed=8 * depth * rows * columns, transcendentals=0
        ),
        name="gather_weights",
    )(block, pieces)
    return out.reshape(2 * depth * rows, columns), pieces


def back_kernel(
    units,
    score_scale,
    d_low_in,
    weights_in,
    q_in,
    k_in,
    v_in,
    turned_in,
    block_in,
    rows_in,
    d_pair_in,
    upstream_in,
    weighted_in,
    lse_in,
    query_seg,
    key_seg,
    query_at,
    key_at,
    cos_in,
    sin_in,
    own_rows_in,
    gain_in,
    d_resid_in,
    gain_two_in,
    side_in,
    out,
    small_out,
    block_out,
    d_rows_out,
    pieces_got,
    gate_out,
    up_out,
    down_out,
    qkv_w,
    turned,
    d_out,
    d_got,
    d_own,
    d_proj,
    part,
    core_got,
    x_got,
    d_rows,
    own,
    y_out,
    hop,
    from_z,
    small_own,
    small_hop,
    small_z,
    small,
    small_got,
    pieces,
    load_sem,
    d_send,
    d_recv,
    tp_send,
    tp_recv,
    y_send,
    y_recv,
    z_send,
    z_recv,
    little_send,
    little_recv,
    small_send,
    small_recv,
    swap_send,
    swap_recv,
    rows_send,
    rows_recv,
    own_sem,
    tile_sem,
    store_sem,
):
    at = Place()
    depth = at.depth
    count = 2 * depth
    heads, tokens, head = q_in.shape
    heads_width = heads * head
    windows = k_in.shape[1] // tokens
    quarter, width = d_rows.shape
    rows = out.shape[0]
    f32, bf16 = jnp.float32, jnp.bfloat16
    across = (((1,), (1,)), ((), ()))
    slot_here, slot_hidden, shared_hidden = units
    routed = slot_here * slot_hidden
    hidden = weighted_in.shape[2]
    few = 16

    def d_copy(w, h):
        peer = (at.ep - (2 - w), at.tp)
        return remote(d_out.at[w, h], d_got.at[w, h], d_send.at[w, h], d_recv.at[w, h], peer)

    def d_arrival(w, h):
        peer = (at.ep + (2 - w), at.tp)
        dst = d_got.at[w, h]
        return remote(dst, dst, d_send.at[w, h], d_recv.at[w, h], peer)

    def core_copy():
        return remote(part.at[:, 1 - at.c], core_got, tp_send.at[0], tp_recv.at[0], at.next_core)

    def x_copy():
        return remote(part.at[1 - at.x, at.c], x_got, tp_send.at[1], tp_recv.at[1], at.next_x)

    def y_copy(j):
        return remote(y_out.at[j], hop.at[j], y_send.at[j], y_recv.at[j], at.next_y)

    def z_copy(j):
        return remote(
            own.at[j], from_z.at[j - 1], z_send.at[j], z_recv.at[j], at.at_z(at.ahead(j))
        )

    def little_y(j):
        return remote(
            small_own.at[at.ahead(j), 1 - at.y],
            small_hop.at[j],
            little_send.at[0, j],
            little_recv.at[0, j],
            at.next_y,
        )

    def little_z(j):
        return remote(
            small_own.at[at.ahead(j), at.y],
            small_z.at[j - 1],
            little_send.at[1, j],
            little_recv.at[1, j],
            at.at_z(at.ahead(j)),
        )

    def small_copy(kind):
        peer = at.next_core if kind == 0 else at.next_x
        return remote(
            small.at[kind], small_got.at[kind], small_send.at[kind], small_recv.at[kind], peer
        )

    ends = ((block_in, block_out), (d_rows, d_rows_out))

    def rows_copy(a, kind):
        mine, gathered = ends[a]
        if kind == 2:
            src = dst = gathered.at[1 - at.x, at.c]
        else:
            src, dst = mine, gathered.at[at.x, at.c]
        peer = at.next_x if kind == 0 else at.next_core
        return remote(src, dst, rows_send.at[a, kind], rows_recv.at[a, kind], peer)

    def rows_own(a):
        mine, gathered = ends[a]
        return pltpu.make_async_copy(mine, gathered.at[at.x, at.c], own_sem.at[a])

    def rows_begin(a):
        for kind in (0, 1):
            rows_copy(a, kind).start()
        rows_own(a).start()

    def rows_pass_on(a):
        rows_copy(a, 0).wait_recv()
        rows_copy(a, 2).start()

    def rows_end(a):
        rows_own(a).wait()
        rows_copy(a, 0).wait_send()
        rows_copy(a, 1).wait()
        rows_copy(a, 2).wait()

    def swap_copies(p, leave):
        some = pl.ds(p * shared_hidden, shared_hidden)
        copies = []
        for k in range(1, count):
            to, back = lax.rem(at.ep + k, count), lax.rem(at.ep + count - k, count)
            if leave:
                src, dst, peer = pieces.at[to, some], pieces_got.at[at.ep, some], to
            else:
                src, dst, peer = pieces.at[back, some], pieces_got.at[back, some], back
            copies.append(remote(src, dst, swap_send.at[p, k], swap_recv.at[p, k], (peer, at.tp)))
        return copies

    def swap_own(p):
        some = pl.ds(p * shared_hidden, shared_hidden)
        return pltpu.make_async_copy(
            pieces.at[at.ep, some], pieces_got.at[at.ep, some], own_sem.at[2 + p]
        )

    late_loads = [
        pltpu.make_async_copy(weights_in.at[:, pl.ds(0, 3 * heads_width)], qkv_w, load_sem.at[0]),
        pltpu.make_async_copy(turned_in, turned, load_sem.at[1]),
    ]
    lane = lax.broadcasted_iota(jnp.int32, (tokens, head), 1)
    sign = jnp.where(lane < head // 2, -1.0, 1.0)

    def unrotated(grads):
        turned_part = pltpu.roll(grads * sin_in[...], head // 2, 1) * sign
        return grads * cos_in[...] - turned_part

    def attention(d_low, out_w, q_all, k_all, v_all, d_att, probs, d_probs):
        pairs = (
            (d_low_in, d_low),
            (weights_in.at[:, pl.ds(3 * heads_width, heads_width)], out_w),
            (q_in, q_all),
            (k_in, k_all),
            (v_in, v_all),
        )
        copies = [
            pltpu.make_async_copy(src, dst, load_sem.at[2 + i])
            for i, (src, dst) in enumerate(pairs)
        ]
        for copy in copies + late_loads:
            copy.start()
        at.greet_row()
        rows_begin(0)
        copies[0].wait()
        copies[1].wait()
        d_attended = jnp.dot(d_low[...], out_w[...], preferred_element_type=f32).astype(bf16)
        for h in range(heads):
            d_att[h] = d_attended[:, h * head : (h + 1) * head]
        for copy in copies[2:]:
            copy.wait()

        def head_body(h, carry):
            queries, d_a = q_all[h], d_att[h]
            delta = jnp.zeros((1, tokens), f32)
            for w in range(windows):
                some = slice(w * tokens, (w + 1) * tokens)
                scores = lax.dot_general(
                    k_all[h, some], queries, across, preferred_element_type=f32
                )
                allowed = (key_seg[some] == query_seg[...]) & (key_at[some] <= query_at[...])
                p = jnp.where(allowed, jnp.exp(scores * score_scale - lse_in[h]), 0.0)
                d_p = lax.dot_general(v_all[h, some], d_a, across, preferred_element_type=f32)
                probs[w] = p
                d_probs[w] = d_p
                delta = delta + jnp.sum(p * d_p, axis=0, keepdims=True)
            d_queries = jnp.zeros((head, tokens), f32)
            for w in range(windows):
                some = slice(w * tokens, (w + 1) * tokens)
                p = probs[w]
                d_scores = (p * (d_probs[w] - delta)).astype(bf16)
                d_keys = jnp.dot(d_scores, queries, preferred_element_type=f32) * score_scale
                d_values = jnp.dot(p.astype(bf16), d_a, preferred_element_type=f32)
                if w < windows - 1:
                    d_out[w, h, :, :head] = d_keys.astype(bf16)
                    d_out[w, h, :, head:] = d_values.astype(bf16)

                    @pl.when(at.ep >= 2 - w)
                    def _():
                        d_copy(w, h).start()

                else:
                    d_own[h, :, :head] = d_keys
                    d_own[h, :, head:] = d_values
                d_queries = d_queries + jnp.dot(
                    k_all[h, some].T, d_scores, preferred_element_type=f32
                )
            here = pl.ds(pl.multiple_of(h * head, head), head)
            d_proj[:, here] = unrotated((d_queries * score_scale).T).astype(bf16)
            return carry

        lax.fori_loop(0, heads, head_body, 0)

    pl.run_scoped(
        attention,
        pltpu.VMEM((tokens, width), bf16),
        pltpu.VMEM((width, heads_width), bf16),
        pltpu.VMEM((heads, tokens, head), bf16),
        pltpu.VMEM((heads, windows * tokens, head), bf16),
        pltpu.VMEM((heads, windows * tokens, head), bf16),
        pltpu.VMEM((heads, tokens, head), bf16),
        pltpu.VMEM((windows, tokens, tokens), f32),
        pltpu.VMEM((windows, tokens, tokens), f32),
    )
    order = [j for j in range(1, depth)] + [0]

    def own_body(h, carry):
        for w in range(windows - 1):

            @pl.when(at.ep + (2 - w) < count)
            def _():
                d_arrival(w, h).wait_recv()
                d_own[h] += d_got[w, h].astype(f32)

        k_here = pl.ds(pl.multiple_of(heads_width + h * head, head), head)
        v_here = pl.ds(pl.multiple_of(2 * heads_width + h * head, head), head)
        d_proj[:, k_here] = unrotated(d_own[h, :, :head]).astype(bf16)
        d_proj[:, v_here] = d_own[h, :, head:].astype(bf16)
        return carry

    def weight_rows(z, y):
        here = pl.ds(pl.multiple_of((z * 2 + y) * rows, rows), rows)
        return jnp.dot(turned[here], d_proj[...], preferred_element_type=f32).astype(bf16)

    def projections():
        lax.fori_loop(0, heads, own_body, 0)
        for copy in late_loads:
            copy.wait()
        for n in range(2):
            some = slice(n * (width // 2), (n + 1) * (width // 2))
            product = lax.dot_general(d_proj[...], qkv_w[some], across, preferred_element_type=f32)
            part[:, :, :, some] = product.astype(bf16).reshape(2, 2, quarter, width // 2)
        core_copy().start()
        for j in order:
            y_out[j] = weight_rows(at.ahead(j), 1 - at.y)
            y_copy(j).start()
        core_copy().wait()
        for x in (0, 1):
            part[x, at.c] = part[x, at.c] + core_got[x]
        x_copy().start()
        for j in order:
            own[j] = weight_rows(at.ahead(j), at.y)
        x_copy().wait()

        def end_body(i, carry):
            here = pl.ds(pl.multiple_of(i * few, few), few)
            grads = part[at.x, at.c, here].astype(f32) + x_got[here].astype(f32)
            inputs = own_rows_in[here].astype(f32)
            scale = lax.rsqrt(jnp.mean(inputs * inputs, axis=1, keepdims=True) + epsilon)
            unit_rows = inputs * scale
            scaled = grads * gain_in[...]
            inner = jnp.mean(scaled * unit_rows, axis=1, keepdims=True)
            total = d_resid_in[here] + scale * (scaled - unit_rows * inner)
            d_rows[here] = total.astype(bf16)
            return carry + jnp.sum(grads * unit_rows, axis=0, keepdims=True)

        d_gain = lax.fori_loop(0, quarter // few, end_body, jnp.zeros((1, width), f32))
        rows_begin(1)
        line = lax.broadcasted_iota(jnp.int32, (128, rows), 0)
        for e in range(count):
            some = slice(e * rows, (e + 1) * rows)
            gains = jnp.where(line == 0, d_gain[:, some], 0.0)
            gains = jnp.where(line == 1, gain_two_in[:, some], gains)
            small_own[e // 2, e % 2] = (gains.T + side_in[some]).astype(bf16)
        for j in order:
            little_y(j).start()

    def after_y(j):
        y_copy(j).wait_recv()

        def body(i, carry):
            some = pl.ds(pl.multiple_of(i * few, few), few)
            own[j, some] = own[j, some] + hop[j, some]
            return carry

        lax.fori_loop(0, rows // few, body, 0)
        if j > 0:
            z_copy(j).start()

    def after_little():
        for j in order:
            little_y(j).wait_recv()
            here = small_own.at[at.ahead(j), at.y]
            here[...] = here[...] + small_hop[j]
            if j > 0:
                little_z(j).start()

    hooks = {(0, 2): [functools.partial(rows_pass_on, 0)]}
    hooks[(1, 2)] = [functools.partial(rows_pass_on, 1)]
    hooks[(1, 3)] = [after_little]
    last_hooks = []
    for i, j in enumerate(order):
        when = count + 5 + 5 * i
        due = functools.partial(after_y, j)
        if when < 3 * count:
            hooks.setdefault((when // count, when % count), []).append(due)
        else:
            last_hooks.append(due)

    def weight_gradients(total, left_tile, right_tile, left, staging):
        lefts = (
            lambda tile: d_pair_in.at[tile, :, pl.ds(0, hidden)],
            lambda tile: d_pair_in.at[tile, :, pl.ds(hidden, hidden)],
            lambda tile: weighted_in.at[tile],
        )
        rights = (
            lambda tile: rows_in.at[tile],
            lambda tile: rows_in.at[tile],
            lambda tile: upstream_in.at[tile, :, pl.ds(0, width)],
        )
        results = (gate_out, up_out, down_out)

        def loads(p, tile):
            slot = lax.rem(tile, 2)
            return [
                pltpu.make_async_copy(lefts[p](tile), left_tile.at[slot], tile_sem.at[0, slot]),
                pltpu.make_async_copy(rights[p](tile), right_tile.at[slot], tile_sem.at[1, slot]),
            ]

        def store(p):
            return pltpu.make_async_copy(staging, results[p], store_sem)

        def run_pass(p):
            def tile_body(tile, carry):
                slot = lax.rem(tile, 2)
                for copy in loads(p, tile):
                    copy.wait()

                @pl.when(tile + 1 < count)
                def _():
                    for copy in loads(p, tile + 1):
                        copy.start()

                if p < 2:

                    @pl.when(tile + 1 == count)
                    def _():
                        for copy in loads(p + 1, 0):
                            copy.start()

                left[...] = left_tile[slot].T
                some_columns = width // 4
                for n in range(4):
                    these = slice(n * some_columns, (n + 1) * some_columns)
                    product = jnp.dot(
                        left[...], right_tile[slot, :, these], preferred_element_type=f32
                    )

                    @pl.when(tile == 0)
                    def _():
                        total[:, these] = product

                    @pl.when(tile > 0)
                    def _():
                        total[:, these] += product

                for (hook_pass, hook_tile), actions in hooks.items():
                    if hook_pass == p:

                        @pl.when(tile == hook_tile)
                        def _():
                            for action in actions:
                                action()

                return carry

            lax.fori_loop(0, count, tile_body, 0)
            columns = width // count
            some = slice(p * shared_hidden, (p + 1) * shared_hidden)
            for e in range(count):
                pieces[e, some] = total[
                    routed : routed + shared_hidden, e * columns : (e + 1) * columns
                ].astype(bf16)
            swap_own(p).start()
            for copy in swap_copies(p, True):
                copy.start()
            if p > 0:
                store(p - 1).wait()
            staging[...] = total[:routed].astype(bf16)
            store(p).start()

        for copy in loads(0, 0):
            copy.start()
        run_pass(0)
        projections()
        run_pass(1)
        run_pass(2)
        for action in last_hooks:
            action()
        store(2).wait()

    pl.run_scoped(
        weight_gradients,
        pltpu.VMEM((hidden, width), f32),
        pltpu.VMEM((2, tokens, hidden), bf16),
        pltpu.VMEM((2, tokens, width), bf16),
        pltpu.VMEM((hidden, tokens), bf16),
        pltpu.VMEM((routed, width), bf16),
    )
    total = small_own[at.z, at.y].astype(f32)
    for j in range(1, depth):
        little_z(j).wait_recv()
        total = total + small_z[j - 1].astype(f32)
    for kind in (0, 1):
        small[kind] = total
        small_copy(kind).start()
        small_copy(kind).wait()
        total = small[kind] + small_got[kind]
    small_out[...] = total
    for j in range(1, depth):
        z_copy(j).wait_recv()

    def total_body(i, carry):
        some = pl.ds(pl.multiple_of(i * few, few), few)
        result = own[0, some].astype(f32)
        for k in range(depth - 1):
            result = result + from_z[k, some].astype(f32)
        out[some] = result
        return carry

    lax.fori_loop(0, rows // few, total_body, 0)
    for j in range(depth):
        y_copy(j).wait_send()
        little_y(j).wait_send()
        if j > 0:
            z_copy(j).wait_send()
            little_z(j).wait_send()
    for a in (0, 1):
        rows_end(a)
    for p in range(3):
        swap_own(p).wait()
        for copy in swap_copies(p, False):
            copy.wait_recv()
        for copy in swap_copies(p, True):
            copy.wait_send()

    def finish(h, carry):
        for w in range(windows - 1):

            @pl.when(at.ep >= 2 - w)
            def _():
                d_copy(w, h).wait_send()

        return carry

    lax.fori_loop(0, heads, finish, 0)


def backward(large, tiles_of, in_place, units, scale):
    d_low, _, queries, keys = large[:4]
    heads, tokens, head = queries.shape
    width = d_low.shape[1]
    ep_count = lax.axis_size("ep")
    depth, rows = ep_count // 2, width // ep_count
    quarter = tokens // lax.axis_size("tp")
    windows = keys.shape[1] // tokens
    columns = 3 * heads * head
    hidden = tiles_of[3].shape[2]
    slot_here, slot_hidden, shared_hidden = units
    f32, bf16 = jnp.float32, jnp.bfloat16
    anywhere = pl.BlockSpec(memory_space=pl.ANY)
    in_vmem = pl.BlockSpec(memory_space=pltpu.VMEM)
    dma = pltpu.SemaphoreType.DMA
    pieces = (ep_count, 3 * shared_hidden, rows)
    gathered = jax.ShapeDtypeStruct((2, 2, quarter, width), bf16)
    routed = jax.ShapeDtypeStruct((slot_here * slot_hidden, width), bf16)

    def vmem(*shape, dtype=bf16):
        return pltpu.VMEM(shape, dtype)

    out, small, block_out, d_rows, pieces, gate, up, down = pl.pallas_call(
        functools.partial(back_kernel, units, scale),
        out_shape=(
            jax.ShapeDtypeStruct((rows, columns), f32),
            jax.ShapeDtypeStruct((rows, 128), f32),
            gathered,
            gathered,
            jax.ShapeDtypeStruct(pieces, bf16),
            routed,
            routed,
            routed,
        ),
        in_specs=[anywhere] * (len(large) + len(tiles_of)) + [in_vmem] * len(in_place),
        out_specs=(in_vmem, in_vmem) + (anywhere,) * 6,
        scratch_shapes=[
            vmem(width, columns),
            vmem(width, tokens),
            vmem(windows - 1, heads, tokens, 2 * head),
            vmem(windows - 1, heads, tokens, 2 * head),
            vmem(heads, tokens, 2 * head, dtype=f32),
            vmem(tokens, columns),
            vmem(2, 2, quarter, width),
            vmem(2, quarter, width),
            vmem(quarter, width),
            vmem(quarter, width),
            vmem(depth, rows, columns),
            vmem(depth, rows, columns),
            vmem(depth, rows, columns),
            vmem(depth - 1, rows, columns),
            vmem(depth, 2, rows, 128),
            vmem(depth, rows, 128),
            vmem(depth - 1, rows, 128),
            vmem(2, rows, 128, dtype=f32),
            vmem(2, rows, 128, dtype=f32),
            vmem(*pieces),
            dma((7,)),
            dma((windows - 1, heads)),
            dma((windows - 1, heads)),
            dma((2,)),
            dma((2,)),
            dma((depth,)),
            dma((depth,)),
            dma((depth,)),
            dma((depth,)),
            dma((2, depth)),
            dma((2, depth)),
            dma((2,)),
            dma((2,)),
            dma((3, ep_count)),
            dma((3, ep_count)),
            dma((2, 3)),
            dma((2, 3)),
            dma((5,)),
            dma((2, 2)),
            dma,
        ],
        compiler_params=pltpu.CompilerParams(
            collective_id=4, has_side_effects=True, vmem_limit_bytes=62 * 2**20
        ),
        cost_estimate=pl.CostEstimate(
            flops=6 * ep_count * tokens * width * hidden,
            bytes_accessed=8 * ep_count * tokens * width,
            transcendentals=heads * tokens * windows * tokens,
        ),
        name="backward",
    )(*large, *tiles_of, *in_place)
    block_out, d_rows = [array.reshape(4 * quarter, width) for array in (block_out, d_rows)]
    return out, small, block_out, d_rows, pieces, (gate, up, down)


def shared_pieces(weights, ep_count):
    rows, hidden = weights[0].shape
    units = hidden // ep_count
    return jnp.concatenate([weight.T.reshape(ep_count, units, rows) for weight in weights], axis=1)


def shared_units_of(pieces, count):
    ep_count, units, rows = pieces.shape
    return pieces.transpose(1, 0, 2).reshape(count, units // count, ep_count * rows)


def shared_whole(pieces, count):
    ep_count, units, columns = pieces.shape
    units = units // count
    pieces = pieces.reshape(ep_count, count, units, columns).astype(jnp.float32)
    return [pieces[:, i].reshape(ep_count * units, columns).T for i in range(count)]


def dense_body(
    tokens,
    lengths,
    routes,
    attn_gain,
    w_query,
    w_key,
    w_value,
    w_out,
    ffn_gain,
    w_router,
    shared_mix,
    shared_gate,
    shared_up,
    shared_down,
    expert_gate,
    expert_up,
    expert_down,
    cotangent,
):
    everywhere = ("ep", "tp")
    rows_here, width = tokens.shape
    ep_count = lax.axis_size("ep")
    tp_count = lax.axis_size("tp")
    ep_index = lax.axis_index("ep")
    offset = ep_index * rows_here
    quarter = rows_here // tp_count
    first_row = lax.axis_index("tp") * quarter
    slot_here, slot_hidden = expert_gate.shape[0], expert_gate.shape[1]
    expert_count = w_router.shape[1]
    bf16, f32 = jnp.bfloat16, jnp.float32

    def my_rows(array):
        return lax.dynamic_slice_in_dim(array, first_row, quarter, 0)

    side_columns = jnp.concatenate(
        [attn_gain[:, None], ffn_gain[:, None], shared_mix[:, None], w_router], axis=1
    )
    side_columns = jnp.pad(side_columns, ((0, 0), (0, -side_columns.shape[1] % 128)))
    joined_weights, pieces = gather_over_ep(
        jnp.concatenate([w_query, w_key, w_value, w_out, side_columns], axis=1),
        shared_pieces((shared_gate, shared_up, shared_down), ep_count),
    )
    cotangent_rows = my_rows(cotangent)
    joined_weights, cotangent_rows = lax.optimization_barrier((joined_weights, cotangent_rows))
    heads_width = w_query.shape[1]
    qkv_weight = joined_weights[:, : 3 * heads_width]
    output_weight = joined_weights[:, 3 * heads_width : 4 * heads_width]
    side_weight = joined_weights[:, 4 * heads_width :]
    picked = jnp.any(
        my_rows(routes)[:, :, None] == jnp.arange(expert_count, dtype=jnp.int32), axis=1
    )
    picked_lanes = jnp.pad(picked.astype(bf16), ((0, 0), (3, 125 - expert_count)))
    upstream_all = lax.all_gather(
        jnp.concatenate([cotangent_rows, picked_lanes], axis=1), everywhere, axis=0, tiled=True
    )
    shared_rows = shared_units_of(pieces, 3)
    shared_units = shared_rows.shape[1]
    routed_units = slot_here * slot_hidden
    gate_cat, up_cat, down_cat = [
        jnp.pad(
            jnp.concatenate([expert.reshape(-1, width), shared], axis=0),
            ((0, -(routed_units + shared_units) % 128), (0, 0)),
        )
        for expert, shared in zip((expert_gate, expert_up, expert_down), shared_rows)
    ]
    pair_cat = jnp.concatenate([gate_cat, up_cat], axis=0)
    hidden_total = gate_cat.shape[0]

    heads_here = heads_width // HD
    score_scale = HD ** (-0.5)
    first_norm_scale = side_weight[:, 0].astype(f32)
    second_norm_scale = side_weight[:, 1].astype(f32)
    mix_f = side_weight[:, 2].astype(f32)
    router_f = side_weight[:, 3 : 3 + expert_count].astype(f32)
    layer_input = tokens.astype(f32)
    normed_wide, norm_one = norm_forward(layer_input, first_norm_scale)
    normed_one = normed_wide.astype(bf16)
    query_at = offset + jnp.arange(rows_here, dtype=jnp.int32)
    key_at = offset - 2 * rows_here + jnp.arange(3 * rows_here, dtype=jnp.int32)
    query_seg, query_pos = sequence_info(lengths, query_at)
    key_seg, _ = sequence_info(lengths, key_at)
    cosine, sine = rope_tables(query_pos, HD)
    projected = jnp.dot(normed_one, qkv_weight, preferred_element_type=f32)
    projected = projected.reshape(rows_here, 3, heads_here, HD)
    queries = rotate(projected[:, 0], cosine, sine).astype(bf16)
    keys = rotate(projected[:, 1], cosine, sine).astype(bf16)
    values = projected[:, 2].astype(bf16)
    carried = jnp.stack([keys, values], axis=0)
    joined = jnp.concatenate(
        [passed_along(carried, "ep", 2), passed_along(carried, "ep", 1), carried], axis=1
    )
    keys_win = joined[0]
    values_win = joined[1]
    allowed = (
        (query_seg[:, None] == key_seg[None, :])
        & (key_at[None, :] <= query_at[:, None])
        & (key_at[None, :] >= 0)
    )
    scores = (
        jnp.einsum("qhd,khd->hqk", queries, keys_win, preferred_element_type=f32) * score_scale
    )
    masked = jnp.where(allowed[None], scores, -1e30)
    peak = jnp.max(masked, axis=-1, keepdims=True)
    expo = jnp.exp(masked - peak)
    total = jnp.sum(expo, axis=-1, keepdims=True)
    log_total = peak + jnp.log(total)
    weights = expo / total
    attended = jnp.einsum(
        "hqk,khd->qhd", weights.astype(bf16), values_win, preferred_element_type=f32
    )
    attended = attended.reshape(rows_here, heads_width).astype(bf16)
    attn_part = jnp.einsum("th,dh->td", attended, output_weight, preferred_element_type=f32)
    resid = my_rows(layer_input) + sum_over_tp(attn_part)
    normed_two_wide, norm_two = norm_forward(resid, second_norm_scale)
    normed_two = normed_two_wide.astype(bf16)

    (
        normed_all,
        weighted_h,
        d_pair_pre,
        block_rows,
        d_resid_low,
        d_resid,
        grad_gain_two,
        d_side,
    ) = ffn_over_all(
        normed_two,
        upstream_all,
        pair_cat,
        down_cat,
        side_weight,
        resid,
        second_norm_scale[None, :],
        (slot_here, slot_hidden, shared_units),
        expert_count,
    )
    grad_side = jnp.dot(normed_two.astype(f32).T, d_side, precision=highest)
    grad_out = jnp.einsum("td,th->dh", d_resid_low, attended, preferred_element_type=f32)
    grad_out = lax.psum_scatter(
        grad_out.astype(bf16), "ep", scatter_dimension=0, tiled=True
    ).astype(f32)
    def by_head(array):
        return array.transpose(1, 0, 2)

    place_in_row = (query_seg[None, :], jnp.where(key_at >= 0, key_seg, -1)[:, None])
    places = place_in_row + (query_at[None, :], key_at[:, None])
    tile_shape = (ep_count, rows_here, -1)
    tiles_of = tuple(
        array.reshape(tile_shape) for array in (normed_all, d_pair_pre, upstream_all, weighted_h)
    )
    units = (slot_here, slot_hidden, shared_units)
    column = jnp.arange(128, dtype=jnp.int32)
    large = (
        d_resid_low,
        joined_weights,
        by_head(queries),
        by_head(keys_win),
        by_head(values_win),
        normed_one.T,
        block_rows,
    )
    in_place = (
        log_total.reshape(heads_here, 1, rows_here),
        *places,
        cosine[:, 0],
        sine[:, 0],
        my_rows(tokens),
        first_norm_scale[None, :],
        d_resid,
        grad_gain_two[None, :],
        jnp.where(column >= 2, grad_side, 0.0),
    )
    grad_weights, small, block_out, grad_tokens, grad_pieces, grad_experts = backward(
        large, tiles_of, in_place, units, score_scale
    )
    grad_shared = shared_whole(grad_pieces, 3)
    grad_tokens = grad_tokens.astype(f32)
    grad_experts = [grad.astype(f32).reshape(expert_gate.shape) for grad in grad_experts]
    parts = [grad_weights[:, i * heads_width : (i + 1) * heads_width] for i in range(3)]
    return (
        block_out,
        grad_tokens,
        small[:, 0],
        parts[0],
        parts[1],
        parts[2],
        grad_out,
        small[:, 1],
        small[:, 3 : 3 + expert_count],
        small[:, 2],
        grad_shared[0],
        grad_shared[1],
        grad_shared[2],
        grad_experts[0],
        grad_experts[1],
        grad_experts[2],
    )


def chosen_body(*arrays):
    rows_here, top_count = arrays[2].shape
    slot_here, expert_count = arrays[14].shape[0], arrays[9].shape[1]
    capacity = rows_here * top_count * 7 // (5 * expert_count)
    grid_of_two = lax.axis_size("ep") % 2 == 0 and lax.axis_size("tp") == 4
    if grid_of_two and rows_here < 2 * slot_here * capacity:
        return dense_body(*arrays)
    return body(*arrays)


def solution(mesh):
    placed = (
        P("ep", None),
        P(),
        P("ep", None),
        P("ep"),
        P("ep", "tp"),
        P("ep", "tp"),
        P("ep", "tp"),
        P("ep", "tp"),
        P("ep"),
        P("ep", None),
        P("ep"),
        P("ep", "tp"),
        P("ep", "tp"),
        P("ep", "tp"),
        P("ep", "tp", None),
        P("ep", "tp", None),
        P("ep", "tp", None),
        P("ep", None),
    )
    return jax.shard_map(
        chosen_body,
        mesh=mesh,
        in_specs=placed,
        out_specs=(
            P("ep", None),
            P("ep", None),
            P("ep"),
            P("ep", "tp"),
            P("ep", "tp"),
            P("ep", "tp"),
            P("ep", "tp"),
            P("ep"),
            P("ep", None),
            P("ep"),
            P("ep", "tp"),
            P("ep", "tp"),
            P("ep", "tp"),
            P("ep", "tp", None),
            P("ep", "tp", None),
            P("ep", "tp", None),
        ),
        check_vma=False,
    )
```

```python
import functools

import jax
import jax.numpy as jnp
from jax import lax
from jax.experimental import pallas as pl
from jax.experimental.pallas import tpu as pltpu
from jax.sharding import PartitionSpec as P

HD = 128


epsilon = 1e-06
rope_base = 1000000.0
highest = lax.Precision.HIGHEST
MESH = pl.DeviceIdType.MESH


def passed_along(block, axis, distance):
    devices = range(lax.axis_size(axis))
    route = [(i - distance, i) for i in devices if i - distance in devices]
    return lax.ppermute(block, axis, route)


def rope_tables(positions, width):
    steps = jnp.arange(0, width, 2, dtype=jnp.float32) / width
    inverse = rope_base ** (-steps)
    angles = positions.astype(jnp.float32)[:, None] * inverse[None, :]
    angles = jnp.concatenate([angles, angles], axis=-1)
    return (jnp.cos(angles)[:, None, :], jnp.sin(angles)[:, None, :])


def turn_half(values):
    middle = values.shape[-1] // 2
    return jnp.concatenate([-values[..., middle:], values[..., :middle]], axis=-1)


def rotate(values, cosine, sine):
    return values * cosine + turn_half(values) * sine


def unrotate(grads, cosine, sine):
    return grads * cosine - turn_half(grads * sine)


def sequence_info(lengths, indices):
    starts = jnp.cumsum(lengths) - lengths
    inside = starts[None, :] <= indices[:, None]
    segment = jnp.sum(inside.astype(jnp.int32), axis=1) - 1
    first = jnp.max(jnp.where(inside, starts[None, :], -1), axis=1)
    return (segment, indices - first)


def norm_forward(values, gain):
    scale = lax.rsqrt(jnp.mean(values * values, axis=-1, keepdims=True) + epsilon)
    return (values * scale * gain, scale)


def norm_backward(values, scale, gain, grads):
    unit = values * scale
    scaled = grads * gain
    inner = jnp.mean(scaled * unit, axis=-1, keepdims=True)
    return (scale * (scaled - unit * inner), jnp.sum(grads * unit, axis=0))


def deliver(rows):
    arrived_rows = lax.all_to_all(rows, "ep", split_axis=0, concat_axis=0, tiled=True)
    return arrived_rows


def bring_back(parts, target, rows_here, top_count):
    moved = lax.all_to_all(parts, "ep", split_axis=0, concat_axis=0, tiled=True)
    piece = moved.shape[3]
    return moved.reshape(-1, piece)[target].reshape(rows_here, top_count, piece)


def body(
    tokens,
    lengths,
    routes,
    attn_gain,
    w_query,
    w_key,
    w_value,
    w_out,
    ffn_gain,
    w_router,
    shared_mix,
    shared_gate,
    shared_up,
    shared_down,
    expert_gate,
    expert_up,
    expert_down,
    cotangent,
):
    rows_here = tokens.shape[0]
    width = tokens.shape[1]
    ep_count = lax.axis_size("ep")
    offset = lax.axis_index("ep") * rows_here
    slot_here = expert_gate.shape[0]
    top_count = routes.shape[1]
    gathered = (
        lax.all_gather(attn_gain, "ep", axis=0, tiled=True),
        lax.all_gather(w_query, "ep", axis=0, tiled=True),
        lax.all_gather(w_key, "ep", axis=0, tiled=True),
        lax.all_gather(w_value, "ep", axis=0, tiled=True),
        lax.all_gather(w_out, "ep", axis=0, tiled=True),
        lax.all_gather(ffn_gain, "ep", axis=0, tiled=True),
        lax.all_gather(w_router, "ep", axis=0, tiled=True),
        lax.all_gather(shared_mix, "ep", axis=0, tiled=True),
        lax.all_gather(shared_gate, "ep", axis=0, tiled=True),
        lax.all_gather(shared_up, "ep", axis=0, tiled=True),
        lax.all_gather(shared_down, "ep", axis=0, tiled=True),
    )
    (
        gain_first,
        query_weight_matrix,
        key_weight_matrix,
        value_weight_matrix,
        output_weight,
        gain_second,
        router_weight,
        shared_mixer_weight,
        shared_gate_weight,
        shared_up_weight,
        shared_down_weight,
    ) = gathered
    expert_count = router_weight.shape[1]
    capacity = (rows_here * top_count * 7 // (5 * expert_count) + 7) // 8 * 8
    heads_here = query_weight_matrix.shape[1] // HD
    score_scale = HD ** (-0.5)
    first_norm_scale = gain_first.astype(jnp.float32)
    second_norm_scale = gain_second.astype(jnp.float32)
    layer_input = tokens.astype(jnp.float32)
    normed_wide, norm_one = norm_forward(layer_input, first_norm_scale)
    normed_one = normed_wide.astype(jnp.bfloat16)
    query_at = offset + jnp.arange(rows_here, dtype=jnp.int32)
    key_at = offset - 2 * rows_here + jnp.arange(3 * rows_here, dtype=jnp.int32)
    query_seg, query_pos = sequence_info(lengths, query_at)
    key_seg, _ = sequence_info(lengths, key_at)
    cosine, sine = rope_tables(query_pos, HD)
    query_pre = jnp.dot(
        normed_one, query_weight_matrix, preferred_element_type=jnp.float32
    ).reshape(rows_here, heads_here, HD)
    key_pre = jnp.dot(normed_one, key_weight_matrix, preferred_element_type=jnp.float32).reshape(
        rows_here, heads_here, HD
    )
    queries = rotate(query_pre, cosine, sine).astype(jnp.bfloat16)
    keys = rotate(key_pre, cosine, sine).astype(jnp.bfloat16)
    values = (
        jnp.dot(normed_one, value_weight_matrix, preferred_element_type=jnp.float32)
        .astype(jnp.bfloat16)
        .reshape(rows_here, heads_here, HD)
    )
    carried = jnp.stack([keys, values], axis=0)
    window = [carried]
    for hop in range(2):
        carried = passed_along(carried, "ep", 1)
        window = [carried] + window
    joined = jnp.concatenate(window, axis=1)
    keys_win = joined[0]
    values_win = joined[1]
    allowed = (
        (query_seg[:, None] == key_seg[None, :])
        & (key_at[None, :] <= query_at[:, None])
        & (key_at[None, :] >= 0)
    )
    scores = (
        jnp.einsum("qhd,khd->hqk", queries, keys_win, preferred_element_type=jnp.float32)
        * score_scale
    )
    masked = jnp.where(allowed[None], scores, -1e30)
    peak = jnp.max(masked, axis=-1, keepdims=True)
    expo = jnp.exp(masked - peak)
    total = jnp.sum(expo, axis=-1, keepdims=True)
    log_total = peak + jnp.log(total)
    weights = expo / total
    attended = jnp.einsum(
        "hqk,khd->qhd", weights.astype(jnp.bfloat16), values_win, preferred_element_type=jnp.float32
    )
    attended = attended.reshape(rows_here, heads_here * HD).astype(jnp.bfloat16)
    attn_part = jnp.einsum("th,dh->td", attended, output_weight, preferred_element_type=jnp.float32)
    resid = layer_input + lax.psum(attn_part, "tp")
    normed_two_wide, norm_two = norm_forward(resid, second_norm_scale)
    normed_two = normed_two_wide.astype(jnp.bfloat16)
    normed_two_f = normed_two.astype(jnp.float32)
    router_f = router_weight.astype(jnp.float32)
    mix_f = shared_mixer_weight.astype(jnp.float32)
    router = jax.nn.softmax(jnp.dot(normed_two_f, router_f, precision=highest), axis=-1)
    picked = routes[:, :, None] == jnp.arange(expert_count, dtype=jnp.int32)[None, None, :]
    gates = jnp.sum(jnp.where(picked, router[:, None, :], 0.0), axis=-1)
    mixer = jax.nn.sigmoid(jnp.dot(normed_two_f, mix_f, precision=highest))
    shared_g = jnp.dot(normed_two, shared_gate_weight, preferred_element_type=jnp.float32)
    shared_u = jnp.dot(normed_two, shared_up_weight, preferred_element_type=jnp.float32)
    shared_h = (jax.nn.silu(shared_g) * shared_u).astype(jnp.bfloat16)
    shared_part = jnp.einsum(
        "tf,df->td", shared_h, shared_down_weight, preferred_element_type=jnp.float32
    )
    flat = routes.reshape(-1)
    hot = (flat[:, None] == jnp.arange(expert_count, dtype=jnp.int32)[None, :]).astype(jnp.int32)
    rank = jnp.sum(jnp.cumsum(hot, axis=0) * hot, axis=1) - 1
    target = flat * capacity + rank
    slot_total = ep_count * slot_here * capacity
    owner_route = (
        jnp.zeros((slot_total,), jnp.int32)
        .at[target]
        .set(jnp.arange(rows_here * top_count, dtype=jnp.int32))
    )
    filled = jnp.zeros((slot_total,), jnp.bool_).at[target].set(True)
    owner_token = owner_route // top_count
    send_rows = jnp.where(filled[:, None], normed_two[owner_token], jnp.zeros((), jnp.bfloat16))
    arrived_rows = deliver(send_rows.reshape(ep_count, slot_here, capacity, width))
    route_g = jnp.einsum(
        "nscd,sfd->nscf", arrived_rows, expert_gate, preferred_element_type=jnp.float32
    )
    route_u = jnp.einsum(
        "nscd,sfd->nscf", arrived_rows, expert_up, preferred_element_type=jnp.float32
    )
    route_h = (jax.nn.silu(route_g) * route_u).astype(jnp.bfloat16)
    route_part = jnp.einsum(
        "nscf,sfd->nscd", route_h, expert_down, preferred_element_type=jnp.float32
    )
    back_rows = bring_back(route_part, target, rows_here, top_count)
    upstream = cotangent.astype(jnp.float32)
    routed = jnp.sum(back_rows * gates[:, :, None], axis=1)
    ffn_part = mixer[:, None] * shared_part + routed
    route_dot = jnp.sum(back_rows * upstream[:, None, :], axis=-1)
    shared_dot = jnp.sum(shared_part * upstream, axis=-1)
    ffn_total, d_gate, d_mixer = lax.psum((ffn_part, route_dot, shared_dot), "tp")
    block_out = (resid + ffn_total).astype(jnp.bfloat16)
    d_router = jnp.sum(jnp.where(picked, d_gate[:, :, None], 0.0), axis=1)
    d_logits = router * (d_router - jnp.sum(router * d_router, axis=-1, keepdims=True))
    d_mixlogit = d_mixer * mixer * (1.0 - mixer)
    side = jnp.dot(d_logits, router_f.T, precision=highest) + d_mixlogit[:, None] * mix_f[None, :]
    grad_router = jnp.dot(normed_two_f.T, d_logits, precision=highest)
    grad_mix = jnp.dot(d_mixlogit, normed_two_f, precision=highest)
    d_shared = (mixer[:, None] * upstream).astype(jnp.bfloat16)
    d_sh = jnp.dot(d_shared, shared_down_weight, preferred_element_type=jnp.float32)
    sig_shared = jax.nn.sigmoid(shared_g)
    d_sg = (d_sh * shared_u * sig_shared * (1.0 + shared_g * (1.0 - sig_shared))).astype(
        jnp.bfloat16
    )
    d_su = (d_sh * shared_g * sig_shared).astype(jnp.bfloat16)
    d_normed_part = jnp.einsum(
        "tf,df->td", d_sg, shared_gate_weight, preferred_element_type=jnp.float32
    )
    d_normed_part = d_normed_part + jnp.einsum(
        "tf,df->td", d_su, shared_up_weight, preferred_element_type=jnp.float32
    )
    grad_sgate = jnp.einsum("td,tf->df", normed_two, d_sg, preferred_element_type=jnp.float32)
    grad_sup = jnp.einsum("td,tf->df", normed_two, d_su, preferred_element_type=jnp.float32)
    grad_sdown = jnp.einsum("td,tf->df", d_shared, shared_h, preferred_element_type=jnp.float32)
    d_route = (
        (gates[:, :, None] * upstream[:, None, :])
        .astype(jnp.bfloat16)
        .reshape(rows_here * top_count, width)
    )
    send_grads = jnp.where(filled[:, None], d_route[owner_route], jnp.zeros((), jnp.bfloat16))
    received_grads = deliver(send_grads.reshape(ep_count, slot_here, capacity, width))
    d_rh = jnp.einsum(
        "nscd,sfd->nscf", received_grads, expert_down, preferred_element_type=jnp.float32
    )
    sig_route = jax.nn.sigmoid(route_g)
    d_rg = (d_rh * route_u * sig_route * (1.0 + route_g * (1.0 - sig_route))).astype(jnp.bfloat16)
    routed_up_gradient = (d_rh * route_g * sig_route).astype(jnp.bfloat16)
    row_grads = jnp.einsum("nscf,sfd->nscd", d_rg, expert_gate, preferred_element_type=jnp.float32)
    row_grads = row_grads + jnp.einsum(
        "nscf,sfd->nscd", routed_up_gradient, expert_up, preferred_element_type=jnp.float32
    )
    grad_egate = jnp.einsum(
        "qxba,qxbr->xar", d_rg, arrived_rows, preferred_element_type=jnp.float32
    )
    expert_up_gradient = jnp.einsum(
        "qxba,qxbr->xar", routed_up_gradient, arrived_rows, preferred_element_type=jnp.float32
    )
    grad_edown = jnp.einsum(
        "qxba,qxbr->xar", route_h, received_grads, preferred_element_type=jnp.float32
    )
    grads_back = bring_back(row_grads, target, rows_here, top_count)
    d_routed = jnp.sum(grads_back, axis=1)
    d_normed_two = lax.psum(d_normed_part + d_routed, "tp") + side
    d_resid_norm, grad_gain_two = norm_backward(resid, norm_two, second_norm_scale, d_normed_two)
    d_resid = upstream + d_resid_norm
    d_resid_low = d_resid.astype(jnp.bfloat16)
    grad_outw = jnp.einsum("td,th->dh", d_resid_low, attended, preferred_element_type=jnp.float32)
    d_attended = jnp.einsum(
        "td,dh->th", d_resid_low, output_weight, preferred_element_type=jnp.float32
    )
    d_attended = d_attended.astype(jnp.bfloat16).reshape(rows_here, heads_here, HD)
    scores_again = (
        jnp.einsum("qhd,khd->hqk", queries, keys_win, preferred_element_type=jnp.float32)
        * score_scale
    )
    probs = jnp.where(allowed[None], jnp.exp(scores_again - log_total), 0.0)
    d_probs = jnp.einsum("qhd,khd->hqk", d_attended, values_win, preferred_element_type=jnp.float32)
    delta = jnp.sum(probs * d_probs, axis=-1, keepdims=True)
    d_scores = (probs * (d_probs - delta)).astype(jnp.bfloat16)
    d_queries = (
        jnp.einsum("hqk,khd->qhd", d_scores, keys_win, preferred_element_type=jnp.float32)
        * score_scale
    )
    d_keys_win = (
        jnp.einsum("hqk,qhd->khd", d_scores, queries, preferred_element_type=jnp.float32)
        * score_scale
    )
    d_values_win = jnp.einsum(
        "hqk,qhd->khd", probs.astype(jnp.bfloat16), d_attended, preferred_element_type=jnp.float32
    )
    pair_grads = jnp.stack([d_keys_win, d_values_win], axis=0)
    older = pair_grads[:, :rows_here]
    later = [pair_grads[:, rows_here : 2 * rows_here], pair_grads[:, 2 * rows_here :]]
    running = older
    for hop in range(2):
        running = passed_along(running, "ep", -1)
        running = running + later[hop]
    d_query_pre = (
        unrotate(d_queries, cosine, sine).astype(jnp.bfloat16).reshape(rows_here, heads_here * HD)
    )
    d_key_pre = (
        unrotate(running[0], cosine, sine).astype(jnp.bfloat16).reshape(rows_here, heads_here * HD)
    )
    d_values = running[1].astype(jnp.bfloat16).reshape(rows_here, heads_here * HD)
    grad_queryw = jnp.einsum(
        "td,th->dh", normed_one, d_query_pre, preferred_element_type=jnp.float32
    )
    grad_keyw = jnp.einsum("td,th->dh", normed_one, d_key_pre, preferred_element_type=jnp.float32)
    grad_valuew = jnp.einsum("td,th->dh", normed_one, d_values, preferred_element_type=jnp.float32)
    d_normed_one = jnp.einsum(
        "th,dh->td", d_query_pre, query_weight_matrix, preferred_element_type=jnp.float32
    )
    d_normed_one = d_normed_one + jnp.einsum(
        "th,dh->td", d_key_pre, key_weight_matrix, preferred_element_type=jnp.float32
    )
    d_normed_one = d_normed_one + jnp.einsum(
        "th,dh->td", d_values, value_weight_matrix, preferred_element_type=jnp.float32
    )
    d_normed_one = lax.psum(d_normed_one, "tp")
    d_input_norm, grad_gain_one = norm_backward(
        layer_input, norm_one, first_norm_scale, d_normed_one
    )
    grad_tokens = d_resid + d_input_norm
    summed = (
        lax.psum_scatter(grad_gain_one, "ep", scatter_dimension=0, tiled=True),
        lax.psum_scatter(grad_queryw, "ep", scatter_dimension=0, tiled=True),
        lax.psum_scatter(grad_keyw, "ep", scatter_dimension=0, tiled=True),
        lax.psum_scatter(grad_valuew, "ep", scatter_dimension=0, tiled=True),
        lax.psum_scatter(grad_outw, "ep", scatter_dimension=0, tiled=True),
        lax.psum_scatter(grad_gain_two, "ep", scatter_dimension=0, tiled=True),
        lax.psum_scatter(grad_router, "ep", scatter_dimension=0, tiled=True),
        lax.psum_scatter(grad_mix, "ep", scatter_dimension=0, tiled=True),
        lax.psum_scatter(grad_sgate, "ep", scatter_dimension=0, tiled=True),
        lax.psum_scatter(grad_sup, "ep", scatter_dimension=0, tiled=True),
        lax.psum_scatter(grad_sdown, "ep", scatter_dimension=0, tiled=True),
    )
    return (
        block_out,
        grad_tokens,
        summed[0],
        summed[1],
        summed[2],
        summed[3],
        summed[4],
        summed[5],
        summed[6],
        summed[7],
        summed[8],
        summed[9],
        summed[10],
        grad_egate,
        expert_up_gradient,
        grad_edown,
    )


class Place:
    def __init__(self):
        self.ep, self.tp = lax.axis_index("ep"), lax.axis_index("tp")
        self.z, self.y = self.ep // 2, self.ep % 2
        self.x, self.c = self.tp // 2, self.tp % 2
        self.depth = lax.axis_size("ep") // 2
        self.next_core = (self.ep, self.x * 2 + 1 - self.c)
        self.next_x = (self.ep, (1 - self.x) * 2 + self.c)
        self.next_y = (self.z * 2 + 1 - self.y, self.tp)

    def at_z(self, z):
        return (z * 2 + self.y, self.tp)

    def ahead(self, steps):
        return lax.rem(self.z + steps, self.depth)

    def behind(self, steps):
        return lax.rem(self.z + self.depth - steps, self.depth)

    def greet(self):
        barrier = pltpu.get_barrier_semaphore()
        peers = [self.next_core, self.next_x, self.next_y]
        peers += [self.at_z(self.ahead(k)) for k in range(1, self.depth)]
        for peer in peers:
            pl.semaphore_signal(barrier, inc=1, device_id=peer, device_id_type=MESH)
        pl.semaphore_wait(barrier, len(peers))

    def greet_row(self):
        barrier = pltpu.get_barrier_semaphore()
        count = 2 * self.depth
        peers = [(lax.rem(self.ep + k, count), self.tp) for k in range(1, count)]
        peers += [self.next_core, self.next_x]
        for peer in peers:
            pl.semaphore_signal(barrier, inc=1, device_id=peer, device_id_type=MESH)
        pl.semaphore_wait(barrier, len(peers))

    def greet_ep(self):
        barrier = pltpu.get_barrier_semaphore()
        count = 2 * self.depth
        for k in range(1, count):
            peer = (lax.rem(self.ep + k, count), self.tp)
            pl.semaphore_signal(barrier, inc=1, device_id=peer, device_id_type=MESH)
        pl.semaphore_wait(barrier, count - 1)


def remote(src, dst, send, recv, peer):
    return pltpu.make_async_remote_copy(
        src_ref=src, dst_ref=dst, send_sem=send, recv_sem=recv, device_id=peer, device_id_type=MESH
    )


def ffn_kernel(
    units,
    expert_count,
    rows_in,
    upstream_in,
    pair_in,
    down_in,
    side_in,
    resid_in,
    gain_in,
    rows_all,
    weighted_out,
    d_pair_out,
    block_out,
    d_resid_low_out,
    d_resid_out,
    d_gain_out,
    d_side_out,
    d_rows_sum,
    out_sum,
    pair_w,
    down_w,
    side_w,
    rows_tile,
    upstream_tile,
    pair_pre,
    d_hidden,
    factors,
    dots,
    weighted_tile,
    d_pair_tile,
    own_rows,
    own_upstream,
    d_resid_low,
    d_rows_tile,
    out_tile,
    d_rows_core,
    out_core,
    d_rows_held,
    out_held,
    d_rows_hop,
    out_hop,
    d_rows_hop2,
    out_hop2,
    d_rows_z,
    out_z,
    d_rows_to_z,
    out_to_z,
    gathered_send,
    gathered_recv,
    hop_send,
    hop_recv,
    weight_sem,
    own_sem,
    z_send,
    z_recv,
    plane_send,
    plane_recv,
    load_sem,
    store_sem,
    sum_send,
    sum_recv,
    end_send,
    end_recv,
    core_credit,
    hop_credit,
    hop2_credit,
):
    at = Place()
    depth = at.depth
    quarter, width = rows_in.shape
    half = quarter // 2
    f32, bf16 = jnp.float32, jnp.bfloat16

    def weight_copies():
        pairs = (
            (pair_in, pair_w),
            (down_in, down_w),
            (side_in, side_w),
            (rows_in, own_rows),
            (upstream_in.at[at.z, at.y, at.x, at.c], own_upstream),
        )
        return [
            pltpu.make_async_copy(src, dst, weight_sem.at[i]) for i, (src, dst) in enumerate(pairs)
        ]

    for copy in weight_copies():
        copy.start()

    def block(j, y, x):
        return rows_all.at[at.behind(j), y, x, at.c]

    def plane_copy(j, kind):
        y, other_y = at.y, 1 - at.y
        own, other_x = at.x, 1 - at.x
        if kind == 0:
            src, peer = block(j, y, own), at.next_x
        elif kind == 1:
            src, peer = block(j, y, own), at.next_y
        elif kind == 2:
            src, peer = block(j, y, other_x).at[pl.ds(0, half)], at.next_y
        elif kind == 3:
            src, peer = block(j, other_y, own).at[pl.ds(half, half)], at.next_x
        else:
            src = block(j, other_y if kind >= 6 else y, other_x if kind % 2 else own)
            peer = at.next_core
        return remote(src, src, plane_send.at[j, kind], plane_recv.at[j, kind], peer)

    def z_copy(k):
        return remote(
            rows_in, block(0, at.y, at.x), z_send.at[k - 1], z_recv.at[k - 1], at.at_z(at.ahead(k))
        )

    def z_arrival(k):
        dst = block(k, at.y, at.x)
        return remote(dst, dst, z_send.at[k - 1], z_recv.at[k - 1], at.at_z(at.behind(k)))

    def begin(j):
        for kind in (0, 1, 4):
            plane_copy(j, kind).start()

    def spread(j):
        plane_copy(j, 0).wait_recv()
        plane_copy(j, 2).start()
        plane_copy(j, 5).start()
        plane_copy(j, 1).wait_recv()
        plane_copy(j, 3).start()
        plane_copy(j, 6).start()

    def begin_later(j):
        z_arrival(j).wait_recv()
        begin(j)

    def last_hop(j):
        plane_copy(j, 2).wait_recv()
        plane_copy(j, 3).wait_recv()
        plane_copy(j, 7).start()

    def near_ready(j):
        plane_copy(j, 4).wait_recv()
        plane_copy(j, 5).wait_recv()

    def far_ready(j):
        plane_copy(j, 6).wait_recv()
        plane_copy(j, 7).wait_recv()

    def parity(step):
        return lax.rem(step, 2)

    def slot_of(turn):
        return lax.rem(turn + 1, depth)

    def other_y(step):
        return lax.rem(parity(step) + (step // 2 + 1) // depth, 2)

    def tile_at(step):
        return at.behind(slot_of(step // 2)), lax.rem(at.y + other_y(step), 2)

    def load_rows(step):
        z, y = tile_at(step)
        return pltpu.make_async_copy(rows_all.at[z, y], rows_tile, load_sem.at[0])

    def load_upstream(step):
        z, y = tile_at(step)
        return pltpu.make_async_copy(upstream_in.at[z, y], upstream_tile, load_sem.at[1])

    def stores(step):
        z, y = tile_at(step)
        pairs = ((weighted_tile, weighted_out), (d_pair_tile, d_pair_out))
        return [
            pltpu.make_async_copy(src, dst.at[z, y], store_sem.at[i])
            for i, (src, dst) in enumerate(pairs)
        ]

    tiles, cores = (d_rows_tile, out_tile), (d_rows_core, out_core)
    helds, sums = (d_rows_held, out_held), (d_rows_sum, out_sum)
    hops, hops2, zs = (d_rows_hop, out_hop), (d_rows_hop2, out_hop2), (d_rows_z, out_z)
    to_zs = (d_rows_to_z, out_to_z)

    def sum_copy(a, kind, src, dst, peer):
        return remote(src, dst, sum_send.at[a, kind], sum_recv.at[a, kind], peer)

    def core_sum(a):
        return sum_copy(a, 0, tiles[a].at[:, 1 - at.c], cores[a], at.next_core)

    def row_hop(turn, other):
        y = lax.rem(at.y + other, 2)
        src = d_rows_held.at[parity(turn), y, 1 - at.x]
        return remote(src, d_rows_hop.at[y], hop_send.at[other], hop_recv.at[other], at.next_x)

    def out_hop_sum(turn):
        return sum_copy(1, 1, out_held.at[parity(turn), 1 - at.y], out_hop, at.next_y)

    def hop2_sum(a, turn):
        slot = parity(turn)
        if a == 0:
            src, peer = helds[0].at[slot, 1 - at.y, at.x], at.next_y
        else:
            src, peer = helds[1].at[slot, at.y, 1 - at.x], at.next_x
        return sum_copy(a, 2, src, hops2[a], peer)

    def z_sum(a, turn):
        return remote(
            to_zs[a].at[turn],
            zs[a].at[turn],
            end_send.at[a, turn],
            end_recv.at[a, turn],
            at.at_z(at.behind(turn + 1)),
        )

    def allow(semaphore, peer):
        pl.semaphore_signal(semaphore, inc=1, device_id=peer, device_id_type=MESH)

    piece = 32

    def add(into, first, second):
        def body(i, carry):
            part = pl.ds(pl.multiple_of(i * piece, piece), piece)
            into[part] = first[part] + second[part]
            return carry

        lax.fori_loop(0, quarter // piece, body, 0)

    def after_core(step):
        turn = step // 2
        other = other_y(step)
        held, y = parity(turn), lax.rem(at.y + other, 2)

        @pl.when((parity(step) == 0) & (turn >= 1))
        def _():
            for a in (0, 1):
                pl.semaphore_wait(hop_credit.at[a], 1)

        for a in (0, 1):
            core_sum(a).wait()
            for x in (1 - at.x, at.x):
                add(helds[a].at[held, y, x], tiles[a].at[x, at.c], cores[a].at[x])
            if a == 0:
                row_hop(turn, other).start()
            else:

                @pl.when(other == 1)
                def _():
                    out_hop_sum(turn).start()

        @pl.when(step + 1 < 2 * depth)
        def _():
            allow(core_credit, at.next_core)

    def after_row_hop(turn, other):
        slot, y = parity(turn), lax.rem(at.y + other, 2)
        row_hop(turn, other).wait()
        into = d_rows_held.at[slot, y, at.x]
        add(into, into, d_rows_hop.at[y])

    def after_out_hop(turn):
        slot = parity(turn)
        out_hop_sum(turn).wait()
        for x in (1 - at.x, at.x):
            into = out_held.at[slot, at.y, x]
            add(into, into, out_hop.at[x])

    def may_hop2(turn, a):
        @pl.when(turn >= 1)
        def _():
            pl.semaphore_wait(hop2_credit.at[a], 1)

    def after_hop(turn):
        after_row_hop(turn, 1)
        may_hop2(turn, 0)
        hop2_sum(0, turn).start()
        after_row_hop(turn, 0)
        after_out_hop(turn)
        may_hop2(turn, 1)
        hop2_sum(1, turn).start()
        allow(hop_credit.at[0], at.next_x)
        allow(hop_credit.at[1], at.next_y)

    def after_hop2(turn):
        slot = parity(turn)
        for a in (0, 1):
            hop2_sum(a, turn).wait()
            add(to_zs[a].at[turn], helds[a].at[slot, at.y, at.x], hops2[a])
            z_sum(a, turn).start()
        allow(hop2_credit.at[0], at.next_y)
        allow(hop2_credit.at[1], at.next_x)

    load_upstream(0).start()
    at.greet()
    z_copy(1).start()
    own_copy = pltpu.make_async_copy(rows_in, block(0, at.y, at.x), own_sem)
    own_copy.start()
    own_copy.wait()
    begin(0)
    begin_later(1)
    for k in range(2, depth):
        z_copy(k).start()
    spread(0)
    spread(1)
    near_ready(1)
    load_rows(0).start()
    for copy in weight_copies():
        copy.wait()

    tile_rows = 4 * quarter
    hidden_total = down_w.shape[0]
    lane = lax.broadcasted_iota(jnp.int32, (tile_rows, 128), 1)
    slot_here, slot_hidden, shared_hidden = units
    routed = slot_here * slot_hidden
    across = (((1,), (1,)), ((), ()))
    few = 16

    def gate_factors(rows, picked):
        logits = jnp.dot(rows, side_w[...], preferred_element_type=f32)
        chooses = (lane >= 3) & (lane < 3 + expert_count)
        peak = jnp.max(jnp.where(chooses, logits, -1e30), axis=1, keepdims=True)
        expo = jnp.where(chooses, jnp.exp(jnp.where(chooses, logits, peak) - peak), 0.0)
        routed_gate = expo / jnp.sum(expo, axis=1, keepdims=True) * picked.astype(f32)
        mix_pre = jnp.sum(jnp.where(lane == 2, logits, 0.0), axis=1, keepdims=True)
        result = jnp.where(lane == slot_here, 1.0 / (1.0 + jnp.exp(-mix_pre)), 0.0)
        for s in range(slot_here):
            chosen = lane == 3 + at.ep * slot_here + s
            gate = jnp.sum(jnp.where(chosen, routed_gate, 0.0), axis=1, keepdims=True)
            result = jnp.where(lane == s, gate, result)
        return result

    few_lane = lax.broadcasted_iota(jnp.int32, (few, 128), 1)
    bounds = [s * slot_hidden for s in range(slot_here)] + [routed, hidden_total]

    def owners(group):
        found = []
        for s in range(slot_here + 1):
            low, high = max(bounds[s] - group * 128, 0), min(bounds[s + 1] - group * 128, 128)
            if low < high:
                found.append((s, low, high))
        return found

    def hidden_rows(i, carry):
        here = pl.ds(pl.multiple_of(i * few, few), few)
        gates = [
            jnp.broadcast_to(factors[here, s : s + 1], (few, 128)) for s in range(slot_here + 1)
        ]
        parts = [None] * (slot_here + 1)
        for group in range(hidden_total // 128):
            units_here = slice(group * 128, (group + 1) * 128)
            units_up = slice(hidden_total + group * 128, hidden_total + (group + 1) * 128)
            gate_pre, up_pre = pair_pre[here, units_here], pair_pre[here, units_up]
            d_h = d_hidden[here, units_here]
            found = owners(group)
            factor = gates[found[0][0]]
            for s, low, _ in found[1:]:
                factor = jnp.where(few_lane >= low, gates[s], factor)
            sig = 0.5 + 0.5 * jnp.tanh(0.5 * gate_pre)
            silu = gate_pre * sig
            hidden = silu * up_pre
            product = hidden * d_h
            gated = factor * d_h
            weighted_tile[here, units_here] = (factor * hidden).astype(bf16)
            slope = sig + silu * (1.0 - sig)
            d_pair_tile[here, units_here] = (gated * up_pre * slope).astype(bf16)
            d_pair_tile[here, units_up] = (gated * silu).astype(bf16)
            for s, low, high in found:
                mine = product
                if high < 128:
                    mine = jnp.where(few_lane < high, mine, 0.0)
                if low > 0:
                    mine = jnp.where(few_lane >= low, mine, 0.0)
                parts[s] = mine if parts[s] is None else parts[s] + mine
        result = jnp.zeros((few, 128), f32)
        for s in range(slot_here + 1):
            dot = jnp.sum(parts[s], axis=1, keepdims=True)
            where = few_lane == (2 if s == slot_here else 3 + at.ep * slot_here + s)
            result = jnp.where(where, dot, result)
        dots[here] = result.astype(bf16)
        return carry

    def first_half(step):
        load_upstream(step).wait()
        upstream = upstream_tile[...].reshape(tile_rows, upstream_tile.shape[-1])
        d_hidden[...] = lax.dot_general(
            upstream[:, :width], down_w[...], across, preferred_element_type=f32
        )
        load_rows(step).wait()
        rows = rows_tile[...].reshape(tile_rows, width)
        factors[...] = gate_factors(rows, upstream[:, width:])
        pair_pre[...] = lax.dot_general(rows, pair_w[...], across, preferred_element_type=f32)

        @pl.when(step + 1 < 2 * depth)
        def _():
            load_upstream(step + 1).start()

        @pl.when(step >= 1)
        def _():
            for copy in stores(step - 1):
                copy.wait()

        lax.fori_loop(0, tile_rows // few, hidden_rows, 0, unroll=2)
        for copy in stores(step):
            copy.start()
        turn = step // 2

        @pl.when(step == 0)
        def _():
            last_hop(0)

        @pl.when((parity(step) == 0) & (turn + 1 < depth))
        def _():
            last_hop(turn + 1)

        @pl.when((step >= 1) & (step + 1 < depth))
        def _():
            spread(step + 1)

        @pl.when(step + 2 < depth)
        def _():
            begin_later(step + 2)

    def second_half(step):
        blocks = (2, 2, quarter)
        some = width // 2
        for n in range(2):
            columns = slice(n * some, (n + 1) * some)
            part = jnp.dot(weighted_tile[...], down_w[:, columns], preferred_element_type=f32)
            out_tile[:, :, :, columns] = part.astype(bf16).reshape(blocks + (some,))
            part = jnp.dot(d_pair_tile[...], pair_w[:, columns], preferred_element_type=f32)
            d_rows_tile[:, :, :, columns] = part.astype(bf16).reshape(blocks + (some,))
        d_rows_tile[:, :, :, width:] = dots[...].reshape(blocks + (128,))

        @pl.when(step >= 1)
        def _():
            pl.semaphore_wait(core_credit, 1)

        for a in (0, 1):
            core_sum(a).start()
        turn = step // 2

        @pl.when((parity(step) == 0) & (turn + 1 < depth))
        def _():
            far_ready(slot_of(turn))

        @pl.when((parity(step) == 1) & (turn + 1 < depth))
        def _():
            near_ready(slot_of(turn + 1))

        @pl.when(step == 2 * depth - 3)
        def _():
            far_ready(slot_of(turn + 1))

        @pl.when(step + 1 < 2 * depth)
        def _():
            load_rows(step + 1).start()

    def step_body(step, carry):
        first_half(step)

        odd = parity(step) == 1

        @pl.when(odd & (step >= 3))
        def _():
            after_hop((step - 3) // 2)

        @pl.when(jnp.logical_not(odd) & (step >= 4))
        def _():
            after_hop2((step - 4) // 2)

        @pl.when(step >= 1)
        def _():
            after_core(step - 1)

        second_half(step)
        return carry

    lax.fori_loop(0, 2 * depth, step_body, 0)
    last = depth - 1
    after_hop2(last - 1)
    after_row_hop(last, 1)
    may_hop2(last, 0)
    hop2_sum(0, last).start()
    after_core(2 * depth - 1)
    after_out_hop(last)
    may_hop2(last, 1)
    hop2_sum(1, last).start()
    after_row_hop(last, 0)

    def total_of(a):
        hop2_sum(a, last).wait()
        held = helds[a].at[last % 2, at.y, at.x]
        for turn in range(last):
            z_sum(a, turn).wait_recv()

        def total_body(i, carry):
            part = pl.ds(pl.multiple_of(i * piece, piece), piece)
            total = held[part].astype(f32) + hops2[a][part].astype(f32)
            for k in range(last):
                total = total + zs[a][k, part].astype(f32)
            sums[a][part] = total
            return carry

        lax.fori_loop(0, quarter // piece, total_body, 0)

    total_of(0)
    own_lane = lax.broadcasted_iota(jnp.int32, (quarter, 128), 1)
    chooses = (own_lane >= 3) & (own_lane < 3 + expert_count)
    rows = own_rows[...]
    logits = jnp.dot(rows, side_w[...], preferred_element_type=f32)
    peak = jnp.max(jnp.where(chooses, logits, -1e30), axis=1, keepdims=True)
    expo = jnp.where(chooses, jnp.exp(jnp.where(chooses, logits, peak) - peak), 0.0)
    router = expo / jnp.sum(expo, axis=1, keepdims=True)
    mixer = 1.0 / (1.0 + jnp.exp(-jnp.where(own_lane == 2, logits, 0.0)))
    gate_dots = d_rows_sum[:, width:]
    d_router = jnp.where(chooses, gate_dots * own_upstream[:, width:].astype(f32), 0.0)
    d_logits = router * (d_router - jnp.sum(router * d_router, axis=1, keepdims=True))
    d_mix = gate_dots * mixer * (1.0 - mixer)
    d_side = jnp.where(own_lane == 2, d_mix, jnp.where(chooses, d_logits, 0.0))
    d_side_out[...] = d_side
    high = d_side.astype(bf16)
    lower = (d_side - high.astype(f32)).astype(bf16)
    for split in (high, lower):
        d_rows_sum[:, :width] += lax.dot_general(
            split, side_w[...], across, preferred_element_type=f32
        )

    def end_body(i, carry):
        part = pl.ds(pl.multiple_of(i * few, few), few)
        resid = resid_in[part]
        scale = lax.rsqrt(jnp.mean(resid * resid, axis=1, keepdims=True) + epsilon)
        unit_rows = resid * scale
        grads = d_rows_sum[part, :width]
        scaled = grads * gain_in[...]
        inner = jnp.mean(scaled * unit_rows, axis=1, keepdims=True)
        d_resid = own_upstream[part, :width].astype(f32) + scale * (scaled - unit_rows * inner)
        d_resid_out[part] = d_resid
        d_resid_low[part] = d_resid.astype(bf16)
        return carry + jnp.sum(grads * unit_rows, axis=0, keepdims=True)

    d_gain_out[...] = lax.fori_loop(0, quarter // few, end_body, jnp.zeros((1, width), f32))

    def gather_copy(kind):
        if kind == 2:
            src = dst = d_resid_low_out.at[1 - at.x, at.c]
        else:
            src, dst = d_resid_low, d_resid_low_out.at[at.x, at.c]
        peer = at.next_x if kind == 0 else at.next_core
        return remote(src, dst, gathered_send.at[kind], gathered_recv.at[kind], peer)

    own_end = pltpu.make_async_copy(d_resid_low, d_resid_low_out.at[at.x, at.c], own_sem)
    own_end.start()
    for kind in (0, 1):
        gather_copy(kind).start()
    total_of(1)
    block_out[...] = (resid_in[...] + out_sum[...]).astype(bf16)
    gather_copy(0).wait_recv()
    gather_copy(2).start()
    own_end.wait()
    gather_copy(0).wait_send()
    gather_copy(1).wait()
    gather_copy(2).wait()
    for copy in stores(2 * depth - 1):
        copy.wait()
    for a in (0, 1):
        for turn in range(depth - 1):
            z_sum(a, turn).wait_send()
    for k in range(1, depth):
        z_copy(k).wait_send()

    def finish(j, carry):
        for kind in range(8):
            plane_copy(j, kind).wait_send()
        return carry

    lax.fori_loop(0, depth, finish, 0)


def ffn_over_all(rows, upstream_all, pair_w, down_w, side_w, resid, gain, units, expert_count):
    quarter, width = rows.shape
    ep_count, tp_count = lax.axis_size("ep"), lax.axis_size("tp")
    depth = ep_count // 2
    hidden = down_w.shape[0]
    bf16, f32 = jnp.bfloat16, jnp.float32
    wide = width + 128
    tile_rows = tp_count * quarter
    tokens = ep_count * tile_rows
    anywhere = pl.BlockSpec(memory_space=pl.ANY)
    in_vmem = pl.BlockSpec(memory_space=pltpu.VMEM)

    def both(*lead):
        return [pltpu.VMEM(lead + (quarter, columns), bf16) for columns in (wide, width)]

    dma = pltpu.SemaphoreType.DMA
    outs = pl.pallas_call(
        functools.partial(ffn_kernel, units, expert_count),
        out_shape=(
            jax.ShapeDtypeStruct((depth, 2, 2, 2, quarter, width), bf16),
            jax.ShapeDtypeStruct((depth, 2, tile_rows, hidden), bf16),
            jax.ShapeDtypeStruct((depth, 2, tile_rows, 2 * hidden), bf16),
            jax.ShapeDtypeStruct((quarter, width), bf16),
            jax.ShapeDtypeStruct((2, 2, quarter, width), bf16),
            jax.ShapeDtypeStruct((quarter, width), f32),
            jax.ShapeDtypeStruct((1, width), f32),
            jax.ShapeDtypeStruct((quarter, 128), f32),
        ),
        in_specs=[anywhere] * 5 + [in_vmem] * 2,
        out_specs=(anywhere,) * 3 + (in_vmem, anywhere) + (in_vmem,) * 3,
        scratch_shapes=[
            pltpu.VMEM((quarter, wide), f32),
            pltpu.VMEM((quarter, width), f32),
            pltpu.VMEM((2 * hidden, width), bf16),
            pltpu.VMEM((hidden, width), bf16),
            pltpu.VMEM((width, 128), bf16),
            pltpu.VMEM((2, 2, quarter, width), bf16),
            pltpu.VMEM((2, 2, quarter, wide), bf16),
            pltpu.VMEM((tile_rows, 2 * hidden), f32),
            pltpu.VMEM((tile_rows, hidden), f32),
            pltpu.VMEM((tile_rows, 128), f32),
            pltpu.VMEM((tile_rows, 128), bf16),
            pltpu.VMEM((tile_rows, hidden), bf16),
            pltpu.VMEM((tile_rows, 2 * hidden), bf16),
            pltpu.VMEM((quarter, width), bf16),
            pltpu.VMEM((quarter, wide), bf16),
            pltpu.VMEM((quarter, width), bf16),
        ]
        + both(2, 2)
        + both(2)
        + both(2, 2, 2)
        + both(2)
        + both()
        + both(depth - 1)
        + both(depth - 1)
        + [
            dma((3,)),
            dma((3,)),
            dma((2,)),
            dma((2,)),
            dma((5,)),
            dma,
            dma((depth - 1,)),
            dma((depth - 1,)),
            dma((depth, 8)),
            dma((depth, 8)),
            dma((2,)),
            dma((2,)),
            dma((2, 3)),
            dma((2, 3)),
            dma((2, depth - 1)),
            dma((2, depth - 1)),
            pltpu.SemaphoreType.REGULAR,
            pltpu.SemaphoreType.REGULAR((2,)),
            pltpu.SemaphoreType.REGULAR((2,)),
        ],
        compiler_params=pltpu.CompilerParams(
            collective_id=1, has_side_effects=True, vmem_limit_bytes=62 * 2**20
        ),
        cost_estimate=pl.CostEstimate(
            flops=12 * tokens * width * hidden,
            bytes_accessed=10 * tokens * width,
            transcendentals=tokens * hidden,
        ),
        name="ffn_all_tokens",
    )(
        rows,
        upstream_all.reshape(depth, 2, 2, 2, quarter, wide),
        pair_w,
        down_w,
        side_w,
        resid,
        gain,
    )
    rows_all, weighted, d_pair, block_out, d_resid_low, d_resid, d_gain, d_side = outs
    return (
        rows_all.reshape(tokens, width),
        weighted.reshape(tokens, hidden),
        d_pair.reshape(tokens, 2 * hidden),
        block_out,
        d_resid_low.reshape(tile_rows, width),
        d_resid,
        d_gain[0],
        d_side,
    )


def over_tp(block, distance):
    devices = range(lax.axis_size("tp"))
    return lax.ppermute(block, "tp", [(i, i ^ distance) for i in devices])


def one_of(array, index, axis):
    return lax.dynamic_index_in_dim(array, index, axis, keepdims=False)


def sum_over_tp(part):
    rows, columns = part.shape
    tp = lax.axis_index("tp")
    x, c = tp // 2, tp % 2
    blocks = part.reshape(2, 2, rows // 4, columns)
    got = over_tp(one_of(blocks, 1 - c, 1).astype(jnp.bfloat16), 1)
    chip = one_of(blocks, c, 1).astype(jnp.float32) + got.astype(jnp.float32)
    got = over_tp(one_of(chip, 1 - x, 0).astype(jnp.bfloat16), 2)
    return one_of(chip, x, 0) + got.astype(jnp.float32)


def gather_over_tp(block):
    tp = lax.axis_index("tp")
    x, c = tp // 2, tp % 2
    got = over_tp(block, 2)
    pair = jnp.where(x == 0, jnp.stack([block, got]), jnp.stack([got, block]))
    got = over_tp(pair, 1)
    four = jnp.where(c == 0, jnp.stack([pair, got], axis=1), jnp.stack([got, pair], axis=1))
    return four.reshape(4 * block.shape[0], block.shape[1])


def swap_copies(at, pieces_in, pieces_out, send_sem, recv_sem, leave):
    count = 2 * at.depth
    copies = []
    for k in range(1, count):
        to, back = lax.rem(at.ep + k, count), lax.rem(at.ep + count - k, count)
        if leave:
            src, dst, peer = pieces_in.at[to], pieces_out.at[at.ep], to
        else:
            src, dst, peer = pieces_in.at[back], pieces_out.at[back], back
        copies.append(remote(src, dst, send_sem.at[k], recv_sem.at[k], (peer, at.tp)))
    return copies


def weights_kernel(
    own_in,
    pieces_in,
    all_out,
    pieces_out,
    own_sem,
    z_send,
    z_recv,
    y_send,
    y_recv,
    swap_send,
    swap_recv,
):
    at = Place()
    depth = at.depth
    half = own_in.shape[0] // 2
    last = depth - 1

    def block(k, y, h):
        return all_out.at[at.z + k, y, pl.ds(h * half, half)]

    def z_copy(k, h, direction):
        if k == 0:
            src = own_in.at[pl.ds(h * half, half)]
        else:
            src = block(k, at.y, h)
        slot = last + k - direction
        return remote(
            src,
            block(k, at.y, h),
            z_send.at[last + k, h, (direction + 1) // 2],
            z_recv.at[slot, h],
            at.at_z(at.z + direction),
        )

    def z_arrival(k, h):
        direction = 1 if k > 0 else -1
        dst = block(k, at.y, h)
        return remote(
            dst, dst, z_send.at[last + k, h, 0], z_recv.at[last + k, h], at.at_z(at.z + direction)
        )

    def y_copy(k, h):
        src = own_in.at[pl.ds(h * half, half)] if k == 0 else block(k, at.y, h)
        return remote(
            src, block(k, at.y, h), y_send.at[last + k, h], y_recv.at[last + k, h], at.next_y
        )

    own_copies = [
        pltpu.make_async_copy(own_in, all_out.at[at.z, at.y], own_sem.at[0]),
        pltpu.make_async_copy(pieces_in.at[at.ep], pieces_out.at[at.ep], own_sem.at[1]),
    ]
    for copy in own_copies:
        copy.start()
    has_up, has_down = at.z + 1 < depth, at.z > 0
    at.greet_ep()

    for h in (0, 1):
        pl.when(has_up)(lambda: z_copy(0, h, 1).start())
        pl.when(has_down)(lambda: z_copy(0, h, -1).start())
        y_copy(0, h).start()
    swap = (at, pieces_in, pieces_out, swap_send, swap_recv)
    for copy in swap_copies(*swap, True):
        copy.start()
    for k in range(1, depth):
        for h in (0, 1):
            for sign in (-1, 1):
                there = at.z + sign * k
                exists = (there >= 0) & (there < depth)
                onward = at.z - sign
                goes_on = exists & (onward >= 0) & (onward < depth)

                @pl.when(exists)
                def _():
                    z_arrival(sign * k, h).wait_recv()

                @pl.when(goes_on)
                def _():
                    z_copy(sign * k, h, -sign).start()

                @pl.when(exists)
                def _():
                    y_copy(sign * k, h).start()

    for copy in own_copies:
        copy.wait()
    for copy in swap_copies(*swap, False):
        copy.wait_recv()
    for copy in swap_copies(*swap, True):
        copy.wait_send()
    for h in (0, 1):
        pl.when(has_up)(lambda: z_copy(0, h, 1).wait_send())
        pl.when(has_down)(lambda: z_copy(0, h, -1).wait_send())
    for k in range(-last, depth):
        there = at.z + k
        exists = (there >= 0) & (there < depth)
        sign = 1 if k > 0 else -1
        onward = at.z - sign
        goes_on = exists & (onward >= 0) & (onward < depth)
        for h in (0, 1):

            @pl.when(exists)
            def _():
                y_copy(k, h).wait()

            if k != 0:

                @pl.when(goes_on)
                def _():
                    z_copy(k, h, -sign).wait_send()


def gather_over_ep(block, pieces):
    rows, columns = block.shape
    depth = lax.axis_size("ep") // 2
    anywhere = pl.BlockSpec(memory_space=pl.ANY)
    slots = 2 * depth - 1
    out, pieces = pl.pallas_call(
        weights_kernel,
        out_shape=(
            jax.ShapeDtypeStruct((depth, 2, rows, columns), block.dtype),
            jax.ShapeDtypeStruct(pieces.shape, pieces.dtype),
        ),
        in_specs=[anywhere] * 2,
        out_specs=(anywhere,) * 2,
        scratch_shapes=[
            pltpu.SemaphoreType.DMA((2,)),
            pltpu.SemaphoreType.DMA((slots, 2, 2)),
            pltpu.SemaphoreType.DMA((slots, 2)),
            pltpu.SemaphoreType.DMA((slots, 2)),
            pltpu.SemaphoreType.DMA((slots, 2)),
            pltpu.SemaphoreType.DMA((2 * depth,)),
            pltpu.SemaphoreType.DMA((2 * depth,)),
        ],
        compiler_params=pltpu.CompilerParams(collective_id=3, has_side_effects=True),
        cost_estimate=pl.CostEstimate(
            flops=0, bytes_accessed=8 * depth * rows * columns, transcendentals=0
        ),
        name="gather_weights",
    )(block, pieces)
    return out.reshape(2 * depth * rows, columns), pieces


def back_kernel(
    units,
    score_scale,
    d_low_in,
    weights_in,
    q_in,
    k_in,
    v_in,
    turned_in,
    block_in,
    rows_in,
    d_pair_in,
    upstream_in,
    weighted_in,
    lse_in,
    query_start,
    query_at,
    cos_in,
    sin_in,
    own_rows_in,
    gain_in,
    d_resid_in,
    gain_two_in,
    side_in,
    out,
    small_out,
    block_out,
    d_rows_out,
    pieces_got,
    gate_out,
    up_out,
    down_out,
    qkv_w,
    turned,
    d_out,
    d_got,
    d_own,
    d_proj,
    part,
    core_got,
    x_got,
    d_rows,
    own,
    y_out,
    hop,
    from_z,
    small_own,
    small_hop,
    small_z,
    small,
    small_got,
    pieces,
    load_sem,
    d_send,
    d_recv,
    tp_send,
    tp_recv,
    y_send,
    y_recv,
    z_send,
    z_recv,
    little_send,
    little_recv,
    small_send,
    small_recv,
    swap_send,
    swap_recv,
    rows_send,
    rows_recv,
    own_sem,
    tile_sem,
    store_sem,
    strip_sem,
):
    at = Place()
    depth = at.depth
    count = 2 * depth
    heads, tokens, head = q_in.shape
    heads_width = heads * head
    windows = k_in.shape[1] // tokens
    quarter, width = d_rows.shape
    rows = out.shape[0]
    f32, bf16 = jnp.float32, jnp.bfloat16
    across = (((1,), (1,)), ((), ()))
    slot_here, slot_hidden, shared_hidden = units
    routed = slot_here * slot_hidden
    hidden = weighted_in.shape[2]
    few = 16

    def d_copy(w, h):
        peer = (at.ep - (2 - w), at.tp)
        return remote(d_out.at[w, h], d_got.at[w, h], d_send.at[w, h], d_recv.at[w, h], peer)

    def d_arrival(w, h):
        peer = (at.ep + (2 - w), at.tp)
        dst = d_got.at[w, h]
        return remote(dst, dst, d_send.at[w, h], d_recv.at[w, h], peer)

    def core_copy():
        return remote(part.at[:, 1 - at.c], core_got, tp_send.at[0], tp_recv.at[0], at.next_core)

    def x_copy():
        return remote(part.at[1 - at.x, at.c], x_got, tp_send.at[1], tp_recv.at[1], at.next_x)

    cuts = (pl.ds(0, heads_width), pl.ds(heads_width, 2 * heads_width))

    def y_copy(q, j):
        return remote(
            y_out.at[j, :, cuts[q]], hop.at[j, :, cuts[q]], y_send.at[q, j], y_recv.at[q, j], at.next_y
        )

    def z_copy(q, j):
        return remote(
            own.at[j, :, cuts[q]],
            from_z.at[j - 1, :, cuts[q]],
            z_send.at[q, j],
            z_recv.at[q, j],
            at.at_z(at.ahead(j)),
        )

    def little_y(j):
        return remote(
            small_own.at[at.ahead(j), 1 - at.y],
            small_hop.at[j],
            little_send.at[0, j],
            little_recv.at[0, j],
            at.next_y,
        )

    def little_z(j):
        return remote(
            small_own.at[at.ahead(j), at.y],
            small_z.at[j - 1],
            little_send.at[1, j],
            little_recv.at[1, j],
            at.at_z(at.ahead(j)),
        )

    def small_copy(kind):
        peer = at.next_core if kind == 0 else at.next_x
        return remote(
            small.at[kind], small_got.at[kind], small_send.at[kind], small_recv.at[kind], peer
        )

    ends = ((block_in, block_out), (d_rows, d_rows_out))

    def rows_copy(a, kind):
        mine, gathered = ends[a]
        if kind == 2:
            src = dst = gathered.at[1 - at.x, at.c]
        else:
            src, dst = mine, gathered.at[at.x, at.c]
        peer = at.next_x if kind == 0 else at.next_core
        return remote(src, dst, rows_send.at[a, kind], rows_recv.at[a, kind], peer)

    def rows_own(a):
        mine, gathered = ends[a]
        return pltpu.make_async_copy(mine, gathered.at[at.x, at.c], own_sem.at[a])

    def rows_begin(a):
        for kind in (0, 1):
            rows_copy(a, kind).start()
        rows_own(a).start()

    def rows_pass_on(a):
        rows_copy(a, 0).wait_recv()
        rows_copy(a, 2).start()

    def rows_end(a):
        rows_own(a).wait()
        rows_copy(a, 0).wait_send()
        rows_copy(a, 1).wait()
        rows_copy(a, 2).wait()

    def swap_copies(p, leave):
        some = pl.ds(p * shared_hidden, shared_hidden)
        copies = []
        for k in range(1, count):
            to, back = lax.rem(at.ep + k, count), lax.rem(at.ep + count - k, count)
            if leave:
                src, dst, peer = pieces.at[to, some], pieces_got.at[at.ep, some], to
            else:
                src, dst, peer = pieces.at[back, some], pieces_got.at[back, some], back
            copies.append(remote(src, dst, swap_send.at[p, k], swap_recv.at[p, k], (peer, at.tp)))
        return copies

    def swap_own(p):
        some = pl.ds(p * shared_hidden, shared_hidden)
        return pltpu.make_async_copy(
            pieces.at[at.ep, some], pieces_got.at[at.ep, some], own_sem.at[2 + p]
        )

    strips = 4
    strip = width // strips

    def load_strip(n):
        src = weights_in.at[pl.ds(n * strip, strip), pl.ds(0, 3 * heads_width)]
        return pltpu.make_async_copy(src, qkv_w.at[n % 2], strip_sem.at[n % 2])

    late_load = pltpu.make_async_copy(turned_in, turned, load_sem.at[1])
    lane = lax.broadcasted_iota(jnp.int32, (tokens, head), 1)
    sign = jnp.where(lane < head // 2, -1.0, 1.0)

    def unrotated(grads):
        turned_part = pltpu.roll(grads * sin_in[...], head // 2, 1) * sign
        return grads * cos_in[...] - turned_part

    def attention(d_low, out_w, q_all, k_all, v_all, d_att, probs, d_probs):
        pairs = (
            (d_low_in, d_low),
            (weights_in.at[:, pl.ds(3 * heads_width, heads_width)], out_w),
            (q_in, q_all),
            (k_in, k_all),
            (v_in, v_all),
        )
        copies = [
            pltpu.make_async_copy(src, dst, load_sem.at[2 + i])
            for i, (src, dst) in enumerate(pairs)
        ]
        for copy in copies + [late_load, load_strip(0), load_strip(1)]:
            copy.start()
        at.greet_row()
        rows_begin(0)
        copies[0].wait()
        copies[1].wait()
        d_attended = jnp.dot(d_low[...], out_w[...], preferred_element_type=f32).astype(bf16)
        for h in range(heads):
            d_att[h] = d_attended[:, h * head : (h + 1) * head]
        for copy in copies[2:]:
            copy.wait()

        def head_body(h, carry):
            queries, d_a = q_all[h], d_att[h]
            delta = jnp.zeros((1, tokens), f32)
            for w in range(windows):
                some = slice(w * tokens, (w + 1) * tokens)
                scores = lax.dot_general(
                    k_all[h, some], queries, across, preferred_element_type=f32
                )
                key_at = lax.broadcasted_iota(jnp.int32, scores.shape, 0)
                key_at = key_at + (at.ep + w + 1 - windows) * tokens
                allowed = (key_at >= query_start[...]) & (key_at <= query_at[...])
                p = jnp.where(allowed, jnp.exp(scores * score_scale - lse_in[h]), 0.0)
                d_p = lax.dot_general(v_all[h, some], d_a, across, preferred_element_type=f32)
                probs[w] = p
                d_probs[w] = d_p
                delta = delta + jnp.sum(p * d_p, axis=0, keepdims=True)
            d_queries = jnp.zeros((head, tokens), f32)
            for w in range(windows):
                some = slice(w * tokens, (w + 1) * tokens)
                p = probs[w]
                d_scores = (p * (d_probs[w] - delta)).astype(bf16)
                d_keys = jnp.dot(d_scores, queries, preferred_element_type=f32) * score_scale
                d_values = jnp.dot(p.astype(bf16), d_a, preferred_element_type=f32)
                if w < windows - 1:
                    d_out[w, h, :, :head] = d_keys.astype(bf16)
                    d_out[w, h, :, head:] = d_values.astype(bf16)

                    @pl.when(at.ep >= 2 - w)
                    def _():
                        d_copy(w, h).start()

                else:
                    d_own[h, :, :head] = d_keys
                    d_own[h, :, head:] = d_values
                d_queries = d_queries + jnp.dot(
                    k_all[h, some].T, d_scores, preferred_element_type=f32
                )
            here = pl.ds(pl.multiple_of(h * head, head), head)
            d_proj[:, here] = unrotated((d_queries * score_scale).T).astype(bf16)
            return carry

        lax.fori_loop(0, heads, head_body, 0)

    pl.run_scoped(
        attention,
        pltpu.VMEM((tokens, width), bf16),
        pltpu.VMEM((width, heads_width), bf16),
        pltpu.VMEM((heads, tokens, head), bf16),
        pltpu.VMEM((heads, windows * tokens, head), bf16),
        pltpu.VMEM((heads, windows * tokens, head), bf16),
        pltpu.VMEM((heads, tokens, head), bf16),
        pltpu.VMEM((windows, tokens, tokens), f32),
        pltpu.VMEM((windows, tokens, tokens), f32),
    )
    order = [j for j in range(1, depth)] + [0]

    def own_body(h, carry):
        for w in range(windows - 1):

            @pl.when(at.ep + (2 - w) < count)
            def _():
                d_arrival(w, h).wait_recv()
                d_own[h] += d_got[w, h].astype(f32)

        k_here = pl.ds(pl.multiple_of(heads_width + h * head, head), head)
        v_here = pl.ds(pl.multiple_of(2 * heads_width + h * head, head), head)
        d_proj[:, k_here] = unrotated(d_own[h, :, :head]).astype(bf16)
        d_proj[:, v_here] = d_own[h, :, head:].astype(bf16)
        return carry

    def weight_rows(into, q, z, y):
        here = pl.ds(pl.multiple_of((z * 2 + y) * rows, rows), rows)
        product = jnp.dot(turned[here], d_proj[:, cuts[q]], preferred_element_type=f32)
        into[:, cuts[q]] = product.astype(bf16)

    def begin_sums(q):
        for j in order:
            weight_rows(y_out.at[j], q, at.ahead(j), 1 - at.y)
            y_copy(q, j).start()

    def own_sums(q):
        for j in order:
            weight_rows(own.at[j], q, at.ahead(j), at.y)

    def projections():
        lax.fori_loop(0, heads, own_body, 0)
        for n in range(strips):
            some = slice(n * strip, (n + 1) * strip)
            load_strip(n).wait()
            product = lax.dot_general(
                d_proj[...], qkv_w[n % 2], across, preferred_element_type=f32
            )
            part[:, :, :, some] = product.astype(bf16).reshape(2, 2, quarter, strip)
            if n + 2 < strips:
                load_strip(n + 2).start()
        core_copy().start()
        begin_sums(1)
        core_copy().wait()
        for x in (0, 1):
            part[x, at.c] = part[x, at.c] + core_got[x]
        x_copy().start()
        own_sums(1)
        x_copy().wait()

        def end_body(i, carry):
            here = pl.ds(pl.multiple_of(i * few, few), few)
            grads = part[at.x, at.c, here].astype(f32) + x_got[here].astype(f32)
            inputs = own_rows_in[here].astype(f32)
            scale = lax.rsqrt(jnp.mean(inputs * inputs, axis=1, keepdims=True) + epsilon)
            unit_rows = inputs * scale
            scaled = grads * gain_in[...]
            inner = jnp.mean(scaled * unit_rows, axis=1, keepdims=True)
            total = d_resid_in[here] + scale * (scaled - unit_rows * inner)
            d_rows[here] = total.astype(bf16)
            return carry + jnp.sum(grads * unit_rows, axis=0, keepdims=True)

        d_gain = lax.fori_loop(0, quarter // few, end_body, jnp.zeros((1, width), f32))
        rows_begin(1)
        line = lax.broadcasted_iota(jnp.int32, (128, rows), 0)
        for e in range(count):
            some = slice(e * rows, (e + 1) * rows)
            gains = jnp.where(line == 0, d_gain[:, some], 0.0)
            gains = jnp.where(line == 1, gain_two_in[:, some], gains)
            small_own[e // 2, e % 2] = (gains.T + side_in[some]).astype(bf16)
        for j in order:
            little_y(j).start()

    def after_y(q, j):
        y_copy(q, j).wait_recv()

        def body(i, carry):
            some = pl.ds(pl.multiple_of(i * few, few), few)
            own[j, some, cuts[q]] = own[j, some, cuts[q]] + hop[j, some, cuts[q]]
            return carry

        lax.fori_loop(0, rows // few, body, 0)
        if j > 0:
            z_copy(q, j).start()

    def after_little():
        for j in order:
            little_y(j).wait_recv()
            here = small_own.at[at.ahead(j), at.y]
            here[...] = here[...] + small_hop[j]
            if j > 0:
                little_z(j).start()

    hooks = {(0, 0): [functools.partial(rows_pass_on, 0)]}
    for i, j in enumerate(order):
        hooks.setdefault((0, min(2 * i + 1, count - 1)), []).append(functools.partial(after_y, 0, j))
    hooks[(1, 2)] = [functools.partial(rows_pass_on, 1)]
    hooks[(1, 3)] = [after_little]
    last_hooks = []
    for i, j in enumerate(order):
        when = count + 5 + 5 * i
        due = functools.partial(after_y, 1, j)
        if when < 3 * count:
            hooks.setdefault((when // count, when % count), []).append(due)
        else:
            last_hooks.append(due)

    def weight_gradients(turned_left, left_tile, right_part, staging):
        lefts = (
            lambda tile: d_pair_in.at[tile, :, pl.ds(0, hidden)],
            lambda tile: d_pair_in.at[tile, :, pl.ds(hidden, hidden)],
            lambda tile: weighted_in.at[tile],
        )
        rights = (rows_in, rows_in, upstream_in)
        results = (gate_out, up_out, down_out)
        columns = width // count

        def load_left(p, tile):
            slot = lax.rem(tile, 2)
            return pltpu.make_async_copy(
                lefts[p](tile), left_tile.at[slot], tile_sem.at[0, slot]
            )

        def load_right(p, n):
            slot = lax.rem(n, 2)
            here = pl.ds(pl.multiple_of(n * columns, columns), columns)
            return pltpu.make_async_copy(
                rights[p].at[:, :, here], right_part.at[slot], tile_sem.at[1, slot]
            )

        def store(p, n):
            slot = lax.rem(n, 2)
            here = pl.ds(pl.multiple_of(n * columns, columns), columns)
            return pltpu.make_async_copy(
                staging.at[slot], results[p].at[:, here], store_sem.at[slot]
            )

        def turn_left(p, tile):
            load_left(p, tile).wait()

            @pl.when(tile + 1 < count)
            def _():
                load_left(p, tile + 1).start()

            here = pl.ds(pl.multiple_of(tile * tokens, tokens), tokens)
            turned_left[:, here] = left_tile[lax.rem(tile, 2)].T

        def run_pass(p):
            def part_body(n, carry):
                slot = lax.rem(n, 2)
                load_right(p, n).wait()

                @pl.when(n + 1 < count)
                def _():
                    load_right(p, n + 1).start()

                if p < 2:

                    @pl.when(n + 1 == count)
                    def _():
                        load_right(p + 1, 0).start()

                @pl.when(n >= 2)
                def _():
                    store(p, n - 2).wait()

                product = jnp.dot(
                    turned_left[...],
                    right_part[slot].reshape(count * tokens, columns),
                    preferred_element_type=f32,
                )
                staging[slot] = product[:routed].astype(bf16)
                pieces[n, p * shared_hidden : (p + 1) * shared_hidden] = product[
                    routed : routed + shared_hidden
                ].astype(bf16)
                store(p, n).start()
                for (hook_pass, hook_part), actions in hooks.items():
                    if hook_pass == p:

                        @pl.when(n == hook_part)
                        def _():
                            for action in actions:
                                action()

                return carry

            def turn_body(tile, carry):
                turn_left(p, tile)
                return carry

            lax.fori_loop(0, count, turn_body, 0)
            if p < 2:
                load_left(p + 1, 0).start()
            lax.fori_loop(0, count, part_body, 0)
            for n in (count - 2, count - 1):
                store(p, n).wait()
            swap_own(p).start()
            for copy in swap_copies(p, True):
                copy.start()

        load_left(0, 0).start()
        load_right(0, 0).start()
        late_load.wait()
        begin_sums(0)
        own_sums(0)

        run_pass(0)
        projections()
        run_pass(1)
        run_pass(2)
        for action in last_hooks:
            action()

    pl.run_scoped(
        weight_gradients,
        pltpu.VMEM((hidden, count * tokens), bf16),
        pltpu.VMEM((2, tokens, hidden), bf16),
        pltpu.VMEM((2, count, tokens, width // count), bf16),
        pltpu.VMEM((2, routed, width // count), bf16),
    )
    total = small_own[at.z, at.y].astype(f32)
    for j in range(1, depth):
        little_z(j).wait_recv()
        total = total + small_z[j - 1].astype(f32)
    for kind in (0, 1):
        small[kind] = total
        small_copy(kind).start()
        small_copy(kind).wait()
        total = small[kind] + small_got[kind]
    small_out[...] = total
    for j in range(1, depth):
        for q in (0, 1):
            z_copy(q, j).wait_recv()

    def total_body(i, carry):
        some = pl.ds(pl.multiple_of(i * few, few), few)
        result = own[0, some].astype(f32)
        for k in range(depth - 1):
            result = result + from_z[k, some].astype(f32)
        out[some] = result
        return carry

    lax.fori_loop(0, rows // few, total_body, 0)
    for j in range(depth):
        little_y(j).wait_send()
        if j > 0:
            little_z(j).wait_send()
        for q in (0, 1):
            y_copy(q, j).wait_send()
            if j > 0:
                z_copy(q, j).wait_send()
    for a in (0, 1):
        rows_end(a)
    for p in range(3):
        swap_own(p).wait()
        for copy in swap_copies(p, False):
            copy.wait_recv()
        for copy in swap_copies(p, True):
            copy.wait_send()

    def finish(h, carry):
        for w in range(windows - 1):

            @pl.when(at.ep >= 2 - w)
            def _():
                d_copy(w, h).wait_send()

        return carry

    lax.fori_loop(0, heads, finish, 0)


def backward(large, tiles_of, in_place, units, scale):
    d_low, _, queries, keys = large[:4]
    heads, tokens, head = queries.shape
    width = d_low.shape[1]
    ep_count = lax.axis_size("ep")
    depth, rows = ep_count // 2, width // ep_count
    quarter = tokens // lax.axis_size("tp")
    windows = keys.shape[1] // tokens
    columns = 3 * heads * head
    hidden = tiles_of[3].shape[2]
    slot_here, slot_hidden, shared_hidden = units
    f32, bf16 = jnp.float32, jnp.bfloat16
    anywhere = pl.BlockSpec(memory_space=pl.ANY)
    in_vmem = pl.BlockSpec(memory_space=pltpu.VMEM)
    dma = pltpu.SemaphoreType.DMA
    pieces = (ep_count, 3 * shared_hidden, rows)
    gathered = jax.ShapeDtypeStruct((2, 2, quarter, width), bf16)
    routed = jax.ShapeDtypeStruct((slot_here * slot_hidden, width), bf16)

    def vmem(*shape, dtype=bf16):
        return pltpu.VMEM(shape, dtype)

    out, small, block_out, d_rows, pieces, gate, up, down = pl.pallas_call(
        functools.partial(back_kernel, units, scale),
        out_shape=(
            jax.ShapeDtypeStruct((rows, columns), f32),
            jax.ShapeDtypeStruct((rows, 128), f32),
            gathered,
            gathered,
            jax.ShapeDtypeStruct(pieces, bf16),
            routed,
            routed,
            routed,
        ),
        in_specs=[anywhere] * (len(large) + len(tiles_of)) + [in_vmem] * len(in_place),
        out_specs=(in_vmem, in_vmem) + (anywhere,) * 6,
        scratch_shapes=[
            vmem(2, width // 4, columns),
            vmem(width, tokens),
            vmem(windows - 1, heads, tokens, 2 * head),
            vmem(windows - 1, heads, tokens, 2 * head),
            vmem(heads, tokens, 2 * head, dtype=f32),
            vmem(tokens, columns),
            vmem(2, 2, quarter, width),
            vmem(2, quarter, width),
            vmem(quarter, width),
            vmem(quarter, width),
            vmem(depth, rows, columns),
            vmem(depth, rows, columns),
            vmem(depth, rows, columns),
            vmem(depth - 1, rows, columns),
            vmem(depth, 2, rows, 128),
            vmem(depth, rows, 128),
            vmem(depth - 1, rows, 128),
            vmem(2, rows, 128, dtype=f32),
            vmem(2, rows, 128, dtype=f32),
            vmem(*pieces),
            dma((7,)),
            dma((windows - 1, heads)),
            dma((windows - 1, heads)),
            dma((2,)),
            dma((2,)),
            dma((2, depth)),
            dma((2, depth)),
            dma((2, depth)),
            dma((2, depth)),
            dma((2, depth)),
            dma((2, depth)),
            dma((2,)),
            dma((2,)),
            dma((3, ep_count)),
            dma((3, ep_count)),
            dma((2, 3)),
            dma((2, 3)),
            dma((5,)),
            dma((2, 2)),
            dma((2,)),
            dma((2,)),
        ],
        compiler_params=pltpu.CompilerParams(
            collective_id=4, has_side_effects=True, vmem_limit_bytes=62 * 2**20
        ),
        cost_estimate=pl.CostEstimate(
            flops=6 * ep_count * tokens * width * hidden,
            bytes_accessed=8 * ep_count * tokens * width,
            transcendentals=heads * tokens * windows * tokens,
        ),
        name="backward",
    )(*large, *tiles_of, *in_place)
    block_out, d_rows = [array.reshape(4 * quarter, width) for array in (block_out, d_rows)]
    return out, small, block_out, d_rows, pieces, (gate, up, down)


def shared_pieces(weights, ep_count):
    rows, hidden = weights[0].shape
    units = hidden // ep_count
    return jnp.concatenate([weight.T.reshape(ep_count, units, rows) for weight in weights], axis=1)


def shared_units_of(pieces, count):
    ep_count, units, rows = pieces.shape
    return pieces.transpose(1, 0, 2).reshape(count, units // count, ep_count * rows)


def shared_whole(pieces, count):
    ep_count, units, columns = pieces.shape
    units = units // count
    pieces = pieces.reshape(ep_count, count, units, columns).astype(jnp.float32)
    return [pieces[:, i].reshape(ep_count * units, columns).T for i in range(count)]


def dense_body(
    tokens,
    lengths,
    routes,
    attn_gain,
    w_query,
    w_key,
    w_value,
    w_out,
    ffn_gain,
    w_router,
    shared_mix,
    shared_gate,
    shared_up,
    shared_down,
    expert_gate,
    expert_up,
    expert_down,
    cotangent,
):
    everywhere = ("ep", "tp")
    rows_here, width = tokens.shape
    ep_count = lax.axis_size("ep")
    tp_count = lax.axis_size("tp")
    ep_index = lax.axis_index("ep")
    offset = ep_index * rows_here
    quarter = rows_here // tp_count
    first_row = lax.axis_index("tp") * quarter
    slot_here, slot_hidden = expert_gate.shape[0], expert_gate.shape[1]
    expert_count = w_router.shape[1]
    bf16, f32 = jnp.bfloat16, jnp.float32

    def my_rows(array):
        return lax.dynamic_slice_in_dim(array, first_row, quarter, 0)

    side_columns = jnp.concatenate(
        [attn_gain[:, None], ffn_gain[:, None], shared_mix[:, None], w_router], axis=1
    )
    side_columns = jnp.pad(side_columns, ((0, 0), (0, -side_columns.shape[1] % 128)))
    joined_weights, pieces = gather_over_ep(
        jnp.concatenate([w_query, w_key, w_value, w_out, side_columns], axis=1),
        shared_pieces((shared_gate, shared_up, shared_down), ep_count),
    )
    cotangent_rows = my_rows(cotangent)
    joined_weights, cotangent_rows = lax.optimization_barrier((joined_weights, cotangent_rows))
    heads_width = w_query.shape[1]
    qkv_weight = joined_weights[:, : 3 * heads_width]
    output_weight = joined_weights[:, 3 * heads_width : 4 * heads_width]
    side_weight = joined_weights[:, 4 * heads_width :]
    picked = jnp.any(
        my_rows(routes)[:, :, None] == jnp.arange(expert_count, dtype=jnp.int32), axis=1
    )
    picked_lanes = jnp.pad(picked.astype(bf16), ((0, 0), (3, 125 - expert_count)))
    upstream_all = lax.all_gather(
        jnp.concatenate([cotangent_rows, picked_lanes], axis=1), everywhere, axis=0, tiled=True
    )
    shared_rows = shared_units_of(pieces, 3)
    shared_units = shared_rows.shape[1]
    routed_units = slot_here * slot_hidden
    gate_cat, up_cat, down_cat = [
        jnp.pad(
            jnp.concatenate([expert.reshape(-1, width), shared], axis=0),
            ((0, -(routed_units + shared_units) % 128), (0, 0)),
        )
        for expert, shared in zip((expert_gate, expert_up, expert_down), shared_rows)
    ]
    pair_cat = jnp.concatenate([gate_cat, up_cat], axis=0)
    hidden_total = gate_cat.shape[0]

    heads_here = heads_width // HD
    score_scale = HD ** (-0.5)
    first_norm_scale = side_weight[:, 0].astype(f32)
    second_norm_scale = side_weight[:, 1].astype(f32)
    mix_f = side_weight[:, 2].astype(f32)
    router_f = side_weight[:, 3 : 3 + expert_count].astype(f32)
    layer_input = tokens.astype(f32)
    normed_wide, norm_one = norm_forward(layer_input, first_norm_scale)
    normed_one = normed_wide.astype(bf16)
    query_at = offset + jnp.arange(rows_here, dtype=jnp.int32)
    key_at = offset - 2 * rows_here + jnp.arange(3 * rows_here, dtype=jnp.int32)
    query_seg, query_pos = sequence_info(lengths, query_at)
    key_seg, _ = sequence_info(lengths, key_at)
    cosine, sine = rope_tables(query_pos, HD)
    projected = jnp.dot(normed_one, qkv_weight, preferred_element_type=f32)
    projected = projected.reshape(rows_here, 3, heads_here, HD)
    queries = rotate(projected[:, 0], cosine, sine).astype(bf16)
    keys = rotate(projected[:, 1], cosine, sine).astype(bf16)
    values = projected[:, 2].astype(bf16)
    carried = jnp.stack([keys, values], axis=0)
    joined = jnp.concatenate(
        [passed_along(carried, "ep", 2), passed_along(carried, "ep", 1), carried], axis=1
    )
    keys_win = joined[0]
    values_win = joined[1]
    allowed = (
        (query_seg[:, None] == key_seg[None, :])
        & (key_at[None, :] <= query_at[:, None])
        & (key_at[None, :] >= 0)
    )
    scores = (
        jnp.einsum("qhd,khd->hqk", queries, keys_win, preferred_element_type=f32) * score_scale
    )
    masked = jnp.where(allowed[None], scores, -1e30)
    peak = jnp.max(masked, axis=-1, keepdims=True)
    expo = jnp.exp(masked - peak)
    total = jnp.sum(expo, axis=-1, keepdims=True)
    log_total = peak + jnp.log(total)
    weights = expo / total
    attended = jnp.einsum(
        "hqk,khd->qhd", weights.astype(bf16), values_win, preferred_element_type=f32
    )
    attended = attended.reshape(rows_here, heads_width).astype(bf16)
    attn_part = jnp.einsum("th,dh->td", attended, output_weight, preferred_element_type=f32)
    resid = my_rows(layer_input) + sum_over_tp(attn_part)
    normed_two_wide, norm_two = norm_forward(resid, second_norm_scale)
    normed_two = normed_two_wide.astype(bf16)

    (
        normed_all,
        weighted_h,
        d_pair_pre,
        block_rows,
        d_resid_low,
        d_resid,
        grad_gain_two,
        d_side,
    ) = ffn_over_all(
        normed_two,
        upstream_all,
        pair_cat,
        down_cat,
        side_weight,
        resid,
        second_norm_scale[None, :],
        (slot_here, slot_hidden, shared_units),
        expert_count,
    )
    grad_side = jnp.dot(normed_two.astype(f32).T, d_side, precision=highest)
    grad_out = jnp.einsum("td,th->dh", d_resid_low, attended, preferred_element_type=f32)
    grad_out = lax.psum_scatter(
        grad_out.astype(bf16), "ep", scatter_dimension=0, tiled=True
    ).astype(f32)
    def by_head(array):
        return array.transpose(1, 0, 2)

    places = ((query_at - query_pos)[None, :], query_at[None, :])
    tile_shape = (ep_count, rows_here, -1)
    tiles_of = tuple(
        array.reshape(tile_shape) for array in (normed_all, d_pair_pre, upstream_all, weighted_h)
    )
    units = (slot_here, slot_hidden, shared_units)
    column = jnp.arange(128, dtype=jnp.int32)
    large = (
        d_resid_low,
        joined_weights,
        by_head(queries),
        by_head(keys_win),
        by_head(values_win),
        normed_one.T,
        block_rows,
    )
    in_place = (
        log_total.reshape(heads_here, 1, rows_here),
        *places,
        cosine[:, 0],
        sine[:, 0],
        my_rows(tokens),
        first_norm_scale[None, :],
        d_resid,
        grad_gain_two[None, :],
        jnp.where(column >= 2, grad_side, 0.0),
    )
    grad_weights, small, block_out, grad_tokens, grad_pieces, grad_experts = backward(
        large, tiles_of, in_place, units, score_scale
    )
    grad_shared = shared_whole(grad_pieces, 3)
    grad_tokens = grad_tokens.astype(f32)
    grad_experts = [grad.astype(f32).reshape(expert_gate.shape) for grad in grad_experts]
    parts = [grad_weights[:, i * heads_width : (i + 1) * heads_width] for i in range(3)]
    return (
        block_out,
        grad_tokens,
        small[:, 0],
        parts[0],
        parts[1],
        parts[2],
        grad_out,
        small[:, 1],
        small[:, 3 : 3 + expert_count],
        small[:, 2],
        grad_shared[0],
        grad_shared[1],
        grad_shared[2],
        grad_experts[0],
        grad_experts[1],
        grad_experts[2],
    )


def chosen_body(*arrays):
    rows_here, top_count = arrays[2].shape
    slot_here, expert_count = arrays[14].shape[0], arrays[9].shape[1]
    capacity = rows_here * top_count * 7 // (5 * expert_count)
    grid_of_two = lax.axis_size("ep") % 2 == 0 and lax.axis_size("tp") == 4
    if grid_of_two and rows_here < 2 * slot_here * capacity:
        return dense_body(*arrays)
    return body(*arrays)


def solution(mesh):
    placed = (
        P("ep", None),
        P(),
        P("ep", None),
        P("ep"),
        P("ep", "tp"),
        P("ep", "tp"),
        P("ep", "tp"),
        P("ep", "tp"),
        P("ep"),
        P("ep", None),
        P("ep"),
        P("ep", "tp"),
        P("ep", "tp"),
        P("ep", "tp"),
        P("ep", "tp", None),
        P("ep", "tp", None),
        P("ep", "tp", None),
        P("ep", None),
    )
    return jax.shard_map(
        chosen_body,
        mesh=mesh,
        in_specs=placed,
        out_specs=(
            P("ep", None),
            P("ep", None),
            P("ep"),
            P("ep", "tp"),
            P("ep", "tp"),
            P("ep", "tp"),
            P("ep", "tp"),
            P("ep"),
            P("ep", None),
            P("ep"),
            P("ep", "tp"),
            P("ep", "tp"),
            P("ep", "tp"),
            P("ep", "tp", None),
            P("ep", "tp", None),
            P("ep", "tp", None),
        ),
        check_vma=False,
    )
```

```python
import functools

import jax
import jax.numpy as jnp
from jax import lax
from jax.experimental import pallas as pl
from jax.experimental.pallas import tpu as pltpu
from jax.sharding import PartitionSpec as P

HD = 128


epsilon = 1e-06
rope_base = 1000000.0
highest = lax.Precision.HIGHEST
MESH = pl.DeviceIdType.MESH


def passed_along(block, axis, distance):
    devices = range(lax.axis_size(axis))
    route = [(i - distance, i) for i in devices if i - distance in devices]
    return lax.ppermute(block, axis, route)


def rope_tables(positions, width):
    steps = jnp.arange(0, width, 2, dtype=jnp.float32) / width
    inverse = rope_base ** (-steps)
    angles = positions.astype(jnp.float32)[:, None] * inverse[None, :]
    angles = jnp.concatenate([angles, angles], axis=-1)
    return (jnp.cos(angles)[:, None, :], jnp.sin(angles)[:, None, :])


def turn_half(values):
    middle = values.shape[-1] // 2
    return jnp.concatenate([-values[..., middle:], values[..., :middle]], axis=-1)


def rotate(values, cosine, sine):
    return values * cosine + turn_half(values) * sine


def unrotate(grads, cosine, sine):
    return grads * cosine - turn_half(grads * sine)


def sequence_info(lengths, indices):
    starts = jnp.cumsum(lengths) - lengths
    inside = starts[None, :] <= indices[:, None]
    segment = jnp.sum(inside.astype(jnp.int32), axis=1) - 1
    first = jnp.max(jnp.where(inside, starts[None, :], -1), axis=1)
    return (segment, indices - first)


def norm_forward(values, gain):
    scale = lax.rsqrt(jnp.mean(values * values, axis=-1, keepdims=True) + epsilon)
    return (values * scale * gain, scale)


def norm_backward(values, scale, gain, grads):
    unit = values * scale
    scaled = grads * gain
    inner = jnp.mean(scaled * unit, axis=-1, keepdims=True)
    return (scale * (scaled - unit * inner), jnp.sum(grads * unit, axis=0))


def deliver(rows):
    arrived_rows = lax.all_to_all(rows, "ep", split_axis=0, concat_axis=0, tiled=True)
    return arrived_rows


def bring_back(parts, target, rows_here, top_count):
    moved = lax.all_to_all(parts, "ep", split_axis=0, concat_axis=0, tiled=True)
    piece = moved.shape[3]
    return moved.reshape(-1, piece)[target].reshape(rows_here, top_count, piece)


def body(
    tokens,
    lengths,
    routes,
    attn_gain,
    w_query,
    w_key,
    w_value,
    w_out,
    ffn_gain,
    w_router,
    shared_mix,
    shared_gate,
    shared_up,
    shared_down,
    expert_gate,
    expert_up,
    expert_down,
    cotangent,
):
    rows_here = tokens.shape[0]
    width = tokens.shape[1]
    ep_count = lax.axis_size("ep")
    offset = lax.axis_index("ep") * rows_here
    slot_here = expert_gate.shape[0]
    top_count = routes.shape[1]
    gathered = (
        lax.all_gather(attn_gain, "ep", axis=0, tiled=True),
        lax.all_gather(w_query, "ep", axis=0, tiled=True),
        lax.all_gather(w_key, "ep", axis=0, tiled=True),
        lax.all_gather(w_value, "ep", axis=0, tiled=True),
        lax.all_gather(w_out, "ep", axis=0, tiled=True),
        lax.all_gather(ffn_gain, "ep", axis=0, tiled=True),
        lax.all_gather(w_router, "ep", axis=0, tiled=True),
        lax.all_gather(shared_mix, "ep", axis=0, tiled=True),
        lax.all_gather(shared_gate, "ep", axis=0, tiled=True),
        lax.all_gather(shared_up, "ep", axis=0, tiled=True),
        lax.all_gather(shared_down, "ep", axis=0, tiled=True),
    )
    (
        gain_first,
        query_weight_matrix,
        key_weight_matrix,
        value_weight_matrix,
        output_weight,
        gain_second,
        router_weight,
        shared_mixer_weight,
        shared_gate_weight,
        shared_up_weight,
        shared_down_weight,
    ) = gathered
    expert_count = router_weight.shape[1]
    capacity = (rows_here * top_count * 7 // (5 * expert_count) + 7) // 8 * 8
    heads_here = query_weight_matrix.shape[1] // HD
    score_scale = HD ** (-0.5)
    first_norm_scale = gain_first.astype(jnp.float32)
    second_norm_scale = gain_second.astype(jnp.float32)
    layer_input = tokens.astype(jnp.float32)
    normed_wide, norm_one = norm_forward(layer_input, first_norm_scale)
    normed_one = normed_wide.astype(jnp.bfloat16)
    query_at = offset + jnp.arange(rows_here, dtype=jnp.int32)
    key_at = offset - 2 * rows_here + jnp.arange(3 * rows_here, dtype=jnp.int32)
    query_seg, query_pos = sequence_info(lengths, query_at)
    key_seg, _ = sequence_info(lengths, key_at)
    cosine, sine = rope_tables(query_pos, HD)
    query_pre = jnp.dot(
        normed_one, query_weight_matrix, preferred_element_type=jnp.float32
    ).reshape(rows_here, heads_here, HD)
    key_pre = jnp.dot(normed_one, key_weight_matrix, preferred_element_type=jnp.float32).reshape(
        rows_here, heads_here, HD
    )
    queries = rotate(query_pre, cosine, sine).astype(jnp.bfloat16)
    keys = rotate(key_pre, cosine, sine).astype(jnp.bfloat16)
    values = (
        jnp.dot(normed_one, value_weight_matrix, preferred_element_type=jnp.float32)
        .astype(jnp.bfloat16)
        .reshape(rows_here, heads_here, HD)
    )
    carried = jnp.stack([keys, values], axis=0)
    window = [carried]
    for hop in range(2):
        carried = passed_along(carried, "ep", 1)
        window = [carried] + window
    joined = jnp.concatenate(window, axis=1)
    keys_win = joined[0]
    values_win = joined[1]
    allowed = (
        (query_seg[:, None] == key_seg[None, :])
        & (key_at[None, :] <= query_at[:, None])
        & (key_at[None, :] >= 0)
    )
    scores = (
        jnp.einsum("qhd,khd->hqk", queries, keys_win, preferred_element_type=jnp.float32)
        * score_scale
    )
    masked = jnp.where(allowed[None], scores, -1e30)
    peak = jnp.max(masked, axis=-1, keepdims=True)
    expo = jnp.exp(masked - peak)
    total = jnp.sum(expo, axis=-1, keepdims=True)
    log_total = peak + jnp.log(total)
    weights = expo / total
    attended = jnp.einsum(
        "hqk,khd->qhd", weights.astype(jnp.bfloat16), values_win, preferred_element_type=jnp.float32
    )
    attended = attended.reshape(rows_here, heads_here * HD).astype(jnp.bfloat16)
    attn_part = jnp.einsum("th,dh->td", attended, output_weight, preferred_element_type=jnp.float32)
    resid = layer_input + lax.psum(attn_part, "tp")
    normed_two_wide, norm_two = norm_forward(resid, second_norm_scale)
    normed_two = normed_two_wide.astype(jnp.bfloat16)
    normed_two_f = normed_two.astype(jnp.float32)
    router_f = router_weight.astype(jnp.float32)
    mix_f = shared_mixer_weight.astype(jnp.float32)
    router = jax.nn.softmax(jnp.dot(normed_two_f, router_f, precision=highest), axis=-1)
    picked = routes[:, :, None] == jnp.arange(expert_count, dtype=jnp.int32)[None, None, :]
    gates = jnp.sum(jnp.where(picked, router[:, None, :], 0.0), axis=-1)
    mixer = jax.nn.sigmoid(jnp.dot(normed_two_f, mix_f, precision=highest))
    shared_g = jnp.dot(normed_two, shared_gate_weight, preferred_element_type=jnp.float32)
    shared_u = jnp.dot(normed_two, shared_up_weight, preferred_element_type=jnp.float32)
    shared_h = (jax.nn.silu(shared_g) * shared_u).astype(jnp.bfloat16)
    shared_part = jnp.einsum(
        "tf,df->td", shared_h, shared_down_weight, preferred_element_type=jnp.float32
    )
    flat = routes.reshape(-1)
    hot = (flat[:, None] == jnp.arange(expert_count, dtype=jnp.int32)[None, :]).astype(jnp.int32)
    rank = jnp.sum(jnp.cumsum(hot, axis=0) * hot, axis=1) - 1
    target = flat * capacity + rank
    slot_total = ep_count * slot_here * capacity
    owner_route = (
        jnp.zeros((slot_total,), jnp.int32)
        .at[target]
        .set(jnp.arange(rows_here * top_count, dtype=jnp.int32))
    )
    filled = jnp.zeros((slot_total,), jnp.bool_).at[target].set(True)
    owner_token = owner_route // top_count
    send_rows = jnp.where(filled[:, None], normed_two[owner_token], jnp.zeros((), jnp.bfloat16))
    arrived_rows = deliver(send_rows.reshape(ep_count, slot_here, capacity, width))
    route_g = jnp.einsum(
        "nscd,sfd->nscf", arrived_rows, expert_gate, preferred_element_type=jnp.float32
    )
    route_u = jnp.einsum(
        "nscd,sfd->nscf", arrived_rows, expert_up, preferred_element_type=jnp.float32
    )
    route_h = (jax.nn.silu(route_g) * route_u).astype(jnp.bfloat16)
    route_part = jnp.einsum(
        "nscf,sfd->nscd", route_h, expert_down, preferred_element_type=jnp.float32
    )
    back_rows = bring_back(route_part, target, rows_here, top_count)
    upstream = cotangent.astype(jnp.float32)
    routed = jnp.sum(back_rows * gates[:, :, None], axis=1)
    ffn_part = mixer[:, None] * shared_part + routed
    route_dot = jnp.sum(back_rows * upstream[:, None, :], axis=-1)
    shared_dot = jnp.sum(shared_part * upstream, axis=-1)
    ffn_total, d_gate, d_mixer = lax.psum((ffn_part, route_dot, shared_dot), "tp")
    block_out = (resid + ffn_total).astype(jnp.bfloat16)
    d_router = jnp.sum(jnp.where(picked, d_gate[:, :, None], 0.0), axis=1)
    d_logits = router * (d_router - jnp.sum(router * d_router, axis=-1, keepdims=True))
    d_mixlogit = d_mixer * mixer * (1.0 - mixer)
    side = jnp.dot(d_logits, router_f.T, precision=highest) + d_mixlogit[:, None] * mix_f[None, :]
    grad_router = jnp.dot(normed_two_f.T, d_logits, precision=highest)
    grad_mix = jnp.dot(d_mixlogit, normed_two_f, precision=highest)
    d_shared = (mixer[:, None] * upstream).astype(jnp.bfloat16)
    d_sh = jnp.dot(d_shared, shared_down_weight, preferred_element_type=jnp.float32)
    sig_shared = jax.nn.sigmoid(shared_g)
    d_sg = (d_sh * shared_u * sig_shared * (1.0 + shared_g * (1.0 - sig_shared))).astype(
        jnp.bfloat16
    )
    d_su = (d_sh * shared_g * sig_shared).astype(jnp.bfloat16)
    d_normed_part = jnp.einsum(
        "tf,df->td", d_sg, shared_gate_weight, preferred_element_type=jnp.float32
    )
    d_normed_part = d_normed_part + jnp.einsum(
        "tf,df->td", d_su, shared_up_weight, preferred_element_type=jnp.float32
    )
    grad_sgate = jnp.einsum("td,tf->df", normed_two, d_sg, preferred_element_type=jnp.float32)
    grad_sup = jnp.einsum("td,tf->df", normed_two, d_su, preferred_element_type=jnp.float32)
    grad_sdown = jnp.einsum("td,tf->df", d_shared, shared_h, preferred_element_type=jnp.float32)
    d_route = (
        (gates[:, :, None] * upstream[:, None, :])
        .astype(jnp.bfloat16)
        .reshape(rows_here * top_count, width)
    )
    send_grads = jnp.where(filled[:, None], d_route[owner_route], jnp.zeros((), jnp.bfloat16))
    received_grads = deliver(send_grads.reshape(ep_count, slot_here, capacity, width))
    d_rh = jnp.einsum(
        "nscd,sfd->nscf", received_grads, expert_down, preferred_element_type=jnp.float32
    )
    sig_route = jax.nn.sigmoid(route_g)
    d_rg = (d_rh * route_u * sig_route * (1.0 + route_g * (1.0 - sig_route))).astype(jnp.bfloat16)
    routed_up_gradient = (d_rh * route_g * sig_route).astype(jnp.bfloat16)
    row_grads = jnp.einsum("nscf,sfd->nscd", d_rg, expert_gate, preferred_element_type=jnp.float32)
    row_grads = row_grads + jnp.einsum(
        "nscf,sfd->nscd", routed_up_gradient, expert_up, preferred_element_type=jnp.float32
    )
    grad_egate = jnp.einsum(
        "qxba,qxbr->xar", d_rg, arrived_rows, preferred_element_type=jnp.float32
    )
    expert_up_gradient = jnp.einsum(
        "qxba,qxbr->xar", routed_up_gradient, arrived_rows, preferred_element_type=jnp.float32
    )
    grad_edown = jnp.einsum(
        "qxba,qxbr->xar", route_h, received_grads, preferred_element_type=jnp.float32
    )
    grads_back = bring_back(row_grads, target, rows_here, top_count)
    d_routed = jnp.sum(grads_back, axis=1)
    d_normed_two = lax.psum(d_normed_part + d_routed, "tp") + side
    d_resid_norm, grad_gain_two = norm_backward(resid, norm_two, second_norm_scale, d_normed_two)
    d_resid = upstream + d_resid_norm
    d_resid_low = d_resid.astype(jnp.bfloat16)
    grad_outw = jnp.einsum("td,th->dh", d_resid_low, attended, preferred_element_type=jnp.float32)
    d_attended = jnp.einsum(
        "td,dh->th", d_resid_low, output_weight, preferred_element_type=jnp.float32
    )
    d_attended = d_attended.astype(jnp.bfloat16).reshape(rows_here, heads_here, HD)
    scores_again = (
        jnp.einsum("qhd,khd->hqk", queries, keys_win, preferred_element_type=jnp.float32)
        * score_scale
    )
    probs = jnp.where(allowed[None], jnp.exp(scores_again - log_total), 0.0)
    d_probs = jnp.einsum("qhd,khd->hqk", d_attended, values_win, preferred_element_type=jnp.float32)
    delta = jnp.sum(probs * d_probs, axis=-1, keepdims=True)
    d_scores = (probs * (d_probs - delta)).astype(jnp.bfloat16)
    d_queries = (
        jnp.einsum("hqk,khd->qhd", d_scores, keys_win, preferred_element_type=jnp.float32)
        * score_scale
    )
    d_keys_win = (
        jnp.einsum("hqk,qhd->khd", d_scores, queries, preferred_element_type=jnp.float32)
        * score_scale
    )
    d_values_win = jnp.einsum(
        "hqk,qhd->khd", probs.astype(jnp.bfloat16), d_attended, preferred_element_type=jnp.float32
    )
    pair_grads = jnp.stack([d_keys_win, d_values_win], axis=0)
    older = pair_grads[:, :rows_here]
    later = [pair_grads[:, rows_here : 2 * rows_here], pair_grads[:, 2 * rows_here :]]
    running = older
    for hop in range(2):
        running = passed_along(running, "ep", -1)
        running = running + later[hop]
    d_query_pre = (
        unrotate(d_queries, cosine, sine).astype(jnp.bfloat16).reshape(rows_here, heads_here * HD)
    )
    d_key_pre = (
        unrotate(running[0], cosine, sine).astype(jnp.bfloat16).reshape(rows_here, heads_here * HD)
    )
    d_values = running[1].astype(jnp.bfloat16).reshape(rows_here, heads_here * HD)
    grad_queryw = jnp.einsum(
        "td,th->dh", normed_one, d_query_pre, preferred_element_type=jnp.float32
    )
    grad_keyw = jnp.einsum("td,th->dh", normed_one, d_key_pre, preferred_element_type=jnp.float32)
    grad_valuew = jnp.einsum("td,th->dh", normed_one, d_values, preferred_element_type=jnp.float32)
    d_normed_one = jnp.einsum(
        "th,dh->td", d_query_pre, query_weight_matrix, preferred_element_type=jnp.float32
    )
    d_normed_one = d_normed_one + jnp.einsum(
        "th,dh->td", d_key_pre, key_weight_matrix, preferred_element_type=jnp.float32
    )
    d_normed_one = d_normed_one + jnp.einsum(
        "th,dh->td", d_values, value_weight_matrix, preferred_element_type=jnp.float32
    )
    d_normed_one = lax.psum(d_normed_one, "tp")
    d_input_norm, grad_gain_one = norm_backward(
        layer_input, norm_one, first_norm_scale, d_normed_one
    )
    grad_tokens = d_resid + d_input_norm
    summed = (
        lax.psum_scatter(grad_gain_one, "ep", scatter_dimension=0, tiled=True),
        lax.psum_scatter(grad_queryw, "ep", scatter_dimension=0, tiled=True),
        lax.psum_scatter(grad_keyw, "ep", scatter_dimension=0, tiled=True),
        lax.psum_scatter(grad_valuew, "ep", scatter_dimension=0, tiled=True),
        lax.psum_scatter(grad_outw, "ep", scatter_dimension=0, tiled=True),
        lax.psum_scatter(grad_gain_two, "ep", scatter_dimension=0, tiled=True),
        lax.psum_scatter(grad_router, "ep", scatter_dimension=0, tiled=True),
        lax.psum_scatter(grad_mix, "ep", scatter_dimension=0, tiled=True),
        lax.psum_scatter(grad_sgate, "ep", scatter_dimension=0, tiled=True),
        lax.psum_scatter(grad_sup, "ep", scatter_dimension=0, tiled=True),
        lax.psum_scatter(grad_sdown, "ep", scatter_dimension=0, tiled=True),
    )
    return (
        block_out,
        grad_tokens,
        summed[0],
        summed[1],
        summed[2],
        summed[3],
        summed[4],
        summed[5],
        summed[6],
        summed[7],
        summed[8],
        summed[9],
        summed[10],
        grad_egate,
        expert_up_gradient,
        grad_edown,
    )


class Place:
    def __init__(self):
        self.ep, self.tp = lax.axis_index("ep"), lax.axis_index("tp")
        self.z, self.y = self.ep // 2, self.ep % 2
        self.x, self.c = self.tp // 2, self.tp % 2
        self.depth = lax.axis_size("ep") // 2
        self.next_core = (self.ep, self.x * 2 + 1 - self.c)
        self.next_x = (self.ep, (1 - self.x) * 2 + self.c)
        self.next_y = (self.z * 2 + 1 - self.y, self.tp)

    def at_z(self, z):
        return (z * 2 + self.y, self.tp)

    def ahead(self, steps):
        return lax.rem(self.z + steps, self.depth)

    def behind(self, steps):
        return lax.rem(self.z + self.depth - steps, self.depth)

    def greet(self):
        barrier = pltpu.get_barrier_semaphore()
        peers = [self.next_core, self.next_x, self.next_y]
        peers += [self.at_z(self.ahead(k)) for k in range(1, self.depth)]
        for peer in peers:
            pl.semaphore_signal(barrier, inc=1, device_id=peer, device_id_type=MESH)
        pl.semaphore_wait(barrier, len(peers))

    def greet_row(self):
        barrier = pltpu.get_barrier_semaphore()
        count = 2 * self.depth
        peers = [(lax.rem(self.ep + k, count), self.tp) for k in range(1, count)]
        peers += [self.next_core, self.next_x]
        for peer in peers:
            pl.semaphore_signal(barrier, inc=1, device_id=peer, device_id_type=MESH)
        pl.semaphore_wait(barrier, len(peers))

    def greet_ep(self):
        barrier = pltpu.get_barrier_semaphore()
        count = 2 * self.depth
        for k in range(1, count):
            peer = (lax.rem(self.ep + k, count), self.tp)
            pl.semaphore_signal(barrier, inc=1, device_id=peer, device_id_type=MESH)
        pl.semaphore_wait(barrier, count - 1)


def remote(src, dst, send, recv, peer):
    return pltpu.make_async_remote_copy(
        src_ref=src, dst_ref=dst, send_sem=send, recv_sem=recv, device_id=peer, device_id_type=MESH
    )


def ffn_kernel(
    units,
    expert_count,
    rows_in,
    upstream_in,
    pair_in,
    down_in,
    side_in,
    resid_in,
    gain_in,
    rows_all,
    weighted_out,
    d_pair_out,
    block_out,
    d_resid_low_out,
    d_resid_out,
    d_gain_out,
    d_side_out,
    d_rows_sum,
    out_sum,
    pair_w,
    down_w,
    side_w,
    rows_tile,
    upstream_tile,
    pair_pre,
    d_hidden,
    factors,
    dots,
    weighted_tile,
    d_pair_tile,
    d_resid_low,
    d_rows_tile,
    out_tile,
    d_rows_core,
    out_core,
    d_rows_held,
    out_held,
    d_rows_hop,
    out_hop,
    d_rows_hop2,
    out_hop2,
    d_rows_z,
    out_z,
    d_rows_to_z,
    out_to_z,
    gathered_send,
    gathered_recv,
    hop_send,
    hop_recv,
    weight_sem,
    own_sem,
    z_send,
    z_recv,
    plane_send,
    plane_recv,
    load_sem,
    store_sem,
    sum_send,
    sum_recv,
    end_send,
    end_recv,
    core_credit,
    hop_credit,
    hop2_credit,
):
    at = Place()
    depth = at.depth
    quarter, width = rows_in.shape
    half = quarter // 2
    f32, bf16 = jnp.float32, jnp.bfloat16

    def weight_copies():
        pairs = (
            (pair_in, pair_w),
            (down_in, down_w),
            (side_in, side_w),
        )
        return [
            pltpu.make_async_copy(src, dst, weight_sem.at[i]) for i, (src, dst) in enumerate(pairs)
        ]

    for copy in weight_copies():
        copy.start()

    def block(j, y, x):
        return rows_all.at[at.behind(j), y, x, at.c]

    def plane_copy(j, kind):
        y, other_y = at.y, 1 - at.y
        own, other_x = at.x, 1 - at.x
        if kind == 0:
            src, peer = block(j, y, own), at.next_x
        elif kind == 1:
            src, peer = block(j, y, own), at.next_y
        elif kind == 2:
            src, peer = block(j, y, other_x).at[pl.ds(0, half)], at.next_y
        elif kind == 3:
            src, peer = block(j, other_y, own).at[pl.ds(half, half)], at.next_x
        else:
            src = block(j, other_y if kind >= 6 else y, other_x if kind % 2 else own)
            peer = at.next_core
        return remote(src, src, plane_send.at[j, kind], plane_recv.at[j, kind], peer)

    def z_copy(k):
        return remote(
            rows_in, block(0, at.y, at.x), z_send.at[k - 1], z_recv.at[k - 1], at.at_z(at.ahead(k))
        )

    def z_arrival(k):
        dst = block(k, at.y, at.x)
        return remote(dst, dst, z_send.at[k - 1], z_recv.at[k - 1], at.at_z(at.behind(k)))

    def begin(j):
        for kind in (0, 1, 4):
            plane_copy(j, kind).start()

    def spread(j):
        plane_copy(j, 0).wait_recv()
        plane_copy(j, 2).start()
        plane_copy(j, 5).start()
        plane_copy(j, 1).wait_recv()
        plane_copy(j, 3).start()
        plane_copy(j, 6).start()

    def begin_later(j):
        z_arrival(j).wait_recv()
        begin(j)

    def last_hop(j):
        plane_copy(j, 2).wait_recv()
        plane_copy(j, 3).wait_recv()
        plane_copy(j, 7).start()

    def near_ready(j):
        plane_copy(j, 4).wait_recv()
        plane_copy(j, 5).wait_recv()

    def far_ready(j):
        plane_copy(j, 6).wait_recv()
        plane_copy(j, 7).wait_recv()

    def parity(step):
        return lax.rem(step, 2)

    def slot_of(turn):
        return lax.rem(turn + 1, depth)

    def other_y(step):
        return lax.rem(parity(step) + (step // 2 + 1) // depth, 2)

    def tile_at(step):
        return at.behind(slot_of(step // 2)), lax.rem(at.y + other_y(step), 2)

    def load_rows(step):
        z, y = tile_at(step)
        return pltpu.make_async_copy(rows_all.at[z, y], rows_tile, load_sem.at[0])

    def load_upstream(step):
        z, y = tile_at(step)
        return pltpu.make_async_copy(upstream_in.at[z, y], upstream_tile, load_sem.at[1])

    def stores(step):
        z, y = tile_at(step)
        pairs = ((weighted_tile, weighted_out), (d_pair_tile, d_pair_out))
        return [
            pltpu.make_async_copy(src, dst.at[z, y], store_sem.at[i])
            for i, (src, dst) in enumerate(pairs)
        ]

    tiles, cores = (d_rows_tile, out_tile), (d_rows_core, out_core)
    helds, sums = (d_rows_held, out_held), (d_rows_sum, out_sum)
    hops, hops2, zs = (d_rows_hop, out_hop), (d_rows_hop2, out_hop2), (d_rows_z, out_z)
    to_zs = (d_rows_to_z, out_to_z)

    def sum_copy(a, kind, src, dst, peer):
        return remote(src, dst, sum_send.at[a, kind], sum_recv.at[a, kind], peer)

    def core_sum(a):
        return sum_copy(a, 0, tiles[a].at[:, 1 - at.c], cores[a], at.next_core)

    def row_hop(turn, other):
        y = lax.rem(at.y + other, 2)
        slot = parity(turn)
        src = d_rows_held.at[slot, y, 1 - at.x]
        return remote(
            src, d_rows_hop.at[slot, y], hop_send.at[slot, other], hop_recv.at[slot, other], at.next_x
        )

    def out_hop_sum(turn):
        slot = parity(turn)
        src = out_held.at[slot, 1 - at.y]
        return remote(
            src, out_hop.at[slot], hop_send.at[slot, 2], hop_recv.at[slot, 2], at.next_y
        )

    def hop2_sum(a, turn):
        slot = parity(turn)
        if a == 0:
            src, peer = helds[0].at[slot, 1 - at.y, at.x], at.next_y
        else:
            src, peer = helds[1].at[slot, at.y, 1 - at.x], at.next_x
        return sum_copy(a, 2, src, hops2[a], peer)

    def z_sum(a, turn):
        return remote(
            to_zs[a].at[parity(turn)],
            zs[a].at[turn],
            end_send.at[a, turn],
            end_recv.at[a, turn],
            at.at_z(at.behind(turn + 1)),
        )

    def allow(semaphore, peer):
        pl.semaphore_signal(semaphore, inc=1, device_id=peer, device_id_type=MESH)

    piece = 32

    def add(into, first, second):
        def body(i, carry):
            part = pl.ds(pl.multiple_of(i * piece, piece), piece)
            into[part] = first[part] + second[part]
            return carry

        lax.fori_loop(0, quarter // piece, body, 0)

    def after_core(step):
        turn = step // 2
        other = other_y(step)
        held, y = parity(turn), lax.rem(at.y + other, 2)

        @pl.when((parity(step) == 0) & (turn >= 2))
        def _():
            for a in (0, 1):
                pl.semaphore_wait(hop_credit.at[a], 1)

        for a in (0, 1):
            core_sum(a).wait()
            for x in (1 - at.x, at.x):
                add(helds[a].at[held, y, x], tiles[a].at[x, at.c], cores[a].at[x])
            if a == 0:
                row_hop(turn, other).start()
            else:

                @pl.when(other == 1)
                def _():
                    out_hop_sum(turn).start()

        @pl.when(step + 1 < 2 * depth)
        def _():
            allow(core_credit, at.next_core)

    def after_row_hop(turn, other):
        slot, y = parity(turn), lax.rem(at.y + other, 2)
        row_hop(turn, other).wait()
        into = d_rows_held.at[slot, y, at.x]
        add(into, into, d_rows_hop.at[slot, y])

    def after_out_hop(turn):
        slot = parity(turn)
        out_hop_sum(turn).wait()
        for x in (1 - at.x, at.x):
            into = out_held.at[slot, at.y, x]
            add(into, into, out_hop.at[slot, x])

    def may_hop2(turn, a):
        @pl.when(turn >= 1)
        def _():
            pl.semaphore_wait(hop2_credit.at[a], 1)

    def after_hop(turn):
        after_row_hop(turn, 1)
        may_hop2(turn, 0)
        hop2_sum(0, turn).start()
        after_row_hop(turn, 0)
        after_out_hop(turn)
        may_hop2(turn, 1)
        hop2_sum(1, turn).start()

        @pl.when(turn + 2 < depth)
        def _():
            allow(hop_credit.at[0], at.next_x)
            allow(hop_credit.at[1], at.next_y)

    def after_hop2(turn):
        slot = parity(turn)
        for a in (0, 1):
            hop2_sum(a, turn).wait()

            @pl.when(turn >= 2)
            def _():
                z_sum(a, turn - 2).wait_send()

            add(to_zs[a].at[slot], helds[a].at[slot, at.y, at.x], hops2[a])
            z_sum(a, turn).start()
        allow(hop2_credit.at[0], at.next_y)
        allow(hop2_credit.at[1], at.next_x)

    load_upstream(0).start()
    at.greet()
    z_copy(1).start()
    own_copy = pltpu.make_async_copy(rows_in, block(0, at.y, at.x), own_sem)
    own_copy.start()
    own_copy.wait()
    begin(0)
    begin_later(1)
    for k in range(2, depth):
        z_copy(k).start()
    spread(0)
    spread(1)
    near_ready(1)
    load_rows(0).start()
    for copy in weight_copies():
        copy.wait()

    tile_rows = 4 * quarter
    hidden_total = down_w.shape[0]
    lane = lax.broadcasted_iota(jnp.int32, (tile_rows, 128), 1)
    slot_here, slot_hidden, shared_hidden = units
    routed = slot_here * slot_hidden
    across = (((1,), (1,)), ((), ()))
    few = 16

    def gate_factors(rows, picked):
        logits = jnp.dot(rows, side_w[...], preferred_element_type=f32)
        chooses = (lane >= 3) & (lane < 3 + expert_count)
        peak = jnp.max(jnp.where(chooses, logits, -1e30), axis=1, keepdims=True)
        expo = jnp.where(chooses, jnp.exp(jnp.where(chooses, logits, peak) - peak), 0.0)
        routed_gate = expo / jnp.sum(expo, axis=1, keepdims=True) * picked.astype(f32)
        mix_pre = jnp.sum(jnp.where(lane == 2, logits, 0.0), axis=1, keepdims=True)
        result = jnp.where(lane == slot_here, 1.0 / (1.0 + jnp.exp(-mix_pre)), 0.0)
        for s in range(slot_here):
            chosen = lane == 3 + at.ep * slot_here + s
            gate = jnp.sum(jnp.where(chosen, routed_gate, 0.0), axis=1, keepdims=True)
            result = jnp.where(lane == s, gate, result)
        return result

    few_lane = lax.broadcasted_iota(jnp.int32, (few, 128), 1)
    bounds = [s * slot_hidden for s in range(slot_here)] + [routed, hidden_total]

    def owners(group):
        found = []
        for s in range(slot_here + 1):
            low, high = max(bounds[s] - group * 128, 0), min(bounds[s + 1] - group * 128, 128)
            if low < high:
                found.append((s, low, high))
        return found

    def hidden_rows(i, carry):
        here = pl.ds(pl.multiple_of(i * few, few), few)
        gates = [
            jnp.broadcast_to(factors[here, s : s + 1], (few, 128)) for s in range(slot_here + 1)
        ]
        parts = [None] * (slot_here + 1)
        for group in range(hidden_total // 128):
            units_here = slice(group * 128, (group + 1) * 128)
            units_up = slice(hidden_total + group * 128, hidden_total + (group + 1) * 128)
            gate_pre, up_pre = pair_pre[here, units_here], pair_pre[here, units_up]
            d_h = d_hidden[here, units_here]
            found = owners(group)
            factor = gates[found[0][0]]
            for s, low, _ in found[1:]:
                factor = jnp.where(few_lane >= low, gates[s], factor)
            sig = 0.5 + 0.5 * jnp.tanh(0.5 * gate_pre)
            silu = gate_pre * sig
            hidden = silu * up_pre
            product = hidden * d_h
            gated = factor * d_h
            weighted_tile[here, units_here] = (factor * hidden).astype(bf16)
            slope = sig + silu * (1.0 - sig)
            d_pair_tile[here, units_here] = (gated * up_pre * slope).astype(bf16)
            d_pair_tile[here, units_up] = (gated * silu).astype(bf16)
            for s, low, high in found:
                mine = product
                if high < 128:
                    mine = jnp.where(few_lane < high, mine, 0.0)
                if low > 0:
                    mine = jnp.where(few_lane >= low, mine, 0.0)
                parts[s] = mine if parts[s] is None else parts[s] + mine
        result = jnp.zeros((few, 128), f32)
        for s in range(slot_here + 1):
            dot = jnp.sum(parts[s], axis=1, keepdims=True)
            where = few_lane == (2 if s == slot_here else 3 + at.ep * slot_here + s)
            result = jnp.where(where, dot, result)
        dots[here] = result.astype(bf16)
        return carry

    def first_half(step):
        load_upstream(step).wait()
        upstream = upstream_tile[...].reshape(tile_rows, upstream_tile.shape[-1])
        d_hidden[...] = lax.dot_general(
            upstream[:, :width], down_w[...], across, preferred_element_type=f32
        )
        load_rows(step).wait()
        rows = rows_tile[...].reshape(tile_rows, width)
        factors[...] = gate_factors(rows, upstream[:, width:])
        pair_pre[...] = lax.dot_general(rows, pair_w[...], across, preferred_element_type=f32)

        @pl.when(step + 1 < 2 * depth)
        def _():
            load_upstream(step + 1).start()

        @pl.when(step >= 1)
        def _():
            for copy in stores(step - 1):
                copy.wait()

        lax.fori_loop(0, tile_rows // few, hidden_rows, 0, unroll=2)
        for copy in stores(step):
            copy.start()
        turn = step // 2

        @pl.when(step == 0)
        def _():
            last_hop(0)

        @pl.when((parity(step) == 0) & (turn + 1 < depth))
        def _():
            last_hop(turn + 1)

        @pl.when((step >= 1) & (step + 1 < depth))
        def _():
            spread(step + 1)

        @pl.when(step + 2 < depth)
        def _():
            begin_later(step + 2)

    def second_half(step):
        blocks = (2, 2, quarter)
        some = width // 2
        for n in range(2):
            columns = slice(n * some, (n + 1) * some)
            part = jnp.dot(weighted_tile[...], down_w[:, columns], preferred_element_type=f32)
            out_tile[:, :, :, columns] = part.astype(bf16).reshape(blocks + (some,))
            part = jnp.dot(d_pair_tile[...], pair_w[:, columns], preferred_element_type=f32)
            d_rows_tile[:, :, :, columns] = part.astype(bf16).reshape(blocks + (some,))
        d_rows_tile[:, :, :, width:] = dots[...].reshape(blocks + (128,))

        @pl.when(step >= 1)
        def _():
            pl.semaphore_wait(core_credit, 1)

        for a in (0, 1):
            core_sum(a).start()
        turn = step // 2

        @pl.when((parity(step) == 0) & (turn + 1 < depth))
        def _():
            far_ready(slot_of(turn))

        @pl.when((parity(step) == 1) & (turn + 1 < depth))
        def _():
            near_ready(slot_of(turn + 1))

        @pl.when(step == 2 * depth - 3)
        def _():
            far_ready(slot_of(turn + 1))

        @pl.when(step + 1 < 2 * depth)
        def _():
            load_rows(step + 1).start()

    def step_body(step, carry):
        first_half(step)

        @pl.when(step == 2 * depth - 1)
        def _():
            after_hop(depth - 2)

        @pl.when(step >= 1)
        def _():
            after_core(step - 1)

        second_half(step)
        odd = parity(step) == 1

        @pl.when(odd & (step >= 3) & (step < 2 * depth - 1))
        def _():
            after_hop((step - 3) // 2)

        @pl.when(jnp.logical_not(odd) & (step >= 4))
        def _():
            after_hop2((step - 4) // 2)

        return carry

    lax.fori_loop(0, 2 * depth, step_body, 0)
    last = depth - 1
    own_rows, own_upstream = rows_tile.at[0, 0], upstream_tile.at[0, 0]
    own_loads = [
        pltpu.make_async_copy(rows_in, own_rows, weight_sem.at[3]),
        pltpu.make_async_copy(
            upstream_in.at[at.z, at.y, at.x, at.c], own_upstream, weight_sem.at[4]
        ),
    ]
    for copy in own_loads:
        copy.start()
    after_hop2(last - 1)
    after_row_hop(last, 1)
    may_hop2(last, 0)
    hop2_sum(0, last).start()
    after_core(2 * depth - 1)
    after_out_hop(last)
    may_hop2(last, 1)
    hop2_sum(1, last).start()
    after_row_hop(last, 0)

    def total_of(a):
        hop2_sum(a, last).wait()
        held = helds[a].at[last % 2, at.y, at.x]
        for turn in range(last):
            z_sum(a, turn).wait_recv()

        def total_body(i, carry):
            part = pl.ds(pl.multiple_of(i * piece, piece), piece)
            total = held[part].astype(f32) + hops2[a][part].astype(f32)
            for k in range(last):
                total = total + zs[a][k, part].astype(f32)
            sums[a][part] = total
            return carry

        lax.fori_loop(0, quarter // piece, total_body, 0)

    total_of(0)
    own_lane = lax.broadcasted_iota(jnp.int32, (quarter, 128), 1)
    chooses = (own_lane >= 3) & (own_lane < 3 + expert_count)
    for copy in own_loads:
        copy.wait()
    rows = own_rows[...]
    logits = jnp.dot(rows, side_w[...], preferred_element_type=f32)
    peak = jnp.max(jnp.where(chooses, logits, -1e30), axis=1, keepdims=True)
    expo = jnp.where(chooses, jnp.exp(jnp.where(chooses, logits, peak) - peak), 0.0)
    router = expo / jnp.sum(expo, axis=1, keepdims=True)
    mixer = 1.0 / (1.0 + jnp.exp(-jnp.where(own_lane == 2, logits, 0.0)))
    gate_dots = d_rows_sum[:, width:]
    d_router = jnp.where(chooses, gate_dots * own_upstream[:, width:].astype(f32), 0.0)
    d_logits = router * (d_router - jnp.sum(router * d_router, axis=1, keepdims=True))
    d_mix = gate_dots * mixer * (1.0 - mixer)
    d_side = jnp.where(own_lane == 2, d_mix, jnp.where(chooses, d_logits, 0.0))
    d_side_out[...] = d_side
    high = d_side.astype(bf16)
    lower = (d_side - high.astype(f32)).astype(bf16)
    for split in (high, lower):
        d_rows_sum[:, :width] += lax.dot_general(
            split, side_w[...], across, preferred_element_type=f32
        )

    def end_body(i, carry):
        part = pl.ds(pl.multiple_of(i * few, few), few)
        resid = resid_in[part]
        scale = lax.rsqrt(jnp.mean(resid * resid, axis=1, keepdims=True) + epsilon)
        unit_rows = resid * scale
        grads = d_rows_sum[part, :width]
        scaled = grads * gain_in[...]
        inner = jnp.mean(scaled * unit_rows, axis=1, keepdims=True)
        d_resid = own_upstream[part, :width].astype(f32) + scale * (scaled - unit_rows * inner)
        d_resid_out[part] = d_resid
        d_resid_low[part] = d_resid.astype(bf16)
        return carry + jnp.sum(grads * unit_rows, axis=0, keepdims=True)

    d_gain_out[...] = lax.fori_loop(0, quarter // few, end_body, jnp.zeros((1, width), f32))

    def gather_copy(kind):
        if kind == 2:
            src = dst = d_resid_low_out.at[1 - at.x, at.c]
        else:
            src, dst = d_resid_low, d_resid_low_out.at[at.x, at.c]
        peer = at.next_x if kind == 0 else at.next_core
        return remote(src, dst, gathered_send.at[kind], gathered_recv.at[kind], peer)

    own_end = pltpu.make_async_copy(d_resid_low, d_resid_low_out.at[at.x, at.c], own_sem)
    own_end.start()
    for kind in (0, 1):
        gather_copy(kind).start()
    total_of(1)
    block_out[...] = (resid_in[...] + out_sum[...]).astype(bf16)
    gather_copy(0).wait_recv()
    gather_copy(2).start()
    own_end.wait()
    gather_copy(0).wait_send()
    gather_copy(1).wait()
    gather_copy(2).wait()
    for copy in stores(2 * depth - 1):
        copy.wait()
    for a in (0, 1):
        for turn in range(max(0, depth - 3), depth - 1):
            z_sum(a, turn).wait_send()
    for k in range(1, depth):
        z_copy(k).wait_send()

    def finish(j, carry):
        for kind in range(8):
            plane_copy(j, kind).wait_send()
        return carry

    lax.fori_loop(0, depth, finish, 0)


def ffn_over_all(rows, upstream_all, pair_w, down_w, side_w, resid, gain, units, expert_count):
    quarter, width = rows.shape
    ep_count, tp_count = lax.axis_size("ep"), lax.axis_size("tp")
    depth = ep_count // 2
    hidden = down_w.shape[0]
    bf16, f32 = jnp.bfloat16, jnp.float32
    wide = width + 128
    tile_rows = tp_count * quarter
    tokens = ep_count * tile_rows
    anywhere = pl.BlockSpec(memory_space=pl.ANY)
    in_vmem = pl.BlockSpec(memory_space=pltpu.VMEM)

    def both(*lead):
        return [pltpu.VMEM(lead + (quarter, columns), bf16) for columns in (wide, width)]

    dma = pltpu.SemaphoreType.DMA
    outs = pl.pallas_call(
        functools.partial(ffn_kernel, units, expert_count),
        out_shape=(
            jax.ShapeDtypeStruct((depth, 2, 2, 2, quarter, width), bf16),
            jax.ShapeDtypeStruct((depth, 2, tile_rows, hidden), bf16),
            jax.ShapeDtypeStruct((depth, 2, tile_rows, 2 * hidden), bf16),
            jax.ShapeDtypeStruct((quarter, width), bf16),
            jax.ShapeDtypeStruct((2, 2, quarter, width), bf16),
            jax.ShapeDtypeStruct((quarter, width), f32),
            jax.ShapeDtypeStruct((1, width), f32),
            jax.ShapeDtypeStruct((quarter, 128), f32),
        ),
        in_specs=[anywhere] * 5 + [in_vmem] * 2,
        out_specs=(anywhere,) * 3 + (in_vmem, anywhere) + (in_vmem,) * 3,
        scratch_shapes=[
            pltpu.VMEM((quarter, wide), f32),
            pltpu.VMEM((quarter, width), f32),
            pltpu.VMEM((2 * hidden, width), bf16),
            pltpu.VMEM((hidden, width), bf16),
            pltpu.VMEM((width, 128), bf16),
            pltpu.VMEM((2, 2, quarter, width), bf16),
            pltpu.VMEM((2, 2, quarter, wide), bf16),
            pltpu.VMEM((tile_rows, 2 * hidden), f32),
            pltpu.VMEM((tile_rows, hidden), f32),
            pltpu.VMEM((tile_rows, 128), f32),
            pltpu.VMEM((tile_rows, 128), bf16),
            pltpu.VMEM((tile_rows, hidden), bf16),
            pltpu.VMEM((tile_rows, 2 * hidden), bf16),
            pltpu.VMEM((quarter, width), bf16),
        ]
        + both(2, 2)
        + both(2)
        + both(2, 2, 2)
        + both(2, 2)
        + both()
        + both(depth - 1)
        + both(2)
        + [
            dma((3,)),
            dma((3,)),
            dma((2, 3)),
            dma((2, 3)),
            dma((5,)),
            dma,
            dma((depth - 1,)),
            dma((depth - 1,)),
            dma((depth, 8)),
            dma((depth, 8)),
            dma((2,)),
            dma((2,)),
            dma((2, 3)),
            dma((2, 3)),
            dma((2, depth - 1)),
            dma((2, depth - 1)),
            pltpu.SemaphoreType.REGULAR,
            pltpu.SemaphoreType.REGULAR((2,)),
            pltpu.SemaphoreType.REGULAR((2,)),
        ],
        compiler_params=pltpu.CompilerParams(
            collective_id=1, has_side_effects=True, vmem_limit_bytes=62 * 2**20
        ),
        cost_estimate=pl.CostEstimate(
            flops=12 * tokens * width * hidden,
            bytes_accessed=10 * tokens * width,
            transcendentals=tokens * hidden,
        ),
        name="ffn_all_tokens",
    )(
        rows,
        upstream_all.reshape(depth, 2, 2, 2, quarter, wide),
        pair_w,
        down_w,
        side_w,
        resid,
        gain,
    )
    rows_all, weighted, d_pair, block_out, d_resid_low, d_resid, d_gain, d_side = outs
    return (
        rows_all.reshape(tokens, width),
        weighted.reshape(tokens, hidden),
        d_pair.reshape(tokens, 2 * hidden),
        block_out,
        d_resid_low.reshape(tile_rows, width),
        d_resid,
        d_gain[0],
        d_side,
    )


def over_tp(block, distance):
    devices = range(lax.axis_size("tp"))
    return lax.ppermute(block, "tp", [(i, i ^ distance) for i in devices])


def one_of(array, index, axis):
    return lax.dynamic_index_in_dim(array, index, axis, keepdims=False)


def sum_over_tp(part):
    rows, columns = part.shape
    tp = lax.axis_index("tp")
    x, c = tp // 2, tp % 2
    blocks = part.reshape(2, 2, rows // 4, columns)
    got = over_tp(one_of(blocks, 1 - c, 1).astype(jnp.bfloat16), 1)
    chip = one_of(blocks, c, 1).astype(jnp.float32) + got.astype(jnp.float32)
    got = over_tp(one_of(chip, 1 - x, 0).astype(jnp.bfloat16), 2)
    return one_of(chip, x, 0) + got.astype(jnp.float32)


def gather_over_tp(block):
    tp = lax.axis_index("tp")
    x, c = tp // 2, tp % 2
    got = over_tp(block, 2)
    pair = jnp.where(x == 0, jnp.stack([block, got]), jnp.stack([got, block]))
    got = over_tp(pair, 1)
    four = jnp.where(c == 0, jnp.stack([pair, got], axis=1), jnp.stack([got, pair], axis=1))
    return four.reshape(4 * block.shape[0], block.shape[1])


def swap_copies(at, pieces_in, pieces_out, send_sem, recv_sem, leave):
    count = 2 * at.depth
    copies = []
    for k in range(1, count):
        to, back = lax.rem(at.ep + k, count), lax.rem(at.ep + count - k, count)
        if leave:
            src, dst, peer = pieces_in.at[to], pieces_out.at[at.ep], to
        else:
            src, dst, peer = pieces_in.at[back], pieces_out.at[back], back
        copies.append(remote(src, dst, send_sem.at[k], recv_sem.at[k], (peer, at.tp)))
    return copies


def weights_kernel(
    own_in,
    pieces_in,
    all_out,
    pieces_out,
    own_sem,
    z_send,
    z_recv,
    y_send,
    y_recv,
    swap_send,
    swap_recv,
):
    at = Place()
    depth = at.depth
    half = own_in.shape[0] // 2
    last = depth - 1

    def block(k, y, h):
        return all_out.at[at.z + k, y, pl.ds(h * half, half)]

    def z_copy(k, h, direction):
        if k == 0:
            src = own_in.at[pl.ds(h * half, half)]
        else:
            src = block(k, at.y, h)
        slot = last + k - direction
        return remote(
            src,
            block(k, at.y, h),
            z_send.at[last + k, h, (direction + 1) // 2],
            z_recv.at[slot, h],
            at.at_z(at.z + direction),
        )

    def z_arrival(k, h):
        direction = 1 if k > 0 else -1
        dst = block(k, at.y, h)
        return remote(
            dst, dst, z_send.at[last + k, h, 0], z_recv.at[last + k, h], at.at_z(at.z + direction)
        )

    def y_copy(k, h):
        src = own_in.at[pl.ds(h * half, half)] if k == 0 else block(k, at.y, h)
        return remote(
            src, block(k, at.y, h), y_send.at[last + k, h], y_recv.at[last + k, h], at.next_y
        )

    own_copies = [
        pltpu.make_async_copy(own_in, all_out.at[at.z, at.y], own_sem.at[0]),
        pltpu.make_async_copy(pieces_in.at[at.ep], pieces_out.at[at.ep], own_sem.at[1]),
    ]
    for copy in own_copies:
        copy.start()
    has_up, has_down = at.z + 1 < depth, at.z > 0
    at.greet_ep()

    for h in (0, 1):
        pl.when(has_up)(lambda: z_copy(0, h, 1).start())
        pl.when(has_down)(lambda: z_copy(0, h, -1).start())
        y_copy(0, h).start()
    swap = (at, pieces_in, pieces_out, swap_send, swap_recv)
    for copy in swap_copies(*swap, True):
        copy.start()
    for k in range(1, depth):
        for h in (0, 1):
            for sign in (-1, 1):
                there = at.z + sign * k
                exists = (there >= 0) & (there < depth)
                onward = at.z - sign
                goes_on = exists & (onward >= 0) & (onward < depth)

                @pl.when(exists)
                def _():
                    z_arrival(sign * k, h).wait_recv()

                @pl.when(goes_on)
                def _():
                    z_copy(sign * k, h, -sign).start()

                @pl.when(exists)
                def _():
                    y_copy(sign * k, h).start()

    for copy in own_copies:
        copy.wait()
    for copy in swap_copies(*swap, False):
        copy.wait_recv()
    for copy in swap_copies(*swap, True):
        copy.wait_send()
    for h in (0, 1):
        pl.when(has_up)(lambda: z_copy(0, h, 1).wait_send())
        pl.when(has_down)(lambda: z_copy(0, h, -1).wait_send())
    for k in range(-last, depth):
        there = at.z + k
        exists = (there >= 0) & (there < depth)
        sign = 1 if k > 0 else -1
        onward = at.z - sign
        goes_on = exists & (onward >= 0) & (onward < depth)
        for h in (0, 1):

            @pl.when(exists)
            def _():
                y_copy(k, h).wait()

            if k != 0:

                @pl.when(goes_on)
                def _():
                    z_copy(k, h, -sign).wait_send()


def gather_over_ep(block, pieces):
    rows, columns = block.shape
    depth = lax.axis_size("ep") // 2
    anywhere = pl.BlockSpec(memory_space=pl.ANY)
    slots = 2 * depth - 1
    out, pieces = pl.pallas_call(
        weights_kernel,
        out_shape=(
            jax.ShapeDtypeStruct((depth, 2, rows, columns), block.dtype),
            jax.ShapeDtypeStruct(pieces.shape, pieces.dtype),
        ),
        in_specs=[anywhere] * 2,
        out_specs=(anywhere,) * 2,
        scratch_shapes=[
            pltpu.SemaphoreType.DMA((2,)),
            pltpu.SemaphoreType.DMA((slots, 2, 2)),
            pltpu.SemaphoreType.DMA((slots, 2)),
            pltpu.SemaphoreType.DMA((slots, 2)),
            pltpu.SemaphoreType.DMA((slots, 2)),
            pltpu.SemaphoreType.DMA((2 * depth,)),
            pltpu.SemaphoreType.DMA((2 * depth,)),
        ],
        compiler_params=pltpu.CompilerParams(collective_id=3, has_side_effects=True),
        cost_estimate=pl.CostEstimate(
            flops=0, bytes_accessed=8 * depth * rows * columns, transcendentals=0
        ),
        name="gather_weights",
    )(block, pieces)
    return out.reshape(2 * depth * rows, columns), pieces


def back_kernel(
    units,
    score_scale,
    d_low_in,
    weights_in,
    q_in,
    k_in,
    v_in,
    turned_in,
    block_in,
    rows_in,
    d_pair_in,
    upstream_in,
    weighted_in,
    lse_in,
    query_start,
    query_at,
    cos_in,
    sin_in,
    own_rows_in,
    gain_in,
    d_resid_in,
    gain_two_in,
    side_in,
    out,
    small_out,
    block_out,
    d_rows_out,
    pieces_got,
    gate_out,
    up_out,
    down_out,
    qkv_w,
    turned,
    d_out,
    d_got,
    d_own,
    d_proj,
    part,
    core_got,
    x_got,
    d_rows,
    own,
    y_out,
    hop,
    from_z,
    small_own,
    small_hop,
    small_z,
    small,
    small_got,
    pieces,
    load_sem,
    d_send,
    d_recv,
    tp_send,
    tp_recv,
    y_send,
    y_recv,
    z_send,
    z_recv,
    little_send,
    little_recv,
    small_send,
    small_recv,
    swap_send,
    swap_recv,
    rows_send,
    rows_recv,
    own_sem,
    tile_sem,
    store_sem,
    strip_sem,
):
    at = Place()
    depth = at.depth
    count = 2 * depth
    heads, tokens, head = q_in.shape
    heads_width = heads * head
    windows = k_in.shape[1] // tokens
    quarter, width = d_rows.shape
    rows = out.shape[0]
    f32, bf16 = jnp.float32, jnp.bfloat16
    across = (((1,), (1,)), ((), ()))
    slot_here, slot_hidden, shared_hidden = units
    routed = slot_here * slot_hidden
    hidden = weighted_in.shape[2]
    few = 16

    def d_copy(w, h):
        peer = (at.ep - (2 - w), at.tp)
        return remote(d_out.at[w, h], d_got.at[w, h], d_send.at[w, h], d_recv.at[w, h], peer)

    def d_arrival(w, h):
        peer = (at.ep + (2 - w), at.tp)
        dst = d_got.at[w, h]
        return remote(dst, dst, d_send.at[w, h], d_recv.at[w, h], peer)

    def core_copy():
        return remote(part.at[:, 1 - at.c], core_got, tp_send.at[0], tp_recv.at[0], at.next_core)

    def x_copy():
        return remote(part.at[1 - at.x, at.c], x_got, tp_send.at[1], tp_recv.at[1], at.next_x)

    cuts = (pl.ds(0, heads_width), pl.ds(heads_width, 2 * heads_width))

    def y_copy(q, j):
        return remote(
            y_out.at[j, :, cuts[q]], hop.at[j, :, cuts[q]], y_send.at[q, j], y_recv.at[q, j], at.next_y
        )

    def z_copy(q, j):
        return remote(
            own.at[j, :, cuts[q]],
            from_z.at[j - 1, :, cuts[q]],
            z_send.at[q, j],
            z_recv.at[q, j],
            at.at_z(at.ahead(j)),
        )

    def little_y(j):
        return remote(
            small_own.at[at.ahead(j), 1 - at.y],
            small_hop.at[j],
            little_send.at[0, j],
            little_recv.at[0, j],
            at.next_y,
        )

    def little_z(j):
        return remote(
            small_own.at[at.ahead(j), at.y],
            small_z.at[j - 1],
            little_send.at[1, j],
            little_recv.at[1, j],
            at.at_z(at.ahead(j)),
        )

    def small_copy(kind):
        peer = at.next_core if kind == 0 else at.next_x
        return remote(
            small.at[kind], small_got.at[kind], small_send.at[kind], small_recv.at[kind], peer
        )

    ends = ((block_in, block_out), (d_rows, d_rows_out))

    def rows_copy(a, kind):
        mine, gathered = ends[a]
        if kind == 2:
            src = dst = gathered.at[1 - at.x, at.c]
        else:
            src, dst = mine, gathered.at[at.x, at.c]
        peer = at.next_x if kind == 0 else at.next_core
        return remote(src, dst, rows_send.at[a, kind], rows_recv.at[a, kind], peer)

    def rows_own(a):
        mine, gathered = ends[a]
        return pltpu.make_async_copy(mine, gathered.at[at.x, at.c], own_sem.at[a])

    def rows_begin(a):
        for kind in (0, 1):
            rows_copy(a, kind).start()
        rows_own(a).start()

    def rows_pass_on(a):
        rows_copy(a, 0).wait_recv()
        rows_copy(a, 2).start()

    def rows_end(a):
        rows_own(a).wait()
        rows_copy(a, 0).wait_send()
        rows_copy(a, 1).wait()
        rows_copy(a, 2).wait()

    def swap_copies(p, leave):
        some = pl.ds(p * shared_hidden, shared_hidden)
        copies = []
        for k in range(1, count):
            to, back = lax.rem(at.ep + k, count), lax.rem(at.ep + count - k, count)
            if leave:
                src, dst, peer = pieces.at[to, some], pieces_got.at[at.ep, some], to
            else:
                src, dst, peer = pieces.at[back, some], pieces_got.at[back, some], back
            copies.append(remote(src, dst, swap_send.at[p, k], swap_recv.at[p, k], (peer, at.tp)))
        return copies

    def swap_own(p):
        some = pl.ds(p * shared_hidden, shared_hidden)
        return pltpu.make_async_copy(
            pieces.at[at.ep, some], pieces_got.at[at.ep, some], own_sem.at[2 + p]
        )

    strips = 4
    strip = width // strips

    def load_strip(n):
        src = weights_in.at[pl.ds(n * strip, strip), pl.ds(0, 3 * heads_width)]
        return pltpu.make_async_copy(src, qkv_w.at[n % 2], strip_sem.at[n % 2])

    late_load = pltpu.make_async_copy(turned_in, turned, load_sem.at[1])
    lane = lax.broadcasted_iota(jnp.int32, (tokens, head), 1)
    sign = jnp.where(lane < head // 2, -1.0, 1.0)

    def unrotated(grads):
        turned_part = pltpu.roll(grads * sin_in[...], head // 2, 1) * sign
        return grads * cos_in[...] - turned_part

    def attention(d_low, out_w, q_all, k_all, v_all, d_att, probs, d_probs):
        pairs = (
            (d_low_in, d_low),
            (weights_in.at[:, pl.ds(3 * heads_width, heads_width)], out_w),
            (q_in, q_all),
            (k_in, k_all),
            (v_in, v_all),
        )
        copies = [
            pltpu.make_async_copy(src, dst, load_sem.at[2 + i])
            for i, (src, dst) in enumerate(pairs)
        ]
        for copy in copies + [late_load, load_strip(0), load_strip(1)]:
            copy.start()
        at.greet_row()
        rows_begin(0)
        copies[0].wait()
        copies[1].wait()
        d_attended = jnp.dot(d_low[...], out_w[...], preferred_element_type=f32).astype(bf16)
        for h in range(heads):
            d_att[h] = d_attended[:, h * head : (h + 1) * head]
        for copy in copies[2:]:
            copy.wait()

        def head_body(h, carry):
            queries, d_a = q_all[h], d_att[h]
            delta = jnp.zeros((1, tokens), f32)
            for w in range(windows):
                some = slice(w * tokens, (w + 1) * tokens)
                scores = lax.dot_general(
                    k_all[h, some], queries, across, preferred_element_type=f32
                )
                key_at = lax.broadcasted_iota(jnp.int32, scores.shape, 0)
                key_at = key_at + (at.ep + w + 1 - windows) * tokens
                allowed = (key_at >= query_start[...]) & (key_at <= query_at[...])
                p = jnp.where(allowed, jnp.exp(scores * score_scale - lse_in[h]), 0.0)
                d_p = lax.dot_general(v_all[h, some], d_a, across, preferred_element_type=f32)
                probs[w] = p
                d_probs[w] = d_p
                delta = delta + jnp.sum(p * d_p, axis=0, keepdims=True)
            d_queries = jnp.zeros((head, tokens), f32)
            for w in range(windows):
                some = slice(w * tokens, (w + 1) * tokens)
                p = probs[w]
                d_scores = (p * (d_probs[w] - delta)).astype(bf16)
                d_keys = jnp.dot(d_scores, queries, preferred_element_type=f32) * score_scale
                d_values = jnp.dot(p.astype(bf16), d_a, preferred_element_type=f32)
                if w < windows - 1:
                    d_out[w, h, :, :head] = d_keys.astype(bf16)
                    d_out[w, h, :, head:] = d_values.astype(bf16)

                    @pl.when(at.ep >= 2 - w)
                    def _():
                        d_copy(w, h).start()

                else:
                    d_own[h, :, :head] = d_keys
                    d_own[h, :, head:] = d_values
                d_queries = d_queries + jnp.dot(
                    k_all[h, some].T, d_scores, preferred_element_type=f32
                )
            here = pl.ds(pl.multiple_of(h * head, head), head)
            d_proj[:, here] = unrotated((d_queries * score_scale).T).astype(bf16)
            return carry

        lax.fori_loop(0, heads, head_body, 0)

    pl.run_scoped(
        attention,
        pltpu.VMEM((tokens, width), bf16),
        pltpu.VMEM((width, heads_width), bf16),
        pltpu.VMEM((heads, tokens, head), bf16),
        pltpu.VMEM((heads, windows * tokens, head), bf16),
        pltpu.VMEM((heads, windows * tokens, head), bf16),
        pltpu.VMEM((heads, tokens, head), bf16),
        pltpu.VMEM((windows, tokens, tokens), f32),
        pltpu.VMEM((windows, tokens, tokens), f32),
    )
    order = [j for j in range(1, depth)] + [0]

    def own_body(h, carry):
        for w in range(windows - 1):

            @pl.when(at.ep + (2 - w) < count)
            def _():
                d_arrival(w, h).wait_recv()
                d_own[h] += d_got[w, h].astype(f32)

        k_here = pl.ds(pl.multiple_of(heads_width + h * head, head), head)
        v_here = pl.ds(pl.multiple_of(2 * heads_width + h * head, head), head)
        d_proj[:, k_here] = unrotated(d_own[h, :, :head]).astype(bf16)
        d_proj[:, v_here] = d_own[h, :, head:].astype(bf16)
        return carry

    def weight_rows(into, q, z, y):
        here = pl.ds(pl.multiple_of((z * 2 + y) * rows, rows), rows)
        product = jnp.dot(turned[here], d_proj[:, cuts[q]], preferred_element_type=f32)
        into[:, cuts[q]] = product.astype(bf16)

    def begin_sums(q):
        for j in order:
            weight_rows(y_out.at[j], q, at.ahead(j), 1 - at.y)
            y_copy(q, j).start()

    def own_sums(q):
        for j in order:
            weight_rows(own.at[j], q, at.ahead(j), at.y)

    def projections():
        lax.fori_loop(0, heads, own_body, 0)
        for n in range(strips):
            some = slice(n * strip, (n + 1) * strip)
            load_strip(n).wait()
            product = lax.dot_general(
                d_proj[...], qkv_w[n % 2], across, preferred_element_type=f32
            )
            part[:, :, :, some] = product.astype(bf16).reshape(2, 2, quarter, strip)
            if n + 2 < strips:
                load_strip(n + 2).start()
        core_copy().start()
        begin_sums(1)
        core_copy().wait()
        for x in (0, 1):
            part[x, at.c] = part[x, at.c] + core_got[x]
        x_copy().start()
        own_sums(1)
        x_copy().wait()

        def end_body(i, carry):
            here = pl.ds(pl.multiple_of(i * few, few), few)
            grads = part[at.x, at.c, here].astype(f32) + x_got[here].astype(f32)
            inputs = own_rows_in[here].astype(f32)
            scale = lax.rsqrt(jnp.mean(inputs * inputs, axis=1, keepdims=True) + epsilon)
            unit_rows = inputs * scale
            scaled = grads * gain_in[...]
            inner = jnp.mean(scaled * unit_rows, axis=1, keepdims=True)
            total = d_resid_in[here] + scale * (scaled - unit_rows * inner)
            d_rows[here] = total.astype(bf16)
            return carry + jnp.sum(grads * unit_rows, axis=0, keepdims=True)

        d_gain = lax.fori_loop(0, quarter // few, end_body, jnp.zeros((1, width), f32))
        rows_begin(1)
        line = lax.broadcasted_iota(jnp.int32, (128, rows), 0)
        for e in range(count):
            some = slice(e * rows, (e + 1) * rows)
            gains = jnp.where(line == 0, d_gain[:, some], 0.0)
            gains = jnp.where(line == 1, gain_two_in[:, some], gains)
            small_own[e // 2, e % 2] = (gains.T + side_in[some]).astype(bf16)
        for j in order:
            little_y(j).start()

    def after_y(q, j):
        y_copy(q, j).wait_recv()

        def body(i, carry):
            some = pl.ds(pl.multiple_of(i * few, few), few)
            own[j, some, cuts[q]] = own[j, some, cuts[q]] + hop[j, some, cuts[q]]
            return carry

        lax.fori_loop(0, rows // few, body, 0)
        if j > 0:
            z_copy(q, j).start()

    def after_little():
        for j in order:
            little_y(j).wait_recv()
            here = small_own.at[at.ahead(j), at.y]
            here[...] = here[...] + small_hop[j]
            if j > 0:
                little_z(j).start()

    hooks = {(0, 0): [functools.partial(rows_pass_on, 0)]}
    for i, j in enumerate(order):
        hooks.setdefault((0, min(2 * i + 1, count - 1)), []).append(functools.partial(after_y, 0, j))
    hooks[(1, 2)] = [functools.partial(rows_pass_on, 1)]
    hooks[(1, 3)] = [after_little]
    last_hooks = []
    for i, j in enumerate(order):
        when = count + 5 + 5 * i
        due = functools.partial(after_y, 1, j)
        if when < 3 * count:
            hooks.setdefault((when // count, when % count), []).append(due)
        else:
            last_hooks.append(due)

    def weight_gradients(turned_left, left_tile, right_part, staging):
        lefts = (
            lambda tile: d_pair_in.at[tile, :, pl.ds(0, hidden)],
            lambda tile: d_pair_in.at[tile, :, pl.ds(hidden, hidden)],
            lambda tile: weighted_in.at[tile],
        )
        rights = (rows_in, rows_in, upstream_in)
        results = (gate_out, up_out, down_out)
        columns = width // count

        def load_left(p, tile):
            slot = lax.rem(tile, 2)
            return pltpu.make_async_copy(
                lefts[p](tile), left_tile.at[slot], tile_sem.at[0, slot]
            )

        def load_right(p, n):
            slot = lax.rem(n, 2)
            here = pl.ds(pl.multiple_of(n * columns, columns), columns)
            return pltpu.make_async_copy(
                rights[p].at[:, :, here], right_part.at[slot], tile_sem.at[1, slot]
            )

        def store(p, n):
            slot = lax.rem(n, 2)
            here = pl.ds(pl.multiple_of(n * columns, columns), columns)
            return pltpu.make_async_copy(
                staging.at[slot], results[p].at[:, here], store_sem.at[slot]
            )

        def turn_left(p, tile):
            load_left(p, tile).wait()

            @pl.when(tile + 1 < count)
            def _():
                load_left(p, tile + 1).start()

            here = pl.ds(pl.multiple_of(tile * tokens, tokens), tokens)
            turned_left[:, here] = left_tile[lax.rem(tile, 2)].T

        def run_pass(p):
            def part_body(n, carry):
                slot = lax.rem(n, 2)
                load_right(p, n).wait()

                @pl.when(n + 1 < count)
                def _():
                    load_right(p, n + 1).start()

                if p < 2:

                    @pl.when(n + 1 == count)
                    def _():
                        load_right(p + 1, 0).start()

                @pl.when(n >= 2)
                def _():
                    store(p, n - 2).wait()

                product = jnp.dot(
                    turned_left[...],
                    right_part[slot].reshape(count * tokens, columns),
                    preferred_element_type=f32,
                )
                staging[slot] = product[:routed].astype(bf16)
                pieces[n, p * shared_hidden : (p + 1) * shared_hidden] = product[
                    routed : routed + shared_hidden
                ].astype(bf16)
                store(p, n).start()
                for (hook_pass, hook_part), actions in hooks.items():
                    if hook_pass == p:

                        @pl.when(n == hook_part)
                        def _():
                            for action in actions:
                                action()

                return carry

            def turn_body(tile, carry):
                turn_left(p, tile)
                return carry

            lax.fori_loop(0, count, turn_body, 0)
            if p < 2:
                load_left(p + 1, 0).start()
            lax.fori_loop(0, count, part_body, 0)
            for n in (count - 2, count - 1):
                store(p, n).wait()
            swap_own(p).start()
            for copy in swap_copies(p, True):
                copy.start()

        load_left(0, 0).start()
        load_right(0, 0).start()
        late_load.wait()
        begin_sums(0)
        own_sums(0)

        run_pass(0)
        projections()
        run_pass(1)
        run_pass(2)
        for action in last_hooks:
            action()

    pl.run_scoped(
        weight_gradients,
        pltpu.VMEM((hidden, count * tokens), bf16),
        pltpu.VMEM((2, tokens, hidden), bf16),
        pltpu.VMEM((2, count, tokens, width // count), bf16),
        pltpu.VMEM((2, routed, width // count), bf16),
    )
    total = small_own[at.z, at.y].astype(f32)
    for j in range(1, depth):
        little_z(j).wait_recv()
        total = total + small_z[j - 1].astype(f32)
    for kind in (0, 1):
        small[kind] = total
        small_copy(kind).start()
        small_copy(kind).wait()
        total = small[kind] + small_got[kind]
    small_out[...] = total
    for j in range(1, depth):
        for q in (0, 1):
            z_copy(q, j).wait_recv()

    def total_body(i, carry):
        some = pl.ds(pl.multiple_of(i * few, few), few)
        result = own[0, some].astype(f32)
        for k in range(depth - 1):
            result = result + from_z[k, some].astype(f32)
        out[some] = result
        return carry

    lax.fori_loop(0, rows // few, total_body, 0)
    for j in range(depth):
        little_y(j).wait_send()
        if j > 0:
            little_z(j).wait_send()
        for q in (0, 1):
            y_copy(q, j).wait_send()
            if j > 0:
                z_copy(q, j).wait_send()
    for a in (0, 1):
        rows_end(a)
    for p in range(3):
        swap_own(p).wait()
        for copy in swap_copies(p, False):
            copy.wait_recv()
        for copy in swap_copies(p, True):
            copy.wait_send()

    def finish(h, carry):
        for w in range(windows - 1):

            @pl.when(at.ep >= 2 - w)
            def _():
                d_copy(w, h).wait_send()

        return carry

    lax.fori_loop(0, heads, finish, 0)


def backward(large, tiles_of, in_place, units, scale):
    d_low, _, queries, keys = large[:4]
    heads, tokens, head = queries.shape
    width = d_low.shape[1]
    ep_count = lax.axis_size("ep")
    depth, rows = ep_count // 2, width // ep_count
    quarter = tokens // lax.axis_size("tp")
    windows = keys.shape[1] // tokens
    columns = 3 * heads * head
    hidden = tiles_of[3].shape[2]
    slot_here, slot_hidden, shared_hidden = units
    f32, bf16 = jnp.float32, jnp.bfloat16
    anywhere = pl.BlockSpec(memory_space=pl.ANY)
    in_vmem = pl.BlockSpec(memory_space=pltpu.VMEM)
    dma = pltpu.SemaphoreType.DMA
    pieces = (ep_count, 3 * shared_hidden, rows)
    gathered = jax.ShapeDtypeStruct((2, 2, quarter, width), bf16)
    routed = jax.ShapeDtypeStruct((slot_here * slot_hidden, width), bf16)

    def vmem(*shape, dtype=bf16):
        return pltpu.VMEM(shape, dtype)

    out, small, block_out, d_rows, pieces, gate, up, down = pl.pallas_call(
        functools.partial(back_kernel, units, scale),
        out_shape=(
            jax.ShapeDtypeStruct((rows, columns), f32),
            jax.ShapeDtypeStruct((rows, 128), f32),
            gathered,
            gathered,
            jax.ShapeDtypeStruct(pieces, bf16),
            routed,
            routed,
            routed,
        ),
        in_specs=[anywhere] * (len(large) + len(tiles_of)) + [in_vmem] * len(in_place),
        out_specs=(in_vmem, in_vmem) + (anywhere,) * 6,
        scratch_shapes=[
            vmem(2, width // 4, columns),
            vmem(width, tokens),
            vmem(windows - 1, heads, tokens, 2 * head),
            vmem(windows - 1, heads, tokens, 2 * head),
            vmem(heads, tokens, 2 * head, dtype=f32),
            vmem(tokens, columns),
            vmem(2, 2, quarter, width),
            vmem(2, quarter, width),
            vmem(quarter, width),
            vmem(quarter, width),
            vmem(depth, rows, columns),
            vmem(depth, rows, columns),
            vmem(depth, rows, columns),
            vmem(depth - 1, rows, columns),
            vmem(depth, 2, rows, 128),
            vmem(depth, rows, 128),
            vmem(depth - 1, rows, 128),
            vmem(2, rows, 128, dtype=f32),
            vmem(2, rows, 128, dtype=f32),
            vmem(*pieces),
            dma((7,)),
            dma((windows - 1, heads)),
            dma((windows - 1, heads)),
            dma((2,)),
            dma((2,)),
            dma((2, depth)),
            dma((2, depth)),
            dma((2, depth)),
            dma((2, depth)),
            dma((2, depth)),
            dma((2, depth)),
            dma((2,)),
            dma((2,)),
            dma((3, ep_count)),
            dma((3, ep_count)),
            dma((2, 3)),
            dma((2, 3)),
            dma((5,)),
            dma((2, 2)),
            dma((2,)),
            dma((2,)),
        ],
        compiler_params=pltpu.CompilerParams(
            collective_id=4, has_side_effects=True, vmem_limit_bytes=62 * 2**20
        ),
        cost_estimate=pl.CostEstimate(
            flops=6 * ep_count * tokens * width * hidden,
            bytes_accessed=8 * ep_count * tokens * width,
            transcendentals=heads * tokens * windows * tokens,
        ),
        name="backward",
    )(*large, *tiles_of, *in_place)
    block_out, d_rows = [array.reshape(4 * quarter, width) for array in (block_out, d_rows)]
    return out, small, block_out, d_rows, pieces, (gate, up, down)


def shared_pieces(weights, ep_count):
    rows, hidden = weights[0].shape
    units = hidden // ep_count
    return jnp.concatenate([weight.T.reshape(ep_count, units, rows) for weight in weights], axis=1)


def shared_units_of(pieces, count):
    ep_count, units, rows = pieces.shape
    return pieces.transpose(1, 0, 2).reshape(count, units // count, ep_count * rows)


def shared_whole(pieces, count):
    ep_count, units, columns = pieces.shape
    units = units // count
    pieces = pieces.reshape(ep_count, count, units, columns).astype(jnp.float32)
    return [pieces[:, i].reshape(ep_count * units, columns).T for i in range(count)]


def dense_body(
    tokens,
    lengths,
    routes,
    attn_gain,
    w_query,
    w_key,
    w_value,
    w_out,
    ffn_gain,
    w_router,
    shared_mix,
    shared_gate,
    shared_up,
    shared_down,
    expert_gate,
    expert_up,
    expert_down,
    cotangent,
):
    everywhere = ("ep", "tp")
    rows_here, width = tokens.shape
    ep_count = lax.axis_size("ep")
    tp_count = lax.axis_size("tp")
    ep_index = lax.axis_index("ep")
    offset = ep_index * rows_here
    quarter = rows_here // tp_count
    first_row = lax.axis_index("tp") * quarter
    slot_here, slot_hidden = expert_gate.shape[0], expert_gate.shape[1]
    expert_count = w_router.shape[1]
    bf16, f32 = jnp.bfloat16, jnp.float32

    def my_rows(array):
        return lax.dynamic_slice_in_dim(array, first_row, quarter, 0)

    side_columns = jnp.concatenate(
        [attn_gain[:, None], ffn_gain[:, None], shared_mix[:, None], w_router], axis=1
    )
    side_columns = jnp.pad(side_columns, ((0, 0), (0, -side_columns.shape[1] % 128)))
    joined_weights, pieces = gather_over_ep(
        jnp.concatenate([w_query, w_key, w_value, w_out, side_columns], axis=1),
        shared_pieces((shared_gate, shared_up, shared_down), ep_count),
    )
    cotangent_rows = my_rows(cotangent)
    joined_weights, cotangent_rows = lax.optimization_barrier((joined_weights, cotangent_rows))
    heads_width = w_query.shape[1]
    qkv_weight = joined_weights[:, : 3 * heads_width]
    output_weight = joined_weights[:, 3 * heads_width : 4 * heads_width]
    side_weight = joined_weights[:, 4 * heads_width :]
    picked = jnp.any(
        my_rows(routes)[:, :, None] == jnp.arange(expert_count, dtype=jnp.int32), axis=1
    )
    picked_lanes = jnp.pad(picked.astype(bf16), ((0, 0), (3, 125 - expert_count)))
    upstream_all = lax.all_gather(
        jnp.concatenate([cotangent_rows, picked_lanes], axis=1), everywhere, axis=0, tiled=True
    )
    shared_rows = shared_units_of(pieces, 3)
    shared_units = shared_rows.shape[1]
    routed_units = slot_here * slot_hidden
    gate_cat, up_cat, down_cat = [
        jnp.pad(
            jnp.concatenate([expert.reshape(-1, width), shared], axis=0),
            ((0, -(routed_units + shared_units) % 128), (0, 0)),
        )
        for expert, shared in zip((expert_gate, expert_up, expert_down), shared_rows)
    ]
    pair_cat = jnp.concatenate([gate_cat, up_cat], axis=0)
    hidden_total = gate_cat.shape[0]

    heads_here = heads_width // HD
    score_scale = HD ** (-0.5)
    first_norm_scale = side_weight[:, 0].astype(f32)
    second_norm_scale = side_weight[:, 1].astype(f32)
    mix_f = side_weight[:, 2].astype(f32)
    router_f = side_weight[:, 3 : 3 + expert_count].astype(f32)
    layer_input = tokens.astype(f32)
    normed_wide, norm_one = norm_forward(layer_input, first_norm_scale)
    normed_one = normed_wide.astype(bf16)
    query_at = offset + jnp.arange(rows_here, dtype=jnp.int32)
    key_at = offset - 2 * rows_here + jnp.arange(3 * rows_here, dtype=jnp.int32)
    query_seg, query_pos = sequence_info(lengths, query_at)
    key_seg, _ = sequence_info(lengths, key_at)
    cosine, sine = rope_tables(query_pos, HD)
    projected = jnp.dot(normed_one, qkv_weight, preferred_element_type=f32)
    projected = projected.reshape(rows_here, 3, heads_here, HD)
    queries = rotate(projected[:, 0], cosine, sine).astype(bf16)
    keys = rotate(projected[:, 1], cosine, sine).astype(bf16)
    values = projected[:, 2].astype(bf16)
    carried = jnp.stack([keys, values], axis=0)
    joined = jnp.concatenate(
        [passed_along(carried, "ep", 2), passed_along(carried, "ep", 1), carried], axis=1
    )
    keys_win = joined[0]
    values_win = joined[1]
    allowed = (
        (query_seg[:, None] == key_seg[None, :])
        & (key_at[None, :] <= query_at[:, None])
        & (key_at[None, :] >= 0)
    )
    scores = (
        jnp.einsum("qhd,khd->hqk", queries, keys_win, preferred_element_type=f32) * score_scale
    )
    masked = jnp.where(allowed[None], scores, -1e30)
    peak = jnp.max(masked, axis=-1, keepdims=True)
    expo = jnp.exp(masked - peak)
    total = jnp.sum(expo, axis=-1, keepdims=True)
    log_total = peak + jnp.log(total)
    weights = expo / total
    attended = jnp.einsum(
        "hqk,khd->qhd", weights.astype(bf16), values_win, preferred_element_type=f32
    )
    attended = attended.reshape(rows_here, heads_width).astype(bf16)
    attn_part = jnp.einsum("th,dh->td", attended, output_weight, preferred_element_type=f32)
    resid = my_rows(layer_input) + sum_over_tp(attn_part)
    normed_two_wide, norm_two = norm_forward(resid, second_norm_scale)
    normed_two = normed_two_wide.astype(bf16)

    (
        normed_all,
        weighted_h,
        d_pair_pre,
        block_rows,
        d_resid_low,
        d_resid,
        grad_gain_two,
        d_side,
    ) = ffn_over_all(
        normed_two,
        upstream_all,
        pair_cat,
        down_cat,
        side_weight,
        resid,
        second_norm_scale[None, :],
        (slot_here, slot_hidden, shared_units),
        expert_count,
    )
    grad_side = jnp.dot(normed_two.astype(f32).T, d_side, precision=highest)
    grad_out = jnp.einsum("td,th->dh", d_resid_low, attended, preferred_element_type=f32)
    grad_out = lax.psum_scatter(
        grad_out.astype(bf16), "ep", scatter_dimension=0, tiled=True
    ).astype(f32)
    def by_head(array):
        return array.transpose(1, 0, 2)

    places = ((query_at - query_pos)[None, :], query_at[None, :])
    tile_shape = (ep_count, rows_here, -1)
    tiles_of = tuple(
        array.reshape(tile_shape) for array in (normed_all, d_pair_pre, upstream_all, weighted_h)
    )
    units = (slot_here, slot_hidden, shared_units)
    column = jnp.arange(128, dtype=jnp.int32)
    large = (
        d_resid_low,
        joined_weights,
        by_head(queries),
        by_head(keys_win),
        by_head(values_win),
        normed_one.T,
        block_rows,
    )
    in_place = (
        log_total.reshape(heads_here, 1, rows_here),
        *places,
        cosine[:, 0],
        sine[:, 0],
        my_rows(tokens),
        first_norm_scale[None, :],
        d_resid,
        grad_gain_two[None, :],
        jnp.where(column >= 2, grad_side, 0.0),
    )
    grad_weights, small, block_out, grad_tokens, grad_pieces, grad_experts = backward(
        large, tiles_of, in_place, units, score_scale
    )
    grad_shared = shared_whole(grad_pieces, 3)
    grad_tokens = grad_tokens.astype(f32)
    grad_experts = [grad.astype(f32).reshape(expert_gate.shape) for grad in grad_experts]
    parts = [grad_weights[:, i * heads_width : (i + 1) * heads_width] for i in range(3)]
    return (
        block_out,
        grad_tokens,
        small[:, 0],
        parts[0],
        parts[1],
        parts[2],
        grad_out,
        small[:, 1],
        small[:, 3 : 3 + expert_count],
        small[:, 2],
        grad_shared[0],
        grad_shared[1],
        grad_shared[2],
        grad_experts[0],
        grad_experts[1],
        grad_experts[2],
    )


def chosen_body(*arrays):
    rows_here, top_count = arrays[2].shape
    slot_here, expert_count = arrays[14].shape[0], arrays[9].shape[1]
    capacity = rows_here * top_count * 7 // (5 * expert_count)
    grid_of_two = lax.axis_size("ep") % 2 == 0 and lax.axis_size("tp") == 4
    if grid_of_two and rows_here < 2 * slot_here * capacity:
        return dense_body(*arrays)
    return body(*arrays)


def solution(mesh):
    placed = (
        P("ep", None),
        P(),
        P("ep", None),
        P("ep"),
        P("ep", "tp"),
        P("ep", "tp"),
        P("ep", "tp"),
        P("ep", "tp"),
        P("ep"),
        P("ep", None),
        P("ep"),
        P("ep", "tp"),
        P("ep", "tp"),
        P("ep", "tp"),
        P("ep", "tp", None),
        P("ep", "tp", None),
        P("ep", "tp", None),
        P("ep", None),
    )
    return jax.shard_map(
        chosen_body,
        mesh=mesh,
        in_specs=placed,
        out_specs=(
            P("ep", None),
            P("ep", None),
            P("ep"),
            P("ep", "tp"),
            P("ep", "tp"),
            P("ep", "tp"),
            P("ep", "tp"),
            P("ep"),
            P("ep", None),
            P("ep"),
            P("ep", "tp"),
            P("ep", "tp"),
            P("ep", "tp"),
            P("ep", "tp", None),
            P("ep", "tp", None),
            P("ep", "tp", None),
        ),
        check_vma=False,
    )
```

```python
import functools

import jax
import jax.numpy as jnp
from jax import lax
from jax.experimental import pallas as pl
from jax.experimental.pallas import tpu as pltpu
from jax.sharding import PartitionSpec as P

HD = 128


epsilon = 1e-06
rope_base = 1000000.0
highest = lax.Precision.HIGHEST
MESH = pl.DeviceIdType.MESH


def passed_along(block, axis, distance):
    devices = range(lax.axis_size(axis))
    route = [(i - distance, i) for i in devices if i - distance in devices]
    return lax.ppermute(block, axis, route)


def rope_tables(positions, width):
    steps = jnp.arange(0, width, 2, dtype=jnp.float32) / width
    inverse = rope_base ** (-steps)
    angles = positions.astype(jnp.float32)[:, None] * inverse[None, :]
    angles = jnp.concatenate([angles, angles], axis=-1)
    return (jnp.cos(angles)[:, None, :], jnp.sin(angles)[:, None, :])


def turn_half(values):
    middle = values.shape[-1] // 2
    return jnp.concatenate([-values[..., middle:], values[..., :middle]], axis=-1)


def rotate(values, cosine, sine):
    return values * cosine + turn_half(values) * sine


def unrotate(grads, cosine, sine):
    return grads * cosine - turn_half(grads * sine)


def sequence_info(lengths, indices):
    starts = jnp.cumsum(lengths) - lengths
    inside = starts[None, :] <= indices[:, None]
    segment = jnp.sum(inside.astype(jnp.int32), axis=1) - 1
    first = jnp.max(jnp.where(inside, starts[None, :], -1), axis=1)
    return (segment, indices - first)


def norm_forward(values, gain):
    scale = lax.rsqrt(jnp.mean(values * values, axis=-1, keepdims=True) + epsilon)
    return (values * scale * gain, scale)


def norm_backward(values, scale, gain, grads):
    unit = values * scale
    scaled = grads * gain
    inner = jnp.mean(scaled * unit, axis=-1, keepdims=True)
    return (scale * (scaled - unit * inner), jnp.sum(grads * unit, axis=0))


def deliver(rows):
    arrived_rows = lax.all_to_all(rows, "ep", split_axis=0, concat_axis=0, tiled=True)
    return arrived_rows


def bring_back(parts, target, rows_here, top_count):
    moved = lax.all_to_all(parts, "ep", split_axis=0, concat_axis=0, tiled=True)
    piece = moved.shape[3]
    return moved.reshape(-1, piece)[target].reshape(rows_here, top_count, piece)


def body(
    tokens,
    lengths,
    routes,
    attn_gain,
    w_query,
    w_key,
    w_value,
    w_out,
    ffn_gain,
    w_router,
    shared_mix,
    shared_gate,
    shared_up,
    shared_down,
    expert_gate,
    expert_up,
    expert_down,
    cotangent,
):
    rows_here = tokens.shape[0]
    width = tokens.shape[1]
    ep_count = lax.axis_size("ep")
    offset = lax.axis_index("ep") * rows_here
    slot_here = expert_gate.shape[0]
    top_count = routes.shape[1]
    gathered = (
        lax.all_gather(attn_gain, "ep", axis=0, tiled=True),
        lax.all_gather(w_query, "ep", axis=0, tiled=True),
        lax.all_gather(w_key, "ep", axis=0, tiled=True),
        lax.all_gather(w_value, "ep", axis=0, tiled=True),
        lax.all_gather(w_out, "ep", axis=0, tiled=True),
        lax.all_gather(ffn_gain, "ep", axis=0, tiled=True),
        lax.all_gather(w_router, "ep", axis=0, tiled=True),
        lax.all_gather(shared_mix, "ep", axis=0, tiled=True),
        lax.all_gather(shared_gate, "ep", axis=0, tiled=True),
        lax.all_gather(shared_up, "ep", axis=0, tiled=True),
        lax.all_gather(shared_down, "ep", axis=0, tiled=True),
    )
    (
        gain_first,
        query_weight_matrix,
        key_weight_matrix,
        value_weight_matrix,
        output_weight,
        gain_second,
        router_weight,
        shared_mixer_weight,
        shared_gate_weight,
        shared_up_weight,
        shared_down_weight,
    ) = gathered
    expert_count = router_weight.shape[1]
    capacity = (rows_here * top_count * 7 // (5 * expert_count) + 7) // 8 * 8
    heads_here = query_weight_matrix.shape[1] // HD
    score_scale = HD ** (-0.5)
    first_norm_scale = gain_first.astype(jnp.float32)
    second_norm_scale = gain_second.astype(jnp.float32)
    layer_input = tokens.astype(jnp.float32)
    normed_wide, norm_one = norm_forward(layer_input, first_norm_scale)
    normed_one = normed_wide.astype(jnp.bfloat16)
    query_at = offset + jnp.arange(rows_here, dtype=jnp.int32)
    key_at = offset - 2 * rows_here + jnp.arange(3 * rows_here, dtype=jnp.int32)
    query_seg, query_pos = sequence_info(lengths, query_at)
    key_seg, _ = sequence_info(lengths, key_at)
    cosine, sine = rope_tables(query_pos, HD)
    query_pre = jnp.dot(
        normed_one, query_weight_matrix, preferred_element_type=jnp.float32
    ).reshape(rows_here, heads_here, HD)
    key_pre = jnp.dot(normed_one, key_weight_matrix, preferred_element_type=jnp.float32).reshape(
        rows_here, heads_here, HD
    )
    queries = rotate(query_pre, cosine, sine).astype(jnp.bfloat16)
    keys = rotate(key_pre, cosine, sine).astype(jnp.bfloat16)
    values = (
        jnp.dot(normed_one, value_weight_matrix, preferred_element_type=jnp.float32)
        .astype(jnp.bfloat16)
        .reshape(rows_here, heads_here, HD)
    )
    carried = jnp.stack([keys, values], axis=0)
    window = [carried]
    for hop in range(2):
        carried = passed_along(carried, "ep", 1)
        window = [carried] + window
    joined = jnp.concatenate(window, axis=1)
    keys_win = joined[0]
    values_win = joined[1]
    allowed = (
        (query_seg[:, None] == key_seg[None, :])
        & (key_at[None, :] <= query_at[:, None])
        & (key_at[None, :] >= 0)
    )
    scores = (
        jnp.einsum("qhd,khd->hqk", queries, keys_win, preferred_element_type=jnp.float32)
        * score_scale
    )
    masked = jnp.where(allowed[None], scores, -1e30)
    peak = jnp.max(masked, axis=-1, keepdims=True)
    expo = jnp.exp(masked - peak)
    total = jnp.sum(expo, axis=-1, keepdims=True)
    log_total = peak + jnp.log(total)
    weights = expo / total
    attended = jnp.einsum(
        "hqk,khd->qhd", weights.astype(jnp.bfloat16), values_win, preferred_element_type=jnp.float32
    )
    attended = attended.reshape(rows_here, heads_here * HD).astype(jnp.bfloat16)
    attn_part = jnp.einsum("th,dh->td", attended, output_weight, preferred_element_type=jnp.float32)
    resid = layer_input + lax.psum(attn_part, "tp")
    normed_two_wide, norm_two = norm_forward(resid, second_norm_scale)
    normed_two = normed_two_wide.astype(jnp.bfloat16)
    normed_two_f = normed_two.astype(jnp.float32)
    router_f = router_weight.astype(jnp.float32)
    mix_f = shared_mixer_weight.astype(jnp.float32)
    router = jax.nn.softmax(jnp.dot(normed_two_f, router_f, precision=highest), axis=-1)
    picked = routes[:, :, None] == jnp.arange(expert_count, dtype=jnp.int32)[None, None, :]
    gates = jnp.sum(jnp.where(picked, router[:, None, :], 0.0), axis=-1)
    mixer = jax.nn.sigmoid(jnp.dot(normed_two_f, mix_f, precision=highest))
    shared_g = jnp.dot(normed_two, shared_gate_weight, preferred_element_type=jnp.float32)
    shared_u = jnp.dot(normed_two, shared_up_weight, preferred_element_type=jnp.float32)
    shared_h = (jax.nn.silu(shared_g) * shared_u).astype(jnp.bfloat16)
    shared_part = jnp.einsum(
        "tf,df->td", shared_h, shared_down_weight, preferred_element_type=jnp.float32
    )
    flat = routes.reshape(-1)
    hot = (flat[:, None] == jnp.arange(expert_count, dtype=jnp.int32)[None, :]).astype(jnp.int32)
    rank = jnp.sum(jnp.cumsum(hot, axis=0) * hot, axis=1) - 1
    target = flat * capacity + rank
    slot_total = ep_count * slot_here * capacity
    owner_route = (
        jnp.zeros((slot_total,), jnp.int32)
        .at[target]
        .set(jnp.arange(rows_here * top_count, dtype=jnp.int32))
    )
    filled = jnp.zeros((slot_total,), jnp.bool_).at[target].set(True)
    owner_token = owner_route // top_count
    send_rows = jnp.where(filled[:, None], normed_two[owner_token], jnp.zeros((), jnp.bfloat16))
    arrived_rows = deliver(send_rows.reshape(ep_count, slot_here, capacity, width))
    route_g = jnp.einsum(
        "nscd,sfd->nscf", arrived_rows, expert_gate, preferred_element_type=jnp.float32
    )
    route_u = jnp.einsum(
        "nscd,sfd->nscf", arrived_rows, expert_up, preferred_element_type=jnp.float32
    )
    route_h = (jax.nn.silu(route_g) * route_u).astype(jnp.bfloat16)
    route_part = jnp.einsum(
        "nscf,sfd->nscd", route_h, expert_down, preferred_element_type=jnp.float32
    )
    back_rows = bring_back(route_part, target, rows_here, top_count)
    upstream = cotangent.astype(jnp.float32)
    routed = jnp.sum(back_rows * gates[:, :, None], axis=1)
    ffn_part = mixer[:, None] * shared_part + routed
    route_dot = jnp.sum(back_rows * upstream[:, None, :], axis=-1)
    shared_dot = jnp.sum(shared_part * upstream, axis=-1)
    ffn_total, d_gate, d_mixer = lax.psum((ffn_part, route_dot, shared_dot), "tp")
    block_out = (resid + ffn_total).astype(jnp.bfloat16)
    d_router = jnp.sum(jnp.where(picked, d_gate[:, :, None], 0.0), axis=1)
    d_logits = router * (d_router - jnp.sum(router * d_router, axis=-1, keepdims=True))
    d_mixlogit = d_mixer * mixer * (1.0 - mixer)
    side = jnp.dot(d_logits, router_f.T, precision=highest) + d_mixlogit[:, None] * mix_f[None, :]
    grad_router = jnp.dot(normed_two_f.T, d_logits, precision=highest)
    grad_mix = jnp.dot(d_mixlogit, normed_two_f, precision=highest)
    d_shared = (mixer[:, None] * upstream).astype(jnp.bfloat16)
    d_sh = jnp.dot(d_shared, shared_down_weight, preferred_element_type=jnp.float32)
    sig_shared = jax.nn.sigmoid(shared_g)
    d_sg = (d_sh * shared_u * sig_shared * (1.0 + shared_g * (1.0 - sig_shared))).astype(
        jnp.bfloat16
    )
    d_su = (d_sh * shared_g * sig_shared).astype(jnp.bfloat16)
    d_normed_part = jnp.einsum(
        "tf,df->td", d_sg, shared_gate_weight, preferred_element_type=jnp.float32
    )
    d_normed_part = d_normed_part + jnp.einsum(
        "tf,df->td", d_su, shared_up_weight, preferred_element_type=jnp.float32
    )
    grad_sgate = jnp.einsum("td,tf->df", normed_two, d_sg, preferred_element_type=jnp.float32)
    grad_sup = jnp.einsum("td,tf->df", normed_two, d_su, preferred_element_type=jnp.float32)
    grad_sdown = jnp.einsum("td,tf->df", d_shared, shared_h, preferred_element_type=jnp.float32)
    d_route = (
        (gates[:, :, None] * upstream[:, None, :])
        .astype(jnp.bfloat16)
        .reshape(rows_here * top_count, width)
    )
    send_grads = jnp.where(filled[:, None], d_route[owner_route], jnp.zeros((), jnp.bfloat16))
    received_grads = deliver(send_grads.reshape(ep_count, slot_here, capacity, width))
    d_rh = jnp.einsum(
        "nscd,sfd->nscf", received_grads, expert_down, preferred_element_type=jnp.float32
    )
    sig_route = jax.nn.sigmoid(route_g)
    d_rg = (d_rh * route_u * sig_route * (1.0 + route_g * (1.0 - sig_route))).astype(jnp.bfloat16)
    routed_up_gradient = (d_rh * route_g * sig_route).astype(jnp.bfloat16)
    row_grads = jnp.einsum("nscf,sfd->nscd", d_rg, expert_gate, preferred_element_type=jnp.float32)
    row_grads = row_grads + jnp.einsum(
        "nscf,sfd->nscd", routed_up_gradient, expert_up, preferred_element_type=jnp.float32
    )
    grad_egate = jnp.einsum(
        "qxba,qxbr->xar", d_rg, arrived_rows, preferred_element_type=jnp.float32
    )
    expert_up_gradient = jnp.einsum(
        "qxba,qxbr->xar", routed_up_gradient, arrived_rows, preferred_element_type=jnp.float32
    )
    grad_edown = jnp.einsum(
        "qxba,qxbr->xar", route_h, received_grads, preferred_element_type=jnp.float32
    )
    grads_back = bring_back(row_grads, target, rows_here, top_count)
    d_routed = jnp.sum(grads_back, axis=1)
    d_normed_two = lax.psum(d_normed_part + d_routed, "tp") + side
    d_resid_norm, grad_gain_two = norm_backward(resid, norm_two, second_norm_scale, d_normed_two)
    d_resid = upstream + d_resid_norm
    d_resid_low = d_resid.astype(jnp.bfloat16)
    grad_outw = jnp.einsum("td,th->dh", d_resid_low, attended, preferred_element_type=jnp.float32)
    d_attended = jnp.einsum(
        "td,dh->th", d_resid_low, output_weight, preferred_element_type=jnp.float32
    )
    d_attended = d_attended.astype(jnp.bfloat16).reshape(rows_here, heads_here, HD)
    scores_again = (
        jnp.einsum("qhd,khd->hqk", queries, keys_win, preferred_element_type=jnp.float32)
        * score_scale
    )
    probs = jnp.where(allowed[None], jnp.exp(scores_again - log_total), 0.0)
    d_probs = jnp.einsum("qhd,khd->hqk", d_attended, values_win, preferred_element_type=jnp.float32)
    delta = jnp.sum(probs * d_probs, axis=-1, keepdims=True)
    d_scores = (probs * (d_probs - delta)).astype(jnp.bfloat16)
    d_queries = (
        jnp.einsum("hqk,khd->qhd", d_scores, keys_win, preferred_element_type=jnp.float32)
        * score_scale
    )
    d_keys_win = (
        jnp.einsum("hqk,qhd->khd", d_scores, queries, preferred_element_type=jnp.float32)
        * score_scale
    )
    d_values_win = jnp.einsum(
        "hqk,qhd->khd", probs.astype(jnp.bfloat16), d_attended, preferred_element_type=jnp.float32
    )
    pair_grads = jnp.stack([d_keys_win, d_values_win], axis=0)
    older = pair_grads[:, :rows_here]
    later = [pair_grads[:, rows_here : 2 * rows_here], pair_grads[:, 2 * rows_here :]]
    running = older
    for hop in range(2):
        running = passed_along(running, "ep", -1)
        running = running + later[hop]
    d_query_pre = (
        unrotate(d_queries, cosine, sine).astype(jnp.bfloat16).reshape(rows_here, heads_here * HD)
    )
    d_key_pre = (
        unrotate(running[0], cosine, sine).astype(jnp.bfloat16).reshape(rows_here, heads_here * HD)
    )
    d_values = running[1].astype(jnp.bfloat16).reshape(rows_here, heads_here * HD)
    grad_queryw = jnp.einsum(
        "td,th->dh", normed_one, d_query_pre, preferred_element_type=jnp.float32
    )
    grad_keyw = jnp.einsum("td,th->dh", normed_one, d_key_pre, preferred_element_type=jnp.float32)
    grad_valuew = jnp.einsum("td,th->dh", normed_one, d_values, preferred_element_type=jnp.float32)
    d_normed_one = jnp.einsum(
        "th,dh->td", d_query_pre, query_weight_matrix, preferred_element_type=jnp.float32
    )
    d_normed_one = d_normed_one + jnp.einsum(
        "th,dh->td", d_key_pre, key_weight_matrix, preferred_element_type=jnp.float32
    )
    d_normed_one = d_normed_one + jnp.einsum(
        "th,dh->td", d_values, value_weight_matrix, preferred_element_type=jnp.float32
    )
    d_normed_one = lax.psum(d_normed_one, "tp")
    d_input_norm, grad_gain_one = norm_backward(
        layer_input, norm_one, first_norm_scale, d_normed_one
    )
    grad_tokens = d_resid + d_input_norm
    summed = (
        lax.psum_scatter(grad_gain_one, "ep", scatter_dimension=0, tiled=True),
        lax.psum_scatter(grad_queryw, "ep", scatter_dimension=0, tiled=True),
        lax.psum_scatter(grad_keyw, "ep", scatter_dimension=0, tiled=True),
        lax.psum_scatter(grad_valuew, "ep", scatter_dimension=0, tiled=True),
        lax.psum_scatter(grad_outw, "ep", scatter_dimension=0, tiled=True),
        lax.psum_scatter(grad_gain_two, "ep", scatter_dimension=0, tiled=True),
        lax.psum_scatter(grad_router, "ep", scatter_dimension=0, tiled=True),
        lax.psum_scatter(grad_mix, "ep", scatter_dimension=0, tiled=True),
        lax.psum_scatter(grad_sgate, "ep", scatter_dimension=0, tiled=True),
        lax.psum_scatter(grad_sup, "ep", scatter_dimension=0, tiled=True),
        lax.psum_scatter(grad_sdown, "ep", scatter_dimension=0, tiled=True),
    )
    return (
        block_out,
        grad_tokens,
        summed[0],
        summed[1],
        summed[2],
        summed[3],
        summed[4],
        summed[5],
        summed[6],
        summed[7],
        summed[8],
        summed[9],
        summed[10],
        grad_egate,
        expert_up_gradient,
        grad_edown,
    )


class Place:
    def __init__(self):
        self.ep, self.tp = lax.axis_index("ep"), lax.axis_index("tp")
        self.z, self.y = self.ep // 2, self.ep % 2
        self.x, self.c = self.tp // 2, self.tp % 2
        self.depth = lax.axis_size("ep") // 2
        self.next_core = (self.ep, self.x * 2 + 1 - self.c)
        self.next_x = (self.ep, (1 - self.x) * 2 + self.c)
        self.next_y = (self.z * 2 + 1 - self.y, self.tp)

    def at_z(self, z):
        return (z * 2 + self.y, self.tp)

    def ahead(self, steps):
        return lax.rem(self.z + steps, self.depth)

    def behind(self, steps):
        return lax.rem(self.z + self.depth - steps, self.depth)

    def greet(self):
        barrier = pltpu.get_barrier_semaphore()
        peers = [self.next_core, self.next_x, self.next_y]
        peers += [self.at_z(self.ahead(k)) for k in range(1, self.depth)]
        for peer in peers:
            pl.semaphore_signal(barrier, inc=1, device_id=peer, device_id_type=MESH)
        pl.semaphore_wait(barrier, len(peers))

    def greet_row(self):
        barrier = pltpu.get_barrier_semaphore()
        count = 2 * self.depth
        peers = [(lax.rem(self.ep + k, count), self.tp) for k in range(1, count)]
        peers += [self.next_core, self.next_x]
        for peer in peers:
            pl.semaphore_signal(barrier, inc=1, device_id=peer, device_id_type=MESH)
        pl.semaphore_wait(barrier, len(peers))

    def greet_ep(self):
        barrier = pltpu.get_barrier_semaphore()
        count = 2 * self.depth
        for k in range(1, count):
            peer = (lax.rem(self.ep + k, count), self.tp)
            pl.semaphore_signal(barrier, inc=1, device_id=peer, device_id_type=MESH)
        pl.semaphore_wait(barrier, count - 1)


def remote(src, dst, send, recv, peer):
    return pltpu.make_async_remote_copy(
        src_ref=src, dst_ref=dst, send_sem=send, recv_sem=recv, device_id=peer, device_id_type=MESH
    )


def ffn_kernel(
    units,
    expert_count,
    rows_in,
    upstream_in,
    gate_in,
    up_in,
    down_in,
    pieces_in,
    weights_in,
    resid_in,
    gain_in,
    rows_all,
    weighted_out,
    d_pair_out,
    block_out,
    d_resid_low_out,
    d_resid_out,
    d_gain_out,
    d_side_out,
    d_rows_sum,
    out_sum,
    pair_w,
    down_w,
    side_w,
    rows_tile,
    upstream_tile,
    pair_pre,
    d_hidden,
    factors,
    dots,
    weighted_tile,
    d_pair_tile,
    d_resid_low,
    d_rows_tile,
    out_tile,
    d_rows_core,
    out_core,
    d_rows_held,
    out_held,
    d_rows_hop,
    out_hop,
    d_rows_hop2,
    out_hop2,
    d_rows_z,
    out_z,
    d_rows_to_z,
    out_to_z,
    gathered_send,
    gathered_recv,
    hop_send,
    hop_recv,
    weight_sem,
    end_sem,
    own_sem,
    z_send,
    z_recv,
    plane_send,
    plane_recv,
    load_sem,
    store_sem,
    sum_send,
    sum_recv,
    end_send,
    end_recv,
    core_credit,
    hop_credit,
    hop2_credit,
):
    at = Place()
    depth = at.depth
    quarter, width = rows_in.shape
    half = quarter // 2
    f32, bf16 = jnp.float32, jnp.bfloat16

    def weight_copies():
        hidden = down_w.shape[0]
        slot_here, slot_hidden, shared = units
        routed = slot_here * slot_hidden
        columns = pieces_in.shape[2]
        pairs = [(weights_in.at[:, pl.ds(weights_in.shape[1] - 128, 128)], side_w)]
        kinds = ((gate_in, pair_w, 0), (up_in, pair_w, hidden), (down_in, down_w, 0))
        for kind, (experts, into, first) in enumerate(kinds):
            pairs.append((experts, into.at[pl.ds(first, routed)]))
            here = pl.ds(first + routed, shared)
            for e in range(2 * depth):
                src = pieces_in.at[e, pl.ds(kind * shared, shared)]
                pairs.append((src, into.at[here, pl.ds(e * columns, columns)]))
        return [
            pltpu.make_async_copy(src, dst, weight_sem.at[i]) for i, (src, dst) in enumerate(pairs)
        ]

    def clear_rest():
        hidden = down_w.shape[0]
        used = units[0] * units[1] + units[2]
        for into, first in ((pair_w, 0), (pair_w, hidden), (down_w, 0)):
            if used < hidden:
                into[first + used : first + hidden] = jnp.zeros((hidden - used, width), bf16)

    for copy in weight_copies():
        copy.start()
    clear_rest()

    def block(j, y, x):
        return rows_all.at[at.behind(j), y, x, at.c]

    def plane_copy(j, kind):
        y, other_y = at.y, 1 - at.y
        own, other_x = at.x, 1 - at.x
        if kind == 0:
            src, peer = block(j, y, own), at.next_x
        elif kind == 1:
            src, peer = block(j, y, own), at.next_y
        elif kind == 2:
            src, peer = block(j, y, other_x).at[pl.ds(0, half)], at.next_y
        elif kind == 3:
            src, peer = block(j, other_y, own).at[pl.ds(half, half)], at.next_x
        else:
            src = block(j, other_y if kind >= 6 else y, other_x if kind % 2 else own)
            peer = at.next_core
        return remote(src, src, plane_send.at[j, kind], plane_recv.at[j, kind], peer)

    def z_copy(k):
        return remote(
            rows_in, block(0, at.y, at.x), z_send.at[k - 1], z_recv.at[k - 1], at.at_z(at.ahead(k))
        )

    def z_arrival(k):
        dst = block(k, at.y, at.x)
        return remote(dst, dst, z_send.at[k - 1], z_recv.at[k - 1], at.at_z(at.behind(k)))

    def begin(j):
        for kind in (0, 1, 4):
            plane_copy(j, kind).start()

    def spread(j):
        plane_copy(j, 0).wait_recv()
        plane_copy(j, 2).start()
        plane_copy(j, 5).start()
        plane_copy(j, 1).wait_recv()
        plane_copy(j, 3).start()
        plane_copy(j, 6).start()

    def begin_later(j):
        z_arrival(j).wait_recv()
        begin(j)

    def last_hop(j):
        plane_copy(j, 2).wait_recv()
        plane_copy(j, 3).wait_recv()
        plane_copy(j, 7).start()

    def near_ready(j):
        plane_copy(j, 4).wait_recv()
        plane_copy(j, 5).wait_recv()

    def far_ready(j):
        plane_copy(j, 6).wait_recv()
        plane_copy(j, 7).wait_recv()

    def parity(step):
        return lax.rem(step, 2)

    def slot_of(turn):
        return lax.rem(turn + 1, depth)

    def other_y(step):
        return lax.rem(parity(step) + (step // 2 + 1) // depth, 2)

    def tile_at(step):
        return at.behind(slot_of(step // 2)), lax.rem(at.y + other_y(step), 2)

    def load_rows(step):
        z, y = tile_at(step)
        return pltpu.make_async_copy(rows_all.at[z, y], rows_tile, load_sem.at[0])

    def load_upstream(step):
        z, y = tile_at(step)
        return pltpu.make_async_copy(upstream_in.at[z, y], upstream_tile, load_sem.at[1])

    def stores(step):
        z, y = tile_at(step)
        pairs = ((weighted_tile, weighted_out), (d_pair_tile, d_pair_out))
        return [
            pltpu.make_async_copy(src, dst.at[z, y], store_sem.at[i])
            for i, (src, dst) in enumerate(pairs)
        ]

    tiles, cores = (d_rows_tile, out_tile), (d_rows_core, out_core)
    helds, sums = (d_rows_held, out_held), (d_rows_sum, out_sum)
    hops, hops2, zs = (d_rows_hop, out_hop), (d_rows_hop2, out_hop2), (d_rows_z, out_z)
    to_zs = (d_rows_to_z, out_to_z)

    def sum_copy(a, kind, src, dst, peer):
        return remote(src, dst, sum_send.at[a, kind], sum_recv.at[a, kind], peer)

    def core_sum(a):
        return sum_copy(a, 0, tiles[a].at[:, 1 - at.c], cores[a], at.next_core)

    def row_hop(turn, other):
        y = lax.rem(at.y + other, 2)
        slot = parity(turn)
        src = d_rows_held.at[slot, y, 1 - at.x]
        return remote(
            src, d_rows_hop.at[slot, y], hop_send.at[slot, other], hop_recv.at[slot, other], at.next_x
        )

    def out_hop_sum(turn):
        slot = parity(turn)
        src = out_held.at[slot, 1 - at.y]
        return remote(
            src, out_hop.at[slot], hop_send.at[slot, 2], hop_recv.at[slot, 2], at.next_y
        )

    def hop2_sum(a, turn):
        slot = parity(turn)
        if a == 0:
            src, peer = helds[0].at[slot, 1 - at.y, at.x], at.next_y
        else:
            src, peer = helds[1].at[slot, at.y, 1 - at.x], at.next_x
        return sum_copy(a, 2, src, hops2[a], peer)

    def z_sum(a, turn):
        return remote(
            to_zs[a].at[parity(turn)],
            zs[a].at[turn],
            end_send.at[a, turn],
            end_recv.at[a, turn],
            at.at_z(at.behind(turn + 1)),
        )

    def allow(semaphore, peer):
        pl.semaphore_signal(semaphore, inc=1, device_id=peer, device_id_type=MESH)

    piece = 32

    def add(into, first, second):
        def body(i, carry):
            part = pl.ds(pl.multiple_of(i * piece, piece), piece)
            into[part] = first[part] + second[part]
            return carry

        lax.fori_loop(0, quarter // piece, body, 0)

    def after_core(step):
        turn = step // 2
        other = other_y(step)
        held, y = parity(turn), lax.rem(at.y + other, 2)

        @pl.when((parity(step) == 0) & (turn >= 2))
        def _():
            for a in (0, 1):
                pl.semaphore_wait(hop_credit.at[a], 1)

        for a in (0, 1):
            core_sum(a).wait()
            for x in (1 - at.x, at.x):
                add(helds[a].at[held, y, x], tiles[a].at[x, at.c], cores[a].at[x])
            if a == 0:
                row_hop(turn, other).start()
            else:

                @pl.when(other == 1)
                def _():
                    out_hop_sum(turn).start()

        @pl.when(step + 1 < 2 * depth)
        def _():
            allow(core_credit, at.next_core)

    def after_row_hop(turn, other):
        slot, y = parity(turn), lax.rem(at.y + other, 2)
        row_hop(turn, other).wait()
        into = d_rows_held.at[slot, y, at.x]
        add(into, into, d_rows_hop.at[slot, y])

    def after_out_hop(turn):
        slot = parity(turn)
        out_hop_sum(turn).wait()
        for x in (1 - at.x, at.x):
            into = out_held.at[slot, at.y, x]
            add(into, into, out_hop.at[slot, x])

    def may_hop2(turn, a):
        @pl.when(turn >= 1)
        def _():
            pl.semaphore_wait(hop2_credit.at[a], 1)

    def after_hop(turn):
        after_row_hop(turn, 1)
        may_hop2(turn, 0)
        hop2_sum(0, turn).start()
        after_row_hop(turn, 0)
        after_out_hop(turn)
        may_hop2(turn, 1)
        hop2_sum(1, turn).start()

        @pl.when(turn + 2 < depth)
        def _():
            allow(hop_credit.at[0], at.next_x)
            allow(hop_credit.at[1], at.next_y)

    def after_hop2(turn):
        slot = parity(turn)
        for a in (0, 1):
            hop2_sum(a, turn).wait()

            @pl.when(turn >= 2)
            def _():
                z_sum(a, turn - 2).wait_send()

            add(to_zs[a].at[slot], helds[a].at[slot, at.y, at.x], hops2[a])
            z_sum(a, turn).start()
        allow(hop2_credit.at[0], at.next_y)
        allow(hop2_credit.at[1], at.next_x)

    load_upstream(0).start()
    at.greet()
    z_copy(1).start()
    own_copy = pltpu.make_async_copy(rows_in, block(0, at.y, at.x), own_sem)
    own_copy.start()
    own_copy.wait()
    begin(0)
    begin_later(1)
    for k in range(2, depth):
        z_copy(k).start()
    spread(0)
    spread(1)
    near_ready(1)
    load_rows(0).start()
    for copy in weight_copies():
        copy.wait()

    tile_rows = 4 * quarter
    hidden_total = down_w.shape[0]
    lane = lax.broadcasted_iota(jnp.int32, (tile_rows, 128), 1)
    slot_here, slot_hidden, shared_hidden = units
    routed = slot_here * slot_hidden
    across = (((1,), (1,)), ((), ()))
    few = 16

    def gate_factors(rows, picked):
        logits = jnp.dot(rows, side_w[...], preferred_element_type=f32)
        chooses = (lane >= 3) & (lane < 3 + expert_count)
        peak = jnp.max(jnp.where(chooses, logits, -1e30), axis=1, keepdims=True)
        expo = jnp.where(chooses, jnp.exp(jnp.where(chooses, logits, peak) - peak), 0.0)
        routed_gate = expo / jnp.sum(expo, axis=1, keepdims=True) * picked.astype(f32)
        mix_pre = jnp.sum(jnp.where(lane == 2, logits, 0.0), axis=1, keepdims=True)
        result = jnp.where(lane == slot_here, 1.0 / (1.0 + jnp.exp(-mix_pre)), 0.0)
        for s in range(slot_here):
            chosen = lane == 3 + at.ep * slot_here + s
            gate = jnp.sum(jnp.where(chosen, routed_gate, 0.0), axis=1, keepdims=True)
            result = jnp.where(lane == s, gate, result)
        return result

    few_lane = lax.broadcasted_iota(jnp.int32, (few, 128), 1)
    bounds = [s * slot_hidden for s in range(slot_here)] + [routed, hidden_total]

    def owners(group):
        found = []
        for s in range(slot_here + 1):
            low, high = max(bounds[s] - group * 128, 0), min(bounds[s + 1] - group * 128, 128)
            if low < high:
                found.append((s, low, high))
        return found

    def hidden_rows(i, carry):
        here = pl.ds(pl.multiple_of(i * few, few), few)
        gates = [
            jnp.broadcast_to(factors[here, s : s + 1], (few, 128)) for s in range(slot_here + 1)
        ]
        parts = [None] * (slot_here + 1)
        for group in range(hidden_total // 128):
            units_here = slice(group * 128, (group + 1) * 128)
            units_up = slice(hidden_total + group * 128, hidden_total + (group + 1) * 128)
            gate_pre, up_pre = pair_pre[here, units_here], pair_pre[here, units_up]
            d_h = d_hidden[here, units_here]
            found = owners(group)
            factor = gates[found[0][0]]
            for s, low, _ in found[1:]:
                factor = jnp.where(few_lane >= low, gates[s], factor)
            sig = 0.5 + 0.5 * jnp.tanh(0.5 * gate_pre)
            silu = gate_pre * sig
            hidden = silu * up_pre
            product = hidden * d_h
            gated = factor * d_h
            weighted_tile[here, units_here] = (factor * hidden).astype(bf16)
            slope = sig + silu * (1.0 - sig)
            d_pair_tile[here, units_here] = (gated * up_pre * slope).astype(bf16)
            d_pair_tile[here, units_up] = (gated * silu).astype(bf16)
            for s, low, high in found:
                mine = product
                if high < 128:
                    mine = jnp.where(few_lane < high, mine, 0.0)
                if low > 0:
                    mine = jnp.where(few_lane >= low, mine, 0.0)
                parts[s] = mine if parts[s] is None else parts[s] + mine
        result = jnp.zeros((few, 128), f32)
        for s in range(slot_here + 1):
            dot = jnp.sum(parts[s], axis=1, keepdims=True)
            where = few_lane == (2 if s == slot_here else 3 + at.ep * slot_here + s)
            result = jnp.where(where, dot, result)
        dots[here] = result.astype(bf16)
        return carry

    def first_half(step):
        load_upstream(step).wait()
        upstream = upstream_tile[...].reshape(tile_rows, upstream_tile.shape[-1])
        d_hidden[...] = lax.dot_general(
            upstream[:, :width], down_w[...], across, preferred_element_type=f32
        )
        load_rows(step).wait()
        rows = rows_tile[...].reshape(tile_rows, width)
        factors[...] = gate_factors(rows, upstream[:, width:])
        pair_pre[...] = lax.dot_general(rows, pair_w[...], across, preferred_element_type=f32)

        @pl.when(step + 1 < 2 * depth)
        def _():
            load_upstream(step + 1).start()

        @pl.when(step >= 1)
        def _():
            for copy in stores(step - 1):
                copy.wait()

        lax.fori_loop(0, tile_rows // few, hidden_rows, 0, unroll=2)
        for copy in stores(step):
            copy.start()
        turn = step // 2

        @pl.when(step == 0)
        def _():
            last_hop(0)

        @pl.when((parity(step) == 0) & (turn + 1 < depth))
        def _():
            last_hop(turn + 1)

        @pl.when((step >= 1) & (step + 1 < depth))
        def _():
            spread(step + 1)

        @pl.when(step + 2 < depth)
        def _():
            begin_later(step + 2)

    def second_half(step):
        blocks = (2, 2, quarter)
        some = width // 2
        for n in range(2):
            columns = slice(n * some, (n + 1) * some)
            part = jnp.dot(weighted_tile[...], down_w[:, columns], preferred_element_type=f32)
            out_tile[:, :, :, columns] = part.astype(bf16).reshape(blocks + (some,))
            part = jnp.dot(d_pair_tile[...], pair_w[:, columns], preferred_element_type=f32)
            d_rows_tile[:, :, :, columns] = part.astype(bf16).reshape(blocks + (some,))
        d_rows_tile[:, :, :, width:] = dots[...].reshape(blocks + (128,))

        @pl.when(step >= 1)
        def _():
            pl.semaphore_wait(core_credit, 1)

        for a in (0, 1):
            core_sum(a).start()
        turn = step // 2

        @pl.when((parity(step) == 0) & (turn + 1 < depth))
        def _():
            far_ready(slot_of(turn))

        @pl.when((parity(step) == 1) & (turn + 1 < depth))
        def _():
            near_ready(slot_of(turn + 1))

        @pl.when(step == 2 * depth - 3)
        def _():
            far_ready(slot_of(turn + 1))

        @pl.when(step + 1 < 2 * depth)
        def _():
            load_rows(step + 1).start()

    def step_body(step, carry):
        first_half(step)

        @pl.when(step == 2 * depth - 1)
        def _():
            after_hop(depth - 2)

        @pl.when(step >= 1)
        def _():
            after_core(step - 1)

        second_half(step)
        odd = parity(step) == 1

        @pl.when(odd & (step >= 3) & (step < 2 * depth - 1))
        def _():
            after_hop((step - 3) // 2)

        @pl.when(jnp.logical_not(odd) & (step >= 4))
        def _():
            after_hop2((step - 4) // 2)

        return carry

    lax.fori_loop(0, 2 * depth, step_body, 0)
    last = depth - 1
    own_rows, own_upstream = rows_tile.at[0, 0], upstream_tile.at[0, 0]
    own_loads = [
        pltpu.make_async_copy(rows_in, own_rows, end_sem.at[0]),
        pltpu.make_async_copy(
            upstream_in.at[at.z, at.y, at.x, at.c], own_upstream, end_sem.at[1]
        ),
    ]
    for copy in own_loads:
        copy.start()
    after_hop2(last - 1)
    after_row_hop(last, 1)
    may_hop2(last, 0)
    hop2_sum(0, last).start()
    after_core(2 * depth - 1)
    after_out_hop(last)
    may_hop2(last, 1)
    hop2_sum(1, last).start()
    after_row_hop(last, 0)

    def total_of(a):
        hop2_sum(a, last).wait()
        held = helds[a].at[last % 2, at.y, at.x]
        for turn in range(last):
            z_sum(a, turn).wait_recv()

        def total_body(i, carry):
            part = pl.ds(pl.multiple_of(i * piece, piece), piece)
            total = held[part].astype(f32) + hops2[a][part].astype(f32)
            for k in range(last):
                total = total + zs[a][k, part].astype(f32)
            sums[a][part] = total
            return carry

        lax.fori_loop(0, quarter // piece, total_body, 0)

    total_of(0)
    own_lane = lax.broadcasted_iota(jnp.int32, (quarter, 128), 1)
    chooses = (own_lane >= 3) & (own_lane < 3 + expert_count)
    for copy in own_loads:
        copy.wait()
    rows = own_rows[...]
    logits = jnp.dot(rows, side_w[...], preferred_element_type=f32)
    peak = jnp.max(jnp.where(chooses, logits, -1e30), axis=1, keepdims=True)
    expo = jnp.where(chooses, jnp.exp(jnp.where(chooses, logits, peak) - peak), 0.0)
    router = expo / jnp.sum(expo, axis=1, keepdims=True)
    mixer = 1.0 / (1.0 + jnp.exp(-jnp.where(own_lane == 2, logits, 0.0)))
    gate_dots = d_rows_sum[:, width:]
    d_router = jnp.where(chooses, gate_dots * own_upstream[:, width:].astype(f32), 0.0)
    d_logits = router * (d_router - jnp.sum(router * d_router, axis=1, keepdims=True))
    d_mix = gate_dots * mixer * (1.0 - mixer)
    d_side = jnp.where(own_lane == 2, d_mix, jnp.where(chooses, d_logits, 0.0))
    d_side_out[...] = d_side
    high = d_side.astype(bf16)
    lower = (d_side - high.astype(f32)).astype(bf16)
    for split in (high, lower):
        d_rows_sum[:, :width] += lax.dot_general(
            split, side_w[...], across, preferred_element_type=f32
        )

    def end_body(i, carry):
        part = pl.ds(pl.multiple_of(i * few, few), few)
        resid = resid_in[part]
        scale = lax.rsqrt(jnp.mean(resid * resid, axis=1, keepdims=True) + epsilon)
        unit_rows = resid * scale
        grads = d_rows_sum[part, :width]
        scaled = grads * gain_in[...]
        inner = jnp.mean(scaled * unit_rows, axis=1, keepdims=True)
        d_resid = own_upstream[part, :width].astype(f32) + scale * (scaled - unit_rows * inner)
        d_resid_out[part] = d_resid
        d_resid_low[part] = d_resid.astype(bf16)
        return carry + jnp.sum(grads * unit_rows, axis=0, keepdims=True)

    d_gain_out[...] = lax.fori_loop(0, quarter // few, end_body, jnp.zeros((1, width), f32))

    def gather_copy(kind):
        if kind == 2:
            src = dst = d_resid_low_out.at[1 - at.x, at.c]
        else:
            src, dst = d_resid_low, d_resid_low_out.at[at.x, at.c]
        peer = at.next_x if kind == 0 else at.next_core
        return remote(src, dst, gathered_send.at[kind], gathered_recv.at[kind], peer)

    own_end = pltpu.make_async_copy(d_resid_low, d_resid_low_out.at[at.x, at.c], own_sem)
    own_end.start()
    for kind in (0, 1):
        gather_copy(kind).start()
    total_of(1)
    block_out[...] = (resid_in[...] + out_sum[...]).astype(bf16)
    gather_copy(0).wait_recv()
    gather_copy(2).start()
    own_end.wait()
    gather_copy(0).wait_send()
    gather_copy(1).wait()
    gather_copy(2).wait()
    for copy in stores(2 * depth - 1):
        copy.wait()
    for a in (0, 1):
        for turn in range(max(0, depth - 3), depth - 1):
            z_sum(a, turn).wait_send()
    for k in range(1, depth):
        z_copy(k).wait_send()

    def finish(j, carry):
        for kind in range(8):
            plane_copy(j, kind).wait_send()
        return carry

    lax.fori_loop(0, depth, finish, 0)


def ffn_over_all(rows, upstream_all, experts, pieces, weights, resid, gain, units, expert_count):
    quarter, width = rows.shape
    ep_count, tp_count = lax.axis_size("ep"), lax.axis_size("tp")
    depth = ep_count // 2
    hidden = -(-(units[0] * units[1] + units[2]) // 128) * 128
    bf16, f32 = jnp.bfloat16, jnp.float32
    wide = width + 128
    tile_rows = tp_count * quarter
    tokens = ep_count * tile_rows
    anywhere = pl.BlockSpec(memory_space=pl.ANY)
    in_vmem = pl.BlockSpec(memory_space=pltpu.VMEM)

    def both(*lead):
        return [pltpu.VMEM(lead + (quarter, columns), bf16) for columns in (wide, width)]

    dma = pltpu.SemaphoreType.DMA
    outs = pl.pallas_call(
        functools.partial(ffn_kernel, units, expert_count),
        out_shape=(
            jax.ShapeDtypeStruct((depth, 2, 2, 2, quarter, width), bf16),
            jax.ShapeDtypeStruct((depth, 2, tile_rows, hidden), bf16),
            jax.ShapeDtypeStruct((depth, 2, tile_rows, 2 * hidden), bf16),
            jax.ShapeDtypeStruct((quarter, width), bf16),
            jax.ShapeDtypeStruct((2, 2, quarter, width), bf16),
            jax.ShapeDtypeStruct((quarter, width), f32),
            jax.ShapeDtypeStruct((1, width), f32),
            jax.ShapeDtypeStruct((quarter, 128), f32),
        ),
        in_specs=[anywhere] * 7 + [in_vmem] * 2,
        out_specs=(anywhere,) * 3 + (in_vmem, anywhere) + (in_vmem,) * 3,
        scratch_shapes=[
            pltpu.VMEM((quarter, wide), f32),
            pltpu.VMEM((quarter, width), f32),
            pltpu.VMEM((2 * hidden, width), bf16),
            pltpu.VMEM((hidden, width), bf16),
            pltpu.VMEM((width, 128), bf16),
            pltpu.VMEM((2, 2, quarter, width), bf16),
            pltpu.VMEM((2, 2, quarter, wide), bf16),
            pltpu.VMEM((tile_rows, 2 * hidden), f32),
            pltpu.VMEM((tile_rows, hidden), f32),
            pltpu.VMEM((tile_rows, 128), f32),
            pltpu.VMEM((tile_rows, 128), bf16),
            pltpu.VMEM((tile_rows, hidden), bf16),
            pltpu.VMEM((tile_rows, 2 * hidden), bf16),
            pltpu.VMEM((quarter, width), bf16),
        ]
        + both(2, 2)
        + both(2)
        + both(2, 2, 2)
        + both(2, 2)
        + both()
        + both(depth - 1)
        + both(2)
        + [
            dma((3,)),
            dma((3,)),
            dma((2, 3)),
            dma((2, 3)),
            dma((4 + 6 * depth,)),
            dma((2,)),
            dma,
            dma((depth - 1,)),
            dma((depth - 1,)),
            dma((depth, 8)),
            dma((depth, 8)),
            dma((2,)),
            dma((2,)),
            dma((2, 3)),
            dma((2, 3)),
            dma((2, depth - 1)),
            dma((2, depth - 1)),
            pltpu.SemaphoreType.REGULAR,
            pltpu.SemaphoreType.REGULAR((2,)),
            pltpu.SemaphoreType.REGULAR((2,)),
        ],
        compiler_params=pltpu.CompilerParams(
            collective_id=1, has_side_effects=True, vmem_limit_bytes=62 * 2**20
        ),
        cost_estimate=pl.CostEstimate(
            flops=12 * tokens * width * hidden,
            bytes_accessed=10 * tokens * width,
            transcendentals=tokens * hidden,
        ),
        name="ffn_all_tokens",
    )(
        rows,
        upstream_all.reshape(depth, 2, 2, 2, quarter, wide),
        *[array.reshape(-1, width) for array in experts],
        pieces,
        weights,
        resid,
        gain,
    )
    rows_all, weighted, d_pair, block_out, d_resid_low, d_resid, d_gain, d_side = outs
    return (
        rows_all.reshape(tokens, width),
        weighted.reshape(tokens, hidden),
        d_pair.reshape(tokens, 2 * hidden),
        block_out,
        d_resid_low.reshape(tile_rows, width),
        d_resid,
        d_gain[0],
        d_side,
    )


def over_tp(block, distance):
    devices = range(lax.axis_size("tp"))
    return lax.ppermute(block, "tp", [(i, i ^ distance) for i in devices])


def one_of(array, index, axis):
    return lax.dynamic_index_in_dim(array, index, axis, keepdims=False)


def sum_over_tp(part):
    rows, columns = part.shape
    tp = lax.axis_index("tp")
    x, c = tp // 2, tp % 2
    blocks = part.reshape(2, 2, rows // 4, columns)
    got = over_tp(one_of(blocks, 1 - c, 1).astype(jnp.bfloat16), 1)
    chip = one_of(blocks, c, 1).astype(jnp.float32) + got.astype(jnp.float32)
    got = over_tp(one_of(chip, 1 - x, 0).astype(jnp.bfloat16), 2)
    return one_of(chip, x, 0) + got.astype(jnp.float32)


def gather_over_tp(block):
    tp = lax.axis_index("tp")
    x, c = tp // 2, tp % 2
    got = over_tp(block, 2)
    pair = jnp.where(x == 0, jnp.stack([block, got]), jnp.stack([got, block]))
    got = over_tp(pair, 1)
    four = jnp.where(c == 0, jnp.stack([pair, got], axis=1), jnp.stack([got, pair], axis=1))
    return four.reshape(4 * block.shape[0], block.shape[1])


def swap_copies(at, pieces_in, pieces_out, send_sem, recv_sem, leave):
    count = 2 * at.depth
    copies = []
    for k in range(1, count):
        to, back = lax.rem(at.ep + k, count), lax.rem(at.ep + count - k, count)
        if leave:
            src, dst, peer = pieces_in.at[to], pieces_out.at[at.ep], to
        else:
            src, dst, peer = pieces_in.at[back], pieces_out.at[back], back
        copies.append(remote(src, dst, send_sem.at[k], recv_sem.at[k], (peer, at.tp)))
    return copies


def weights_kernel(
    own_in,
    pieces_in,
    all_out,
    pieces_out,
    own_sem,
    z_send,
    z_recv,
    y_send,
    y_recv,
    swap_send,
    swap_recv,
):
    at = Place()
    depth = at.depth
    half = own_in.shape[0] // 2
    last = depth - 1

    def block(k, y, h):
        return all_out.at[at.z + k, y, pl.ds(h * half, half)]

    def z_copy(k, h, direction):
        if k == 0:
            src = own_in.at[pl.ds(h * half, half)]
        else:
            src = block(k, at.y, h)
        slot = last + k - direction
        return remote(
            src,
            block(k, at.y, h),
            z_send.at[last + k, h, (direction + 1) // 2],
            z_recv.at[slot, h],
            at.at_z(at.z + direction),
        )

    def z_arrival(k, h):
        direction = 1 if k > 0 else -1
        dst = block(k, at.y, h)
        return remote(
            dst, dst, z_send.at[last + k, h, 0], z_recv.at[last + k, h], at.at_z(at.z + direction)
        )

    def y_copy(k, h):
        src = own_in.at[pl.ds(h * half, half)] if k == 0 else block(k, at.y, h)
        return remote(
            src, block(k, at.y, h), y_send.at[last + k, h], y_recv.at[last + k, h], at.next_y
        )

    own_copies = [
        pltpu.make_async_copy(own_in, all_out.at[at.z, at.y], own_sem.at[0]),
        pltpu.make_async_copy(pieces_in.at[at.ep], pieces_out.at[at.ep], own_sem.at[1]),
    ]
    for copy in own_copies:
        copy.start()
    has_up, has_down = at.z + 1 < depth, at.z > 0
    at.greet_ep()

    for h in (0, 1):
        pl.when(has_up)(lambda: z_copy(0, h, 1).start())
        pl.when(has_down)(lambda: z_copy(0, h, -1).start())
        y_copy(0, h).start()
    swap = (at, pieces_in, pieces_out, swap_send, swap_recv)
    for copy in swap_copies(*swap, True):
        copy.start()
    for k in range(1, depth):
        for h in (0, 1):
            for sign in (-1, 1):
                there = at.z + sign * k
                exists = (there >= 0) & (there < depth)
                onward = at.z - sign
                goes_on = exists & (onward >= 0) & (onward < depth)

                @pl.when(exists)
                def _():
                    z_arrival(sign * k, h).wait_recv()

                @pl.when(goes_on)
                def _():
                    z_copy(sign * k, h, -sign).start()

                @pl.when(exists)
                def _():
                    y_copy(sign * k, h).start()

    for copy in own_copies:
        copy.wait()
    for copy in swap_copies(*swap, False):
        copy.wait_recv()
    for copy in swap_copies(*swap, True):
        copy.wait_send()
    for h in (0, 1):
        pl.when(has_up)(lambda: z_copy(0, h, 1).wait_send())
        pl.when(has_down)(lambda: z_copy(0, h, -1).wait_send())
    for k in range(-last, depth):
        there = at.z + k
        exists = (there >= 0) & (there < depth)
        sign = 1 if k > 0 else -1
        onward = at.z - sign
        goes_on = exists & (onward >= 0) & (onward < depth)
        for h in (0, 1):

            @pl.when(exists)
            def _():
                y_copy(k, h).wait()

            if k != 0:

                @pl.when(goes_on)
                def _():
                    z_copy(k, h, -sign).wait_send()


def gather_over_ep(block, pieces):
    rows, columns = block.shape
    depth = lax.axis_size("ep") // 2
    anywhere = pl.BlockSpec(memory_space=pl.ANY)
    slots = 2 * depth - 1
    out, pieces = pl.pallas_call(
        weights_kernel,
        out_shape=(
            jax.ShapeDtypeStruct((depth, 2, rows, columns), block.dtype),
            jax.ShapeDtypeStruct(pieces.shape, pieces.dtype),
        ),
        in_specs=[anywhere] * 2,
        out_specs=(anywhere,) * 2,
        scratch_shapes=[
            pltpu.SemaphoreType.DMA((2,)),
            pltpu.SemaphoreType.DMA((slots, 2, 2)),
            pltpu.SemaphoreType.DMA((slots, 2)),
            pltpu.SemaphoreType.DMA((slots, 2)),
            pltpu.SemaphoreType.DMA((slots, 2)),
            pltpu.SemaphoreType.DMA((2 * depth,)),
            pltpu.SemaphoreType.DMA((2 * depth,)),
        ],
        compiler_params=pltpu.CompilerParams(collective_id=3, has_side_effects=True),
        cost_estimate=pl.CostEstimate(
            flops=0, bytes_accessed=8 * depth * rows * columns, transcendentals=0
        ),
        name="gather_weights",
    )(block, pieces)
    return out.reshape(2 * depth * rows, columns), pieces


class RowGather:
    def __init__(self, at, mine, everywhere, z_send, z_recv, plane_send, plane_recv):
        self.at, self.mine, self.everywhere = at, mine, everywhere
        self.z_sems, self.plane_sems = (z_send, z_recv), (plane_send, plane_recv)
        self.half = mine.shape[0] // 2

    def block(self, j, y, x):
        return self.everywhere.at[self.at.behind(j), y, x, self.at.c]

    def plane_copy(self, j, kind):
        at, half = self.at, self.half
        if kind == 0:
            src, peer = self.block(j, at.y, at.x), at.next_x
        elif kind == 1:
            src, peer = self.block(j, at.y, at.x), at.next_y
        elif kind == 2:
            src, peer = self.block(j, at.y, 1 - at.x).at[pl.ds(0, half)], at.next_y
        elif kind == 3:
            src, peer = self.block(j, 1 - at.y, at.x).at[pl.ds(half, half)], at.next_x
        else:
            y, x = 1 - at.y if kind >= 6 else at.y, 1 - at.x if kind % 2 else at.x
            src, peer = self.block(j, y, x), at.next_core
        send, recv = self.plane_sems
        return remote(src, src, send.at[j, kind], recv.at[j, kind], peer)

    def z_copy(self, k):
        send, recv = self.z_sems
        dst = self.block(0, self.at.y, self.at.x)
        peer = self.at.at_z(self.at.ahead(k))
        return remote(self.mine, dst, send.at[k - 1], recv.at[k - 1], peer)

    def begin(self, j):
        if j > 0:
            send, recv = self.z_sems
            dst = self.block(j, self.at.y, self.at.x)
            peer = self.at.at_z(self.at.behind(j))
            remote(dst, dst, send.at[j - 1], recv.at[j - 1], peer).wait_recv()
        for kind in (0, 1, 4):
            self.plane_copy(j, kind).start()

    def spread(self, j):
        self.plane_copy(j, 0).wait_recv()
        self.plane_copy(j, 2).start()
        self.plane_copy(j, 5).start()
        self.plane_copy(j, 1).wait_recv()
        self.plane_copy(j, 3).start()
        self.plane_copy(j, 6).start()

    def last_hop(self, j):
        self.plane_copy(j, 2).wait_recv()
        self.plane_copy(j, 3).wait_recv()
        self.plane_copy(j, 7).start()

    def finish(self):
        for k in range(1, self.at.depth):
            self.z_copy(k).wait_send()
        for j in range(self.at.depth):
            for kind in range(8):
                if kind >= 4:
                    self.plane_copy(j, kind).wait_recv()
                self.plane_copy(j, kind).wait_send()


def front_kernel(
    score_scale,
    normed_in,
    weights_in,
    upstream_in,
    cos_in,
    sin_in,
    query_start,
    query_at,
    tokens_in,
    gain_in,
    upstream_all,
    k_out,
    v_out,
    q_out,
    lse_out,
    attended_out,
    resid_out,
    rows_out,
    normed,
    qkv_w,
    out_w,
    k_all,
    v_all,
    scores_of,
    part,
    core_got,
    x_got,
    load_sem,
    z_send,
    z_recv,
    plane_send,
    plane_recv,
    kv_send,
    kv_recv,
    tp_send,
    tp_recv,
):
    at = Place()
    depth = at.depth
    count = 2 * depth
    heads, tokens, head = q_out.shape
    heads_width = heads * head
    windows = k_all.shape[1] // tokens
    quarter, width = resid_out.shape
    f32, bf16 = jnp.float32, jnp.bfloat16
    across = (((1,), (1,)), ((), ()))
    gather = RowGather(at, upstream_in, upstream_all, z_send, z_recv, plane_send, plane_recv)
    own = (windows - 1) * tokens

    def kv_copy(kind, w):
        held = (k_all, v_all)[kind]
        return remote(
            held.at[:, pl.ds(own, tokens)],
            held.at[:, pl.ds(w * tokens, tokens)],
            kv_send.at[kind, w],
            kv_recv.at[kind, w],
            (at.ep + (windows - 1 - w), at.tp),
        )

    def kv_arrival(kind, w):
        dst = (k_all, v_all)[kind].at[:, pl.ds(w * tokens, tokens)]
        peer = (at.ep - (windows - 1 - w), at.tp)
        return remote(dst, dst, kv_send.at[kind, w], kv_recv.at[kind, w], peer)

    def core_copy():
        return remote(part.at[:, 1 - at.c], core_got, tp_send.at[0], tp_recv.at[0], at.next_core)

    def x_copy():
        return remote(part.at[1 - at.x, at.c], x_got, tp_send.at[1], tp_recv.at[1], at.next_x)

    pairs = (
        (normed_in, normed),
        (weights_in.at[:, pl.ds(0, 3 * heads_width)], qkv_w),
        (weights_in.at[:, pl.ds(3 * heads_width, heads_width)], out_w),
    )
    loads = [pltpu.make_async_copy(src, dst, load_sem.at[i]) for i, (src, dst) in enumerate(pairs)]
    for copy in loads:
        copy.start()
    at.greet_row()
    own_copy = pltpu.make_async_copy(
        upstream_in, gather.block(0, at.y, at.x), load_sem.at[len(pairs)]
    )
    own_copy.start()
    own_copy.wait()
    gather.begin(0)
    loads[0].wait()
    loads[1].wait()
    lane = lax.broadcasted_iota(jnp.int32, (tokens, head), 1)
    sign = jnp.where(lane < head // 2, -1.0, 1.0)

    def rotated(array):
        return array * cos_in[...] + pltpu.roll(array, head // 2, 1) * sign * sin_in[...]

    keys = jnp.dot(
        normed[...], qkv_w[:, heads_width : 2 * heads_width], preferred_element_type=f32
    )
    for h in range(heads):
        k_all[h, own:] = rotated(keys[:, h * head : (h + 1) * head]).astype(bf16)
    values = jnp.dot(normed[...], qkv_w[:, 2 * heads_width :], preferred_element_type=f32)
    for h in range(heads):
        v_all[h, own:] = values[:, h * head : (h + 1) * head].astype(bf16)
    for w in reversed(range(windows - 1)):

        @pl.when(at.ep + (windows - 1 - w) < count)
        def _():
            for kind in (0, 1):
                kv_copy(kind, w).start()

    gather.z_copy(1).start()
    gather.spread(0)
    queries = jnp.dot(normed[...], qkv_w[:, :heads_width], preferred_element_type=f32)
    for h in range(heads):
        q_out[h] = rotated(queries[:, h * head : (h + 1) * head]).astype(bf16)
    gather.last_hop(0)
    for w in range(windows - 1):

        @pl.when(at.ep < windows - 1 - w)
        def _():
            for held in (k_all, v_all):
                held[:, w * tokens : (w + 1) * tokens] = jnp.zeros((heads, tokens, head), bf16)

        @pl.when(at.ep >= windows - 1 - w)
        def _():
            for kind in (0, 1):
                kv_arrival(kind, w).wait_recv()

    outs = [
        pltpu.make_async_copy(src, dst, load_sem.at[i])
        for i, (src, dst) in enumerate(((k_all, k_out), (v_all, v_out)))
    ]
    for copy in outs:
        copy.start()
    for k in range(2, depth):
        gather.z_copy(k).start()
    due = [functools.partial(gather.begin, 1)]
    for j in range(1, depth):
        due.append(functools.partial(gather.spread, j))
        if j + 1 < depth:
            due.append(functools.partial(gather.begin, j + 1))
        due.append(functools.partial(gather.last_hop, j))

    def head_body(h, carry):
        q = q_out[h]
        peak = jnp.full((1, tokens), -1e30, f32)
        for w in range(windows):
            some = slice(w * tokens, (w + 1) * tokens)
            scores = lax.dot_general(k_all[h, some], q, across, preferred_element_type=f32)
            key_at = lax.broadcasted_iota(jnp.int32, scores.shape, 0)
            key_at = key_at + (at.ep + w + 1 - windows) * tokens
            allowed = (key_at >= query_start[...]) & (key_at <= query_at[...])
            scores = jnp.where(allowed, scores * score_scale, -1e30)
            scores_of[w] = scores
            peak = jnp.maximum(peak, jnp.max(scores, axis=0, keepdims=True))
        total = jnp.zeros((1, tokens), f32)
        for w in range(windows):
            expo = jnp.exp(scores_of[w] - peak)
            scores_of[w] = expo
            total = total + jnp.sum(expo, axis=0, keepdims=True)
        lse_out[h] = peak + jnp.log(total)
        each = 1.0 / total
        attended = jnp.zeros((head, tokens), f32)
        for w in range(windows):
            some = slice(w * tokens, (w + 1) * tokens)
            probs = (scores_of[w] * each).astype(bf16)
            attended = attended + jnp.dot(
                v_all[h, some].T, probs, preferred_element_type=f32
            )
        here = pl.ds(pl.multiple_of(h * head, head), head)
        attended_out[:, here] = attended.T.astype(bf16)
        for i in range(heads):

            @pl.when(h == i)
            def _():
                for action in due[i : i + 1]:
                    action()

        return carry

    lax.fori_loop(0, heads, head_body, 0)
    loads[2].wait()
    strips = 4
    strip = width // strips
    for n in range(strips):
        some = slice(n * strip, (n + 1) * strip)
        product = lax.dot_general(
            attended_out[...], out_w[some], across, preferred_element_type=f32
        )
        part[:, :, :, some] = product.astype(bf16).reshape(2, 2, quarter, strip)
    core_copy().start()
    rest = due[heads:]
    for action in rest[:2]:
        action()
    core_copy().wait()
    for x in (0, 1):
        part[x, at.c] = part[x, at.c] + core_got[x]
    x_copy().start()
    for action in rest[2:]:
        action()
    x_copy().wait()
    few = 16

    def end_body(i, carry):
        here = pl.ds(pl.multiple_of(i * few, few), few)
        total = part[at.x, at.c, here].astype(f32) + x_got[here].astype(f32)
        resid = tokens_in[here].astype(f32) + total
        scale = lax.rsqrt(jnp.mean(resid * resid, axis=1, keepdims=True) + epsilon)
        resid_out[here] = resid
        rows_out[here] = (resid * scale * gain_in[...]).astype(bf16)
        return carry

    lax.fori_loop(0, quarter // few, end_body, 0)
    for copy in outs:
        copy.wait()
    for w in range(windows - 1):

        @pl.when(at.ep + (windows - 1 - w) < count)
        def _():
            for kind in (0, 1):
                kv_copy(kind, w).wait_send()

    gather.finish()


def attention_front(normed, weights, upstream, in_place, heads, scale):
    tokens, width = normed.shape
    quarter, wide = upstream.shape
    depth = lax.axis_size("ep") // 2
    head, windows = HD, 3
    f32, bf16 = jnp.float32, jnp.bfloat16
    anywhere = pl.BlockSpec(memory_space=pl.ANY)
    in_vmem = pl.BlockSpec(memory_space=pltpu.VMEM)
    dma = pltpu.SemaphoreType.DMA
    shape = jax.ShapeDtypeStruct
    window = (heads, windows * tokens, head)
    outs = pl.pallas_call(
        functools.partial(front_kernel, scale),
        out_shape=(
            shape((depth, 2, 2, 2, quarter, wide), bf16),
            shape(window, bf16),
            shape(window, bf16),
            shape((heads, tokens, head), bf16),
            shape((heads, 1, tokens), f32),
            shape((tokens, heads * head), bf16),
            shape((quarter, width), f32),
            shape((quarter, width), bf16),
        ),
        in_specs=[anywhere] * 3 + [in_vmem] * len(in_place),
        out_specs=(anywhere,) * 3 + (in_vmem,) * 5,
        scratch_shapes=[
            pltpu.VMEM((tokens, width), bf16),
            pltpu.VMEM((width, 3 * heads * head), bf16),
            pltpu.VMEM((width, heads * head), bf16),
            pltpu.VMEM(window, bf16),
            pltpu.VMEM(window, bf16),
            pltpu.VMEM((windows, tokens, tokens), f32),
            pltpu.VMEM((2, 2, quarter, width), bf16),
            pltpu.VMEM((2, quarter, width), bf16),
            pltpu.VMEM((quarter, width), bf16),
            dma((4,)),
            dma((depth - 1,)),
            dma((depth - 1,)),
            dma((depth, 8)),
            dma((depth, 8)),
            dma((2, windows - 1)),
            dma((2, windows - 1)),
            dma((2,)),
            dma((2,)),
        ],
        compiler_params=pltpu.CompilerParams(
            collective_id=5, has_side_effects=True, vmem_limit_bytes=50 * 2**20
        ),
        cost_estimate=pl.CostEstimate(
            flops=8 * tokens * width * heads * head,
            bytes_accessed=2 * 8 * depth * quarter * wide,
            transcendentals=heads * tokens * windows * tokens,
        ),
        name="attention_front",
    )(normed, weights, upstream, *in_place)
    return (outs[0].reshape(8 * depth * quarter, wide),) + tuple(outs[1:])


def back_kernel(
    units,
    score_scale,
    d_low_in,
    weights_in,
    q_in,
    k_in,
    v_in,
    turned_in,
    block_in,
    rows_in,
    d_pair_in,
    upstream_in,
    weighted_in,
    lse_in,
    query_start,
    query_at,
    cos_in,
    sin_in,
    own_rows_in,
    gain_in,
    d_resid_in,
    gain_two_in,
    side_in,
    out,
    small_out,
    block_out,
    d_rows_out,
    pieces_got,
    gate_out,
    up_out,
    down_out,
    qkv_w,
    turned,
    d_out,
    d_got,
    d_own,
    d_proj,
    part,
    core_got,
    x_got,
    d_rows,
    own,
    y_out,
    hop,
    from_z,
    small_own,
    small_hop,
    small_z,
    small,
    small_got,
    pieces,
    load_sem,
    d_send,
    d_recv,
    tp_send,
    tp_recv,
    y_send,
    y_recv,
    z_send,
    z_recv,
    little_send,
    little_recv,
    small_send,
    small_recv,
    swap_send,
    swap_recv,
    rows_send,
    rows_recv,
    own_sem,
    tile_sem,
    store_sem,
    strip_sem,
):
    at = Place()
    depth = at.depth
    count = 2 * depth
    heads, tokens, head = q_in.shape
    heads_width = heads * head
    windows = k_in.shape[1] // tokens
    quarter, width = d_rows.shape
    rows = out.shape[0]
    f32, bf16 = jnp.float32, jnp.bfloat16
    across = (((1,), (1,)), ((), ()))
    slot_here, slot_hidden, shared_hidden = units
    routed = slot_here * slot_hidden
    hidden = weighted_in.shape[2]
    few = 16

    def d_copy(w, h):
        peer = (at.ep - (2 - w), at.tp)
        return remote(d_out.at[w, h], d_got.at[w, h], d_send.at[w, h], d_recv.at[w, h], peer)

    def d_arrival(w, h):
        peer = (at.ep + (2 - w), at.tp)
        dst = d_got.at[w, h]
        return remote(dst, dst, d_send.at[w, h], d_recv.at[w, h], peer)

    def core_copy():
        return remote(part.at[:, 1 - at.c], core_got, tp_send.at[0], tp_recv.at[0], at.next_core)

    def x_copy():
        return remote(part.at[1 - at.x, at.c], x_got, tp_send.at[1], tp_recv.at[1], at.next_x)

    cuts = (pl.ds(0, heads_width), pl.ds(heads_width, 2 * heads_width))

    def y_copy(q, j):
        return remote(
            y_out.at[j, :, cuts[q]], hop.at[j, :, cuts[q]], y_send.at[q, j], y_recv.at[q, j], at.next_y
        )

    def z_copy(q, j):
        return remote(
            own.at[j, :, cuts[q]],
            from_z.at[j - 1, :, cuts[q]],
            z_send.at[q, j],
            z_recv.at[q, j],
            at.at_z(at.ahead(j)),
        )

    def little_y(j):
        return remote(
            small_own.at[at.ahead(j), 1 - at.y],
            small_hop.at[j],
            little_send.at[0, j],
            little_recv.at[0, j],
            at.next_y,
        )

    def little_z(j):
        return remote(
            small_own.at[at.ahead(j), at.y],
            small_z.at[j - 1],
            little_send.at[1, j],
            little_recv.at[1, j],
            at.at_z(at.ahead(j)),
        )

    def small_copy(kind):
        peer = at.next_core if kind == 0 else at.next_x
        return remote(
            small.at[kind], small_got.at[kind], small_send.at[kind], small_recv.at[kind], peer
        )

    ends = ((block_in, block_out), (d_rows, d_rows_out))

    def rows_copy(a, kind):
        mine, gathered = ends[a]
        if kind == 2:
            src = dst = gathered.at[1 - at.x, at.c]
        else:
            src, dst = mine, gathered.at[at.x, at.c]
        peer = at.next_x if kind == 0 else at.next_core
        return remote(src, dst, rows_send.at[a, kind], rows_recv.at[a, kind], peer)

    def rows_own(a):
        mine, gathered = ends[a]
        return pltpu.make_async_copy(mine, gathered.at[at.x, at.c], own_sem.at[a])

    def rows_begin(a):
        for kind in (0, 1):
            rows_copy(a, kind).start()
        rows_own(a).start()

    def rows_pass_on(a):
        rows_copy(a, 0).wait_recv()
        rows_copy(a, 2).start()

    def rows_end(a):
        rows_own(a).wait()
        rows_copy(a, 0).wait_send()
        rows_copy(a, 1).wait()
        rows_copy(a, 2).wait()

    def swap_copies(p, leave):
        some = pl.ds(p * shared_hidden, shared_hidden)
        copies = []
        for k in range(1, count):
            to, back = lax.rem(at.ep + k, count), lax.rem(at.ep + count - k, count)
            if leave:
                src, dst, peer = pieces.at[to, some], pieces_got.at[at.ep, some], to
            else:
                src, dst, peer = pieces.at[back, some], pieces_got.at[back, some], back
            copies.append(remote(src, dst, swap_send.at[p, k], swap_recv.at[p, k], (peer, at.tp)))
        return copies

    def swap_own(p):
        some = pl.ds(p * shared_hidden, shared_hidden)
        return pltpu.make_async_copy(
            pieces.at[at.ep, some], pieces_got.at[at.ep, some], own_sem.at[2 + p]
        )

    strips = 4
    strip = width // strips

    def load_strip(n):
        src = weights_in.at[pl.ds(n * strip, strip), pl.ds(0, 3 * heads_width)]
        return pltpu.make_async_copy(src, qkv_w.at[n % 2], strip_sem.at[n % 2])

    late_load = pltpu.make_async_copy(turned_in, turned, load_sem.at[1])
    lane = lax.broadcasted_iota(jnp.int32, (tokens, head), 1)
    sign = jnp.where(lane < head // 2, -1.0, 1.0)

    def unrotated(grads):
        turned_part = pltpu.roll(grads * sin_in[...], head // 2, 1) * sign
        return grads * cos_in[...] - turned_part

    def attention(d_low, out_w, q_all, k_all, v_all, d_att, probs, d_probs):
        pairs = (
            (d_low_in, d_low),
            (weights_in.at[:, pl.ds(3 * heads_width, heads_width)], out_w),
            (q_in, q_all),
            (k_in, k_all),
            (v_in, v_all),
        )
        copies = [
            pltpu.make_async_copy(src, dst, load_sem.at[2 + i])
            for i, (src, dst) in enumerate(pairs)
        ]
        for copy in copies + [late_load, load_strip(0), load_strip(1)]:
            copy.start()
        at.greet_row()
        rows_begin(0)
        copies[0].wait()
        copies[1].wait()
        d_attended = jnp.dot(d_low[...], out_w[...], preferred_element_type=f32).astype(bf16)
        for h in range(heads):
            d_att[h] = d_attended[:, h * head : (h + 1) * head]
        for copy in copies[2:]:
            copy.wait()

        def head_body(h, carry):
            queries, d_a = q_all[h], d_att[h]
            delta = jnp.zeros((1, tokens), f32)
            for w in range(windows):
                some = slice(w * tokens, (w + 1) * tokens)
                scores = lax.dot_general(
                    k_all[h, some], queries, across, preferred_element_type=f32
                )
                key_at = lax.broadcasted_iota(jnp.int32, scores.shape, 0)
                key_at = key_at + (at.ep + w + 1 - windows) * tokens
                allowed = (key_at >= query_start[...]) & (key_at <= query_at[...])
                p = jnp.where(allowed, jnp.exp(scores * score_scale - lse_in[h]), 0.0)
                d_p = lax.dot_general(v_all[h, some], d_a, across, preferred_element_type=f32)
                probs[w] = p
                d_probs[w] = d_p
                delta = delta + jnp.sum(p * d_p, axis=0, keepdims=True)
            d_queries = jnp.zeros((head, tokens), f32)
            for w in range(windows):
                some = slice(w * tokens, (w + 1) * tokens)
                p = probs[w]
                d_scores = (p * (d_probs[w] - delta)).astype(bf16)
                d_keys = jnp.dot(d_scores, queries, preferred_element_type=f32) * score_scale
                d_values = jnp.dot(p.astype(bf16), d_a, preferred_element_type=f32)
                if w < windows - 1:
                    d_out[w, h, :, :head] = d_keys.astype(bf16)
                    d_out[w, h, :, head:] = d_values.astype(bf16)

                    @pl.when(at.ep >= 2 - w)
                    def _():
                        d_copy(w, h).start()

                else:
                    d_own[h, :, :head] = d_keys
                    d_own[h, :, head:] = d_values
                d_queries = d_queries + jnp.dot(
                    k_all[h, some].T, d_scores, preferred_element_type=f32
                )
            here = pl.ds(pl.multiple_of(h * head, head), head)
            d_proj[:, here] = unrotated((d_queries * score_scale).T).astype(bf16)
            return carry

        lax.fori_loop(0, heads, head_body, 0)

    pl.run_scoped(
        attention,
        pltpu.VMEM((tokens, width), bf16),
        pltpu.VMEM((width, heads_width), bf16),
        pltpu.VMEM((heads, tokens, head), bf16),
        pltpu.VMEM((heads, windows * tokens, head), bf16),
        pltpu.VMEM((heads, windows * tokens, head), bf16),
        pltpu.VMEM((heads, tokens, head), bf16),
        pltpu.VMEM((windows, tokens, tokens), f32),
        pltpu.VMEM((windows, tokens, tokens), f32),
    )
    order = [j for j in range(1, depth)] + [0]

    def own_body(h, carry):
        for w in range(windows - 1):

            @pl.when(at.ep + (2 - w) < count)
            def _():
                d_arrival(w, h).wait_recv()
                d_own[h] += d_got[w, h].astype(f32)

        k_here = pl.ds(pl.multiple_of(heads_width + h * head, head), head)
        v_here = pl.ds(pl.multiple_of(2 * heads_width + h * head, head), head)
        d_proj[:, k_here] = unrotated(d_own[h, :, :head]).astype(bf16)
        d_proj[:, v_here] = d_own[h, :, head:].astype(bf16)
        return carry

    def weight_rows(into, q, z, y):
        here = pl.ds(pl.multiple_of((z * 2 + y) * rows, rows), rows)
        product = jnp.dot(turned[here], d_proj[:, cuts[q]], preferred_element_type=f32)
        into[:, cuts[q]] = product.astype(bf16)

    def begin_sums(q):
        for j in order:
            weight_rows(y_out.at[j], q, at.ahead(j), 1 - at.y)
            y_copy(q, j).start()

    def own_sums(q):
        for j in order:
            weight_rows(own.at[j], q, at.ahead(j), at.y)

    def projections():
        lax.fori_loop(0, heads, own_body, 0)
        for n in range(strips):
            some = slice(n * strip, (n + 1) * strip)
            load_strip(n).wait()
            product = lax.dot_general(
                d_proj[...], qkv_w[n % 2], across, preferred_element_type=f32
            )
            part[:, :, :, some] = product.astype(bf16).reshape(2, 2, quarter, strip)
            if n + 2 < strips:
                load_strip(n + 2).start()
        core_copy().start()
        begin_sums(1)
        core_copy().wait()
        for x in (0, 1):
            part[x, at.c] = part[x, at.c] + core_got[x]
        x_copy().start()
        own_sums(1)
        x_copy().wait()

        def end_body(i, carry):
            here = pl.ds(pl.multiple_of(i * few, few), few)
            grads = part[at.x, at.c, here].astype(f32) + x_got[here].astype(f32)
            inputs = own_rows_in[here].astype(f32)
            scale = lax.rsqrt(jnp.mean(inputs * inputs, axis=1, keepdims=True) + epsilon)
            unit_rows = inputs * scale
            scaled = grads * gain_in[...]
            inner = jnp.mean(scaled * unit_rows, axis=1, keepdims=True)
            total = d_resid_in[here] + scale * (scaled - unit_rows * inner)
            d_rows[here] = total.astype(bf16)
            return carry + jnp.sum(grads * unit_rows, axis=0, keepdims=True)

        d_gain = lax.fori_loop(0, quarter // few, end_body, jnp.zeros((1, width), f32))
        rows_begin(1)
        line = lax.broadcasted_iota(jnp.int32, (128, rows), 0)
        for e in range(count):
            some = slice(e * rows, (e + 1) * rows)
            gains = jnp.where(line == 0, d_gain[:, some], 0.0)
            gains = jnp.where(line == 1, gain_two_in[:, some], gains)
            small_own[e // 2, e % 2] = (gains.T + side_in[some]).astype(bf16)
        for j in order:
            little_y(j).start()

    def after_y(q, j):
        y_copy(q, j).wait_recv()

        def body(i, carry):
            some = pl.ds(pl.multiple_of(i * few, few), few)
            own[j, some, cuts[q]] = own[j, some, cuts[q]] + hop[j, some, cuts[q]]
            return carry

        lax.fori_loop(0, rows // few, body, 0)
        if j > 0:
            z_copy(q, j).start()

    def after_little():
        for j in order:
            little_y(j).wait_recv()
            here = small_own.at[at.ahead(j), at.y]
            here[...] = here[...] + small_hop[j]
            if j > 0:
                little_z(j).start()

    hooks = {(0, 0): [functools.partial(rows_pass_on, 0)]}
    for i, j in enumerate(order):
        hooks.setdefault((0, min(2 * i + 1, count - 1)), []).append(functools.partial(after_y, 0, j))
    hooks[(1, 2)] = [functools.partial(rows_pass_on, 1)]
    hooks[(1, 3)] = [after_little]
    last_hooks = []
    for i, j in enumerate(order):
        when = count + 5 + 5 * i
        due = functools.partial(after_y, 1, j)
        if when < 3 * count:
            hooks.setdefault((when // count, when % count), []).append(due)
        else:
            last_hooks.append(due)

    def weight_gradients(turned_left, left_tile, right_part, staging):
        lefts = (
            lambda tile: d_pair_in.at[tile, :, pl.ds(0, hidden)],
            lambda tile: d_pair_in.at[tile, :, pl.ds(hidden, hidden)],
            lambda tile: weighted_in.at[tile],
        )
        rights = (rows_in, rows_in, upstream_in)
        results = (gate_out, up_out, down_out)
        columns = width // count

        def load_left(p, tile):
            slot = lax.rem(tile, 2)
            return pltpu.make_async_copy(
                lefts[p](tile), left_tile.at[slot], tile_sem.at[0, slot]
            )

        def load_right(p, n):
            slot = lax.rem(n, 2)
            here = pl.ds(pl.multiple_of(n * columns, columns), columns)
            return pltpu.make_async_copy(
                rights[p].at[:, :, here], right_part.at[slot], tile_sem.at[1, slot]
            )

        def store(p, n):
            slot = lax.rem(n, 2)
            here = pl.ds(pl.multiple_of(n * columns, columns), columns)
            return pltpu.make_async_copy(
                staging.at[slot], results[p].at[:, here], store_sem.at[slot]
            )

        def turn_left(p, tile):
            load_left(p, tile).wait()

            @pl.when(tile + 1 < count)
            def _():
                load_left(p, tile + 1).start()

            here = pl.ds(pl.multiple_of(tile * tokens, tokens), tokens)
            turned_left[:, here] = left_tile[lax.rem(tile, 2)].T

        def run_pass(p):
            def part_body(n, carry):
                slot = lax.rem(n, 2)
                load_right(p, n).wait()

                @pl.when(n + 1 < count)
                def _():
                    load_right(p, n + 1).start()

                if p < 2:

                    @pl.when(n + 1 == count)
                    def _():
                        load_right(p + 1, 0).start()

                @pl.when(n >= 2)
                def _():
                    store(p, n - 2).wait()

                product = jnp.dot(
                    turned_left[...],
                    right_part[slot].reshape(count * tokens, columns),
                    preferred_element_type=f32,
                )
                staging[slot] = product[:routed].astype(bf16)
                pieces[n, p * shared_hidden : (p + 1) * shared_hidden] = product[
                    routed : routed + shared_hidden
                ].astype(bf16)
                store(p, n).start()
                for (hook_pass, hook_part), actions in hooks.items():
                    if hook_pass == p:

                        @pl.when(n == hook_part)
                        def _():
                            for action in actions:
                                action()

                return carry

            def turn_body(tile, carry):
                turn_left(p, tile)
                return carry

            lax.fori_loop(0, count, turn_body, 0)
            if p < 2:
                load_left(p + 1, 0).start()
            lax.fori_loop(0, count, part_body, 0)
            for n in (count - 2, count - 1):
                store(p, n).wait()
            swap_own(p).start()
            for copy in swap_copies(p, True):
                copy.start()

        load_left(0, 0).start()
        load_right(0, 0).start()
        late_load.wait()
        begin_sums(0)
        own_sums(0)

        run_pass(0)
        projections()
        run_pass(1)
        run_pass(2)
        for action in last_hooks:
            action()

    pl.run_scoped(
        weight_gradients,
        pltpu.VMEM((hidden, count * tokens), bf16),
        pltpu.VMEM((2, tokens, hidden), bf16),
        pltpu.VMEM((2, count, tokens, width // count), bf16),
        pltpu.VMEM((2, routed, width // count), bf16),
    )
    total = small_own[at.z, at.y].astype(f32)
    for j in range(1, depth):
        little_z(j).wait_recv()
        total = total + small_z[j - 1].astype(f32)
    for kind in (0, 1):
        small[kind] = total
        small_copy(kind).start()
        small_copy(kind).wait()
        total = small[kind] + small_got[kind]
    small_out[...] = total
    for j in range(1, depth):
        for q in (0, 1):
            z_copy(q, j).wait_recv()

    def total_body(i, carry):
        some = pl.ds(pl.multiple_of(i * few, few), few)
        result = own[0, some].astype(f32)
        for k in range(depth - 1):
            result = result + from_z[k, some].astype(f32)
        out[some] = result
        return carry

    lax.fori_loop(0, rows // few, total_body, 0)
    for j in range(depth):
        little_y(j).wait_send()
        if j > 0:
            little_z(j).wait_send()
        for q in (0, 1):
            y_copy(q, j).wait_send()
            if j > 0:
                z_copy(q, j).wait_send()
    for a in (0, 1):
        rows_end(a)
    for p in range(3):
        swap_own(p).wait()
        for copy in swap_copies(p, False):
            copy.wait_recv()
        for copy in swap_copies(p, True):
            copy.wait_send()

    def finish(h, carry):
        for w in range(windows - 1):

            @pl.when(at.ep >= 2 - w)
            def _():
                d_copy(w, h).wait_send()

        return carry

    lax.fori_loop(0, heads, finish, 0)


def backward(large, tiles_of, in_place, units, scale):
    d_low, _, queries, keys = large[:4]
    heads, tokens, head = queries.shape
    width = d_low.shape[1]
    ep_count = lax.axis_size("ep")
    depth, rows = ep_count // 2, width // ep_count
    quarter = tokens // lax.axis_size("tp")
    windows = keys.shape[1] // tokens
    columns = 3 * heads * head
    hidden = tiles_of[3].shape[2]
    slot_here, slot_hidden, shared_hidden = units
    f32, bf16 = jnp.float32, jnp.bfloat16
    anywhere = pl.BlockSpec(memory_space=pl.ANY)
    in_vmem = pl.BlockSpec(memory_space=pltpu.VMEM)
    dma = pltpu.SemaphoreType.DMA
    pieces = (ep_count, 3 * shared_hidden, rows)
    gathered = jax.ShapeDtypeStruct((2, 2, quarter, width), bf16)
    routed = jax.ShapeDtypeStruct((slot_here * slot_hidden, width), bf16)

    def vmem(*shape, dtype=bf16):
        return pltpu.VMEM(shape, dtype)

    out, small, block_out, d_rows, pieces, gate, up, down = pl.pallas_call(
        functools.partial(back_kernel, units, scale),
        out_shape=(
            jax.ShapeDtypeStruct((rows, columns), f32),
            jax.ShapeDtypeStruct((rows, 128), f32),
            gathered,
            gathered,
            jax.ShapeDtypeStruct(pieces, bf16),
            routed,
            routed,
            routed,
        ),
        in_specs=[anywhere] * (len(large) + len(tiles_of)) + [in_vmem] * len(in_place),
        out_specs=(in_vmem, in_vmem) + (anywhere,) * 6,
        scratch_shapes=[
            vmem(2, width // 4, columns),
            vmem(width, tokens),
            vmem(windows - 1, heads, tokens, 2 * head),
            vmem(windows - 1, heads, tokens, 2 * head),
            vmem(heads, tokens, 2 * head, dtype=f32),
            vmem(tokens, columns),
            vmem(2, 2, quarter, width),
            vmem(2, quarter, width),
            vmem(quarter, width),
            vmem(quarter, width),
            vmem(depth, rows, columns),
            vmem(depth, rows, columns),
            vmem(depth, rows, columns),
            vmem(depth - 1, rows, columns),
            vmem(depth, 2, rows, 128),
            vmem(depth, rows, 128),
            vmem(depth - 1, rows, 128),
            vmem(2, rows, 128, dtype=f32),
            vmem(2, rows, 128, dtype=f32),
            vmem(*pieces),
            dma((7,)),
            dma((windows - 1, heads)),
            dma((windows - 1, heads)),
            dma((2,)),
            dma((2,)),
            dma((2, depth)),
            dma((2, depth)),
            dma((2, depth)),
            dma((2, depth)),
            dma((2, depth)),
            dma((2, depth)),
            dma((2,)),
            dma((2,)),
            dma((3, ep_count)),
            dma((3, ep_count)),
            dma((2, 3)),
            dma((2, 3)),
            dma((5,)),
            dma((2, 2)),
            dma((2,)),
            dma((2,)),
        ],
        compiler_params=pltpu.CompilerParams(
            collective_id=4, has_side_effects=True, vmem_limit_bytes=62 * 2**20
        ),
        cost_estimate=pl.CostEstimate(
            flops=6 * ep_count * tokens * width * hidden,
            bytes_accessed=8 * ep_count * tokens * width,
            transcendentals=heads * tokens * windows * tokens,
        ),
        name="backward",
    )(*large, *tiles_of, *in_place)
    block_out, d_rows = [array.reshape(4 * quarter, width) for array in (block_out, d_rows)]
    return out, small, block_out, d_rows, pieces, (gate, up, down)


def shared_pieces(weights, ep_count):
    rows, hidden = weights[0].shape
    units = hidden // ep_count
    return jnp.concatenate([weight.T.reshape(ep_count, units, rows) for weight in weights], axis=1)


def shared_whole(pieces, count):
    ep_count, units, columns = pieces.shape
    units = units // count
    pieces = pieces.reshape(ep_count, count, units, columns).astype(jnp.float32)
    return [pieces[:, i].reshape(ep_count * units, columns).T for i in range(count)]


def dense_body(
    tokens,
    lengths,
    routes,
    attn_gain,
    w_query,
    w_key,
    w_value,
    w_out,
    ffn_gain,
    w_router,
    shared_mix,
    shared_gate,
    shared_up,
    shared_down,
    expert_gate,
    expert_up,
    expert_down,
    cotangent,
):
    rows_here, width = tokens.shape
    ep_count = lax.axis_size("ep")
    tp_count = lax.axis_size("tp")
    ep_index = lax.axis_index("ep")
    offset = ep_index * rows_here
    quarter = rows_here // tp_count
    first_row = lax.axis_index("tp") * quarter
    slot_here, slot_hidden = expert_gate.shape[0], expert_gate.shape[1]
    expert_count = w_router.shape[1]
    bf16, f32 = jnp.bfloat16, jnp.float32

    def my_rows(array):
        return lax.dynamic_slice_in_dim(array, first_row, quarter, 0)

    side_columns = jnp.concatenate(
        [attn_gain[:, None], ffn_gain[:, None], shared_mix[:, None], w_router], axis=1
    )
    side_columns = jnp.pad(side_columns, ((0, 0), (0, -side_columns.shape[1] % 128)))
    joined_weights, pieces = gather_over_ep(
        jnp.concatenate([w_query, w_key, w_value, w_out, side_columns], axis=1),
        shared_pieces((shared_gate, shared_up, shared_down), ep_count),
    )
    heads_width = w_query.shape[1]
    side_weight = joined_weights[:, 4 * heads_width :]
    picked = jnp.any(
        my_rows(routes)[:, :, None] == jnp.arange(expert_count, dtype=jnp.int32), axis=1
    )
    picked_lanes = jnp.pad(picked.astype(bf16), ((0, 0), (3, 125 - expert_count)))
    upstream_rows = jnp.concatenate([my_rows(cotangent), picked_lanes], axis=1)
    shared_units = pieces.shape[1] // 3
    routed_units = slot_here * slot_hidden
    heads_here = heads_width // HD
    score_scale = HD ** (-0.5)
    first_norm_scale = side_weight[:, 0].astype(f32)
    second_norm_scale = side_weight[:, 1].astype(f32)
    normed_wide, _ = norm_forward(tokens.astype(f32), first_norm_scale)
    normed_one = normed_wide.astype(bf16)
    query_at = offset + jnp.arange(rows_here, dtype=jnp.int32)
    _, query_pos = sequence_info(lengths, query_at)
    cosine, sine = rope_tables(query_pos, HD)
    tables = (cosine[:, 0], sine[:, 0], (query_at - query_pos)[None, :], query_at[None, :])
    (
        upstream_all,
        keys_win,
        values_win,
        queries,
        log_total,
        attended,
        resid,
        normed_two,
    ) = attention_front(
        normed_one,
        joined_weights,
        upstream_rows,
        tables + (my_rows(tokens), second_norm_scale[None, :]),
        heads_here,
        score_scale,
    )
    (
        normed_all,
        weighted_h,
        d_pair_pre,
        block_rows,
        d_resid_low,
        d_resid,
        grad_gain_two,
        d_side,
    ) = ffn_over_all(
        normed_two,
        upstream_all,
        (expert_gate, expert_up, expert_down),
        pieces,
        joined_weights,
        resid,
        second_norm_scale[None, :],
        (slot_here, slot_hidden, shared_units),
        expert_count,
    )
    grad_side = jnp.dot(normed_two.astype(f32).T, d_side, precision=highest)
    grad_out = jnp.einsum("td,th->dh", d_resid_low, attended, preferred_element_type=f32)
    grad_out = lax.psum_scatter(
        grad_out.astype(bf16), "ep", scatter_dimension=0, tiled=True
    ).astype(f32)
    tile_shape = (ep_count, rows_here, -1)
    tiles_of = tuple(
        array.reshape(tile_shape) for array in (normed_all, d_pair_pre, upstream_all, weighted_h)
    )
    units = (slot_here, slot_hidden, shared_units)
    column = jnp.arange(128, dtype=jnp.int32)
    large = (
        d_resid_low,
        joined_weights,
        queries,
        keys_win,
        values_win,
        normed_one.T,
        block_rows,
    )
    in_place = (
        log_total,
        tables[2],
        tables[3],
        tables[0],
        tables[1],
        my_rows(tokens),
        first_norm_scale[None, :],
        d_resid,
        grad_gain_two[None, :],
        jnp.where(column >= 2, grad_side, 0.0),
    )
    grad_weights, small, block_out, grad_tokens, grad_pieces, grad_experts = backward(
        large, tiles_of, in_place, units, score_scale
    )
    grad_shared = shared_whole(grad_pieces, 3)
    grad_tokens = grad_tokens.astype(f32)
    grad_experts = [grad.astype(f32).reshape(expert_gate.shape) for grad in grad_experts]
    parts = [grad_weights[:, i * heads_width : (i + 1) * heads_width] for i in range(3)]
    return (
        block_out,
        grad_tokens,
        small[:, 0],
        parts[0],
        parts[1],
        parts[2],
        grad_out,
        small[:, 1],
        small[:, 3 : 3 + expert_count],
        small[:, 2],
        grad_shared[0],
        grad_shared[1],
        grad_shared[2],
        grad_experts[0],
        grad_experts[1],
        grad_experts[2],
    )


def chosen_body(*arrays):
    rows_here, top_count = arrays[2].shape
    slot_here, expert_count = arrays[14].shape[0], arrays[9].shape[1]
    capacity = rows_here * top_count * 7 // (5 * expert_count)
    grid_of_two = lax.axis_size("ep") % 2 == 0 and lax.axis_size("tp") == 4
    if grid_of_two and rows_here < 2 * slot_here * capacity:
        return dense_body(*arrays)
    return body(*arrays)


def solution(mesh):
    placed = (
        P("ep", None),
        P(),
        P("ep", None),
        P("ep"),
        P("ep", "tp"),
        P("ep", "tp"),
        P("ep", "tp"),
        P("ep", "tp"),
        P("ep"),
        P("ep", None),
        P("ep"),
        P("ep", "tp"),
        P("ep", "tp"),
        P("ep", "tp"),
        P("ep", "tp", None),
        P("ep", "tp", None),
        P("ep", "tp", None),
        P("ep", None),
    )
    return jax.shard_map(
        chosen_body,
        mesh=mesh,
        in_specs=placed,
        out_specs=(
            P("ep", None),
            P("ep", None),
            P("ep"),
            P("ep", "tp"),
            P("ep", "tp"),
            P("ep", "tp"),
            P("ep", "tp"),
            P("ep"),
            P("ep", None),
            P("ep"),
            P("ep", "tp"),
            P("ep", "tp"),
            P("ep", "tp"),
            P("ep", "tp", None),
            P("ep", "tp", None),
            P("ep", "tp", None),
        ),
        check_vma=False,
    )
```

```python
import functools

import jax
import jax.numpy as jnp
from jax import lax
from jax.experimental import pallas as pl
from jax.experimental.pallas import tpu as pltpu
from jax.sharding import PartitionSpec as P

HD = 128


epsilon = 1e-06
rope_base = 1000000.0
highest = lax.Precision.HIGHEST
MESH = pl.DeviceIdType.MESH


def passed_along(block, axis, distance):
    devices = range(lax.axis_size(axis))
    route = [(i - distance, i) for i in devices if i - distance in devices]
    return lax.ppermute(block, axis, route)


def rope_tables(positions, width):
    steps = jnp.arange(0, width, 2, dtype=jnp.float32) / width
    inverse = rope_base ** (-steps)
    angles = positions.astype(jnp.float32)[:, None] * inverse[None, :]
    angles = jnp.concatenate([angles, angles], axis=-1)
    return (jnp.cos(angles)[:, None, :], jnp.sin(angles)[:, None, :])


def turn_half(values):
    middle = values.shape[-1] // 2
    return jnp.concatenate([-values[..., middle:], values[..., :middle]], axis=-1)


def rotate(values, cosine, sine):
    return values * cosine + turn_half(values) * sine


def unrotate(grads, cosine, sine):
    return grads * cosine - turn_half(grads * sine)


def sequence_info(lengths, indices):
    starts = jnp.cumsum(lengths) - lengths
    inside = starts[None, :] <= indices[:, None]
    segment = jnp.sum(inside.astype(jnp.int32), axis=1) - 1
    first = jnp.max(jnp.where(inside, starts[None, :], -1), axis=1)
    return (segment, indices - first)


def norm_forward(values, gain):
    scale = lax.rsqrt(jnp.mean(values * values, axis=-1, keepdims=True) + epsilon)
    return (values * scale * gain, scale)


def norm_backward(values, scale, gain, grads):
    unit = values * scale
    scaled = grads * gain
    inner = jnp.mean(scaled * unit, axis=-1, keepdims=True)
    return (scale * (scaled - unit * inner), jnp.sum(grads * unit, axis=0))


def deliver(rows):
    arrived_rows = lax.all_to_all(rows, "ep", split_axis=0, concat_axis=0, tiled=True)
    return arrived_rows


def bring_back(parts, target, rows_here, top_count):
    moved = lax.all_to_all(parts, "ep", split_axis=0, concat_axis=0, tiled=True)
    piece = moved.shape[3]
    return moved.reshape(-1, piece)[target].reshape(rows_here, top_count, piece)


def body(
    tokens,
    lengths,
    routes,
    attn_gain,
    w_query,
    w_key,
    w_value,
    w_out,
    ffn_gain,
    w_router,
    shared_mix,
    shared_gate,
    shared_up,
    shared_down,
    expert_gate,
    expert_up,
    expert_down,
    cotangent,
):
    rows_here = tokens.shape[0]
    width = tokens.shape[1]
    ep_count = lax.axis_size("ep")
    offset = lax.axis_index("ep") * rows_here
    slot_here = expert_gate.shape[0]
    top_count = routes.shape[1]
    gathered = (
        lax.all_gather(attn_gain, "ep", axis=0, tiled=True),
        lax.all_gather(w_query, "ep", axis=0, tiled=True),
        lax.all_gather(w_key, "ep", axis=0, tiled=True),
        lax.all_gather(w_value, "ep", axis=0, tiled=True),
        lax.all_gather(w_out, "ep", axis=0, tiled=True),
        lax.all_gather(ffn_gain, "ep", axis=0, tiled=True),
        lax.all_gather(w_router, "ep", axis=0, tiled=True),
        lax.all_gather(shared_mix, "ep", axis=0, tiled=True),
        lax.all_gather(shared_gate, "ep", axis=0, tiled=True),
        lax.all_gather(shared_up, "ep", axis=0, tiled=True),
        lax.all_gather(shared_down, "ep", axis=0, tiled=True),
    )
    (
        gain_first,
        query_weight_matrix,
        key_weight_matrix,
        value_weight_matrix,
        output_weight,
        gain_second,
        router_weight,
        shared_mixer_weight,
        shared_gate_weight,
        shared_up_weight,
        shared_down_weight,
    ) = gathered
    expert_count = router_weight.shape[1]
    capacity = (rows_here * top_count * 7 // (5 * expert_count) + 7) // 8 * 8
    heads_here = query_weight_matrix.shape[1] // HD
    score_scale = HD ** (-0.5)
    first_norm_scale = gain_first.astype(jnp.float32)
    second_norm_scale = gain_second.astype(jnp.float32)
    layer_input = tokens.astype(jnp.float32)
    normed_wide, norm_one = norm_forward(layer_input, first_norm_scale)
    normed_one = normed_wide.astype(jnp.bfloat16)
    query_at = offset + jnp.arange(rows_here, dtype=jnp.int32)
    key_at = offset - 2 * rows_here + jnp.arange(3 * rows_here, dtype=jnp.int32)
    query_seg, query_pos = sequence_info(lengths, query_at)
    key_seg, _ = sequence_info(lengths, key_at)
    cosine, sine = rope_tables(query_pos, HD)
    query_pre = jnp.dot(
        normed_one, query_weight_matrix, preferred_element_type=jnp.float32
    ).reshape(rows_here, heads_here, HD)
    key_pre = jnp.dot(normed_one, key_weight_matrix, preferred_element_type=jnp.float32).reshape(
        rows_here, heads_here, HD
    )
    queries = rotate(query_pre, cosine, sine).astype(jnp.bfloat16)
    keys = rotate(key_pre, cosine, sine).astype(jnp.bfloat16)
    values = (
        jnp.dot(normed_one, value_weight_matrix, preferred_element_type=jnp.float32)
        .astype(jnp.bfloat16)
        .reshape(rows_here, heads_here, HD)
    )
    carried = jnp.stack([keys, values], axis=0)
    window = [carried]
    for hop in range(2):
        carried = passed_along(carried, "ep", 1)
        window = [carried] + window
    joined = jnp.concatenate(window, axis=1)
    keys_win = joined[0]
    values_win = joined[1]
    allowed = (
        (query_seg[:, None] == key_seg[None, :])
        & (key_at[None, :] <= query_at[:, None])
        & (key_at[None, :] >= 0)
    )
    scores = (
        jnp.einsum("qhd,khd->hqk", queries, keys_win, preferred_element_type=jnp.float32)
        * score_scale
    )
    masked = jnp.where(allowed[None], scores, -1e30)
    peak = jnp.max(masked, axis=-1, keepdims=True)
    expo = jnp.exp(masked - peak)
    total = jnp.sum(expo, axis=-1, keepdims=True)
    log_total = peak + jnp.log(total)
    weights = expo / total
    attended = jnp.einsum(
        "hqk,khd->qhd", weights.astype(jnp.bfloat16), values_win, preferred_element_type=jnp.float32
    )
    attended = attended.reshape(rows_here, heads_here * HD).astype(jnp.bfloat16)
    attn_part = jnp.einsum("th,dh->td", attended, output_weight, preferred_element_type=jnp.float32)
    resid = layer_input + lax.psum(attn_part, "tp")
    normed_two_wide, norm_two = norm_forward(resid, second_norm_scale)
    normed_two = normed_two_wide.astype(jnp.bfloat16)
    normed_two_f = normed_two.astype(jnp.float32)
    router_f = router_weight.astype(jnp.float32)
    mix_f = shared_mixer_weight.astype(jnp.float32)
    router = jax.nn.softmax(jnp.dot(normed_two_f, router_f, precision=highest), axis=-1)
    picked = routes[:, :, None] == jnp.arange(expert_count, dtype=jnp.int32)[None, None, :]
    gates = jnp.sum(jnp.where(picked, router[:, None, :], 0.0), axis=-1)
    mixer = jax.nn.sigmoid(jnp.dot(normed_two_f, mix_f, precision=highest))
    shared_g = jnp.dot(normed_two, shared_gate_weight, preferred_element_type=jnp.float32)
    shared_u = jnp.dot(normed_two, shared_up_weight, preferred_element_type=jnp.float32)
    shared_h = (jax.nn.silu(shared_g) * shared_u).astype(jnp.bfloat16)
    shared_part = jnp.einsum(
        "tf,df->td", shared_h, shared_down_weight, preferred_element_type=jnp.float32
    )
    flat = routes.reshape(-1)
    hot = (flat[:, None] == jnp.arange(expert_count, dtype=jnp.int32)[None, :]).astype(jnp.int32)
    rank = jnp.sum(jnp.cumsum(hot, axis=0) * hot, axis=1) - 1
    target = flat * capacity + rank
    slot_total = ep_count * slot_here * capacity
    owner_route = (
        jnp.zeros((slot_total,), jnp.int32)
        .at[target]
        .set(jnp.arange(rows_here * top_count, dtype=jnp.int32))
    )
    filled = jnp.zeros((slot_total,), jnp.bool_).at[target].set(True)
    owner_token = owner_route // top_count
    send_rows = jnp.where(filled[:, None], normed_two[owner_token], jnp.zeros((), jnp.bfloat16))
    arrived_rows = deliver(send_rows.reshape(ep_count, slot_here, capacity, width))
    route_g = jnp.einsum(
        "nscd,sfd->nscf", arrived_rows, expert_gate, preferred_element_type=jnp.float32
    )
    route_u = jnp.einsum(
        "nscd,sfd->nscf", arrived_rows, expert_up, preferred_element_type=jnp.float32
    )
    route_h = (jax.nn.silu(route_g) * route_u).astype(jnp.bfloat16)
    route_part = jnp.einsum(
        "nscf,sfd->nscd", route_h, expert_down, preferred_element_type=jnp.float32
    )
    back_rows = bring_back(route_part, target, rows_here, top_count)
    upstream = cotangent.astype(jnp.float32)
    routed = jnp.sum(back_rows * gates[:, :, None], axis=1)
    ffn_part = mixer[:, None] * shared_part + routed
    route_dot = jnp.sum(back_rows * upstream[:, None, :], axis=-1)
    shared_dot = jnp.sum(shared_part * upstream, axis=-1)
    ffn_total, d_gate, d_mixer = lax.psum((ffn_part, route_dot, shared_dot), "tp")
    block_out = (resid + ffn_total).astype(jnp.bfloat16)
    d_router = jnp.sum(jnp.where(picked, d_gate[:, :, None], 0.0), axis=1)
    d_logits = router * (d_router - jnp.sum(router * d_router, axis=-1, keepdims=True))
    d_mixlogit = d_mixer * mixer * (1.0 - mixer)
    side = jnp.dot(d_logits, router_f.T, precision=highest) + d_mixlogit[:, None] * mix_f[None, :]
    grad_router = jnp.dot(normed_two_f.T, d_logits, precision=highest)
    grad_mix = jnp.dot(d_mixlogit, normed_two_f, precision=highest)
    d_shared = (mixer[:, None] * upstream).astype(jnp.bfloat16)
    d_sh = jnp.dot(d_shared, shared_down_weight, preferred_element_type=jnp.float32)
    sig_shared = jax.nn.sigmoid(shared_g)
    d_sg = (d_sh * shared_u * sig_shared * (1.0 + shared_g * (1.0 - sig_shared))).astype(
        jnp.bfloat16
    )
    d_su = (d_sh * shared_g * sig_shared).astype(jnp.bfloat16)
    d_normed_part = jnp.einsum(
        "tf,df->td", d_sg, shared_gate_weight, preferred_element_type=jnp.float32
    )
    d_normed_part = d_normed_part + jnp.einsum(
        "tf,df->td", d_su, shared_up_weight, preferred_element_type=jnp.float32
    )
    grad_sgate = jnp.einsum("td,tf->df", normed_two, d_sg, preferred_element_type=jnp.float32)
    grad_sup = jnp.einsum("td,tf->df", normed_two, d_su, preferred_element_type=jnp.float32)
    grad_sdown = jnp.einsum("td,tf->df", d_shared, shared_h, preferred_element_type=jnp.float32)
    d_route = (
        (gates[:, :, None] * upstream[:, None, :])
        .astype(jnp.bfloat16)
        .reshape(rows_here * top_count, width)
    )
    send_grads = jnp.where(filled[:, None], d_route[owner_route], jnp.zeros((), jnp.bfloat16))
    received_grads = deliver(send_grads.reshape(ep_count, slot_here, capacity, width))
    d_rh = jnp.einsum(
        "nscd,sfd->nscf", received_grads, expert_down, preferred_element_type=jnp.float32
    )
    sig_route = jax.nn.sigmoid(route_g)
    d_rg = (d_rh * route_u * sig_route * (1.0 + route_g * (1.0 - sig_route))).astype(jnp.bfloat16)
    routed_up_gradient = (d_rh * route_g * sig_route).astype(jnp.bfloat16)
    row_grads = jnp.einsum("nscf,sfd->nscd", d_rg, expert_gate, preferred_element_type=jnp.float32)
    row_grads = row_grads + jnp.einsum(
        "nscf,sfd->nscd", routed_up_gradient, expert_up, preferred_element_type=jnp.float32
    )
    grad_egate = jnp.einsum(
        "qxba,qxbr->xar", d_rg, arrived_rows, preferred_element_type=jnp.float32
    )
    expert_up_gradient = jnp.einsum(
        "qxba,qxbr->xar", routed_up_gradient, arrived_rows, preferred_element_type=jnp.float32
    )
    grad_edown = jnp.einsum(
        "qxba,qxbr->xar", route_h, received_grads, preferred_element_type=jnp.float32
    )
    grads_back = bring_back(row_grads, target, rows_here, top_count)
    d_routed = jnp.sum(grads_back, axis=1)
    d_normed_two = lax.psum(d_normed_part + d_routed, "tp") + side
    d_resid_norm, grad_gain_two = norm_backward(resid, norm_two, second_norm_scale, d_normed_two)
    d_resid = upstream + d_resid_norm
    d_resid_low = d_resid.astype(jnp.bfloat16)
    grad_outw = jnp.einsum("td,th->dh", d_resid_low, attended, preferred_element_type=jnp.float32)
    d_attended = jnp.einsum(
        "td,dh->th", d_resid_low, output_weight, preferred_element_type=jnp.float32
    )
    d_attended = d_attended.astype(jnp.bfloat16).reshape(rows_here, heads_here, HD)
    scores_again = (
        jnp.einsum("qhd,khd->hqk", queries, keys_win, preferred_element_type=jnp.float32)
        * score_scale
    )
    probs = jnp.where(allowed[None], jnp.exp(scores_again - log_total), 0.0)
    d_probs = jnp.einsum("qhd,khd->hqk", d_attended, values_win, preferred_element_type=jnp.float32)
    delta = jnp.sum(probs * d_probs, axis=-1, keepdims=True)
    d_scores = (probs * (d_probs - delta)).astype(jnp.bfloat16)
    d_queries = (
        jnp.einsum("hqk,khd->qhd", d_scores, keys_win, preferred_element_type=jnp.float32)
        * score_scale
    )
    d_keys_win = (
        jnp.einsum("hqk,qhd->khd", d_scores, queries, preferred_element_type=jnp.float32)
        * score_scale
    )
    d_values_win = jnp.einsum(
        "hqk,qhd->khd", probs.astype(jnp.bfloat16), d_attended, preferred_element_type=jnp.float32
    )
    pair_grads = jnp.stack([d_keys_win, d_values_win], axis=0)
    older = pair_grads[:, :rows_here]
    later = [pair_grads[:, rows_here : 2 * rows_here], pair_grads[:, 2 * rows_here :]]
    running = older
    for hop in range(2):
        running = passed_along(running, "ep", -1)
        running = running + later[hop]
    d_query_pre = (
        unrotate(d_queries, cosine, sine).astype(jnp.bfloat16).reshape(rows_here, heads_here * HD)
    )
    d_key_pre = (
        unrotate(running[0], cosine, sine).astype(jnp.bfloat16).reshape(rows_here, heads_here * HD)
    )
    d_values = running[1].astype(jnp.bfloat16).reshape(rows_here, heads_here * HD)
    grad_queryw = jnp.einsum(
        "td,th->dh", normed_one, d_query_pre, preferred_element_type=jnp.float32
    )
    grad_keyw = jnp.einsum("td,th->dh", normed_one, d_key_pre, preferred_element_type=jnp.float32)
    grad_valuew = jnp.einsum("td,th->dh", normed_one, d_values, preferred_element_type=jnp.float32)
    d_normed_one = jnp.einsum(
        "th,dh->td", d_query_pre, query_weight_matrix, preferred_element_type=jnp.float32
    )
    d_normed_one = d_normed_one + jnp.einsum(
        "th,dh->td", d_key_pre, key_weight_matrix, preferred_element_type=jnp.float32
    )
    d_normed_one = d_normed_one + jnp.einsum(
        "th,dh->td", d_values, value_weight_matrix, preferred_element_type=jnp.float32
    )
    d_normed_one = lax.psum(d_normed_one, "tp")
    d_input_norm, grad_gain_one = norm_backward(
        layer_input, norm_one, first_norm_scale, d_normed_one
    )
    grad_tokens = d_resid + d_input_norm
    summed = (
        lax.psum_scatter(grad_gain_one, "ep", scatter_dimension=0, tiled=True),
        lax.psum_scatter(grad_queryw, "ep", scatter_dimension=0, tiled=True),
        lax.psum_scatter(grad_keyw, "ep", scatter_dimension=0, tiled=True),
        lax.psum_scatter(grad_valuew, "ep", scatter_dimension=0, tiled=True),
        lax.psum_scatter(grad_outw, "ep", scatter_dimension=0, tiled=True),
        lax.psum_scatter(grad_gain_two, "ep", scatter_dimension=0, tiled=True),
        lax.psum_scatter(grad_router, "ep", scatter_dimension=0, tiled=True),
        lax.psum_scatter(grad_mix, "ep", scatter_dimension=0, tiled=True),
        lax.psum_scatter(grad_sgate, "ep", scatter_dimension=0, tiled=True),
        lax.psum_scatter(grad_sup, "ep", scatter_dimension=0, tiled=True),
        lax.psum_scatter(grad_sdown, "ep", scatter_dimension=0, tiled=True),
    )
    return (
        block_out,
        grad_tokens,
        summed[0],
        summed[1],
        summed[2],
        summed[3],
        summed[4],
        summed[5],
        summed[6],
        summed[7],
        summed[8],
        summed[9],
        summed[10],
        grad_egate,
        expert_up_gradient,
        grad_edown,
    )


class Place:
    def __init__(self):
        self.ep, self.tp = lax.axis_index("ep"), lax.axis_index("tp")
        self.z, self.y = self.ep // 2, self.ep % 2
        self.x, self.c = self.tp // 2, self.tp % 2
        self.depth = lax.axis_size("ep") // 2
        self.next_core = (self.ep, self.x * 2 + 1 - self.c)
        self.next_x = (self.ep, (1 - self.x) * 2 + self.c)
        self.next_y = (self.z * 2 + 1 - self.y, self.tp)

    def at_z(self, z):
        return (z * 2 + self.y, self.tp)

    def ahead(self, steps):
        return lax.rem(self.z + steps, self.depth)

    def behind(self, steps):
        return lax.rem(self.z + self.depth - steps, self.depth)

    def greet(self):
        barrier = pltpu.get_barrier_semaphore()
        peers = [self.next_core, self.next_x, self.next_y]
        peers += [self.at_z(self.ahead(k)) for k in range(1, self.depth)]
        for peer in peers:
            pl.semaphore_signal(barrier, inc=1, device_id=peer, device_id_type=MESH)
        pl.semaphore_wait(barrier, len(peers))

    def greet_row(self):
        barrier = pltpu.get_barrier_semaphore()
        count = 2 * self.depth
        peers = [(lax.rem(self.ep + k, count), self.tp) for k in range(1, count)]
        peers += [self.next_core, self.next_x]
        for peer in peers:
            pl.semaphore_signal(barrier, inc=1, device_id=peer, device_id_type=MESH)
        pl.semaphore_wait(barrier, len(peers))

    def greet_ep(self):
        barrier = pltpu.get_barrier_semaphore()
        count = 2 * self.depth
        for k in range(1, count):
            peer = (lax.rem(self.ep + k, count), self.tp)
            pl.semaphore_signal(barrier, inc=1, device_id=peer, device_id_type=MESH)
        pl.semaphore_wait(barrier, count - 1)


def remote(src, dst, send, recv, peer):
    return pltpu.make_async_remote_copy(
        src_ref=src, dst_ref=dst, send_sem=send, recv_sem=recv, device_id=peer, device_id_type=MESH
    )


def ffn_kernel(
    units,
    expert_count,
    rows_in,
    upstream_in,
    gate_in,
    up_in,
    down_in,
    pieces_in,
    weights_in,
    resid_in,
    gain_in,
    rows_all,
    weighted_out,
    d_pair_out,
    block_out,
    d_resid_low_out,
    d_resid_out,
    d_gain_out,
    d_side_out,
    d_rows_sum,
    out_sum,
    pair_w,
    down_w,
    side_w,
    rows_tile,
    upstream_tile,
    pair_pre,
    d_hidden,
    factors,
    dots,
    weighted_tile,
    d_pair_tile,
    d_resid_low,
    d_rows_tile,
    out_tile,
    d_rows_core,
    out_core,
    d_rows_held,
    out_held,
    d_rows_hop,
    out_hop,
    d_rows_hop2,
    out_hop2,
    d_rows_z,
    out_z,
    d_rows_to_z,
    out_to_z,
    gathered_send,
    gathered_recv,
    hop_send,
    hop_recv,
    weight_sem,
    end_sem,
    own_sem,
    z_send,
    z_recv,
    plane_send,
    plane_recv,
    load_sem,
    store_sem,
    sum_send,
    sum_recv,
    end_send,
    end_recv,
    core_credit,
    hop_credit,
    hop2_credit,
):
    at = Place()
    depth = at.depth
    quarter, width = rows_in.shape
    half = quarter // 2
    f32, bf16 = jnp.float32, jnp.bfloat16

    def weight_copies():
        hidden = down_w.shape[0]
        slot_here, slot_hidden, shared = units
        routed = slot_here * slot_hidden
        columns = pieces_in.shape[2]
        pairs = [(weights_in.at[:, pl.ds(weights_in.shape[1] - 128, 128)], side_w)]
        kinds = ((gate_in, pair_w, 0), (up_in, pair_w, hidden), (down_in, down_w, 0))
        for kind, (experts, into, first) in enumerate(kinds):
            pairs.append((experts, into.at[pl.ds(first, routed)]))
            here = pl.ds(first + routed, shared)
            for e in range(2 * depth):
                src = pieces_in.at[e, pl.ds(kind * shared, shared)]
                pairs.append((src, into.at[here, pl.ds(e * columns, columns)]))
        return [
            pltpu.make_async_copy(src, dst, weight_sem.at[i]) for i, (src, dst) in enumerate(pairs)
        ]

    def clear_rest():
        hidden = down_w.shape[0]
        used = units[0] * units[1] + units[2]
        for into, first in ((pair_w, 0), (pair_w, hidden), (down_w, 0)):
            if used < hidden:
                into[first + used : first + hidden] = jnp.zeros((hidden - used, width), bf16)

    for copy in weight_copies():
        copy.start()
    clear_rest()

    def block(j, y, x):
        return rows_all.at[at.behind(j), y, x, at.c]

    def plane_copy(j, kind):
        y, other_y = at.y, 1 - at.y
        own, other_x = at.x, 1 - at.x
        if kind == 0:
            src, peer = block(j, y, own), at.next_x
        elif kind == 1:
            src, peer = block(j, y, own), at.next_y
        elif kind == 2:
            src, peer = block(j, y, other_x).at[pl.ds(0, half)], at.next_y
        elif kind == 3:
            src, peer = block(j, other_y, own).at[pl.ds(half, half)], at.next_x
        else:
            src = block(j, other_y if kind >= 6 else y, other_x if kind % 2 else own)
            peer = at.next_core
        return remote(src, src, plane_send.at[j, kind], plane_recv.at[j, kind], peer)

    def z_copy(k):
        return remote(
            rows_in, block(0, at.y, at.x), z_send.at[k - 1], z_recv.at[k - 1], at.at_z(at.ahead(k))
        )

    def z_arrival(k):
        dst = block(k, at.y, at.x)
        return remote(dst, dst, z_send.at[k - 1], z_recv.at[k - 1], at.at_z(at.behind(k)))

    def begin(j):
        for kind in (0, 1, 4):
            plane_copy(j, kind).start()

    def spread(j):
        plane_copy(j, 0).wait_recv()
        plane_copy(j, 2).start()
        plane_copy(j, 5).start()
        plane_copy(j, 1).wait_recv()
        plane_copy(j, 3).start()
        plane_copy(j, 6).start()

    def begin_later(j):
        z_arrival(j).wait_recv()
        begin(j)

    def last_hop(j):
        plane_copy(j, 2).wait_recv()
        plane_copy(j, 3).wait_recv()
        plane_copy(j, 7).start()

    def near_ready(j):
        plane_copy(j, 4).wait_recv()
        plane_copy(j, 5).wait_recv()

    def far_ready(j):
        plane_copy(j, 6).wait_recv()
        plane_copy(j, 7).wait_recv()

    def parity(step):
        return lax.rem(step, 2)

    def slot_of(turn):
        return lax.rem(turn + 1, depth)

    def other_y(step):
        return lax.rem(parity(step) + (step // 2 + 1) // depth, 2)

    def tile_at(step):
        return at.behind(slot_of(step // 2)), lax.rem(at.y + other_y(step), 2)

    def load_rows(step):
        z, y = tile_at(step)
        return pltpu.make_async_copy(rows_all.at[z, y], rows_tile, load_sem.at[0])

    def load_upstream(step):
        z, y = tile_at(step)
        return pltpu.make_async_copy(upstream_in.at[z, y], upstream_tile, load_sem.at[1])

    def stores(step):
        z, y = tile_at(step)
        pairs = ((weighted_tile, weighted_out), (d_pair_tile, d_pair_out))
        return [
            pltpu.make_async_copy(src, dst.at[z, y], store_sem.at[i])
            for i, (src, dst) in enumerate(pairs)
        ]

    tiles, cores = (d_rows_tile, out_tile), (d_rows_core, out_core)
    helds, sums = (d_rows_held, out_held), (d_rows_sum, out_sum)
    hops, hops2, zs = (d_rows_hop, out_hop), (d_rows_hop2, out_hop2), (d_rows_z, out_z)
    to_zs = (d_rows_to_z, out_to_z)

    def sum_copy(a, kind, src, dst, peer):
        return remote(src, dst, sum_send.at[a, kind], sum_recv.at[a, kind], peer)

    def core_sum(a):
        return sum_copy(a, 0, tiles[a].at[:, 1 - at.c], cores[a], at.next_core)

    def row_hop(turn, other):
        y = lax.rem(at.y + other, 2)
        slot = parity(turn)
        src = d_rows_held.at[slot, y, 1 - at.x]
        return remote(
            src, d_rows_hop.at[slot, y], hop_send.at[slot, other], hop_recv.at[slot, other], at.next_x
        )

    def out_hop_sum(turn):
        slot = parity(turn)
        src = out_held.at[slot, 1 - at.y]
        return remote(
            src, out_hop.at[slot], hop_send.at[slot, 2], hop_recv.at[slot, 2], at.next_y
        )

    def hop2_sum(a, turn):
        slot = parity(turn)
        if a == 0:
            src, peer = helds[0].at[slot, 1 - at.y, at.x], at.next_y
        else:
            src, peer = helds[1].at[slot, at.y, 1 - at.x], at.next_x
        return sum_copy(a, 2, src, hops2[a], peer)

    def z_sum(a, turn):
        return remote(
            to_zs[a].at[parity(turn)],
            zs[a].at[turn],
            end_send.at[a, turn],
            end_recv.at[a, turn],
            at.at_z(at.behind(turn + 1)),
        )

    def allow(semaphore, peer):
        pl.semaphore_signal(semaphore, inc=1, device_id=peer, device_id_type=MESH)

    piece = 32

    def add(into, first, second):
        def body(i, carry):
            part = pl.ds(pl.multiple_of(i * piece, piece), piece)
            into[part] = first[part] + second[part]
            return carry

        lax.fori_loop(0, quarter // piece, body, 0)

    def after_core(step):
        turn = step // 2
        other = other_y(step)
        held, y = parity(turn), lax.rem(at.y + other, 2)

        @pl.when((parity(step) == 0) & (turn >= 2))
        def _():
            for a in (0, 1):
                pl.semaphore_wait(hop_credit.at[a], 1)

        for a in (0, 1):
            core_sum(a).wait()
            for x in (1 - at.x, at.x):
                add(helds[a].at[held, y, x], tiles[a].at[x, at.c], cores[a].at[x])
            if a == 0:
                row_hop(turn, other).start()
            else:

                @pl.when(other == 1)
                def _():
                    out_hop_sum(turn).start()

        @pl.when(step + 1 < 2 * depth)
        def _():
            allow(core_credit, at.next_core)

    def after_row_hop(turn, other):
        slot, y = parity(turn), lax.rem(at.y + other, 2)
        row_hop(turn, other).wait()
        into = d_rows_held.at[slot, y, at.x]
        add(into, into, d_rows_hop.at[slot, y])

    def after_out_hop(turn):
        slot = parity(turn)
        out_hop_sum(turn).wait()
        for x in (1 - at.x, at.x):
            into = out_held.at[slot, at.y, x]
            add(into, into, out_hop.at[slot, x])

    def may_hop2(turn, a):
        @pl.when(turn >= 1)
        def _():
            pl.semaphore_wait(hop2_credit.at[a], 1)

    def after_hop(turn):
        after_row_hop(turn, 1)
        may_hop2(turn, 0)
        hop2_sum(0, turn).start()
        after_row_hop(turn, 0)
        after_out_hop(turn)
        may_hop2(turn, 1)
        hop2_sum(1, turn).start()

        @pl.when(turn + 2 < depth)
        def _():
            allow(hop_credit.at[0], at.next_x)
            allow(hop_credit.at[1], at.next_y)

    def after_hop2(turn):
        slot = parity(turn)
        for a in (0, 1):
            hop2_sum(a, turn).wait()

            @pl.when(turn >= 2)
            def _():
                z_sum(a, turn - 2).wait_send()

            add(to_zs[a].at[slot], helds[a].at[slot, at.y, at.x], hops2[a])
            z_sum(a, turn).start()
        allow(hop2_credit.at[0], at.next_y)
        allow(hop2_credit.at[1], at.next_x)

    load_upstream(0).start()
    at.greet()
    z_copy(1).start()
    own_copy = pltpu.make_async_copy(rows_in, block(0, at.y, at.x), own_sem)
    own_copy.start()
    own_copy.wait()
    begin(0)
    begin_later(1)
    for k in range(2, depth):
        z_copy(k).start()
    spread(0)
    spread(1)
    near_ready(1)
    load_rows(0).start()
    for copy in weight_copies():
        copy.wait()

    tile_rows = 4 * quarter
    hidden_total = down_w.shape[0]
    lane = lax.broadcasted_iota(jnp.int32, (tile_rows, 128), 1)
    slot_here, slot_hidden, shared_hidden = units
    routed = slot_here * slot_hidden
    across = (((1,), (1,)), ((), ()))
    few = 16

    def gate_factors(rows, picked):
        logits = jnp.dot(rows, side_w[...], preferred_element_type=f32)
        chooses = (lane >= 3) & (lane < 3 + expert_count)
        peak = jnp.max(jnp.where(chooses, logits, -1e30), axis=1, keepdims=True)
        expo = jnp.where(chooses, jnp.exp(jnp.where(chooses, logits, peak) - peak), 0.0)
        routed_gate = expo / jnp.sum(expo, axis=1, keepdims=True) * picked.astype(f32)
        mix_pre = jnp.sum(jnp.where(lane == 2, logits, 0.0), axis=1, keepdims=True)
        result = jnp.where(lane == slot_here, 1.0 / (1.0 + jnp.exp(-mix_pre)), 0.0)
        for s in range(slot_here):
            chosen = lane == 3 + at.ep * slot_here + s
            gate = jnp.sum(jnp.where(chosen, routed_gate, 0.0), axis=1, keepdims=True)
            result = jnp.where(lane == s, gate, result)
        return result

    few_lane = lax.broadcasted_iota(jnp.int32, (few, 128), 1)
    bounds = [s * slot_hidden for s in range(slot_here)] + [routed, hidden_total]

    def owners(group):
        found = []
        for s in range(slot_here + 1):
            low, high = max(bounds[s] - group * 128, 0), min(bounds[s + 1] - group * 128, 128)
            if low < high:
                found.append((s, low, high))
        return found

    def hidden_rows(i, carry):
        here = pl.ds(pl.multiple_of(i * few, few), few)
        gates = [
            jnp.broadcast_to(factors[here, s : s + 1], (few, 128)) for s in range(slot_here + 1)
        ]
        parts = [None] * (slot_here + 1)
        for group in range(hidden_total // 128):
            units_here = slice(group * 128, (group + 1) * 128)
            units_up = slice(hidden_total + group * 128, hidden_total + (group + 1) * 128)
            gate_pre, up_pre = pair_pre[here, units_here], pair_pre[here, units_up]
            d_h = d_hidden[here, units_here]
            found = owners(group)
            factor = gates[found[0][0]]
            for s, low, _ in found[1:]:
                factor = jnp.where(few_lane >= low, gates[s], factor)
            sig = 0.5 + 0.5 * jnp.tanh(0.5 * gate_pre)
            silu = gate_pre * sig
            hidden = silu * up_pre
            product = hidden * d_h
            gated = factor * d_h
            weighted_tile[here, units_here] = (factor * hidden).astype(bf16)
            slope = sig + silu * (1.0 - sig)
            d_pair_tile[here, units_here] = (gated * up_pre * slope).astype(bf16)
            d_pair_tile[here, units_up] = (gated * silu).astype(bf16)
            for s, low, high in found:
                mine = product
                if high < 128:
                    mine = jnp.where(few_lane < high, mine, 0.0)
                if low > 0:
                    mine = jnp.where(few_lane >= low, mine, 0.0)
                parts[s] = mine if parts[s] is None else parts[s] + mine
        result = jnp.zeros((few, 128), f32)
        for s in range(slot_here + 1):
            dot = jnp.sum(parts[s], axis=1, keepdims=True)
            where = few_lane == (2 if s == slot_here else 3 + at.ep * slot_here + s)
            result = jnp.where(where, dot, result)
        dots[here] = result.astype(bf16)
        return carry

    def first_half(step):
        load_upstream(step).wait()
        upstream = upstream_tile[...].reshape(tile_rows, upstream_tile.shape[-1])
        d_hidden[...] = lax.dot_general(
            upstream[:, :width], down_w[...], across, preferred_element_type=f32
        )
        load_rows(step).wait()
        rows = rows_tile[...].reshape(tile_rows, width)
        factors[...] = gate_factors(rows, upstream[:, width:])
        pair_pre[...] = lax.dot_general(rows, pair_w[...], across, preferred_element_type=f32)

        @pl.when(step + 1 < 2 * depth)
        def _():
            load_upstream(step + 1).start()

        @pl.when(step >= 1)
        def _():
            for copy in stores(step - 1):
                copy.wait()

        lax.fori_loop(0, tile_rows // few, hidden_rows, 0, unroll=2)
        for copy in stores(step):
            copy.start()
        turn = step // 2

        @pl.when(step == 0)
        def _():
            last_hop(0)

        @pl.when((parity(step) == 0) & (turn + 1 < depth))
        def _():
            last_hop(turn + 1)

        @pl.when((step >= 1) & (step + 1 < depth))
        def _():
            spread(step + 1)

        @pl.when(step + 2 < depth)
        def _():
            begin_later(step + 2)

    def second_half(step):
        blocks = (2, 2, quarter)
        some = width // 2
        for n in range(2):
            columns = slice(n * some, (n + 1) * some)
            part = jnp.dot(weighted_tile[...], down_w[:, columns], preferred_element_type=f32)
            out_tile[:, :, :, columns] = part.astype(bf16).reshape(blocks + (some,))
            part = jnp.dot(d_pair_tile[...], pair_w[:, columns], preferred_element_type=f32)
            d_rows_tile[:, :, :, columns] = part.astype(bf16).reshape(blocks + (some,))
        d_rows_tile[:, :, :, width:] = dots[...].reshape(blocks + (128,))

        @pl.when(step >= 1)
        def _():
            pl.semaphore_wait(core_credit, 1)

        for a in (0, 1):
            core_sum(a).start()
        turn = step // 2

        @pl.when((parity(step) == 0) & (turn + 1 < depth))
        def _():
            far_ready(slot_of(turn))

        @pl.when((parity(step) == 1) & (turn + 1 < depth))
        def _():
            near_ready(slot_of(turn + 1))

        @pl.when(step == 2 * depth - 3)
        def _():
            far_ready(slot_of(turn + 1))

        @pl.when(step + 1 < 2 * depth)
        def _():
            load_rows(step + 1).start()

    def step_body(step, carry):
        first_half(step)

        @pl.when(step == 2 * depth - 1)
        def _():
            after_hop(depth - 2)

        @pl.when(step >= 1)
        def _():
            after_core(step - 1)

        second_half(step)
        odd = parity(step) == 1

        @pl.when(odd & (step >= 3) & (step < 2 * depth - 1))
        def _():
            after_hop((step - 3) // 2)

        @pl.when(jnp.logical_not(odd) & (step >= 4))
        def _():
            after_hop2((step - 4) // 2)

        return carry

    lax.fori_loop(0, 2 * depth, step_body, 0)
    last = depth - 1
    own_rows, own_upstream = rows_tile.at[0, 0], upstream_tile.at[0, 0]
    own_loads = [
        pltpu.make_async_copy(rows_in, own_rows, end_sem.at[0]),
        pltpu.make_async_copy(
            upstream_in.at[at.z, at.y, at.x, at.c], own_upstream, end_sem.at[1]
        ),
    ]
    for copy in own_loads:
        copy.start()
    after_hop2(last - 1)
    after_row_hop(last, 1)
    may_hop2(last, 0)
    hop2_sum(0, last).start()
    after_core(2 * depth - 1)
    after_out_hop(last)
    may_hop2(last, 1)
    hop2_sum(1, last).start()
    after_row_hop(last, 0)

    def total_of(a):
        hop2_sum(a, last).wait()
        held = helds[a].at[last % 2, at.y, at.x]
        for turn in range(last):
            z_sum(a, turn).wait_recv()

        def total_body(i, carry):
            part = pl.ds(pl.multiple_of(i * piece, piece), piece)
            total = held[part].astype(f32) + hops2[a][part].astype(f32)
            for k in range(last):
                total = total + zs[a][k, part].astype(f32)
            sums[a][part] = total
            return carry

        lax.fori_loop(0, quarter // piece, total_body, 0)

    total_of(0)
    own_lane = lax.broadcasted_iota(jnp.int32, (quarter, 128), 1)
    chooses = (own_lane >= 3) & (own_lane < 3 + expert_count)
    for copy in own_loads:
        copy.wait()
    rows = own_rows[...]
    logits = jnp.dot(rows, side_w[...], preferred_element_type=f32)
    peak = jnp.max(jnp.where(chooses, logits, -1e30), axis=1, keepdims=True)
    expo = jnp.where(chooses, jnp.exp(jnp.where(chooses, logits, peak) - peak), 0.0)
    router = expo / jnp.sum(expo, axis=1, keepdims=True)
    mixer = 1.0 / (1.0 + jnp.exp(-jnp.where(own_lane == 2, logits, 0.0)))
    gate_dots = d_rows_sum[:, width:]
    d_router = jnp.where(chooses, gate_dots * own_upstream[:, width:].astype(f32), 0.0)
    d_logits = router * (d_router - jnp.sum(router * d_router, axis=1, keepdims=True))
    d_mix = gate_dots * mixer * (1.0 - mixer)
    d_side = jnp.where(own_lane == 2, d_mix, jnp.where(chooses, d_logits, 0.0))
    d_side_out[...] = d_side
    high = d_side.astype(bf16)
    lower = (d_side - high.astype(f32)).astype(bf16)
    for split in (high, lower):
        d_rows_sum[:, :width] += lax.dot_general(
            split, side_w[...], across, preferred_element_type=f32
        )

    def end_body(i, carry):
        part = pl.ds(pl.multiple_of(i * few, few), few)
        resid = resid_in[part]
        scale = lax.rsqrt(jnp.mean(resid * resid, axis=1, keepdims=True) + epsilon)
        unit_rows = resid * scale
        grads = d_rows_sum[part, :width]
        scaled = grads * gain_in[...]
        inner = jnp.mean(scaled * unit_rows, axis=1, keepdims=True)
        d_resid = own_upstream[part, :width].astype(f32) + scale * (scaled - unit_rows * inner)
        d_resid_out[part] = d_resid
        d_resid_low[part] = d_resid.astype(bf16)
        return carry + jnp.sum(grads * unit_rows, axis=0, keepdims=True)

    d_gain_out[...] = lax.fori_loop(0, quarter // few, end_body, jnp.zeros((1, width), f32))

    def gather_copy(kind):
        if kind == 2:
            src = dst = d_resid_low_out.at[1 - at.x, at.c]
        else:
            src, dst = d_resid_low, d_resid_low_out.at[at.x, at.c]
        peer = at.next_x if kind == 0 else at.next_core
        return remote(src, dst, gathered_send.at[kind], gathered_recv.at[kind], peer)

    own_end = pltpu.make_async_copy(d_resid_low, d_resid_low_out.at[at.x, at.c], own_sem)
    own_end.start()
    for kind in (0, 1):
        gather_copy(kind).start()
    total_of(1)
    block_out[...] = (resid_in[...] + out_sum[...]).astype(bf16)
    gather_copy(0).wait_recv()
    gather_copy(2).start()
    own_end.wait()
    gather_copy(0).wait_send()
    gather_copy(1).wait()
    gather_copy(2).wait()
    for copy in stores(2 * depth - 1):
        copy.wait()
    for a in (0, 1):
        for turn in range(max(0, depth - 3), depth - 1):
            z_sum(a, turn).wait_send()
    for k in range(1, depth):
        z_copy(k).wait_send()

    def finish(j, carry):
        for kind in range(8):
            plane_copy(j, kind).wait_send()
        return carry

    lax.fori_loop(0, depth, finish, 0)


def ffn_over_all(rows, upstream_all, experts, pieces, weights, resid, gain, units, expert_count):
    quarter, width = rows.shape
    ep_count, tp_count = lax.axis_size("ep"), lax.axis_size("tp")
    depth = ep_count // 2
    hidden = -(-(units[0] * units[1] + units[2]) // 128) * 128
    bf16, f32 = jnp.bfloat16, jnp.float32
    wide = width + 128
    tile_rows = tp_count * quarter
    tokens = ep_count * tile_rows
    anywhere = pl.BlockSpec(memory_space=pl.ANY)
    in_vmem = pl.BlockSpec(memory_space=pltpu.VMEM)

    def both(*lead):
        return [pltpu.VMEM(lead + (quarter, columns), bf16) for columns in (wide, width)]

    dma = pltpu.SemaphoreType.DMA
    outs = pl.pallas_call(
        functools.partial(ffn_kernel, units, expert_count),
        out_shape=(
            jax.ShapeDtypeStruct((depth, 2, 2, 2, quarter, width), bf16),
            jax.ShapeDtypeStruct((depth, 2, tile_rows, hidden), bf16),
            jax.ShapeDtypeStruct((depth, 2, tile_rows, 2 * hidden), bf16),
            jax.ShapeDtypeStruct((quarter, width), bf16),
            jax.ShapeDtypeStruct((2, 2, quarter, width), bf16),
            jax.ShapeDtypeStruct((quarter, width), f32),
            jax.ShapeDtypeStruct((1, width), f32),
            jax.ShapeDtypeStruct((quarter, 128), f32),
        ),
        in_specs=[anywhere] * 7 + [in_vmem] * 2,
        out_specs=(anywhere,) * 3 + (in_vmem, anywhere) + (in_vmem,) * 3,
        scratch_shapes=[
            pltpu.VMEM((quarter, wide), f32),
            pltpu.VMEM((quarter, width), f32),
            pltpu.VMEM((2 * hidden, width), bf16),
            pltpu.VMEM((hidden, width), bf16),
            pltpu.VMEM((width, 128), bf16),
            pltpu.VMEM((2, 2, quarter, width), bf16),
            pltpu.VMEM((2, 2, quarter, wide), bf16),
            pltpu.VMEM((tile_rows, 2 * hidden), f32),
            pltpu.VMEM((tile_rows, hidden), f32),
            pltpu.VMEM((tile_rows, 128), f32),
            pltpu.VMEM((tile_rows, 128), bf16),
            pltpu.VMEM((tile_rows, hidden), bf16),
            pltpu.VMEM((tile_rows, 2 * hidden), bf16),
            pltpu.VMEM((quarter, width), bf16),
        ]
        + both(2, 2)
        + both(2)
        + both(2, 2, 2)
        + both(2, 2)
        + both()
        + both(depth - 1)
        + both(2)
        + [
            dma((3,)),
            dma((3,)),
            dma((2, 3)),
            dma((2, 3)),
            dma((4 + 6 * depth,)),
            dma((2,)),
            dma,
            dma((depth - 1,)),
            dma((depth - 1,)),
            dma((depth, 8)),
            dma((depth, 8)),
            dma((2,)),
            dma((2,)),
            dma((2, 3)),
            dma((2, 3)),
            dma((2, depth - 1)),
            dma((2, depth - 1)),
            pltpu.SemaphoreType.REGULAR,
            pltpu.SemaphoreType.REGULAR((2,)),
            pltpu.SemaphoreType.REGULAR((2,)),
        ],
        compiler_params=pltpu.CompilerParams(
            collective_id=1, has_side_effects=True, vmem_limit_bytes=62 * 2**20
        ),
        cost_estimate=pl.CostEstimate(
            flops=12 * tokens * width * hidden,
            bytes_accessed=10 * tokens * width,
            transcendentals=tokens * hidden,
        ),
        name="ffn_all_tokens",
    )(
        rows,
        upstream_all.reshape(depth, 2, 2, 2, quarter, wide),
        *[array.reshape(-1, width) for array in experts],
        pieces,
        weights,
        resid,
        gain,
    )
    rows_all, weighted, d_pair, block_out, d_resid_low, d_resid, d_gain, d_side = outs
    return (
        rows_all.reshape(tokens, width),
        weighted.reshape(tokens, hidden),
        d_pair.reshape(tokens, 2 * hidden),
        block_out,
        d_resid_low.reshape(tile_rows, width),
        d_resid,
        d_gain[0],
        d_side,
    )


def swap_copies(at, pieces_in, pieces_out, send_sem, recv_sem, leave):
    count = 2 * at.depth
    copies = []
    for k in range(1, count):
        to, back = lax.rem(at.ep + k, count), lax.rem(at.ep + count - k, count)
        if leave:
            src, dst, peer = pieces_in.at[to], pieces_out.at[at.ep], to
        else:
            src, dst, peer = pieces_in.at[back], pieces_out.at[back], back
        copies.append(remote(src, dst, send_sem.at[k], recv_sem.at[k], (peer, at.tp)))
    return copies


def weights_kernel(
    own_in,
    pieces_in,
    all_out,
    pieces_out,
    own_sem,
    z_send,
    z_recv,
    y_send,
    y_recv,
    swap_send,
    swap_recv,
):
    at = Place()
    depth = at.depth
    half = own_in.shape[0] // 2
    last = depth - 1

    def block(k, y, h):
        return all_out.at[at.z + k, y, pl.ds(h * half, half)]

    def z_copy(k, h, direction):
        if k == 0:
            src = own_in.at[pl.ds(h * half, half)]
        else:
            src = block(k, at.y, h)
        slot = last + k - direction
        return remote(
            src,
            block(k, at.y, h),
            z_send.at[last + k, h, (direction + 1) // 2],
            z_recv.at[slot, h],
            at.at_z(at.z + direction),
        )

    def z_arrival(k, h):
        direction = 1 if k > 0 else -1
        dst = block(k, at.y, h)
        return remote(
            dst, dst, z_send.at[last + k, h, 0], z_recv.at[last + k, h], at.at_z(at.z + direction)
        )

    def y_copy(k, h):
        src = own_in.at[pl.ds(h * half, half)] if k == 0 else block(k, at.y, h)
        return remote(
            src, block(k, at.y, h), y_send.at[last + k, h], y_recv.at[last + k, h], at.next_y
        )

    own_copies = [
        pltpu.make_async_copy(own_in, all_out.at[at.z, at.y], own_sem.at[0]),
        pltpu.make_async_copy(pieces_in.at[at.ep], pieces_out.at[at.ep], own_sem.at[1]),
    ]
    for copy in own_copies:
        copy.start()
    has_up, has_down = at.z + 1 < depth, at.z > 0
    at.greet_ep()

    for h in (0, 1):
        pl.when(has_up)(lambda: z_copy(0, h, 1).start())
        pl.when(has_down)(lambda: z_copy(0, h, -1).start())
        y_copy(0, h).start()
    swap = (at, pieces_in, pieces_out, swap_send, swap_recv)
    for copy in swap_copies(*swap, True):
        copy.start()
    for k in range(1, depth):
        for h in (0, 1):
            for sign in (-1, 1):
                there = at.z + sign * k
                exists = (there >= 0) & (there < depth)
                onward = at.z - sign
                goes_on = exists & (onward >= 0) & (onward < depth)

                @pl.when(exists)
                def _():
                    z_arrival(sign * k, h).wait_recv()

                @pl.when(goes_on)
                def _():
                    z_copy(sign * k, h, -sign).start()

                @pl.when(exists)
                def _():
                    y_copy(sign * k, h).start()

    for copy in own_copies:
        copy.wait()
    for copy in swap_copies(*swap, False):
        copy.wait_recv()
    for copy in swap_copies(*swap, True):
        copy.wait_send()
    for h in (0, 1):
        pl.when(has_up)(lambda: z_copy(0, h, 1).wait_send())
        pl.when(has_down)(lambda: z_copy(0, h, -1).wait_send())
    for k in range(-last, depth):
        there = at.z + k
        exists = (there >= 0) & (there < depth)
        sign = 1 if k > 0 else -1
        onward = at.z - sign
        goes_on = exists & (onward >= 0) & (onward < depth)
        for h in (0, 1):

            @pl.when(exists)
            def _():
                y_copy(k, h).wait()

            if k != 0:

                @pl.when(goes_on)
                def _():
                    z_copy(k, h, -sign).wait_send()


def gather_over_ep(block, pieces):
    rows, columns = block.shape
    depth = lax.axis_size("ep") // 2
    anywhere = pl.BlockSpec(memory_space=pl.ANY)
    slots = 2 * depth - 1
    out, pieces = pl.pallas_call(
        weights_kernel,
        out_shape=(
            jax.ShapeDtypeStruct((depth, 2, rows, columns), block.dtype),
            jax.ShapeDtypeStruct(pieces.shape, pieces.dtype),
        ),
        in_specs=[anywhere] * 2,
        out_specs=(anywhere,) * 2,
        scratch_shapes=[
            pltpu.SemaphoreType.DMA((2,)),
            pltpu.SemaphoreType.DMA((slots, 2, 2)),
            pltpu.SemaphoreType.DMA((slots, 2)),
            pltpu.SemaphoreType.DMA((slots, 2)),
            pltpu.SemaphoreType.DMA((slots, 2)),
            pltpu.SemaphoreType.DMA((2 * depth,)),
            pltpu.SemaphoreType.DMA((2 * depth,)),
        ],
        compiler_params=pltpu.CompilerParams(collective_id=3, has_side_effects=True),
        cost_estimate=pl.CostEstimate(
            flops=0, bytes_accessed=8 * depth * rows * columns, transcendentals=0
        ),
        name="gather_weights",
    )(block, pieces)
    return out.reshape(2 * depth * rows, columns), pieces


class RowGather:
    def __init__(self, at, mine, everywhere, z_send, z_recv, plane_send, plane_recv):
        self.at, self.mine, self.everywhere = at, mine, everywhere
        self.z_sems, self.plane_sems = (z_send, z_recv), (plane_send, plane_recv)
        self.half = mine.shape[0] // 2

    def block(self, j, y, x):
        return self.everywhere.at[self.at.behind(j), y, x, self.at.c]

    def plane_copy(self, j, kind):
        at, half = self.at, self.half
        if kind == 0:
            src, peer = self.block(j, at.y, at.x), at.next_x
        elif kind == 1:
            src, peer = self.block(j, at.y, at.x), at.next_y
        elif kind == 2:
            src, peer = self.block(j, at.y, 1 - at.x).at[pl.ds(0, half)], at.next_y
        elif kind == 3:
            src, peer = self.block(j, 1 - at.y, at.x).at[pl.ds(half, half)], at.next_x
        else:
            y, x = 1 - at.y if kind >= 6 else at.y, 1 - at.x if kind % 2 else at.x
            src, peer = self.block(j, y, x), at.next_core
        send, recv = self.plane_sems
        return remote(src, src, send.at[j, kind], recv.at[j, kind], peer)

    def z_copy(self, k):
        send, recv = self.z_sems
        dst = self.block(0, self.at.y, self.at.x)
        peer = self.at.at_z(self.at.ahead(k))
        return remote(self.mine, dst, send.at[k - 1], recv.at[k - 1], peer)

    def begin(self, j):
        if j > 0:
            send, recv = self.z_sems
            dst = self.block(j, self.at.y, self.at.x)
            peer = self.at.at_z(self.at.behind(j))
            remote(dst, dst, send.at[j - 1], recv.at[j - 1], peer).wait_recv()
        for kind in (0, 1, 4):
            self.plane_copy(j, kind).start()

    def spread(self, j):
        self.plane_copy(j, 0).wait_recv()
        self.plane_copy(j, 2).start()
        self.plane_copy(j, 5).start()
        self.plane_copy(j, 1).wait_recv()
        self.plane_copy(j, 3).start()
        self.plane_copy(j, 6).start()

    def last_hop(self, j):
        self.plane_copy(j, 2).wait_recv()
        self.plane_copy(j, 3).wait_recv()
        self.plane_copy(j, 7).start()

    def finish(self):
        for k in range(1, self.at.depth):
            self.z_copy(k).wait_send()
        for j in range(self.at.depth):
            for kind in range(8):
                if kind >= 4:
                    self.plane_copy(j, kind).wait_recv()
                self.plane_copy(j, kind).wait_send()


def front_kernel(
    score_scale,
    block_in,
    weights_in,
    upstream_in,
    cos_in,
    sin_in,
    query_start,
    query_at,
    tokens_in,
    first_gain,
    gain_in,
    upstream_all,
    turned_out,
    k_out,
    v_out,
    q_out,
    lse_out,
    attended_out,
    resid_out,
    rows_out,
    normed,
    turned,
    qkv_w,
    out_w,
    k_all,
    v_all,
    scores_of,
    part,
    core_got,
    x_got,
    load_sem,
    z_send,
    z_recv,
    plane_send,
    plane_recv,
    kv_send,
    kv_recv,
    tp_send,
    tp_recv,
):
    at = Place()
    depth = at.depth
    count = 2 * depth
    heads, tokens, head = q_out.shape
    heads_width = heads * head
    windows = k_all.shape[1] // tokens
    quarter, width = resid_out.shape
    f32, bf16 = jnp.float32, jnp.bfloat16
    across = (((1,), (1,)), ((), ()))
    gather = RowGather(at, upstream_in, upstream_all, z_send, z_recv, plane_send, plane_recv)
    own = (windows - 1) * tokens

    def kv_copy(kind, w):
        held = (k_all, v_all)[kind]
        return remote(
            held.at[:, pl.ds(own, tokens)],
            held.at[:, pl.ds(w * tokens, tokens)],
            kv_send.at[kind, w],
            kv_recv.at[kind, w],
            (at.ep + (windows - 1 - w), at.tp),
        )

    def kv_arrival(kind, w):
        dst = (k_all, v_all)[kind].at[:, pl.ds(w * tokens, tokens)]
        peer = (at.ep - (windows - 1 - w), at.tp)
        return remote(dst, dst, kv_send.at[kind, w], kv_recv.at[kind, w], peer)

    def core_copy():
        return remote(part.at[:, 1 - at.c], core_got, tp_send.at[0], tp_recv.at[0], at.next_core)

    def x_copy():
        return remote(part.at[1 - at.x, at.c], x_got, tp_send.at[1], tp_recv.at[1], at.next_x)

    pairs = (
        (block_in, normed),
        (weights_in.at[:, pl.ds(0, 3 * heads_width)], qkv_w),
        (weights_in.at[:, pl.ds(3 * heads_width, heads_width)], out_w),
    )
    loads = [pltpu.make_async_copy(src, dst, load_sem.at[i]) for i, (src, dst) in enumerate(pairs)]
    for copy in loads:
        copy.start()
    at.greet_row()
    own_copy = pltpu.make_async_copy(
        upstream_in, gather.block(0, at.y, at.x), load_sem.at[len(pairs)]
    )
    own_copy.start()
    gather.z_copy(1).start()
    own_copy.wait()
    gather.begin(0)
    loads[0].wait()
    few = 16

    def norm_body(i, carry):
        here = pl.ds(pl.multiple_of(i * few, few), few)
        inputs = normed[here].astype(f32)
        scale = lax.rsqrt(jnp.mean(inputs * inputs, axis=1, keepdims=True) + epsilon)
        normed[here] = (inputs * scale * first_gain[...]).astype(bf16)
        return carry

    lax.fori_loop(0, tokens // few, norm_body, 0, unroll=2)
    loads[1].wait()
    lane = lax.broadcasted_iota(jnp.int32, (tokens, head), 1)
    sign = jnp.where(lane < head // 2, -1.0, 1.0)

    def rotated(array):
        return array * cos_in[...] + pltpu.roll(array, head // 2, 1) * sign * sin_in[...]

    keys = jnp.dot(
        normed[...], qkv_w[:, heads_width : 2 * heads_width], preferred_element_type=f32
    )
    for h in range(heads):
        k_all[h, own:] = rotated(keys[:, h * head : (h + 1) * head]).astype(bf16)
    values = jnp.dot(normed[...], qkv_w[:, 2 * heads_width :], preferred_element_type=f32)
    for h in range(heads):
        v_all[h, own:] = values[:, h * head : (h + 1) * head].astype(bf16)
    for w in reversed(range(windows - 1)):

        @pl.when(at.ep + (windows - 1 - w) < count)
        def _():
            for kind in (0, 1):
                kv_copy(kind, w).start()

    for k in range(2, depth):
        gather.z_copy(k).start()
    gather.spread(0)
    queries = jnp.dot(normed[...], qkv_w[:, :heads_width], preferred_element_type=f32)
    for h in range(heads):
        q_out[h] = rotated(queries[:, h * head : (h + 1) * head]).astype(bf16)
    gather.last_hop(0)
    gather.begin(1)
    turned[...] = normed[...].T
    turned_copy = pltpu.make_async_copy(turned, turned_out, load_sem.at[0])
    turned_copy.start()
    gather.spread(1)
    for w in range(windows - 1):

        @pl.when(at.ep < windows - 1 - w)
        def _():
            for held in (k_all, v_all):
                held[:, w * tokens : (w + 1) * tokens] = jnp.zeros((heads, tokens, head), bf16)

        @pl.when(at.ep >= windows - 1 - w)
        def _():
            for kind in (0, 1):
                kv_arrival(kind, w).wait_recv()

    outs = [
        pltpu.make_async_copy(src, dst, load_sem.at[i])
        for i, (src, dst) in ((1, (k_all, k_out)), (3, (v_all, v_out)))
    ]
    for copy in outs:
        copy.start()
    due = [functools.partial(gather.last_hop, 1)]
    for j in range(2, depth):
        due.append(functools.partial(gather.begin, j))
        due.append(functools.partial(gather.spread, j))
        due.append(functools.partial(gather.last_hop, j))

    def head_body(h, carry):
        q = q_out[h]
        peak = jnp.full((1, tokens), -1e30, f32)
        for w in range(windows):
            some = slice(w * tokens, (w + 1) * tokens)
            scores = lax.dot_general(k_all[h, some], q, across, preferred_element_type=f32)
            key_at = lax.broadcasted_iota(jnp.int32, scores.shape, 0)
            key_at = key_at + (at.ep + w + 1 - windows) * tokens
            allowed = (key_at >= query_start[...]) & (key_at <= query_at[...])
            scores = jnp.where(allowed, scores * score_scale, -1e30)
            scores_of[w] = scores
            peak = jnp.maximum(peak, jnp.max(scores, axis=0, keepdims=True))
        total = jnp.zeros((1, tokens), f32)
        for w in range(windows):
            expo = jnp.exp(scores_of[w] - peak)
            scores_of[w] = expo
            total = total + jnp.sum(expo, axis=0, keepdims=True)
        lse_out[h] = peak + jnp.log(total)
        each = 1.0 / total
        attended = jnp.zeros((head, tokens), f32)
        for w in range(windows):
            some = slice(w * tokens, (w + 1) * tokens)
            probs = (scores_of[w] * each).astype(bf16)
            attended = attended + jnp.dot(
                v_all[h, some].T, probs, preferred_element_type=f32
            )
        here = pl.ds(pl.multiple_of(h * head, head), head)
        attended_out[:, here] = attended.T.astype(bf16)
        for i in range(heads):

            @pl.when(h == i)
            def _():
                for action in due[i : i + 1]:
                    action()

        return carry

    lax.fori_loop(0, heads, head_body, 0)
    loads[2].wait()
    strips = 4
    strip = width // strips
    for n in range(strips):
        some = slice(n * strip, (n + 1) * strip)
        product = lax.dot_general(
            attended_out[...], out_w[some], across, preferred_element_type=f32
        )
        part[:, :, :, some] = product.astype(bf16).reshape(2, 2, quarter, strip)
    core_copy().start()
    rest = due[heads:]
    for action in rest[:2]:
        action()
    core_copy().wait()
    for x in (0, 1):
        part[x, at.c] = part[x, at.c] + core_got[x]
    x_copy().start()
    for action in rest[2:]:
        action()
    x_copy().wait()

    def end_body(i, carry):
        here = pl.ds(pl.multiple_of(i * few, few), few)
        total = part[at.x, at.c, here].astype(f32) + x_got[here].astype(f32)
        resid = tokens_in[here].astype(f32) + total
        scale = lax.rsqrt(jnp.mean(resid * resid, axis=1, keepdims=True) + epsilon)
        resid_out[here] = resid
        rows_out[here] = (resid * scale * gain_in[...]).astype(bf16)
        return carry

    lax.fori_loop(0, quarter // few, end_body, 0)
    turned_copy.wait()
    for copy in outs:
        copy.wait()
    for w in range(windows - 1):

        @pl.when(at.ep + (windows - 1 - w) < count)
        def _():
            for kind in (0, 1):
                kv_copy(kind, w).wait_send()

    gather.finish()


def attention_front(block, weights, upstream, in_place, heads, scale):
    tokens, width = block.shape
    quarter, wide = upstream.shape
    depth = lax.axis_size("ep") // 2
    head, windows = HD, 3
    f32, bf16 = jnp.float32, jnp.bfloat16
    anywhere = pl.BlockSpec(memory_space=pl.ANY)
    in_vmem = pl.BlockSpec(memory_space=pltpu.VMEM)
    dma = pltpu.SemaphoreType.DMA
    shape = jax.ShapeDtypeStruct
    window = (heads, windows * tokens, head)
    outs = pl.pallas_call(
        functools.partial(front_kernel, scale),
        out_shape=(
            shape((depth, 2, 2, 2, quarter, wide), bf16),
            shape((width, tokens), bf16),
            shape(window, bf16),
            shape(window, bf16),
            shape((heads, tokens, head), bf16),
            shape((heads, 1, tokens), f32),
            shape((tokens, heads * head), bf16),
            shape((quarter, width), f32),
            shape((quarter, width), bf16),
        ),
        in_specs=[anywhere] * 3 + [in_vmem] * len(in_place),
        out_specs=(anywhere,) * 4 + (in_vmem,) * 5,
        scratch_shapes=[
            pltpu.VMEM((tokens, width), bf16),
            pltpu.VMEM((width, tokens), bf16),
            pltpu.VMEM((width, 3 * heads * head), bf16),
            pltpu.VMEM((width, heads * head), bf16),
            pltpu.VMEM(window, bf16),
            pltpu.VMEM(window, bf16),
            pltpu.VMEM((windows, tokens, tokens), f32),
            pltpu.VMEM((2, 2, quarter, width), bf16),
            pltpu.VMEM((2, quarter, width), bf16),
            pltpu.VMEM((quarter, width), bf16),
            dma((4,)),
            dma((depth - 1,)),
            dma((depth - 1,)),
            dma((depth, 8)),
            dma((depth, 8)),
            dma((2, windows - 1)),
            dma((2, windows - 1)),
            dma((2,)),
            dma((2,)),
        ],
        compiler_params=pltpu.CompilerParams(
            collective_id=5, has_side_effects=True, vmem_limit_bytes=50 * 2**20
        ),
        cost_estimate=pl.CostEstimate(
            flops=8 * tokens * width * heads * head,
            bytes_accessed=2 * 8 * depth * quarter * wide,
            transcendentals=heads * tokens * windows * tokens,
        ),
        name="attention_front",
    )(block, weights, upstream, *in_place)
    return (outs[0].reshape(8 * depth * quarter, wide),) + tuple(outs[1:])


def back_kernel(
    units,
    score_scale,
    d_low_in,
    weights_in,
    q_in,
    k_in,
    v_in,
    turned_in,
    block_in,
    rows_in,
    d_pair_in,
    upstream_in,
    weighted_in,
    lse_in,
    query_start,
    query_at,
    cos_in,
    sin_in,
    own_rows_in,
    gain_in,
    d_resid_in,
    gain_two_in,
    side_in,
    out,
    small_out,
    block_out,
    d_rows_out,
    pieces_got,
    gate_out,
    up_out,
    down_out,
    qkv_w,
    turned,
    d_out,
    d_got,
    d_own,
    d_proj,
    part,
    core_got,
    x_got,
    d_rows,
    own,
    y_out,
    hop,
    from_z,
    small_own,
    small_hop,
    small_z,
    small,
    small_got,
    pieces,
    load_sem,
    d_send,
    d_recv,
    tp_send,
    tp_recv,
    y_send,
    y_recv,
    z_send,
    z_recv,
    little_send,
    little_recv,
    small_send,
    small_recv,
    swap_send,
    swap_recv,
    rows_send,
    rows_recv,
    own_sem,
    tile_sem,
    store_sem,
    strip_sem,
):
    at = Place()
    depth = at.depth
    count = 2 * depth
    heads, tokens, head = q_in.shape
    heads_width = heads * head
    windows = k_in.shape[1] // tokens
    quarter, width = d_rows.shape
    rows = out.shape[0]
    f32, bf16 = jnp.float32, jnp.bfloat16
    across = (((1,), (1,)), ((), ()))
    slot_here, slot_hidden, shared_hidden = units
    routed = slot_here * slot_hidden
    hidden = weighted_in.shape[2]
    few = 16

    def d_copy(w, h):
        peer = (at.ep - (2 - w), at.tp)
        return remote(d_out.at[w, h], d_got.at[w, h], d_send.at[w, h], d_recv.at[w, h], peer)

    def d_arrival(w, h):
        peer = (at.ep + (2 - w), at.tp)
        dst = d_got.at[w, h]
        return remote(dst, dst, d_send.at[w, h], d_recv.at[w, h], peer)

    def core_copy():
        return remote(part.at[:, 1 - at.c], core_got, tp_send.at[0], tp_recv.at[0], at.next_core)

    def x_copy():
        return remote(part.at[1 - at.x, at.c], x_got, tp_send.at[1], tp_recv.at[1], at.next_x)

    cuts = (pl.ds(0, heads_width), pl.ds(heads_width, 2 * heads_width))

    def y_copy(q, j):
        return remote(
            y_out.at[j, :, cuts[q]], hop.at[j, :, cuts[q]], y_send.at[q, j], y_recv.at[q, j], at.next_y
        )

    def z_copy(q, j):
        return remote(
            own.at[j, :, cuts[q]],
            from_z.at[j - 1, :, cuts[q]],
            z_send.at[q, j],
            z_recv.at[q, j],
            at.at_z(at.ahead(j)),
        )

    def little_y(j):
        return remote(
            small_own.at[at.ahead(j), 1 - at.y],
            small_hop.at[j],
            little_send.at[0, j],
            little_recv.at[0, j],
            at.next_y,
        )

    def little_z(j):
        return remote(
            small_own.at[at.ahead(j), at.y],
            small_z.at[j - 1],
            little_send.at[1, j],
            little_recv.at[1, j],
            at.at_z(at.ahead(j)),
        )

    def small_copy(kind):
        peer = at.next_core if kind == 0 else at.next_x
        return remote(
            small.at[kind], small_got.at[kind], small_send.at[kind], small_recv.at[kind], peer
        )

    ends = ((block_in, block_out), (d_rows, d_rows_out))

    def rows_copy(a, kind):
        mine, gathered = ends[a]
        if kind == 2:
            src = dst = gathered.at[1 - at.x, at.c]
        else:
            src, dst = mine, gathered.at[at.x, at.c]
        peer = at.next_x if kind == 0 else at.next_core
        return remote(src, dst, rows_send.at[a, kind], rows_recv.at[a, kind], peer)

    def rows_own(a):
        mine, gathered = ends[a]
        return pltpu.make_async_copy(mine, gathered.at[at.x, at.c], own_sem.at[a])

    def rows_begin(a):
        for kind in (0, 1):
            rows_copy(a, kind).start()
        rows_own(a).start()

    def rows_pass_on(a):
        rows_copy(a, 0).wait_recv()
        rows_copy(a, 2).start()

    def rows_end(a):
        rows_own(a).wait()
        rows_copy(a, 0).wait_send()
        rows_copy(a, 1).wait()
        rows_copy(a, 2).wait()

    def swap_copies(p, leave):
        some = pl.ds(p * shared_hidden, shared_hidden)
        copies = []
        for k in range(1, count):
            to, back = lax.rem(at.ep + k, count), lax.rem(at.ep + count - k, count)
            if leave:
                src, dst, peer = pieces.at[to, some], pieces_got.at[at.ep, some], to
            else:
                src, dst, peer = pieces.at[back, some], pieces_got.at[back, some], back
            copies.append(remote(src, dst, swap_send.at[p, k], swap_recv.at[p, k], (peer, at.tp)))
        return copies

    def swap_own(p):
        some = pl.ds(p * shared_hidden, shared_hidden)
        return pltpu.make_async_copy(
            pieces.at[at.ep, some], pieces_got.at[at.ep, some], own_sem.at[2 + p]
        )

    strips = 4
    strip = width // strips

    def load_strip(n):
        src = weights_in.at[pl.ds(n * strip, strip), pl.ds(0, 3 * heads_width)]
        return pltpu.make_async_copy(src, qkv_w.at[n % 2], strip_sem.at[n % 2])

    late_load = pltpu.make_async_copy(turned_in, turned, load_sem.at[1])
    lane = lax.broadcasted_iota(jnp.int32, (tokens, head), 1)
    sign = jnp.where(lane < head // 2, -1.0, 1.0)

    def unrotated(grads):
        turned_part = pltpu.roll(grads * sin_in[...], head // 2, 1) * sign
        return grads * cos_in[...] - turned_part

    def attention(d_low, out_w, q_all, k_all, v_all, d_att, probs, d_probs):
        pairs = (
            (d_low_in, d_low),
            (weights_in.at[:, pl.ds(3 * heads_width, heads_width)], out_w),
            (q_in, q_all),
            (k_in, k_all),
            (v_in, v_all),
        )
        copies = [
            pltpu.make_async_copy(src, dst, load_sem.at[2 + i])
            for i, (src, dst) in enumerate(pairs)
        ]
        for copy in copies + [late_load, load_strip(0), load_strip(1)]:
            copy.start()
        at.greet_row()
        rows_begin(0)
        copies[0].wait()
        copies[1].wait()
        d_attended = jnp.dot(d_low[...], out_w[...], preferred_element_type=f32).astype(bf16)
        for h in range(heads):
            d_att[h] = d_attended[:, h * head : (h + 1) * head]
        for copy in copies[2:]:
            copy.wait()

        def head_body(h, carry):
            queries, d_a = q_all[h], d_att[h]
            delta = jnp.zeros((1, tokens), f32)
            for w in range(windows):
                some = slice(w * tokens, (w + 1) * tokens)
                scores = lax.dot_general(
                    k_all[h, some], queries, across, preferred_element_type=f32
                )
                key_at = lax.broadcasted_iota(jnp.int32, scores.shape, 0)
                key_at = key_at + (at.ep + w + 1 - windows) * tokens
                allowed = (key_at >= query_start[...]) & (key_at <= query_at[...])
                p = jnp.where(allowed, jnp.exp(scores * score_scale - lse_in[h]), 0.0)
                d_p = lax.dot_general(v_all[h, some], d_a, across, preferred_element_type=f32)
                probs[w] = p
                d_probs[w] = d_p
                delta = delta + jnp.sum(p * d_p, axis=0, keepdims=True)
            d_queries = jnp.zeros((head, tokens), f32)
            for w in range(windows):
                some = slice(w * tokens, (w + 1) * tokens)
                p = probs[w]
                d_scores = (p * (d_probs[w] - delta)).astype(bf16)
                d_keys = jnp.dot(d_scores, queries, preferred_element_type=f32) * score_scale
                d_values = jnp.dot(p.astype(bf16), d_a, preferred_element_type=f32)
                if w < windows - 1:
                    d_out[w, h, :, :head] = d_keys.astype(bf16)
                    d_out[w, h, :, head:] = d_values.astype(bf16)

                    @pl.when(at.ep >= 2 - w)
                    def _():
                        d_copy(w, h).start()

                else:
                    d_own[h, :, :head] = d_keys
                    d_own[h, :, head:] = d_values
                d_queries = d_queries + jnp.dot(
                    k_all[h, some].T, d_scores, preferred_element_type=f32
                )
            here = pl.ds(pl.multiple_of(h * head, head), head)
            d_proj[:, here] = unrotated((d_queries * score_scale).T).astype(bf16)
            return carry

        lax.fori_loop(0, heads, head_body, 0)

    pl.run_scoped(
        attention,
        pltpu.VMEM((tokens, width), bf16),
        pltpu.VMEM((width, heads_width), bf16),
        pltpu.VMEM((heads, tokens, head), bf16),
        pltpu.VMEM((heads, windows * tokens, head), bf16),
        pltpu.VMEM((heads, windows * tokens, head), bf16),
        pltpu.VMEM((heads, tokens, head), bf16),
        pltpu.VMEM((windows, tokens, tokens), f32),
        pltpu.VMEM((windows, tokens, tokens), f32),
    )
    order = [j for j in range(1, depth)] + [0]

    def own_body(h, carry):
        for w in range(windows - 1):

            @pl.when(at.ep + (2 - w) < count)
            def _():
                d_arrival(w, h).wait_recv()
                d_own[h] += d_got[w, h].astype(f32)

        k_here = pl.ds(pl.multiple_of(heads_width + h * head, head), head)
        v_here = pl.ds(pl.multiple_of(2 * heads_width + h * head, head), head)
        d_proj[:, k_here] = unrotated(d_own[h, :, :head]).astype(bf16)
        d_proj[:, v_here] = d_own[h, :, head:].astype(bf16)
        return carry

    def weight_rows(into, q, z, y):
        here = pl.ds(pl.multiple_of((z * 2 + y) * rows, rows), rows)
        product = jnp.dot(turned[here], d_proj[:, cuts[q]], preferred_element_type=f32)
        into[:, cuts[q]] = product.astype(bf16)

    def begin_sums(q):
        for j in order:
            weight_rows(y_out.at[j], q, at.ahead(j), 1 - at.y)
            y_copy(q, j).start()

    def own_sums(q):
        for j in order:
            weight_rows(own.at[j], q, at.ahead(j), at.y)

    def projections():
        lax.fori_loop(0, heads, own_body, 0)
        for n in range(strips):
            some = slice(n * strip, (n + 1) * strip)
            load_strip(n).wait()
            product = lax.dot_general(
                d_proj[...], qkv_w[n % 2], across, preferred_element_type=f32
            )
            part[:, :, :, some] = product.astype(bf16).reshape(2, 2, quarter, strip)
            if n + 2 < strips:
                load_strip(n + 2).start()
        core_copy().start()
        begin_sums(1)
        core_copy().wait()
        for x in (0, 1):
            part[x, at.c] = part[x, at.c] + core_got[x]
        x_copy().start()
        own_sums(1)
        x_copy().wait()

        def end_body(i, carry):
            here = pl.ds(pl.multiple_of(i * few, few), few)
            grads = part[at.x, at.c, here].astype(f32) + x_got[here].astype(f32)
            inputs = own_rows_in[here].astype(f32)
            scale = lax.rsqrt(jnp.mean(inputs * inputs, axis=1, keepdims=True) + epsilon)
            unit_rows = inputs * scale
            scaled = grads * gain_in[...]
            inner = jnp.mean(scaled * unit_rows, axis=1, keepdims=True)
            total = d_resid_in[here] + scale * (scaled - unit_rows * inner)
            d_rows[here] = total.astype(bf16)
            return carry + jnp.sum(grads * unit_rows, axis=0, keepdims=True)

        d_gain = lax.fori_loop(0, quarter // few, end_body, jnp.zeros((1, width), f32))
        rows_begin(1)
        line = lax.broadcasted_iota(jnp.int32, (128, rows), 0)
        for e in range(count):
            some = slice(e * rows, (e + 1) * rows)
            gains = jnp.where(line == 0, d_gain[:, some], 0.0)
            gains = jnp.where(line == 1, gain_two_in[:, some], gains)
            small_own[e // 2, e % 2] = (gains.T + side_in[some]).astype(bf16)
        for j in order:
            little_y(j).start()

    def after_y(q, j):
        y_copy(q, j).wait_recv()

        def body(i, carry):
            some = pl.ds(pl.multiple_of(i * few, few), few)
            own[j, some, cuts[q]] = own[j, some, cuts[q]] + hop[j, some, cuts[q]]
            return carry

        lax.fori_loop(0, rows // few, body, 0)
        if j > 0:
            z_copy(q, j).start()

    def after_little():
        for j in order:
            little_y(j).wait_recv()
            here = small_own.at[at.ahead(j), at.y]
            here[...] = here[...] + small_hop[j]
            if j > 0:
                little_z(j).start()

    hooks = {(0, 0): [functools.partial(rows_pass_on, 0)]}
    for i, j in enumerate(order):
        hooks.setdefault((0, min(2 * i + 1, count - 1)), []).append(functools.partial(after_y, 0, j))
    hooks[(1, 2)] = [functools.partial(rows_pass_on, 1)]
    hooks[(1, 3)] = [after_little]
    last_hooks = []
    for i, j in enumerate(order):
        when = count + 5 + 5 * i
        due = functools.partial(after_y, 1, j)
        if when < 3 * count:
            hooks.setdefault((when // count, when % count), []).append(due)
        else:
            last_hooks.append(due)

    def weight_gradients(turned_left, left_tile, right_part, staging):
        lefts = (
            lambda tile: d_pair_in.at[tile, :, pl.ds(0, hidden)],
            lambda tile: d_pair_in.at[tile, :, pl.ds(hidden, hidden)],
            lambda tile: weighted_in.at[tile],
        )
        rights = (rows_in, rows_in, upstream_in)
        results = (gate_out, up_out, down_out)
        columns = width // count

        def load_left(p, tile):
            slot = lax.rem(tile, 2)
            return pltpu.make_async_copy(
                lefts[p](tile), left_tile.at[slot], tile_sem.at[0, slot]
            )

        def load_right(p, n):
            slot = lax.rem(n, 2)
            here = pl.ds(pl.multiple_of(n * columns, columns), columns)
            return pltpu.make_async_copy(
                rights[p].at[:, :, here], right_part.at[slot], tile_sem.at[1, slot]
            )

        def store(p, n):
            slot = lax.rem(n, 2)
            here = pl.ds(pl.multiple_of(n * columns, columns), columns)
            return pltpu.make_async_copy(
                staging.at[slot], results[p].at[:, here], store_sem.at[slot]
            )

        def turn_left(p, tile):
            load_left(p, tile).wait()

            @pl.when(tile + 1 < count)
            def _():
                load_left(p, tile + 1).start()

            here = pl.ds(pl.multiple_of(tile * tokens, tokens), tokens)
            turned_left[:, here] = left_tile[lax.rem(tile, 2)].T

        def run_pass(p):
            def part_body(n, carry):
                slot = lax.rem(n, 2)
                load_right(p, n).wait()

                @pl.when(n + 1 < count)
                def _():
                    load_right(p, n + 1).start()

                if p < 2:

                    @pl.when(n + 1 == count)
                    def _():
                        load_right(p + 1, 0).start()

                @pl.when(n >= 2)
                def _():
                    store(p, n - 2).wait()

                product = jnp.dot(
                    turned_left[...],
                    right_part[slot].reshape(count * tokens, columns),
                    preferred_element_type=f32,
                )
                staging[slot] = product[:routed].astype(bf16)
                pieces[n, p * shared_hidden : (p + 1) * shared_hidden] = product[
                    routed : routed + shared_hidden
                ].astype(bf16)
                store(p, n).start()
                for (hook_pass, hook_part), actions in hooks.items():
                    if hook_pass == p:

                        @pl.when(n == hook_part)
                        def _():
                            for action in actions:
                                action()

                return carry

            def turn_body(tile, carry):
                turn_left(p, tile)
                return carry

            lax.fori_loop(0, count, turn_body, 0)
            if p < 2:
                load_left(p + 1, 0).start()
            lax.fori_loop(0, count, part_body, 0)
            for n in (count - 2, count - 1):
                store(p, n).wait()
            swap_own(p).start()
            for copy in swap_copies(p, True):
                copy.start()

        load_left(0, 0).start()
        load_right(0, 0).start()
        late_load.wait()
        begin_sums(0)
        own_sums(0)

        run_pass(0)
        projections()
        run_pass(1)
        run_pass(2)
        for action in last_hooks:
            action()

    pl.run_scoped(
        weight_gradients,
        pltpu.VMEM((hidden, count * tokens), bf16),
        pltpu.VMEM((2, tokens, hidden), bf16),
        pltpu.VMEM((2, count, tokens, width // count), bf16),
        pltpu.VMEM((2, routed, width // count), bf16),
    )
    total = small_own[at.z, at.y].astype(f32)
    for j in range(1, depth):
        little_z(j).wait_recv()
        total = total + small_z[j - 1].astype(f32)
    for kind in (0, 1):
        small[kind] = total
        small_copy(kind).start()
        small_copy(kind).wait()
        total = small[kind] + small_got[kind]
    small_out[...] = total
    for j in range(1, depth):
        for q in (0, 1):
            z_copy(q, j).wait_recv()

    def total_body(i, carry):
        some = pl.ds(pl.multiple_of(i * few, few), few)
        result = own[0, some].astype(f32)
        for k in range(depth - 1):
            result = result + from_z[k, some].astype(f32)
        out[some] = result
        return carry

    lax.fori_loop(0, rows // few, total_body, 0)
    for j in range(depth):
        little_y(j).wait_send()
        if j > 0:
            little_z(j).wait_send()
        for q in (0, 1):
            y_copy(q, j).wait_send()
            if j > 0:
                z_copy(q, j).wait_send()
    for a in (0, 1):
        rows_end(a)
    for p in range(3):
        swap_own(p).wait()
        for copy in swap_copies(p, False):
            copy.wait_recv()
        for copy in swap_copies(p, True):
            copy.wait_send()

    def finish(h, carry):
        for w in range(windows - 1):

            @pl.when(at.ep >= 2 - w)
            def _():
                d_copy(w, h).wait_send()

        return carry

    lax.fori_loop(0, heads, finish, 0)


def backward(large, tiles_of, in_place, units, scale):
    d_low, _, queries, keys = large[:4]
    heads, tokens, head = queries.shape
    width = d_low.shape[1]
    ep_count = lax.axis_size("ep")
    depth, rows = ep_count // 2, width // ep_count
    quarter = tokens // lax.axis_size("tp")
    windows = keys.shape[1] // tokens
    columns = 3 * heads * head
    hidden = tiles_of[3].shape[2]
    slot_here, slot_hidden, shared_hidden = units
    f32, bf16 = jnp.float32, jnp.bfloat16
    anywhere = pl.BlockSpec(memory_space=pl.ANY)
    in_vmem = pl.BlockSpec(memory_space=pltpu.VMEM)
    dma = pltpu.SemaphoreType.DMA
    pieces = (ep_count, 3 * shared_hidden, rows)
    gathered = jax.ShapeDtypeStruct((2, 2, quarter, width), bf16)
    routed = jax.ShapeDtypeStruct((slot_here * slot_hidden, width), bf16)

    def vmem(*shape, dtype=bf16):
        return pltpu.VMEM(shape, dtype)

    out, small, block_out, d_rows, pieces, gate, up, down = pl.pallas_call(
        functools.partial(back_kernel, units, scale),
        out_shape=(
            jax.ShapeDtypeStruct((rows, columns), f32),
            jax.ShapeDtypeStruct((rows, 128), f32),
            gathered,
            gathered,
            jax.ShapeDtypeStruct(pieces, bf16),
            routed,
            routed,
            routed,
        ),
        in_specs=[anywhere] * (len(large) + len(tiles_of)) + [in_vmem] * len(in_place),
        out_specs=(in_vmem, in_vmem) + (anywhere,) * 6,
        scratch_shapes=[
            vmem(2, width // 4, columns),
            vmem(width, tokens),
            vmem(windows - 1, heads, tokens, 2 * head),
            vmem(windows - 1, heads, tokens, 2 * head),
            vmem(heads, tokens, 2 * head, dtype=f32),
            vmem(tokens, columns),
            vmem(2, 2, quarter, width),
            vmem(2, quarter, width),
            vmem(quarter, width),
            vmem(quarter, width),
            vmem(depth, rows, columns),
            vmem(depth, rows, columns),
            vmem(depth, rows, columns),
            vmem(depth - 1, rows, columns),
            vmem(depth, 2, rows, 128),
            vmem(depth, rows, 128),
            vmem(depth - 1, rows, 128),
            vmem(2, rows, 128, dtype=f32),
            vmem(2, rows, 128, dtype=f32),
            vmem(*pieces),
            dma((7,)),
            dma((windows - 1, heads)),
            dma((windows - 1, heads)),
            dma((2,)),
            dma((2,)),
            dma((2, depth)),
            dma((2, depth)),
            dma((2, depth)),
            dma((2, depth)),
            dma((2, depth)),
            dma((2, depth)),
            dma((2,)),
            dma((2,)),
            dma((3, ep_count)),
            dma((3, ep_count)),
            dma((2, 3)),
            dma((2, 3)),
            dma((5,)),
            dma((2, 2)),
            dma((2,)),
            dma((2,)),
        ],
        compiler_params=pltpu.CompilerParams(
            collective_id=4, has_side_effects=True, vmem_limit_bytes=62 * 2**20
        ),
        cost_estimate=pl.CostEstimate(
            flops=6 * ep_count * tokens * width * hidden,
            bytes_accessed=8 * ep_count * tokens * width,
            transcendentals=heads * tokens * windows * tokens,
        ),
        name="backward",
    )(*large, *tiles_of, *in_place)
    block_out, d_rows = [array.reshape(4 * quarter, width) for array in (block_out, d_rows)]
    return out, small, block_out, d_rows, pieces, (gate, up, down)


def shared_pieces(weights, ep_count):
    rows, hidden = weights[0].shape
    units = hidden // ep_count
    return jnp.concatenate([weight.T.reshape(ep_count, units, rows) for weight in weights], axis=1)


def shared_whole(pieces, count):
    ep_count, units, columns = pieces.shape
    units = units // count
    pieces = pieces.reshape(ep_count, count, units, columns).astype(jnp.float32)
    return [pieces[:, i].reshape(ep_count * units, columns).T for i in range(count)]


def dense_body(
    tokens,
    lengths,
    routes,
    attn_gain,
    w_query,
    w_key,
    w_value,
    w_out,
    ffn_gain,
    w_router,
    shared_mix,
    shared_gate,
    shared_up,
    shared_down,
    expert_gate,
    expert_up,
    expert_down,
    cotangent,
):
    rows_here, width = tokens.shape
    ep_count = lax.axis_size("ep")
    tp_count = lax.axis_size("tp")
    ep_index = lax.axis_index("ep")
    offset = ep_index * rows_here
    quarter = rows_here // tp_count
    first_row = lax.axis_index("tp") * quarter
    slot_here, slot_hidden = expert_gate.shape[0], expert_gate.shape[1]
    expert_count = w_router.shape[1]
    bf16, f32 = jnp.bfloat16, jnp.float32

    def my_rows(array):
        return lax.dynamic_slice_in_dim(array, first_row, quarter, 0)

    side_columns = jnp.concatenate(
        [attn_gain[:, None], ffn_gain[:, None], shared_mix[:, None], w_router], axis=1
    )
    side_columns = jnp.pad(side_columns, ((0, 0), (0, -side_columns.shape[1] % 128)))
    joined_weights, pieces = gather_over_ep(
        jnp.concatenate([w_query, w_key, w_value, w_out, side_columns], axis=1),
        shared_pieces((shared_gate, shared_up, shared_down), ep_count),
    )
    heads_width = w_query.shape[1]
    side_weight = joined_weights[:, 4 * heads_width :]
    picked = jnp.any(
        my_rows(routes)[:, :, None] == jnp.arange(expert_count, dtype=jnp.int32), axis=1
    )
    picked_lanes = jnp.pad(picked.astype(bf16), ((0, 0), (3, 125 - expert_count)))
    upstream_rows = jnp.concatenate([my_rows(cotangent), picked_lanes], axis=1)
    shared_units = pieces.shape[1] // 3
    routed_units = slot_here * slot_hidden
    heads_here = heads_width // HD
    score_scale = HD ** (-0.5)
    first_norm_scale = side_weight[:, 0].astype(f32)
    second_norm_scale = side_weight[:, 1].astype(f32)
    query_at = offset + jnp.arange(rows_here, dtype=jnp.int32)
    _, query_pos = sequence_info(lengths, query_at)
    cosine, sine = rope_tables(query_pos, HD)
    tables = (cosine[:, 0], sine[:, 0], (query_at - query_pos)[None, :], query_at[None, :])
    (
        upstream_all,
        normed_one_turned,
        keys_win,
        values_win,
        queries,
        log_total,
        attended,
        resid,
        normed_two,
    ) = attention_front(
        tokens,
        joined_weights,
        upstream_rows,
        tables + (my_rows(tokens), first_norm_scale[None, :], second_norm_scale[None, :]),
        heads_here,
        score_scale,
    )
    (
        normed_all,
        weighted_h,
        d_pair_pre,
        block_rows,
        d_resid_low,
        d_resid,
        grad_gain_two,
        d_side,
    ) = ffn_over_all(
        normed_two,
        upstream_all,
        (expert_gate, expert_up, expert_down),
        pieces,
        joined_weights,
        resid,
        second_norm_scale[None, :],
        (slot_here, slot_hidden, shared_units),
        expert_count,
    )
    grad_side = jnp.dot(normed_two.astype(f32).T, d_side, precision=highest)
    grad_out = jnp.einsum("td,th->dh", d_resid_low, attended, preferred_element_type=f32)
    grad_out = lax.psum_scatter(
        grad_out.astype(bf16), "ep", scatter_dimension=0, tiled=True
    ).astype(f32)
    tile_shape = (ep_count, rows_here, -1)
    tiles_of = tuple(
        array.reshape(tile_shape) for array in (normed_all, d_pair_pre, upstream_all, weighted_h)
    )
    units = (slot_here, slot_hidden, shared_units)
    column = jnp.arange(128, dtype=jnp.int32)
    large = (
        d_resid_low,
        joined_weights,
        queries,
        keys_win,
        values_win,
        normed_one_turned,
        block_rows,
    )
    in_place = (
        log_total,
        tables[2],
        tables[3],
        tables[0],
        tables[1],
        my_rows(tokens),
        first_norm_scale[None, :],
        d_resid,
        grad_gain_two[None, :],
        jnp.where(column >= 2, grad_side, 0.0),
    )
    grad_weights, small, block_out, grad_tokens, grad_pieces, grad_experts = backward(
        large, tiles_of, in_place, units, score_scale
    )
    grad_shared = shared_whole(grad_pieces, 3)
    grad_tokens = grad_tokens.astype(f32)
    grad_experts = [grad.astype(f32).reshape(expert_gate.shape) for grad in grad_experts]
    parts = [grad_weights[:, i * heads_width : (i + 1) * heads_width] for i in range(3)]
    return (
        block_out,
        grad_tokens,
        small[:, 0],
        parts[0],
        parts[1],
        parts[2],
        grad_out,
        small[:, 1],
        small[:, 3 : 3 + expert_count],
        small[:, 2],
        grad_shared[0],
        grad_shared[1],
        grad_shared[2],
        grad_experts[0],
        grad_experts[1],
        grad_experts[2],
    )


def chosen_body(*arrays):
    rows_here, top_count = arrays[2].shape
    slot_here, expert_count = arrays[14].shape[0], arrays[9].shape[1]
    capacity = rows_here * top_count * 7 // (5 * expert_count)
    grid_of_two = lax.axis_size("ep") % 2 == 0 and lax.axis_size("tp") == 4
    if grid_of_two and rows_here < 2 * slot_here * capacity:
        return dense_body(*arrays)
    return body(*arrays)


def solution(mesh):
    placed = (
        P("ep", None),
        P(),
        P("ep", None),
        P("ep"),
        P("ep", "tp"),
        P("ep", "tp"),
        P("ep", "tp"),
        P("ep", "tp"),
        P("ep"),
        P("ep", None),
        P("ep"),
        P("ep", "tp"),
        P("ep", "tp"),
        P("ep", "tp"),
        P("ep", "tp", None),
        P("ep", "tp", None),
        P("ep", "tp", None),
        P("ep", None),
    )
    return jax.shard_map(
        chosen_body,
        mesh=mesh,
        in_specs=placed,
        out_specs=(
            P("ep", None),
            P("ep", None),
            P("ep"),
            P("ep", "tp"),
            P("ep", "tp"),
            P("ep", "tp"),
            P("ep", "tp"),
            P("ep"),
            P("ep", None),
            P("ep"),
            P("ep", "tp"),
            P("ep", "tp"),
            P("ep", "tp"),
            P("ep", "tp", None),
            P("ep", "tp", None),
            P("ep", "tp", None),
        ),
        check_vma=False,
    )
```

```python
import functools

import jax
import jax.numpy as jnp
from jax import lax
from jax.experimental import pallas as pl
from jax.experimental.pallas import tpu as pltpu
from jax.sharding import PartitionSpec as P

HD = 128


epsilon = 1e-06
rope_base = 1000000.0
highest = lax.Precision.HIGHEST
MESH = pl.DeviceIdType.MESH


def passed_along(block, axis, distance):
    devices = range(lax.axis_size(axis))
    route = [(i - distance, i) for i in devices if i - distance in devices]
    return lax.ppermute(block, axis, route)


def rope_tables(positions, width):
    steps = jnp.arange(0, width, 2, dtype=jnp.float32) / width
    inverse = rope_base ** (-steps)
    angles = positions.astype(jnp.float32)[:, None] * inverse[None, :]
    angles = jnp.concatenate([angles, angles], axis=-1)
    return (jnp.cos(angles)[:, None, :], jnp.sin(angles)[:, None, :])


def turn_half(values):
    middle = values.shape[-1] // 2
    return jnp.concatenate([-values[..., middle:], values[..., :middle]], axis=-1)


def rotate(values, cosine, sine):
    return values * cosine + turn_half(values) * sine


def unrotate(grads, cosine, sine):
    return grads * cosine - turn_half(grads * sine)


def sequence_info(lengths, indices):
    starts = jnp.cumsum(lengths) - lengths
    inside = starts[None, :] <= indices[:, None]
    segment = jnp.sum(inside.astype(jnp.int32), axis=1) - 1
    first = jnp.max(jnp.where(inside, starts[None, :], -1), axis=1)
    return (segment, indices - first)


def norm_forward(values, gain):
    scale = lax.rsqrt(jnp.mean(values * values, axis=-1, keepdims=True) + epsilon)
    return (values * scale * gain, scale)


def norm_backward(values, scale, gain, grads):
    unit = values * scale
    scaled = grads * gain
    inner = jnp.mean(scaled * unit, axis=-1, keepdims=True)
    return (scale * (scaled - unit * inner), jnp.sum(grads * unit, axis=0))


def deliver(rows):
    arrived_rows = lax.all_to_all(rows, "ep", split_axis=0, concat_axis=0, tiled=True)
    return arrived_rows


def bring_back(parts, target, rows_here, top_count):
    moved = lax.all_to_all(parts, "ep", split_axis=0, concat_axis=0, tiled=True)
    piece = moved.shape[3]
    return moved.reshape(-1, piece)[target].reshape(rows_here, top_count, piece)


def body(
    tokens,
    lengths,
    routes,
    attn_gain,
    w_query,
    w_key,
    w_value,
    w_out,
    ffn_gain,
    w_router,
    shared_mix,
    shared_gate,
    shared_up,
    shared_down,
    expert_gate,
    expert_up,
    expert_down,
    cotangent,
):
    rows_here = tokens.shape[0]
    width = tokens.shape[1]
    ep_count = lax.axis_size("ep")
    offset = lax.axis_index("ep") * rows_here
    slot_here = expert_gate.shape[0]
    top_count = routes.shape[1]
    gathered = (
        lax.all_gather(attn_gain, "ep", axis=0, tiled=True),
        lax.all_gather(w_query, "ep", axis=0, tiled=True),
        lax.all_gather(w_key, "ep", axis=0, tiled=True),
        lax.all_gather(w_value, "ep", axis=0, tiled=True),
        lax.all_gather(w_out, "ep", axis=0, tiled=True),
        lax.all_gather(ffn_gain, "ep", axis=0, tiled=True),
        lax.all_gather(w_router, "ep", axis=0, tiled=True),
        lax.all_gather(shared_mix, "ep", axis=0, tiled=True),
        lax.all_gather(shared_gate, "ep", axis=0, tiled=True),
        lax.all_gather(shared_up, "ep", axis=0, tiled=True),
        lax.all_gather(shared_down, "ep", axis=0, tiled=True),
    )
    (
        gain_first,
        query_weight_matrix,
        key_weight_matrix,
        value_weight_matrix,
        output_weight,
        gain_second,
        router_weight,
        shared_mixer_weight,
        shared_gate_weight,
        shared_up_weight,
        shared_down_weight,
    ) = gathered
    expert_count = router_weight.shape[1]
    capacity = (rows_here * top_count * 7 // (5 * expert_count) + 7) // 8 * 8
    heads_here = query_weight_matrix.shape[1] // HD
    score_scale = HD ** (-0.5)
    first_norm_scale = gain_first.astype(jnp.float32)
    second_norm_scale = gain_second.astype(jnp.float32)
    layer_input = tokens.astype(jnp.float32)
    normed_wide, norm_one = norm_forward(layer_input, first_norm_scale)
    normed_one = normed_wide.astype(jnp.bfloat16)
    query_at = offset + jnp.arange(rows_here, dtype=jnp.int32)
    key_at = offset - 2 * rows_here + jnp.arange(3 * rows_here, dtype=jnp.int32)
    query_seg, query_pos = sequence_info(lengths, query_at)
    key_seg, _ = sequence_info(lengths, key_at)
    cosine, sine = rope_tables(query_pos, HD)
    query_pre = jnp.dot(
        normed_one, query_weight_matrix, preferred_element_type=jnp.float32
    ).reshape(rows_here, heads_here, HD)
    key_pre = jnp.dot(normed_one, key_weight_matrix, preferred_element_type=jnp.float32).reshape(
        rows_here, heads_here, HD
    )
    queries = rotate(query_pre, cosine, sine).astype(jnp.bfloat16)
    keys = rotate(key_pre, cosine, sine).astype(jnp.bfloat16)
    values = (
        jnp.dot(normed_one, value_weight_matrix, preferred_element_type=jnp.float32)
        .astype(jnp.bfloat16)
        .reshape(rows_here, heads_here, HD)
    )
    carried = jnp.stack([keys, values], axis=0)
    window = [carried]
    for hop in range(2):
        carried = passed_along(carried, "ep", 1)
        window = [carried] + window
    joined = jnp.concatenate(window, axis=1)
    keys_win = joined[0]
    values_win = joined[1]
    allowed = (
        (query_seg[:, None] == key_seg[None, :])
        & (key_at[None, :] <= query_at[:, None])
        & (key_at[None, :] >= 0)
    )
    scores = (
        jnp.einsum("qhd,khd->hqk", queries, keys_win, preferred_element_type=jnp.float32)
        * score_scale
    )
    masked = jnp.where(allowed[None], scores, -1e30)
    peak = jnp.max(masked, axis=-1, keepdims=True)
    expo = jnp.exp(masked - peak)
    total = jnp.sum(expo, axis=-1, keepdims=True)
    log_total = peak + jnp.log(total)
    weights = expo / total
    attended = jnp.einsum(
        "hqk,khd->qhd", weights.astype(jnp.bfloat16), values_win, preferred_element_type=jnp.float32
    )
    attended = attended.reshape(rows_here, heads_here * HD).astype(jnp.bfloat16)
    attn_part = jnp.einsum("th,dh->td", attended, output_weight, preferred_element_type=jnp.float32)
    resid = layer_input + lax.psum(attn_part, "tp")
    normed_two_wide, norm_two = norm_forward(resid, second_norm_scale)
    normed_two = normed_two_wide.astype(jnp.bfloat16)
    normed_two_f = normed_two.astype(jnp.float32)
    router_f = router_weight.astype(jnp.float32)
    mix_f = shared_mixer_weight.astype(jnp.float32)
    router = jax.nn.softmax(jnp.dot(normed_two_f, router_f, precision=highest), axis=-1)
    picked = routes[:, :, None] == jnp.arange(expert_count, dtype=jnp.int32)[None, None, :]
    gates = jnp.sum(jnp.where(picked, router[:, None, :], 0.0), axis=-1)
    mixer = jax.nn.sigmoid(jnp.dot(normed_two_f, mix_f, precision=highest))
    shared_g = jnp.dot(normed_two, shared_gate_weight, preferred_element_type=jnp.float32)
    shared_u = jnp.dot(normed_two, shared_up_weight, preferred_element_type=jnp.float32)
    shared_h = (jax.nn.silu(shared_g) * shared_u).astype(jnp.bfloat16)
    shared_part = jnp.einsum(
        "tf,df->td", shared_h, shared_down_weight, preferred_element_type=jnp.float32
    )
    flat = routes.reshape(-1)
    hot = (flat[:, None] == jnp.arange(expert_count, dtype=jnp.int32)[None, :]).astype(jnp.int32)
    rank = jnp.sum(jnp.cumsum(hot, axis=0) * hot, axis=1) - 1
    target = flat * capacity + rank
    slot_total = ep_count * slot_here * capacity
    owner_route = (
        jnp.zeros((slot_total,), jnp.int32)
        .at[target]
        .set(jnp.arange(rows_here * top_count, dtype=jnp.int32))
    )
    filled = jnp.zeros((slot_total,), jnp.bool_).at[target].set(True)
    owner_token = owner_route // top_count
    send_rows = jnp.where(filled[:, None], normed_two[owner_token], jnp.zeros((), jnp.bfloat16))
    arrived_rows = deliver(send_rows.reshape(ep_count, slot_here, capacity, width))
    route_g = jnp.einsum(
        "nscd,sfd->nscf", arrived_rows, expert_gate, preferred_element_type=jnp.float32
    )
    route_u = jnp.einsum(
        "nscd,sfd->nscf", arrived_rows, expert_up, preferred_element_type=jnp.float32
    )
    route_h = (jax.nn.silu(route_g) * route_u).astype(jnp.bfloat16)
    route_part = jnp.einsum(
        "nscf,sfd->nscd", route_h, expert_down, preferred_element_type=jnp.float32
    )
    back_rows = bring_back(route_part, target, rows_here, top_count)
    upstream = cotangent.astype(jnp.float32)
    routed = jnp.sum(back_rows * gates[:, :, None], axis=1)
    ffn_part = mixer[:, None] * shared_part + routed
    route_dot = jnp.sum(back_rows * upstream[:, None, :], axis=-1)
    shared_dot = jnp.sum(shared_part * upstream, axis=-1)
    ffn_total, d_gate, d_mixer = lax.psum((ffn_part, route_dot, shared_dot), "tp")
    block_out = (resid + ffn_total).astype(jnp.bfloat16)
    d_router = jnp.sum(jnp.where(picked, d_gate[:, :, None], 0.0), axis=1)
    d_logits = router * (d_router - jnp.sum(router * d_router, axis=-1, keepdims=True))
    d_mixlogit = d_mixer * mixer * (1.0 - mixer)
    side = jnp.dot(d_logits, router_f.T, precision=highest) + d_mixlogit[:, None] * mix_f[None, :]
    grad_router = jnp.dot(normed_two_f.T, d_logits, precision=highest)
    grad_mix = jnp.dot(d_mixlogit, normed_two_f, precision=highest)
    d_shared = (mixer[:, None] * upstream).astype(jnp.bfloat16)
    d_sh = jnp.dot(d_shared, shared_down_weight, preferred_element_type=jnp.float32)
    sig_shared = jax.nn.sigmoid(shared_g)
    d_sg = (d_sh * shared_u * sig_shared * (1.0 + shared_g * (1.0 - sig_shared))).astype(
        jnp.bfloat16
    )
    d_su = (d_sh * shared_g * sig_shared).astype(jnp.bfloat16)
    d_normed_part = jnp.einsum(
        "tf,df->td", d_sg, shared_gate_weight, preferred_element_type=jnp.float32
    )
    d_normed_part = d_normed_part + jnp.einsum(
        "tf,df->td", d_su, shared_up_weight, preferred_element_type=jnp.float32
    )
    grad_sgate = jnp.einsum("td,tf->df", normed_two, d_sg, preferred_element_type=jnp.float32)
    grad_sup = jnp.einsum("td,tf->df", normed_two, d_su, preferred_element_type=jnp.float32)
    grad_sdown = jnp.einsum("td,tf->df", d_shared, shared_h, preferred_element_type=jnp.float32)
    d_route = (
        (gates[:, :, None] * upstream[:, None, :])
        .astype(jnp.bfloat16)
        .reshape(rows_here * top_count, width)
    )
    send_grads = jnp.where(filled[:, None], d_route[owner_route], jnp.zeros((), jnp.bfloat16))
    received_grads = deliver(send_grads.reshape(ep_count, slot_here, capacity, width))
    d_rh = jnp.einsum(
        "nscd,sfd->nscf", received_grads, expert_down, preferred_element_type=jnp.float32
    )
    sig_route = jax.nn.sigmoid(route_g)
    d_rg = (d_rh * route_u * sig_route * (1.0 + route_g * (1.0 - sig_route))).astype(jnp.bfloat16)
    routed_up_gradient = (d_rh * route_g * sig_route).astype(jnp.bfloat16)
    row_grads = jnp.einsum("nscf,sfd->nscd", d_rg, expert_gate, preferred_element_type=jnp.float32)
    row_grads = row_grads + jnp.einsum(
        "nscf,sfd->nscd", routed_up_gradient, expert_up, preferred_element_type=jnp.float32
    )
    grad_egate = jnp.einsum(
        "qxba,qxbr->xar", d_rg, arrived_rows, preferred_element_type=jnp.float32
    )
    expert_up_gradient = jnp.einsum(
        "qxba,qxbr->xar", routed_up_gradient, arrived_rows, preferred_element_type=jnp.float32
    )
    grad_edown = jnp.einsum(
        "qxba,qxbr->xar", route_h, received_grads, preferred_element_type=jnp.float32
    )
    grads_back = bring_back(row_grads, target, rows_here, top_count)
    d_routed = jnp.sum(grads_back, axis=1)
    d_normed_two = lax.psum(d_normed_part + d_routed, "tp") + side
    d_resid_norm, grad_gain_two = norm_backward(resid, norm_two, second_norm_scale, d_normed_two)
    d_resid = upstream + d_resid_norm
    d_resid_low = d_resid.astype(jnp.bfloat16)
    grad_outw = jnp.einsum("td,th->dh", d_resid_low, attended, preferred_element_type=jnp.float32)
    d_attended = jnp.einsum(
        "td,dh->th", d_resid_low, output_weight, preferred_element_type=jnp.float32
    )
    d_attended = d_attended.astype(jnp.bfloat16).reshape(rows_here, heads_here, HD)
    scores_again = (
        jnp.einsum("qhd,khd->hqk", queries, keys_win, preferred_element_type=jnp.float32)
        * score_scale
    )
    probs = jnp.where(allowed[None], jnp.exp(scores_again - log_total), 0.0)
    d_probs = jnp.einsum("qhd,khd->hqk", d_attended, values_win, preferred_element_type=jnp.float32)
    delta = jnp.sum(probs * d_probs, axis=-1, keepdims=True)
    d_scores = (probs * (d_probs - delta)).astype(jnp.bfloat16)
    d_queries = (
        jnp.einsum("hqk,khd->qhd", d_scores, keys_win, preferred_element_type=jnp.float32)
        * score_scale
    )
    d_keys_win = (
        jnp.einsum("hqk,qhd->khd", d_scores, queries, preferred_element_type=jnp.float32)
        * score_scale
    )
    d_values_win = jnp.einsum(
        "hqk,qhd->khd", probs.astype(jnp.bfloat16), d_attended, preferred_element_type=jnp.float32
    )
    pair_grads = jnp.stack([d_keys_win, d_values_win], axis=0)
    older = pair_grads[:, :rows_here]
    later = [pair_grads[:, rows_here : 2 * rows_here], pair_grads[:, 2 * rows_here :]]
    running = older
    for hop in range(2):
        running = passed_along(running, "ep", -1)
        running = running + later[hop]
    d_query_pre = (
        unrotate(d_queries, cosine, sine).astype(jnp.bfloat16).reshape(rows_here, heads_here * HD)
    )
    d_key_pre = (
        unrotate(running[0], cosine, sine).astype(jnp.bfloat16).reshape(rows_here, heads_here * HD)
    )
    d_values = running[1].astype(jnp.bfloat16).reshape(rows_here, heads_here * HD)
    grad_queryw = jnp.einsum(
        "td,th->dh", normed_one, d_query_pre, preferred_element_type=jnp.float32
    )
    grad_keyw = jnp.einsum("td,th->dh", normed_one, d_key_pre, preferred_element_type=jnp.float32)
    grad_valuew = jnp.einsum("td,th->dh", normed_one, d_values, preferred_element_type=jnp.float32)
    d_normed_one = jnp.einsum(
        "th,dh->td", d_query_pre, query_weight_matrix, preferred_element_type=jnp.float32
    )
    d_normed_one = d_normed_one + jnp.einsum(
        "th,dh->td", d_key_pre, key_weight_matrix, preferred_element_type=jnp.float32
    )
    d_normed_one = d_normed_one + jnp.einsum(
        "th,dh->td", d_values, value_weight_matrix, preferred_element_type=jnp.float32
    )
    d_normed_one = lax.psum(d_normed_one, "tp")
    d_input_norm, grad_gain_one = norm_backward(
        layer_input, norm_one, first_norm_scale, d_normed_one
    )
    grad_tokens = d_resid + d_input_norm
    summed = (
        lax.psum_scatter(grad_gain_one, "ep", scatter_dimension=0, tiled=True),
        lax.psum_scatter(grad_queryw, "ep", scatter_dimension=0, tiled=True),
        lax.psum_scatter(grad_keyw, "ep", scatter_dimension=0, tiled=True),
        lax.psum_scatter(grad_valuew, "ep", scatter_dimension=0, tiled=True),
        lax.psum_scatter(grad_outw, "ep", scatter_dimension=0, tiled=True),
        lax.psum_scatter(grad_gain_two, "ep", scatter_dimension=0, tiled=True),
        lax.psum_scatter(grad_router, "ep", scatter_dimension=0, tiled=True),
        lax.psum_scatter(grad_mix, "ep", scatter_dimension=0, tiled=True),
        lax.psum_scatter(grad_sgate, "ep", scatter_dimension=0, tiled=True),
        lax.psum_scatter(grad_sup, "ep", scatter_dimension=0, tiled=True),
        lax.psum_scatter(grad_sdown, "ep", scatter_dimension=0, tiled=True),
    )
    return (
        block_out,
        grad_tokens,
        summed[0],
        summed[1],
        summed[2],
        summed[3],
        summed[4],
        summed[5],
        summed[6],
        summed[7],
        summed[8],
        summed[9],
        summed[10],
        grad_egate,
        expert_up_gradient,
        grad_edown,
    )


class Place:
    def __init__(self):
        self.ep, self.tp = lax.axis_index("ep"), lax.axis_index("tp")
        self.z, self.y = self.ep // 2, self.ep % 2
        self.x, self.c = self.tp // 2, self.tp % 2
        self.depth = lax.axis_size("ep") // 2
        self.next_core = (self.ep, self.x * 2 + 1 - self.c)
        self.next_x = (self.ep, (1 - self.x) * 2 + self.c)
        self.next_y = (self.z * 2 + 1 - self.y, self.tp)

    def at_z(self, z):
        return (z * 2 + self.y, self.tp)

    def ahead(self, steps):
        return lax.rem(self.z + steps, self.depth)

    def behind(self, steps):
        return lax.rem(self.z + self.depth - steps, self.depth)

    def greet(self):
        barrier = pltpu.get_barrier_semaphore()
        peers = [self.next_core, self.next_x, self.next_y]
        peers += [self.at_z(self.ahead(k)) for k in range(1, self.depth)]
        for peer in peers:
            pl.semaphore_signal(barrier, inc=1, device_id=peer, device_id_type=MESH)
        pl.semaphore_wait(barrier, len(peers))

    def greet_row(self):
        barrier = pltpu.get_barrier_semaphore()
        count = 2 * self.depth
        peers = [(lax.rem(self.ep + k, count), self.tp) for k in range(1, count)]
        peers += [self.next_core, self.next_x]
        for peer in peers:
            pl.semaphore_signal(barrier, inc=1, device_id=peer, device_id_type=MESH)
        pl.semaphore_wait(barrier, len(peers))

    def greet_ep(self):
        barrier = pltpu.get_barrier_semaphore()
        count = 2 * self.depth
        for k in range(1, count):
            peer = (lax.rem(self.ep + k, count), self.tp)
            pl.semaphore_signal(barrier, inc=1, device_id=peer, device_id_type=MESH)
        pl.semaphore_wait(barrier, count - 1)


def remote(src, dst, send, recv, peer):
    return pltpu.make_async_remote_copy(
        src_ref=src, dst_ref=dst, send_sem=send, recv_sem=recv, device_id=peer, device_id_type=MESH
    )


def ffn_kernel(
    units,
    expert_count,
    rows_in,
    upstream_in,
    gate_in,
    up_in,
    down_in,
    pieces_in,
    weights_in,
    resid_in,
    gain_in,
    rows_all,
    weighted_out,
    d_pair_out,
    block_out,
    d_resid_low_out,
    d_resid_out,
    d_gain_out,
    d_side_out,
    d_rows_sum,
    out_sum,
    pair_w,
    down_w,
    side_w,
    rows_tile,
    upstream_tile,
    pair_pre,
    d_hidden,
    factors,
    dots,
    weighted_tile,
    d_pair_tile,
    d_resid_low,
    d_rows_tile,
    out_tile,
    d_rows_core,
    out_core,
    d_rows_held,
    out_held,
    d_rows_hop,
    out_hop,
    d_rows_hop2,
    out_hop2,
    d_rows_z,
    out_z,
    d_rows_to_z,
    out_to_z,
    gathered_send,
    gathered_recv,
    hop_send,
    hop_recv,
    weight_sem,
    end_sem,
    own_sem,
    z_send,
    z_recv,
    plane_send,
    plane_recv,
    load_sem,
    store_sem,
    sum_send,
    sum_recv,
    end_send,
    end_recv,
    core_credit,
    hop_credit,
    hop2_credit,
):
    at = Place()
    depth = at.depth
    quarter, width = rows_in.shape
    half = quarter // 2
    f32, bf16 = jnp.float32, jnp.bfloat16

    def weight_copies():
        hidden = down_w.shape[0]
        slot_here, slot_hidden, shared = units
        routed = slot_here * slot_hidden
        columns = pieces_in.shape[2]
        pairs = [(weights_in.at[:, pl.ds(weights_in.shape[1] - 128, 128)], side_w)]
        kinds = ((gate_in, pair_w, 0), (up_in, pair_w, hidden), (down_in, down_w, 0))
        for kind, (experts, into, first) in enumerate(kinds):
            pairs.append((experts, into.at[pl.ds(first, routed)]))
            here = pl.ds(first + routed, shared)
            for e in range(2 * depth):
                src = pieces_in.at[e, pl.ds(kind * shared, shared)]
                pairs.append((src, into.at[here, pl.ds(e * columns, columns)]))
        return [
            pltpu.make_async_copy(src, dst, weight_sem.at[i]) for i, (src, dst) in enumerate(pairs)
        ]

    def clear_rest():
        hidden = down_w.shape[0]
        used = units[0] * units[1] + units[2]
        for into, first in ((pair_w, 0), (pair_w, hidden), (down_w, 0)):
            if used < hidden:
                into[first + used : first + hidden] = jnp.zeros((hidden - used, width), bf16)

    for copy in weight_copies():
        copy.start()
    clear_rest()

    def block(j, y, x):
        return rows_all.at[at.behind(j), y, x, at.c]

    def plane_copy(j, kind):
        y, other_y = at.y, 1 - at.y
        own, other_x = at.x, 1 - at.x
        if kind == 0:
            src, peer = block(j, y, own), at.next_x
        elif kind == 1:
            src, peer = block(j, y, own), at.next_y
        elif kind == 2:
            src, peer = block(j, y, other_x).at[pl.ds(0, half)], at.next_y
        elif kind == 3:
            src, peer = block(j, other_y, own).at[pl.ds(half, half)], at.next_x
        else:
            src = block(j, other_y if kind >= 6 else y, other_x if kind % 2 else own)
            peer = at.next_core
        return remote(src, src, plane_send.at[j, kind], plane_recv.at[j, kind], peer)

    def z_copy(k):
        return remote(
            rows_in, block(0, at.y, at.x), z_send.at[k - 1], z_recv.at[k - 1], at.at_z(at.ahead(k))
        )

    def z_arrival(k):
        dst = block(k, at.y, at.x)
        return remote(dst, dst, z_send.at[k - 1], z_recv.at[k - 1], at.at_z(at.behind(k)))

    def begin(j):
        for kind in (0, 1, 4):
            plane_copy(j, kind).start()

    def spread(j):
        plane_copy(j, 0).wait_recv()
        plane_copy(j, 2).start()
        plane_copy(j, 5).start()
        plane_copy(j, 1).wait_recv()
        plane_copy(j, 3).start()
        plane_copy(j, 6).start()

    def begin_later(j):
        z_arrival(j).wait_recv()
        begin(j)

    def last_hop(j):
        plane_copy(j, 2).wait_recv()
        plane_copy(j, 3).wait_recv()
        plane_copy(j, 7).start()

    def near_ready(j):
        plane_copy(j, 4).wait_recv()
        plane_copy(j, 5).wait_recv()

    def far_ready(j):
        plane_copy(j, 6).wait_recv()
        plane_copy(j, 7).wait_recv()

    def parity(step):
        return lax.rem(step, 2)

    def slot_of(turn):
        return lax.rem(turn + 1, depth)

    def other_y(step):
        return lax.rem(parity(step) + (step // 2 + 1) // depth, 2)

    def tile_at(step):
        return at.behind(slot_of(step // 2)), lax.rem(at.y + other_y(step), 2)

    def load_rows(step):
        z, y = tile_at(step)
        return pltpu.make_async_copy(rows_all.at[z, y], rows_tile, load_sem.at[0])

    def load_upstream(step):
        z, y = tile_at(step)
        return pltpu.make_async_copy(upstream_in.at[z, y], upstream_tile, load_sem.at[1])

    def stores(step):
        z, y = tile_at(step)
        pairs = ((weighted_tile, weighted_out), (d_pair_tile, d_pair_out))
        return [
            pltpu.make_async_copy(src, dst.at[z, y], store_sem.at[i])
            for i, (src, dst) in enumerate(pairs)
        ]

    tiles, cores = (d_rows_tile, out_tile), (d_rows_core, out_core)
    helds, sums = (d_rows_held, out_held), (d_rows_sum, out_sum)
    hops, hops2, zs = (d_rows_hop, out_hop), (d_rows_hop2, out_hop2), (d_rows_z, out_z)
    to_zs = (d_rows_to_z, out_to_z)

    def sum_copy(a, kind, src, dst, peer):
        return remote(src, dst, sum_send.at[a, kind], sum_recv.at[a, kind], peer)

    def core_sum(a):
        return sum_copy(a, 0, tiles[a].at[:, 1 - at.c], cores[a], at.next_core)

    def row_hop(turn, other):
        y = lax.rem(at.y + other, 2)
        slot = parity(turn)
        src = d_rows_held.at[slot, y, 1 - at.x]
        return remote(
            src, d_rows_hop.at[slot, y], hop_send.at[slot, other], hop_recv.at[slot, other], at.next_x
        )

    def out_hop_sum(turn):
        slot = parity(turn)
        src = out_held.at[slot, 1 - at.y]
        return remote(
            src, out_hop.at[slot], hop_send.at[slot, 2], hop_recv.at[slot, 2], at.next_y
        )

    def hop2_sum(a, turn):
        slot = parity(turn)
        if a == 0:
            src, peer = helds[0].at[slot, 1 - at.y, at.x], at.next_y
        else:
            src, peer = helds[1].at[slot, at.y, 1 - at.x], at.next_x
        return sum_copy(a, 2, src, hops2[a], peer)

    def z_sum(a, turn):
        return remote(
            to_zs[a].at[parity(turn)],
            zs[a].at[turn],
            end_send.at[a, turn],
            end_recv.at[a, turn],
            at.at_z(at.behind(turn + 1)),
        )

    def allow(semaphore, peer):
        pl.semaphore_signal(semaphore, inc=1, device_id=peer, device_id_type=MESH)

    piece = 32

    def add(into, first, second):
        def body(i, carry):
            part = pl.ds(pl.multiple_of(i * piece, piece), piece)
            into[part] = first[part] + second[part]
            return carry

        lax.fori_loop(0, quarter // piece, body, 0)

    def after_core(step):
        turn = step // 2
        other = other_y(step)
        held, y = parity(turn), lax.rem(at.y + other, 2)

        @pl.when((parity(step) == 0) & (turn >= 2))
        def _():
            for a in (0, 1):
                pl.semaphore_wait(hop_credit.at[a], 1)

        for a in (0, 1):
            core_sum(a).wait()
            for x in (1 - at.x, at.x):
                add(helds[a].at[held, y, x], tiles[a].at[x, at.c], cores[a].at[x])
            if a == 0:
                row_hop(turn, other).start()
            else:

                @pl.when(other == 1)
                def _():
                    out_hop_sum(turn).start()

        @pl.when(step + 1 < 2 * depth)
        def _():
            allow(core_credit, at.next_core)

    def after_row_hop(turn, other):
        slot, y = parity(turn), lax.rem(at.y + other, 2)
        row_hop(turn, other).wait()
        into = d_rows_held.at[slot, y, at.x]
        add(into, into, d_rows_hop.at[slot, y])

    def after_out_hop(turn):
        slot = parity(turn)
        out_hop_sum(turn).wait()
        for x in (1 - at.x, at.x):
            into = out_held.at[slot, at.y, x]
            add(into, into, out_hop.at[slot, x])

    def may_hop2(turn, a):
        @pl.when(turn >= 1)
        def _():
            pl.semaphore_wait(hop2_credit.at[a], 1)

    def after_hop(turn):
        after_row_hop(turn, 1)
        may_hop2(turn, 0)
        hop2_sum(0, turn).start()
        after_row_hop(turn, 0)
        after_out_hop(turn)
        may_hop2(turn, 1)
        hop2_sum(1, turn).start()

        @pl.when(turn + 2 < depth)
        def _():
            allow(hop_credit.at[0], at.next_x)
            allow(hop_credit.at[1], at.next_y)

    def after_hop2(turn):
        slot = parity(turn)
        for a in (0, 1):
            hop2_sum(a, turn).wait()

            @pl.when(turn >= 2)
            def _():
                z_sum(a, turn - 2).wait_send()

            add(to_zs[a].at[slot], helds[a].at[slot, at.y, at.x], hops2[a])
            z_sum(a, turn).start()
        allow(hop2_credit.at[0], at.next_y)
        allow(hop2_credit.at[1], at.next_x)

    load_upstream(0).start()
    at.greet()
    z_copy(1).start()
    own_copy = pltpu.make_async_copy(rows_in, block(0, at.y, at.x), own_sem)
    own_copy.start()
    own_copy.wait()
    begin(0)
    begin_later(1)
    for k in range(2, depth):
        z_copy(k).start()
    spread(0)
    spread(1)
    near_ready(1)
    load_rows(0).start()
    for copy in weight_copies():
        copy.wait()

    tile_rows = 4 * quarter
    hidden_total = down_w.shape[0]
    lane = lax.broadcasted_iota(jnp.int32, (tile_rows, 128), 1)
    slot_here, slot_hidden, shared_hidden = units
    routed = slot_here * slot_hidden
    across = (((1,), (1,)), ((), ()))
    few = 16

    def gate_factors(rows, picked):
        logits = jnp.dot(rows, side_w[...], preferred_element_type=f32)
        chooses = (lane >= 3) & (lane < 3 + expert_count)
        peak = jnp.max(jnp.where(chooses, logits, -1e30), axis=1, keepdims=True)
        expo = jnp.where(chooses, jnp.exp(jnp.where(chooses, logits, peak) - peak), 0.0)
        routed_gate = expo / jnp.sum(expo, axis=1, keepdims=True) * picked.astype(f32)
        mix_pre = jnp.sum(jnp.where(lane == 2, logits, 0.0), axis=1, keepdims=True)
        result = jnp.where(lane == slot_here, 1.0 / (1.0 + jnp.exp(-mix_pre)), 0.0)
        for s in range(slot_here):
            chosen = lane == 3 + at.ep * slot_here + s
            gate = jnp.sum(jnp.where(chosen, routed_gate, 0.0), axis=1, keepdims=True)
            result = jnp.where(lane == s, gate, result)
        return result

    few_lane = lax.broadcasted_iota(jnp.int32, (few, 128), 1)
    bounds = [s * slot_hidden for s in range(slot_here)] + [routed, hidden_total]

    def owners(group):
        found = []
        for s in range(slot_here + 1):
            low, high = max(bounds[s] - group * 128, 0), min(bounds[s + 1] - group * 128, 128)
            if low < high:
                found.append((s, low, high))
        return found

    def hidden_rows(i, carry):
        here = pl.ds(pl.multiple_of(i * few, few), few)
        gates = [
            jnp.broadcast_to(factors[here, s : s + 1], (few, 128)) for s in range(slot_here + 1)
        ]
        parts = [None] * (slot_here + 1)
        for group in range(hidden_total // 128):
            units_here = slice(group * 128, (group + 1) * 128)
            units_up = slice(hidden_total + group * 128, hidden_total + (group + 1) * 128)
            gate_pre, up_pre = pair_pre[here, units_here], pair_pre[here, units_up]
            d_h = d_hidden[here, units_here]
            found = owners(group)
            factor = gates[found[0][0]]
            for s, low, _ in found[1:]:
                factor = jnp.where(few_lane >= low, gates[s], factor)
            sig = 0.5 + 0.5 * jnp.tanh(0.5 * gate_pre)
            silu = gate_pre * sig
            hidden = silu * up_pre
            product = hidden * d_h
            gated = factor * d_h
            weighted_tile[here, units_here] = (factor * hidden).astype(bf16)
            slope = sig + silu * (1.0 - sig)
            d_pair_tile[here, units_here] = (gated * up_pre * slope).astype(bf16)
            d_pair_tile[here, units_up] = (gated * silu).astype(bf16)
            for s, low, high in found:
                mine = product
                if high < 128:
                    mine = jnp.where(few_lane < high, mine, 0.0)
                if low > 0:
                    mine = jnp.where(few_lane >= low, mine, 0.0)
                parts[s] = mine if parts[s] is None else parts[s] + mine
        result = jnp.zeros((few, 128), f32)
        for s in range(slot_here + 1):
            dot = jnp.sum(parts[s], axis=1, keepdims=True)
            where = few_lane == (2 if s == slot_here else 3 + at.ep * slot_here + s)
            result = jnp.where(where, dot, result)
        dots[here] = result.astype(bf16)
        return carry

    def first_half(step):
        load_upstream(step).wait()
        upstream = upstream_tile[...].reshape(tile_rows, upstream_tile.shape[-1])
        d_hidden[...] = lax.dot_general(
            upstream[:, :width], down_w[...], across, preferred_element_type=f32
        )
        load_rows(step).wait()
        rows = rows_tile[...].reshape(tile_rows, width)
        factors[...] = gate_factors(rows, upstream[:, width:])
        pair_pre[...] = lax.dot_general(rows, pair_w[...], across, preferred_element_type=f32)

        @pl.when(step + 1 < 2 * depth)
        def _():
            load_upstream(step + 1).start()

        @pl.when(step >= 1)
        def _():
            for copy in stores(step - 1):
                copy.wait()

        lax.fori_loop(0, tile_rows // few, hidden_rows, 0, unroll=2)
        for copy in stores(step):
            copy.start()
        turn = step // 2

        @pl.when(step == 0)
        def _():
            last_hop(0)

        @pl.when((parity(step) == 0) & (turn + 1 < depth))
        def _():
            last_hop(turn + 1)

        @pl.when((step >= 1) & (step + 1 < depth))
        def _():
            spread(step + 1)

        @pl.when(step + 2 < depth)
        def _():
            begin_later(step + 2)

    def second_half(step):
        blocks = (2, 2, quarter)
        some = width // 2
        for n in range(2):
            columns = slice(n * some, (n + 1) * some)
            part = jnp.dot(weighted_tile[...], down_w[:, columns], preferred_element_type=f32)
            out_tile[:, :, :, columns] = part.astype(bf16).reshape(blocks + (some,))
            part = jnp.dot(d_pair_tile[...], pair_w[:, columns], preferred_element_type=f32)
            d_rows_tile[:, :, :, columns] = part.astype(bf16).reshape(blocks + (some,))
        d_rows_tile[:, :, :, width:] = dots[...].reshape(blocks + (128,))

        @pl.when(step >= 1)
        def _():
            pl.semaphore_wait(core_credit, 1)

        for a in (0, 1):
            core_sum(a).start()
        turn = step // 2

        @pl.when((parity(step) == 0) & (turn + 1 < depth))
        def _():
            far_ready(slot_of(turn))

        @pl.when((parity(step) == 1) & (turn + 1 < depth))
        def _():
            near_ready(slot_of(turn + 1))

        @pl.when(step == 2 * depth - 3)
        def _():
            far_ready(slot_of(turn + 1))

        @pl.when(step + 1 < 2 * depth)
        def _():
            load_rows(step + 1).start()

    def step_body(step, carry):
        first_half(step)

        @pl.when(step == 2 * depth - 1)
        def _():
            after_hop(depth - 2)

        @pl.when(step >= 1)
        def _():
            after_core(step - 1)

        second_half(step)
        odd = parity(step) == 1

        @pl.when(odd & (step >= 3) & (step < 2 * depth - 1))
        def _():
            after_hop((step - 3) // 2)

        @pl.when(jnp.logical_not(odd) & (step >= 4))
        def _():
            after_hop2((step - 4) // 2)

        return carry

    lax.fori_loop(0, 2 * depth, step_body, 0)
    last = depth - 1
    own_rows, own_upstream = rows_tile.at[0, 0], upstream_tile.at[0, 0]
    own_loads = [
        pltpu.make_async_copy(rows_in, own_rows, end_sem.at[0]),
        pltpu.make_async_copy(
            upstream_in.at[at.z, at.y, at.x, at.c], own_upstream, end_sem.at[1]
        ),
    ]
    for copy in own_loads:
        copy.start()
    after_hop2(last - 1)
    after_row_hop(last, 1)
    may_hop2(last, 0)
    hop2_sum(0, last).start()
    after_core(2 * depth - 1)
    after_out_hop(last)
    may_hop2(last, 1)
    hop2_sum(1, last).start()
    after_row_hop(last, 0)

    def total_of(a):
        hop2_sum(a, last).wait()
        held = helds[a].at[last % 2, at.y, at.x]
        for turn in range(last):
            z_sum(a, turn).wait_recv()

        def total_body(i, carry):
            part = pl.ds(pl.multiple_of(i * piece, piece), piece)
            total = held[part].astype(f32) + hops2[a][part].astype(f32)
            for k in range(last):
                total = total + zs[a][k, part].astype(f32)
            sums[a][part] = total
            return carry

        lax.fori_loop(0, quarter // piece, total_body, 0)

    total_of(0)
    own_lane = lax.broadcasted_iota(jnp.int32, (quarter, 128), 1)
    chooses = (own_lane >= 3) & (own_lane < 3 + expert_count)
    for copy in own_loads:
        copy.wait()
    rows = own_rows[...]
    logits = jnp.dot(rows, side_w[...], preferred_element_type=f32)
    peak = jnp.max(jnp.where(chooses, logits, -1e30), axis=1, keepdims=True)
    expo = jnp.where(chooses, jnp.exp(jnp.where(chooses, logits, peak) - peak), 0.0)
    router = expo / jnp.sum(expo, axis=1, keepdims=True)
    mixer = 1.0 / (1.0 + jnp.exp(-jnp.where(own_lane == 2, logits, 0.0)))
    gate_dots = d_rows_sum[:, width:]
    d_router = jnp.where(chooses, gate_dots * own_upstream[:, width:].astype(f32), 0.0)
    d_logits = router * (d_router - jnp.sum(router * d_router, axis=1, keepdims=True))
    d_mix = gate_dots * mixer * (1.0 - mixer)
    d_side = jnp.where(own_lane == 2, d_mix, jnp.where(chooses, d_logits, 0.0))
    d_side_out[...] = d_side
    high = d_side.astype(bf16)
    lower = (d_side - high.astype(f32)).astype(bf16)
    for split in (high, lower):
        d_rows_sum[:, :width] += lax.dot_general(
            split, side_w[...], across, preferred_element_type=f32
        )

    def end_body(i, carry):
        part = pl.ds(pl.multiple_of(i * few, few), few)
        resid = resid_in[part]
        scale = lax.rsqrt(jnp.mean(resid * resid, axis=1, keepdims=True) + epsilon)
        unit_rows = resid * scale
        grads = d_rows_sum[part, :width]
        scaled = grads * gain_in[...]
        inner = jnp.mean(scaled * unit_rows, axis=1, keepdims=True)
        d_resid = own_upstream[part, :width].astype(f32) + scale * (scaled - unit_rows * inner)
        d_resid_out[part] = d_resid
        d_resid_low[part] = d_resid.astype(bf16)
        return carry + jnp.sum(grads * unit_rows, axis=0, keepdims=True)

    d_gain_out[...] = lax.fori_loop(0, quarter // few, end_body, jnp.zeros((1, width), f32))

    def gather_copy(kind):
        if kind == 2:
            src = dst = d_resid_low_out.at[1 - at.x, at.c]
        else:
            src, dst = d_resid_low, d_resid_low_out.at[at.x, at.c]
        peer = at.next_x if kind == 0 else at.next_core
        return remote(src, dst, gathered_send.at[kind], gathered_recv.at[kind], peer)

    own_end = pltpu.make_async_copy(d_resid_low, d_resid_low_out.at[at.x, at.c], own_sem)
    own_end.start()
    for kind in (0, 1):
        gather_copy(kind).start()
    total_of(1)
    block_out[...] = (resid_in[...] + out_sum[...]).astype(bf16)
    gather_copy(0).wait_recv()
    gather_copy(2).start()
    own_end.wait()
    gather_copy(0).wait_send()
    gather_copy(1).wait()
    gather_copy(2).wait()
    for copy in stores(2 * depth - 1):
        copy.wait()
    for a in (0, 1):
        for turn in range(max(0, depth - 3), depth - 1):
            z_sum(a, turn).wait_send()
    for k in range(1, depth):
        z_copy(k).wait_send()

    def finish(j, carry):
        for kind in range(8):
            plane_copy(j, kind).wait_send()
        return carry

    lax.fori_loop(0, depth, finish, 0)


def ffn_over_all(rows, upstream_all, experts, pieces, weights, resid, gain, units, expert_count):
    quarter, width = rows.shape
    ep_count, tp_count = lax.axis_size("ep"), lax.axis_size("tp")
    depth = ep_count // 2
    hidden = -(-(units[0] * units[1] + units[2]) // 128) * 128
    bf16, f32 = jnp.bfloat16, jnp.float32
    wide = width + 128
    tile_rows = tp_count * quarter
    tokens = ep_count * tile_rows
    anywhere = pl.BlockSpec(memory_space=pl.ANY)
    in_vmem = pl.BlockSpec(memory_space=pltpu.VMEM)

    def both(*lead):
        return [pltpu.VMEM(lead + (quarter, columns), bf16) for columns in (wide, width)]

    dma = pltpu.SemaphoreType.DMA
    outs = pl.pallas_call(
        functools.partial(ffn_kernel, units, expert_count),
        out_shape=(
            jax.ShapeDtypeStruct((depth, 2, 2, 2, quarter, width), bf16),
            jax.ShapeDtypeStruct((depth, 2, tile_rows, hidden), bf16),
            jax.ShapeDtypeStruct((depth, 2, tile_rows, 2 * hidden), bf16),
            jax.ShapeDtypeStruct((quarter, width), bf16),
            jax.ShapeDtypeStruct((2, 2, quarter, width), bf16),
            jax.ShapeDtypeStruct((quarter, width), f32),
            jax.ShapeDtypeStruct((1, width), f32),
            jax.ShapeDtypeStruct((quarter, 128), f32),
        ),
        in_specs=[anywhere] * 7 + [in_vmem] * 2,
        out_specs=(anywhere,) * 3 + (in_vmem, anywhere) + (in_vmem,) * 3,
        scratch_shapes=[
            pltpu.VMEM((quarter, wide), f32),
            pltpu.VMEM((quarter, width), f32),
            pltpu.VMEM((2 * hidden, width), bf16),
            pltpu.VMEM((hidden, width), bf16),
            pltpu.VMEM((width, 128), bf16),
            pltpu.VMEM((2, 2, quarter, width), bf16),
            pltpu.VMEM((2, 2, quarter, wide), bf16),
            pltpu.VMEM((tile_rows, 2 * hidden), f32),
            pltpu.VMEM((tile_rows, hidden), f32),
            pltpu.VMEM((tile_rows, 128), f32),
            pltpu.VMEM((tile_rows, 128), bf16),
            pltpu.VMEM((tile_rows, hidden), bf16),
            pltpu.VMEM((tile_rows, 2 * hidden), bf16),
            pltpu.VMEM((quarter, width), bf16),
        ]
        + both(2, 2)
        + both(2)
        + both(2, 2, 2)
        + both(2, 2)
        + both()
        + both(depth - 1)
        + both(2)
        + [
            dma((3,)),
            dma((3,)),
            dma((2, 3)),
            dma((2, 3)),
            dma((4 + 6 * depth,)),
            dma((2,)),
            dma,
            dma((depth - 1,)),
            dma((depth - 1,)),
            dma((depth, 8)),
            dma((depth, 8)),
            dma((2,)),
            dma((2,)),
            dma((2, 3)),
            dma((2, 3)),
            dma((2, depth - 1)),
            dma((2, depth - 1)),
            pltpu.SemaphoreType.REGULAR,
            pltpu.SemaphoreType.REGULAR((2,)),
            pltpu.SemaphoreType.REGULAR((2,)),
        ],
        compiler_params=pltpu.CompilerParams(
            collective_id=1, has_side_effects=True, vmem_limit_bytes=62 * 2**20
        ),
        cost_estimate=pl.CostEstimate(
            flops=12 * tokens * width * hidden,
            bytes_accessed=10 * tokens * width,
            transcendentals=tokens * hidden,
        ),
        name="ffn_all_tokens",
    )(
        rows,
        upstream_all.reshape(depth, 2, 2, 2, quarter, wide),
        *[array.reshape(-1, width) for array in experts],
        pieces,
        weights,
        resid,
        gain,
    )
    rows_all, weighted, d_pair, block_out, d_resid_low, d_resid, d_gain, d_side = outs
    return (
        rows_all.reshape(tokens, width),
        weighted.reshape(tokens, hidden),
        d_pair.reshape(tokens, 2 * hidden),
        block_out,
        d_resid_low.reshape(tile_rows, width),
        d_resid,
        d_gain[0],
        d_side,
    )


def swap_copies(at, pieces_in, pieces_out, send_sem, recv_sem, leave):
    count = 2 * at.depth
    copies = []
    for k in range(1, count):
        to, back = lax.rem(at.ep + k, count), lax.rem(at.ep + count - k, count)
        if leave:
            src, dst, peer = pieces_in.at[to], pieces_out.at[at.ep], to
        else:
            src, dst, peer = pieces_in.at[back], pieces_out.at[back], back
        copies.append(remote(src, dst, send_sem.at[k], recv_sem.at[k], (peer, at.tp)))
    return copies


def weights_kernel(
    own_in,
    pieces_in,
    all_out,
    pieces_out,
    own_sem,
    z_send,
    z_recv,
    y_send,
    y_recv,
    swap_send,
    swap_recv,
):
    at = Place()
    depth = at.depth
    half = own_in.shape[0] // 2
    last = depth - 1

    def block(k, y, h):
        return all_out.at[at.z + k, y, pl.ds(h * half, half)]

    def z_copy(k, h, direction):
        if k == 0:
            src = own_in.at[pl.ds(h * half, half)]
        else:
            src = block(k, at.y, h)
        slot = last + k - direction
        return remote(
            src,
            block(k, at.y, h),
            z_send.at[last + k, h, (direction + 1) // 2],
            z_recv.at[slot, h],
            at.at_z(at.z + direction),
        )

    def z_arrival(k, h):
        direction = 1 if k > 0 else -1
        dst = block(k, at.y, h)
        return remote(
            dst, dst, z_send.at[last + k, h, 0], z_recv.at[last + k, h], at.at_z(at.z + direction)
        )

    def y_copy(k, h):
        src = own_in.at[pl.ds(h * half, half)] if k == 0 else block(k, at.y, h)
        return remote(
            src, block(k, at.y, h), y_send.at[last + k, h], y_recv.at[last + k, h], at.next_y
        )

    own_copies = [
        pltpu.make_async_copy(own_in, all_out.at[at.z, at.y], own_sem.at[0]),
        pltpu.make_async_copy(pieces_in.at[at.ep], pieces_out.at[at.ep], own_sem.at[1]),
    ]
    for copy in own_copies:
        copy.start()
    has_up, has_down = at.z + 1 < depth, at.z > 0
    at.greet_ep()

    for h in (0, 1):
        pl.when(has_up)(lambda: z_copy(0, h, 1).start())
        pl.when(has_down)(lambda: z_copy(0, h, -1).start())
        y_copy(0, h).start()
    swap = (at, pieces_in, pieces_out, swap_send, swap_recv)
    for copy in swap_copies(*swap, True):
        copy.start()
    for k in range(1, depth):
        for h in (0, 1):
            for sign in (-1, 1):
                there = at.z + sign * k
                exists = (there >= 0) & (there < depth)
                onward = at.z - sign
                goes_on = exists & (onward >= 0) & (onward < depth)

                @pl.when(exists)
                def _():
                    z_arrival(sign * k, h).wait_recv()

                @pl.when(goes_on)
                def _():
                    z_copy(sign * k, h, -sign).start()

                @pl.when(exists)
                def _():
                    y_copy(sign * k, h).start()

    for copy in own_copies:
        copy.wait()
    for copy in swap_copies(*swap, False):
        copy.wait_recv()
    for copy in swap_copies(*swap, True):
        copy.wait_send()
    for h in (0, 1):
        pl.when(has_up)(lambda: z_copy(0, h, 1).wait_send())
        pl.when(has_down)(lambda: z_copy(0, h, -1).wait_send())
    for k in range(-last, depth):
        there = at.z + k
        exists = (there >= 0) & (there < depth)
        sign = 1 if k > 0 else -1
        onward = at.z - sign
        goes_on = exists & (onward >= 0) & (onward < depth)
        for h in (0, 1):

            @pl.when(exists)
            def _():
                y_copy(k, h).wait()

            if k != 0:

                @pl.when(goes_on)
                def _():
                    z_copy(k, h, -sign).wait_send()


def gather_over_ep(block, pieces):
    rows, columns = block.shape
    depth = lax.axis_size("ep") // 2
    anywhere = pl.BlockSpec(memory_space=pl.ANY)
    slots = 2 * depth - 1
    out, pieces = pl.pallas_call(
        weights_kernel,
        out_shape=(
            jax.ShapeDtypeStruct((depth, 2, rows, columns), block.dtype),
            jax.ShapeDtypeStruct(pieces.shape, pieces.dtype),
        ),
        in_specs=[anywhere] * 2,
        out_specs=(anywhere,) * 2,
        scratch_shapes=[
            pltpu.SemaphoreType.DMA((2,)),
            pltpu.SemaphoreType.DMA((slots, 2, 2)),
            pltpu.SemaphoreType.DMA((slots, 2)),
            pltpu.SemaphoreType.DMA((slots, 2)),
            pltpu.SemaphoreType.DMA((slots, 2)),
            pltpu.SemaphoreType.DMA((2 * depth,)),
            pltpu.SemaphoreType.DMA((2 * depth,)),
        ],
        compiler_params=pltpu.CompilerParams(collective_id=3, has_side_effects=True),
        cost_estimate=pl.CostEstimate(
            flops=0, bytes_accessed=8 * depth * rows * columns, transcendentals=0
        ),
        name="gather_weights",
    )(block, pieces)
    return out.reshape(2 * depth * rows, columns), pieces


class RowGather:
    def __init__(self, at, mine, everywhere, z_send, z_recv, plane_send, plane_recv):
        self.at, self.mine, self.everywhere = at, mine, everywhere
        self.z_sems, self.plane_sems = (z_send, z_recv), (plane_send, plane_recv)
        self.half = mine.shape[0] // 2

    def block(self, j, y, x):
        return self.everywhere.at[self.at.behind(j), y, x, self.at.c]

    def plane_copy(self, j, kind):
        at, half = self.at, self.half
        if kind == 0:
            src, peer = self.block(j, at.y, at.x), at.next_x
        elif kind == 1:
            src, peer = self.block(j, at.y, at.x), at.next_y
        elif kind == 2:
            src, peer = self.block(j, at.y, 1 - at.x).at[pl.ds(0, half)], at.next_y
        elif kind == 3:
            src, peer = self.block(j, 1 - at.y, at.x).at[pl.ds(half, half)], at.next_x
        else:
            y, x = 1 - at.y if kind >= 6 else at.y, 1 - at.x if kind % 2 else at.x
            src, peer = self.block(j, y, x), at.next_core
        send, recv = self.plane_sems
        return remote(src, src, send.at[j, kind], recv.at[j, kind], peer)

    def z_copy(self, k):
        send, recv = self.z_sems
        dst = self.block(0, self.at.y, self.at.x)
        peer = self.at.at_z(self.at.ahead(k))
        return remote(self.mine, dst, send.at[k - 1], recv.at[k - 1], peer)

    def z_onward(self, j):
        send, recv = self.z_sems
        src = self.block(j, self.at.y, self.at.x)
        peer = self.at.at_z(self.at.z + 1)
        return remote(src, src, send.at[self.at.depth - 1 + j], recv.at[j], peer)

    def sends(self, k):
        down = self.at.z + k >= self.at.depth
        return down | (self.at.z + 1 < self.at.depth) if k == 1 else down

    def goes_on(self, j):
        return (self.at.z >= j) & (self.at.z + 1 < self.at.depth)

    def z_start(self):
        for k in range(1, self.at.depth):

            @pl.when(self.sends(k))
            def _():
                self.z_copy(k).start()

    def begin(self, j):
        if j > 0:
            send, recv = self.z_sems
            dst = self.block(j, self.at.y, self.at.x)
            peer = self.at.at_z(self.at.behind(j))
            remote(dst, dst, send.at[j - 1], recv.at[j - 1], peer).wait_recv()
            if j + 1 < self.at.depth:

                @pl.when(self.goes_on(j))
                def _():
                    self.z_onward(j).start()

        for kind in (0, 1, 4):
            self.plane_copy(j, kind).start()

    def spread(self, j):
        self.plane_copy(j, 0).wait_recv()
        self.plane_copy(j, 2).start()
        self.plane_copy(j, 5).start()
        self.plane_copy(j, 1).wait_recv()
        self.plane_copy(j, 3).start()
        self.plane_copy(j, 6).start()

    def last_hop(self, j):
        self.plane_copy(j, 2).wait_recv()
        self.plane_copy(j, 3).wait_recv()
        self.plane_copy(j, 7).start()

    def finish(self):
        for k in range(1, self.at.depth):

            @pl.when(self.sends(k))
            def _():
                self.z_copy(k).wait_send()

            if k + 1 < self.at.depth:

                @pl.when(self.goes_on(k))
                def _():
                    self.z_onward(k).wait_send()

        for j in range(self.at.depth):
            for kind in range(8):
                if kind >= 4:
                    self.plane_copy(j, kind).wait_recv()
                self.plane_copy(j, kind).wait_send()


def front_kernel(
    score_scale,
    block_in,
    weights_in,
    upstream_in,
    cos_in,
    sin_in,
    query_start,
    query_at,
    tokens_in,
    first_gain,
    gain_in,
    upstream_all,
    turned_out,
    k_out,
    v_out,
    q_out,
    lse_out,
    attended_out,
    resid_out,
    rows_out,
    normed,
    turned,
    qkv_w,
    out_w,
    k_all,
    v_all,
    scores_of,
    part,
    core_got,
    x_got,
    load_sem,
    z_send,
    z_recv,
    plane_send,
    plane_recv,
    kv_send,
    kv_recv,
    tp_send,
    tp_recv,
):
    at = Place()
    depth = at.depth
    count = 2 * depth
    heads, tokens, head = q_out.shape
    heads_width = heads * head
    windows = k_all.shape[1] // tokens
    quarter, width = resid_out.shape
    f32, bf16 = jnp.float32, jnp.bfloat16
    across = (((1,), (1,)), ((), ()))
    gather = RowGather(at, upstream_in, upstream_all, z_send, z_recv, plane_send, plane_recv)
    own = (windows - 1) * tokens

    def kv_copy(kind, w):
        held = (k_all, v_all)[kind]
        return remote(
            held.at[:, pl.ds(own, tokens)],
            held.at[:, pl.ds(w * tokens, tokens)],
            kv_send.at[kind, w],
            kv_recv.at[kind, w],
            (at.ep + (windows - 1 - w), at.tp),
        )

    def kv_arrival(kind, w):
        dst = (k_all, v_all)[kind].at[:, pl.ds(w * tokens, tokens)]
        peer = (at.ep - (windows - 1 - w), at.tp)
        return remote(dst, dst, kv_send.at[kind, w], kv_recv.at[kind, w], peer)

    def core_copy():
        return remote(part.at[:, 1 - at.c], core_got, tp_send.at[0], tp_recv.at[0], at.next_core)

    def x_copy():
        return remote(part.at[1 - at.x, at.c], x_got, tp_send.at[1], tp_recv.at[1], at.next_x)

    pairs = (
        (block_in, normed),
        (weights_in.at[:, pl.ds(0, 3 * heads_width)], qkv_w),
        (weights_in.at[:, pl.ds(3 * heads_width, heads_width)], out_w),
    )
    loads = [pltpu.make_async_copy(src, dst, load_sem.at[i]) for i, (src, dst) in enumerate(pairs)]
    for copy in loads:
        copy.start()
    at.greet_row()
    own_copy = pltpu.make_async_copy(
        upstream_in, gather.block(0, at.y, at.x), load_sem.at[len(pairs)]
    )
    own_copy.start()
    gather.z_start()
    own_copy.wait()
    gather.begin(0)
    loads[0].wait()
    few = 16

    def norm_body(i, carry):
        here = pl.ds(pl.multiple_of(i * few, few), few)
        inputs = normed[here].astype(f32)
        scale = lax.rsqrt(jnp.mean(inputs * inputs, axis=1, keepdims=True) + epsilon)
        normed[here] = (inputs * scale * first_gain[...]).astype(bf16)
        return carry

    lax.fori_loop(0, tokens // few, norm_body, 0, unroll=2)
    loads[1].wait()
    lane = lax.broadcasted_iota(jnp.int32, (tokens, head), 1)
    sign = jnp.where(lane < head // 2, -1.0, 1.0)

    def rotated(array):
        return array * cos_in[...] + pltpu.roll(array, head // 2, 1) * sign * sin_in[...]

    keys = jnp.dot(
        normed[...], qkv_w[:, heads_width : 2 * heads_width], preferred_element_type=f32
    )
    for h in range(heads):
        k_all[h, own:] = rotated(keys[:, h * head : (h + 1) * head]).astype(bf16)
    values = jnp.dot(normed[...], qkv_w[:, 2 * heads_width :], preferred_element_type=f32)
    for h in range(heads):
        v_all[h, own:] = values[:, h * head : (h + 1) * head].astype(bf16)
    for w in reversed(range(windows - 1)):

        @pl.when(at.ep + (windows - 1 - w) < count)
        def _():
            for kind in (0, 1):
                kv_copy(kind, w).start()

    gather.spread(0)
    queries = jnp.dot(normed[...], qkv_w[:, :heads_width], preferred_element_type=f32)
    for h in range(heads):
        q_out[h] = rotated(queries[:, h * head : (h + 1) * head]).astype(bf16)
    gather.last_hop(0)
    gather.begin(1)
    turned[...] = normed[...].T
    turned_copy = pltpu.make_async_copy(turned, turned_out, load_sem.at[0])
    turned_copy.start()
    gather.spread(1)
    for w in range(windows - 1):

        @pl.when(at.ep < windows - 1 - w)
        def _():
            for held in (k_all, v_all):
                held[:, w * tokens : (w + 1) * tokens] = jnp.zeros((heads, tokens, head), bf16)

        @pl.when(at.ep >= windows - 1 - w)
        def _():
            for kind in (0, 1):
                kv_arrival(kind, w).wait_recv()

    outs = [
        pltpu.make_async_copy(src, dst, load_sem.at[i])
        for i, (src, dst) in ((1, (k_all, k_out)), (3, (v_all, v_out)))
    ]
    for copy in outs:
        copy.start()
    due = [functools.partial(gather.last_hop, 1)]
    for j in range(2, depth):
        due.append(functools.partial(gather.begin, j))
        due.append(functools.partial(gather.spread, j))
        due.append(functools.partial(gather.last_hop, j))

    def head_body(h, carry):
        q = q_out[h]
        peak = jnp.full((1, tokens), -1e30, f32)
        for w in range(windows):
            some = slice(w * tokens, (w + 1) * tokens)
            scores = lax.dot_general(k_all[h, some], q, across, preferred_element_type=f32)
            key_at = lax.broadcasted_iota(jnp.int32, scores.shape, 0)
            key_at = key_at + (at.ep + w + 1 - windows) * tokens
            allowed = (key_at >= query_start[...]) & (key_at <= query_at[...])
            scores = jnp.where(allowed, scores * score_scale, -1e30)
            scores_of[w] = scores
            peak = jnp.maximum(peak, jnp.max(scores, axis=0, keepdims=True))
        total = jnp.zeros((1, tokens), f32)
        for w in range(windows):
            expo = jnp.exp(scores_of[w] - peak)
            scores_of[w] = expo
            total = total + jnp.sum(expo, axis=0, keepdims=True)
        lse_out[h] = peak + jnp.log(total)
        each = 1.0 / total
        attended = jnp.zeros((head, tokens), f32)
        for w in range(windows):
            some = slice(w * tokens, (w + 1) * tokens)
            probs = (scores_of[w] * each).astype(bf16)
            attended = attended + jnp.dot(
                v_all[h, some].T, probs, preferred_element_type=f32
            )
        here = pl.ds(pl.multiple_of(h * head, head), head)
        attended_out[:, here] = attended.T.astype(bf16)
        for i in range(heads):

            @pl.when(h == i)
            def _():
                for action in due[i : i + 1]:
                    action()

        return carry

    lax.fori_loop(0, heads, head_body, 0)
    loads[2].wait()
    strips = 4
    strip = width // strips
    for n in range(strips):
        some = slice(n * strip, (n + 1) * strip)
        product = lax.dot_general(
            attended_out[...], out_w[some], across, preferred_element_type=f32
        )
        part[:, :, :, some] = product.astype(bf16).reshape(2, 2, quarter, strip)
    core_copy().start()
    rest = due[heads:]
    for action in rest[:2]:
        action()
    core_copy().wait()
    for x in (0, 1):
        part[x, at.c] = part[x, at.c] + core_got[x]
    x_copy().start()
    for action in rest[2:]:
        action()
    x_copy().wait()

    def end_body(i, carry):
        here = pl.ds(pl.multiple_of(i * few, few), few)
        total = part[at.x, at.c, here].astype(f32) + x_got[here].astype(f32)
        resid = tokens_in[here].astype(f32) + total
        scale = lax.rsqrt(jnp.mean(resid * resid, axis=1, keepdims=True) + epsilon)
        resid_out[here] = resid
        rows_out[here] = (resid * scale * gain_in[...]).astype(bf16)
        return carry

    lax.fori_loop(0, quarter // few, end_body, 0)
    turned_copy.wait()
    for copy in outs:
        copy.wait()
    for w in range(windows - 1):

        @pl.when(at.ep + (windows - 1 - w) < count)
        def _():
            for kind in (0, 1):
                kv_copy(kind, w).wait_send()

    gather.finish()


def attention_front(block, weights, upstream, in_place, heads, scale):
    tokens, width = block.shape
    quarter, wide = upstream.shape
    depth = lax.axis_size("ep") // 2
    head, windows = HD, 3
    f32, bf16 = jnp.float32, jnp.bfloat16
    anywhere = pl.BlockSpec(memory_space=pl.ANY)
    in_vmem = pl.BlockSpec(memory_space=pltpu.VMEM)
    dma = pltpu.SemaphoreType.DMA
    shape = jax.ShapeDtypeStruct
    window = (heads, windows * tokens, head)
    outs = pl.pallas_call(
        functools.partial(front_kernel, scale),
        out_shape=(
            shape((depth, 2, 2, 2, quarter, wide), bf16),
            shape((width, tokens), bf16),
            shape(window, bf16),
            shape(window, bf16),
            shape((heads, tokens, head), bf16),
            shape((heads, 1, tokens), f32),
            shape((tokens, heads * head), bf16),
            shape((quarter, width), f32),
            shape((quarter, width), bf16),
        ),
        in_specs=[anywhere] * 3 + [in_vmem] * len(in_place),
        out_specs=(anywhere,) * 4 + (in_vmem,) * 5,
        scratch_shapes=[
            pltpu.VMEM((tokens, width), bf16),
            pltpu.VMEM((width, tokens), bf16),
            pltpu.VMEM((width, 3 * heads * head), bf16),
            pltpu.VMEM((width, heads * head), bf16),
            pltpu.VMEM(window, bf16),
            pltpu.VMEM(window, bf16),
            pltpu.VMEM((windows, tokens, tokens), f32),
            pltpu.VMEM((2, 2, quarter, width), bf16),
            pltpu.VMEM((2, quarter, width), bf16),
            pltpu.VMEM((quarter, width), bf16),
            dma((4,)),
            dma((2 * depth,)),
            dma((depth - 1,)),
            dma((depth, 8)),
            dma((depth, 8)),
            dma((2, windows - 1)),
            dma((2, windows - 1)),
            dma((2,)),
            dma((2,)),
        ],
        compiler_params=pltpu.CompilerParams(
            collective_id=5, has_side_effects=True, vmem_limit_bytes=50 * 2**20
        ),
        cost_estimate=pl.CostEstimate(
            flops=8 * tokens * width * heads * head,
            bytes_accessed=2 * 8 * depth * quarter * wide,
            transcendentals=heads * tokens * windows * tokens,
        ),
        name="attention_front",
    )(block, weights, upstream, *in_place)
    return (outs[0].reshape(8 * depth * quarter, wide),) + tuple(outs[1:])


def back_kernel(
    units,
    score_scale,
    d_low_in,
    weights_in,
    q_in,
    k_in,
    v_in,
    turned_in,
    block_in,
    rows_in,
    d_pair_in,
    upstream_in,
    weighted_in,
    lse_in,
    query_start,
    query_at,
    cos_in,
    sin_in,
    own_rows_in,
    gain_in,
    d_resid_in,
    gain_two_in,
    side_in,
    out,
    small_out,
    block_out,
    d_rows_out,
    pieces_got,
    gate_out,
    up_out,
    down_out,
    qkv_w,
    turned,
    d_out,
    d_got,
    d_own,
    d_proj,
    part,
    core_got,
    x_got,
    d_rows,
    own,
    y_out,
    hop,
    from_z,
    small_own,
    small_hop,
    small_z,
    small,
    small_got,
    pieces,
    load_sem,
    d_send,
    d_recv,
    tp_send,
    tp_recv,
    y_send,
    y_recv,
    z_send,
    z_recv,
    little_send,
    little_recv,
    small_send,
    small_recv,
    swap_send,
    swap_recv,
    rows_send,
    rows_recv,
    own_sem,
    tile_sem,
    store_sem,
    strip_sem,
):
    at = Place()
    depth = at.depth
    count = 2 * depth
    heads, tokens, head = q_in.shape
    heads_width = heads * head
    windows = k_in.shape[1] // tokens
    quarter, width = d_rows.shape
    rows = out.shape[0]
    f32, bf16 = jnp.float32, jnp.bfloat16
    across = (((1,), (1,)), ((), ()))
    slot_here, slot_hidden, shared_hidden = units
    routed = slot_here * slot_hidden
    hidden = weighted_in.shape[2]
    few = 16

    def d_copy(w, h):
        peer = (at.ep - (2 - w), at.tp)
        return remote(d_out.at[w, h], d_got.at[w, h], d_send.at[w, h], d_recv.at[w, h], peer)

    def d_arrival(w, h):
        peer = (at.ep + (2 - w), at.tp)
        dst = d_got.at[w, h]
        return remote(dst, dst, d_send.at[w, h], d_recv.at[w, h], peer)

    def core_copy():
        return remote(part.at[:, 1 - at.c], core_got, tp_send.at[0], tp_recv.at[0], at.next_core)

    def x_copy():
        return remote(part.at[1 - at.x, at.c], x_got, tp_send.at[1], tp_recv.at[1], at.next_x)

    cuts = (pl.ds(0, heads_width), pl.ds(heads_width, 2 * heads_width))

    def y_copy(q, j):
        return remote(
            y_out.at[j, :, cuts[q]], hop.at[j, :, cuts[q]], y_send.at[q, j], y_recv.at[q, j], at.next_y
        )

    def z_copy(q, j):
        return remote(
            own.at[j, :, cuts[q]],
            from_z.at[j - 1, :, cuts[q]],
            z_send.at[q, j],
            z_recv.at[q, j],
            at.at_z(at.ahead(j)),
        )

    def little_y(j):
        return remote(
            small_own.at[at.ahead(j), 1 - at.y],
            small_hop.at[j],
            little_send.at[0, j],
            little_recv.at[0, j],
            at.next_y,
        )

    def little_z(j):
        return remote(
            small_own.at[at.ahead(j), at.y],
            small_z.at[j - 1],
            little_send.at[1, j],
            little_recv.at[1, j],
            at.at_z(at.ahead(j)),
        )

    def small_copy(kind):
        peer = at.next_core if kind == 0 else at.next_x
        return remote(
            small.at[kind], small_got.at[kind], small_send.at[kind], small_recv.at[kind], peer
        )

    ends = ((block_in, block_out), (d_rows, d_rows_out))

    def rows_copy(a, kind):
        mine, gathered = ends[a]
        if kind == 2:
            src = dst = gathered.at[1 - at.x, at.c]
        else:
            src, dst = mine, gathered.at[at.x, at.c]
        peer = at.next_x if kind == 0 else at.next_core
        return remote(src, dst, rows_send.at[a, kind], rows_recv.at[a, kind], peer)

    def rows_own(a):
        mine, gathered = ends[a]
        return pltpu.make_async_copy(mine, gathered.at[at.x, at.c], own_sem.at[a])

    def rows_begin(a):
        for kind in (0, 1):
            rows_copy(a, kind).start()
        rows_own(a).start()

    def rows_pass_on(a):
        rows_copy(a, 0).wait_recv()
        rows_copy(a, 2).start()

    def rows_end(a):
        rows_own(a).wait()
        rows_copy(a, 0).wait_send()
        rows_copy(a, 1).wait()
        rows_copy(a, 2).wait()

    def swap_copies(p, leave):
        some = pl.ds(p * shared_hidden, shared_hidden)
        copies = []
        for k in range(1, count):
            to, back = lax.rem(at.ep + k, count), lax.rem(at.ep + count - k, count)
            if leave:
                src, dst, peer = pieces.at[to, some], pieces_got.at[at.ep, some], to
            else:
                src, dst, peer = pieces.at[back, some], pieces_got.at[back, some], back
            copies.append(remote(src, dst, swap_send.at[p, k], swap_recv.at[p, k], (peer, at.tp)))
        return copies

    def swap_own(p):
        some = pl.ds(p * shared_hidden, shared_hidden)
        return pltpu.make_async_copy(
            pieces.at[at.ep, some], pieces_got.at[at.ep, some], own_sem.at[2 + p]
        )

    strips = 4
    strip = width // strips

    def load_strip(n):
        src = weights_in.at[pl.ds(n * strip, strip), pl.ds(0, 3 * heads_width)]
        return pltpu.make_async_copy(src, qkv_w.at[n % 2], strip_sem.at[n % 2])

    late_load = pltpu.make_async_copy(turned_in, turned, load_sem.at[1])
    lane = lax.broadcasted_iota(jnp.int32, (tokens, head), 1)
    sign = jnp.where(lane < head // 2, -1.0, 1.0)

    def unrotated(grads):
        turned_part = pltpu.roll(grads * sin_in[...], head // 2, 1) * sign
        return grads * cos_in[...] - turned_part

    def attention(d_low, out_w, q_all, k_all, v_all, d_att, probs, d_probs):
        pairs = (
            (d_low_in, d_low),
            (weights_in.at[:, pl.ds(3 * heads_width, heads_width)], out_w),
            (q_in, q_all),
            (k_in, k_all),
            (v_in, v_all),
        )
        copies = [
            pltpu.make_async_copy(src, dst, load_sem.at[2 + i])
            for i, (src, dst) in enumerate(pairs)
        ]
        for copy in copies + [late_load, load_strip(0), load_strip(1)]:
            copy.start()
        at.greet_row()
        rows_begin(0)
        copies[0].wait()
        copies[1].wait()
        d_attended = jnp.dot(d_low[...], out_w[...], preferred_element_type=f32).astype(bf16)
        for h in range(heads):
            d_att[h] = d_attended[:, h * head : (h + 1) * head]
        for copy in copies[2:]:
            copy.wait()

        def head_body(h, carry):
            queries, d_a = q_all[h], d_att[h]
            delta = jnp.zeros((1, tokens), f32)
            for w in range(windows):
                some = slice(w * tokens, (w + 1) * tokens)
                scores = lax.dot_general(
                    k_all[h, some], queries, across, preferred_element_type=f32
                )
                key_at = lax.broadcasted_iota(jnp.int32, scores.shape, 0)
                key_at = key_at + (at.ep + w + 1 - windows) * tokens
                allowed = (key_at >= query_start[...]) & (key_at <= query_at[...])
                p = jnp.where(allowed, jnp.exp(scores * score_scale - lse_in[h]), 0.0)
                d_p = lax.dot_general(v_all[h, some], d_a, across, preferred_element_type=f32)
                probs[w] = p
                d_probs[w] = d_p
                delta = delta + jnp.sum(p * d_p, axis=0, keepdims=True)
            d_queries = jnp.zeros((head, tokens), f32)
            for w in range(windows):
                some = slice(w * tokens, (w + 1) * tokens)
                p = probs[w]
                d_scores = (p * (d_probs[w] - delta)).astype(bf16)
                d_keys = jnp.dot(d_scores, queries, preferred_element_type=f32) * score_scale
                d_values = jnp.dot(p.astype(bf16), d_a, preferred_element_type=f32)
                if w < windows - 1:
                    d_out[w, h, :, :head] = d_keys.astype(bf16)
                    d_out[w, h, :, head:] = d_values.astype(bf16)

                    @pl.when(at.ep >= 2 - w)
                    def _():
                        d_copy(w, h).start()

                else:
                    d_own[h, :, :head] = d_keys
                    d_own[h, :, head:] = d_values
                d_queries = d_queries + jnp.dot(
                    k_all[h, some].T, d_scores, preferred_element_type=f32
                )
            here = pl.ds(pl.multiple_of(h * head, head), head)
            d_proj[:, here] = unrotated((d_queries * score_scale).T).astype(bf16)
            return carry

        lax.fori_loop(0, heads, head_body, 0)

    pl.run_scoped(
        attention,
        pltpu.VMEM((tokens, width), bf16),
        pltpu.VMEM((width, heads_width), bf16),
        pltpu.VMEM((heads, tokens, head), bf16),
        pltpu.VMEM((heads, windows * tokens, head), bf16),
        pltpu.VMEM((heads, windows * tokens, head), bf16),
        pltpu.VMEM((heads, tokens, head), bf16),
        pltpu.VMEM((windows, tokens, tokens), f32),
        pltpu.VMEM((windows, tokens, tokens), f32),
    )
    order = [j for j in range(1, depth)] + [0]

    def own_body(h, carry):
        for w in range(windows - 1):

            @pl.when(at.ep + (2 - w) < count)
            def _():
                d_arrival(w, h).wait_recv()
                d_own[h] += d_got[w, h].astype(f32)

        k_here = pl.ds(pl.multiple_of(heads_width + h * head, head), head)
        v_here = pl.ds(pl.multiple_of(2 * heads_width + h * head, head), head)
        d_proj[:, k_here] = unrotated(d_own[h, :, :head]).astype(bf16)
        d_proj[:, v_here] = d_own[h, :, head:].astype(bf16)
        return carry

    def weight_rows(into, q, z, y):
        here = pl.ds(pl.multiple_of((z * 2 + y) * rows, rows), rows)
        product = jnp.dot(turned[here], d_proj[:, cuts[q]], preferred_element_type=f32)
        into[:, cuts[q]] = product.astype(bf16)

    def begin_sums(q):
        for j in order:
            weight_rows(y_out.at[j], q, at.ahead(j), 1 - at.y)
            y_copy(q, j).start()

    def own_sums(q):
        for j in order:
            weight_rows(own.at[j], q, at.ahead(j), at.y)

    def projections():
        lax.fori_loop(0, heads, own_body, 0)
        for n in range(strips):
            some = slice(n * strip, (n + 1) * strip)
            load_strip(n).wait()
            product = lax.dot_general(
                d_proj[...], qkv_w[n % 2], across, preferred_element_type=f32
            )
            part[:, :, :, some] = product.astype(bf16).reshape(2, 2, quarter, strip)
            if n + 2 < strips:
                load_strip(n + 2).start()
        core_copy().start()
        begin_sums(1)
        core_copy().wait()
        for x in (0, 1):
            part[x, at.c] = part[x, at.c] + core_got[x]
        x_copy().start()
        own_sums(1)
        x_copy().wait()

        def end_body(i, carry):
            here = pl.ds(pl.multiple_of(i * few, few), few)
            grads = part[at.x, at.c, here].astype(f32) + x_got[here].astype(f32)
            inputs = own_rows_in[here].astype(f32)
            scale = lax.rsqrt(jnp.mean(inputs * inputs, axis=1, keepdims=True) + epsilon)
            unit_rows = inputs * scale
            scaled = grads * gain_in[...]
            inner = jnp.mean(scaled * unit_rows, axis=1, keepdims=True)
            total = d_resid_in[here] + scale * (scaled - unit_rows * inner)
            d_rows[here] = total.astype(bf16)
            return carry + jnp.sum(grads * unit_rows, axis=0, keepdims=True)

        d_gain = lax.fori_loop(0, quarter // few, end_body, jnp.zeros((1, width), f32))
        rows_begin(1)
        line = lax.broadcasted_iota(jnp.int32, (128, rows), 0)
        for e in range(count):
            some = slice(e * rows, (e + 1) * rows)
            gains = jnp.where(line == 0, d_gain[:, some], 0.0)
            gains = jnp.where(line == 1, gain_two_in[:, some], gains)
            small_own[e // 2, e % 2] = (gains.T + side_in[some]).astype(bf16)
        for j in order:
            little_y(j).start()

    def after_y(q, j):
        y_copy(q, j).wait_recv()

        def body(i, carry):
            some = pl.ds(pl.multiple_of(i * few, few), few)
            own[j, some, cuts[q]] = own[j, some, cuts[q]] + hop[j, some, cuts[q]]
            return carry

        lax.fori_loop(0, rows // few, body, 0)
        if j > 0:
            z_copy(q, j).start()

    def after_little():
        for j in order:
            little_y(j).wait_recv()
            here = small_own.at[at.ahead(j), at.y]
            here[...] = here[...] + small_hop[j]
            if j > 0:
                little_z(j).start()

    hooks = {(0, 0): [functools.partial(rows_pass_on, 0)]}
    for i, j in enumerate(order):
        here = (1, min(count // 2 + i, count - 1))
        hooks.setdefault(here, []).append(functools.partial(after_y, 0, j))
    hooks[(2, 2)] = [functools.partial(rows_pass_on, 1)]
    hooks[(2, 3)] = [after_little]
    last_hooks = []
    for i, j in enumerate(order):
        when = 2 + 5 * i
        due = functools.partial(after_y, 1, j)
        if when < count:
            hooks.setdefault((2, when), []).append(due)
        else:
            last_hooks.append(due)

    def weight_gradients(turned_left, left_tile, right_part, staging):
        lefts = (
            lambda tile: d_pair_in.at[tile, :, pl.ds(0, hidden)],
            lambda tile: d_pair_in.at[tile, :, pl.ds(hidden, hidden)],
            lambda tile: weighted_in.at[tile],
        )
        rights = (rows_in, rows_in, upstream_in)
        results = (gate_out, up_out, down_out)
        columns = width // count

        def load_left(p, tile):
            slot = lax.rem(tile, 2)
            return pltpu.make_async_copy(
                lefts[p](tile), left_tile.at[slot], tile_sem.at[0, slot]
            )

        def load_right(p, n):
            slot = lax.rem(n, 2)
            here = pl.ds(pl.multiple_of(n * columns, columns), columns)
            return pltpu.make_async_copy(
                rights[p].at[:, :, here], right_part.at[slot], tile_sem.at[1, slot]
            )

        def store(p, n):
            slot = lax.rem(n, 2)
            here = pl.ds(pl.multiple_of(n * columns, columns), columns)
            return pltpu.make_async_copy(
                staging.at[slot], results[p].at[:, here], store_sem.at[slot]
            )

        def turn_left(p, tile):
            load_left(p, tile).wait()

            @pl.when(tile + 1 < count)
            def _():
                load_left(p, tile + 1).start()

            here = pl.ds(pl.multiple_of(tile * tokens, tokens), tokens)
            turned_left[:, here] = left_tile[lax.rem(tile, 2)].T

        def run_pass(p):
            def part_body(n, carry):
                slot = lax.rem(n, 2)
                load_right(p, n).wait()

                @pl.when(n + 1 < count)
                def _():
                    load_right(p, n + 1).start()

                if p < 2:

                    @pl.when(n + 1 == count)
                    def _():
                        load_right(p + 1, 0).start()

                @pl.when(n >= 2)
                def _():
                    store(p, n - 2).wait()

                product = jnp.dot(
                    turned_left[...],
                    right_part[slot].reshape(count * tokens, columns),
                    preferred_element_type=f32,
                )
                staging[slot] = product[:routed].astype(bf16)
                pieces[n, p * shared_hidden : (p + 1) * shared_hidden] = product[
                    routed : routed + shared_hidden
                ].astype(bf16)
                store(p, n).start()
                for (hook_pass, hook_part), actions in hooks.items():
                    if hook_pass == p:

                        @pl.when(n == hook_part)
                        def _():
                            for action in actions:
                                action()

                return carry

            def turn_body(tile, carry):
                turn_left(p, tile)
                return carry

            lax.fori_loop(0, count, turn_body, 0)
            if p < 2:
                load_left(p + 1, 0).start()
            lax.fori_loop(0, count, part_body, 0)
            for n in (count - 2, count - 1):
                store(p, n).wait()
            swap_own(p).start()
            if p > 0:
                start_swap(p)

        def start_swap(p):
            for copy in swap_copies(p, True):
                copy.start()

        hooks.setdefault((1, count - 2), []).append(functools.partial(start_swap, 0))
        load_left(0, 0).start()
        load_right(0, 0).start()
        late_load.wait()
        begin_sums(0)
        own_sums(0)

        run_pass(0)
        run_pass(1)
        projections()
        run_pass(2)
        for action in last_hooks:
            action()

    pl.run_scoped(
        weight_gradients,
        pltpu.VMEM((hidden, count * tokens), bf16),
        pltpu.VMEM((2, tokens, hidden), bf16),
        pltpu.VMEM((2, count, tokens, width // count), bf16),
        pltpu.VMEM((2, routed, width // count), bf16),
    )
    total = small_own[at.z, at.y].astype(f32)
    for j in range(1, depth):
        little_z(j).wait_recv()
        total = total + small_z[j - 1].astype(f32)
    for kind in (0, 1):
        small[kind] = total
        small_copy(kind).start()
        small_copy(kind).wait()
        total = small[kind] + small_got[kind]
    small_out[...] = total
    for j in range(1, depth):
        for q in (0, 1):
            z_copy(q, j).wait_recv()

    def total_body(i, carry):
        some = pl.ds(pl.multiple_of(i * few, few), few)
        result = own[0, some].astype(f32)
        for k in range(depth - 1):
            result = result + from_z[k, some].astype(f32)
        out[some] = result
        return carry

    lax.fori_loop(0, rows // few, total_body, 0)
    for j in range(depth):
        little_y(j).wait_send()
        if j > 0:
            little_z(j).wait_send()
        for q in (0, 1):
            y_copy(q, j).wait_send()
            if j > 0:
                z_copy(q, j).wait_send()
    for a in (0, 1):
        rows_end(a)
    for p in range(3):
        swap_own(p).wait()
        for copy in swap_copies(p, False):
            copy.wait_recv()
        for copy in swap_copies(p, True):
            copy.wait_send()

    def finish(h, carry):
        for w in range(windows - 1):

            @pl.when(at.ep >= 2 - w)
            def _():
                d_copy(w, h).wait_send()

        return carry

    lax.fori_loop(0, heads, finish, 0)


def backward(large, tiles_of, in_place, units, scale):
    d_low, _, queries, keys = large[:4]
    heads, tokens, head = queries.shape
    width = d_low.shape[1]
    ep_count = lax.axis_size("ep")
    depth, rows = ep_count // 2, width // ep_count
    quarter = tokens // lax.axis_size("tp")
    windows = keys.shape[1] // tokens
    columns = 3 * heads * head
    hidden = tiles_of[3].shape[2]
    slot_here, slot_hidden, shared_hidden = units
    f32, bf16 = jnp.float32, jnp.bfloat16
    anywhere = pl.BlockSpec(memory_space=pl.ANY)
    in_vmem = pl.BlockSpec(memory_space=pltpu.VMEM)
    dma = pltpu.SemaphoreType.DMA
    pieces = (ep_count, 3 * shared_hidden, rows)
    gathered = jax.ShapeDtypeStruct((2, 2, quarter, width), bf16)
    routed = jax.ShapeDtypeStruct((slot_here * slot_hidden, width), bf16)

    def vmem(*shape, dtype=bf16):
        return pltpu.VMEM(shape, dtype)

    out, small, block_out, d_rows, pieces, gate, up, down = pl.pallas_call(
        functools.partial(back_kernel, units, scale),
        out_shape=(
            jax.ShapeDtypeStruct((rows, columns), f32),
            jax.ShapeDtypeStruct((rows, 128), f32),
            gathered,
            gathered,
            jax.ShapeDtypeStruct(pieces, bf16),
            routed,
            routed,
            routed,
        ),
        in_specs=[anywhere] * (len(large) + len(tiles_of)) + [in_vmem] * len(in_place),
        out_specs=(in_vmem, in_vmem) + (anywhere,) * 6,
        scratch_shapes=[
            vmem(2, width // 4, columns),
            vmem(width, tokens),
            vmem(windows - 1, heads, tokens, 2 * head),
            vmem(windows - 1, heads, tokens, 2 * head),
            vmem(heads, tokens, 2 * head, dtype=f32),
            vmem(tokens, columns),
            vmem(2, 2, quarter, width),
            vmem(2, quarter, width),
            vmem(quarter, width),
            vmem(quarter, width),
            vmem(depth, rows, columns),
            vmem(depth, rows, columns),
            vmem(depth, rows, columns),
            vmem(depth - 1, rows, columns),
            vmem(depth, 2, rows, 128),
            vmem(depth, rows, 128),
            vmem(depth - 1, rows, 128),
            vmem(2, rows, 128, dtype=f32),
            vmem(2, rows, 128, dtype=f32),
            vmem(*pieces),
            dma((7,)),
            dma((windows - 1, heads)),
            dma((windows - 1, heads)),
            dma((2,)),
            dma((2,)),
            dma((2, depth)),
            dma((2, depth)),
            dma((2, depth)),
            dma((2, depth)),
            dma((2, depth)),
            dma((2, depth)),
            dma((2,)),
            dma((2,)),
            dma((3, ep_count)),
            dma((3, ep_count)),
            dma((2, 3)),
            dma((2, 3)),
            dma((5,)),
            dma((2, 2)),
            dma((2,)),
            dma((2,)),
        ],
        compiler_params=pltpu.CompilerParams(
            collective_id=4, has_side_effects=True, vmem_limit_bytes=62 * 2**20
        ),
        cost_estimate=pl.CostEstimate(
            flops=6 * ep_count * tokens * width * hidden,
            bytes_accessed=8 * ep_count * tokens * width,
            transcendentals=heads * tokens * windows * tokens,
        ),
        name="backward",
    )(*large, *tiles_of, *in_place)
    block_out, d_rows = [array.reshape(4 * quarter, width) for array in (block_out, d_rows)]
    return out, small, block_out, d_rows, pieces, (gate, up, down)


def shared_pieces(weights, ep_count):
    rows, hidden = weights[0].shape
    units = hidden // ep_count
    return jnp.concatenate([weight.T.reshape(ep_count, units, rows) for weight in weights], axis=1)


def shared_whole(pieces, count):
    ep_count, units, columns = pieces.shape
    units = units // count
    pieces = pieces.reshape(ep_count, count, units, columns).astype(jnp.float32)
    return [pieces[:, i].reshape(ep_count * units, columns).T for i in range(count)]


def dense_body(
    tokens,
    lengths,
    routes,
    attn_gain,
    w_query,
    w_key,
    w_value,
    w_out,
    ffn_gain,
    w_router,
    shared_mix,
    shared_gate,
    shared_up,
    shared_down,
    expert_gate,
    expert_up,
    expert_down,
    cotangent,
):
    rows_here, width = tokens.shape
    ep_count = lax.axis_size("ep")
    tp_count = lax.axis_size("tp")
    ep_index = lax.axis_index("ep")
    offset = ep_index * rows_here
    quarter = rows_here // tp_count
    first_row = lax.axis_index("tp") * quarter
    slot_here, slot_hidden = expert_gate.shape[0], expert_gate.shape[1]
    expert_count = w_router.shape[1]
    bf16, f32 = jnp.bfloat16, jnp.float32

    def my_rows(array):
        return lax.dynamic_slice_in_dim(array, first_row, quarter, 0)

    side_columns = jnp.concatenate(
        [attn_gain[:, None], ffn_gain[:, None], shared_mix[:, None], w_router], axis=1
    )
    side_columns = jnp.pad(side_columns, ((0, 0), (0, -side_columns.shape[1] % 128)))
    joined_weights, pieces = gather_over_ep(
        jnp.concatenate([w_query, w_key, w_value, w_out, side_columns], axis=1),
        shared_pieces((shared_gate, shared_up, shared_down), ep_count),
    )
    heads_width = w_query.shape[1]
    side_weight = joined_weights[:, 4 * heads_width :]
    picked = jnp.any(
        my_rows(routes)[:, :, None] == jnp.arange(expert_count, dtype=jnp.int32), axis=1
    )
    picked_lanes = jnp.pad(picked.astype(bf16), ((0, 0), (3, 125 - expert_count)))
    upstream_rows = jnp.concatenate([my_rows(cotangent), picked_lanes], axis=1)
    shared_units = pieces.shape[1] // 3
    routed_units = slot_here * slot_hidden
    heads_here = heads_width // HD
    score_scale = HD ** (-0.5)
    first_norm_scale = side_weight[:, 0].astype(f32)
    second_norm_scale = side_weight[:, 1].astype(f32)
    query_at = offset + jnp.arange(rows_here, dtype=jnp.int32)
    _, query_pos = sequence_info(lengths, query_at)
    cosine, sine = rope_tables(query_pos, HD)
    tables = (cosine[:, 0], sine[:, 0], (query_at - query_pos)[None, :], query_at[None, :])
    (
        upstream_all,
        normed_one_turned,
        keys_win,
        values_win,
        queries,
        log_total,
        attended,
        resid,
        normed_two,
    ) = attention_front(
        tokens,
        joined_weights,
        upstream_rows,
        tables + (my_rows(tokens), first_norm_scale[None, :], second_norm_scale[None, :]),
        heads_here,
        score_scale,
    )
    (
        normed_all,
        weighted_h,
        d_pair_pre,
        block_rows,
        d_resid_low,
        d_resid,
        grad_gain_two,
        d_side,
    ) = ffn_over_all(
        normed_two,
        upstream_all,
        (expert_gate, expert_up, expert_down),
        pieces,
        joined_weights,
        resid,
        second_norm_scale[None, :],
        (slot_here, slot_hidden, shared_units),
        expert_count,
    )
    grad_side = jnp.dot(normed_two.astype(f32).T, d_side, precision=highest)
    grad_out = jnp.einsum("td,th->dh", d_resid_low, attended, preferred_element_type=f32)
    grad_out = lax.psum_scatter(
        grad_out.astype(bf16), "ep", scatter_dimension=0, tiled=True
    ).astype(f32)
    tile_shape = (ep_count, rows_here, -1)
    tiles_of = tuple(
        array.reshape(tile_shape) for array in (normed_all, d_pair_pre, upstream_all, weighted_h)
    )
    units = (slot_here, slot_hidden, shared_units)
    column = jnp.arange(128, dtype=jnp.int32)
    large = (
        d_resid_low,
        joined_weights,
        queries,
        keys_win,
        values_win,
        normed_one_turned,
        block_rows,
    )
    in_place = (
        log_total,
        tables[2],
        tables[3],
        tables[0],
        tables[1],
        my_rows(tokens),
        first_norm_scale[None, :],
        d_resid,
        grad_gain_two[None, :],
        jnp.where(column >= 2, grad_side, 0.0),
    )
    grad_weights, small, block_out, grad_tokens, grad_pieces, grad_experts = backward(
        large, tiles_of, in_place, units, score_scale
    )
    grad_shared = shared_whole(grad_pieces, 3)
    grad_tokens = grad_tokens.astype(f32)
    grad_experts = [grad.astype(f32).reshape(expert_gate.shape) for grad in grad_experts]
    parts = [grad_weights[:, i * heads_width : (i + 1) * heads_width] for i in range(3)]
    return (
        block_out,
        grad_tokens,
        small[:, 0],
        parts[0],
        parts[1],
        parts[2],
        grad_out,
        small[:, 1],
        small[:, 3 : 3 + expert_count],
        small[:, 2],
        grad_shared[0],
        grad_shared[1],
        grad_shared[2],
        grad_experts[0],
        grad_experts[1],
        grad_experts[2],
    )


def chosen_body(*arrays):
    rows_here, top_count = arrays[2].shape
    slot_here, expert_count = arrays[14].shape[0], arrays[9].shape[1]
    capacity = rows_here * top_count * 7 // (5 * expert_count)
    grid_of_two = lax.axis_size("ep") % 2 == 0 and lax.axis_size("tp") == 4
    if grid_of_two and rows_here < 2 * slot_here * capacity:
        return dense_body(*arrays)
    return body(*arrays)


def solution(mesh):
    placed = (
        P("ep", None),
        P(),
        P("ep", None),
        P("ep"),
        P("ep", "tp"),
        P("ep", "tp"),
        P("ep", "tp"),
        P("ep", "tp"),
        P("ep"),
        P("ep", None),
        P("ep"),
        P("ep", "tp"),
        P("ep", "tp"),
        P("ep", "tp"),
        P("ep", "tp", None),
        P("ep", "tp", None),
        P("ep", "tp", None),
        P("ep", None),
    )
    return jax.shard_map(
        chosen_body,
        mesh=mesh,
        in_specs=placed,
        out_specs=(
            P("ep", None),
            P("ep", None),
            P("ep"),
            P("ep", "tp"),
            P("ep", "tp"),
            P("ep", "tp"),
            P("ep", "tp"),
            P("ep"),
            P("ep", None),
            P("ep"),
            P("ep", "tp"),
            P("ep", "tp"),
            P("ep", "tp"),
            P("ep", "tp", None),
            P("ep", "tp", None),
            P("ep", "tp", None),
        ),
        check_vma=False,
    )
```

```python
import functools

import jax
import jax.numpy as jnp
from jax import lax
from jax.experimental import pallas as pl
from jax.experimental.pallas import tpu as pltpu
from jax.sharding import PartitionSpec as P

HD = 128


epsilon = 1e-06
rope_base = 1000000.0
highest = lax.Precision.HIGHEST
MESH = pl.DeviceIdType.MESH


def passed_along(block, axis, distance):
    devices = range(lax.axis_size(axis))
    route = [(i - distance, i) for i in devices if i - distance in devices]
    return lax.ppermute(block, axis, route)


def rope_tables(positions, width):
    steps = jnp.arange(0, width, 2, dtype=jnp.float32) / width
    inverse = rope_base ** (-steps)
    angles = positions.astype(jnp.float32)[:, None] * inverse[None, :]
    angles = jnp.concatenate([angles, angles], axis=-1)
    return (jnp.cos(angles)[:, None, :], jnp.sin(angles)[:, None, :])


def turn_half(values):
    middle = values.shape[-1] // 2
    return jnp.concatenate([-values[..., middle:], values[..., :middle]], axis=-1)


def rotate(values, cosine, sine):
    return values * cosine + turn_half(values) * sine


def unrotate(grads, cosine, sine):
    return grads * cosine - turn_half(grads * sine)


def sequence_info(lengths, indices):
    starts = jnp.cumsum(lengths) - lengths
    inside = starts[None, :] <= indices[:, None]
    segment = jnp.sum(inside.astype(jnp.int32), axis=1) - 1
    first = jnp.max(jnp.where(inside, starts[None, :], -1), axis=1)
    return (segment, indices - first)


def norm_forward(values, gain):
    scale = lax.rsqrt(jnp.mean(values * values, axis=-1, keepdims=True) + epsilon)
    return (values * scale * gain, scale)


def norm_backward(values, scale, gain, grads):
    unit = values * scale
    scaled = grads * gain
    inner = jnp.mean(scaled * unit, axis=-1, keepdims=True)
    return (scale * (scaled - unit * inner), jnp.sum(grads * unit, axis=0))


def deliver(rows):
    arrived_rows = lax.all_to_all(rows, "ep", split_axis=0, concat_axis=0, tiled=True)
    return arrived_rows


def bring_back(parts, target, rows_here, top_count):
    moved = lax.all_to_all(parts, "ep", split_axis=0, concat_axis=0, tiled=True)
    piece = moved.shape[3]
    return moved.reshape(-1, piece)[target].reshape(rows_here, top_count, piece)


def body(
    tokens,
    lengths,
    routes,
    attn_gain,
    w_query,
    w_key,
    w_value,
    w_out,
    ffn_gain,
    w_router,
    shared_mix,
    shared_gate,
    shared_up,
    shared_down,
    expert_gate,
    expert_up,
    expert_down,
    cotangent,
):
    rows_here = tokens.shape[0]
    width = tokens.shape[1]
    ep_count = lax.axis_size("ep")
    offset = lax.axis_index("ep") * rows_here
    slot_here = expert_gate.shape[0]
    top_count = routes.shape[1]
    gathered = (
        lax.all_gather(attn_gain, "ep", axis=0, tiled=True),
        lax.all_gather(w_query, "ep", axis=0, tiled=True),
        lax.all_gather(w_key, "ep", axis=0, tiled=True),
        lax.all_gather(w_value, "ep", axis=0, tiled=True),
        lax.all_gather(w_out, "ep", axis=0, tiled=True),
        lax.all_gather(ffn_gain, "ep", axis=0, tiled=True),
        lax.all_gather(w_router, "ep", axis=0, tiled=True),
        lax.all_gather(shared_mix, "ep", axis=0, tiled=True),
        lax.all_gather(shared_gate, "ep", axis=0, tiled=True),
        lax.all_gather(shared_up, "ep", axis=0, tiled=True),
        lax.all_gather(shared_down, "ep", axis=0, tiled=True),
    )
    (
        gain_first,
        query_weight_matrix,
        key_weight_matrix,
        value_weight_matrix,
        output_weight,
        gain_second,
        router_weight,
        shared_mixer_weight,
        shared_gate_weight,
        shared_up_weight,
        shared_down_weight,
    ) = gathered
    expert_count = router_weight.shape[1]
    capacity = (rows_here * top_count * 7 // (5 * expert_count) + 7) // 8 * 8
    heads_here = query_weight_matrix.shape[1] // HD
    score_scale = HD ** (-0.5)
    first_norm_scale = gain_first.astype(jnp.float32)
    second_norm_scale = gain_second.astype(jnp.float32)
    layer_input = tokens.astype(jnp.float32)
    normed_wide, norm_one = norm_forward(layer_input, first_norm_scale)
    normed_one = normed_wide.astype(jnp.bfloat16)
    query_at = offset + jnp.arange(rows_here, dtype=jnp.int32)
    key_at = offset - 2 * rows_here + jnp.arange(3 * rows_here, dtype=jnp.int32)
    query_seg, query_pos = sequence_info(lengths, query_at)
    key_seg, _ = sequence_info(lengths, key_at)
    cosine, sine = rope_tables(query_pos, HD)
    query_pre = jnp.dot(
        normed_one, query_weight_matrix, preferred_element_type=jnp.float32
    ).reshape(rows_here, heads_here, HD)
    key_pre = jnp.dot(normed_one, key_weight_matrix, preferred_element_type=jnp.float32).reshape(
        rows_here, heads_here, HD
    )
    queries = rotate(query_pre, cosine, sine).astype(jnp.bfloat16)
    keys = rotate(key_pre, cosine, sine).astype(jnp.bfloat16)
    values = (
        jnp.dot(normed_one, value_weight_matrix, preferred_element_type=jnp.float32)
        .astype(jnp.bfloat16)
        .reshape(rows_here, heads_here, HD)
    )
    carried = jnp.stack([keys, values], axis=0)
    window = [carried]
    for hop in range(2):
        carried = passed_along(carried, "ep", 1)
        window = [carried] + window
    joined = jnp.concatenate(window, axis=1)
    keys_win = joined[0]
    values_win = joined[1]
    allowed = (
        (query_seg[:, None] == key_seg[None, :])
        & (key_at[None, :] <= query_at[:, None])
        & (key_at[None, :] >= 0)
    )
    scores = (
        jnp.einsum("qhd,khd->hqk", queries, keys_win, preferred_element_type=jnp.float32)
        * score_scale
    )
    masked = jnp.where(allowed[None], scores, -1e30)
    peak = jnp.max(masked, axis=-1, keepdims=True)
    expo = jnp.exp(masked - peak)
    total = jnp.sum(expo, axis=-1, keepdims=True)
    log_total = peak + jnp.log(total)
    weights = expo / total
    attended = jnp.einsum(
        "hqk,khd->qhd", weights.astype(jnp.bfloat16), values_win, preferred_element_type=jnp.float32
    )
    attended = attended.reshape(rows_here, heads_here * HD).astype(jnp.bfloat16)
    attn_part = jnp.einsum("th,dh->td", attended, output_weight, preferred_element_type=jnp.float32)
    resid = layer_input + lax.psum(attn_part, "tp")
    normed_two_wide, norm_two = norm_forward(resid, second_norm_scale)
    normed_two = normed_two_wide.astype(jnp.bfloat16)
    normed_two_f = normed_two.astype(jnp.float32)
    router_f = router_weight.astype(jnp.float32)
    mix_f = shared_mixer_weight.astype(jnp.float32)
    router = jax.nn.softmax(jnp.dot(normed_two_f, router_f, precision=highest), axis=-1)
    picked = routes[:, :, None] == jnp.arange(expert_count, dtype=jnp.int32)[None, None, :]
    gates = jnp.sum(jnp.where(picked, router[:, None, :], 0.0), axis=-1)
    mixer = jax.nn.sigmoid(jnp.dot(normed_two_f, mix_f, precision=highest))
    shared_g = jnp.dot(normed_two, shared_gate_weight, preferred_element_type=jnp.float32)
    shared_u = jnp.dot(normed_two, shared_up_weight, preferred_element_type=jnp.float32)
    shared_h = (jax.nn.silu(shared_g) * shared_u).astype(jnp.bfloat16)
    shared_part = jnp.einsum(
        "tf,df->td", shared_h, shared_down_weight, preferred_element_type=jnp.float32
    )
    flat = routes.reshape(-1)
    hot = (flat[:, None] == jnp.arange(expert_count, dtype=jnp.int32)[None, :]).astype(jnp.int32)
    rank = jnp.sum(jnp.cumsum(hot, axis=0) * hot, axis=1) - 1
    target = flat * capacity + rank
    slot_total = ep_count * slot_here * capacity
    owner_route = (
        jnp.zeros((slot_total,), jnp.int32)
        .at[target]
        .set(jnp.arange(rows_here * top_count, dtype=jnp.int32))
    )
    filled = jnp.zeros((slot_total,), jnp.bool_).at[target].set(True)
    owner_token = owner_route // top_count
    send_rows = jnp.where(filled[:, None], normed_two[owner_token], jnp.zeros((), jnp.bfloat16))
    arrived_rows = deliver(send_rows.reshape(ep_count, slot_here, capacity, width))
    route_g = jnp.einsum(
        "nscd,sfd->nscf", arrived_rows, expert_gate, preferred_element_type=jnp.float32
    )
    route_u = jnp.einsum(
        "nscd,sfd->nscf", arrived_rows, expert_up, preferred_element_type=jnp.float32
    )
    route_h = (jax.nn.silu(route_g) * route_u).astype(jnp.bfloat16)
    route_part = jnp.einsum(
        "nscf,sfd->nscd", route_h, expert_down, preferred_element_type=jnp.float32
    )
    back_rows = bring_back(route_part, target, rows_here, top_count)
    upstream = cotangent.astype(jnp.float32)
    routed = jnp.sum(back_rows * gates[:, :, None], axis=1)
    ffn_part = mixer[:, None] * shared_part + routed
    route_dot = jnp.sum(back_rows * upstream[:, None, :], axis=-1)
    shared_dot = jnp.sum(shared_part * upstream, axis=-1)
    ffn_total, d_gate, d_mixer = lax.psum((ffn_part, route_dot, shared_dot), "tp")
    block_out = (resid + ffn_total).astype(jnp.bfloat16)
    d_router = jnp.sum(jnp.where(picked, d_gate[:, :, None], 0.0), axis=1)
    d_logits = router * (d_router - jnp.sum(router * d_router, axis=-1, keepdims=True))
    d_mixlogit = d_mixer * mixer * (1.0 - mixer)
    side = jnp.dot(d_logits, router_f.T, precision=highest) + d_mixlogit[:, None] * mix_f[None, :]
    grad_router = jnp.dot(normed_two_f.T, d_logits, precision=highest)
    grad_mix = jnp.dot(d_mixlogit, normed_two_f, precision=highest)
    d_shared = (mixer[:, None] * upstream).astype(jnp.bfloat16)
    d_sh = jnp.dot(d_shared, shared_down_weight, preferred_element_type=jnp.float32)
    sig_shared = jax.nn.sigmoid(shared_g)
    d_sg = (d_sh * shared_u * sig_shared * (1.0 + shared_g * (1.0 - sig_shared))).astype(
        jnp.bfloat16
    )
    d_su = (d_sh * shared_g * sig_shared).astype(jnp.bfloat16)
    d_normed_part = jnp.einsum(
        "tf,df->td", d_sg, shared_gate_weight, preferred_element_type=jnp.float32
    )
    d_normed_part = d_normed_part + jnp.einsum(
        "tf,df->td", d_su, shared_up_weight, preferred_element_type=jnp.float32
    )
    grad_sgate = jnp.einsum("td,tf->df", normed_two, d_sg, preferred_element_type=jnp.float32)
    grad_sup = jnp.einsum("td,tf->df", normed_two, d_su, preferred_element_type=jnp.float32)
    grad_sdown = jnp.einsum("td,tf->df", d_shared, shared_h, preferred_element_type=jnp.float32)
    d_route = (
        (gates[:, :, None] * upstream[:, None, :])
        .astype(jnp.bfloat16)
        .reshape(rows_here * top_count, width)
    )
    send_grads = jnp.where(filled[:, None], d_route[owner_route], jnp.zeros((), jnp.bfloat16))
    received_grads = deliver(send_grads.reshape(ep_count, slot_here, capacity, width))
    d_rh = jnp.einsum(
        "nscd,sfd->nscf", received_grads, expert_down, preferred_element_type=jnp.float32
    )
    sig_route = jax.nn.sigmoid(route_g)
    d_rg = (d_rh * route_u * sig_route * (1.0 + route_g * (1.0 - sig_route))).astype(jnp.bfloat16)
    routed_up_gradient = (d_rh * route_g * sig_route).astype(jnp.bfloat16)
    row_grads = jnp.einsum("nscf,sfd->nscd", d_rg, expert_gate, preferred_element_type=jnp.float32)
    row_grads = row_grads + jnp.einsum(
        "nscf,sfd->nscd", routed_up_gradient, expert_up, preferred_element_type=jnp.float32
    )
    grad_egate = jnp.einsum(
        "qxba,qxbr->xar", d_rg, arrived_rows, preferred_element_type=jnp.float32
    )
    expert_up_gradient = jnp.einsum(
        "qxba,qxbr->xar", routed_up_gradient, arrived_rows, preferred_element_type=jnp.float32
    )
    grad_edown = jnp.einsum(
        "qxba,qxbr->xar", route_h, received_grads, preferred_element_type=jnp.float32
    )
    grads_back = bring_back(row_grads, target, rows_here, top_count)
    d_routed = jnp.sum(grads_back, axis=1)
    d_normed_two = lax.psum(d_normed_part + d_routed, "tp") + side
    d_resid_norm, grad_gain_two = norm_backward(resid, norm_two, second_norm_scale, d_normed_two)
    d_resid = upstream + d_resid_norm
    d_resid_low = d_resid.astype(jnp.bfloat16)
    grad_outw = jnp.einsum("td,th->dh", d_resid_low, attended, preferred_element_type=jnp.float32)
    d_attended = jnp.einsum(
        "td,dh->th", d_resid_low, output_weight, preferred_element_type=jnp.float32
    )
    d_attended = d_attended.astype(jnp.bfloat16).reshape(rows_here, heads_here, HD)
    scores_again = (
        jnp.einsum("qhd,khd->hqk", queries, keys_win, preferred_element_type=jnp.float32)
        * score_scale
    )
    probs = jnp.where(allowed[None], jnp.exp(scores_again - log_total), 0.0)
    d_probs = jnp.einsum("qhd,khd->hqk", d_attended, values_win, preferred_element_type=jnp.float32)
    delta = jnp.sum(probs * d_probs, axis=-1, keepdims=True)
    d_scores = (probs * (d_probs - delta)).astype(jnp.bfloat16)
    d_queries = (
        jnp.einsum("hqk,khd->qhd", d_scores, keys_win, preferred_element_type=jnp.float32)
        * score_scale
    )
    d_keys_win = (
        jnp.einsum("hqk,qhd->khd", d_scores, queries, preferred_element_type=jnp.float32)
        * score_scale
    )
    d_values_win = jnp.einsum(
        "hqk,qhd->khd", probs.astype(jnp.bfloat16), d_attended, preferred_element_type=jnp.float32
    )
    pair_grads = jnp.stack([d_keys_win, d_values_win], axis=0)
    older = pair_grads[:, :rows_here]
    later = [pair_grads[:, rows_here : 2 * rows_here], pair_grads[:, 2 * rows_here :]]
    running = older
    for hop in range(2):
        running = passed_along(running, "ep", -1)
        running = running + later[hop]
    d_query_pre = (
        unrotate(d_queries, cosine, sine).astype(jnp.bfloat16).reshape(rows_here, heads_here * HD)
    )
    d_key_pre = (
        unrotate(running[0], cosine, sine).astype(jnp.bfloat16).reshape(rows_here, heads_here * HD)
    )
    d_values = running[1].astype(jnp.bfloat16).reshape(rows_here, heads_here * HD)
    grad_queryw = jnp.einsum(
        "td,th->dh", normed_one, d_query_pre, preferred_element_type=jnp.float32
    )
    grad_keyw = jnp.einsum("td,th->dh", normed_one, d_key_pre, preferred_element_type=jnp.float32)
    grad_valuew = jnp.einsum("td,th->dh", normed_one, d_values, preferred_element_type=jnp.float32)
    d_normed_one = jnp.einsum(
        "th,dh->td", d_query_pre, query_weight_matrix, preferred_element_type=jnp.float32
    )
    d_normed_one = d_normed_one + jnp.einsum(
        "th,dh->td", d_key_pre, key_weight_matrix, preferred_element_type=jnp.float32
    )
    d_normed_one = d_normed_one + jnp.einsum(
        "th,dh->td", d_values, value_weight_matrix, preferred_element_type=jnp.float32
    )
    d_normed_one = lax.psum(d_normed_one, "tp")
    d_input_norm, grad_gain_one = norm_backward(
        layer_input, norm_one, first_norm_scale, d_normed_one
    )
    grad_tokens = d_resid + d_input_norm
    summed = (
        lax.psum_scatter(grad_gain_one, "ep", scatter_dimension=0, tiled=True),
        lax.psum_scatter(grad_queryw, "ep", scatter_dimension=0, tiled=True),
        lax.psum_scatter(grad_keyw, "ep", scatter_dimension=0, tiled=True),
        lax.psum_scatter(grad_valuew, "ep", scatter_dimension=0, tiled=True),
        lax.psum_scatter(grad_outw, "ep", scatter_dimension=0, tiled=True),
        lax.psum_scatter(grad_gain_two, "ep", scatter_dimension=0, tiled=True),
        lax.psum_scatter(grad_router, "ep", scatter_dimension=0, tiled=True),
        lax.psum_scatter(grad_mix, "ep", scatter_dimension=0, tiled=True),
        lax.psum_scatter(grad_sgate, "ep", scatter_dimension=0, tiled=True),
        lax.psum_scatter(grad_sup, "ep", scatter_dimension=0, tiled=True),
        lax.psum_scatter(grad_sdown, "ep", scatter_dimension=0, tiled=True),
    )
    return (
        block_out,
        grad_tokens,
        summed[0],
        summed[1],
        summed[2],
        summed[3],
        summed[4],
        summed[5],
        summed[6],
        summed[7],
        summed[8],
        summed[9],
        summed[10],
        grad_egate,
        expert_up_gradient,
        grad_edown,
    )


class Place:
    def __init__(self):
        self.ep, self.tp = lax.axis_index("ep"), lax.axis_index("tp")
        self.z, self.y = self.ep // 2, self.ep % 2
        self.x, self.c = self.tp // 2, self.tp % 2
        self.depth = lax.axis_size("ep") // 2
        self.next_core = (self.ep, self.x * 2 + 1 - self.c)
        self.next_x = (self.ep, (1 - self.x) * 2 + self.c)
        self.next_y = (self.z * 2 + 1 - self.y, self.tp)

    def at_z(self, z):
        return (z * 2 + self.y, self.tp)

    def ahead(self, steps):
        return lax.rem(self.z + steps, self.depth)

    def behind(self, steps):
        return lax.rem(self.z + self.depth - steps, self.depth)

    def greet(self):
        barrier = pltpu.get_barrier_semaphore()
        peers = [self.next_core, self.next_x, self.next_y]
        peers += [self.at_z(self.ahead(k)) for k in range(1, self.depth)]
        for peer in peers:
            pl.semaphore_signal(barrier, inc=1, device_id=peer, device_id_type=MESH)
        pl.semaphore_wait(barrier, len(peers))

    def greet_row(self):
        barrier = pltpu.get_barrier_semaphore()
        count = 2 * self.depth
        peers = [(lax.rem(self.ep + k, count), self.tp) for k in range(1, count)]
        peers += [self.next_core, self.next_x]
        for peer in peers:
            pl.semaphore_signal(barrier, inc=1, device_id=peer, device_id_type=MESH)
        pl.semaphore_wait(barrier, len(peers))

    def greet_ep(self):
        barrier = pltpu.get_barrier_semaphore()
        count = 2 * self.depth
        for k in range(1, count):
            peer = (lax.rem(self.ep + k, count), self.tp)
            pl.semaphore_signal(barrier, inc=1, device_id=peer, device_id_type=MESH)
        pl.semaphore_wait(barrier, count - 1)


def remote(src, dst, send, recv, peer):
    return pltpu.make_async_remote_copy(
        src_ref=src, dst_ref=dst, send_sem=send, recv_sem=recv, device_id=peer, device_id_type=MESH
    )


def ffn_kernel(
    units,
    expert_count,
    rows_in,
    upstream_in,
    gate_in,
    up_in,
    down_in,
    pieces_in,
    weights_in,
    resid_in,
    gain_in,
    rows_all,
    weighted_out,
    d_pair_out,
    block_out,
    d_resid_low_out,
    d_resid_out,
    d_gain_out,
    d_side_out,
    d_rows_sum,
    out_sum,
    pair_w,
    down_w,
    side_w,
    rows_tile,
    upstream_tile,
    pair_pre,
    d_hidden,
    factors,
    dots,
    weighted_tile,
    d_pair_tile,
    d_resid_low,
    d_rows_tile,
    out_tile,
    d_rows_core,
    out_core,
    d_rows_held,
    out_held,
    d_rows_hop,
    out_hop,
    d_rows_hop2,
    out_hop2,
    d_rows_z,
    out_z,
    d_rows_to_z,
    out_to_z,
    gathered_send,
    gathered_recv,
    hop_send,
    hop_recv,
    weight_sem,
    end_sem,
    own_sem,
    z_send,
    z_recv,
    plane_send,
    plane_recv,
    load_sem,
    store_sem,
    sum_send,
    sum_recv,
    end_send,
    end_recv,
    core_credit,
    hop_credit,
    hop2_credit,
):
    at = Place()
    depth = at.depth
    quarter, width = rows_in.shape
    half = quarter // 2
    f32, bf16 = jnp.float32, jnp.bfloat16

    def weight_copies():
        hidden = down_w.shape[0]
        slot_here, slot_hidden, shared = units
        routed = slot_here * slot_hidden
        columns = pieces_in.shape[2]
        pairs = [(weights_in.at[:, pl.ds(weights_in.shape[1] - 128, 128)], side_w)]
        kinds = ((gate_in, pair_w, 0), (up_in, pair_w, hidden), (down_in, down_w, 0))
        for kind, (experts, into, first) in enumerate(kinds):
            pairs.append((experts, into.at[pl.ds(first, routed)]))
            here = pl.ds(first + routed, shared)
            for e in range(2 * depth):
                src = pieces_in.at[e, pl.ds(kind * shared, shared)]
                pairs.append((src, into.at[here, pl.ds(e * columns, columns)]))
        return [
            pltpu.make_async_copy(src, dst, weight_sem.at[i]) for i, (src, dst) in enumerate(pairs)
        ]

    def clear_rest():
        hidden = down_w.shape[0]
        used = units[0] * units[1] + units[2]
        for into, first in ((pair_w, 0), (pair_w, hidden), (down_w, 0)):
            if used < hidden:
                into[first + used : first + hidden] = jnp.zeros((hidden - used, width), bf16)

    for copy in weight_copies():
        copy.start()
    clear_rest()

    def block(j, y, x):
        return rows_all.at[at.behind(j), y, x, at.c]

    def plane_copy(j, kind):
        y, other_y = at.y, 1 - at.y
        own, other_x = at.x, 1 - at.x
        if kind == 0:
            src, peer = block(j, y, own), at.next_x
        elif kind == 1:
            src, peer = block(j, y, own), at.next_y
        elif kind == 2:
            src, peer = block(j, y, other_x).at[pl.ds(0, half)], at.next_y
        elif kind == 3:
            src, peer = block(j, other_y, own).at[pl.ds(half, half)], at.next_x
        else:
            src = block(j, other_y if kind >= 6 else y, other_x if kind % 2 else own)
            peer = at.next_core
        return remote(src, src, plane_send.at[j, kind], plane_recv.at[j, kind], peer)

    def z_copy(k):
        return remote(
            rows_in, block(0, at.y, at.x), z_send.at[k - 1], z_recv.at[k - 1], at.at_z(at.ahead(k))
        )

    def z_arrival(k):
        dst = block(k, at.y, at.x)
        return remote(dst, dst, z_send.at[k - 1], z_recv.at[k - 1], at.at_z(at.behind(k)))

    def begin(j):
        for kind in (0, 1, 4):
            plane_copy(j, kind).start()

    def spread(j):
        plane_copy(j, 0).wait_recv()
        plane_copy(j, 2).start()
        plane_copy(j, 5).start()
        plane_copy(j, 1).wait_recv()
        plane_copy(j, 3).start()
        plane_copy(j, 6).start()

    def begin_later(j):
        z_arrival(j).wait_recv()
        begin(j)

    def last_hop(j):
        plane_copy(j, 2).wait_recv()
        plane_copy(j, 3).wait_recv()
        plane_copy(j, 7).start()

    def near_ready(j):
        plane_copy(j, 4).wait_recv()
        plane_copy(j, 5).wait_recv()

    def far_ready(j):
        plane_copy(j, 6).wait_recv()
        plane_copy(j, 7).wait_recv()

    def parity(step):
        return lax.rem(step, 2)

    def slot_of(turn):
        return lax.rem(turn + 1, depth)

    def other_y(step):
        return lax.rem(parity(step) + (step // 2 + 1) // depth, 2)

    def tile_at(step):
        return at.behind(slot_of(step // 2)), lax.rem(at.y + other_y(step), 2)

    def load_rows(step):
        z, y = tile_at(step)
        return pltpu.make_async_copy(rows_all.at[z, y], rows_tile, load_sem.at[0])

    def load_upstream(step):
        z, y = tile_at(step)
        return pltpu.make_async_copy(upstream_in.at[z, y], upstream_tile, load_sem.at[1])

    def stores(step):
        z, y = tile_at(step)
        pairs = ((weighted_tile, weighted_out), (d_pair_tile, d_pair_out))
        return [
            pltpu.make_async_copy(src, dst.at[z, y], store_sem.at[i])
            for i, (src, dst) in enumerate(pairs)
        ]

    tiles, cores = (d_rows_tile, out_tile), (d_rows_core, out_core)
    helds, sums = (d_rows_held, out_held), (d_rows_sum, out_sum)
    hops, hops2, zs = (d_rows_hop, out_hop), (d_rows_hop2, out_hop2), (d_rows_z, out_z)
    to_zs = (d_rows_to_z, out_to_z)

    def sum_copy(a, kind, src, dst, peer):
        return remote(src, dst, sum_send.at[a, kind], sum_recv.at[a, kind], peer)

    def core_sum(a):
        return sum_copy(a, 0, tiles[a].at[:, 1 - at.c], cores[a], at.next_core)

    def row_hop(turn, other):
        y = lax.rem(at.y + other, 2)
        slot = parity(turn)
        src = d_rows_held.at[slot, y, 1 - at.x]
        return remote(
            src, d_rows_hop.at[slot, y], hop_send.at[slot, other], hop_recv.at[slot, other], at.next_x
        )

    def out_hop_sum(turn):
        slot = parity(turn)
        src = out_held.at[slot, 1 - at.y]
        return remote(
            src, out_hop.at[slot], hop_send.at[slot, 2], hop_recv.at[slot, 2], at.next_y
        )

    def hop2_sum(a, turn):
        slot = parity(turn)
        if a == 0:
            src, peer = helds[0].at[slot, 1 - at.y, at.x], at.next_y
        else:
            src, peer = helds[1].at[slot, at.y, 1 - at.x], at.next_x
        return sum_copy(a, 2, src, hops2[a], peer)

    def z_sum(a, turn):
        return remote(
            to_zs[a].at[parity(turn)],
            zs[a].at[turn],
            end_send.at[a, turn],
            end_recv.at[a, turn],
            at.at_z(at.behind(turn + 1)),
        )

    def allow(semaphore, peer):
        pl.semaphore_signal(semaphore, inc=1, device_id=peer, device_id_type=MESH)

    piece = 32

    def add(into, first, second):
        def body(i, carry):
            part = pl.ds(pl.multiple_of(i * piece, piece), piece)
            into[part] = first[part] + second[part]
            return carry

        lax.fori_loop(0, quarter // piece, body, 0)

    def after_core(step):
        turn = step // 2
        other = other_y(step)
        held, y = parity(turn), lax.rem(at.y + other, 2)

        @pl.when((parity(step) == 0) & (turn >= 2))
        def _():
            for a in (0, 1):
                pl.semaphore_wait(hop_credit.at[a], 1)

        for a in (0, 1):
            core_sum(a).wait()
            for x in (1 - at.x, at.x):
                add(helds[a].at[held, y, x], tiles[a].at[x, at.c], cores[a].at[x])
            if a == 0:
                row_hop(turn, other).start()
            else:

                @pl.when(other == 1)
                def _():
                    out_hop_sum(turn).start()

        @pl.when(step + 1 < 2 * depth)
        def _():
            allow(core_credit, at.next_core)

    def after_row_hop(turn, other):
        slot, y = parity(turn), lax.rem(at.y + other, 2)
        row_hop(turn, other).wait()
        into = d_rows_held.at[slot, y, at.x]
        add(into, into, d_rows_hop.at[slot, y])

    def after_out_hop(turn):
        slot = parity(turn)
        out_hop_sum(turn).wait()
        for x in (1 - at.x, at.x):
            into = out_held.at[slot, at.y, x]
            add(into, into, out_hop.at[slot, x])

    def may_hop2(turn, a):
        @pl.when(turn >= 1)
        def _():
            pl.semaphore_wait(hop2_credit.at[a], 1)

    def after_hop(turn):
        after_row_hop(turn, 1)
        may_hop2(turn, 0)
        hop2_sum(0, turn).start()
        after_row_hop(turn, 0)
        after_out_hop(turn)
        may_hop2(turn, 1)
        hop2_sum(1, turn).start()

        @pl.when(turn + 2 < depth)
        def _():
            allow(hop_credit.at[0], at.next_x)
            allow(hop_credit.at[1], at.next_y)

    def after_hop2(turn):
        slot = parity(turn)
        for a in (0, 1):
            hop2_sum(a, turn).wait()

            @pl.when(turn >= 2)
            def _():
                z_sum(a, turn - 2).wait_send()

            add(to_zs[a].at[slot], helds[a].at[slot, at.y, at.x], hops2[a])
            z_sum(a, turn).start()
        allow(hop2_credit.at[0], at.next_y)
        allow(hop2_credit.at[1], at.next_x)

    load_upstream(0).start()
    at.greet()
    z_copy(1).start()
    own_copy = pltpu.make_async_copy(rows_in, block(0, at.y, at.x), own_sem)
    own_copy.start()
    own_copy.wait()
    begin(0)
    begin_later(1)
    for k in range(2, depth):
        z_copy(k).start()
    spread(0)
    spread(1)
    near_ready(1)
    load_rows(0).start()
    for copy in weight_copies():
        copy.wait()

    tile_rows = 4 * quarter
    hidden_total = down_w.shape[0]
    lane = lax.broadcasted_iota(jnp.int32, (tile_rows, 128), 1)
    slot_here, slot_hidden, shared_hidden = units
    routed = slot_here * slot_hidden
    across = (((1,), (1,)), ((), ()))
    few = 16

    def gate_factors(rows, picked):
        logits = jnp.dot(rows, side_w[...], preferred_element_type=f32)
        chooses = (lane >= 3) & (lane < 3 + expert_count)
        peak = jnp.max(jnp.where(chooses, logits, -1e30), axis=1, keepdims=True)
        expo = jnp.where(chooses, jnp.exp(jnp.where(chooses, logits, peak) - peak), 0.0)
        routed_gate = expo / jnp.sum(expo, axis=1, keepdims=True) * picked.astype(f32)
        mix_pre = jnp.sum(jnp.where(lane == 2, logits, 0.0), axis=1, keepdims=True)
        result = jnp.where(lane == slot_here, 1.0 / (1.0 + jnp.exp(-mix_pre)), 0.0)
        for s in range(slot_here):
            chosen = lane == 3 + at.ep * slot_here + s
            gate = jnp.sum(jnp.where(chosen, routed_gate, 0.0), axis=1, keepdims=True)
            result = jnp.where(lane == s, gate, result)
        return result

    few_lane = lax.broadcasted_iota(jnp.int32, (few, 128), 1)
    bounds = [s * slot_hidden for s in range(slot_here)] + [routed, hidden_total]

    def owners(group):
        found = []
        for s in range(slot_here + 1):
            low, high = max(bounds[s] - group * 128, 0), min(bounds[s + 1] - group * 128, 128)
            if low < high:
                found.append((s, low, high))
        return found

    def hidden_rows(i, carry):
        here = pl.ds(pl.multiple_of(i * few, few), few)
        gates = [
            jnp.broadcast_to(factors[here, s : s + 1], (few, 128)) for s in range(slot_here + 1)
        ]
        parts = [None] * (slot_here + 1)
        for group in range(hidden_total // 128):
            units_here = slice(group * 128, (group + 1) * 128)
            units_up = slice(hidden_total + group * 128, hidden_total + (group + 1) * 128)
            gate_pre, up_pre = pair_pre[here, units_here], pair_pre[here, units_up]
            d_h = d_hidden[here, units_here]
            found = owners(group)
            factor = gates[found[0][0]]
            for s, low, _ in found[1:]:
                factor = jnp.where(few_lane >= low, gates[s], factor)
            sig = 0.5 + 0.5 * jnp.tanh(0.5 * gate_pre)
            silu = gate_pre * sig
            hidden = silu * up_pre
            product = hidden * d_h
            gated = factor * d_h
            weighted_tile[here, units_here] = (factor * hidden).astype(bf16)
            slope = sig + silu * (1.0 - sig)
            d_pair_tile[here, units_here] = (gated * up_pre * slope).astype(bf16)
            d_pair_tile[here, units_up] = (gated * silu).astype(bf16)
            for s, low, high in found:
                mine = product
                if high < 128:
                    mine = jnp.where(few_lane < high, mine, 0.0)
                if low > 0:
                    mine = jnp.where(few_lane >= low, mine, 0.0)
                parts[s] = mine if parts[s] is None else parts[s] + mine
        result = jnp.zeros((few, 128), f32)
        for s in range(slot_here + 1):
            dot = jnp.sum(parts[s], axis=1, keepdims=True)
            where = few_lane == (2 if s == slot_here else 3 + at.ep * slot_here + s)
            result = jnp.where(where, dot, result)
        dots[here] = result.astype(bf16)
        return carry

    def first_half(step):
        load_upstream(step).wait()
        upstream = upstream_tile[...].reshape(tile_rows, upstream_tile.shape[-1])
        d_hidden[...] = lax.dot_general(
            upstream[:, :width], down_w[...], across, preferred_element_type=f32
        )
        load_rows(step).wait()
        rows = rows_tile[...].reshape(tile_rows, width)
        factors[...] = gate_factors(rows, upstream[:, width:])
        pair_pre[...] = lax.dot_general(rows, pair_w[...], across, preferred_element_type=f32)

        @pl.when(step + 1 < 2 * depth)
        def _():
            load_upstream(step + 1).start()

        @pl.when(step >= 1)
        def _():
            for copy in stores(step - 1):
                copy.wait()

        lax.fori_loop(0, tile_rows // few, hidden_rows, 0, unroll=2)
        for copy in stores(step):
            copy.start()
        turn = step // 2

        @pl.when(step == 0)
        def _():
            last_hop(0)

        @pl.when((parity(step) == 0) & (turn + 1 < depth))
        def _():
            last_hop(turn + 1)

        @pl.when((step >= 1) & (step + 1 < depth))
        def _():
            spread(step + 1)

        @pl.when(step + 2 < depth)
        def _():
            begin_later(step + 2)

    def second_half(step):
        blocks = (2, 2, quarter)
        some = width // 2
        for n in range(2):
            columns = slice(n * some, (n + 1) * some)
            part = jnp.dot(weighted_tile[...], down_w[:, columns], preferred_element_type=f32)
            out_tile[:, :, :, columns] = part.astype(bf16).reshape(blocks + (some,))
            part = jnp.dot(d_pair_tile[...], pair_w[:, columns], preferred_element_type=f32)
            d_rows_tile[:, :, :, columns] = part.astype(bf16).reshape(blocks + (some,))
        d_rows_tile[:, :, :, width:] = dots[...].reshape(blocks + (128,))

        @pl.when(step >= 1)
        def _():
            pl.semaphore_wait(core_credit, 1)

        for a in (0, 1):
            core_sum(a).start()
        turn = step // 2

        @pl.when((parity(step) == 0) & (turn + 1 < depth))
        def _():
            far_ready(slot_of(turn))

        @pl.when((parity(step) == 1) & (turn + 1 < depth))
        def _():
            near_ready(slot_of(turn + 1))

        @pl.when(step == 2 * depth - 3)
        def _():
            far_ready(slot_of(turn + 1))

        @pl.when(step + 1 < 2 * depth)
        def _():
            load_rows(step + 1).start()

    def step_body(step, carry):
        first_half(step)

        @pl.when(step == 2 * depth - 1)
        def _():
            after_hop(depth - 2)

        @pl.when(step >= 1)
        def _():
            after_core(step - 1)

        second_half(step)
        odd = parity(step) == 1

        @pl.when(odd & (step >= 3) & (step < 2 * depth - 1))
        def _():
            after_hop((step - 3) // 2)

        @pl.when(jnp.logical_not(odd) & (step >= 4))
        def _():
            after_hop2((step - 4) // 2)

        return carry

    lax.fori_loop(0, 2 * depth, step_body, 0)
    last = depth - 1
    own_rows, own_upstream = rows_tile.at[0, 0], upstream_tile.at[0, 0]
    own_loads = [
        pltpu.make_async_copy(rows_in, own_rows, end_sem.at[0]),
        pltpu.make_async_copy(
            upstream_in.at[at.z, at.y, at.x, at.c], own_upstream, end_sem.at[1]
        ),
    ]
    for copy in own_loads:
        copy.start()
    after_hop2(last - 1)
    after_row_hop(last, 1)
    may_hop2(last, 0)
    hop2_sum(0, last).start()
    after_core(2 * depth - 1)
    after_out_hop(last)
    may_hop2(last, 1)
    hop2_sum(1, last).start()
    after_row_hop(last, 0)

    def total_of(a):
        hop2_sum(a, last).wait()
        held = helds[a].at[last % 2, at.y, at.x]
        for turn in range(last):
            z_sum(a, turn).wait_recv()

        def total_body(i, carry):
            part = pl.ds(pl.multiple_of(i * piece, piece), piece)
            total = held[part].astype(f32) + hops2[a][part].astype(f32)
            for k in range(last):
                total = total + zs[a][k, part].astype(f32)
            sums[a][part] = total
            return carry

        lax.fori_loop(0, quarter // piece, total_body, 0)

    total_of(0)
    own_lane = lax.broadcasted_iota(jnp.int32, (quarter, 128), 1)
    chooses = (own_lane >= 3) & (own_lane < 3 + expert_count)
    for copy in own_loads:
        copy.wait()
    rows = own_rows[...]
    logits = jnp.dot(rows, side_w[...], preferred_element_type=f32)
    peak = jnp.max(jnp.where(chooses, logits, -1e30), axis=1, keepdims=True)
    expo = jnp.where(chooses, jnp.exp(jnp.where(chooses, logits, peak) - peak), 0.0)
    router = expo / jnp.sum(expo, axis=1, keepdims=True)
    mixer = 1.0 / (1.0 + jnp.exp(-jnp.where(own_lane == 2, logits, 0.0)))
    gate_dots = d_rows_sum[:, width:]
    d_router = jnp.where(chooses, gate_dots * own_upstream[:, width:].astype(f32), 0.0)
    d_logits = router * (d_router - jnp.sum(router * d_router, axis=1, keepdims=True))
    d_mix = gate_dots * mixer * (1.0 - mixer)
    d_side = jnp.where(own_lane == 2, d_mix, jnp.where(chooses, d_logits, 0.0))
    d_side_out[...] = d_side
    high = d_side.astype(bf16)
    lower = (d_side - high.astype(f32)).astype(bf16)
    for split in (high, lower):
        d_rows_sum[:, :width] += lax.dot_general(
            split, side_w[...], across, preferred_element_type=f32
        )

    def end_body(i, carry):
        part = pl.ds(pl.multiple_of(i * few, few), few)
        resid = resid_in[part]
        scale = lax.rsqrt(jnp.mean(resid * resid, axis=1, keepdims=True) + epsilon)
        unit_rows = resid * scale
        grads = d_rows_sum[part, :width]
        scaled = grads * gain_in[...]
        inner = jnp.mean(scaled * unit_rows, axis=1, keepdims=True)
        d_resid = own_upstream[part, :width].astype(f32) + scale * (scaled - unit_rows * inner)
        d_resid_out[part] = d_resid
        d_resid_low[part] = d_resid.astype(bf16)
        return carry + jnp.sum(grads * unit_rows, axis=0, keepdims=True)

    d_gain_out[...] = lax.fori_loop(0, quarter // few, end_body, jnp.zeros((1, width), f32))

    def gather_copy(kind):
        if kind == 2:
            src = dst = d_resid_low_out.at[1 - at.x, at.c]
        else:
            src, dst = d_resid_low, d_resid_low_out.at[at.x, at.c]
        peer = at.next_x if kind == 0 else at.next_core
        return remote(src, dst, gathered_send.at[kind], gathered_recv.at[kind], peer)

    own_end = pltpu.make_async_copy(d_resid_low, d_resid_low_out.at[at.x, at.c], own_sem)
    own_end.start()
    for kind in (0, 1):
        gather_copy(kind).start()
    total_of(1)
    block_out[...] = (resid_in[...] + out_sum[...]).astype(bf16)
    gather_copy(0).wait_recv()
    gather_copy(2).start()
    own_end.wait()
    gather_copy(0).wait_send()
    gather_copy(1).wait()
    gather_copy(2).wait()
    for copy in stores(2 * depth - 1):
        copy.wait()
    for a in (0, 1):
        for turn in range(max(0, depth - 3), depth - 1):
            z_sum(a, turn).wait_send()
    for k in range(1, depth):
        z_copy(k).wait_send()

    def finish(j, carry):
        for kind in range(8):
            plane_copy(j, kind).wait_send()
        return carry

    lax.fori_loop(0, depth, finish, 0)


def ffn_over_all(rows, upstream_all, experts, pieces, weights, resid, gain, units, expert_count):
    quarter, width = rows.shape
    ep_count, tp_count = lax.axis_size("ep"), lax.axis_size("tp")
    depth = ep_count // 2
    hidden = -(-(units[0] * units[1] + units[2]) // 128) * 128
    bf16, f32 = jnp.bfloat16, jnp.float32
    wide = width + 128
    tile_rows = tp_count * quarter
    tokens = ep_count * tile_rows
    anywhere = pl.BlockSpec(memory_space=pl.ANY)
    in_vmem = pl.BlockSpec(memory_space=pltpu.VMEM)

    def both(*lead):
        return [pltpu.VMEM(lead + (quarter, columns), bf16) for columns in (wide, width)]

    dma = pltpu.SemaphoreType.DMA
    outs = pl.pallas_call(
        functools.partial(ffn_kernel, units, expert_count),
        out_shape=(
            jax.ShapeDtypeStruct((depth, 2, 2, 2, quarter, width), bf16),
            jax.ShapeDtypeStruct((depth, 2, tile_rows, hidden), bf16),
            jax.ShapeDtypeStruct((depth, 2, tile_rows, 2 * hidden), bf16),
            jax.ShapeDtypeStruct((quarter, width), bf16),
            jax.ShapeDtypeStruct((2, 2, quarter, width), bf16),
            jax.ShapeDtypeStruct((quarter, width), f32),
            jax.ShapeDtypeStruct((1, width), f32),
            jax.ShapeDtypeStruct((quarter, 128), f32),
        ),
        in_specs=[anywhere] * 7 + [in_vmem] * 2,
        out_specs=(anywhere,) * 3 + (in_vmem, anywhere) + (in_vmem,) * 3,
        scratch_shapes=[
            pltpu.VMEM((quarter, wide), f32),
            pltpu.VMEM((quarter, width), f32),
            pltpu.VMEM((2 * hidden, width), bf16),
            pltpu.VMEM((hidden, width), bf16),
            pltpu.VMEM((width, 128), bf16),
            pltpu.VMEM((2, 2, quarter, width), bf16),
            pltpu.VMEM((2, 2, quarter, wide), bf16),
            pltpu.VMEM((tile_rows, 2 * hidden), f32),
            pltpu.VMEM((tile_rows, hidden), f32),
            pltpu.VMEM((tile_rows, 128), f32),
            pltpu.VMEM((tile_rows, 128), bf16),
            pltpu.VMEM((tile_rows, hidden), bf16),
            pltpu.VMEM((tile_rows, 2 * hidden), bf16),
            pltpu.VMEM((quarter, width), bf16),
        ]
        + both(2, 2)
        + both(2)
        + both(2, 2, 2)
        + both(2, 2)
        + both()
        + both(depth - 1)
        + both(2)
        + [
            dma((3,)),
            dma((3,)),
            dma((2, 3)),
            dma((2, 3)),
            dma((4 + 6 * depth,)),
            dma((2,)),
            dma,
            dma((depth - 1,)),
            dma((depth - 1,)),
            dma((depth, 8)),
            dma((depth, 8)),
            dma((2,)),
            dma((2,)),
            dma((2, 3)),
            dma((2, 3)),
            dma((2, depth - 1)),
            dma((2, depth - 1)),
            pltpu.SemaphoreType.REGULAR,
            pltpu.SemaphoreType.REGULAR((2,)),
            pltpu.SemaphoreType.REGULAR((2,)),
        ],
        compiler_params=pltpu.CompilerParams(
            collective_id=1, has_side_effects=True, vmem_limit_bytes=62 * 2**20
        ),
        cost_estimate=pl.CostEstimate(
            flops=12 * tokens * width * hidden,
            bytes_accessed=10 * tokens * width,
            transcendentals=tokens * hidden,
        ),
        name="ffn_all_tokens",
    )(
        rows,
        upstream_all.reshape(depth, 2, 2, 2, quarter, wide),
        *[array.reshape(-1, width) for array in experts],
        pieces,
        weights,
        resid,
        gain,
    )
    rows_all, weighted, d_pair, block_out, d_resid_low, d_resid, d_gain, d_side = outs
    return (
        rows_all.reshape(tokens, width),
        weighted.reshape(tokens, hidden),
        d_pair.reshape(tokens, 2 * hidden),
        block_out,
        d_resid_low.reshape(tile_rows, width),
        d_resid,
        d_gain[0],
        d_side,
    )


def swap_copies(at, pieces_in, pieces_out, send_sem, recv_sem, leave):
    count = 2 * at.depth
    copies = []
    for k in range(1, count):
        to, back = lax.rem(at.ep + k, count), lax.rem(at.ep + count - k, count)
        if leave:
            src, dst, peer = pieces_in.at[to], pieces_out.at[at.ep], to
        else:
            src, dst, peer = pieces_in.at[back], pieces_out.at[back], back
        copies.append(remote(src, dst, send_sem.at[k], recv_sem.at[k], (peer, at.tp)))
    return copies


def weights_kernel(
    own_in,
    pieces_in,
    all_out,
    pieces_out,
    own_sem,
    z_send,
    z_recv,
    y_send,
    y_recv,
    swap_send,
    swap_recv,
):
    at = Place()
    depth = at.depth
    half = own_in.shape[0] // 2
    last = depth - 1

    def block(k, y, h):
        return all_out.at[at.z + k, y, pl.ds(h * half, half)]

    def z_copy(k, h, direction):
        if k == 0:
            src = own_in.at[pl.ds(h * half, half)]
        else:
            src = block(k, at.y, h)
        slot = last + k - direction
        return remote(
            src,
            block(k, at.y, h),
            z_send.at[last + k, h, (direction + 1) // 2],
            z_recv.at[slot, h],
            at.at_z(at.z + direction),
        )

    def z_arrival(k, h):
        direction = 1 if k > 0 else -1
        dst = block(k, at.y, h)
        return remote(
            dst, dst, z_send.at[last + k, h, 0], z_recv.at[last + k, h], at.at_z(at.z + direction)
        )

    def y_copy(k, h):
        src = own_in.at[pl.ds(h * half, half)] if k == 0 else block(k, at.y, h)
        return remote(
            src, block(k, at.y, h), y_send.at[last + k, h], y_recv.at[last + k, h], at.next_y
        )

    own_copies = [
        pltpu.make_async_copy(own_in, all_out.at[at.z, at.y], own_sem.at[0]),
        pltpu.make_async_copy(pieces_in.at[at.ep], pieces_out.at[at.ep], own_sem.at[1]),
    ]
    for copy in own_copies:
        copy.start()
    has_up, has_down = at.z + 1 < depth, at.z > 0
    at.greet_ep()

    for h in (0, 1):
        pl.when(has_up)(lambda: z_copy(0, h, 1).start())
        pl.when(has_down)(lambda: z_copy(0, h, -1).start())
        y_copy(0, h).start()
    swap = (at, pieces_in, pieces_out, swap_send, swap_recv)
    for copy in swap_copies(*swap, True):
        copy.start()
    for k in range(1, depth):
        for h in (0, 1):
            for sign in (-1, 1):
                there = at.z + sign * k
                exists = (there >= 0) & (there < depth)
                onward = at.z - sign
                goes_on = exists & (onward >= 0) & (onward < depth)

                @pl.when(exists)
                def _():
                    z_arrival(sign * k, h).wait_recv()

                @pl.when(goes_on)
                def _():
                    z_copy(sign * k, h, -sign).start()

                @pl.when(exists)
                def _():
                    y_copy(sign * k, h).start()

    for copy in own_copies:
        copy.wait()
    for copy in swap_copies(*swap, False):
        copy.wait_recv()
    for copy in swap_copies(*swap, True):
        copy.wait_send()
    for h in (0, 1):
        pl.when(has_up)(lambda: z_copy(0, h, 1).wait_send())
        pl.when(has_down)(lambda: z_copy(0, h, -1).wait_send())
    for k in range(-last, depth):
        there = at.z + k
        exists = (there >= 0) & (there < depth)
        sign = 1 if k > 0 else -1
        onward = at.z - sign
        goes_on = exists & (onward >= 0) & (onward < depth)
        for h in (0, 1):

            @pl.when(exists)
            def _():
                y_copy(k, h).wait()

            if k != 0:

                @pl.when(goes_on)
                def _():
                    z_copy(k, h, -sign).wait_send()


def gather_over_ep(block, pieces):
    rows, columns = block.shape
    depth = lax.axis_size("ep") // 2
    anywhere = pl.BlockSpec(memory_space=pl.ANY)
    slots = 2 * depth - 1
    out, pieces = pl.pallas_call(
        weights_kernel,
        out_shape=(
            jax.ShapeDtypeStruct((depth, 2, rows, columns), block.dtype),
            jax.ShapeDtypeStruct(pieces.shape, pieces.dtype),
        ),
        in_specs=[anywhere] * 2,
        out_specs=(anywhere,) * 2,
        scratch_shapes=[
            pltpu.SemaphoreType.DMA((2,)),
            pltpu.SemaphoreType.DMA((slots, 2, 2)),
            pltpu.SemaphoreType.DMA((slots, 2)),
            pltpu.SemaphoreType.DMA((slots, 2)),
            pltpu.SemaphoreType.DMA((slots, 2)),
            pltpu.SemaphoreType.DMA((2 * depth,)),
            pltpu.SemaphoreType.DMA((2 * depth,)),
        ],
        compiler_params=pltpu.CompilerParams(collective_id=3, has_side_effects=True),
        cost_estimate=pl.CostEstimate(
            flops=0, bytes_accessed=8 * depth * rows * columns, transcendentals=0
        ),
        name="gather_weights",
    )(block, pieces)
    return out.reshape(2 * depth * rows, columns), pieces


class RowGather:
    def __init__(self, at, mine, everywhere, z_send, z_recv, plane_send, plane_recv):
        self.at, self.mine, self.everywhere = at, mine, everywhere
        self.z_sems, self.plane_sems = (z_send, z_recv), (plane_send, plane_recv)
        self.half = mine.shape[0] // 2

    def block(self, j, y, x):
        return self.everywhere.at[self.at.behind(j), y, x, self.at.c]

    def plane_copy(self, j, kind):
        at, half = self.at, self.half
        if kind == 0:
            src, peer = self.block(j, at.y, at.x), at.next_x
        elif kind == 1:
            src, peer = self.block(j, at.y, at.x), at.next_y
        elif kind == 2:
            src, peer = self.block(j, at.y, 1 - at.x).at[pl.ds(0, half)], at.next_y
        elif kind == 3:
            src, peer = self.block(j, 1 - at.y, at.x).at[pl.ds(half, half)], at.next_x
        else:
            y, x = 1 - at.y if kind >= 6 else at.y, 1 - at.x if kind % 2 else at.x
            src, peer = self.block(j, y, x), at.next_core
        send, recv = self.plane_sems
        return remote(src, src, send.at[j, kind], recv.at[j, kind], peer)

    def z_copy(self, k):
        send, recv = self.z_sems
        dst = self.block(0, self.at.y, self.at.x)
        peer = self.at.at_z(self.at.ahead(k))
        return remote(self.mine, dst, send.at[k - 1], recv.at[k - 1], peer)

    def z_onward(self, j):
        send, recv = self.z_sems
        src = self.block(j, self.at.y, self.at.x)
        peer = self.at.at_z(self.at.z + 1)
        return remote(src, src, send.at[self.at.depth - 1 + j], recv.at[j], peer)

    def sends(self, k):
        down = self.at.z + k >= self.at.depth
        return down | (self.at.z + 1 < self.at.depth) if k == 1 else down

    def goes_on(self, j):
        return (self.at.z >= j) & (self.at.z + 1 < self.at.depth)

    def z_start(self):
        for k in range(1, self.at.depth):

            @pl.when(self.sends(k))
            def _():
                self.z_copy(k).start()

    def begin(self, j):
        if j > 0:
            send, recv = self.z_sems
            dst = self.block(j, self.at.y, self.at.x)
            peer = self.at.at_z(self.at.behind(j))
            remote(dst, dst, send.at[j - 1], recv.at[j - 1], peer).wait_recv()
            if j + 1 < self.at.depth:

                @pl.when(self.goes_on(j))
                def _():
                    self.z_onward(j).start()

        for kind in (0, 1, 4):
            self.plane_copy(j, kind).start()

    def spread(self, j):
        self.plane_copy(j, 0).wait_recv()
        self.plane_copy(j, 2).start()
        self.plane_copy(j, 5).start()
        self.plane_copy(j, 1).wait_recv()
        self.plane_copy(j, 3).start()
        self.plane_copy(j, 6).start()

    def last_hop(self, j):
        self.plane_copy(j, 2).wait_recv()
        self.plane_copy(j, 3).wait_recv()
        self.plane_copy(j, 7).start()

    def finish(self):
        for k in range(1, self.at.depth):

            @pl.when(self.sends(k))
            def _():
                self.z_copy(k).wait_send()

            if k + 1 < self.at.depth:

                @pl.when(self.goes_on(k))
                def _():
                    self.z_onward(k).wait_send()

        for j in range(self.at.depth):
            for kind in range(8):
                if kind >= 4:
                    self.plane_copy(j, kind).wait_recv()
                self.plane_copy(j, kind).wait_send()


def front_kernel(
    score_scale,
    block_in,
    weights_in,
    upstream_in,
    cos_in,
    sin_in,
    query_start,
    query_at,
    tokens_in,
    first_gain,
    gain_in,
    upstream_all,
    turned_out,
    k_out,
    v_out,
    q_out,
    lse_out,
    attended_out,
    resid_out,
    rows_out,
    normed,
    turned,
    qkv_w,
    out_w,
    k_all,
    v_all,
    scores_of,
    part,
    core_got,
    x_got,
    load_sem,
    z_send,
    z_recv,
    plane_send,
    plane_recv,
    kv_send,
    kv_recv,
    tp_send,
    tp_recv,
):
    at = Place()
    depth = at.depth
    count = 2 * depth
    heads, tokens, head = q_out.shape
    heads_width = heads * head
    windows = k_all.shape[1] // tokens
    quarter, width = resid_out.shape
    f32, bf16 = jnp.float32, jnp.bfloat16
    across = (((1,), (1,)), ((), ()))
    gather = RowGather(at, upstream_in, upstream_all, z_send, z_recv, plane_send, plane_recv)
    own = (windows - 1) * tokens

    def kv_copy(kind, w):
        held = (k_all, v_all)[kind]
        return remote(
            held.at[:, pl.ds(own, tokens)],
            held.at[:, pl.ds(w * tokens, tokens)],
            kv_send.at[kind, w],
            kv_recv.at[kind, w],
            (at.ep + (windows - 1 - w), at.tp),
        )

    def kv_arrival(kind, w):
        dst = (k_all, v_all)[kind].at[:, pl.ds(w * tokens, tokens)]
        peer = (at.ep - (windows - 1 - w), at.tp)
        return remote(dst, dst, kv_send.at[kind, w], kv_recv.at[kind, w], peer)

    def core_copy():
        return remote(part.at[:, 1 - at.c], core_got, tp_send.at[0], tp_recv.at[0], at.next_core)

    def x_copy():
        return remote(part.at[1 - at.x, at.c], x_got, tp_send.at[1], tp_recv.at[1], at.next_x)

    pairs = (
        (block_in, normed),
        (weights_in.at[:, pl.ds(0, 3 * heads_width)], qkv_w),
        (weights_in.at[:, pl.ds(3 * heads_width, heads_width)], out_w),
    )
    loads = [pltpu.make_async_copy(src, dst, load_sem.at[i]) for i, (src, dst) in enumerate(pairs)]
    for copy in loads:
        copy.start()
    at.greet_row()
    own_copy = pltpu.make_async_copy(
        upstream_in, gather.block(0, at.y, at.x), load_sem.at[len(pairs)]
    )
    own_copy.start()
    gather.z_start()
    own_copy.wait()
    gather.begin(0)
    loads[0].wait()
    few = 16

    def norm_body(i, carry):
        here = pl.ds(pl.multiple_of(i * few, few), few)
        inputs = normed[here].astype(f32)
        scale = lax.rsqrt(jnp.mean(inputs * inputs, axis=1, keepdims=True) + epsilon)
        normed[here] = (inputs * scale * first_gain[...]).astype(bf16)
        return carry

    lax.fori_loop(0, tokens // few, norm_body, 0, unroll=2)
    loads[1].wait()
    lane = lax.broadcasted_iota(jnp.int32, (tokens, head), 1)
    sign = jnp.where(lane < head // 2, -1.0, 1.0)

    def rotated(array):
        return array * cos_in[...] + pltpu.roll(array, head // 2, 1) * sign * sin_in[...]

    keys = jnp.dot(
        normed[...], qkv_w[:, heads_width : 2 * heads_width], preferred_element_type=f32
    )
    for h in range(heads):
        k_all[h, own:] = rotated(keys[:, h * head : (h + 1) * head]).astype(bf16)
    values = jnp.dot(normed[...], qkv_w[:, 2 * heads_width :], preferred_element_type=f32)
    for h in range(heads):
        v_all[h, own:] = values[:, h * head : (h + 1) * head].astype(bf16)
    for w in reversed(range(windows - 1)):

        @pl.when(at.ep + (windows - 1 - w) < count)
        def _():
            for kind in (0, 1):
                kv_copy(kind, w).start()

    gather.spread(0)
    queries = jnp.dot(normed[...], qkv_w[:, :heads_width], preferred_element_type=f32)
    for h in range(heads):
        q_out[h] = rotated(queries[:, h * head : (h + 1) * head]).astype(bf16)
    gather.last_hop(0)
    gather.begin(1)
    turned[...] = normed[...].T
    turned_copy = pltpu.make_async_copy(turned, turned_out, load_sem.at[0])
    turned_copy.start()
    gather.spread(1)
    for w in range(windows - 1):

        @pl.when(at.ep < windows - 1 - w)
        def _():
            for held in (k_all, v_all):
                held[:, w * tokens : (w + 1) * tokens] = jnp.zeros((heads, tokens, head), bf16)

        @pl.when(at.ep >= windows - 1 - w)
        def _():
            for kind in (0, 1):
                kv_arrival(kind, w).wait_recv()

    outs = [
        pltpu.make_async_copy(src, dst, load_sem.at[i])
        for i, (src, dst) in ((1, (k_all, k_out)), (3, (v_all, v_out)))
    ]
    for copy in outs:
        copy.start()
    due = [functools.partial(gather.last_hop, 1)]
    for j in range(2, depth):
        due.append(functools.partial(gather.begin, j))
        due.append(functools.partial(gather.spread, j))
        due.append(functools.partial(gather.last_hop, j))

    def head_body(h, carry):
        q = q_out[h]
        peak = jnp.full((1, tokens), -1e30, f32)
        for w in range(windows):
            some = slice(w * tokens, (w + 1) * tokens)
            scores = lax.dot_general(k_all[h, some], q, across, preferred_element_type=f32)
            key_at = lax.broadcasted_iota(jnp.int32, scores.shape, 0)
            key_at = key_at + (at.ep + w + 1 - windows) * tokens
            allowed = (key_at >= query_start[...]) & (key_at <= query_at[...])
            scores = jnp.where(allowed, scores * score_scale, -1e30)
            scores_of[w] = scores
            peak = jnp.maximum(peak, jnp.max(scores, axis=0, keepdims=True))
        total = jnp.zeros((1, tokens), f32)
        for w in range(windows):
            expo = jnp.exp(scores_of[w] - peak)
            scores_of[w] = expo
            total = total + jnp.sum(expo, axis=0, keepdims=True)
        lse_out[h] = peak + jnp.log(total)
        each = 1.0 / total
        attended = jnp.zeros((head, tokens), f32)
        for w in range(windows):
            some = slice(w * tokens, (w + 1) * tokens)
            probs = (scores_of[w] * each).astype(bf16)
            attended = attended + jnp.dot(
                v_all[h, some].T, probs, preferred_element_type=f32
            )
        here = pl.ds(pl.multiple_of(h * head, head), head)
        attended_out[:, here] = attended.T.astype(bf16)
        for i in range(heads):

            @pl.when(h == i)
            def _():
                for action in due[i : i + 1]:
                    action()

        return carry

    lax.fori_loop(0, heads, head_body, 0)
    loads[2].wait()
    strips = 4
    strip = width // strips
    for n in range(strips):
        some = slice(n * strip, (n + 1) * strip)
        product = lax.dot_general(
            attended_out[...], out_w[some], across, preferred_element_type=f32
        )
        part[:, :, :, some] = product.astype(bf16).reshape(2, 2, quarter, strip)
    core_copy().start()
    rest = due[heads:]
    for action in rest[:2]:
        action()
    core_copy().wait()
    for x in (0, 1):
        part[x, at.c] = part[x, at.c] + core_got[x]
    x_copy().start()
    for action in rest[2:]:
        action()
    x_copy().wait()

    def end_body(i, carry):
        here = pl.ds(pl.multiple_of(i * few, few), few)
        total = part[at.x, at.c, here].astype(f32) + x_got[here].astype(f32)
        resid = tokens_in[here].astype(f32) + total
        scale = lax.rsqrt(jnp.mean(resid * resid, axis=1, keepdims=True) + epsilon)
        resid_out[here] = resid
        rows_out[here] = (resid * scale * gain_in[...]).astype(bf16)
        return carry

    lax.fori_loop(0, quarter // few, end_body, 0)
    turned_copy.wait()
    for copy in outs:
        copy.wait()
    for w in range(windows - 1):

        @pl.when(at.ep + (windows - 1 - w) < count)
        def _():
            for kind in (0, 1):
                kv_copy(kind, w).wait_send()

    gather.finish()


def attention_front(block, weights, upstream, in_place, heads, scale):
    tokens, width = block.shape
    quarter, wide = upstream.shape
    depth = lax.axis_size("ep") // 2
    head, windows = HD, 3
    f32, bf16 = jnp.float32, jnp.bfloat16
    anywhere = pl.BlockSpec(memory_space=pl.ANY)
    in_vmem = pl.BlockSpec(memory_space=pltpu.VMEM)
    dma = pltpu.SemaphoreType.DMA
    shape = jax.ShapeDtypeStruct
    window = (heads, windows * tokens, head)
    outs = pl.pallas_call(
        functools.partial(front_kernel, scale),
        out_shape=(
            shape((depth, 2, 2, 2, quarter, wide), bf16),
            shape((width, tokens), bf16),
            shape(window, bf16),
            shape(window, bf16),
            shape((heads, tokens, head), bf16),
            shape((heads, 1, tokens), f32),
            shape((tokens, heads * head), bf16),
            shape((quarter, width), f32),
            shape((quarter, width), bf16),
        ),
        in_specs=[anywhere] * 3 + [in_vmem] * len(in_place),
        out_specs=(anywhere,) * 4 + (in_vmem,) * 5,
        scratch_shapes=[
            pltpu.VMEM((tokens, width), bf16),
            pltpu.VMEM((width, tokens), bf16),
            pltpu.VMEM((width, 3 * heads * head), bf16),
            pltpu.VMEM((width, heads * head), bf16),
            pltpu.VMEM(window, bf16),
            pltpu.VMEM(window, bf16),
            pltpu.VMEM((windows, tokens, tokens), f32),
            pltpu.VMEM((2, 2, quarter, width), bf16),
            pltpu.VMEM((2, quarter, width), bf16),
            pltpu.VMEM((quarter, width), bf16),
            dma((4,)),
            dma((2 * depth,)),
            dma((depth - 1,)),
            dma((depth, 8)),
            dma((depth, 8)),
            dma((2, windows - 1)),
            dma((2, windows - 1)),
            dma((2,)),
            dma((2,)),
        ],
        compiler_params=pltpu.CompilerParams(
            collective_id=5, has_side_effects=True, vmem_limit_bytes=50 * 2**20
        ),
        cost_estimate=pl.CostEstimate(
            flops=8 * tokens * width * heads * head,
            bytes_accessed=2 * 8 * depth * quarter * wide,
            transcendentals=heads * tokens * windows * tokens,
        ),
        name="attention_front",
    )(block, weights, upstream, *in_place)
    return (outs[0].reshape(8 * depth * quarter, wide),) + tuple(outs[1:])


def back_kernel(
    units,
    score_scale,
    d_low_in,
    weights_in,
    q_in,
    k_in,
    v_in,
    turned_in,
    block_in,
    rows_in,
    d_pair_in,
    upstream_in,
    weighted_in,
    lse_in,
    query_start,
    query_at,
    cos_in,
    sin_in,
    own_rows_in,
    gain_in,
    d_resid_in,
    gain_two_in,
    side_in,
    out,
    small_out,
    block_out,
    d_rows_out,
    pieces_got,
    gate_out,
    up_out,
    down_out,
    qkv_w,
    turned,
    d_out,
    d_got,
    d_own,
    d_proj,
    part,
    core_got,
    x_got,
    d_rows,
    own,
    y_out,
    hop,
    from_z,
    small_own,
    small_hop,
    small_z,
    small,
    small_got,
    pieces,
    load_sem,
    d_send,
    d_recv,
    tp_send,
    tp_recv,
    y_send,
    y_recv,
    z_send,
    z_recv,
    little_send,
    little_recv,
    small_send,
    small_recv,
    swap_send,
    swap_recv,
    rows_send,
    rows_recv,
    own_sem,
    tile_sem,
    store_sem,
    strip_sem,
):
    at = Place()
    depth = at.depth
    count = 2 * depth
    heads, tokens, head = q_in.shape
    heads_width = heads * head
    windows = k_in.shape[1] // tokens
    quarter, width = d_rows.shape
    rows = out.shape[0]
    f32, bf16 = jnp.float32, jnp.bfloat16
    across = (((1,), (1,)), ((), ()))
    slot_here, slot_hidden, shared_hidden = units
    routed = slot_here * slot_hidden
    hidden = weighted_in.shape[2]
    few = 16

    def d_copy(w, h):
        peer = (at.ep - (2 - w), at.tp)
        return remote(d_out.at[w, h], d_got.at[w, h], d_send.at[w, h], d_recv.at[w, h], peer)

    def d_arrival(w, h):
        peer = (at.ep + (2 - w), at.tp)
        dst = d_got.at[w, h]
        return remote(dst, dst, d_send.at[w, h], d_recv.at[w, h], peer)

    def core_copy():
        return remote(part.at[:, 1 - at.c], core_got, tp_send.at[0], tp_recv.at[0], at.next_core)

    def x_copy():
        return remote(part.at[1 - at.x, at.c], x_got, tp_send.at[1], tp_recv.at[1], at.next_x)

    cuts = (pl.ds(0, heads_width), pl.ds(heads_width, 2 * heads_width))

    def y_copy(q, j):
        return remote(
            y_out.at[j, :, cuts[q]], hop.at[j, :, cuts[q]], y_send.at[q, j], y_recv.at[q, j], at.next_y
        )

    def z_copy(q, j):
        down = (at.z + j) // depth
        upper, lower = depth if j == 1 else j - 1, 0 if j == depth - 1 else j + 1
        slot = upper + down * (lower - upper)
        return remote(
            own.at[j, :, cuts[q]],
            from_z.at[slot, :, cuts[q]],
            z_send.at[q, j],
            z_recv.at[q, slot],
            at.at_z(at.z + 1 - 2 * down),
        )

    def z_arrival(q, slot):
        dst = from_z.at[slot, :, cuts[q]]
        return remote(dst, dst, z_send.at[q, 0], z_recv.at[q, slot], at.next_y)

    def little_y(j):
        return remote(
            small_own.at[at.ahead(j), 1 - at.y],
            small_hop.at[j],
            little_send.at[0, j],
            little_recv.at[0, j],
            at.next_y,
        )

    def little_z(j):
        return remote(
            small_own.at[at.ahead(j), at.y],
            small_z.at[j - 1],
            little_send.at[1, j],
            little_recv.at[1, j],
            at.at_z(at.ahead(j)),
        )

    def small_copy(kind):
        peer = at.next_core if kind == 0 else at.next_x
        return remote(
            small.at[kind], small_got.at[kind], small_send.at[kind], small_recv.at[kind], peer
        )

    ends = ((block_in, block_out), (d_rows, d_rows_out))

    def rows_copy(a, kind):
        mine, gathered = ends[a]
        if kind == 2:
            src = dst = gathered.at[1 - at.x, at.c]
        else:
            src, dst = mine, gathered.at[at.x, at.c]
        peer = at.next_x if kind == 0 else at.next_core
        return remote(src, dst, rows_send.at[a, kind], rows_recv.at[a, kind], peer)

    def rows_own(a):
        mine, gathered = ends[a]
        return pltpu.make_async_copy(mine, gathered.at[at.x, at.c], own_sem.at[a])

    def rows_begin(a):
        for kind in (0, 1):
            rows_copy(a, kind).start()
        rows_own(a).start()

    def rows_pass_on(a):
        rows_copy(a, 0).wait_recv()
        rows_copy(a, 2).start()

    def rows_end(a):
        rows_own(a).wait()
        rows_copy(a, 0).wait_send()
        rows_copy(a, 1).wait()
        rows_copy(a, 2).wait()

    def swap_copies(p, leave):
        some = pl.ds(p * shared_hidden, shared_hidden)
        copies = []
        for k in range(1, count):
            to, back = lax.rem(at.ep + k, count), lax.rem(at.ep + count - k, count)
            if leave:
                src, dst, peer = pieces.at[to, some], pieces_got.at[at.ep, some], to
            else:
                src, dst, peer = pieces.at[back, some], pieces_got.at[back, some], back
            copies.append(remote(src, dst, swap_send.at[p, k], swap_recv.at[p, k], (peer, at.tp)))
        return copies

    def swap_own(p):
        some = pl.ds(p * shared_hidden, shared_hidden)
        return pltpu.make_async_copy(
            pieces.at[at.ep, some], pieces_got.at[at.ep, some], own_sem.at[2 + p]
        )

    strips = 4
    strip = width // strips

    def load_strip(n):
        src = weights_in.at[pl.ds(n * strip, strip), pl.ds(0, 3 * heads_width)]
        return pltpu.make_async_copy(src, qkv_w.at[n % 2], strip_sem.at[n % 2])

    late_load = pltpu.make_async_copy(turned_in, turned, load_sem.at[1])
    lane = lax.broadcasted_iota(jnp.int32, (tokens, head), 1)
    sign = jnp.where(lane < head // 2, -1.0, 1.0)

    def unrotated(grads):
        turned_part = pltpu.roll(grads * sin_in[...], head // 2, 1) * sign
        return grads * cos_in[...] - turned_part

    def attention(d_low, out_w, q_all, k_all, v_all, d_att, probs, d_probs):
        pairs = (
            (d_low_in, d_low),
            (weights_in.at[:, pl.ds(3 * heads_width, heads_width)], out_w),
            (q_in, q_all),
            (k_in, k_all),
            (v_in, v_all),
        )
        copies = [
            pltpu.make_async_copy(src, dst, load_sem.at[2 + i])
            for i, (src, dst) in enumerate(pairs)
        ]
        for copy in copies + [late_load, load_strip(0), load_strip(1)]:
            copy.start()
        at.greet_row()
        rows_begin(0)
        copies[0].wait()
        copies[1].wait()
        d_attended = jnp.dot(d_low[...], out_w[...], preferred_element_type=f32).astype(bf16)
        for h in range(heads):
            d_att[h] = d_attended[:, h * head : (h + 1) * head]
        for copy in copies[2:]:
            copy.wait()

        def head_body(h, carry):
            queries, d_a = q_all[h], d_att[h]
            delta = jnp.zeros((1, tokens), f32)
            for w in range(windows):
                some = slice(w * tokens, (w + 1) * tokens)
                scores = lax.dot_general(
                    k_all[h, some], queries, across, preferred_element_type=f32
                )
                key_at = lax.broadcasted_iota(jnp.int32, scores.shape, 0)
                key_at = key_at + (at.ep + w + 1 - windows) * tokens
                allowed = (key_at >= query_start[...]) & (key_at <= query_at[...])
                p = jnp.where(allowed, jnp.exp(scores * score_scale - lse_in[h]), 0.0)
                d_p = lax.dot_general(v_all[h, some], d_a, across, preferred_element_type=f32)
                probs[w] = p
                d_probs[w] = d_p
                delta = delta + jnp.sum(p * d_p, axis=0, keepdims=True)
            d_queries = jnp.zeros((head, tokens), f32)
            for w in range(windows):
                some = slice(w * tokens, (w + 1) * tokens)
                p = probs[w]
                d_scores = (p * (d_probs[w] - delta)).astype(bf16)
                d_keys = jnp.dot(d_scores, queries, preferred_element_type=f32) * score_scale
                d_values = jnp.dot(p.astype(bf16), d_a, preferred_element_type=f32)
                if w < windows - 1:
                    d_out[w, h, :, :head] = d_keys.astype(bf16)
                    d_out[w, h, :, head:] = d_values.astype(bf16)

                    @pl.when(at.ep >= 2 - w)
                    def _():
                        d_copy(w, h).start()

                else:
                    d_own[h, :, :head] = d_keys
                    d_own[h, :, head:] = d_values
                d_queries = d_queries + jnp.dot(
                    k_all[h, some].T, d_scores, preferred_element_type=f32
                )
            here = pl.ds(pl.multiple_of(h * head, head), head)
            d_proj[:, here] = unrotated((d_queries * score_scale).T).astype(bf16)
            return carry

        lax.fori_loop(0, heads, head_body, 0)

    pl.run_scoped(
        attention,
        pltpu.VMEM((tokens, width), bf16),
        pltpu.VMEM((width, heads_width), bf16),
        pltpu.VMEM((heads, tokens, head), bf16),
        pltpu.VMEM((heads, windows * tokens, head), bf16),
        pltpu.VMEM((heads, windows * tokens, head), bf16),
        pltpu.VMEM((heads, tokens, head), bf16),
        pltpu.VMEM((windows, tokens, tokens), f32),
        pltpu.VMEM((windows, tokens, tokens), f32),
    )
    order = [j for j in range(depth - 1, 0, -1)] + [0]

    def own_body(h, carry):
        for w in range(windows - 1):

            @pl.when(at.ep + (2 - w) < count)
            def _():
                d_arrival(w, h).wait_recv()
                d_own[h] += d_got[w, h].astype(f32)

        k_here = pl.ds(pl.multiple_of(heads_width + h * head, head), head)
        v_here = pl.ds(pl.multiple_of(2 * heads_width + h * head, head), head)
        d_proj[:, k_here] = unrotated(d_own[h, :, :head]).astype(bf16)
        d_proj[:, v_here] = d_own[h, :, head:].astype(bf16)
        return carry

    def weight_rows(into, q, z, y):
        here = pl.ds(pl.multiple_of((z * 2 + y) * rows, rows), rows)
        product = jnp.dot(turned[here], d_proj[:, cuts[q]], preferred_element_type=f32)
        into[:, cuts[q]] = product.astype(bf16)

    def begin_sums(q):
        for j in order:
            weight_rows(y_out.at[j], q, at.ahead(j), 1 - at.y)
            y_copy(q, j).start()

    def own_sums(q):
        for j in order:
            weight_rows(own.at[j], q, at.ahead(j), at.y)

    def projections():
        lax.fori_loop(0, heads, own_body, 0)
        for n in range(strips):
            some = slice(n * strip, (n + 1) * strip)
            load_strip(n).wait()
            product = lax.dot_general(
                d_proj[...], qkv_w[n % 2], across, preferred_element_type=f32
            )
            part[:, :, :, some] = product.astype(bf16).reshape(2, 2, quarter, strip)
            if n + 2 < strips:
                load_strip(n + 2).start()
        core_copy().start()
        begin_sums(1)
        core_copy().wait()
        for x in (0, 1):
            part[x, at.c] = part[x, at.c] + core_got[x]
        x_copy().start()
        own_sums(1)
        x_copy().wait()

        def end_body(i, carry):
            here = pl.ds(pl.multiple_of(i * few, few), few)
            grads = part[at.x, at.c, here].astype(f32) + x_got[here].astype(f32)
            inputs = own_rows_in[here].astype(f32)
            scale = lax.rsqrt(jnp.mean(inputs * inputs, axis=1, keepdims=True) + epsilon)
            unit_rows = inputs * scale
            scaled = grads * gain_in[...]
            inner = jnp.mean(scaled * unit_rows, axis=1, keepdims=True)
            total = d_resid_in[here] + scale * (scaled - unit_rows * inner)
            d_rows[here] = total.astype(bf16)
            return carry + jnp.sum(grads * unit_rows, axis=0, keepdims=True)

        d_gain = lax.fori_loop(0, quarter // few, end_body, jnp.zeros((1, width), f32))
        rows_begin(1)
        line = lax.broadcasted_iota(jnp.int32, (128, rows), 0)
        for e in range(count):
            some = slice(e * rows, (e + 1) * rows)
            gains = jnp.where(line == 0, d_gain[:, some], 0.0)
            gains = jnp.where(line == 1, gain_two_in[:, some], gains)
            small_own[e // 2, e % 2] = (gains.T + side_in[some]).astype(bf16)
        for j in order:
            little_y(j).start()

    def add_rows(q, j, other):
        def body(i, carry):
            some = pl.ds(pl.multiple_of(i * few, few), few)
            own[j, some, cuts[q]] = own[j, some, cuts[q]] + other[j, some, cuts[q]]
            return carry

        lax.fori_loop(0, rows // few, body, 0)

    def pass_on(q, turn, slots):
        for j in slots:
            down = (at.z + j) // depth
            before = down * (depth - 1 - at.z) + (1 - down) * at.z

            @pl.when(before == turn)
            def _():
                if turn > 0:
                    z_arrival(q, j).wait_recv()
                    add_rows(q, j, from_z)
                z_copy(q, j).start()

    def after_y(q, j):
        y_copy(q, j).wait_recv()
        add_rows(q, j, hop)
        if j > 0:
            pass_on(q, 0, [j])

    def after_little():
        for j in order:
            little_y(j).wait_recv()
            here = small_own.at[at.ahead(j), at.y]
            here[...] = here[...] + small_hop[j]
            if j > 0:
                little_z(j).start()

    hooks = {(0, 0): [functools.partial(rows_pass_on, 0)]}
    for i, j in enumerate(order):
        here = (1, min(count // 2 + i, count - 1))
        hooks.setdefault(here, []).append(functools.partial(after_y, 0, j))
    hooks[(2, 2)] = [functools.partial(rows_pass_on, 1)]
    hooks[(2, 3)] = [after_little]
    for turn in range(1, depth - 1):
        here = (2, min(4 * (turn - 1), count - 1))
        hooks.setdefault(here, []).append(functools.partial(pass_on, 0, turn, order[:-1]))
    last_hooks = []
    for i, j in enumerate(order):
        when = 2 + 5 * i
        due = functools.partial(after_y, 1, j)
        if when < count:
            hooks.setdefault((2, when), []).append(due)
        else:
            last_hooks.append(due)

    def weight_gradients(turned_left, left_tile, right_part, staging):
        lefts = (
            lambda tile: d_pair_in.at[tile, :, pl.ds(0, hidden)],
            lambda tile: d_pair_in.at[tile, :, pl.ds(hidden, hidden)],
            lambda tile: weighted_in.at[tile],
        )
        rights = (rows_in, rows_in, upstream_in)
        results = (gate_out, up_out, down_out)
        columns = width // count

        def load_left(p, tile):
            slot = lax.rem(tile, 2)
            return pltpu.make_async_copy(
                lefts[p](tile), left_tile.at[slot], tile_sem.at[0, slot]
            )

        def load_right(p, n):
            slot = lax.rem(n, 2)
            here = pl.ds(pl.multiple_of(n * columns, columns), columns)
            return pltpu.make_async_copy(
                rights[p].at[:, :, here], right_part.at[slot], tile_sem.at[1, slot]
            )

        def store(p, n):
            slot = lax.rem(n, 2)
            here = pl.ds(pl.multiple_of(n * columns, columns), columns)
            return pltpu.make_async_copy(
                staging.at[slot], results[p].at[:, here], store_sem.at[slot]
            )

        def turn_left(p, tile):
            load_left(p, tile).wait()

            @pl.when(tile + 1 < count)
            def _():
                load_left(p, tile + 1).start()

            here = pl.ds(pl.multiple_of(tile * tokens, tokens), tokens)
            turned_left[:, here] = left_tile[lax.rem(tile, 2)].T

        def run_pass(p):
            def part_body(n, carry):
                slot = lax.rem(n, 2)
                load_right(p, n).wait()

                @pl.when(n + 1 < count)
                def _():
                    load_right(p, n + 1).start()

                if p < 2:

                    @pl.when(n + 1 == count)
                    def _():
                        load_right(p + 1, 0).start()

                @pl.when(n >= 2)
                def _():
                    store(p, n - 2).wait()

                product = jnp.dot(
                    turned_left[...],
                    right_part[slot].reshape(count * tokens, columns),
                    preferred_element_type=f32,
                )
                staging[slot] = product[:routed].astype(bf16)
                pieces[n, p * shared_hidden : (p + 1) * shared_hidden] = product[
                    routed : routed + shared_hidden
                ].astype(bf16)
                store(p, n).start()
                for (hook_pass, hook_part), actions in hooks.items():
                    if hook_pass == p:

                        @pl.when(n == hook_part)
                        def _():
                            for action in actions:
                                action()

                return carry

            def turn_body(tile, carry):
                turn_left(p, tile)
                return carry

            lax.fori_loop(0, count, turn_body, 0)
            if p < 2:
                load_left(p + 1, 0).start()
            lax.fori_loop(0, count, part_body, 0)
            for n in (count - 2, count - 1):
                store(p, n).wait()
            swap_own(p).start()
            if p > 0:
                start_swap(p)

        def start_swap(p):
            for copy in swap_copies(p, True):
                copy.start()

        hooks.setdefault((1, count - 2), []).append(functools.partial(start_swap, 0))
        load_left(0, 0).start()
        load_right(0, 0).start()
        late_load.wait()
        begin_sums(0)
        own_sums(0)

        run_pass(0)
        run_pass(1)
        projections()
        run_pass(2)
        for action in last_hooks:
            action()
        for turn in range(1, depth - 1):
            pass_on(1, turn, order[:-1])

    pl.run_scoped(
        weight_gradients,
        pltpu.VMEM((hidden, count * tokens), bf16),
        pltpu.VMEM((2, tokens, hidden), bf16),
        pltpu.VMEM((2, count, tokens, width // count), bf16),
        pltpu.VMEM((2, routed, width // count), bf16),
    )
    total = small_own[at.z, at.y].astype(f32)
    for j in range(1, depth):
        little_z(j).wait_recv()
        total = total + small_z[j - 1].astype(f32)
    for kind in (0, 1):
        small[kind] = total
        small_copy(kind).start()
        small_copy(kind).wait()
        total = small[kind] + small_got[kind]
    small_out[...] = total

    def total_body(i, carry):
        some = pl.ds(pl.multiple_of(i * few, few), few)
        out[some] = own[0, some].astype(f32)
        return carry

    lax.fori_loop(0, rows // few, total_body, 0)

    def add_arrived(slot):
        for q in (0, 1):
            z_arrival(q, slot).wait_recv()

        def body(i, carry):
            some = pl.ds(pl.multiple_of(i * few, few), few)
            out[some] += from_z[slot, some].astype(f32)
            return carry

        lax.fori_loop(0, rows // few, body, 0)

    pl.when(at.z + 1 < depth)(lambda: add_arrived(0))
    pl.when(at.z > 0)(lambda: add_arrived(depth))
    for j in range(depth):
        little_y(j).wait_send()
        if j > 0:
            little_z(j).wait_send()
        for q in (0, 1):
            y_copy(q, j).wait_send()
            if j > 0:
                z_copy(q, j).wait_send()
    for a in (0, 1):
        rows_end(a)
    for p in range(3):
        swap_own(p).wait()
        for copy in swap_copies(p, False):
            copy.wait_recv()
        for copy in swap_copies(p, True):
            copy.wait_send()

    def finish(h, carry):
        for w in range(windows - 1):

            @pl.when(at.ep >= 2 - w)
            def _():
                d_copy(w, h).wait_send()

        return carry

    lax.fori_loop(0, heads, finish, 0)


def backward(large, tiles_of, in_place, units, scale):
    d_low, _, queries, keys = large[:4]
    heads, tokens, head = queries.shape
    width = d_low.shape[1]
    ep_count = lax.axis_size("ep")
    depth, rows = ep_count // 2, width // ep_count
    quarter = tokens // lax.axis_size("tp")
    windows = keys.shape[1] // tokens
    columns = 3 * heads * head
    hidden = tiles_of[3].shape[2]
    slot_here, slot_hidden, shared_hidden = units
    f32, bf16 = jnp.float32, jnp.bfloat16
    anywhere = pl.BlockSpec(memory_space=pl.ANY)
    in_vmem = pl.BlockSpec(memory_space=pltpu.VMEM)
    dma = pltpu.SemaphoreType.DMA
    pieces = (ep_count, 3 * shared_hidden, rows)
    gathered = jax.ShapeDtypeStruct((2, 2, quarter, width), bf16)
    routed = jax.ShapeDtypeStruct((slot_here * slot_hidden, width), bf16)

    def vmem(*shape, dtype=bf16):
        return pltpu.VMEM(shape, dtype)

    out, small, block_out, d_rows, pieces, gate, up, down = pl.pallas_call(
        functools.partial(back_kernel, units, scale),
        out_shape=(
            jax.ShapeDtypeStruct((rows, columns), f32),
            jax.ShapeDtypeStruct((rows, 128), f32),
            gathered,
            gathered,
            jax.ShapeDtypeStruct(pieces, bf16),
            routed,
            routed,
            routed,
        ),
        in_specs=[anywhere] * (len(large) + len(tiles_of)) + [in_vmem] * len(in_place),
        out_specs=(in_vmem, in_vmem) + (anywhere,) * 6,
        scratch_shapes=[
            vmem(2, width // 4, columns),
            vmem(width, tokens),
            vmem(windows - 1, heads, tokens, 2 * head),
            vmem(windows - 1, heads, tokens, 2 * head),
            vmem(heads, tokens, 2 * head, dtype=f32),
            vmem(tokens, columns),
            vmem(2, 2, quarter, width),
            vmem(2, quarter, width),
            vmem(quarter, width),
            vmem(quarter, width),
            vmem(depth, rows, columns),
            vmem(depth, rows, columns),
            vmem(depth, rows, columns),
            vmem(depth + 1, rows, columns),
            vmem(depth, 2, rows, 128),
            vmem(depth, rows, 128),
            vmem(depth - 1, rows, 128),
            vmem(2, rows, 128, dtype=f32),
            vmem(2, rows, 128, dtype=f32),
            vmem(*pieces),
            dma((7,)),
            dma((windows - 1, heads)),
            dma((windows - 1, heads)),
            dma((2,)),
            dma((2,)),
            dma((2, depth)),
            dma((2, depth)),
            dma((2, depth)),
            dma((2, depth + 1)),
            dma((2, depth)),
            dma((2, depth)),
            dma((2,)),
            dma((2,)),
            dma((3, ep_count)),
            dma((3, ep_count)),
            dma((2, 3)),
            dma((2, 3)),
            dma((5,)),
            dma((2, 2)),
            dma((2,)),
            dma((2,)),
        ],
        compiler_params=pltpu.CompilerParams(
            collective_id=4, has_side_effects=True, vmem_limit_bytes=62 * 2**20
        ),
        cost_estimate=pl.CostEstimate(
            flops=6 * ep_count * tokens * width * hidden,
            bytes_accessed=8 * ep_count * tokens * width,
            transcendentals=heads * tokens * windows * tokens,
        ),
        name="backward",
    )(*large, *tiles_of, *in_place)
    block_out, d_rows = [array.reshape(4 * quarter, width) for array in (block_out, d_rows)]
    return out, small, block_out, d_rows, pieces, (gate, up, down)


def shared_pieces(weights, ep_count):
    rows, hidden = weights[0].shape
    units = hidden // ep_count
    return jnp.concatenate([weight.T.reshape(ep_count, units, rows) for weight in weights], axis=1)


def shared_whole(pieces, count):
    ep_count, units, columns = pieces.shape
    units = units // count
    pieces = pieces.reshape(ep_count, count, units, columns).astype(jnp.float32)
    return [pieces[:, i].reshape(ep_count * units, columns).T for i in range(count)]


def dense_body(
    tokens,
    lengths,
    routes,
    attn_gain,
    w_query,
    w_key,
    w_value,
    w_out,
    ffn_gain,
    w_router,
    shared_mix,
    shared_gate,
    shared_up,
    shared_down,
    expert_gate,
    expert_up,
    expert_down,
    cotangent,
):
    rows_here, width = tokens.shape
    ep_count = lax.axis_size("ep")
    tp_count = lax.axis_size("tp")
    ep_index = lax.axis_index("ep")
    offset = ep_index * rows_here
    quarter = rows_here // tp_count
    first_row = lax.axis_index("tp") * quarter
    slot_here, slot_hidden = expert_gate.shape[0], expert_gate.shape[1]
    expert_count = w_router.shape[1]
    bf16, f32 = jnp.bfloat16, jnp.float32

    def my_rows(array):
        return lax.dynamic_slice_in_dim(array, first_row, quarter, 0)

    side_columns = jnp.concatenate(
        [attn_gain[:, None], ffn_gain[:, None], shared_mix[:, None], w_router], axis=1
    )
    side_columns = jnp.pad(side_columns, ((0, 0), (0, -side_columns.shape[1] % 128)))
    joined_weights, pieces = gather_over_ep(
        jnp.concatenate([w_query, w_key, w_value, w_out, side_columns], axis=1),
        shared_pieces((shared_gate, shared_up, shared_down), ep_count),
    )
    heads_width = w_query.shape[1]
    side_weight = joined_weights[:, 4 * heads_width :]
    picked = jnp.any(
        my_rows(routes)[:, :, None] == jnp.arange(expert_count, dtype=jnp.int32), axis=1
    )
    picked_lanes = jnp.pad(picked.astype(bf16), ((0, 0), (3, 125 - expert_count)))
    upstream_rows = jnp.concatenate([my_rows(cotangent), picked_lanes], axis=1)
    shared_units = pieces.shape[1] // 3
    routed_units = slot_here * slot_hidden
    heads_here = heads_width // HD
    score_scale = HD ** (-0.5)
    first_norm_scale = side_weight[:, 0].astype(f32)
    second_norm_scale = side_weight[:, 1].astype(f32)
    query_at = offset + jnp.arange(rows_here, dtype=jnp.int32)
    _, query_pos = sequence_info(lengths, query_at)
    cosine, sine = rope_tables(query_pos, HD)
    tables = (cosine[:, 0], sine[:, 0], (query_at - query_pos)[None, :], query_at[None, :])
    (
        upstream_all,
        normed_one_turned,
        keys_win,
        values_win,
        queries,
        log_total,
        attended,
        resid,
        normed_two,
    ) = attention_front(
        tokens,
        joined_weights,
        upstream_rows,
        tables + (my_rows(tokens), first_norm_scale[None, :], second_norm_scale[None, :]),
        heads_here,
        score_scale,
    )
    (
        normed_all,
        weighted_h,
        d_pair_pre,
        block_rows,
        d_resid_low,
        d_resid,
        grad_gain_two,
        d_side,
    ) = ffn_over_all(
        normed_two,
        upstream_all,
        (expert_gate, expert_up, expert_down),
        pieces,
        joined_weights,
        resid,
        second_norm_scale[None, :],
        (slot_here, slot_hidden, shared_units),
        expert_count,
    )
    grad_side = jnp.dot(normed_two.astype(f32).T, d_side, precision=highest)
    grad_out = jnp.einsum("td,th->dh", d_resid_low, attended, preferred_element_type=f32)
    grad_out = lax.psum_scatter(
        grad_out.astype(bf16), "ep", scatter_dimension=0, tiled=True
    ).astype(f32)
    tile_shape = (ep_count, rows_here, -1)
    tiles_of = tuple(
        array.reshape(tile_shape) for array in (normed_all, d_pair_pre, upstream_all, weighted_h)
    )
    units = (slot_here, slot_hidden, shared_units)
    column = jnp.arange(128, dtype=jnp.int32)
    large = (
        d_resid_low,
        joined_weights,
        queries,
        keys_win,
        values_win,
        normed_one_turned,
        block_rows,
    )
    in_place = (
        log_total,
        tables[2],
        tables[3],
        tables[0],
        tables[1],
        my_rows(tokens),
        first_norm_scale[None, :],
        d_resid,
        grad_gain_two[None, :],
        jnp.where(column >= 2, grad_side, 0.0),
    )
    grad_weights, small, block_out, grad_tokens, grad_pieces, grad_experts = backward(
        large, tiles_of, in_place, units, score_scale
    )
    grad_shared = shared_whole(grad_pieces, 3)
    grad_tokens = grad_tokens.astype(f32)
    grad_experts = [grad.astype(f32).reshape(expert_gate.shape) for grad in grad_experts]
    parts = [grad_weights[:, i * heads_width : (i + 1) * heads_width] for i in range(3)]
    return (
        block_out,
        grad_tokens,
        small[:, 0],
        parts[0],
        parts[1],
        parts[2],
        grad_out,
        small[:, 1],
        small[:, 3 : 3 + expert_count],
        small[:, 2],
        grad_shared[0],
        grad_shared[1],
        grad_shared[2],
        grad_experts[0],
        grad_experts[1],
        grad_experts[2],
    )


def chosen_body(*arrays):
    rows_here, top_count = arrays[2].shape
    slot_here, expert_count = arrays[14].shape[0], arrays[9].shape[1]
    capacity = rows_here * top_count * 7 // (5 * expert_count)
    grid_of_two = lax.axis_size("ep") % 2 == 0 and lax.axis_size("tp") == 4
    if grid_of_two and rows_here < 2 * slot_here * capacity:
        return dense_body(*arrays)
    return body(*arrays)


def solution(mesh):
    placed = (
        P("ep", None),
        P(),
        P("ep", None),
        P("ep"),
        P("ep", "tp"),
        P("ep", "tp"),
        P("ep", "tp"),
        P("ep", "tp"),
        P("ep"),
        P("ep", None),
        P("ep"),
        P("ep", "tp"),
        P("ep", "tp"),
        P("ep", "tp"),
        P("ep", "tp", None),
        P("ep", "tp", None),
        P("ep", "tp", None),
        P("ep", None),
    )
    return jax.shard_map(
        chosen_body,
        mesh=mesh,
        in_specs=placed,
        out_specs=(
            P("ep", None),
            P("ep", None),
            P("ep"),
            P("ep", "tp"),
            P("ep", "tp"),
            P("ep", "tp"),
            P("ep", "tp"),
            P("ep"),
            P("ep", None),
            P("ep"),
            P("ep", "tp"),
            P("ep", "tp"),
            P("ep", "tp"),
            P("ep", "tp", None),
            P("ep", "tp", None),
            P("ep", "tp", None),
        ),
        check_vma=False,
    )
```

```python
import functools

import jax
import jax.numpy as jnp
from jax import lax
from jax.experimental import pallas as pl
from jax.experimental.pallas import tpu as pltpu
from jax.sharding import PartitionSpec as P

HD = 128


epsilon = 1e-06
rope_base = 1000000.0
highest = lax.Precision.HIGHEST
MESH = pl.DeviceIdType.MESH


def passed_along(block, axis, distance):
    devices = range(lax.axis_size(axis))
    route = [(i - distance, i) for i in devices if i - distance in devices]
    return lax.ppermute(block, axis, route)


def rope_tables(positions, width):
    steps = jnp.arange(0, width, 2, dtype=jnp.float32) / width
    inverse = rope_base ** (-steps)
    angles = positions.astype(jnp.float32)[:, None] * inverse[None, :]
    angles = jnp.concatenate([angles, angles], axis=-1)
    return (jnp.cos(angles)[:, None, :], jnp.sin(angles)[:, None, :])


def turn_half(values):
    middle = values.shape[-1] // 2
    return jnp.concatenate([-values[..., middle:], values[..., :middle]], axis=-1)


def rotate(values, cosine, sine):
    return values * cosine + turn_half(values) * sine


def unrotate(grads, cosine, sine):
    return grads * cosine - turn_half(grads * sine)


def sequence_info(lengths, indices):
    starts = jnp.cumsum(lengths) - lengths
    inside = starts[None, :] <= indices[:, None]
    segment = jnp.sum(inside.astype(jnp.int32), axis=1) - 1
    first = jnp.max(jnp.where(inside, starts[None, :], -1), axis=1)
    return (segment, indices - first)


def norm_forward(values, gain):
    scale = lax.rsqrt(jnp.mean(values * values, axis=-1, keepdims=True) + epsilon)
    return (values * scale * gain, scale)


def norm_backward(values, scale, gain, grads):
    unit = values * scale
    scaled = grads * gain
    inner = jnp.mean(scaled * unit, axis=-1, keepdims=True)
    return (scale * (scaled - unit * inner), jnp.sum(grads * unit, axis=0))


def deliver(rows):
    arrived_rows = lax.all_to_all(rows, "ep", split_axis=0, concat_axis=0, tiled=True)
    return arrived_rows


def bring_back(parts, target, rows_here, top_count):
    moved = lax.all_to_all(parts, "ep", split_axis=0, concat_axis=0, tiled=True)
    piece = moved.shape[3]
    return moved.reshape(-1, piece)[target].reshape(rows_here, top_count, piece)


def body(
    tokens,
    lengths,
    routes,
    attn_gain,
    w_query,
    w_key,
    w_value,
    w_out,
    ffn_gain,
    w_router,
    shared_mix,
    shared_gate,
    shared_up,
    shared_down,
    expert_gate,
    expert_up,
    expert_down,
    cotangent,
):
    rows_here = tokens.shape[0]
    width = tokens.shape[1]
    ep_count = lax.axis_size("ep")
    offset = lax.axis_index("ep") * rows_here
    slot_here = expert_gate.shape[0]
    top_count = routes.shape[1]
    gathered = (
        lax.all_gather(attn_gain, "ep", axis=0, tiled=True),
        lax.all_gather(w_query, "ep", axis=0, tiled=True),
        lax.all_gather(w_key, "ep", axis=0, tiled=True),
        lax.all_gather(w_value, "ep", axis=0, tiled=True),
        lax.all_gather(w_out, "ep", axis=0, tiled=True),
        lax.all_gather(ffn_gain, "ep", axis=0, tiled=True),
        lax.all_gather(w_router, "ep", axis=0, tiled=True),
        lax.all_gather(shared_mix, "ep", axis=0, tiled=True),
        lax.all_gather(shared_gate, "ep", axis=0, tiled=True),
        lax.all_gather(shared_up, "ep", axis=0, tiled=True),
        lax.all_gather(shared_down, "ep", axis=0, tiled=True),
    )
    (
        gain_first,
        query_weight_matrix,
        key_weight_matrix,
        value_weight_matrix,
        output_weight,
        gain_second,
        router_weight,
        shared_mixer_weight,
        shared_gate_weight,
        shared_up_weight,
        shared_down_weight,
    ) = gathered
    expert_count = router_weight.shape[1]
    capacity = (rows_here * top_count * 7 // (5 * expert_count) + 7) // 8 * 8
    heads_here = query_weight_matrix.shape[1] // HD
    score_scale = HD ** (-0.5)
    first_norm_scale = gain_first.astype(jnp.float32)
    second_norm_scale = gain_second.astype(jnp.float32)
    layer_input = tokens.astype(jnp.float32)
    normed_wide, norm_one = norm_forward(layer_input, first_norm_scale)
    normed_one = normed_wide.astype(jnp.bfloat16)
    query_at = offset + jnp.arange(rows_here, dtype=jnp.int32)
    key_at = offset - 2 * rows_here + jnp.arange(3 * rows_here, dtype=jnp.int32)
    query_seg, query_pos = sequence_info(lengths, query_at)
    key_seg, _ = sequence_info(lengths, key_at)
    cosine, sine = rope_tables(query_pos, HD)
    query_pre = jnp.dot(
        normed_one, query_weight_matrix, preferred_element_type=jnp.float32
    ).reshape(rows_here, heads_here, HD)
    key_pre = jnp.dot(normed_one, key_weight_matrix, preferred_element_type=jnp.float32).reshape(
        rows_here, heads_here, HD
    )
    queries = rotate(query_pre, cosine, sine).astype(jnp.bfloat16)
    keys = rotate(key_pre, cosine, sine).astype(jnp.bfloat16)
    values = (
        jnp.dot(normed_one, value_weight_matrix, preferred_element_type=jnp.float32)
        .astype(jnp.bfloat16)
        .reshape(rows_here, heads_here, HD)
    )
    carried = jnp.stack([keys, values], axis=0)
    window = [carried]
    for hop in range(2):
        carried = passed_along(carried, "ep", 1)
        window = [carried] + window
    joined = jnp.concatenate(window, axis=1)
    keys_win = joined[0]
    values_win = joined[1]
    allowed = (
        (query_seg[:, None] == key_seg[None, :])
        & (key_at[None, :] <= query_at[:, None])
        & (key_at[None, :] >= 0)
    )
    scores = (
        jnp.einsum("qhd,khd->hqk", queries, keys_win, preferred_element_type=jnp.float32)
        * score_scale
    )
    masked = jnp.where(allowed[None], scores, -1e30)
    peak = jnp.max(masked, axis=-1, keepdims=True)
    expo = jnp.exp(masked - peak)
    total = jnp.sum(expo, axis=-1, keepdims=True)
    log_total = peak + jnp.log(total)
    weights = expo / total
    attended = jnp.einsum(
        "hqk,khd->qhd", weights.astype(jnp.bfloat16), values_win, preferred_element_type=jnp.float32
    )
    attended = attended.reshape(rows_here, heads_here * HD).astype(jnp.bfloat16)
    attn_part = jnp.einsum("th,dh->td", attended, output_weight, preferred_element_type=jnp.float32)
    resid = layer_input + lax.psum(attn_part, "tp")
    normed_two_wide, norm_two = norm_forward(resid, second_norm_scale)
    normed_two = normed_two_wide.astype(jnp.bfloat16)
    normed_two_f = normed_two.astype(jnp.float32)
    router_f = router_weight.astype(jnp.float32)
    mix_f = shared_mixer_weight.astype(jnp.float32)
    router = jax.nn.softmax(jnp.dot(normed_two_f, router_f, precision=highest), axis=-1)
    picked = routes[:, :, None] == jnp.arange(expert_count, dtype=jnp.int32)[None, None, :]
    gates = jnp.sum(jnp.where(picked, router[:, None, :], 0.0), axis=-1)
    mixer = jax.nn.sigmoid(jnp.dot(normed_two_f, mix_f, precision=highest))
    shared_g = jnp.dot(normed_two, shared_gate_weight, preferred_element_type=jnp.float32)
    shared_u = jnp.dot(normed_two, shared_up_weight, preferred_element_type=jnp.float32)
    shared_h = (jax.nn.silu(shared_g) * shared_u).astype(jnp.bfloat16)
    shared_part = jnp.einsum(
        "tf,df->td", shared_h, shared_down_weight, preferred_element_type=jnp.float32
    )
    flat = routes.reshape(-1)
    hot = (flat[:, None] == jnp.arange(expert_count, dtype=jnp.int32)[None, :]).astype(jnp.int32)
    rank = jnp.sum(jnp.cumsum(hot, axis=0) * hot, axis=1) - 1
    target = flat * capacity + rank
    slot_total = ep_count * slot_here * capacity
    owner_route = (
        jnp.zeros((slot_total,), jnp.int32)
        .at[target]
        .set(jnp.arange(rows_here * top_count, dtype=jnp.int32))
    )
    filled = jnp.zeros((slot_total,), jnp.bool_).at[target].set(True)
    owner_token = owner_route // top_count
    send_rows = jnp.where(filled[:, None], normed_two[owner_token], jnp.zeros((), jnp.bfloat16))
    arrived_rows = deliver(send_rows.reshape(ep_count, slot_here, capacity, width))
    route_g = jnp.einsum(
        "nscd,sfd->nscf", arrived_rows, expert_gate, preferred_element_type=jnp.float32
    )
    route_u = jnp.einsum(
        "nscd,sfd->nscf", arrived_rows, expert_up, preferred_element_type=jnp.float32
    )
    route_h = (jax.nn.silu(route_g) * route_u).astype(jnp.bfloat16)
    route_part = jnp.einsum(
        "nscf,sfd->nscd", route_h, expert_down, preferred_element_type=jnp.float32
    )
    back_rows = bring_back(route_part, target, rows_here, top_count)
    upstream = cotangent.astype(jnp.float32)
    routed = jnp.sum(back_rows * gates[:, :, None], axis=1)
    ffn_part = mixer[:, None] * shared_part + routed
    route_dot = jnp.sum(back_rows * upstream[:, None, :], axis=-1)
    shared_dot = jnp.sum(shared_part * upstream, axis=-1)
    ffn_total, d_gate, d_mixer = lax.psum((ffn_part, route_dot, shared_dot), "tp")
    block_out = (resid + ffn_total).astype(jnp.bfloat16)
    d_router = jnp.sum(jnp.where(picked, d_gate[:, :, None], 0.0), axis=1)
    d_logits = router * (d_router - jnp.sum(router * d_router, axis=-1, keepdims=True))
    d_mixlogit = d_mixer * mixer * (1.0 - mixer)
    side = jnp.dot(d_logits, router_f.T, precision=highest) + d_mixlogit[:, None] * mix_f[None, :]
    grad_router = jnp.dot(normed_two_f.T, d_logits, precision=highest)
    grad_mix = jnp.dot(d_mixlogit, normed_two_f, precision=highest)
    d_shared = (mixer[:, None] * upstream).astype(jnp.bfloat16)
    d_sh = jnp.dot(d_shared, shared_down_weight, preferred_element_type=jnp.float32)
    sig_shared = jax.nn.sigmoid(shared_g)
    d_sg = (d_sh * shared_u * sig_shared * (1.0 + shared_g * (1.0 - sig_shared))).astype(
        jnp.bfloat16
    )
    d_su = (d_sh * shared_g * sig_shared).astype(jnp.bfloat16)
    d_normed_part = jnp.einsum(
        "tf,df->td", d_sg, shared_gate_weight, preferred_element_type=jnp.float32
    )
    d_normed_part = d_normed_part + jnp.einsum(
        "tf,df->td", d_su, shared_up_weight, preferred_element_type=jnp.float32
    )
    grad_sgate = jnp.einsum("td,tf->df", normed_two, d_sg, preferred_element_type=jnp.float32)
    grad_sup = jnp.einsum("td,tf->df", normed_two, d_su, preferred_element_type=jnp.float32)
    grad_sdown = jnp.einsum("td,tf->df", d_shared, shared_h, preferred_element_type=jnp.float32)
    d_route = (
        (gates[:, :, None] * upstream[:, None, :])
        .astype(jnp.bfloat16)
        .reshape(rows_here * top_count, width)
    )
    send_grads = jnp.where(filled[:, None], d_route[owner_route], jnp.zeros((), jnp.bfloat16))
    received_grads = deliver(send_grads.reshape(ep_count, slot_here, capacity, width))
    d_rh = jnp.einsum(
        "nscd,sfd->nscf", received_grads, expert_down, preferred_element_type=jnp.float32
    )
    sig_route = jax.nn.sigmoid(route_g)
    d_rg = (d_rh * route_u * sig_route * (1.0 + route_g * (1.0 - sig_route))).astype(jnp.bfloat16)
    routed_up_gradient = (d_rh * route_g * sig_route).astype(jnp.bfloat16)
    row_grads = jnp.einsum("nscf,sfd->nscd", d_rg, expert_gate, preferred_element_type=jnp.float32)
    row_grads = row_grads + jnp.einsum(
        "nscf,sfd->nscd", routed_up_gradient, expert_up, preferred_element_type=jnp.float32
    )
    grad_egate = jnp.einsum(
        "qxba,qxbr->xar", d_rg, arrived_rows, preferred_element_type=jnp.float32
    )
    expert_up_gradient = jnp.einsum(
        "qxba,qxbr->xar", routed_up_gradient, arrived_rows, preferred_element_type=jnp.float32
    )
    grad_edown = jnp.einsum(
        "qxba,qxbr->xar", route_h, received_grads, preferred_element_type=jnp.float32
    )
    grads_back = bring_back(row_grads, target, rows_here, top_count)
    d_routed = jnp.sum(grads_back, axis=1)
    d_normed_two = lax.psum(d_normed_part + d_routed, "tp") + side
    d_resid_norm, grad_gain_two = norm_backward(resid, norm_two, second_norm_scale, d_normed_two)
    d_resid = upstream + d_resid_norm
    d_resid_low = d_resid.astype(jnp.bfloat16)
    grad_outw = jnp.einsum("td,th->dh", d_resid_low, attended, preferred_element_type=jnp.float32)
    d_attended = jnp.einsum(
        "td,dh->th", d_resid_low, output_weight, preferred_element_type=jnp.float32
    )
    d_attended = d_attended.astype(jnp.bfloat16).reshape(rows_here, heads_here, HD)
    scores_again = (
        jnp.einsum("qhd,khd->hqk", queries, keys_win, preferred_element_type=jnp.float32)
        * score_scale
    )
    probs = jnp.where(allowed[None], jnp.exp(scores_again - log_total), 0.0)
    d_probs = jnp.einsum("qhd,khd->hqk", d_attended, values_win, preferred_element_type=jnp.float32)
    delta = jnp.sum(probs * d_probs, axis=-1, keepdims=True)
    d_scores = (probs * (d_probs - delta)).astype(jnp.bfloat16)
    d_queries = (
        jnp.einsum("hqk,khd->qhd", d_scores, keys_win, preferred_element_type=jnp.float32)
        * score_scale
    )
    d_keys_win = (
        jnp.einsum("hqk,qhd->khd", d_scores, queries, preferred_element_type=jnp.float32)
        * score_scale
    )
    d_values_win = jnp.einsum(
        "hqk,qhd->khd", probs.astype(jnp.bfloat16), d_attended, preferred_element_type=jnp.float32
    )
    pair_grads = jnp.stack([d_keys_win, d_values_win], axis=0)
    older = pair_grads[:, :rows_here]
    later = [pair_grads[:, rows_here : 2 * rows_here], pair_grads[:, 2 * rows_here :]]
    running = older
    for hop in range(2):
        running = passed_along(running, "ep", -1)
        running = running + later[hop]
    d_query_pre = (
        unrotate(d_queries, cosine, sine).astype(jnp.bfloat16).reshape(rows_here, heads_here * HD)
    )
    d_key_pre = (
        unrotate(running[0], cosine, sine).astype(jnp.bfloat16).reshape(rows_here, heads_here * HD)
    )
    d_values = running[1].astype(jnp.bfloat16).reshape(rows_here, heads_here * HD)
    grad_queryw = jnp.einsum(
        "td,th->dh", normed_one, d_query_pre, preferred_element_type=jnp.float32
    )
    grad_keyw = jnp.einsum("td,th->dh", normed_one, d_key_pre, preferred_element_type=jnp.float32)
    grad_valuew = jnp.einsum("td,th->dh", normed_one, d_values, preferred_element_type=jnp.float32)
    d_normed_one = jnp.einsum(
        "th,dh->td", d_query_pre, query_weight_matrix, preferred_element_type=jnp.float32
    )
    d_normed_one = d_normed_one + jnp.einsum(
        "th,dh->td", d_key_pre, key_weight_matrix, preferred_element_type=jnp.float32
    )
    d_normed_one = d_normed_one + jnp.einsum(
        "th,dh->td", d_values, value_weight_matrix, preferred_element_type=jnp.float32
    )
    d_normed_one = lax.psum(d_normed_one, "tp")
    d_input_norm, grad_gain_one = norm_backward(
        layer_input, norm_one, first_norm_scale, d_normed_one
    )
    grad_tokens = d_resid + d_input_norm
    summed = (
        lax.psum_scatter(grad_gain_one, "ep", scatter_dimension=0, tiled=True),
        lax.psum_scatter(grad_queryw, "ep", scatter_dimension=0, tiled=True),
        lax.psum_scatter(grad_keyw, "ep", scatter_dimension=0, tiled=True),
        lax.psum_scatter(grad_valuew, "ep", scatter_dimension=0, tiled=True),
        lax.psum_scatter(grad_outw, "ep", scatter_dimension=0, tiled=True),
        lax.psum_scatter(grad_gain_two, "ep", scatter_dimension=0, tiled=True),
        lax.psum_scatter(grad_router, "ep", scatter_dimension=0, tiled=True),
        lax.psum_scatter(grad_mix, "ep", scatter_dimension=0, tiled=True),
        lax.psum_scatter(grad_sgate, "ep", scatter_dimension=0, tiled=True),
        lax.psum_scatter(grad_sup, "ep", scatter_dimension=0, tiled=True),
        lax.psum_scatter(grad_sdown, "ep", scatter_dimension=0, tiled=True),
    )
    return (
        block_out,
        grad_tokens,
        summed[0],
        summed[1],
        summed[2],
        summed[3],
        summed[4],
        summed[5],
        summed[6],
        summed[7],
        summed[8],
        summed[9],
        summed[10],
        grad_egate,
        expert_up_gradient,
        grad_edown,
    )


class Place:
    def __init__(self):
        self.ep, self.tp = lax.axis_index("ep"), lax.axis_index("tp")
        self.z, self.y = self.ep // 2, self.ep % 2
        self.x, self.c = self.tp // 2, self.tp % 2
        self.depth = lax.axis_size("ep") // 2
        self.next_core = (self.ep, self.x * 2 + 1 - self.c)
        self.next_x = (self.ep, (1 - self.x) * 2 + self.c)
        self.next_y = (self.z * 2 + 1 - self.y, self.tp)

    def at_z(self, z):
        return (z * 2 + self.y, self.tp)

    def ahead(self, steps):
        return lax.rem(self.z + steps, self.depth)

    def behind(self, steps):
        return lax.rem(self.z + self.depth - steps, self.depth)

    def greet(self):
        barrier = pltpu.get_barrier_semaphore()
        peers = [self.next_core, self.next_x, self.next_y]
        peers += [self.at_z(self.ahead(k)) for k in range(1, self.depth)]
        for peer in peers:
            pl.semaphore_signal(barrier, inc=1, device_id=peer, device_id_type=MESH)
        pl.semaphore_wait(barrier, len(peers))

    def greet_row(self):
        barrier = pltpu.get_barrier_semaphore()
        count = 2 * self.depth
        peers = [(lax.rem(self.ep + k, count), self.tp) for k in range(1, count)]
        peers += [self.next_core, self.next_x]
        for peer in peers:
            pl.semaphore_signal(barrier, inc=1, device_id=peer, device_id_type=MESH)
        pl.semaphore_wait(barrier, len(peers))

    def greet_ep(self):
        barrier = pltpu.get_barrier_semaphore()
        count = 2 * self.depth
        for k in range(1, count):
            peer = (lax.rem(self.ep + k, count), self.tp)
            pl.semaphore_signal(barrier, inc=1, device_id=peer, device_id_type=MESH)
        pl.semaphore_wait(barrier, count - 1)


def remote(src, dst, send, recv, peer):
    return pltpu.make_async_remote_copy(
        src_ref=src, dst_ref=dst, send_sem=send, recv_sem=recv, device_id=peer, device_id_type=MESH
    )


def ffn_kernel(
    units,
    expert_count,
    rows_in,
    upstream_in,
    gate_in,
    up_in,
    down_in,
    pieces_in,
    weights_in,
    resid_in,
    gain_in,
    rows_all,
    weighted_out,
    d_pair_out,
    block_out,
    d_resid_low_out,
    d_resid_out,
    d_gain_out,
    d_side_out,
    d_rows_sum,
    out_sum,
    pair_w,
    down_w,
    side_w,
    rows_tile,
    upstream_tile,
    pair_pre,
    d_hidden,
    factors,
    dots,
    weighted_tile,
    d_pair_tile,
    d_resid_low,
    d_rows_tile,
    out_tile,
    d_rows_core,
    out_core,
    d_rows_held,
    out_held,
    d_rows_hop,
    out_hop,
    d_rows_hop2,
    out_hop2,
    d_rows_z,
    out_z,
    d_rows_to_z,
    out_to_z,
    gathered_send,
    gathered_recv,
    hop_send,
    hop_recv,
    weight_sem,
    end_sem,
    own_sem,
    z_send,
    z_recv,
    plane_send,
    plane_recv,
    load_sem,
    store_sem,
    sum_send,
    sum_recv,
    end_send,
    end_recv,
    core_credit,
    hop_credit,
    hop2_credit,
):
    at = Place()
    depth = at.depth
    quarter, width = rows_in.shape
    half = quarter // 2
    f32, bf16 = jnp.float32, jnp.bfloat16

    def weight_copies():
        hidden = down_w.shape[0]
        slot_here, slot_hidden, shared = units
        routed = slot_here * slot_hidden
        columns = pieces_in.shape[2]
        pairs = [(weights_in.at[:, pl.ds(weights_in.shape[1] - 128, 128)], side_w)]
        kinds = ((gate_in, pair_w, 0), (up_in, pair_w, hidden), (down_in, down_w, 0))
        for kind, (experts, into, first) in enumerate(kinds):
            pairs.append((experts, into.at[pl.ds(first, routed)]))
            here = pl.ds(first + routed, shared)
            for e in range(2 * depth):
                src = pieces_in.at[e, pl.ds(kind * shared, shared)]
                pairs.append((src, into.at[here, pl.ds(e * columns, columns)]))
        return [
            pltpu.make_async_copy(src, dst, weight_sem.at[i]) for i, (src, dst) in enumerate(pairs)
        ]

    def clear_rest():
        hidden = down_w.shape[0]
        used = units[0] * units[1] + units[2]
        for into, first in ((pair_w, 0), (pair_w, hidden), (down_w, 0)):
            if used < hidden:
                into[first + used : first + hidden] = jnp.zeros((hidden - used, width), bf16)

    for copy in weight_copies():
        copy.start()
    clear_rest()

    def block(j, y, x):
        return rows_all.at[at.behind(j), y, x, at.c]

    def plane_copy(j, kind):
        y, other_y = at.y, 1 - at.y
        own, other_x = at.x, 1 - at.x
        if kind == 0:
            src, peer = block(j, y, own), at.next_x
        elif kind == 1:
            src, peer = block(j, y, own), at.next_y
        elif kind == 2:
            src, peer = block(j, y, other_x).at[pl.ds(0, half)], at.next_y
        elif kind == 3:
            src, peer = block(j, other_y, own).at[pl.ds(half, half)], at.next_x
        else:
            src = block(j, other_y if kind >= 6 else y, other_x if kind % 2 else own)
            peer = at.next_core
        return remote(src, src, plane_send.at[j, kind], plane_recv.at[j, kind], peer)

    def z_copy(k):
        return remote(
            rows_in, block(0, at.y, at.x), z_send.at[k - 1], z_recv.at[k - 1], at.at_z(at.ahead(k))
        )

    def z_arrival(k):
        dst = block(k, at.y, at.x)
        return remote(dst, dst, z_send.at[k - 1], z_recv.at[k - 1], at.at_z(at.behind(k)))

    def begin(j):
        for kind in (0, 1, 4):
            plane_copy(j, kind).start()

    def spread(j):
        plane_copy(j, 0).wait_recv()
        plane_copy(j, 2).start()
        plane_copy(j, 5).start()
        plane_copy(j, 1).wait_recv()
        plane_copy(j, 3).start()
        plane_copy(j, 6).start()

    def begin_later(j):
        z_arrival(j).wait_recv()
        begin(j)

    def last_hop(j):
        plane_copy(j, 2).wait_recv()
        plane_copy(j, 3).wait_recv()
        plane_copy(j, 7).start()

    def near_ready(j):
        plane_copy(j, 4).wait_recv()
        plane_copy(j, 5).wait_recv()

    def far_ready(j):
        plane_copy(j, 6).wait_recv()
        plane_copy(j, 7).wait_recv()

    def parity(step):
        return lax.rem(step, 2)

    def slot_of(turn):
        return lax.rem(turn + 1, depth)

    def other_y(step):
        return lax.rem(parity(step) + (step // 2 + 1) // depth, 2)

    def tile_at(step):
        return at.behind(slot_of(step // 2)), lax.rem(at.y + other_y(step), 2)

    def load_rows(step):
        z, y = tile_at(step)
        return pltpu.make_async_copy(rows_all.at[z, y], rows_tile, load_sem.at[0])

    def load_upstream(step):
        z, y = tile_at(step)
        return pltpu.make_async_copy(upstream_in.at[z, y], upstream_tile, load_sem.at[1])

    def stores(step):
        z, y = tile_at(step)
        pairs = ((weighted_tile, weighted_out), (d_pair_tile, d_pair_out))
        return [
            pltpu.make_async_copy(src, dst.at[z, y], store_sem.at[i])
            for i, (src, dst) in enumerate(pairs)
        ]

    tiles, cores = (d_rows_tile, out_tile), (d_rows_core, out_core)
    helds, sums = (d_rows_held, out_held), (d_rows_sum, out_sum)
    hops, hops2, zs = (d_rows_hop, out_hop), (d_rows_hop2, out_hop2), (d_rows_z, out_z)
    to_zs = (d_rows_to_z, out_to_z)

    def sum_copy(a, kind, src, dst, peer):
        return remote(src, dst, sum_send.at[a, kind], sum_recv.at[a, kind], peer)

    def core_sum(a):
        return sum_copy(a, 0, tiles[a].at[:, 1 - at.c], cores[a], at.next_core)

    def row_hop(turn, other):
        y = lax.rem(at.y + other, 2)
        slot = parity(turn)
        src = d_rows_held.at[slot, y, 1 - at.x]
        return remote(
            src, d_rows_hop.at[slot, y], hop_send.at[slot, other], hop_recv.at[slot, other], at.next_x
        )

    def out_hop_sum(turn):
        slot = parity(turn)
        src = out_held.at[slot, 1 - at.y]
        return remote(
            src, out_hop.at[slot], hop_send.at[slot, 2], hop_recv.at[slot, 2], at.next_y
        )

    def hop2_sum(a, turn):
        slot = parity(turn)
        if a == 0:
            src, peer = helds[0].at[slot, 1 - at.y, at.x], at.next_y
        else:
            src, peer = helds[1].at[slot, at.y, 1 - at.x], at.next_x
        return sum_copy(a, 2, src, hops2[a], peer)

    def z_sum(a, turn):
        return remote(
            to_zs[a].at[parity(turn)],
            zs[a].at[turn],
            end_send.at[a, turn],
            end_recv.at[a, turn],
            at.at_z(at.behind(turn + 1)),
        )

    def allow(semaphore, peer):
        pl.semaphore_signal(semaphore, inc=1, device_id=peer, device_id_type=MESH)

    piece = 32

    def add(into, first, second):
        def body(i, carry):
            part = pl.ds(pl.multiple_of(i * piece, piece), piece)
            into[part] = first[part] + second[part]
            return carry

        lax.fori_loop(0, quarter // piece, body, 0)

    def after_core(step):
        turn = step // 2
        other = other_y(step)
        held, y = parity(turn), lax.rem(at.y + other, 2)

        @pl.when((parity(step) == 0) & (turn >= 2))
        def _():
            for a in (0, 1):
                pl.semaphore_wait(hop_credit.at[a], 1)

        for a in (0, 1):
            core_sum(a).wait()
            for x in (1 - at.x, at.x):
                add(helds[a].at[held, y, x], tiles[a].at[x, at.c], cores[a].at[x])
            if a == 0:
                row_hop(turn, other).start()
            else:

                @pl.when(other == 1)
                def _():
                    out_hop_sum(turn).start()

        @pl.when(step + 1 < 2 * depth)
        def _():
            allow(core_credit, at.next_core)

    def after_row_hop(turn, other):
        slot, y = parity(turn), lax.rem(at.y + other, 2)
        row_hop(turn, other).wait()
        into = d_rows_held.at[slot, y, at.x]
        add(into, into, d_rows_hop.at[slot, y])

    def after_out_hop(turn):
        slot = parity(turn)
        out_hop_sum(turn).wait()
        for x in (1 - at.x, at.x):
            into = out_held.at[slot, at.y, x]
            add(into, into, out_hop.at[slot, x])

    def may_hop2(turn, a):
        @pl.when(turn >= 1)
        def _():
            pl.semaphore_wait(hop2_credit.at[a], 1)

    def after_hop(turn):
        after_row_hop(turn, 1)
        may_hop2(turn, 0)
        hop2_sum(0, turn).start()
        after_row_hop(turn, 0)
        after_out_hop(turn)
        may_hop2(turn, 1)
        hop2_sum(1, turn).start()

        @pl.when(turn + 2 < depth)
        def _():
            allow(hop_credit.at[0], at.next_x)
            allow(hop_credit.at[1], at.next_y)

    def after_hop2(turn):
        slot = parity(turn)
        for a in (0, 1):
            hop2_sum(a, turn).wait()

            @pl.when(turn >= 2)
            def _():
                z_sum(a, turn - 2).wait_send()

            add(to_zs[a].at[slot], helds[a].at[slot, at.y, at.x], hops2[a])
            z_sum(a, turn).start()
        allow(hop2_credit.at[0], at.next_y)
        allow(hop2_credit.at[1], at.next_x)

    load_upstream(0).start()
    at.greet()
    z_copy(1).start()
    own_copy = pltpu.make_async_copy(rows_in, block(0, at.y, at.x), own_sem)
    own_copy.start()
    own_copy.wait()
    begin(0)
    begin_later(1)
    for k in range(2, depth):
        z_copy(k).start()
    spread(0)
    spread(1)
    near_ready(1)
    load_rows(0).start()
    for copy in weight_copies():
        copy.wait()

    tile_rows = 4 * quarter
    hidden_total = down_w.shape[0]
    lane = lax.broadcasted_iota(jnp.int32, (tile_rows, 128), 1)
    slot_here, slot_hidden, shared_hidden = units
    routed = slot_here * slot_hidden
    across = (((1,), (1,)), ((), ()))
    few = 16

    def gate_factors(rows, picked):
        logits = jnp.dot(rows, side_w[...], preferred_element_type=f32)
        chooses = (lane >= 3) & (lane < 3 + expert_count)
        peak = jnp.max(jnp.where(chooses, logits, -1e30), axis=1, keepdims=True)
        expo = jnp.where(chooses, jnp.exp(jnp.where(chooses, logits, peak) - peak), 0.0)
        routed_gate = expo / jnp.sum(expo, axis=1, keepdims=True) * picked.astype(f32)
        mix_pre = jnp.sum(jnp.where(lane == 2, logits, 0.0), axis=1, keepdims=True)
        result = jnp.where(lane == slot_here, 1.0 / (1.0 + jnp.exp(-mix_pre)), 0.0)
        for s in range(slot_here):
            chosen = lane == 3 + at.ep * slot_here + s
            gate = jnp.sum(jnp.where(chosen, routed_gate, 0.0), axis=1, keepdims=True)
            result = jnp.where(lane == s, gate, result)
        return result

    few_lane = lax.broadcasted_iota(jnp.int32, (few, 128), 1)
    bounds = [s * slot_hidden for s in range(slot_here)] + [routed, hidden_total]

    def owners(group):
        found = []
        for s in range(slot_here + 1):
            low, high = max(bounds[s] - group * 128, 0), min(bounds[s + 1] - group * 128, 128)
            if low < high:
                found.append((s, low, high))
        return found

    def hidden_rows(i, carry):
        here = pl.ds(pl.multiple_of(i * few, few), few)
        gates = [
            jnp.broadcast_to(factors[here, s : s + 1], (few, 128)) for s in range(slot_here + 1)
        ]
        parts = [None] * (slot_here + 1)
        for group in range(hidden_total // 128):
            units_here = slice(group * 128, (group + 1) * 128)
            units_up = slice(hidden_total + group * 128, hidden_total + (group + 1) * 128)
            gate_pre, up_pre = pair_pre[here, units_here], pair_pre[here, units_up]
            d_h = d_hidden[here, units_here]
            found = owners(group)
            factor = gates[found[0][0]]
            for s, low, _ in found[1:]:
                factor = jnp.where(few_lane >= low, gates[s], factor)
            sig = 0.5 + 0.5 * jnp.tanh(0.5 * gate_pre)
            silu = gate_pre * sig
            hidden = silu * up_pre
            product = hidden * d_h
            gated = factor * d_h
            weighted_tile[here, units_here] = (factor * hidden).astype(bf16)
            slope = sig + silu * (1.0 - sig)
            d_pair_tile[here, units_here] = (gated * up_pre * slope).astype(bf16)
            d_pair_tile[here, units_up] = (gated * silu).astype(bf16)
            for s, low, high in found:
                mine = product
                if high < 128:
                    mine = jnp.where(few_lane < high, mine, 0.0)
                if low > 0:
                    mine = jnp.where(few_lane >= low, mine, 0.0)
                parts[s] = mine if parts[s] is None else parts[s] + mine
        result = jnp.zeros((few, 128), f32)
        for s in range(slot_here + 1):
            dot = jnp.sum(parts[s], axis=1, keepdims=True)
            where = few_lane == (2 if s == slot_here else 3 + at.ep * slot_here + s)
            result = jnp.where(where, dot, result)
        dots[here] = result.astype(bf16)
        return carry

    def first_half(step):
        load_upstream(step).wait()
        upstream = upstream_tile[...].reshape(tile_rows, upstream_tile.shape[-1])
        d_hidden[...] = lax.dot_general(
            upstream[:, :width], down_w[...], across, preferred_element_type=f32
        )
        load_rows(step).wait()
        rows = rows_tile[...].reshape(tile_rows, width)
        factors[...] = gate_factors(rows, upstream[:, width:])
        pair_pre[...] = lax.dot_general(rows, pair_w[...], across, preferred_element_type=f32)

        @pl.when(step + 1 < 2 * depth)
        def _():
            load_upstream(step + 1).start()

        @pl.when(step >= 1)
        def _():
            for copy in stores(step - 1):
                copy.wait()

        lax.fori_loop(0, tile_rows // few, hidden_rows, 0, unroll=2)
        for copy in stores(step):
            copy.start()
        turn = step // 2

        @pl.when(step == 0)
        def _():
            last_hop(0)

        @pl.when((parity(step) == 0) & (turn + 1 < depth))
        def _():
            last_hop(turn + 1)

        @pl.when((step >= 1) & (step + 1 < depth))
        def _():
            spread(step + 1)

        @pl.when(step + 2 < depth)
        def _():
            begin_later(step + 2)

    def second_half(step):
        blocks = (2, 2, quarter)
        some = width // 2
        for n in range(2):
            columns = slice(n * some, (n + 1) * some)
            part = jnp.dot(weighted_tile[...], down_w[:, columns], preferred_element_type=f32)
            out_tile[:, :, :, columns] = part.astype(bf16).reshape(blocks + (some,))
            part = jnp.dot(d_pair_tile[...], pair_w[:, columns], preferred_element_type=f32)
            d_rows_tile[:, :, :, columns] = part.astype(bf16).reshape(blocks + (some,))
        d_rows_tile[:, :, :, width:] = dots[...].reshape(blocks + (128,))

        @pl.when(step >= 1)
        def _():
            pl.semaphore_wait(core_credit, 1)

        for a in (0, 1):
            core_sum(a).start()
        turn = step // 2

        @pl.when((parity(step) == 0) & (turn + 1 < depth))
        def _():
            far_ready(slot_of(turn))

        @pl.when((parity(step) == 1) & (turn + 1 < depth))
        def _():
            near_ready(slot_of(turn + 1))

        @pl.when(step == 2 * depth - 3)
        def _():
            far_ready(slot_of(turn + 1))

        @pl.when(step + 1 < 2 * depth)
        def _():
            load_rows(step + 1).start()

    def step_body(step, carry):
        first_half(step)

        @pl.when(step == 2 * depth - 1)
        def _():
            after_hop(depth - 2)

        @pl.when(step >= 1)
        def _():
            after_core(step - 1)

        second_half(step)
        odd = parity(step) == 1

        @pl.when(odd & (step >= 3) & (step < 2 * depth - 1))
        def _():
            after_hop((step - 3) // 2)

        @pl.when(jnp.logical_not(odd) & (step >= 4))
        def _():
            after_hop2((step - 4) // 2)

        return carry

    lax.fori_loop(0, 2 * depth, step_body, 0)
    last = depth - 1
    own_rows, own_upstream = rows_tile.at[0, 0], upstream_tile.at[0, 0]
    own_loads = [
        pltpu.make_async_copy(rows_in, own_rows, end_sem.at[0]),
        pltpu.make_async_copy(
            upstream_in.at[at.z, at.y, at.x, at.c], own_upstream, end_sem.at[1]
        ),
    ]
    for copy in own_loads:
        copy.start()
    after_hop2(last - 1)
    after_row_hop(last, 1)
    may_hop2(last, 0)
    hop2_sum(0, last).start()
    after_core(2 * depth - 1)
    after_out_hop(last)
    may_hop2(last, 1)
    hop2_sum(1, last).start()
    after_row_hop(last, 0)

    def total_of(a):
        hop2_sum(a, last).wait()
        held = helds[a].at[last % 2, at.y, at.x]
        for turn in range(last):
            z_sum(a, turn).wait_recv()

        def total_body(i, carry):
            part = pl.ds(pl.multiple_of(i * piece, piece), piece)
            total = held[part].astype(f32) + hops2[a][part].astype(f32)
            for k in range(last):
                total = total + zs[a][k, part].astype(f32)
            sums[a][part] = total
            return carry

        lax.fori_loop(0, quarter // piece, total_body, 0)

    total_of(0)
    own_lane = lax.broadcasted_iota(jnp.int32, (quarter, 128), 1)
    chooses = (own_lane >= 3) & (own_lane < 3 + expert_count)
    for copy in own_loads:
        copy.wait()
    rows = own_rows[...]
    logits = jnp.dot(rows, side_w[...], preferred_element_type=f32)
    peak = jnp.max(jnp.where(chooses, logits, -1e30), axis=1, keepdims=True)
    expo = jnp.where(chooses, jnp.exp(jnp.where(chooses, logits, peak) - peak), 0.0)
    router = expo / jnp.sum(expo, axis=1, keepdims=True)
    mixer = 1.0 / (1.0 + jnp.exp(-jnp.where(own_lane == 2, logits, 0.0)))
    gate_dots = d_rows_sum[:, width:]
    d_router = jnp.where(chooses, gate_dots * own_upstream[:, width:].astype(f32), 0.0)
    d_logits = router * (d_router - jnp.sum(router * d_router, axis=1, keepdims=True))
    d_mix = gate_dots * mixer * (1.0 - mixer)
    d_side = jnp.where(own_lane == 2, d_mix, jnp.where(chooses, d_logits, 0.0))
    d_side_out[...] = d_side
    high = d_side.astype(bf16)
    lower = (d_side - high.astype(f32)).astype(bf16)
    for split in (high, lower):
        d_rows_sum[:, :width] += lax.dot_general(
            split, side_w[...], across, preferred_element_type=f32
        )

    def end_body(i, carry):
        part = pl.ds(pl.multiple_of(i * few, few), few)
        resid = resid_in[part]
        scale = lax.rsqrt(jnp.mean(resid * resid, axis=1, keepdims=True) + epsilon)
        unit_rows = resid * scale
        grads = d_rows_sum[part, :width]
        scaled = grads * gain_in[...]
        inner = jnp.mean(scaled * unit_rows, axis=1, keepdims=True)
        d_resid = own_upstream[part, :width].astype(f32) + scale * (scaled - unit_rows * inner)
        d_resid_out[part] = d_resid
        d_resid_low[part] = d_resid.astype(bf16)
        return carry + jnp.sum(grads * unit_rows, axis=0, keepdims=True)

    d_gain_out[...] = lax.fori_loop(0, quarter // few, end_body, jnp.zeros((1, width), f32))

    def gather_copy(kind):
        if kind == 2:
            src = dst = d_resid_low_out.at[1 - at.x, at.c]
        else:
            src, dst = d_resid_low, d_resid_low_out.at[at.x, at.c]
        peer = at.next_x if kind == 0 else at.next_core
        return remote(src, dst, gathered_send.at[kind], gathered_recv.at[kind], peer)

    own_end = pltpu.make_async_copy(d_resid_low, d_resid_low_out.at[at.x, at.c], own_sem)
    own_end.start()
    for kind in (0, 1):
        gather_copy(kind).start()
    total_of(1)
    block_out[...] = (resid_in[...] + out_sum[...]).astype(bf16)
    gather_copy(0).wait_recv()
    gather_copy(2).start()
    own_end.wait()
    gather_copy(0).wait_send()
    gather_copy(1).wait()
    gather_copy(2).wait()
    for copy in stores(2 * depth - 1):
        copy.wait()
    for a in (0, 1):
        for turn in range(max(0, depth - 3), depth - 1):
            z_sum(a, turn).wait_send()
    for k in range(1, depth):
        z_copy(k).wait_send()

    def finish(j, carry):
        for kind in range(8):
            plane_copy(j, kind).wait_send()
        return carry

    lax.fori_loop(0, depth, finish, 0)


def ffn_over_all(rows, upstream_all, experts, pieces, weights, resid, gain, units, expert_count):
    quarter, width = rows.shape
    ep_count, tp_count = lax.axis_size("ep"), lax.axis_size("tp")
    depth = ep_count // 2
    hidden = -(-(units[0] * units[1] + units[2]) // 128) * 128
    bf16, f32 = jnp.bfloat16, jnp.float32
    wide = width + 128
    tile_rows = tp_count * quarter
    tokens = ep_count * tile_rows
    anywhere = pl.BlockSpec(memory_space=pl.ANY)
    in_vmem = pl.BlockSpec(memory_space=pltpu.VMEM)

    def both(*lead):
        return [pltpu.VMEM(lead + (quarter, columns), bf16) for columns in (wide, width)]

    dma = pltpu.SemaphoreType.DMA
    outs = pl.pallas_call(
        functools.partial(ffn_kernel, units, expert_count),
        out_shape=(
            jax.ShapeDtypeStruct((depth, 2, 2, 2, quarter, width), bf16),
            jax.ShapeDtypeStruct((depth, 2, tile_rows, hidden), bf16),
            jax.ShapeDtypeStruct((depth, 2, tile_rows, 2 * hidden), bf16),
            jax.ShapeDtypeStruct((quarter, width), bf16),
            jax.ShapeDtypeStruct((2, 2, quarter, width), bf16),
            jax.ShapeDtypeStruct((quarter, width), f32),
            jax.ShapeDtypeStruct((1, width), f32),
            jax.ShapeDtypeStruct((quarter, 128), f32),
        ),
        in_specs=[anywhere] * 7 + [in_vmem] * 2,
        out_specs=(anywhere,) * 3 + (in_vmem, anywhere) + (in_vmem,) * 3,
        scratch_shapes=[
            pltpu.VMEM((quarter, wide), f32),
            pltpu.VMEM((quarter, width), f32),
            pltpu.VMEM((2 * hidden, width), bf16),
            pltpu.VMEM((hidden, width), bf16),
            pltpu.VMEM((width, 128), bf16),
            pltpu.VMEM((2, 2, quarter, width), bf16),
            pltpu.VMEM((2, 2, quarter, wide), bf16),
            pltpu.VMEM((tile_rows, 2 * hidden), f32),
            pltpu.VMEM((tile_rows, hidden), f32),
            pltpu.VMEM((tile_rows, 128), f32),
            pltpu.VMEM((tile_rows, 128), bf16),
            pltpu.VMEM((tile_rows, hidden), bf16),
            pltpu.VMEM((tile_rows, 2 * hidden), bf16),
            pltpu.VMEM((quarter, width), bf16),
        ]
        + both(2, 2)
        + both(2)
        + both(2, 2, 2)
        + both(2, 2)
        + both()
        + both(depth - 1)
        + both(2)
        + [
            dma((3,)),
            dma((3,)),
            dma((2, 3)),
            dma((2, 3)),
            dma((4 + 6 * depth,)),
            dma((2,)),
            dma,
            dma((depth - 1,)),
            dma((depth - 1,)),
            dma((depth, 8)),
            dma((depth, 8)),
            dma((2,)),
            dma((2,)),
            dma((2, 3)),
            dma((2, 3)),
            dma((2, depth - 1)),
            dma((2, depth - 1)),
            pltpu.SemaphoreType.REGULAR,
            pltpu.SemaphoreType.REGULAR((2,)),
            pltpu.SemaphoreType.REGULAR((2,)),
        ],
        compiler_params=pltpu.CompilerParams(
            collective_id=1, has_side_effects=True, vmem_limit_bytes=62 * 2**20
        ),
        cost_estimate=pl.CostEstimate(
            flops=12 * tokens * width * hidden,
            bytes_accessed=10 * tokens * width,
            transcendentals=tokens * hidden,
        ),
        name="ffn_all_tokens",
    )(
        rows,
        upstream_all.reshape(depth, 2, 2, 2, quarter, wide),
        *[array.reshape(-1, width) for array in experts],
        pieces,
        weights,
        resid,
        gain,
    )
    rows_all, weighted, d_pair, block_out, d_resid_low, d_resid, d_gain, d_side = outs
    return (
        rows_all.reshape(tokens, width),
        weighted.reshape(tokens, hidden),
        d_pair.reshape(tokens, 2 * hidden),
        block_out,
        d_resid_low.reshape(tile_rows, width),
        d_resid,
        d_gain[0],
        d_side,
    )


def swap_copies(at, pieces_in, pieces_out, send_sem, recv_sem, leave):
    count = 2 * at.depth
    copies = []
    for k in range(1, count):
        to, back = lax.rem(at.ep + k, count), lax.rem(at.ep + count - k, count)
        if leave:
            src, dst, peer = pieces_in.at[to], pieces_out.at[at.ep], to
        else:
            src, dst, peer = pieces_in.at[back], pieces_out.at[back], back
        copies.append(remote(src, dst, send_sem.at[k], recv_sem.at[k], (peer, at.tp)))
    return copies


def weights_kernel(
    q_in,
    k_in,
    v_in,
    o_in,
    side_in,
    pieces_in,
    all_out,
    pieces_out,
    own_sem,
    z_send,
    z_recv,
    y_send,
    y_recv,
    swap_send,
    swap_recv,
):
    at = Place()
    depth = at.depth
    half = q_in.shape[0] // 2
    last = depth - 1

    def block(k, y, h):
        return all_out.at[at.z + k, y, pl.ds(h * half, half)]

    def z_copy(k, h, direction):
        src = block(k, at.y, h)
        slot = last + k - direction
        return remote(
            src,
            block(k, at.y, h),
            z_send.at[last + k, h, (direction + 1) // 2],
            z_recv.at[slot, h],
            at.at_z(at.z + direction),
        )

    def z_arrival(k, h):
        direction = 1 if k > 0 else -1
        dst = block(k, at.y, h)
        return remote(
            dst, dst, z_send.at[last + k, h, 0], z_recv.at[last + k, h], at.at_z(at.z + direction)
        )

    def y_copy(k, h):
        src = block(k, at.y, h)
        return remote(
            src, src, y_send.at[last + k, h], y_recv.at[last + k, h], at.next_y
        )

    own_copies, first = [], 0
    for i, array in enumerate((q_in, k_in, v_in, o_in, side_in)):
        here = all_out.at[at.z, at.y, :, pl.ds(first, array.shape[1])]
        own_copies.append(pltpu.make_async_copy(array, here, own_sem.at[i]))
        first += array.shape[1]
    piece_copy = pltpu.make_async_copy(
        pieces_in.at[at.ep], pieces_out.at[at.ep], own_sem.at[len(own_copies)]
    )
    for copy in own_copies + [piece_copy]:
        copy.start()
    has_up, has_down = at.z + 1 < depth, at.z > 0
    at.greet_ep()
    for copy in own_copies:
        copy.wait()

    for h in (0, 1):
        pl.when(has_up)(lambda: z_copy(0, h, 1).start())
        pl.when(has_down)(lambda: z_copy(0, h, -1).start())
        y_copy(0, h).start()
    swap = (at, pieces_in, pieces_out, swap_send, swap_recv)
    for copy in swap_copies(*swap, True):
        copy.start()
    for k in range(1, depth):
        for h in (0, 1):
            for sign in (-1, 1):
                there = at.z + sign * k
                exists = (there >= 0) & (there < depth)
                onward = at.z - sign
                goes_on = exists & (onward >= 0) & (onward < depth)

                @pl.when(exists)
                def _():
                    z_arrival(sign * k, h).wait_recv()

                @pl.when(goes_on)
                def _():
                    z_copy(sign * k, h, -sign).start()

                @pl.when(exists)
                def _():
                    y_copy(sign * k, h).start()

    piece_copy.wait()
    for copy in swap_copies(*swap, False):
        copy.wait_recv()
    for copy in swap_copies(*swap, True):
        copy.wait_send()
    for h in (0, 1):
        pl.when(has_up)(lambda: z_copy(0, h, 1).wait_send())
        pl.when(has_down)(lambda: z_copy(0, h, -1).wait_send())
    for k in range(-last, depth):
        there = at.z + k
        exists = (there >= 0) & (there < depth)
        sign = 1 if k > 0 else -1
        onward = at.z - sign
        goes_on = exists & (onward >= 0) & (onward < depth)
        for h in (0, 1):

            @pl.when(exists)
            def _():
                y_copy(k, h).wait()

            if k != 0:

                @pl.when(goes_on)
                def _():
                    z_copy(k, h, -sign).wait_send()


def gather_over_ep(blocks, pieces):
    rows, columns = blocks[0].shape[0], sum(block.shape[1] for block in blocks)
    depth = lax.axis_size("ep") // 2
    anywhere = pl.BlockSpec(memory_space=pl.ANY)
    slots = 2 * depth - 1
    out, pieces = pl.pallas_call(
        weights_kernel,
        out_shape=(
            jax.ShapeDtypeStruct((depth, 2, rows, columns), pieces.dtype),
            jax.ShapeDtypeStruct(pieces.shape, pieces.dtype),
        ),
        in_specs=[anywhere] * (len(blocks) + 1),
        out_specs=(anywhere,) * 2,
        scratch_shapes=[
            pltpu.SemaphoreType.DMA((len(blocks) + 1,)),
            pltpu.SemaphoreType.DMA((slots, 2, 2)),
            pltpu.SemaphoreType.DMA((slots, 2)),
            pltpu.SemaphoreType.DMA((slots, 2)),
            pltpu.SemaphoreType.DMA((slots, 2)),
            pltpu.SemaphoreType.DMA((2 * depth,)),
            pltpu.SemaphoreType.DMA((2 * depth,)),
        ],
        compiler_params=pltpu.CompilerParams(collective_id=3, has_side_effects=True),
        cost_estimate=pl.CostEstimate(
            flops=0, bytes_accessed=8 * depth * rows * columns, transcendentals=0
        ),
        name="gather_weights",
    )(*blocks, pieces)
    return out.reshape(2 * depth * rows, columns), pieces


class RowGather:
    def __init__(self, at, mine, everywhere, z_send, z_recv, plane_send, plane_recv):
        self.at, self.mine, self.everywhere = at, mine, everywhere
        self.z_sems, self.plane_sems = (z_send, z_recv), (plane_send, plane_recv)
        self.half = mine.shape[0] // 2

    def block(self, j, y, x):
        return self.everywhere.at[self.at.behind(j), y, x, self.at.c]

    def plane_copy(self, j, kind):
        at, half = self.at, self.half
        if kind == 0:
            src, peer = self.block(j, at.y, at.x), at.next_x
        elif kind == 1:
            src, peer = self.block(j, at.y, at.x), at.next_y
        elif kind == 2:
            src, peer = self.block(j, at.y, 1 - at.x).at[pl.ds(0, half)], at.next_y
        elif kind == 3:
            src, peer = self.block(j, 1 - at.y, at.x).at[pl.ds(half, half)], at.next_x
        else:
            y, x = 1 - at.y if kind >= 6 else at.y, 1 - at.x if kind % 2 else at.x
            src, peer = self.block(j, y, x), at.next_core
        send, recv = self.plane_sems
        return remote(src, src, send.at[j, kind], recv.at[j, kind], peer)

    def z_copy(self, k):
        send, recv = self.z_sems
        dst = self.block(0, self.at.y, self.at.x)
        peer = self.at.at_z(self.at.ahead(k))
        return remote(self.mine, dst, send.at[k - 1], recv.at[k - 1], peer)

    def z_onward(self, j):
        send, recv = self.z_sems
        src = self.block(j, self.at.y, self.at.x)
        peer = self.at.at_z(self.at.z + 1)
        return remote(src, src, send.at[self.at.depth - 1 + j], recv.at[j], peer)

    def sends(self, k):
        down = self.at.z + k >= self.at.depth
        return down | (self.at.z + 1 < self.at.depth) if k == 1 else down

    def goes_on(self, j):
        return (self.at.z >= j) & (self.at.z + 1 < self.at.depth)

    def z_start(self):
        for k in range(1, self.at.depth):

            @pl.when(self.sends(k))
            def _():
                self.z_copy(k).start()

    def begin(self, j):
        if j > 0:
            send, recv = self.z_sems
            dst = self.block(j, self.at.y, self.at.x)
            peer = self.at.at_z(self.at.behind(j))
            remote(dst, dst, send.at[j - 1], recv.at[j - 1], peer).wait_recv()
            if j + 1 < self.at.depth:

                @pl.when(self.goes_on(j))
                def _():
                    self.z_onward(j).start()

        for kind in (0, 1, 4):
            self.plane_copy(j, kind).start()

    def spread(self, j):
        self.plane_copy(j, 0).wait_recv()
        self.plane_copy(j, 2).start()
        self.plane_copy(j, 5).start()
        self.plane_copy(j, 1).wait_recv()
        self.plane_copy(j, 3).start()
        self.plane_copy(j, 6).start()

    def last_hop(self, j):
        self.plane_copy(j, 2).wait_recv()
        self.plane_copy(j, 3).wait_recv()
        self.plane_copy(j, 7).start()

    def finish(self):
        for k in range(1, self.at.depth):

            @pl.when(self.sends(k))
            def _():
                self.z_copy(k).wait_send()

            if k + 1 < self.at.depth:

                @pl.when(self.goes_on(k))
                def _():
                    self.z_onward(k).wait_send()

        for j in range(self.at.depth):
            for kind in range(8):
                if kind >= 4:
                    self.plane_copy(j, kind).wait_recv()
                self.plane_copy(j, kind).wait_send()


def front_kernel(
    score_scale,
    block_in,
    weights_in,
    upstream_in,
    cos_in,
    sin_in,
    query_start,
    query_at,
    tokens_in,
    first_gain,
    gain_in,
    upstream_all,
    turned_out,
    k_out,
    v_out,
    q_out,
    lse_out,
    attended_out,
    resid_out,
    rows_out,
    normed,
    turned,
    qkv_w,
    out_w,
    k_all,
    v_all,
    scores_of,
    part,
    core_got,
    x_got,
    load_sem,
    z_send,
    z_recv,
    plane_send,
    plane_recv,
    kv_send,
    kv_recv,
    tp_send,
    tp_recv,
):
    at = Place()
    depth = at.depth
    count = 2 * depth
    heads, tokens, head = q_out.shape
    heads_width = heads * head
    windows = k_all.shape[1] // tokens
    quarter, width = resid_out.shape
    f32, bf16 = jnp.float32, jnp.bfloat16
    across = (((1,), (1,)), ((), ()))
    gather = RowGather(at, upstream_in, upstream_all, z_send, z_recv, plane_send, plane_recv)
    own = (windows - 1) * tokens

    def kv_copy(kind, w):
        held = (k_all, v_all)[kind]
        return remote(
            held.at[:, pl.ds(own, tokens)],
            held.at[:, pl.ds(w * tokens, tokens)],
            kv_send.at[kind, w],
            kv_recv.at[kind, w],
            (at.ep + (windows - 1 - w), at.tp),
        )

    def kv_arrival(kind, w):
        dst = (k_all, v_all)[kind].at[:, pl.ds(w * tokens, tokens)]
        peer = (at.ep - (windows - 1 - w), at.tp)
        return remote(dst, dst, kv_send.at[kind, w], kv_recv.at[kind, w], peer)

    def core_copy():
        return remote(part.at[:, 1 - at.c], core_got, tp_send.at[0], tp_recv.at[0], at.next_core)

    def x_copy():
        return remote(part.at[1 - at.x, at.c], x_got, tp_send.at[1], tp_recv.at[1], at.next_x)

    pairs = (
        (block_in, normed),
        (weights_in.at[:, pl.ds(0, 3 * heads_width)], qkv_w),
        (weights_in.at[:, pl.ds(3 * heads_width, heads_width)], out_w),
    )
    loads = [pltpu.make_async_copy(src, dst, load_sem.at[i]) for i, (src, dst) in enumerate(pairs)]
    for copy in loads:
        copy.start()
    at.greet_row()
    own_copy = pltpu.make_async_copy(
        upstream_in, gather.block(0, at.y, at.x), load_sem.at[len(pairs)]
    )
    own_copy.start()
    gather.z_start()
    own_copy.wait()
    gather.begin(0)
    loads[0].wait()
    few = 16

    def norm_body(i, carry):
        here = pl.ds(pl.multiple_of(i * few, few), few)
        inputs = normed[here].astype(f32)
        scale = lax.rsqrt(jnp.mean(inputs * inputs, axis=1, keepdims=True) + epsilon)
        normed[here] = (inputs * scale * first_gain[...]).astype(bf16)
        return carry

    lax.fori_loop(0, tokens // few, norm_body, 0, unroll=2)
    loads[1].wait()
    lane = lax.broadcasted_iota(jnp.int32, (tokens, head), 1)
    sign = jnp.where(lane < head // 2, -1.0, 1.0)

    def rotated(array):
        return array * cos_in[...] + pltpu.roll(array, head // 2, 1) * sign * sin_in[...]

    keys = jnp.dot(
        normed[...], qkv_w[:, heads_width : 2 * heads_width], preferred_element_type=f32
    )
    for h in range(heads):
        k_all[h, own:] = rotated(keys[:, h * head : (h + 1) * head]).astype(bf16)
    values = jnp.dot(normed[...], qkv_w[:, 2 * heads_width :], preferred_element_type=f32)
    for h in range(heads):
        v_all[h, own:] = values[:, h * head : (h + 1) * head].astype(bf16)
    for w in reversed(range(windows - 1)):

        @pl.when(at.ep + (windows - 1 - w) < count)
        def _():
            for kind in (0, 1):
                kv_copy(kind, w).start()

    gather.spread(0)
    queries = jnp.dot(normed[...], qkv_w[:, :heads_width], preferred_element_type=f32)
    for h in range(heads):
        q_out[h] = rotated(queries[:, h * head : (h + 1) * head]).astype(bf16)
    gather.last_hop(0)
    gather.begin(1)
    turned[...] = normed[...].T
    turned_copy = pltpu.make_async_copy(turned, turned_out, load_sem.at[0])
    turned_copy.start()
    gather.spread(1)
    for w in range(windows - 1):

        @pl.when(at.ep < windows - 1 - w)
        def _():
            for held in (k_all, v_all):
                held[:, w * tokens : (w + 1) * tokens] = jnp.zeros((heads, tokens, head), bf16)

        @pl.when(at.ep >= windows - 1 - w)
        def _():
            for kind in (0, 1):
                kv_arrival(kind, w).wait_recv()

    outs = [
        pltpu.make_async_copy(src, dst, load_sem.at[i])
        for i, (src, dst) in ((1, (k_all, k_out)), (3, (v_all, v_out)))
    ]
    for copy in outs:
        copy.start()
    due = [functools.partial(gather.last_hop, 1)]
    for j in range(2, depth):
        due.append(functools.partial(gather.begin, j))
        due.append(functools.partial(gather.spread, j))
        due.append(functools.partial(gather.last_hop, j))

    def head_body(h, carry):
        q = q_out[h]
        peak = jnp.full((1, tokens), -1e30, f32)
        for w in range(windows):
            some = slice(w * tokens, (w + 1) * tokens)
            scores = lax.dot_general(k_all[h, some], q, across, preferred_element_type=f32)
            key_at = lax.broadcasted_iota(jnp.int32, scores.shape, 0)
            key_at = key_at + (at.ep + w + 1 - windows) * tokens
            allowed = (key_at >= query_start[...]) & (key_at <= query_at[...])
            scores = jnp.where(allowed, scores * score_scale, -1e30)
            scores_of[w] = scores
            peak = jnp.maximum(peak, jnp.max(scores, axis=0, keepdims=True))
        total = jnp.zeros((1, tokens), f32)
        for w in range(windows):
            expo = jnp.exp(scores_of[w] - peak)
            scores_of[w] = expo
            total = total + jnp.sum(expo, axis=0, keepdims=True)
        lse_out[h] = peak + jnp.log(total)
        each = 1.0 / total
        attended = jnp.zeros((head, tokens), f32)
        for w in range(windows):
            some = slice(w * tokens, (w + 1) * tokens)
            probs = (scores_of[w] * each).astype(bf16)
            attended = attended + jnp.dot(
                v_all[h, some].T, probs, preferred_element_type=f32
            )
        here = pl.ds(pl.multiple_of(h * head, head), head)
        attended_out[:, here] = attended.T.astype(bf16)
        for i in range(heads):

            @pl.when(h == i)
            def _():
                for action in due[i : i + 1]:
                    action()

        return carry

    lax.fori_loop(0, heads, head_body, 0)
    loads[2].wait()
    strips = 4
    strip = width // strips
    for n in range(strips):
        some = slice(n * strip, (n + 1) * strip)
        product = lax.dot_general(
            attended_out[...], out_w[some], across, preferred_element_type=f32
        )
        part[:, :, :, some] = product.astype(bf16).reshape(2, 2, quarter, strip)
    core_copy().start()
    rest = due[heads:]
    for action in rest[:2]:
        action()
    core_copy().wait()
    for x in (0, 1):
        part[x, at.c] = part[x, at.c] + core_got[x]
    x_copy().start()
    for action in rest[2:]:
        action()
    x_copy().wait()

    def end_body(i, carry):
        here = pl.ds(pl.multiple_of(i * few, few), few)
        total = part[at.x, at.c, here].astype(f32) + x_got[here].astype(f32)
        resid = tokens_in[here].astype(f32) + total
        scale = lax.rsqrt(jnp.mean(resid * resid, axis=1, keepdims=True) + epsilon)
        resid_out[here] = resid
        rows_out[here] = (resid * scale * gain_in[...]).astype(bf16)
        return carry

    lax.fori_loop(0, quarter // few, end_body, 0)
    turned_copy.wait()
    for copy in outs:
        copy.wait()
    for w in range(windows - 1):

        @pl.when(at.ep + (windows - 1 - w) < count)
        def _():
            for kind in (0, 1):
                kv_copy(kind, w).wait_send()

    gather.finish()


def attention_front(block, weights, upstream, in_place, heads, scale):
    tokens, width = block.shape
    quarter, wide = upstream.shape
    depth = lax.axis_size("ep") // 2
    head, windows = HD, 3
    f32, bf16 = jnp.float32, jnp.bfloat16
    anywhere = pl.BlockSpec(memory_space=pl.ANY)
    in_vmem = pl.BlockSpec(memory_space=pltpu.VMEM)
    dma = pltpu.SemaphoreType.DMA
    shape = jax.ShapeDtypeStruct
    window = (heads, windows * tokens, head)
    outs = pl.pallas_call(
        functools.partial(front_kernel, scale),
        out_shape=(
            shape((depth, 2, 2, 2, quarter, wide), bf16),
            shape((width, tokens), bf16),
            shape(window, bf16),
            shape(window, bf16),
            shape((heads, tokens, head), bf16),
            shape((heads, 1, tokens), f32),
            shape((tokens, heads * head), bf16),
            shape((quarter, width), f32),
            shape((quarter, width), bf16),
        ),
        in_specs=[anywhere] * 3 + [in_vmem] * len(in_place),
        out_specs=(anywhere,) * 4 + (in_vmem,) * 5,
        scratch_shapes=[
            pltpu.VMEM((tokens, width), bf16),
            pltpu.VMEM((width, tokens), bf16),
            pltpu.VMEM((width, 3 * heads * head), bf16),
            pltpu.VMEM((width, heads * head), bf16),
            pltpu.VMEM(window, bf16),
            pltpu.VMEM(window, bf16),
            pltpu.VMEM((windows, tokens, tokens), f32),
            pltpu.VMEM((2, 2, quarter, width), bf16),
            pltpu.VMEM((2, quarter, width), bf16),
            pltpu.VMEM((quarter, width), bf16),
            dma((4,)),
            dma((2 * depth,)),
            dma((depth - 1,)),
            dma((depth, 8)),
            dma((depth, 8)),
            dma((2, windows - 1)),
            dma((2, windows - 1)),
            dma((2,)),
            dma((2,)),
        ],
        compiler_params=pltpu.CompilerParams(
            collective_id=5, has_side_effects=True, vmem_limit_bytes=50 * 2**20
        ),
        cost_estimate=pl.CostEstimate(
            flops=8 * tokens * width * heads * head,
            bytes_accessed=2 * 8 * depth * quarter * wide,
            transcendentals=heads * tokens * windows * tokens,
        ),
        name="attention_front",
    )(block, weights, upstream, *in_place)
    return (outs[0].reshape(8 * depth * quarter, wide),) + tuple(outs[1:])


def back_kernel(
    units,
    score_scale,
    d_low_in,
    weights_in,
    q_in,
    k_in,
    v_in,
    turned_in,
    block_in,
    rows_in,
    d_pair_in,
    upstream_in,
    weighted_in,
    lse_in,
    query_start,
    query_at,
    cos_in,
    sin_in,
    own_rows_in,
    gain_in,
    d_resid_in,
    gain_two_in,
    side_in,
    out,
    small_out,
    block_out,
    d_rows_out,
    pieces_got,
    gate_out,
    up_out,
    down_out,
    qkv_w,
    turned,
    d_out,
    d_got,
    d_own,
    d_proj,
    part,
    core_got,
    x_got,
    d_rows,
    own,
    y_out,
    hop,
    from_z,
    small_own,
    small_hop,
    small_z,
    small,
    small_got,
    pieces,
    load_sem,
    d_send,
    d_recv,
    tp_send,
    tp_recv,
    y_send,
    y_recv,
    z_send,
    z_recv,
    little_send,
    little_recv,
    small_send,
    small_recv,
    swap_send,
    swap_recv,
    rows_send,
    rows_recv,
    own_sem,
    tile_sem,
    store_sem,
    strip_sem,
):
    at = Place()
    depth = at.depth
    count = 2 * depth
    heads, tokens, head = q_in.shape
    heads_width = heads * head
    windows = k_in.shape[1] // tokens
    quarter, width = d_rows.shape
    rows = out.shape[0]
    f32, bf16 = jnp.float32, jnp.bfloat16
    across = (((1,), (1,)), ((), ()))
    slot_here, slot_hidden, shared_hidden = units
    routed = slot_here * slot_hidden
    hidden = weighted_in.shape[2]
    few = 16

    def d_copy(w, h):
        peer = (at.ep - (2 - w), at.tp)
        return remote(d_out.at[w, h], d_got.at[w, h], d_send.at[w, h], d_recv.at[w, h], peer)

    def d_arrival(w, h):
        peer = (at.ep + (2 - w), at.tp)
        dst = d_got.at[w, h]
        return remote(dst, dst, d_send.at[w, h], d_recv.at[w, h], peer)

    def core_copy():
        return remote(part.at[:, 1 - at.c], core_got, tp_send.at[0], tp_recv.at[0], at.next_core)

    def x_copy():
        return remote(part.at[1 - at.x, at.c], x_got, tp_send.at[1], tp_recv.at[1], at.next_x)

    cuts = (pl.ds(0, heads_width), pl.ds(heads_width, 2 * heads_width))

    def y_copy(q, j):
        return remote(
            y_out.at[j, :, cuts[q]], hop.at[j, :, cuts[q]], y_send.at[q, j], y_recv.at[q, j], at.next_y
        )

    def z_copy(q, j):
        return remote(
            own.at[j, :, cuts[q]],
            from_z.at[j - 1, :, cuts[q]],
            z_send.at[q, j],
            z_recv.at[q, j],
            at.at_z(at.ahead(j)),
        )

    def little_y(j):
        return remote(
            small_own.at[at.ahead(j), 1 - at.y],
            small_hop.at[j],
            little_send.at[0, j],
            little_recv.at[0, j],
            at.next_y,
        )

    def little_z(j):
        return remote(
            small_own.at[at.ahead(j), at.y],
            small_z.at[j - 1],
            little_send.at[1, j],
            little_recv.at[1, j],
            at.at_z(at.ahead(j)),
        )

    def small_copy(kind):
        peer = at.next_core if kind == 0 else at.next_x
        return remote(
            small.at[kind], small_got.at[kind], small_send.at[kind], small_recv.at[kind], peer
        )

    ends = ((block_in, block_out), (d_rows, d_rows_out))

    def rows_copy(a, kind):
        mine, gathered = ends[a]
        if kind == 2:
            src = dst = gathered.at[1 - at.x, at.c]
        else:
            src, dst = mine, gathered.at[at.x, at.c]
        peer = at.next_x if kind == 0 else at.next_core
        return remote(src, dst, rows_send.at[a, kind], rows_recv.at[a, kind], peer)

    def rows_own(a):
        mine, gathered = ends[a]
        return pltpu.make_async_copy(mine, gathered.at[at.x, at.c], own_sem.at[a])

    def rows_begin(a):
        for kind in (0, 1):
            rows_copy(a, kind).start()
        rows_own(a).start()

    def rows_pass_on(a):
        rows_copy(a, 0).wait_recv()
        rows_copy(a, 2).start()

    def rows_end(a):
        rows_own(a).wait()
        rows_copy(a, 0).wait_send()
        rows_copy(a, 1).wait()
        rows_copy(a, 2).wait()

    def swap_copies(p, leave):
        some = pl.ds(p * shared_hidden, shared_hidden)
        copies = []
        for k in range(1, count):
            to, back = lax.rem(at.ep + k, count), lax.rem(at.ep + count - k, count)
            if leave:
                src, dst, peer = pieces.at[to, some], pieces_got.at[at.ep, some], to
            else:
                src, dst, peer = pieces.at[back, some], pieces_got.at[back, some], back
            copies.append(remote(src, dst, swap_send.at[p, k], swap_recv.at[p, k], (peer, at.tp)))
        return copies

    def swap_own(p):
        some = pl.ds(p * shared_hidden, shared_hidden)
        return pltpu.make_async_copy(
            pieces.at[at.ep, some], pieces_got.at[at.ep, some], own_sem.at[2 + p]
        )

    strips = 4
    strip = width // strips

    def load_strip(n):
        src = weights_in.at[pl.ds(n * strip, strip), pl.ds(0, 3 * heads_width)]
        return pltpu.make_async_copy(src, qkv_w.at[n % 2], strip_sem.at[n % 2])

    late_load = pltpu.make_async_copy(turned_in, turned, load_sem.at[1])
    lane = lax.broadcasted_iota(jnp.int32, (tokens, head), 1)
    sign = jnp.where(lane < head // 2, -1.0, 1.0)

    def unrotated(grads):
        turned_part = pltpu.roll(grads * sin_in[...], head // 2, 1) * sign
        return grads * cos_in[...] - turned_part

    def attention(d_low, out_w, q_all, k_all, v_all, d_att, probs, d_probs):
        pairs = (
            (d_low_in, d_low),
            (weights_in.at[:, pl.ds(3 * heads_width, heads_width)], out_w),
            (q_in, q_all),
            (k_in, k_all),
            (v_in, v_all),
        )
        copies = [
            pltpu.make_async_copy(src, dst, load_sem.at[2 + i])
            for i, (src, dst) in enumerate(pairs)
        ]
        for copy in copies + [late_load, load_strip(0), load_strip(1)]:
            copy.start()
        at.greet_row()
        rows_begin(0)
        copies[0].wait()
        copies[1].wait()
        d_attended = jnp.dot(d_low[...], out_w[...], preferred_element_type=f32).astype(bf16)
        for h in range(heads):
            d_att[h] = d_attended[:, h * head : (h + 1) * head]
        for copy in copies[2:]:
            copy.wait()

        def head_body(h, carry):
            queries, d_a = q_all[h], d_att[h]
            delta = jnp.zeros((1, tokens), f32)
            for w in range(windows):
                some = slice(w * tokens, (w + 1) * tokens)
                scores = lax.dot_general(
                    k_all[h, some], queries, across, preferred_element_type=f32
                )
                key_at = lax.broadcasted_iota(jnp.int32, scores.shape, 0)
                key_at = key_at + (at.ep + w + 1 - windows) * tokens
                allowed = (key_at >= query_start[...]) & (key_at <= query_at[...])
                p = jnp.where(allowed, jnp.exp(scores * score_scale - lse_in[h]), 0.0)
                d_p = lax.dot_general(v_all[h, some], d_a, across, preferred_element_type=f32)
                probs[w] = p
                d_probs[w] = d_p
                delta = delta + jnp.sum(p * d_p, axis=0, keepdims=True)
            d_queries = jnp.zeros((head, tokens), f32)
            for w in range(windows):
                some = slice(w * tokens, (w + 1) * tokens)
                p = probs[w]
                d_scores = (p * (d_probs[w] - delta)).astype(bf16)
                d_keys = jnp.dot(d_scores, queries, preferred_element_type=f32) * score_scale
                d_values = jnp.dot(p.astype(bf16), d_a, preferred_element_type=f32)
                if w < windows - 1:
                    d_out[w, h, :, :head] = d_keys.astype(bf16)
                    d_out[w, h, :, head:] = d_values.astype(bf16)

                    @pl.when(at.ep >= 2 - w)
                    def _():
                        d_copy(w, h).start()

                else:
                    d_own[h, :, :head] = d_keys
                    d_own[h, :, head:] = d_values
                d_queries = d_queries + jnp.dot(
                    k_all[h, some].T, d_scores, preferred_element_type=f32
                )
            here = pl.ds(pl.multiple_of(h * head, head), head)
            d_proj[:, here] = unrotated((d_queries * score_scale).T).astype(bf16)
            return carry

        lax.fori_loop(0, heads, head_body, 0)

    pl.run_scoped(
        attention,
        pltpu.VMEM((tokens, width), bf16),
        pltpu.VMEM((width, heads_width), bf16),
        pltpu.VMEM((heads, tokens, head), bf16),
        pltpu.VMEM((heads, windows * tokens, head), bf16),
        pltpu.VMEM((heads, windows * tokens, head), bf16),
        pltpu.VMEM((heads, tokens, head), bf16),
        pltpu.VMEM((windows, tokens, tokens), f32),
        pltpu.VMEM((windows, tokens, tokens), f32),
    )
    order = [j for j in range(1, depth)] + [0]

    def own_body(h, carry):
        for w in range(windows - 1):

            @pl.when(at.ep + (2 - w) < count)
            def _():
                d_arrival(w, h).wait_recv()
                d_own[h] += d_got[w, h].astype(f32)

        k_here = pl.ds(pl.multiple_of(heads_width + h * head, head), head)
        v_here = pl.ds(pl.multiple_of(2 * heads_width + h * head, head), head)
        d_proj[:, k_here] = unrotated(d_own[h, :, :head]).astype(bf16)
        d_proj[:, v_here] = d_own[h, :, head:].astype(bf16)
        return carry

    def weight_rows(into, q, z, y):
        here = pl.ds(pl.multiple_of((z * 2 + y) * rows, rows), rows)
        product = jnp.dot(turned[here], d_proj[:, cuts[q]], preferred_element_type=f32)
        into[:, cuts[q]] = product.astype(bf16)

    def begin_sums(q):
        for j in order:
            weight_rows(y_out.at[j], q, at.ahead(j), 1 - at.y)
            y_copy(q, j).start()

    def own_sums(q):
        for j in order:
            weight_rows(own.at[j], q, at.ahead(j), at.y)

    def projections():
        lax.fori_loop(0, heads, own_body, 0)
        for n in range(strips):
            some = slice(n * strip, (n + 1) * strip)
            load_strip(n).wait()
            product = lax.dot_general(
                d_proj[...], qkv_w[n % 2], across, preferred_element_type=f32
            )
            part[:, :, :, some] = product.astype(bf16).reshape(2, 2, quarter, strip)
            if n + 2 < strips:
                load_strip(n + 2).start()
        core_copy().start()
        begin_sums(1)
        core_copy().wait()
        for x in (0, 1):
            part[x, at.c] = part[x, at.c] + core_got[x]
        x_copy().start()
        own_sums(1)
        x_copy().wait()

        def end_body(i, carry):
            here = pl.ds(pl.multiple_of(i * few, few), few)
            grads = part[at.x, at.c, here].astype(f32) + x_got[here].astype(f32)
            inputs = own_rows_in[here].astype(f32)
            scale = lax.rsqrt(jnp.mean(inputs * inputs, axis=1, keepdims=True) + epsilon)
            unit_rows = inputs * scale
            scaled = grads * gain_in[...]
            inner = jnp.mean(scaled * unit_rows, axis=1, keepdims=True)
            total = d_resid_in[here] + scale * (scaled - unit_rows * inner)
            d_rows[here] = total.astype(bf16)
            return carry + jnp.sum(grads * unit_rows, axis=0, keepdims=True)

        d_gain = lax.fori_loop(0, quarter // few, end_body, jnp.zeros((1, width), f32))
        rows_begin(1)
        line = lax.broadcasted_iota(jnp.int32, (128, rows), 0)
        for e in range(count):
            some = slice(e * rows, (e + 1) * rows)
            gains = jnp.where(line == 0, d_gain[:, some], 0.0)
            gains = jnp.where(line == 1, gain_two_in[:, some], gains)
            small_own[e // 2, e % 2] = (gains.T + side_in[some]).astype(bf16)
        for j in order:
            little_y(j).start()

    def after_y(q, j):
        y_copy(q, j).wait_recv()

        def body(i, carry):
            some = pl.ds(pl.multiple_of(i * few, few), few)
            own[j, some, cuts[q]] = own[j, some, cuts[q]] + hop[j, some, cuts[q]]
            return carry

        lax.fori_loop(0, rows // few, body, 0)
        if j > 0:
            z_copy(q, j).start()

    def after_little():
        for j in order:
            little_y(j).wait_recv()
            here = small_own.at[at.ahead(j), at.y]
            here[...] = here[...] + small_hop[j]
            if j > 0:
                little_z(j).start()

    hooks = {(0, 0): [functools.partial(rows_pass_on, 0)]}
    for i, j in enumerate(order):
        here = (1, min(count // 2 + i, count - 1))
        hooks.setdefault(here, []).append(functools.partial(after_y, 0, j))
    hooks[(2, 2)] = [functools.partial(rows_pass_on, 1)]
    hooks[(2, 3)] = [after_little]
    last_hooks = []
    for i, j in enumerate(order):
        when = 2 + 5 * i
        due = functools.partial(after_y, 1, j)
        if when < count:
            hooks.setdefault((2, when), []).append(due)
        else:
            last_hooks.append(due)

    def weight_gradients(turned_left, left_tile, right_part, staging):
        lefts = (
            lambda tile: d_pair_in.at[tile, :, pl.ds(0, hidden)],
            lambda tile: d_pair_in.at[tile, :, pl.ds(hidden, hidden)],
            lambda tile: weighted_in.at[tile],
        )
        rights = (rows_in, rows_in, upstream_in)
        results = (gate_out, up_out, down_out)
        columns = width // count

        def load_left(p, tile):
            slot = lax.rem(tile, 2)
            return pltpu.make_async_copy(
                lefts[p](tile), left_tile.at[slot], tile_sem.at[0, slot]
            )

        def load_right(p, n):
            slot = lax.rem(n, 2)
            here = pl.ds(pl.multiple_of(n * columns, columns), columns)
            return pltpu.make_async_copy(
                rights[p].at[:, :, here], right_part.at[slot], tile_sem.at[1, slot]
            )

        def store(p, n):
            slot = lax.rem(n, 2)
            here = pl.ds(pl.multiple_of(n * columns, columns), columns)
            return pltpu.make_async_copy(
                staging.at[slot], results[p].at[:, here], store_sem.at[slot]
            )

        def turn_left(p, tile):
            load_left(p, tile).wait()

            @pl.when(tile + 1 < count)
            def _():
                load_left(p, tile + 1).start()

            here = pl.ds(pl.multiple_of(tile * tokens, tokens), tokens)
            turned_left[:, here] = left_tile[lax.rem(tile, 2)].T

        def run_pass(p):
            def part_body(n, carry):
                slot = lax.rem(n, 2)
                load_right(p, n).wait()

                @pl.when(n + 1 < count)
                def _():
                    load_right(p, n + 1).start()

                if p < 2:

                    @pl.when(n + 1 == count)
                    def _():
                        load_right(p + 1, 0).start()

                @pl.when(n >= 2)
                def _():
                    store(p, n - 2).wait()

                product = jnp.dot(
                    turned_left[...],
                    right_part[slot].reshape(count * tokens, columns),
                    preferred_element_type=f32,
                )
                staging[slot] = product[:routed].astype(bf16)
                pieces[n, p * shared_hidden : (p + 1) * shared_hidden] = product[
                    routed : routed + shared_hidden
                ].astype(bf16)
                store(p, n).start()
                for (hook_pass, hook_part), actions in hooks.items():
                    if hook_pass == p:

                        @pl.when(n == hook_part)
                        def _():
                            for action in actions:
                                action()

                return carry

            def turn_body(tile, carry):
                turn_left(p, tile)
                return carry

            lax.fori_loop(0, count, turn_body, 0)
            if p < 2:
                load_left(p + 1, 0).start()
            lax.fori_loop(0, count, part_body, 0)
            for n in (count - 2, count - 1):
                store(p, n).wait()
            swap_own(p).start()
            if p > 0:
                start_swap(p)

        def start_swap(p):
            for copy in swap_copies(p, True):
                copy.start()

        hooks.setdefault((1, count - 2), []).append(functools.partial(start_swap, 0))
        load_left(0, 0).start()
        load_right(0, 0).start()
        late_load.wait()
        begin_sums(0)
        own_sums(0)

        run_pass(0)
        run_pass(1)
        projections()
        run_pass(2)
        for action in last_hooks:
            action()

    pl.run_scoped(
        weight_gradients,
        pltpu.VMEM((hidden, count * tokens), bf16),
        pltpu.VMEM((2, tokens, hidden), bf16),
        pltpu.VMEM((2, count, tokens, width // count), bf16),
        pltpu.VMEM((2, routed, width // count), bf16),
    )
    total = small_own[at.z, at.y].astype(f32)
    for j in range(1, depth):
        little_z(j).wait_recv()
        total = total + small_z[j - 1].astype(f32)
    for kind in (0, 1):
        small[kind] = total
        small_copy(kind).start()
        small_copy(kind).wait()
        total = small[kind] + small_got[kind]
    small_out[...] = total
    for j in range(1, depth):
        for q in (0, 1):
            z_copy(q, j).wait_recv()

    def total_body(i, carry):
        some = pl.ds(pl.multiple_of(i * few, few), few)
        result = own[0, some].astype(f32)
        for k in range(depth - 1):
            result = result + from_z[k, some].astype(f32)
        out[some] = result
        return carry

    lax.fori_loop(0, rows // few, total_body, 0)
    for j in range(depth):
        little_y(j).wait_send()
        if j > 0:
            little_z(j).wait_send()
        for q in (0, 1):
            y_copy(q, j).wait_send()
            if j > 0:
                z_copy(q, j).wait_send()
    for a in (0, 1):
        rows_end(a)
    for p in range(3):
        swap_own(p).wait()
        for copy in swap_copies(p, False):
            copy.wait_recv()
        for copy in swap_copies(p, True):
            copy.wait_send()

    def finish(h, carry):
        for w in range(windows - 1):

            @pl.when(at.ep >= 2 - w)
            def _():
                d_copy(w, h).wait_send()

        return carry

    lax.fori_loop(0, heads, finish, 0)


def backward(large, tiles_of, in_place, units, scale):
    d_low, _, queries, keys = large[:4]
    heads, tokens, head = queries.shape
    width = d_low.shape[1]
    ep_count = lax.axis_size("ep")
    depth, rows = ep_count // 2, width // ep_count
    quarter = tokens // lax.axis_size("tp")
    windows = keys.shape[1] // tokens
    columns = 3 * heads * head
    hidden = tiles_of[3].shape[2]
    slot_here, slot_hidden, shared_hidden = units
    f32, bf16 = jnp.float32, jnp.bfloat16
    anywhere = pl.BlockSpec(memory_space=pl.ANY)
    in_vmem = pl.BlockSpec(memory_space=pltpu.VMEM)
    dma = pltpu.SemaphoreType.DMA
    pieces = (ep_count, 3 * shared_hidden, rows)
    gathered = jax.ShapeDtypeStruct((2, 2, quarter, width), bf16)
    routed = jax.ShapeDtypeStruct((slot_here * slot_hidden, width), bf16)

    def vmem(*shape, dtype=bf16):
        return pltpu.VMEM(shape, dtype)

    out, small, block_out, d_rows, pieces, gate, up, down = pl.pallas_call(
        functools.partial(back_kernel, units, scale),
        out_shape=(
            jax.ShapeDtypeStruct((rows, columns), f32),
            jax.ShapeDtypeStruct((rows, 128), f32),
            gathered,
            gathered,
            jax.ShapeDtypeStruct(pieces, bf16),
            routed,
            routed,
            routed,
        ),
        in_specs=[anywhere] * (len(large) + len(tiles_of)) + [in_vmem] * len(in_place),
        out_specs=(in_vmem, in_vmem) + (anywhere,) * 6,
        scratch_shapes=[
            vmem(2, width // 4, columns),
            vmem(width, tokens),
            vmem(windows - 1, heads, tokens, 2 * head),
            vmem(windows - 1, heads, tokens, 2 * head),
            vmem(heads, tokens, 2 * head, dtype=f32),
            vmem(tokens, columns),
            vmem(2, 2, quarter, width),
            vmem(2, quarter, width),
            vmem(quarter, width),
            vmem(quarter, width),
            vmem(depth, rows, columns),
            vmem(depth, rows, columns),
            vmem(depth, rows, columns),
            vmem(depth - 1, rows, columns),
            vmem(depth, 2, rows, 128),
            vmem(depth, rows, 128),
            vmem(depth - 1, rows, 128),
            vmem(2, rows, 128, dtype=f32),
            vmem(2, rows, 128, dtype=f32),
            vmem(*pieces),
            dma((7,)),
            dma((windows - 1, heads)),
            dma((windows - 1, heads)),
            dma((2,)),
            dma((2,)),
            dma((2, depth)),
            dma((2, depth)),
            dma((2, depth)),
            dma((2, depth)),
            dma((2, depth)),
            dma((2, depth)),
            dma((2,)),
            dma((2,)),
            dma((3, ep_count)),
            dma((3, ep_count)),
            dma((2, 3)),
            dma((2, 3)),
            dma((5,)),
            dma((2, 2)),
            dma((2,)),
            dma((2,)),
        ],
        compiler_params=pltpu.CompilerParams(
            collective_id=4, has_side_effects=True, vmem_limit_bytes=62 * 2**20
        ),
        cost_estimate=pl.CostEstimate(
            flops=6 * ep_count * tokens * width * hidden,
            bytes_accessed=8 * ep_count * tokens * width,
            transcendentals=heads * tokens * windows * tokens,
        ),
        name="backward",
    )(*large, *tiles_of, *in_place)
    block_out, d_rows = [array.reshape(4 * quarter, width) for array in (block_out, d_rows)]
    return out, small, block_out, d_rows, pieces, (gate, up, down)


def shared_pieces(weights, ep_count):
    rows, hidden = weights[0].shape
    units = hidden // ep_count
    return jnp.concatenate([weight.T.reshape(ep_count, units, rows) for weight in weights], axis=1)


def shared_whole(pieces, count):
    ep_count, units, columns = pieces.shape
    units = units // count
    pieces = pieces.reshape(ep_count, count, units, columns).astype(jnp.float32)
    return [pieces[:, i].reshape(ep_count * units, columns).T for i in range(count)]


def dense_body(
    tokens,
    lengths,
    routes,
    attn_gain,
    w_query,
    w_key,
    w_value,
    w_out,
    ffn_gain,
    w_router,
    shared_mix,
    shared_gate,
    shared_up,
    shared_down,
    expert_gate,
    expert_up,
    expert_down,
    cotangent,
):
    rows_here, width = tokens.shape
    ep_count = lax.axis_size("ep")
    tp_count = lax.axis_size("tp")
    ep_index = lax.axis_index("ep")
    offset = ep_index * rows_here
    quarter = rows_here // tp_count
    first_row = lax.axis_index("tp") * quarter
    slot_here, slot_hidden = expert_gate.shape[0], expert_gate.shape[1]
    expert_count = w_router.shape[1]
    bf16, f32 = jnp.bfloat16, jnp.float32

    def my_rows(array):
        return lax.dynamic_slice_in_dim(array, first_row, quarter, 0)

    side_columns = jnp.concatenate(
        [attn_gain[:, None], ffn_gain[:, None], shared_mix[:, None], w_router], axis=1
    )
    side_columns = jnp.pad(side_columns, ((0, 0), (0, -side_columns.shape[1] % 128)))
    joined_weights, pieces = gather_over_ep(
        (w_query, w_key, w_value, w_out, side_columns),
        shared_pieces((shared_gate, shared_up, shared_down), ep_count),
    )
    heads_width = w_query.shape[1]
    side_weight = joined_weights[:, 4 * heads_width :]
    picked = jnp.any(
        my_rows(routes)[:, :, None] == jnp.arange(expert_count, dtype=jnp.int32), axis=1
    )
    picked_lanes = jnp.pad(picked.astype(bf16), ((0, 0), (3, 125 - expert_count)))
    upstream_rows = jnp.concatenate([my_rows(cotangent), picked_lanes], axis=1)
    shared_units = pieces.shape[1] // 3
    routed_units = slot_here * slot_hidden
    heads_here = heads_width // HD
    score_scale = HD ** (-0.5)
    first_norm_scale = side_weight[:, 0].astype(f32)
    second_norm_scale = side_weight[:, 1].astype(f32)
    query_at = offset + jnp.arange(rows_here, dtype=jnp.int32)
    _, query_pos = sequence_info(lengths, query_at)
    cosine, sine = rope_tables(query_pos, HD)
    tables = (cosine[:, 0], sine[:, 0], (query_at - query_pos)[None, :], query_at[None, :])
    (
        upstream_all,
        normed_one_turned,
        keys_win,
        values_win,
        queries,
        log_total,
        attended,
        resid,
        normed_two,
    ) = attention_front(
        tokens,
        joined_weights,
        upstream_rows,
        tables + (my_rows(tokens), first_norm_scale[None, :], second_norm_scale[None, :]),
        heads_here,
        score_scale,
    )
    (
        normed_all,
        weighted_h,
        d_pair_pre,
        block_rows,
        d_resid_low,
        d_resid,
        grad_gain_two,
        d_side,
    ) = ffn_over_all(
        normed_two,
        upstream_all,
        (expert_gate, expert_up, expert_down),
        pieces,
        joined_weights,
        resid,
        second_norm_scale[None, :],
        (slot_here, slot_hidden, shared_units),
        expert_count,
    )
    grad_side = jnp.dot(normed_two.astype(f32).T, d_side, precision=highest)
    grad_out = jnp.einsum("td,th->dh", d_resid_low, attended, preferred_element_type=f32)
    grad_out = lax.psum_scatter(
        grad_out.astype(bf16), "ep", scatter_dimension=0, tiled=True
    ).astype(f32)
    tile_shape = (ep_count, rows_here, -1)
    tiles_of = tuple(
        array.reshape(tile_shape) for array in (normed_all, d_pair_pre, upstream_all, weighted_h)
    )
    units = (slot_here, slot_hidden, shared_units)
    column = jnp.arange(128, dtype=jnp.int32)
    large = (
        d_resid_low,
        joined_weights,
        queries,
        keys_win,
        values_win,
        normed_one_turned,
        block_rows,
    )
    in_place = (
        log_total,
        tables[2],
        tables[3],
        tables[0],
        tables[1],
        my_rows(tokens),
        first_norm_scale[None, :],
        d_resid,
        grad_gain_two[None, :],
        jnp.where(column >= 2, grad_side, 0.0),
    )
    grad_weights, small, block_out, grad_tokens, grad_pieces, grad_experts = backward(
        large, tiles_of, in_place, units, score_scale
    )
    grad_shared = shared_whole(grad_pieces, 3)
    grad_tokens = grad_tokens.astype(f32)
    grad_experts = [grad.astype(f32).reshape(expert_gate.shape) for grad in grad_experts]
    parts = [grad_weights[:, i * heads_width : (i + 1) * heads_width] for i in range(3)]
    return (
        block_out,
        grad_tokens,
        small[:, 0],
        parts[0],
        parts[1],
        parts[2],
        grad_out,
        small[:, 1],
        small[:, 3 : 3 + expert_count],
        small[:, 2],
        grad_shared[0],
        grad_shared[1],
        grad_shared[2],
        grad_experts[0],
        grad_experts[1],
        grad_experts[2],
    )


def chosen_body(*arrays):
    rows_here, top_count = arrays[2].shape
    slot_here, expert_count = arrays[14].shape[0], arrays[9].shape[1]
    capacity = rows_here * top_count * 7 // (5 * expert_count)
    grid_of_two = lax.axis_size("ep") % 2 == 0 and lax.axis_size("tp") == 4
    if grid_of_two and rows_here < 2 * slot_here * capacity:
        return dense_body(*arrays)
    return body(*arrays)


def solution(mesh):
    placed = (
        P("ep", None),
        P(),
        P("ep", None),
        P("ep"),
        P("ep", "tp"),
        P("ep", "tp"),
        P("ep", "tp"),
        P("ep", "tp"),
        P("ep"),
        P("ep", None),
        P("ep"),
        P("ep", "tp"),
        P("ep", "tp"),
        P("ep", "tp"),
        P("ep", "tp", None),
        P("ep", "tp", None),
        P("ep", "tp", None),
        P("ep", None),
    )
    return jax.shard_map(
        chosen_body,
        mesh=mesh,
        in_specs=placed,
        out_specs=(
            P("ep", None),
            P("ep", None),
            P("ep"),
            P("ep", "tp"),
            P("ep", "tp"),
            P("ep", "tp"),
            P("ep", "tp"),
            P("ep"),
            P("ep", None),
            P("ep"),
            P("ep", "tp"),
            P("ep", "tp"),
            P("ep", "tp"),
            P("ep", "tp", None),
            P("ep", "tp", None),
            P("ep", "tp", None),
        ),
        check_vma=False,
    )
```
